32 devices in a mesh: basin: 8 (over z, x), tm: 4 (over y, core).
Axes of the slice: x: 2, y: 2, z: 4, core: 2. Of those that a mesh axis runs over, the one named last changes fastest.
Arguments:
- incidence: int32 [256, 16, 128], P('basin'), may hold values 0 or 1
- row_gauge: int32 [4096], P('basin'), may hold values from 0 to 2047, as said below
- gauge_kernel: int32 [2048], P('basin'), may hold values from 0 to 31
- kernels: float32 [32, 128], replicated, may hold values from 0 to 0.0156
- observed: float32 [2048, 512], P('basin', 'tm'), may hold values from -8 to 8
- first_guess: float32 [32768, 512], P('basin', 'tm'), may hold values from -4 to 4
Outputs:
- inflows: float32 [32768, 512], P('basin', 'tm')
The draws below stay inside these ranges and needn't reach their ends.
Inputs may be any that keep to these rules, and one draw needn't show every extreme that they name: `row_gauge`: the 512 slots of one index of basin name gauges of any one owner (gauges o * 256 to o * 256 + 255 belong to owner o) at most 128 times; in every draw one owner is named exactly 128 times by the slots of every index of basin.
All inputs are finite; a program needn't handle non-finite values. No bound on the sum of `incidence` on one device may be relied on, other than what follows from the above.
Results may differ from the reference program's by a relative error of at most 0.0001.
Values sent between devices are 32-bit elements; how exact they have to be, the bound alone decides.
No kernel may reach another device: no remote copies, remote signals or barrier semaphores. Data moves between devices by JAX's collectives and lax.ppermute only.
A program may use at most 128 MiB of HBM per device.

```python
import jax
import jax.numpy as jnp
from jax import lax

BLK = 128
BSLOT = 16
RB = 32
G_DEV = 256
TAPS = 128
NK = 32
ITERS = 3
BLOCKS = 256
REACHES = 32768
GAUGES = 2048
HOURS = 512
CAP = 128
N_BASIN = 8


def draw_row_gauge(key, part):
    rows = RB * BSLOT
    key_busy, key_shift, key_perm, key_local = jax.random.split(jax.random.fold_in(key, 11), 4)
    busy = jax.random.randint(key_busy, (), 0, N_BASIN)
    index = jnp.arange(rows, dtype=jnp.int32)[None, :]
    offset = jax.random.randint(key_shift, (N_BASIN, 1), 0, N_BASIN - 1)
    other = (index - CAP + offset) % (N_BASIN - 1)
    other = other + (other >= busy).astype(jnp.int32)
    owner = jnp.where(index < CAP, busy, other).astype(jnp.int32)
    orders = jax.vmap(lambda sub: jax.random.permutation(sub, rows))(jax.random.split(key_perm, N_BASIN))
    owner = jnp.take_along_axis(owner, orders.astype(jnp.int32), axis=1).reshape(-1)
    local = jax.random.randint(key_local, (N_BASIN * rows,), 0, G_DEV)
    lowest = jnp.argmin(owner)
    highest = jnp.argmax(owner)
    local = local.at[lowest].set(0)
    local = local.at[highest].set(G_DEV - 1)
    return (owner * G_DEV + local).astype(jnp.int32)


def draw_observed(key, part):
    key_base, key_hour = jax.random.split(jax.random.fold_in(key, 23), 2)
    rows = jnp.arange(GAUGES, dtype=jnp.float32)[:, None] / GAUGES
    ramp = jnp.exp(2.302585 * rows)
    hour_scale = jnp.exp(2.302585 * jax.random.uniform(key_hour, (1, HOURS), jnp.float32))
    base = jnp.clip(jax.random.normal(key_base, (GAUGES, HOURS), jnp.float32), -4.0, 4.0)
    return (0.02 * base * ramp * hour_scale).astype(jnp.float32)


def plant(drawn, stream_key, low, top_value):
    longest = drawn.shape.index(max(drawn.shape))
    spots = []
    for shift in (0, 1):
        where = [jax.random.randint(jax.random.fold_in(stream_key, axis), (), 0, length) for axis, length in enumerate(drawn.shape)]
        where[longest] = (where[longest] + shift) % drawn.shape[longest]
        spots.append(tuple(where))
    return drawn.at[spots[0]].set(low).at[spots[1]].set(top_value)


def block_levels(own_key, extent, shards, smallest, high):
    gain, own = 1.0, jax.random.fold_in(own_key, 6)
    for position, blocks in shards:
        steps = jnp.exp(jax.random.uniform(jax.random.fold_in(own, position), (blocks,), jnp.float32, smallest / len(shards), high / len(shards)))
        gain = gain * jnp.repeat(steps, extent[position] // blocks).reshape([-1 if axis == position else 1 for axis in range(len(extent))])
    return gain


def gaussian(stream_key, shape, scale, limit, shards=(), kind=jnp.bfloat16):
    result = jax.random.normal(stream_key, shape, jnp.float32) * scale
    if len(shards) > 0:
        result = block_levels(stream_key, shape, shards, -0.22, 0.18) * result
    return jnp.clip(result, min=-limit, max=limit).astype(kind)


def setup_inputs(seed: int = 0) -> dict:
    key_list = jax.random.split(jax.random.key(seed), 7)
    return {
        "incidence": plant((jax.random.randint(key_list[0], (BLOCKS, BSLOT, BLK), 0, 2) < 1).astype(jnp.int32), jax.random.fold_in(key_list[0], 1), 0, 1),
        "row_gauge": draw_row_gauge(jax.random.fold_in(key_list[6], 71), 0),
        "gauge_kernel": plant(jax.random.randint(key_list[2], (GAUGES,), 0, NK), jax.random.fold_in(key_list[2], 1), 0, NK - 1).astype(jnp.int32),
        "kernels": jnp.clip(jax.random.uniform(key_list[3], (NK, TAPS), jnp.float32, 0.0, 0.0156), 0.0, 0.0156),
        "observed": draw_observed(jax.random.fold_in(key_list[6], 71), 0),
        "first_guess": gaussian(key_list[5], (REACHES, HOURS), 0.3, 4.0, ((0, 8), (1, 4)), jnp.float32),
    }


HIGH = lax.Precision.HIGHEST

def subtree(field, incidence):
    blocks = incidence.shape[0]
    weights = incidence.astype(jnp.float32)
    shaped = field.reshape(blocks, BLK, HOURS)
    return jnp.einsum('bjr,brt->bjt', weights, shaped, precision=HIGH).reshape(blocks * BSLOT, HOURS)

def spread_rows(rows, incidence):
    blocks = incidence.shape[0]
    weights = incidence.astype(jnp.float32)
    shaped = rows.reshape(blocks, BSLOT, HOURS)
    return jnp.einsum('bjr,bjt->brt', weights, shaped, precision=HIGH).reshape(blocks * BLK, HOURS)

def delay(series, taps_of):
    padded = jnp.pad(series, ((0, 0), (TAPS - 1, 0)))

    def step(tau, total):
        piece = lax.dynamic_slice_in_dim(padded, TAPS - 1 - tau, HOURS, 1)
        weight = lax.dynamic_slice_in_dim(taps_of, tau, 1, 1)
        return total + weight * piece
    return lax.fori_loop(0, TAPS, step, jnp.zeros(series.shape, jnp.float32))

def advance(series, taps_of):
    padded = jnp.pad(series, ((0, 0), (0, TAPS - 1)))

    def step(tau, total):
        piece = lax.dynamic_slice_in_dim(padded, tau, HOURS, 1)
        weight = lax.dynamic_slice_in_dim(taps_of, tau, 1, 1)
        return total + weight * piece
    return lax.fori_loop(0, TAPS, step, jnp.zeros(series.shape, jnp.float32))

def norm_of(values):
    return jnp.sqrt(jnp.sum(values * values))

def reference(incidence, row_gauge, gauge_kernel, kernels, observed, first_guess):
    taps_of = kernels[gauge_kernel]

    def forward(field):
        partial_value = subtree(field, incidence)
        sums = jnp.zeros((GAUGES, HOURS), jnp.float32).at[row_gauge].add(partial_value)
        return delay(sums, taps_of)

    def backward(series):
        upstream = advance(series, taps_of)
        return spread_rows(upstream[row_gauge], incidence)
    start = observed - forward(first_guess)
    beta = norm_of(start)
    u = start / beta
    pulled = backward(u)
    alpha = norm_of(pulled)
    v = pulled / alpha
    w = v
    correction = jnp.zeros(first_guess.shape, jnp.float32)
    phibar = beta
    rhobar = alpha
    for step in range(ITERS):
        p = forward(v) - alpha * u
        beta = norm_of(p)
        u = p / beta
        rho = jnp.sqrt(rhobar * rhobar + beta * beta)
        cosine = rhobar / rho
        sine = beta / rho
        phi = cosine * phibar
        phibar = sine * phibar
        correction = correction + phi / rho * w
        if step < ITERS - 1:
            pulled = backward(u) - beta * v
            alpha = norm_of(pulled)
            v = pulled / alpha
            theta = sine * alpha
            rhobar = -cosine * alpha
            w = v - theta / rho * w
    return first_guess + correction
```

```python
import functools

import jax
import jax.numpy as jnp
import numpy as np
from jax import lax
from jax.experimental import pallas as pl
from jax.experimental.pallas import tpu as pltpu
from jax.sharding import PartitionSpec as P

F32 = jnp.float32
BF16 = jnp.bfloat16
HIGH = lax.Precision.HIGHEST
SPAN = 256
VMEM_BYTES = 56 * 1024 * 1024


def params():
    return pltpu.CompilerParams(vmem_limit_bytes=VMEM_BYTES)


def transforms():
    half = SPAN // 2
    freq = 2.0 * np.pi * (np.arange(half) + 0.5) / SPAN
    phase = np.arange(SPAN)[:, None] * freq[None, :]
    forward = np.concatenate([np.cos(phase), -np.sin(phase)], axis=1)
    inverse = forward.T * (2.0 / SPAN)
    return (
        jnp.asarray(forward, F32),
        jnp.asarray(inverse[:, :half], F32),
        jnp.asarray(inverse[:, half:], F32),
    )


def dot(a, b):
    return jnp.dot(a, b, preferred_element_type=F32)


def exact(a, b):
    return jnp.dot(a, b, precision=HIGH, preferred_element_type=F32)


def pieces(value, count):
    out = []
    for _ in range(count):
        piece = value.astype(BF16)
        out.append(piece)
        value = value - piece.astype(F32)
    return out


def pick(hot, value):
    return sum(dot(hot, piece) for piece in pieces(value, 3))


def prepare_kernel(inc_ref, field_ref, partial_ref, gram_ref):
    blocks, slots, width = inc_ref.shape
    rows = blocks * slots
    weights = inc_ref[...].astype(F32).astype(BF16)
    for b in range(blocks):
        value = field_ref[pl.ds(b * width, width), :]
        partial_ref[pl.ds(b * slots, slots), :] = pick(weights[b], value)
    flat = weights.reshape(rows, width)
    full = lax.dot_general(flat, flat, (((1,), (1,)), ((), ())), preferred_element_type=F32)
    row = lax.broadcasted_iota(jnp.int32, (rows, rows), 0)
    col = lax.broadcasted_iota(jnp.int32, (rows, rows), 1)
    own = jnp.where(row // slots == col // slots, full, 0.0)
    gram_ref[...] = jnp.sum(own.reshape(blocks, slots, rows), axis=0)


def prepare(incidence, field):
    blocks, slots, width = incidence.shape
    hours = field.shape[1]
    step = 8
    return pl.pallas_call(
        prepare_kernel,
        grid=(blocks // step,),
        in_specs=[
            pl.BlockSpec((step, slots, width), lambda i: (i, 0, 0)),
            pl.BlockSpec((step * width, hours), lambda i: (i, 0)),
        ],
        out_specs=[
            pl.BlockSpec((step * slots, hours), lambda i: (i, 0)),
            pl.BlockSpec((slots, step * slots), lambda i: (0, i)),
        ],
        out_shape=[
            jax.ShapeDtypeStruct((blocks * slots, hours), F32),
            jax.ShapeDtypeStruct((slots, blocks * slots), F32),
        ],
        compiler_params=params(),
        name="prepare",
    )(incidence, field)


def table_kernel(gauge_ref, partial_ref, out_ref):
    slots = partial_ref.shape[0]
    rows = out_ref.shape[0]
    first = pl.program_id(0) * rows
    gauge = lax.broadcasted_iota(jnp.int32, (rows, slots), 0) + first
    hot = jnp.where(gauge_ref[...] == gauge, 1.0, 0.0).astype(BF16)
    out_ref[...] = pick(hot, partial_ref[...])


def table(row_gauge, partial, gauges):
    slots, hours = partial.shape
    step = 256
    return pl.pallas_call(
        table_kernel,
        grid=(gauges // step,),
        in_specs=[
            pl.BlockSpec((1, slots), lambda i: (0, 0)),
            pl.BlockSpec((slots, hours), lambda i: (0, 0)),
        ],
        out_specs=pl.BlockSpec((step, hours), lambda i: (i, 0)),
        out_shape=jax.ShapeDtypeStruct((gauges, hours), F32),
        compiler_params=params(),
        name="table",
    )(row_gauge.reshape(1, slots), partial)


def couple_kernel(first_ref, lane_ref, sub_ref, gram_ref, high_ref, low_ref, near_ref):
    slots = gram_ref.shape[0]
    count = lane_ref.shape[1]
    rows, cols = high_ref.shape
    tile = 256
    first = first_ref[0]

    @pl.when(pl.program_id(0) == 0)
    def _():
        row = lax.broadcasted_iota(jnp.int32, (tile, tile), 0)
        col = lax.broadcasted_iota(jnp.int32, (tile, tile), 1)
        same = row // slots == col // slots
        mine = lax.broadcasted_iota(jnp.int32, (rows, tile), 0) + first

        def body(i, carry):
            here = pl.ds(pl.multiple_of(i * tile, tile), tile)
            block = jnp.concatenate([gram_ref[:, here]] * (tile // slots), axis=0)
            block = jnp.where(same, block, 0.0).astype(BF16)
            hot = jnp.where(lane_ref[:, here] == mine, 1.0, 0.0).astype(BF16)
            near_ref[:, here] = dot(hot, block)
            return carry

        lax.fori_loop(0, count // tile, body, 0)

    def chunk(i, total):
        here = pl.ds(pl.multiple_of(i * 1024, 1024), 1024)
        gauge = lax.broadcasted_iota(jnp.int32, (1024, cols), 1) + pl.program_id(0) * cols
        hot = jnp.where(sub_ref[here, :] == gauge, 1.0, 0.0).astype(BF16)
        near = near_ref[:, here]
        high = near.astype(BF16)
        low = (near - high.astype(F32)).astype(BF16)
        return total + dot(high, hot) + dot(low, hot)

    total = lax.fori_loop(0, count // 1024, chunk, jnp.zeros((rows, cols), F32))
    high, low = pieces(total, 2)
    high_ref[...] = high
    low_ref[...] = low


def couple(first, row_gauge, gram, rows, gauges):
    count = row_gauge.shape[0]
    step = 256
    return pl.pallas_call(
        couple_kernel,
        grid=(gauges // step,),
        in_specs=[
            pl.BlockSpec(memory_space=pltpu.SMEM),
            pl.BlockSpec((1, count), lambda i: (0, 0)),
            pl.BlockSpec((count, 1), lambda i: (0, 0)),
            pl.BlockSpec(gram.shape, lambda i: (0, 0)),
        ],
        out_specs=[pl.BlockSpec((rows, step), lambda i: (0, i))] * 2,
        out_shape=[jax.ShapeDtypeStruct((rows, gauges), BF16)] * 2,
        scratch_shapes=[pltpu.VMEM((rows, count), F32)],
        compiler_params=params(),
        name="couple",
    )(first, row_gauge.reshape(1, count), row_gauge.reshape(count, 1), gram)


def mix_kernel(high_ref, low_ref, value_ref, out_ref):
    high = high_ref[...]
    low = low_ref[...]
    one, two, three = pieces(value_ref[...], 3)
    out_ref[...] = (dot(high, three) + dot(low, two)) + (dot(high, two) + dot(low, one)) + dot(high, one)


def mix(high, low, value):
    return pl.pallas_call(
        mix_kernel,
        out_shape=jax.ShapeDtypeStruct((high.shape[0], value.shape[1]), F32),
        compiler_params=params(),
        name="mix",
    )(high, low, value)


def spectrum_kernel(class_ref, kernels_ref, forward_ref, out_ref):
    rows = class_ref.shape[0]
    classes, taps = kernels_ref.shape
    kind = lax.broadcasted_iota(jnp.int32, (rows, classes), 1)
    hot = jnp.where(class_ref[...] == kind, 1.0, 0.0)
    out_ref[...] = exact(exact(hot, kernels_ref[...]), forward_ref[pl.ds(0, taps), :])


def spectrum(gauge_kernel, kernels, forward):
    rows = gauge_kernel.shape[0]
    return pl.pallas_call(
        spectrum_kernel,
        out_shape=jax.ShapeDtypeStruct((rows, SPAN), F32),
        compiler_params=params(),
        name="spectrum",
    )(gauge_kernel.reshape(rows, 1), kernels, forward)


def delayed(before, here, after, spec, forward, inverse_last):
    rows, half = here.shape
    stacked = jnp.concatenate(
        [jnp.concatenate([before, here], axis=1), jnp.concatenate([here, after], axis=1)], axis=0
    )
    waves = exact(stacked, forward)
    real, imag = waves[:, :half], waves[:, half:]
    kr = jnp.concatenate([spec[:, :half]] * 2, axis=0)
    ki = jnp.concatenate([spec[:, half:]] * 2, axis=0)
    turned = jnp.concatenate([real * kr - imag * ki, real * ki + imag * kr], axis=1)
    out = exact(turned, inverse_last)
    return out[:rows], out[rows:]


def advanced(here, after, spec, forward, inverse_first):
    half = here.shape[1]
    waves = exact(jnp.concatenate([here, after], axis=1), forward)
    real, imag = waves[:, :half], waves[:, half:]
    kr, ki = spec[:, :half], spec[:, half:]
    turned = jnp.concatenate([real * kr + imag * ki, imag * kr - real * ki], axis=1)
    return exact(turned, inverse_first)


def lanes(a, b):
    return jnp.sum(a * b, axis=0, keepdims=True)


def total(ref, row):
    return jnp.sum(ref[row : row + 1, :], axis=1, keepdims=True)


def ratios(ref):
    square = total(ref, 0)
    alpha = jnp.sqrt(square)
    beta = jnp.sqrt(jnp.maximum(total(ref, 1) / square - 2.0 * total(ref, 2) + square, 0.0))
    return alpha, beta


def first_kernel(
    more_ref, sums_ref, observed_ref, spec_ref, forward_ref, first_ref, last_ref, out_ref, note_ref
):
    rows, half = observed_ref.shape[0] // 2, observed_ref.shape[1]
    spec, forward = spec_ref[...], forward_ref[...]
    before, here, after = (sums_ref[pl.ds(i * rows, rows), :] for i in range(3))
    now, later = delayed(before, here, after, spec, forward, last_ref[...])
    start = observed_ref[pl.ds(0, rows), :] - now
    start_later = (observed_ref[pl.ds(rows, rows), :] - later) * more_ref[0]
    out_ref[...] = advanced(start, start_later, spec, forward, first_ref[...])
    note_ref[...] = jnp.concatenate([lanes(start, start), jnp.zeros((7, half), F32)], axis=0)


def first_step(more, sums, observed, spec, mats):
    rows, half = spec.shape[0], observed.shape[1]
    return pl.pallas_call(
        first_kernel,
        in_specs=[pl.BlockSpec(memory_space=pltpu.SMEM)] + [pl.BlockSpec(memory_space=pltpu.VMEM)] * 6,
        out_shape=[jax.ShapeDtypeStruct((rows, half), F32), jax.ShapeDtypeStruct((8, half), F32)],
        compiler_params=params(),
        name="first_step",
    )(more, sums, observed, spec, *mats)


def step_kernel(
    opening,
    final,
    more_ref,
    note_ref,
    sums_ref,
    spec_ref,
    forward_ref,
    first_ref,
    last_ref,
    pulled_ref,
    *refs,
):
    if opening:
        state_ref = None
    else:
        state_ref, *refs = refs
    if final:
        (out_note_ref,) = refs
    else:
        new_ref, out_ref, out_note_ref = refs
    rows, half = pulled_ref.shape
    spec, forward = spec_ref[...], forward_ref[...]
    if opening:
        scale = 1.0 / jnp.sqrt(total(note_ref, 0))
        along = sums_ref[...] * scale
        new_s, new_su = along, along
        new_zu = pulled_ref[...] * scale
        new_z = new_zu
    else:
        alpha, beta = ratios(note_ref)
        a, b, g = 1.0 / (alpha * beta), alpha / beta, beta / alpha
        wide = pl.ds(0, 3 * rows), pl.ds(3 * rows, 3 * rows)
        new_su = sums_ref[...] * a - state_ref[wide[1], :] * b
        new_s = new_su - state_ref[wide[0], :] * g
        new_zu = pulled_ref[...] * a - state_ref[pl.ds(7 * rows, rows), :] * b
        new_z = new_zu - state_ref[pl.ds(6 * rows, rows), :] * g
    before, here, after = (new_s[i * rows : (i + 1) * rows] for i in range(3))
    now, later = delayed(before, here, after, spec, forward, last_ref[...])
    out_note_ref[...] = jnp.concatenate(
        [lanes(new_z, here), lanes(now, now), lanes(new_zu, here), jnp.zeros((5, half), F32)], axis=0
    )
    if not final:
        new_ref[pl.ds(0, 3 * rows), :] = new_s
        new_ref[pl.ds(3 * rows, 3 * rows), :] = new_su
        new_ref[pl.ds(6 * rows, rows), :] = new_z
        new_ref[pl.ds(7 * rows, rows), :] = new_zu
        out_ref[...] = advanced(now, later * more_ref[0], spec, forward, first_ref[...])


def next_step(more, note, sums, spec, mats, pulled, state, final):
    rows, half = pulled.shape
    opening = state is None
    shapes = [
        jax.ShapeDtypeStruct((8 * rows, half), F32),
        jax.ShapeDtypeStruct((rows, half), F32),
        jax.ShapeDtypeStruct((8, half), F32),
    ]
    args = [more, note, sums, spec, *mats, pulled] + ([] if opening else [state])
    return pl.pallas_call(
        functools.partial(step_kernel, opening, final),
        in_specs=[pl.BlockSpec(memory_space=pltpu.SMEM)]
        + [pl.BlockSpec(memory_space=pltpu.VMEM)] * (len(args) - 1),
        out_shape=shapes[2:] if final else shapes,
        compiler_params=params(),
        name="next_step",
    )(*args)


def weights_of(notes):
    start = jnp.sqrt(total(notes[0], 0))
    zero = jnp.zeros_like(start)
    units = [1.0 / start, zero, zero]
    z, zu = list(units), list(units)
    phibar = start
    alpha, beta = ratios(notes[1])
    rhobar = alpha
    w = [value / alpha for value in z]
    result = [zero] * 3
    steps = len(notes) - 1
    for k in range(steps):
        rho = jnp.sqrt(rhobar * rhobar + beta * beta)
        cosine, sine = rhobar / rho, beta / rho
        phi, phibar = cosine * phibar, sine * phibar
        result = [r + phi / rho * value for r, value in zip(result, w)]
        if k < steps - 1:
            a, b, g = 1.0 / (alpha * beta), alpha / beta, beta / alpha
            zu = [(a if i == k + 1 else 0.0) - b * value for i, value in enumerate(zu)]
            z = [value - g * old for value, old in zip(zu, z)]
            alpha, beta = ratios(notes[k + 2])
            theta = sine * alpha
            rhobar = -cosine * alpha
            w = [value / alpha - theta / rho * old for value, old in zip(z, w)]
    return result


def finish_kernel(n0, n1, n2, n3, gauge_ref, q0, q1, q2, inc_ref, field_ref, out_ref, rows_ref):
    blocks, slots, width = inc_ref.shape
    count = rows_ref.shape[0]
    gauges = q0.shape[0]
    step = pl.program_id(0)

    @pl.when(step == 0)
    def _():
        e0, e1, e2 = weights_of([n0, n1, n2, n3])
        width_ = 512

        def body(i, value):
            here = pl.ds(pl.multiple_of(i * width_, width_), width_)
            mixed = q0[here, :] * e0 + q1[here, :] * e1 + q2[here, :] * e2
            gauge = lax.broadcasted_iota(jnp.int32, (count, width_), 1) + i * width_
            hot = jnp.where(gauge_ref[...] == gauge, 1.0, 0.0).astype(BF16)
            return value + pick(hot, mixed)

        rows_ref[...] = lax.fori_loop(0, gauges // width_, body, jnp.zeros(rows_ref.shape, F32))

    weights = inc_ref[...].astype(F32).astype(BF16)
    for b in range(blocks):
        here = pl.ds(b * width, width)
        rows = rows_ref[pl.ds(pl.multiple_of((step * blocks + b) * slots, slots), slots), :]
        added = sum(
            lax.dot_general(weights[b], piece, (((0,), (0,)), ((), ())), preferred_element_type=F32)
            for piece in pieces(rows, 3)
        )
        out_ref[here, :] = field_ref[here, :] + added


def finish(notes, row_gauge, gathered, incidence, field):
    blocks, slots, width = incidence.shape
    hours = field.shape[1]
    count = row_gauge.shape[0]
    step = 8
    whole = lambda shape: pl.BlockSpec(shape, lambda i: (0, 0))
    return pl.pallas_call(
        finish_kernel,
        grid=(blocks // step,),
        in_specs=[whole(n.shape) for n in notes]
        + [whole((count, 1))]
        + [whole(q.shape) for q in gathered]
        + [
            pl.BlockSpec((step, slots, width), lambda i: (i, 0, 0)),
            pl.BlockSpec((step * width, hours), lambda i: (i, 0)),
        ],
        out_specs=pl.BlockSpec((step * width, hours), lambda i: (i, 0)),
        out_shape=jax.ShapeDtypeStruct(field.shape, F32),
        scratch_shapes=[pltpu.VMEM((count, hours), F32)],
        compiler_params=params(),
        name="finish",
    )(*notes, row_gauge.reshape(count, 1), *gathered, incidence, field)


def shifted(value, axis, by):
    devices = lax.axis_size(axis)
    pairs = [(i, i + by) for i in range(devices) if 0 <= i + by < devices]
    return lax.ppermute(value, axis, pairs)


def window(value):
    return jnp.concatenate([shifted(value, "tm", 1), value, shifted(value, "tm", -1)], axis=0)


def gathered_rows(value):
    owners = lax.axis_size("basin")
    copies = jnp.broadcast_to(value[None], (owners,) + value.shape)
    return lax.all_to_all(copies, "basin", 0, 0, tiled=False)


def over_hours(note):
    blocks = lax.axis_size("tm")
    result = note
    for by in range(1, blocks):
        result = result + lax.ppermute(note, "tm", [(i, (i + by) % blocks) for i in range(blocks)])
    return result


def shards(incidence, row_gauge, gauge_kernel, kernels, observed, first_guess):
    owners = lax.axis_size("basin")
    rows, hours = observed.shape
    gauges = rows * owners
    mats = transforms()
    spec = spectrum(gauge_kernel, kernels, mats[0])
    more = (lax.axis_index("tm") < lax.axis_size("tm") - 1).astype(F32).reshape(1)
    partial, gram = prepare(incidence, first_guess)
    all_gram = lax.all_gather(gram, "basin", axis=1, tiled=True)
    all_rows = lax.all_gather(row_gauge, "basin", axis=0, tiled=True)
    dense = table(row_gauge, partial, gauges).reshape(owners, rows, hours)
    sums = jnp.sum(lax.all_to_all(dense, "basin", 0, 0, tiled=False), axis=0)
    both = jnp.concatenate([observed, shifted(observed, "tm", -1)], axis=0)
    first = (lax.axis_index("basin") * rows).astype(jnp.int32).reshape(1)
    high, low = couple(first, all_rows, all_gram, rows, gauges)

    pulled, note = first_step(more, window(sums), both, spec, mats)
    notes, kept, state = [], [], None
    for k in range(3):
        everyone = gathered_rows(jnp.concatenate([pulled, note], axis=0))
        value = everyone[:, :rows].reshape(gauges, hours)
        notes.append(over_hours(jnp.sum(everyone[:, rows:], axis=0)))
        kept.append(value)
        around = window(mix(high, low, value))
        final = k == 2
        result = next_step(more, notes[-1], around, spec, mats, pulled, state, final)
        if final:
            (note,) = result
        else:
            state, pulled, note = result
    notes.append(over_hours(jnp.sum(gathered_rows(note), axis=0)))
    return finish(notes, row_gauge, kept, incidence, first_guess)


def solution(mesh):
    in_specs = (
        P("basin", None, None),
        P("basin"),
        P("basin"),
        P(),
        P("basin", "tm"),
        P("basin", "tm"),
    )
    return jax.shard_map(
        shards, mesh=mesh, in_specs=in_specs, out_specs=P("basin", "tm"), check_vma=False
    )
```

```python
import functools

import jax
import jax.numpy as jnp
import numpy as np
from jax import lax
from jax.experimental import pallas as pl
from jax.experimental.pallas import tpu as pltpu
from jax.sharding import PartitionSpec as P

F32 = jnp.float32
BF16 = jnp.bfloat16
HIGH = lax.Precision.HIGHEST
SPAN = 256
VMEM_BYTES = 56 * 1024 * 1024


def params():
    return pltpu.CompilerParams(vmem_limit_bytes=VMEM_BYTES)


def transforms():
    half = SPAN // 2
    freq = 2.0 * np.pi * (np.arange(half) + 0.5) / SPAN
    phase = np.arange(SPAN)[:, None] * freq[None, :]
    forward = np.concatenate([np.cos(phase), -np.sin(phase)], axis=1)
    inverse = forward.T * (2.0 / SPAN)
    return (
        jnp.asarray(forward, F32),
        jnp.asarray(inverse[:, :half], F32),
        jnp.asarray(inverse[:, half:], F32),
    )


def dot(a, b):
    return jnp.dot(a, b, preferred_element_type=F32)


def exact(a, b):
    return jnp.dot(a, b, precision=HIGH, preferred_element_type=F32)


def pieces(value, count):
    out = []
    for _ in range(count):
        piece = value.astype(BF16)
        out.append(piece)
        value = value - piece.astype(F32)
    return out


def pick(hot, value):
    return sum(dot(hot, piece) for piece in pieces(value, 3))


def prepare_kernel(inc_ref, field_ref, partial_ref, gram_ref):
    blocks, slots, width = inc_ref.shape
    rows = blocks * slots
    weights = inc_ref[...].astype(F32).astype(BF16)
    for b in range(blocks):
        value = field_ref[pl.ds(b * width, width), :]
        partial_ref[pl.ds(b * slots, slots), :] = pick(weights[b], value)
    flat = weights.reshape(rows, width)
    full = lax.dot_general(flat, flat, (((1,), (1,)), ((), ())), preferred_element_type=F32)
    row = lax.broadcasted_iota(jnp.int32, (rows, rows), 0)
    col = lax.broadcasted_iota(jnp.int32, (rows, rows), 1)
    own = jnp.where(row // slots == col // slots, full, 0.0)
    gram_ref[...] = jnp.sum(own.reshape(blocks, slots, rows), axis=0)


def prepare(incidence, field):
    blocks, slots, width = incidence.shape
    hours = field.shape[1]
    step = 8
    return pl.pallas_call(
        prepare_kernel,
        grid=(blocks // step,),
        in_specs=[
            pl.BlockSpec((step, slots, width), lambda i: (i, 0, 0)),
            pl.BlockSpec((step * width, hours), lambda i: (i, 0)),
        ],
        out_specs=[
            pl.BlockSpec((step * slots, hours), lambda i: (i, 0)),
            pl.BlockSpec((slots, step * slots), lambda i: (0, i)),
        ],
        out_shape=[
            jax.ShapeDtypeStruct((blocks * slots, hours), F32),
            jax.ShapeDtypeStruct((slots, blocks * slots), F32),
        ],
        compiler_params=params(),
        name="prepare",
    )(incidence, field)


def table_kernel(gauge_ref, partial_ref, out_ref):
    slots = partial_ref.shape[0]
    rows = out_ref.shape[0]
    first = pl.program_id(0) * rows
    gauge = lax.broadcasted_iota(jnp.int32, (rows, slots), 0) + first
    hot = jnp.where(gauge_ref[...] == gauge, 1.0, 0.0).astype(BF16)
    out_ref[...] = pick(hot, partial_ref[...])


def table(row_gauge, partial, gauges):
    slots, hours = partial.shape
    step = 256
    return pl.pallas_call(
        table_kernel,
        grid=(gauges // step,),
        in_specs=[
            pl.BlockSpec((1, slots), lambda i: (0, 0)),
            pl.BlockSpec((slots, hours), lambda i: (0, 0)),
        ],
        out_specs=pl.BlockSpec((step, hours), lambda i: (i, 0)),
        out_shape=jax.ShapeDtypeStruct((gauges, hours), F32),
        compiler_params=params(),
        name="table",
    )(row_gauge.reshape(1, slots), partial)


def couple_kernel(first_ref, lane_ref, sub_ref, gram_ref, high_ref, low_ref, near_ref):
    slots = gram_ref.shape[0]
    count = lane_ref.shape[1]
    rows, cols = high_ref.shape
    tile = 256
    first = first_ref[0]

    @pl.when(pl.program_id(0) == 0)
    def _():
        row = lax.broadcasted_iota(jnp.int32, (tile, tile), 0)
        col = lax.broadcasted_iota(jnp.int32, (tile, tile), 1)
        same = row // slots == col // slots
        mine = lax.broadcasted_iota(jnp.int32, (rows, tile), 0) + first

        def body(i, carry):
            here = pl.ds(pl.multiple_of(i * tile, tile), tile)
            block = jnp.concatenate([gram_ref[:, here]] * (tile // slots), axis=0)
            block = jnp.where(same, block, 0.0).astype(BF16)
            hot = jnp.where(lane_ref[:, here] == mine, 1.0, 0.0).astype(BF16)
            near_ref[:, here] = dot(hot, block)
            return carry

        lax.fori_loop(0, count // tile, body, 0)

    def chunk(i, total):
        here = pl.ds(pl.multiple_of(i * 1024, 1024), 1024)
        gauge = lax.broadcasted_iota(jnp.int32, (1024, cols), 1) + pl.program_id(0) * cols
        hot = jnp.where(sub_ref[here, :] == gauge, 1.0, 0.0).astype(BF16)
        near = near_ref[:, here]
        high = near.astype(BF16)
        low = (near - high.astype(F32)).astype(BF16)
        return total + dot(high, hot) + dot(low, hot)

    total = lax.fori_loop(0, count // 1024, chunk, jnp.zeros((rows, cols), F32))
    high, low = pieces(total, 2)
    high_ref[...] = high
    low_ref[...] = low


def couple(first, row_gauge, gram, rows, gauges):
    count = row_gauge.shape[0]
    step = 256
    return pl.pallas_call(
        couple_kernel,
        grid=(gauges // step,),
        in_specs=[
            pl.BlockSpec(memory_space=pltpu.SMEM),
            pl.BlockSpec((1, count), lambda i: (0, 0)),
            pl.BlockSpec((count, 1), lambda i: (0, 0)),
            pl.BlockSpec(gram.shape, lambda i: (0, 0)),
        ],
        out_specs=[pl.BlockSpec((rows, step), lambda i: (0, i))] * 2,
        out_shape=[jax.ShapeDtypeStruct((rows, gauges), BF16)] * 2,
        scratch_shapes=[pltpu.VMEM((rows, count), F32)],
        compiler_params=params(),
        name="couple",
    )(first, row_gauge.reshape(1, count), row_gauge.reshape(count, 1), gram)


def mix_kernel(high_ref, low_ref, value_ref, out_ref):
    high = high_ref[...]
    low = low_ref[...]
    one, two, three = pieces(value_ref[...], 3)
    out_ref[...] = (dot(high, three) + dot(low, two)) + (dot(high, two) + dot(low, one)) + dot(high, one)


def mix(high, low, value):
    return pl.pallas_call(
        mix_kernel,
        out_shape=jax.ShapeDtypeStruct((high.shape[0], value.shape[1]), F32),
        compiler_params=params(),
        name="mix",
    )(high, low, value)


def spectrum_kernel(class_ref, kernels_ref, forward_ref, out_ref):
    rows = class_ref.shape[0]
    classes, taps = kernels_ref.shape
    kind = lax.broadcasted_iota(jnp.int32, (rows, classes), 1)
    hot = jnp.where(class_ref[...] == kind, 1.0, 0.0)
    out_ref[...] = exact(exact(hot, kernels_ref[...]), forward_ref[pl.ds(0, taps), :])


def spectrum(gauge_kernel, kernels, forward):
    rows = gauge_kernel.shape[0]
    return pl.pallas_call(
        spectrum_kernel,
        out_shape=jax.ShapeDtypeStruct((rows, SPAN), F32),
        compiler_params=params(),
        name="spectrum",
    )(gauge_kernel.reshape(rows, 1), kernels, forward)


def delayed(before, here, after, spec, forward, inverse_last):
    rows, half = here.shape
    stacked = jnp.concatenate(
        [jnp.concatenate([before, here], axis=1), jnp.concatenate([here, after], axis=1)], axis=0
    )
    waves = exact(stacked, forward)
    real, imag = waves[:, :half], waves[:, half:]
    kr = jnp.concatenate([spec[:, :half]] * 2, axis=0)
    ki = jnp.concatenate([spec[:, half:]] * 2, axis=0)
    turned = jnp.concatenate([real * kr - imag * ki, real * ki + imag * kr], axis=1)
    out = exact(turned, inverse_last)
    return out[:rows], out[rows:]


def advanced(here, after, spec, forward, inverse_first):
    half = here.shape[1]
    waves = exact(jnp.concatenate([here, after], axis=1), forward)
    real, imag = waves[:, :half], waves[:, half:]
    kr, ki = spec[:, :half], spec[:, half:]
    turned = jnp.concatenate([real * kr + imag * ki, imag * kr - real * ki], axis=1)
    return exact(turned, inverse_first)


def lanes(a, b):
    return jnp.sum(a * b, axis=0, keepdims=True)


def total(ref, row):
    return jnp.sum(ref[row : row + 1, :], axis=1, keepdims=True)


def ratios(ref):
    square = total(ref, 0)
    alpha = jnp.sqrt(square)
    beta = jnp.sqrt(jnp.maximum(total(ref, 1) / square - 2.0 * total(ref, 2) + square, 0.0))
    return alpha, beta


def first_kernel(
    more_ref, sums_ref, observed_ref, spec_ref, forward_ref, first_ref, last_ref, out_ref, note_ref
):
    rows, half = observed_ref.shape[0] // 2, observed_ref.shape[1]
    spec, forward = spec_ref[...], forward_ref[...]
    before, here, after = (sums_ref[pl.ds(i * rows, rows), :] for i in range(3))
    now, later = delayed(before, here, after, spec, forward, last_ref[...])
    start = observed_ref[pl.ds(0, rows), :] - now
    start_later = (observed_ref[pl.ds(rows, rows), :] - later) * more_ref[0]
    out_ref[...] = advanced(start, start_later, spec, forward, first_ref[...])
    note_ref[...] = jnp.concatenate([lanes(start, start), jnp.zeros((7, half), F32)], axis=0)


def first_step(more, sums, observed, spec, mats):
    rows, half = spec.shape[0], observed.shape[1]
    return pl.pallas_call(
        first_kernel,
        in_specs=[pl.BlockSpec(memory_space=pltpu.SMEM)] + [pl.BlockSpec(memory_space=pltpu.VMEM)] * 6,
        out_shape=[jax.ShapeDtypeStruct((rows, half), F32), jax.ShapeDtypeStruct((8, half), F32)],
        compiler_params=params(),
        name="first_step",
    )(more, sums, observed, spec, *mats)


def step_kernel(
    opening,
    final,
    more_ref,
    note_ref,
    sums_ref,
    spec_ref,
    forward_ref,
    first_ref,
    last_ref,
    pulled_ref,
    *refs,
):
    if opening:
        state_ref = None
    else:
        state_ref, *refs = refs
    if final:
        (out_note_ref,) = refs
    else:
        new_ref, out_ref, out_note_ref = refs
    rows, half = pulled_ref.shape
    spec, forward = spec_ref[...], forward_ref[...]
    if opening:
        scale = 1.0 / jnp.sqrt(total(note_ref, 0))
        along = sums_ref[...] * scale
        new_s, new_su = along, along
        new_zu = pulled_ref[...] * scale
        new_z = new_zu
    else:
        alpha, beta = ratios(note_ref)
        a, b, g = 1.0 / (alpha * beta), alpha / beta, beta / alpha
        wide = pl.ds(0, 3 * rows), pl.ds(3 * rows, 3 * rows)
        new_su = sums_ref[...] * a - state_ref[wide[1], :] * b
        new_s = new_su - state_ref[wide[0], :] * g
        new_zu = pulled_ref[...] * a - state_ref[pl.ds(7 * rows, rows), :] * b
        new_z = new_zu - state_ref[pl.ds(6 * rows, rows), :] * g
    before, here, after = (new_s[i * rows : (i + 1) * rows] for i in range(3))
    now, later = delayed(before, here, after, spec, forward, last_ref[...])
    out_note_ref[...] = jnp.concatenate(
        [lanes(new_z, here), lanes(now, now), lanes(new_zu, here), jnp.zeros((5, half), F32)], axis=0
    )
    if not final:
        new_ref[pl.ds(0, 3 * rows), :] = new_s
        new_ref[pl.ds(3 * rows, 3 * rows), :] = new_su
        new_ref[pl.ds(6 * rows, rows), :] = new_z
        new_ref[pl.ds(7 * rows, rows), :] = new_zu
        out_ref[...] = advanced(now, later * more_ref[0], spec, forward, first_ref[...])


def next_step(more, note, sums, spec, mats, pulled, state, final):
    rows, half = pulled.shape
    opening = state is None
    shapes = [
        jax.ShapeDtypeStruct((8 * rows, half), F32),
        jax.ShapeDtypeStruct((rows, half), F32),
        jax.ShapeDtypeStruct((8, half), F32),
    ]
    args = [more, note, sums, spec, *mats, pulled] + ([] if opening else [state])
    return pl.pallas_call(
        functools.partial(step_kernel, opening, final),
        in_specs=[pl.BlockSpec(memory_space=pltpu.SMEM)]
        + [pl.BlockSpec(memory_space=pltpu.VMEM)] * (len(args) - 1),
        out_shape=shapes[2:] if final else shapes,
        compiler_params=params(),
        name="next_step",
    )(*args)


def weights_of(notes):
    start = jnp.sqrt(total(notes[0], 0))
    zero = jnp.zeros_like(start)
    units = [1.0 / start, zero, zero]
    z, zu = list(units), list(units)
    phibar = start
    alpha, beta = ratios(notes[1])
    rhobar = alpha
    w = [value / alpha for value in z]
    result = [zero] * 3
    steps = len(notes) - 1
    for k in range(steps):
        rho = jnp.sqrt(rhobar * rhobar + beta * beta)
        cosine, sine = rhobar / rho, beta / rho
        phi, phibar = cosine * phibar, sine * phibar
        result = [r + phi / rho * value for r, value in zip(result, w)]
        if k < steps - 1:
            a, b, g = 1.0 / (alpha * beta), alpha / beta, beta / alpha
            zu = [(a if i == k + 1 else 0.0) - b * value for i, value in enumerate(zu)]
            z = [value - g * old for value, old in zip(zu, z)]
            alpha, beta = ratios(notes[k + 2])
            theta = sine * alpha
            rhobar = -cosine * alpha
            w = [value / alpha - theta / rho * old for value, old in zip(z, w)]
    return result


def finish_kernel(n0, n1, n2, n3, gauge_ref, q0, q1, q2, inc_ref, field_ref, out_ref, rows_ref):
    blocks, slots, width = inc_ref.shape
    count = rows_ref.shape[0]
    gauges = q0.shape[0]
    step = pl.program_id(0)

    @pl.when(step == 0)
    def _():
        e0, e1, e2 = weights_of([n0, n1, n2, n3])
        width_ = 512

        def body(i, value):
            here = pl.ds(pl.multiple_of(i * width_, width_), width_)
            mixed = q0[here, :] * e0 + q1[here, :] * e1 + q2[here, :] * e2
            gauge = lax.broadcasted_iota(jnp.int32, (count, width_), 1) + i * width_
            hot = jnp.where(gauge_ref[...] == gauge, 1.0, 0.0).astype(BF16)
            return value + pick(hot, mixed)

        rows_ref[...] = lax.fori_loop(0, gauges // width_, body, jnp.zeros(rows_ref.shape, F32))

    weights = inc_ref[...].astype(F32).astype(BF16)
    for b in range(blocks):
        here = pl.ds(b * width, width)
        rows = rows_ref[pl.ds(pl.multiple_of((step * blocks + b) * slots, slots), slots), :]
        added = sum(
            lax.dot_general(weights[b], piece, (((0,), (0,)), ((), ())), preferred_element_type=F32)
            for piece in pieces(rows, 3)
        )
        out_ref[here, :] = field_ref[here, :] + added


def finish(notes, row_gauge, gathered, incidence, field):
    blocks, slots, width = incidence.shape
    hours = field.shape[1]
    count = row_gauge.shape[0]
    step = 8
    whole = lambda shape: pl.BlockSpec(shape, lambda i: (0, 0))
    return pl.pallas_call(
        finish_kernel,
        grid=(blocks // step,),
        in_specs=[whole(n.shape) for n in notes]
        + [whole((count, 1))]
        + [whole(q.shape) for q in gathered]
        + [
            pl.BlockSpec((step, slots, width), lambda i: (i, 0, 0)),
            pl.BlockSpec((step * width, hours), lambda i: (i, 0)),
        ],
        out_specs=pl.BlockSpec((step * width, hours), lambda i: (i, 0)),
        out_shape=jax.ShapeDtypeStruct(field.shape, F32),
        scratch_shapes=[pltpu.VMEM((count, hours), F32)],
        compiler_params=params(),
        name="finish",
    )(*notes, row_gauge.reshape(count, 1), *gathered, incidence, field)


def shifted(value, axis, by):
    devices = lax.axis_size(axis)
    pairs = [(i, i + by) for i in range(devices) if 0 <= i + by < devices]
    return lax.ppermute(value, axis, pairs)


def window(value):
    return jnp.concatenate([shifted(value, "tm", 1), value, shifted(value, "tm", -1)], axis=0)


def gathered_rows(value):
    owners = lax.axis_size("basin")
    copies = jnp.broadcast_to(value[None], (owners,) + value.shape)
    return lax.all_to_all(copies, "basin", 0, 0, tiled=False)


def over_hours(note):
    blocks = lax.axis_size("tm")
    result = note
    for by in range(1, blocks):
        result = result + lax.ppermute(note, "tm", [(i, (i + by) % blocks) for i in range(blocks)])
    return result


def shards(incidence, row_gauge, gauge_kernel, kernels, observed, first_guess):
    owners = lax.axis_size("basin")
    rows, hours = observed.shape
    gauges = rows * owners
    mats = transforms()
    spec = spectrum(gauge_kernel, kernels, mats[0])
    more = (lax.axis_index("tm") < lax.axis_size("tm") - 1).astype(F32).reshape(1)
    partial, gram = prepare(incidence, first_guess)
    all_gram = lax.all_gather(gram, "basin", axis=1, tiled=True)
    all_rows = lax.all_gather(row_gauge, "basin", axis=0, tiled=True)
    dense = table(row_gauge, partial, gauges).reshape(owners, rows, hours)
    sums = jnp.sum(lax.all_to_all(dense, "basin", 0, 0, tiled=False), axis=0)
    both = jnp.concatenate([observed, shifted(observed, "tm", -1)], axis=0)
    first = (lax.axis_index("basin") * rows).astype(jnp.int32).reshape(1)
    high, low = couple(first, all_rows, all_gram, rows, gauges)

    pulled, note = first_step(more, window(sums), both, spec, mats)
    notes, kept, state = [], [], None
    for k in range(3):
        everyone = gathered_rows(jnp.concatenate([pulled, note], axis=0))
        value = everyone[:, :rows].reshape(gauges, hours)
        notes.append(over_hours(jnp.sum(everyone[:, rows:], axis=0)))
        kept.append(value)
        around = window(mix(high, low, value))
        final = k == 2
        result = next_step(more, notes[-1], around, spec, mats, pulled, state, final)
        if final:
            (note,) = result
        else:
            state, pulled, note = result
    notes.append(over_hours(jnp.sum(gathered_rows(note), axis=0)))
    return finish(notes, row_gauge, kept, incidence, first_guess)


Z_, X_, Y_, C_ = 4, 2, 2, 2
NOTE = 8


def device(z, x, y, c):
    return (z * X_ + x) * (Y_ * C_) + y * C_ + c


def moved(value, where):
    pairs = []
    for z, x, y, c in np.ndindex(Z_, X_, Y_, C_):
        target = where(z, x, y, c)
        if target is not None:
            pairs.append((device(z, x, y, c), device(*target)))
    return lax.ppermute(value, ("basin", "tm"), pairs)


def to_plane(z, x, y, c):
    return 2 * y + c, x, z & 1, z >> 1


def to_plane_before(z, x, y, c):
    t = 2 * y + c
    return (t - 1, x, z & 1, z >> 1) if t else None


def from_plane(z, x, y, c):
    return 2 * c + y, x, z >> 1, z & 1


def over_x(z, x, y, c):
    return z, 1 - x, y, c


def over_y(z, x, y, c):
    return z, x, 1 - y, c


def over_xy(z, x, y, c):
    return z, 1 - x, 1 - y, c


def over_core(z, x, y, c):
    return z, x, y, 1 - c


def z_pair(z, x, y, c):
    return z ^ 1, x, y, c


def z_middle(z, x, y, c):
    return (3 - z, x, y, c) if z in (1, 2) else None


def z_two(z, x, y, c):
    return z ^ 2, x, y, c


def z_mirror(z, x, y, c):
    return 3 - z, x, y, c


SQUARE = (over_x, over_y, over_xy)


def split_constant(value):
    out = []
    for _ in range(3):
        piece = value.astype(jnp.bfloat16)
        out.append(jnp.asarray(piece))
        value = value - piece.astype(np.float64)
    return out


def turned_transforms():
    half = SPAN // 2
    freq = 2.0 * np.pi * (np.arange(half) + 0.5) / SPAN
    phase = freq[:, None] * np.arange(SPAN)[None, :]
    forward = np.concatenate([np.cos(phase), -np.sin(phase)], axis=0)
    inverse = forward.T * (2.0 / SPAN)
    return split_constant(forward), split_constant(inverse[:half]), split_constant(inverse[half:])


def product(mats, value, order):
    parts = pieces(value, order)
    result = None
    for level in reversed(range(order)):
        for i in range(level + 1):
            term = dot(mats[i][...], parts[level - i])
            result = term if result is None else result + term
    return result


def turn(waves, spec, sign):
    half = waves.shape[0] // 2
    real, imag = waves[:half], waves[half:]
    kr, ki = spec[:half], spec[half:] * sign
    return jnp.concatenate([real * kr - imag * ki, real * ki + imag * kr], axis=0)


def plane_delayed(before, here, after, spec, forward, last, order):
    out = []
    for pair in ((before, here), (here, after)):
        waves = product(forward, jnp.concatenate(pair, axis=0), order)
        out.append(product(last, turn(waves, spec, 1.0), order))
    return out


def plane_advanced(here, after, spec, forward, first, order):
    waves = product(forward, jnp.concatenate([here, after], axis=0), order)
    return product(first, turn(waves, spec, -1.0), order)


def send_kernel(inc_ref, field_ref, gauge_ref, out_ref):
    blocks, slots, width = inc_ref.shape
    rows = blocks * slots
    hours = field_ref.shape[1]
    weights = inc_ref[...].astype(F32).astype(BF16)
    parts = []
    for b in range(blocks):
        parts.append(pick(weights[b], field_ref[pl.ds(b * width, width), :]))
    out_ref[pl.ds(0, hours), :] = jnp.transpose(jnp.concatenate(parts, axis=0))
    flat = weights.reshape(rows, width)
    full = lax.dot_general(flat, flat, (((1,), (1,)), ((), ())), preferred_element_type=F32)
    row = lax.broadcasted_iota(jnp.int32, (rows, rows), 0)
    col = lax.broadcasted_iota(jnp.int32, (rows, rows), 1)
    own = jnp.where(row // slots == col // slots, full, 0.0)
    out_ref[pl.ds(hours, slots), :] = jnp.sum(own.reshape(blocks, slots, rows), axis=0)
    out_ref[pl.ds(hours + slots, 8), :] = jnp.broadcast_to(gauge_ref[...].astype(F32), (8, rows))


def send(incidence, field, row_gauge):
    blocks, slots, width = incidence.shape
    hours = field.shape[1]
    step = 8
    height = hours + slots + 8
    return pl.pallas_call(
        send_kernel,
        grid=(blocks // step,),
        in_specs=[
            pl.BlockSpec((step, slots, width), lambda i: (i, 0, 0)),
            pl.BlockSpec((step * width, hours), lambda i: (i, 0)),
            pl.BlockSpec((1, step * slots), lambda i: (0, i)),
        ],
        out_specs=pl.BlockSpec((height, step * slots), lambda i: (0, i)),
        out_shape=jax.ShapeDtypeStruct((height, blocks * slots), F32),
        compiler_params=params(),
        name="send",
    )(incidence, field, row_gauge.reshape(1, blocks * slots))


def hot_rows(gauge, first, rows):
    mine = (lax.broadcasted_iota(jnp.int32, (rows, gauge.shape[1]), 0) + first).astype(F32)
    return jnp.where(gauge == mine, 1.0, 0.0).astype(BF16)


def spread_kernel(first_ref, mine_ref, other_ref, *out_refs):
    hours, rows = out_refs[0].shape
    slots = mine_ref.shape[0] - hours - 8
    where = hours + slots
    for m, out_ref in enumerate(out_refs):
        result = None
        for ref in (mine_ref, other_ref):
            hot = hot_rows(ref[where : where + 1, :], first_ref[m], rows)
            for piece in reversed(pieces(ref[pl.ds(0, hours), :], 3)):
                term = lax.dot_general(
                    piece, hot, (((1,), (1,)), ((), ())), preferred_element_type=F32
                )
                result = term if result is None else result + term
        out_ref[...] = result


def spread(first, mine, other, hours, rows):
    return pl.pallas_call(
        spread_kernel,
        in_specs=[pl.BlockSpec(memory_space=pltpu.SMEM)] + [pl.BlockSpec(memory_space=pltpu.VMEM)] * 2,
        out_shape=[jax.ShapeDtypeStruct((hours, rows), F32)] * 4,
        compiler_params=params(),
        name="spread",
    )(first, mine, other)


def plane_couple_kernel(first_ref, a_ref, b_ref, c_ref, d_ref, high_ref, low_ref, total_ref, meta_ref):
    height, double = a_ref.shape
    slots = height - 8
    count = double // 2
    cols, rows = high_ref.shape
    part = cols // 4
    tile = 256
    for i, ref in enumerate((a_ref, b_ref, c_ref, d_ref)):
        for j in range(2):
            meta_ref[2 * i + j] = ref[:, j * count : (j + 1) * count]
    row = lax.broadcasted_iota(jnp.int32, (tile, tile), 0)
    col = lax.broadcasted_iota(jnp.int32, (tile, tile), 1)
    same = row // slots == col // slots
    total_ref[...] = jnp.zeros_like(total_ref)

    def body(i, carry):
        gauge = meta_ref[i, slots : slots + 1, :]
        near = []
        for j in range(count // tile):
            here = slice(j * tile, (j + 1) * tile)
            block = jnp.concatenate([meta_ref[i, :slots, here]] * (tile // slots), axis=0)
            block = jnp.where(same, block, 0.0).astype(BF16)
            mine = jnp.concatenate(
                [hot_rows(gauge[:, here], first_ref[4 + h], rows // 2) for h in range(2)], axis=0
            )
            near.append(
                lax.dot_general(block, mine, (((1,), (1,)), ((), ())), preferred_element_type=F32)
            )
        near = jnp.concatenate(near, axis=0)
        high = near.astype(BF16)
        rest = near - high.astype(F32)
        hot = jnp.concatenate([hot_rows(gauge, first_ref[m], part) for m in range(4)], axis=0)
        total_ref[...] += dot(hot, high)

        @pl.when(jnp.max(jnp.abs(rest)) > 0.0)
        def _():
            total_ref[...] += dot(hot, rest.astype(BF16))

        return carry

    lax.fori_loop(0, 8, body, 0)
    high, low = pieces(total_ref[...], 2)
    high_ref[...] = high
    low_ref[...] = low


def plane_couple(first, metas, rows):
    height, double = metas[0].shape
    return pl.pallas_call(
        plane_couple_kernel,
        in_specs=[pl.BlockSpec(memory_space=pltpu.SMEM)] + [pl.BlockSpec(memory_space=pltpu.VMEM)] * 4,
        out_shape=[jax.ShapeDtypeStruct((4 * rows, 2 * rows), BF16)] * 2,
        scratch_shapes=[
            pltpu.VMEM((4 * rows, 2 * rows), F32),
            pltpu.VMEM((8, height, double // 2), F32),
        ],
        compiler_params=params(),
        name="plane_couple",
        cost_estimate=pl.CostEstimate(flops=14_000_000_000, bytes_accessed=4_000_000, transcendentals=0),
    )(first, *metas)


def plane_mix_kernel(high_ref, low_ref, a_ref, b_ref, c_ref, d_ref, mine_ref, other_ref):
    refs = (a_ref, b_ref, c_ref, d_ref)
    height, rows = a_ref.shape
    hours = height - NOTE
    value = jnp.concatenate([ref[pl.ds(0, hours), :] for ref in refs], axis=1)
    one, two = pieces(value, 2)
    high, low = high_ref[...], low_ref[...]
    result = (dot(two, high) + dot(one, low)) + dot(one, high)
    note = sum(ref[pl.ds(hours, NOTE), :] for ref in refs)
    mine_ref[pl.ds(0, hours), :] = result[:, :rows]
    other_ref[pl.ds(0, hours), :] = result[:, rows:]
    mine_ref[pl.ds(hours, NOTE), :] = note
    other_ref[pl.ds(hours, NOTE), :] = note


def plane_mix(high, low, values):
    return pl.pallas_call(
        plane_mix_kernel,
        out_shape=[jax.ShapeDtypeStruct(values[0].shape, F32)] * 2,
        compiler_params=params(),
        name="plane_mix",
    )(high, low, *values)


def plane_rows_kernel(first_ref, mine_ref, other_ref, a_ref, b_ref, c_ref, d_ref, out_mine_ref, out_other_ref):
    height, rows = a_ref.shape
    hours = height - NOTE
    where = mine_ref.shape[0] - 8
    for ref, out_ref in ((mine_ref, out_mine_ref), (other_ref, out_other_ref)):
        gauge = ref[where : where + 1, :]
        result = None
        for m, value_ref in enumerate((a_ref, b_ref, c_ref, d_ref)):
            hot = hot_rows(gauge, first_ref[m], rows)
            for piece in reversed(pieces(value_ref[pl.ds(0, hours), :], 2)):
                term = dot(piece, hot)
                result = term if result is None else result + term
        out_ref[...] = result


def plane_rows(first, mine, other, values):
    hours = values[0].shape[0] - NOTE
    slots = mine.shape[1]
    return pl.pallas_call(
        plane_rows_kernel,
        in_specs=[pl.BlockSpec(memory_space=pltpu.SMEM)] + [pl.BlockSpec(memory_space=pltpu.VMEM)] * 6,
        out_shape=[jax.ShapeDtypeStruct((hours, slots), F32)] * 2,
        compiler_params=params(),
        name="plane_rows",
        cost_estimate=pl.CostEstimate(flops=1_000_000_000, bytes_accessed=2_000_000, transcendentals=0),
    )(first, mine, other, *values)


def plane_spectrum_kernel(class_ref, kernels_ref, f0_ref, f1_ref, f2_ref, out_ref):
    classes, taps = kernels_ref.shape
    kind = jnp.concatenate([class_ref[0:1, :], class_ref[1:2, :]], axis=1)
    hot = jnp.where(
        lax.broadcasted_iota(jnp.int32, (classes, kind.shape[1]), 0).astype(F32) == kind, 1.0, 0.0
    ).astype(BF16)
    chosen = None
    for piece in reversed(pieces(jnp.transpose(kernels_ref[...]), 3)):
        term = dot(piece, hot)
        chosen = term if chosen is None else chosen + term
    mats = [ref[:, :taps] for ref in (f0_ref, f1_ref, f2_ref)]
    out_ref[...] = product(mats, chosen, 3)


def plane_spectrum(kinds, kernels, forward):
    return pl.pallas_call(
        plane_spectrum_kernel,
        out_shape=jax.ShapeDtypeStruct((SPAN, 2 * kinds.shape[1]), F32),
        compiler_params=params(),
        name="plane_spectrum",
    )(kinds, kernels, *forward)


def sides(even, pair, middle):
    return jnp.where(even, middle, pair), jnp.where(even, pair, middle)


def plane_first_kernel(
    flag_ref, here_ref, pair_ref, middle_ref, seen_ref, seen_later_ref, spec_ref, *refs
):
    *mats, out_ref = refs
    forward, first, last = mats[0:3], mats[3:6], mats[6:9]
    hours, rows = here_ref.shape
    spec = spec_ref[...]
    before, after = sides(flag_ref[0] > 0.5, pair_ref[...], middle_ref[...])
    now, later = plane_delayed(before, here_ref[...], after, spec, forward, last, 3)
    start = jnp.transpose(seen_ref[pl.ds(0, rows), :]) - now
    start_later = (jnp.transpose(seen_later_ref[...]) - later) * flag_ref[1]
    out_ref[pl.ds(0, hours), :] = plane_advanced(start, start_later, spec, forward, first, 3)
    out_ref[pl.ds(hours, NOTE), :] = jnp.concatenate(
        [lanes(start, start), jnp.zeros((NOTE - 1, rows), F32)], axis=0
    )


def plane_first(flags, sums, seen, seen_later, spec, mats):
    hours, rows = sums[0].shape
    args = [flags, *sums, seen, seen_later, spec, *mats]
    return pl.pallas_call(
        plane_first_kernel,
        in_specs=[pl.BlockSpec(memory_space=pltpu.SMEM)]
        + [pl.BlockSpec(memory_space=pltpu.VMEM)] * (len(args) - 1),
        out_shape=jax.ShapeDtypeStruct((hours + NOTE, rows), F32),
        compiler_params=params(),
        name="plane_first",
    )(*args)


def plane_step_kernel(opening, final, flag_ref, here_ref, pair_ref, middle_ref, two_ref, mirror_ref, pulled_ref, spec_ref, *refs):
    mats, refs = refs[:9], refs[9:]
    forward, first, last = mats[0:3], mats[3:6], mats[6:9]
    if not opening:
        state_ref, *refs = refs
    if final:
        total_ref, out_ref = refs
    else:
        total_ref, out_ref, new_ref = refs
    height, rows = pulled_ref.shape
    hours = height - NOTE
    tail, body = pl.ds(hours, NOTE), pl.ds(0, hours)
    total_ref[...] = (here_ref[tail, :] + pair_ref[tail, :]) + (two_ref[...] + mirror_ref[...])
    spec = spec_ref[...]
    pulled = pulled_ref[body, :]
    sums = [ref[body, :] for ref in (here_ref, pair_ref, middle_ref)]
    if opening:
        scale = 1.0 / jnp.sqrt(total(total_ref, 0))
        new_su = [value * scale for value in sums]
        new_s = new_su
        new_zu = pulled * scale
        new_z = new_zu
    else:
        alpha, beta = ratios(total_ref)
        a, b, g = 1.0 / (alpha * beta), alpha / beta, beta / alpha
        old = lambda i: state_ref[pl.ds(i * hours, hours), :]
        new_su = [value * a - old(3 + i) * b for i, value in enumerate(sums)]
        new_s = [value - old(i) * g for i, value in enumerate(new_su)]
        new_zu = pulled * a - old(7) * b
        new_z = new_zu - old(6) * g
    here = new_s[0]
    before, after = sides(flag_ref[0] > 0.5, new_s[1], new_s[2])
    now, later = plane_delayed(before, here, after, spec, forward, last, 2)
    note = jnp.concatenate(
        [lanes(new_z, here), lanes(now, now), lanes(new_zu, here), jnp.zeros((NOTE - 3, rows), F32)],
        axis=0,
    )
    if final:
        out_ref[...] = note[:, : rows // 2] + note[:, rows // 2 :]
    else:
        for i, value in enumerate(new_s + new_su + [new_z, new_zu]):
            new_ref[pl.ds(i * hours, hours), :] = value
        out_ref[body, :] = plane_advanced(now, later * flag_ref[1], spec, forward, first, 2)
        out_ref[tail, :] = note


def plane_step(flags, sums, two, mirror, pulled, spec, mats, state, final):
    height, rows = pulled.shape
    hours = height - NOTE
    opening = state is None
    args = [flags, *sums, two, mirror, pulled, spec, *mats] + ([] if opening else [state])
    out = [jax.ShapeDtypeStruct((NOTE, rows), F32)]
    if final:
        out += [jax.ShapeDtypeStruct((NOTE, rows // 2), F32)]
    else:
        out += [jax.ShapeDtypeStruct((height, rows), F32), jax.ShapeDtypeStruct((8 * hours, rows), F32)]
    return pl.pallas_call(
        functools.partial(plane_step_kernel, opening, final),
        in_specs=[pl.BlockSpec(memory_space=pltpu.SMEM)]
        + [pl.BlockSpec(memory_space=pltpu.VMEM)] * (len(args) - 1),
        out_shape=out,
        compiler_params=params(),
        name="plane_step",
    )(*args)


def plane_finish_kernel(n0, n1, n2, n3, q0, q1, q2, inc_ref, field_ref, out_ref, rows_ref):
    blocks, slots, width = inc_ref.shape
    step = pl.program_id(0)

    @pl.when(step == 0)
    def _():
        e0, e1, e2 = weights_of([n0, n1, n2, n3])
        rows_ref[...] = jnp.transpose(q0[...] * e0 + q1[...] * e1 + q2[...] * e2)

    weights = inc_ref[...].astype(F32).astype(BF16)
    for b in range(blocks):
        here = pl.ds(b * width, width)
        rows = rows_ref[pl.ds(pl.multiple_of((step * blocks + b) * slots, slots), slots), :]
        added = sum(
            lax.dot_general(weights[b], piece, (((0,), (0,)), ((), ())), preferred_element_type=F32)
            for piece in pieces(rows, 2)
        )
        out_ref[here, :] = field_ref[here, :] + added


def plane_finish(notes, rows, incidence, field):
    blocks, slots, width = incidence.shape
    hours = field.shape[1]
    step = 8
    whole = lambda shape: pl.BlockSpec(shape, lambda i: (0, 0))
    return pl.pallas_call(
        plane_finish_kernel,
        grid=(blocks // step,),
        in_specs=[whole(n.shape) for n in notes]
        + [whole(q.shape) for q in rows]
        + [
            pl.BlockSpec((step, slots, width), lambda i: (i, 0, 0)),
            pl.BlockSpec((step * width, hours), lambda i: (i, 0)),
        ],
        out_specs=pl.BlockSpec((step * width, hours), lambda i: (i, 0)),
        out_shape=jax.ShapeDtypeStruct(field.shape, F32),
        scratch_shapes=[pltpu.VMEM((blocks * slots, hours), F32)],
        compiler_params=params(),
        name="plane_finish",
    )(*notes, *rows, incidence, field)


def plane_shards(incidence, row_gauge, gauge_kernel, kernels, observed, first_guess):
    rows, hours = observed.shape
    slots = incidence.shape[1]
    basin, tm = lax.axis_index("basin"), lax.axis_index("tm")
    z, x, y, c = basin // X_, basin % X_, tm // C_, tm % C_
    place = 2 * y + x
    first = jnp.stack([4 * c + (place ^ m) for m in range(4)] + [4 * c + place, 4 * (1 - c) + place])
    first = (first * rows).astype(jnp.int32)
    flags = jnp.stack([1 - z % 2, (z < Z_ - 1).astype(z.dtype)]).astype(F32)
    forward, inverse_first, inverse_last = turned_transforms()
    mats = [*forward, *inverse_first, *inverse_last]

    kinds = gauge_kernel.astype(F32).reshape(rows // hours, hours)
    parcel = moved(send(incidence, first_guess, row_gauge), to_plane)
    seen, kinds, parcel = lax.optimization_barrier((observed, kinds, parcel))
    seen_later = moved(seen, to_plane_before)
    seen = moved(jnp.concatenate([seen, kinds, jnp.zeros((8 - kinds.shape[0], hours), F32)]), to_plane)
    spec = plane_spectrum(seen[rows : rows + kinds.shape[0]], kernels, forward)

    beside = moved(parcel, over_core)
    meta = jnp.concatenate([parcel[hours:], beside[hours:]], axis=1)
    metas = [meta] + [moved(meta, where) for where in SQUARE]
    dense = spread(first, parcel, beside, hours, rows)
    sums = dense[0] + sum(moved(value, where) for value, where in zip(dense[1:], SQUARE))
    sums = [sums, moved(sums, z_pair), moved(sums, z_middle)]
    high, low = plane_couple(first, metas, rows)
    pulled = plane_first(flags, sums, seen, seen_later, spec, mats)
    notes, kept, state = [], [], None
    for k in range(3):
        values = [pulled] + [moved(pulled, where) for where in SQUARE]
        mine, other = plane_mix(high, low, values)
        mixed = mine + moved(other, over_core)
        note = mixed[hours:]
        sums = [mixed, moved(mixed, z_pair), moved(mixed, z_middle)]
        two, mirror = moved(note, z_two), moved(note, z_mirror)
        rows_mine, rows_other = plane_rows(first, parcel, beside, values)
        kept.append(moved(rows_mine + moved(rows_other, over_core), from_plane))
        result = plane_step(flags, sums, two, mirror, pulled, spec, mats, state, k == 2)
        if k == 2:
            total_note, last = result
        else:
            total_note, pulled, state = result
        notes.append(total_note)
    copies = jnp.broadcast_to(last[None], (Z_ * X_ * Y_ * C_,) + last.shape)
    notes.append(jnp.sum(lax.all_to_all(copies, ("basin", "tm"), 0, 0, tiled=False), axis=0))
    return plane_finish(notes, kept, incidence, first_guess)


def solution(mesh):
    planes = dict(mesh.shape) == {"basin": Z_ * X_, "tm": Y_ * C_}
    in_specs = (
        P("basin", None, None),
        P("basin"),
        P("basin"),
        P(),
        P("basin", "tm"),
        P("basin", "tm"),
    )
    return jax.shard_map(
        plane_shards if planes else shards, mesh=mesh, in_specs=in_specs, out_specs=P("basin", "tm"), check_vma=False
    )
```

```python
import functools

import jax
import jax.numpy as jnp
import numpy as np
from jax import lax
from jax.experimental import pallas as pl
from jax.experimental.pallas import tpu as pltpu
from jax.sharding import PartitionSpec as P

F32 = jnp.float32
BF16 = jnp.bfloat16
HIGH = lax.Precision.HIGHEST
SPAN = 256
MIB = 1024 * 1024


def params(mib=16):
    return pltpu.CompilerParams(vmem_limit_bytes=mib * MIB)


def transforms():
    half = SPAN // 2
    freq = 2.0 * np.pi * (np.arange(half) + 0.5) / SPAN
    phase = np.arange(SPAN)[:, None] * freq[None, :]
    forward = np.concatenate([np.cos(phase), -np.sin(phase)], axis=1)
    inverse = forward.T * (2.0 / SPAN)
    return (
        jnp.asarray(forward, F32),
        jnp.asarray(inverse[:, :half], F32),
        jnp.asarray(inverse[:, half:], F32),
    )


def dot(a, b):
    return jnp.dot(a, b, preferred_element_type=F32)


def exact(a, b):
    return jnp.dot(a, b, precision=HIGH, preferred_element_type=F32)


def pieces(value, count):
    out = []
    for _ in range(count):
        piece = value.astype(BF16)
        out.append(piece)
        value = value - piece.astype(F32)
    return out


def pick(hot, value):
    return sum(dot(hot, piece) for piece in pieces(value, 3))


def prepare_kernel(inc_ref, field_ref, partial_ref, gram_ref):
    blocks, slots, width = inc_ref.shape
    rows = blocks * slots
    weights = inc_ref[...].astype(F32).astype(BF16)
    for b in range(blocks):
        value = field_ref[pl.ds(b * width, width), :]
        partial_ref[pl.ds(b * slots, slots), :] = pick(weights[b], value)
    flat = weights.reshape(rows, width)
    full = lax.dot_general(flat, flat, (((1,), (1,)), ((), ())), preferred_element_type=F32)
    row = lax.broadcasted_iota(jnp.int32, (rows, rows), 0)
    col = lax.broadcasted_iota(jnp.int32, (rows, rows), 1)
    own = jnp.where(row // slots == col // slots, full, 0.0)
    gram_ref[...] = jnp.sum(own.reshape(blocks, slots, rows), axis=0)


def prepare(incidence, field):
    blocks, slots, width = incidence.shape
    hours = field.shape[1]
    step = 8
    return pl.pallas_call(
        prepare_kernel,
        grid=(blocks // step,),
        in_specs=[
            pl.BlockSpec((step, slots, width), lambda i: (i, 0, 0)),
            pl.BlockSpec((step * width, hours), lambda i: (i, 0)),
        ],
        out_specs=[
            pl.BlockSpec((step * slots, hours), lambda i: (i, 0)),
            pl.BlockSpec((slots, step * slots), lambda i: (0, i)),
        ],
        out_shape=[
            jax.ShapeDtypeStruct((blocks * slots, hours), F32),
            jax.ShapeDtypeStruct((slots, blocks * slots), F32),
        ],
        compiler_params=params(56),
        name="prepare",
    )(incidence, field)


def table_kernel(gauge_ref, partial_ref, out_ref):
    slots = partial_ref.shape[0]
    rows = out_ref.shape[0]
    first = pl.program_id(0) * rows
    gauge = lax.broadcasted_iota(jnp.int32, (rows, slots), 0) + first
    hot = jnp.where(gauge_ref[...] == gauge, 1.0, 0.0).astype(BF16)
    out_ref[...] = pick(hot, partial_ref[...])


def table(row_gauge, partial, gauges):
    slots, hours = partial.shape
    step = 256
    return pl.pallas_call(
        table_kernel,
        grid=(gauges // step,),
        in_specs=[
            pl.BlockSpec((1, slots), lambda i: (0, 0)),
            pl.BlockSpec((slots, hours), lambda i: (0, 0)),
        ],
        out_specs=pl.BlockSpec((step, hours), lambda i: (i, 0)),
        out_shape=jax.ShapeDtypeStruct((gauges, hours), F32),
        compiler_params=params(56),
        name="table",
    )(row_gauge.reshape(1, slots), partial)


def couple_kernel(first_ref, lane_ref, sub_ref, gram_ref, high_ref, low_ref, near_ref):
    slots = gram_ref.shape[0]
    count = lane_ref.shape[1]
    rows, cols = high_ref.shape
    tile = 256
    first = first_ref[0]

    @pl.when(pl.program_id(0) == 0)
    def _():
        row = lax.broadcasted_iota(jnp.int32, (tile, tile), 0)
        col = lax.broadcasted_iota(jnp.int32, (tile, tile), 1)
        same = row // slots == col // slots
        mine = lax.broadcasted_iota(jnp.int32, (rows, tile), 0) + first

        def body(i, carry):
            here = pl.ds(pl.multiple_of(i * tile, tile), tile)
            block = jnp.concatenate([gram_ref[:, here]] * (tile // slots), axis=0)
            block = jnp.where(same, block, 0.0).astype(BF16)
            hot = jnp.where(lane_ref[:, here] == mine, 1.0, 0.0).astype(BF16)
            near_ref[:, here] = dot(hot, block)
            return carry

        lax.fori_loop(0, count // tile, body, 0)

    def chunk(i, total):
        here = pl.ds(pl.multiple_of(i * 1024, 1024), 1024)
        gauge = lax.broadcasted_iota(jnp.int32, (1024, cols), 1) + pl.program_id(0) * cols
        hot = jnp.where(sub_ref[here, :] == gauge, 1.0, 0.0).astype(BF16)
        near = near_ref[:, here]
        high = near.astype(BF16)
        low = (near - high.astype(F32)).astype(BF16)
        return total + dot(high, hot) + dot(low, hot)

    total = lax.fori_loop(0, count // 1024, chunk, jnp.zeros((rows, cols), F32))
    high, low = pieces(total, 2)
    high_ref[...] = high
    low_ref[...] = low


def couple(first, row_gauge, gram, rows, gauges):
    count = row_gauge.shape[0]
    step = 256
    return pl.pallas_call(
        couple_kernel,
        grid=(gauges // step,),
        in_specs=[
            pl.BlockSpec(memory_space=pltpu.SMEM),
            pl.BlockSpec((1, count), lambda i: (0, 0)),
            pl.BlockSpec((count, 1), lambda i: (0, 0)),
            pl.BlockSpec(gram.shape, lambda i: (0, 0)),
        ],
        out_specs=[pl.BlockSpec((rows, step), lambda i: (0, i))] * 2,
        out_shape=[jax.ShapeDtypeStruct((rows, gauges), BF16)] * 2,
        scratch_shapes=[pltpu.VMEM((rows, count), F32)],
        compiler_params=params(56),
        name="couple",
    )(first, row_gauge.reshape(1, count), row_gauge.reshape(count, 1), gram)


def mix_kernel(high_ref, low_ref, value_ref, out_ref):
    high = high_ref[...]
    low = low_ref[...]
    one, two, three = pieces(value_ref[...], 3)
    out_ref[...] = (dot(high, three) + dot(low, two)) + (dot(high, two) + dot(low, one)) + dot(high, one)


def mix(high, low, value):
    return pl.pallas_call(
        mix_kernel,
        out_shape=jax.ShapeDtypeStruct((high.shape[0], value.shape[1]), F32),
        compiler_params=params(56),
        name="mix",
    )(high, low, value)


def spectrum_kernel(class_ref, kernels_ref, forward_ref, out_ref):
    rows = class_ref.shape[0]
    classes, taps = kernels_ref.shape
    kind = lax.broadcasted_iota(jnp.int32, (rows, classes), 1)
    hot = jnp.where(class_ref[...] == kind, 1.0, 0.0)
    out_ref[...] = exact(exact(hot, kernels_ref[...]), forward_ref[pl.ds(0, taps), :])


def spectrum(gauge_kernel, kernels, forward):
    rows = gauge_kernel.shape[0]
    return pl.pallas_call(
        spectrum_kernel,
        out_shape=jax.ShapeDtypeStruct((rows, SPAN), F32),
        compiler_params=params(56),
        name="spectrum",
    )(gauge_kernel.reshape(rows, 1), kernels, forward)


def delayed(before, here, after, spec, forward, inverse_last):
    rows, half = here.shape
    stacked = jnp.concatenate(
        [jnp.concatenate([before, here], axis=1), jnp.concatenate([here, after], axis=1)], axis=0
    )
    waves = exact(stacked, forward)
    real, imag = waves[:, :half], waves[:, half:]
    kr = jnp.concatenate([spec[:, :half]] * 2, axis=0)
    ki = jnp.concatenate([spec[:, half:]] * 2, axis=0)
    turned = jnp.concatenate([real * kr - imag * ki, real * ki + imag * kr], axis=1)
    out = exact(turned, inverse_last)
    return out[:rows], out[rows:]


def advanced(here, after, spec, forward, inverse_first):
    half = here.shape[1]
    waves = exact(jnp.concatenate([here, after], axis=1), forward)
    real, imag = waves[:, :half], waves[:, half:]
    kr, ki = spec[:, :half], spec[:, half:]
    turned = jnp.concatenate([real * kr + imag * ki, imag * kr - real * ki], axis=1)
    return exact(turned, inverse_first)


def lanes(a, b):
    return jnp.sum(a * b, axis=0, keepdims=True)


def total(ref, row):
    return jnp.sum(ref[row : row + 1, :], axis=1, keepdims=True)


def ratios(ref):
    square = total(ref, 0)
    alpha = jnp.sqrt(square)
    beta = jnp.sqrt(jnp.maximum(total(ref, 1) / square - 2.0 * total(ref, 2) + square, 0.0))
    return alpha, beta


def first_kernel(
    more_ref, sums_ref, observed_ref, spec_ref, forward_ref, first_ref, last_ref, out_ref, note_ref
):
    rows, half = observed_ref.shape[0] // 2, observed_ref.shape[1]
    spec, forward = spec_ref[...], forward_ref[...]
    before, here, after = (sums_ref[pl.ds(i * rows, rows), :] for i in range(3))
    now, later = delayed(before, here, after, spec, forward, last_ref[...])
    start = observed_ref[pl.ds(0, rows), :] - now
    start_later = (observed_ref[pl.ds(rows, rows), :] - later) * more_ref[0]
    out_ref[...] = advanced(start, start_later, spec, forward, first_ref[...])
    note_ref[...] = jnp.concatenate([lanes(start, start), jnp.zeros((7, half), F32)], axis=0)


def first_step(more, sums, observed, spec, mats):
    rows, half = spec.shape[0], observed.shape[1]
    return pl.pallas_call(
        first_kernel,
        in_specs=[pl.BlockSpec(memory_space=pltpu.SMEM)] + [pl.BlockSpec(memory_space=pltpu.VMEM)] * 6,
        out_shape=[jax.ShapeDtypeStruct((rows, half), F32), jax.ShapeDtypeStruct((8, half), F32)],
        compiler_params=params(56),
        name="first_step",
    )(more, sums, observed, spec, *mats)


def step_kernel(
    opening,
    final,
    more_ref,
    note_ref,
    sums_ref,
    spec_ref,
    forward_ref,
    first_ref,
    last_ref,
    pulled_ref,
    *refs,
):
    if opening:
        state_ref = None
    else:
        state_ref, *refs = refs
    if final:
        (out_note_ref,) = refs
    else:
        new_ref, out_ref, out_note_ref = refs
    rows, half = pulled_ref.shape
    spec, forward = spec_ref[...], forward_ref[...]
    if opening:
        scale = 1.0 / jnp.sqrt(total(note_ref, 0))
        along = sums_ref[...] * scale
        new_s, new_su = along, along
        new_zu = pulled_ref[...] * scale
        new_z = new_zu
    else:
        alpha, beta = ratios(note_ref)
        a, b, g = 1.0 / (alpha * beta), alpha / beta, beta / alpha
        wide = pl.ds(0, 3 * rows), pl.ds(3 * rows, 3 * rows)
        new_su = sums_ref[...] * a - state_ref[wide[1], :] * b
        new_s = new_su - state_ref[wide[0], :] * g
        new_zu = pulled_ref[...] * a - state_ref[pl.ds(7 * rows, rows), :] * b
        new_z = new_zu - state_ref[pl.ds(6 * rows, rows), :] * g
    before, here, after = (new_s[i * rows : (i + 1) * rows] for i in range(3))
    now, later = delayed(before, here, after, spec, forward, last_ref[...])
    out_note_ref[...] = jnp.concatenate(
        [lanes(new_z, here), lanes(now, now), lanes(new_zu, here), jnp.zeros((5, half), F32)], axis=0
    )
    if not final:
        new_ref[pl.ds(0, 3 * rows), :] = new_s
        new_ref[pl.ds(3 * rows, 3 * rows), :] = new_su
        new_ref[pl.ds(6 * rows, rows), :] = new_z
        new_ref[pl.ds(7 * rows, rows), :] = new_zu
        out_ref[...] = advanced(now, later * more_ref[0], spec, forward, first_ref[...])


def next_step(more, note, sums, spec, mats, pulled, state, final):
    rows, half = pulled.shape
    opening = state is None
    shapes = [
        jax.ShapeDtypeStruct((8 * rows, half), F32),
        jax.ShapeDtypeStruct((rows, half), F32),
        jax.ShapeDtypeStruct((8, half), F32),
    ]
    args = [more, note, sums, spec, *mats, pulled] + ([] if opening else [state])
    return pl.pallas_call(
        functools.partial(step_kernel, opening, final),
        in_specs=[pl.BlockSpec(memory_space=pltpu.SMEM)]
        + [pl.BlockSpec(memory_space=pltpu.VMEM)] * (len(args) - 1),
        out_shape=shapes[2:] if final else shapes,
        compiler_params=params(56),
        name="next_step",
    )(*args)


def weights_of(notes):
    start = jnp.sqrt(total(notes[0], 0))
    zero = jnp.zeros_like(start)
    units = [1.0 / start, zero, zero]
    z, zu = list(units), list(units)
    phibar = start
    alpha, beta = ratios(notes[1])
    rhobar = alpha
    w = [value / alpha for value in z]
    result = [zero] * 3
    steps = len(notes) - 1
    for k in range(steps):
        rho = jnp.sqrt(rhobar * rhobar + beta * beta)
        cosine, sine = rhobar / rho, beta / rho
        phi, phibar = cosine * phibar, sine * phibar
        result = [r + phi / rho * value for r, value in zip(result, w)]
        if k < steps - 1:
            a, b, g = 1.0 / (alpha * beta), alpha / beta, beta / alpha
            zu = [(a if i == k + 1 else 0.0) - b * value for i, value in enumerate(zu)]
            z = [value - g * old for value, old in zip(zu, z)]
            alpha, beta = ratios(notes[k + 2])
            theta = sine * alpha
            rhobar = -cosine * alpha
            w = [value / alpha - theta / rho * old for value, old in zip(z, w)]
    return result


def finish_kernel(n0, n1, n2, n3, gauge_ref, q0, q1, q2, inc_ref, field_ref, out_ref, rows_ref):
    blocks, slots, width = inc_ref.shape
    count = rows_ref.shape[0]
    gauges = q0.shape[0]
    step = pl.program_id(0)

    @pl.when(step == 0)
    def _():
        e0, e1, e2 = weights_of([n0, n1, n2, n3])
        width_ = 512

        def body(i, value):
            here = pl.ds(pl.multiple_of(i * width_, width_), width_)
            mixed = q0[here, :] * e0 + q1[here, :] * e1 + q2[here, :] * e2
            gauge = lax.broadcasted_iota(jnp.int32, (count, width_), 1) + i * width_
            hot = jnp.where(gauge_ref[...] == gauge, 1.0, 0.0).astype(BF16)
            return value + pick(hot, mixed)

        rows_ref[...] = lax.fori_loop(0, gauges // width_, body, jnp.zeros(rows_ref.shape, F32))

    weights = inc_ref[...].astype(F32).astype(BF16)
    for b in range(blocks):
        here = pl.ds(b * width, width)
        rows = rows_ref[pl.ds(pl.multiple_of((step * blocks + b) * slots, slots), slots), :]
        added = sum(
            lax.dot_general(weights[b], piece, (((0,), (0,)), ((), ())), preferred_element_type=F32)
            for piece in pieces(rows, 3)
        )
        out_ref[here, :] = field_ref[here, :] + added


def finish(notes, row_gauge, gathered, incidence, field):
    blocks, slots, width = incidence.shape
    hours = field.shape[1]
    count = row_gauge.shape[0]
    step = 8
    whole = lambda shape: pl.BlockSpec(shape, lambda i: (0, 0))
    return pl.pallas_call(
        finish_kernel,
        grid=(blocks // step,),
        in_specs=[whole(n.shape) for n in notes]
        + [whole((count, 1))]
        + [whole(q.shape) for q in gathered]
        + [
            pl.BlockSpec((step, slots, width), lambda i: (i, 0, 0)),
            pl.BlockSpec((step * width, hours), lambda i: (i, 0)),
        ],
        out_specs=pl.BlockSpec((step * width, hours), lambda i: (i, 0)),
        out_shape=jax.ShapeDtypeStruct(field.shape, F32),
        scratch_shapes=[pltpu.VMEM((count, hours), F32)],
        compiler_params=params(56),
        name="finish",
    )(*notes, row_gauge.reshape(count, 1), *gathered, incidence, field)


def shifted(value, axis, by):
    devices = lax.axis_size(axis)
    pairs = [(i, i + by) for i in range(devices) if 0 <= i + by < devices]
    return lax.ppermute(value, axis, pairs)


def window(value):
    return jnp.concatenate([shifted(value, "tm", 1), value, shifted(value, "tm", -1)], axis=0)


def gathered_rows(value):
    owners = lax.axis_size("basin")
    copies = jnp.broadcast_to(value[None], (owners,) + value.shape)
    return lax.all_to_all(copies, "basin", 0, 0, tiled=False)


def over_hours(note):
    blocks = lax.axis_size("tm")
    result = note
    for by in range(1, blocks):
        result = result + lax.ppermute(note, "tm", [(i, (i + by) % blocks) for i in range(blocks)])
    return result


def shards(incidence, row_gauge, gauge_kernel, kernels, observed, first_guess):
    owners = lax.axis_size("basin")
    rows, hours = observed.shape
    gauges = rows * owners
    mats = transforms()
    spec = spectrum(gauge_kernel, kernels, mats[0])
    more = (lax.axis_index("tm") < lax.axis_size("tm") - 1).astype(F32).reshape(1)
    partial, gram = prepare(incidence, first_guess)
    all_gram = lax.all_gather(gram, "basin", axis=1, tiled=True)
    all_rows = lax.all_gather(row_gauge, "basin", axis=0, tiled=True)
    dense = table(row_gauge, partial, gauges).reshape(owners, rows, hours)
    sums = jnp.sum(lax.all_to_all(dense, "basin", 0, 0, tiled=False), axis=0)
    both = jnp.concatenate([observed, shifted(observed, "tm", -1)], axis=0)
    first = (lax.axis_index("basin") * rows).astype(jnp.int32).reshape(1)
    high, low = couple(first, all_rows, all_gram, rows, gauges)

    pulled, note = first_step(more, window(sums), both, spec, mats)
    notes, kept, state = [], [], None
    for k in range(3):
        everyone = gathered_rows(jnp.concatenate([pulled, note], axis=0))
        value = everyone[:, :rows].reshape(gauges, hours)
        notes.append(over_hours(jnp.sum(everyone[:, rows:], axis=0)))
        kept.append(value)
        around = window(mix(high, low, value))
        final = k == 2
        result = next_step(more, notes[-1], around, spec, mats, pulled, state, final)
        if final:
            (note,) = result
        else:
            state, pulled, note = result
    notes.append(over_hours(jnp.sum(gathered_rows(note), axis=0)))
    return finish(notes, row_gauge, kept, incidence, first_guess)


Z_, X_, Y_, C_ = 4, 2, 2, 2
NOTE = 8


def device(z, x, y, c):
    return (z * X_ + x) * (Y_ * C_) + y * C_ + c


def moved(value, where):
    pairs = []
    for z, x, y, c in np.ndindex(Z_, X_, Y_, C_):
        target = where(z, x, y, c)
        if target is not None:
            pairs.append((device(z, x, y, c), device(*target)))
    return lax.ppermute(value, ("basin", "tm"), pairs)


def to_plane(z, x, y, c):
    return 2 * y + c, x, z & 1, z >> 1


def to_plane_before(z, x, y, c):
    t = 2 * y + c
    return (t - 1, x, z & 1, z >> 1) if t else None


def from_plane(z, x, y, c):
    return 2 * c + y, x, z >> 1, z & 1


def over_x(z, x, y, c):
    return z, 1 - x, y, c


def over_y(z, x, y, c):
    return z, x, 1 - y, c


def over_xy(z, x, y, c):
    return z, 1 - x, 1 - y, c


def over_core(z, x, y, c):
    return z, x, y, 1 - c


def z_pair(z, x, y, c):
    return z ^ 1, x, y, c


def z_middle(z, x, y, c):
    return (3 - z, x, y, c) if z in (1, 2) else None


def z_two(z, x, y, c):
    return z ^ 2, x, y, c


def z_mirror(z, x, y, c):
    return 3 - z, x, y, c


SQUARE = (over_x, over_y, over_xy)


def split_constant(value):
    out = []
    for _ in range(3):
        piece = value.astype(jnp.bfloat16)
        out.append(jnp.asarray(piece))
        value = value - piece.astype(np.float64)
    return out


def turned_transforms():
    half = SPAN // 2
    freq = 2.0 * np.pi * (np.arange(half) + 0.5) / SPAN
    phase = freq[:, None] * np.arange(SPAN)[None, :]
    forward = np.concatenate([np.cos(phase), -np.sin(phase)], axis=0)
    inverse = forward.T * (2.0 / SPAN)
    return split_constant(forward), split_constant(inverse[:half]), split_constant(inverse[half:])


def product(mats, value, order):
    parts = pieces(value, order)
    result = None
    for level in reversed(range(order)):
        for i in range(level + 1):
            term = dot(mats[i][...], parts[level - i])
            result = term if result is None else result + term
    return result


def turn(waves, spec, sign):
    half = waves.shape[0] // 2
    real, imag = waves[:half], waves[half:]
    kr, ki = spec[:half], spec[half:] * sign
    return jnp.concatenate([real * kr - imag * ki, real * ki + imag * kr], axis=0)


def plane_delayed(before, here, after, spec, forward, last, order):
    out = []
    for pair in ((before, here), (here, after)):
        waves = product(forward, jnp.concatenate(pair, axis=0), order)
        out.append(product(last, turn(waves, spec, 1.0), order))
    return out


def plane_advanced(here, after, spec, forward, first, order):
    waves = product(forward, jnp.concatenate([here, after], axis=0), order)
    return product(first, turn(waves, spec, -1.0), order)


def send_kernel(inc_ref, field_ref, gauge_ref, out_ref):
    blocks, slots, width = inc_ref.shape
    rows = blocks * slots
    hours = field_ref.shape[1]
    weights = inc_ref[...].astype(F32).astype(BF16)
    parts = []
    for b in range(blocks):
        parts.append(pick(weights[b], field_ref[pl.ds(b * width, width), :]))
    out_ref[pl.ds(0, hours), :] = jnp.transpose(jnp.concatenate(parts, axis=0))
    flat = weights.reshape(rows, width)
    full = lax.dot_general(flat, flat, (((1,), (1,)), ((), ())), preferred_element_type=F32)
    row = lax.broadcasted_iota(jnp.int32, (rows, rows), 0)
    col = lax.broadcasted_iota(jnp.int32, (rows, rows), 1)
    own = jnp.where(row // slots == col // slots, full, 0.0)
    out_ref[pl.ds(hours, slots), :] = jnp.sum(own.reshape(blocks, slots, rows), axis=0)
    out_ref[pl.ds(hours + slots, 8), :] = jnp.broadcast_to(gauge_ref[...].astype(F32), (8, rows))


def send(incidence, field, row_gauge):
    blocks, slots, width = incidence.shape
    hours = field.shape[1]
    step = 8
    height = hours + slots + 8
    return pl.pallas_call(
        send_kernel,
        grid=(blocks // step,),
        in_specs=[
            pl.BlockSpec((step, slots, width), lambda i: (i, 0, 0)),
            pl.BlockSpec((step * width, hours), lambda i: (i, 0)),
            pl.BlockSpec((1, step * slots), lambda i: (0, i)),
        ],
        out_specs=pl.BlockSpec((height, step * slots), lambda i: (0, i)),
        out_shape=jax.ShapeDtypeStruct((height, blocks * slots), F32),
        compiler_params=params(),
        name="send",
    )(incidence, field, row_gauge.reshape(1, blocks * slots))


def hot_rows(gauge, first, rows):
    mine = (lax.broadcasted_iota(jnp.int32, (rows, gauge.shape[1]), 0) + first).astype(F32)
    return jnp.where(gauge == mine, 1.0, 0.0).astype(BF16)


def spread_kernel(first_ref, mine_ref, other_ref, *out_refs):
    hours, rows = out_refs[0].shape
    slots = mine_ref.shape[0] - hours - 8
    where = hours + slots
    for m, out_ref in enumerate(out_refs):
        result = None
        for ref in (mine_ref, other_ref):
            hot = hot_rows(ref[where : where + 1, :], first_ref[m], rows)
            for piece in reversed(pieces(ref[pl.ds(0, hours), :], 3)):
                term = lax.dot_general(
                    piece, hot, (((1,), (1,)), ((), ())), preferred_element_type=F32
                )
                result = term if result is None else result + term
        out_ref[...] = result


def spread(first, mine, other, hours, rows):
    return pl.pallas_call(
        spread_kernel,
        in_specs=[pl.BlockSpec(memory_space=pltpu.SMEM)] + [pl.BlockSpec(memory_space=pltpu.VMEM)] * 2,
        out_shape=[jax.ShapeDtypeStruct((hours, rows), F32)] * 4,
        compiler_params=params(),
        name="spread",
    )(first, mine, other)


def plane_couple_kernel(first_ref, a_ref, b_ref, c_ref, d_ref, high_ref, low_ref, total_ref, meta_ref):
    height, double = a_ref.shape
    slots = height - 8
    count = double // 2
    cols, rows = high_ref.shape
    part = cols // 4
    tile = 256
    for i, ref in enumerate((a_ref, b_ref, c_ref, d_ref)):
        for j in range(2):
            meta_ref[2 * i + j] = ref[:, j * count : (j + 1) * count]
    row = lax.broadcasted_iota(jnp.int32, (tile, tile), 0)
    col = lax.broadcasted_iota(jnp.int32, (tile, tile), 1)
    same = row // slots == col // slots
    total_ref[...] = jnp.zeros_like(total_ref)

    def body(i, carry):
        gauge = meta_ref[i, slots : slots + 1, :]
        near = []
        for j in range(count // tile):
            here = slice(j * tile, (j + 1) * tile)
            block = jnp.concatenate([meta_ref[i, :slots, here]] * (tile // slots), axis=0)
            block = jnp.where(same, block, 0.0).astype(BF16)
            mine = jnp.concatenate(
                [hot_rows(gauge[:, here], first_ref[4 + h], rows // 2) for h in range(2)], axis=0
            )
            near.append(
                lax.dot_general(block, mine, (((1,), (1,)), ((), ())), preferred_element_type=F32)
            )
        near = jnp.concatenate(near, axis=0)
        high = near.astype(BF16)
        rest = near - high.astype(F32)
        hot = jnp.concatenate([hot_rows(gauge, first_ref[m], part) for m in range(4)], axis=0)
        total_ref[...] += dot(hot, high)

        @pl.when(jnp.max(jnp.abs(rest)) > 0.0)
        def _():
            total_ref[...] += dot(hot, rest.astype(BF16))

        return carry

    lax.fori_loop(0, 8, body, 0)
    high, low = pieces(total_ref[...], 2)
    high_ref[...] = high
    low_ref[...] = low


def plane_couple(first, metas, rows):
    height, double = metas[0].shape
    return pl.pallas_call(
        plane_couple_kernel,
        in_specs=[pl.BlockSpec(memory_space=pltpu.SMEM)] + [pl.BlockSpec(memory_space=pltpu.VMEM)] * 4,
        out_shape=[jax.ShapeDtypeStruct((4 * rows, 2 * rows), BF16)] * 2,
        scratch_shapes=[
            pltpu.VMEM((4 * rows, 2 * rows), F32),
            pltpu.VMEM((8, height, double // 2), F32),
        ],
        compiler_params=params(),
        name="plane_couple",
        cost_estimate=pl.CostEstimate(flops=14_000_000_000, bytes_accessed=4_000_000, transcendentals=0),
    )(first, *metas)


def plane_mix_kernel(high_ref, low_ref, a_ref, b_ref, c_ref, d_ref, mine_ref, other_ref):
    refs = (a_ref, b_ref, c_ref, d_ref)
    height, rows = a_ref.shape
    hours = height - NOTE
    value = jnp.concatenate([ref[pl.ds(0, hours), :] for ref in refs], axis=1)
    one, two = pieces(value, 2)
    high, low = high_ref[...], low_ref[...]
    result = (dot(two, high) + dot(one, low)) + dot(one, high)
    note = sum(ref[pl.ds(hours, NOTE), :] for ref in refs)
    mine_ref[pl.ds(0, hours), :] = result[:, :rows]
    other_ref[pl.ds(0, hours), :] = result[:, rows:]
    mine_ref[pl.ds(hours, NOTE), :] = note
    other_ref[pl.ds(hours, NOTE), :] = note


def plane_mix(high, low, values):
    return pl.pallas_call(
        plane_mix_kernel,
        out_shape=[jax.ShapeDtypeStruct(values[0].shape, F32)] * 2,
        compiler_params=params(),
        name="plane_mix",
    )(high, low, *values)


def plane_rows_kernel(first_ref, mine_ref, other_ref, a_ref, b_ref, c_ref, d_ref, out_mine_ref, out_other_ref):
    height, rows = a_ref.shape
    hours = height - NOTE
    where = mine_ref.shape[0] - 8
    for ref, out_ref in ((mine_ref, out_mine_ref), (other_ref, out_other_ref)):
        gauge = ref[where : where + 1, :]
        result = None
        for m, value_ref in enumerate((a_ref, b_ref, c_ref, d_ref)):
            hot = hot_rows(gauge, first_ref[m], rows)
            for piece in reversed(pieces(value_ref[pl.ds(0, hours), :], 2)):
                term = dot(piece, hot)
                result = term if result is None else result + term
        out_ref[...] = result


def plane_rows(first, mine, other, values):
    hours = values[0].shape[0] - NOTE
    slots = mine.shape[1]
    return pl.pallas_call(
        plane_rows_kernel,
        in_specs=[pl.BlockSpec(memory_space=pltpu.SMEM)] + [pl.BlockSpec(memory_space=pltpu.VMEM)] * 6,
        out_shape=[jax.ShapeDtypeStruct((hours, slots), F32)] * 2,
        compiler_params=params(),
        name="plane_rows",
        cost_estimate=pl.CostEstimate(flops=1_000_000_000, bytes_accessed=2_000_000, transcendentals=0),
    )(first, mine, other, *values)


def plane_spectrum_kernel(class_ref, kernels_ref, f0_ref, f1_ref, f2_ref, out_ref):
    classes, taps = kernels_ref.shape
    kind = jnp.concatenate([class_ref[0:1, :], class_ref[1:2, :]], axis=1)
    hot = jnp.where(
        lax.broadcasted_iota(jnp.int32, (classes, kind.shape[1]), 0).astype(F32) == kind, 1.0, 0.0
    ).astype(BF16)
    chosen = None
    for piece in reversed(pieces(jnp.transpose(kernels_ref[...]), 3)):
        term = dot(piece, hot)
        chosen = term if chosen is None else chosen + term
    mats = [ref[:, :taps] for ref in (f0_ref, f1_ref, f2_ref)]
    out_ref[...] = product(mats, chosen, 3)


def plane_spectrum(kinds, kernels, forward):
    return pl.pallas_call(
        plane_spectrum_kernel,
        out_shape=jax.ShapeDtypeStruct((SPAN, 2 * kinds.shape[1]), F32),
        compiler_params=params(),
        name="plane_spectrum",
    )(kinds, kernels, *forward)


def sides(even, pair, middle):
    return jnp.where(even, middle, pair), jnp.where(even, pair, middle)


def plane_first_kernel(
    flag_ref, here_ref, pair_ref, middle_ref, seen_ref, seen_later_ref, spec_ref, *refs
):
    *mats, out_ref = refs
    forward, first, last = mats[0:3], mats[3:6], mats[6:9]
    hours, rows = here_ref.shape
    spec = spec_ref[...]
    before, after = sides(flag_ref[0] > 0.5, pair_ref[...], middle_ref[...])
    now, later = plane_delayed(before, here_ref[...], after, spec, forward, last, 3)
    start = jnp.transpose(seen_ref[pl.ds(0, rows), :]) - now
    start_later = (jnp.transpose(seen_later_ref[...]) - later) * flag_ref[1]
    out_ref[pl.ds(0, hours), :] = plane_advanced(start, start_later, spec, forward, first, 3)
    out_ref[pl.ds(hours, NOTE), :] = jnp.concatenate(
        [lanes(start, start), jnp.zeros((NOTE - 1, rows), F32)], axis=0
    )


def plane_first(flags, sums, seen, seen_later, spec, mats):
    hours, rows = sums[0].shape
    args = [flags, *sums, seen, seen_later, spec, *mats]
    return pl.pallas_call(
        plane_first_kernel,
        in_specs=[pl.BlockSpec(memory_space=pltpu.SMEM)]
        + [pl.BlockSpec(memory_space=pltpu.VMEM)] * (len(args) - 1),
        out_shape=jax.ShapeDtypeStruct((hours + NOTE, rows), F32),
        compiler_params=params(),
        name="plane_first",
    )(*args)


def plane_step_kernel(opening, final, flag_ref, here_ref, pair_ref, middle_ref, two_ref, mirror_ref, pulled_ref, spec_ref, *refs):
    mats, refs = refs[:9], refs[9:]
    forward, first, last = mats[0:3], mats[3:6], mats[6:9]
    if not opening:
        state_ref, *refs = refs
    if final:
        total_ref, out_ref = refs
    else:
        total_ref, out_ref, new_ref = refs
    height, rows = pulled_ref.shape
    hours = height - NOTE
    tail, body = pl.ds(hours, NOTE), pl.ds(0, hours)
    total_ref[...] = (here_ref[tail, :] + pair_ref[tail, :]) + (two_ref[...] + mirror_ref[...])
    spec = spec_ref[...]
    pulled = pulled_ref[body, :]
    sums = [ref[body, :] for ref in (here_ref, pair_ref, middle_ref)]
    if opening:
        scale = 1.0 / jnp.sqrt(total(total_ref, 0))
        new_su = [value * scale for value in sums]
        new_s = new_su
        new_zu = pulled * scale
        new_z = new_zu
    else:
        alpha, beta = ratios(total_ref)
        a, b, g = 1.0 / (alpha * beta), alpha / beta, beta / alpha
        old = lambda i: state_ref[pl.ds(i * hours, hours), :]
        new_su = [value * a - old(3 + i) * b for i, value in enumerate(sums)]
        new_s = [value - old(i) * g for i, value in enumerate(new_su)]
        new_zu = pulled * a - old(7) * b
        new_z = new_zu - old(6) * g
    here = new_s[0]
    before, after = sides(flag_ref[0] > 0.5, new_s[1], new_s[2])
    now, later = plane_delayed(before, here, after, spec, forward, last, 2)
    note = jnp.concatenate(
        [lanes(new_z, here), lanes(now, now), lanes(new_zu, here), jnp.zeros((NOTE - 3, rows), F32)],
        axis=0,
    )
    if final:
        out_ref[...] = note[:, : rows // 2] + note[:, rows // 2 :]
    else:
        for i, value in enumerate(new_s + new_su + [new_z, new_zu]):
            new_ref[pl.ds(i * hours, hours), :] = value
        out_ref[body, :] = plane_advanced(now, later * flag_ref[1], spec, forward, first, 2)
        out_ref[tail, :] = note


def plane_step(flags, sums, two, mirror, pulled, spec, mats, state, final):
    height, rows = pulled.shape
    hours = height - NOTE
    opening = state is None
    args = [flags, *sums, two, mirror, pulled, spec, *mats] + ([] if opening else [state])
    out = [jax.ShapeDtypeStruct((NOTE, rows), F32)]
    if final:
        out += [jax.ShapeDtypeStruct((NOTE, rows // 2), F32)]
    else:
        out += [jax.ShapeDtypeStruct((height, rows), F32), jax.ShapeDtypeStruct((8 * hours, rows), F32)]
    return pl.pallas_call(
        functools.partial(plane_step_kernel, opening, final),
        in_specs=[pl.BlockSpec(memory_space=pltpu.SMEM)]
        + [pl.BlockSpec(memory_space=pltpu.VMEM)] * (len(args) - 1),
        out_shape=out,
        compiler_params=params(),
        name="plane_step",
    )(*args)


def plane_finish_kernel(n0, n1, n2, n3, q0, q1, q2, inc_ref, field_ref, out_ref, rows_ref):
    blocks, slots, width = inc_ref.shape
    step = pl.program_id(0)

    @pl.when(step == 0)
    def _():
        e0, e1, e2 = weights_of([n0, n1, n2, n3])
        rows_ref[...] = jnp.transpose(q0[...] * e0 + q1[...] * e1 + q2[...] * e2)

    weights = inc_ref[...].astype(F32).astype(BF16)
    for b in range(blocks):
        here = pl.ds(b * width, width)
        rows = rows_ref[pl.ds(pl.multiple_of((step * blocks + b) * slots, slots), slots), :]
        added = sum(
            lax.dot_general(weights[b], piece, (((0,), (0,)), ((), ())), preferred_element_type=F32)
            for piece in pieces(rows, 2)
        )
        out_ref[here, :] = field_ref[here, :] + added


def plane_finish(notes, rows, incidence, field):
    blocks, slots, width = incidence.shape
    hours = field.shape[1]
    step = 8
    whole = lambda shape: pl.BlockSpec(shape, lambda i: (0, 0))
    return pl.pallas_call(
        plane_finish_kernel,
        grid=(blocks // step,),
        in_specs=[whole(n.shape) for n in notes]
        + [whole(q.shape) for q in rows]
        + [
            pl.BlockSpec((step, slots, width), lambda i: (i, 0, 0)),
            pl.BlockSpec((step * width, hours), lambda i: (i, 0)),
        ],
        out_specs=pl.BlockSpec((step * width, hours), lambda i: (i, 0)),
        out_shape=jax.ShapeDtypeStruct(field.shape, F32),
        scratch_shapes=[pltpu.VMEM((blocks * slots, hours), F32)],
        compiler_params=params(),
        name="plane_finish",
    )(*notes, *rows, incidence, field)


def plane_shards(incidence, row_gauge, gauge_kernel, kernels, observed, first_guess):
    rows, hours = observed.shape
    slots = incidence.shape[1]
    basin, tm = lax.axis_index("basin"), lax.axis_index("tm")
    z, x, y, c = basin // X_, basin % X_, tm // C_, tm % C_
    place = 2 * y + x
    first = jnp.stack([4 * c + (place ^ m) for m in range(4)] + [4 * c + place, 4 * (1 - c) + place])
    first = (first * rows).astype(jnp.int32)
    flags = jnp.stack([1 - z % 2, (z < Z_ - 1).astype(z.dtype)]).astype(F32)
    forward, inverse_first, inverse_last = turned_transforms()
    mats = [*forward, *inverse_first, *inverse_last]

    kinds = gauge_kernel.astype(F32).reshape(rows // hours, hours)
    parcel = moved(send(incidence, first_guess, row_gauge), to_plane)
    seen, kinds, parcel = lax.optimization_barrier((observed, kinds, parcel))
    seen_later = moved(seen, to_plane_before)
    seen = moved(jnp.concatenate([seen, kinds, jnp.zeros((8 - kinds.shape[0], hours), F32)]), to_plane)
    spec = plane_spectrum(seen[rows : rows + kinds.shape[0]], kernels, forward)

    beside = moved(parcel, over_core)
    meta = jnp.concatenate([parcel[hours:], beside[hours:]], axis=1)
    metas = [meta] + [moved(meta, where) for where in SQUARE]
    dense = spread(first, parcel, beside, hours, rows)
    sums = dense[0] + sum(moved(value, where) for value, where in zip(dense[1:], SQUARE))
    sums = [sums, moved(sums, z_pair), moved(sums, z_middle)]
    high, low = plane_couple(first, metas, rows)
    pulled = plane_first(flags, sums, seen, seen_later, spec, mats)
    notes, kept, state = [], [], None
    for k in range(3):
        values = [pulled] + [moved(pulled, where) for where in SQUARE]
        mine, other = plane_mix(high, low, values)
        mixed = mine + moved(other, over_core)
        note = mixed[hours:]
        sums = [mixed, moved(mixed, z_pair), moved(mixed, z_middle)]
        two, mirror = moved(note, z_two), moved(note, z_mirror)
        rows_mine, rows_other = plane_rows(first, parcel, beside, values)
        kept.append(moved(rows_mine + moved(rows_other, over_core), from_plane))
        result = plane_step(flags, sums, two, mirror, pulled, spec, mats, state, k == 2)
        if k == 2:
            total_note, last = result
        else:
            total_note, pulled, state = result
        notes.append(total_note)
    copies = jnp.broadcast_to(last[None], (Z_ * X_ * Y_ * C_,) + last.shape)
    notes.append(jnp.sum(lax.all_to_all(copies, ("basin", "tm"), 0, 0, tiled=False), axis=0))
    return plane_finish(notes, kept, incidence, first_guess)


def solution(mesh):
    planes = dict(mesh.shape) == {"basin": Z_ * X_, "tm": Y_ * C_}
    in_specs = (
        P("basin", None, None),
        P("basin"),
        P("basin"),
        P(),
        P("basin", "tm"),
        P("basin", "tm"),
    )
    return jax.shard_map(
        plane_shards if planes else shards, mesh=mesh, in_specs=in_specs, out_specs=P("basin", "tm"), check_vma=False
    )
```

```python
import functools

import jax
import jax.numpy as jnp
import numpy as np
from jax import lax
from jax.experimental import pallas as pl
from jax.experimental.pallas import tpu as pltpu
from jax.sharding import PartitionSpec as P

F32 = jnp.float32
BF16 = jnp.bfloat16
HIGH = lax.Precision.HIGHEST
SPAN = 256
MIB = 1024 * 1024


def params(mib=16):
    return pltpu.CompilerParams(vmem_limit_bytes=mib * MIB)


def transforms():
    half = SPAN // 2
    freq = 2.0 * np.pi * (np.arange(half) + 0.5) / SPAN
    phase = np.arange(SPAN)[:, None] * freq[None, :]
    forward = np.concatenate([np.cos(phase), -np.sin(phase)], axis=1)
    inverse = forward.T * (2.0 / SPAN)
    return (
        jnp.asarray(forward, F32),
        jnp.asarray(inverse[:, :half], F32),
        jnp.asarray(inverse[:, half:], F32),
    )


def dot(a, b):
    return jnp.dot(a, b, preferred_element_type=F32)


def exact(a, b):
    return jnp.dot(a, b, precision=HIGH, preferred_element_type=F32)


def pieces(value, count):
    out = []
    for _ in range(count):
        piece = value.astype(BF16)
        out.append(piece)
        value = value - piece.astype(F32)
    return out


def pick(hot, value):
    return sum(dot(hot, piece) for piece in pieces(value, 3))


def prepare_kernel(inc_ref, field_ref, partial_ref, gram_ref):
    blocks, slots, width = inc_ref.shape
    rows = blocks * slots
    weights = inc_ref[...].astype(F32).astype(BF16)
    for b in range(blocks):
        value = field_ref[pl.ds(b * width, width), :]
        partial_ref[pl.ds(b * slots, slots), :] = pick(weights[b], value)
    flat = weights.reshape(rows, width)
    full = lax.dot_general(flat, flat, (((1,), (1,)), ((), ())), preferred_element_type=F32)
    row = lax.broadcasted_iota(jnp.int32, (rows, rows), 0)
    col = lax.broadcasted_iota(jnp.int32, (rows, rows), 1)
    own = jnp.where(row // slots == col // slots, full, 0.0)
    gram_ref[...] = jnp.sum(own.reshape(blocks, slots, rows), axis=0)


def prepare(incidence, field):
    blocks, slots, width = incidence.shape
    hours = field.shape[1]
    step = 8
    return pl.pallas_call(
        prepare_kernel,
        grid=(blocks // step,),
        in_specs=[
            pl.BlockSpec((step, slots, width), lambda i: (i, 0, 0)),
            pl.BlockSpec((step * width, hours), lambda i: (i, 0)),
        ],
        out_specs=[
            pl.BlockSpec((step * slots, hours), lambda i: (i, 0)),
            pl.BlockSpec((slots, step * slots), lambda i: (0, i)),
        ],
        out_shape=[
            jax.ShapeDtypeStruct((blocks * slots, hours), F32),
            jax.ShapeDtypeStruct((slots, blocks * slots), F32),
        ],
        compiler_params=params(56),
        name="prepare",
    )(incidence, field)


def table_kernel(gauge_ref, partial_ref, out_ref):
    slots = partial_ref.shape[0]
    rows = out_ref.shape[0]
    first = pl.program_id(0) * rows
    gauge = lax.broadcasted_iota(jnp.int32, (rows, slots), 0) + first
    hot = jnp.where(gauge_ref[...] == gauge, 1.0, 0.0).astype(BF16)
    out_ref[...] = pick(hot, partial_ref[...])


def table(row_gauge, partial, gauges):
    slots, hours = partial.shape
    step = 256
    return pl.pallas_call(
        table_kernel,
        grid=(gauges // step,),
        in_specs=[
            pl.BlockSpec((1, slots), lambda i: (0, 0)),
            pl.BlockSpec((slots, hours), lambda i: (0, 0)),
        ],
        out_specs=pl.BlockSpec((step, hours), lambda i: (i, 0)),
        out_shape=jax.ShapeDtypeStruct((gauges, hours), F32),
        compiler_params=params(56),
        name="table",
    )(row_gauge.reshape(1, slots), partial)


def couple_kernel(first_ref, lane_ref, sub_ref, gram_ref, high_ref, low_ref, near_ref):
    slots = gram_ref.shape[0]
    count = lane_ref.shape[1]
    rows, cols = high_ref.shape
    tile = 256
    first = first_ref[0]

    @pl.when(pl.program_id(0) == 0)
    def _():
        row = lax.broadcasted_iota(jnp.int32, (tile, tile), 0)
        col = lax.broadcasted_iota(jnp.int32, (tile, tile), 1)
        same = row // slots == col // slots
        mine = lax.broadcasted_iota(jnp.int32, (rows, tile), 0) + first

        def body(i, carry):
            here = pl.ds(pl.multiple_of(i * tile, tile), tile)
            block = jnp.concatenate([gram_ref[:, here]] * (tile // slots), axis=0)
            block = jnp.where(same, block, 0.0).astype(BF16)
            hot = jnp.where(lane_ref[:, here] == mine, 1.0, 0.0).astype(BF16)
            near_ref[:, here] = dot(hot, block)
            return carry

        lax.fori_loop(0, count // tile, body, 0)

    def chunk(i, total):
        here = pl.ds(pl.multiple_of(i * 1024, 1024), 1024)
        gauge = lax.broadcasted_iota(jnp.int32, (1024, cols), 1) + pl.program_id(0) * cols
        hot = jnp.where(sub_ref[here, :] == gauge, 1.0, 0.0).astype(BF16)
        near = near_ref[:, here]
        high = near.astype(BF16)
        low = (near - high.astype(F32)).astype(BF16)
        return total + dot(high, hot) + dot(low, hot)

    total = lax.fori_loop(0, count // 1024, chunk, jnp.zeros((rows, cols), F32))
    high, low = pieces(total, 2)
    high_ref[...] = high
    low_ref[...] = low


def couple(first, row_gauge, gram, rows, gauges):
    count = row_gauge.shape[0]
    step = 256
    return pl.pallas_call(
        couple_kernel,
        grid=(gauges // step,),
        in_specs=[
            pl.BlockSpec(memory_space=pltpu.SMEM),
            pl.BlockSpec((1, count), lambda i: (0, 0)),
            pl.BlockSpec((count, 1), lambda i: (0, 0)),
            pl.BlockSpec(gram.shape, lambda i: (0, 0)),
        ],
        out_specs=[pl.BlockSpec((rows, step), lambda i: (0, i))] * 2,
        out_shape=[jax.ShapeDtypeStruct((rows, gauges), BF16)] * 2,
        scratch_shapes=[pltpu.VMEM((rows, count), F32)],
        compiler_params=params(56),
        name="couple",
    )(first, row_gauge.reshape(1, count), row_gauge.reshape(count, 1), gram)


def mix_kernel(high_ref, low_ref, value_ref, out_ref):
    high = high_ref[...]
    low = low_ref[...]
    one, two, three = pieces(value_ref[...], 3)
    out_ref[...] = (dot(high, three) + dot(low, two)) + (dot(high, two) + dot(low, one)) + dot(high, one)


def mix(high, low, value):
    return pl.pallas_call(
        mix_kernel,
        out_shape=jax.ShapeDtypeStruct((high.shape[0], value.shape[1]), F32),
        compiler_params=params(56),
        name="mix",
    )(high, low, value)


def spectrum_kernel(class_ref, kernels_ref, forward_ref, out_ref):
    rows = class_ref.shape[0]
    classes, taps = kernels_ref.shape
    kind = lax.broadcasted_iota(jnp.int32, (rows, classes), 1)
    hot = jnp.where(class_ref[...] == kind, 1.0, 0.0)
    out_ref[...] = exact(exact(hot, kernels_ref[...]), forward_ref[pl.ds(0, taps), :])


def spectrum(gauge_kernel, kernels, forward):
    rows = gauge_kernel.shape[0]
    return pl.pallas_call(
        spectrum_kernel,
        out_shape=jax.ShapeDtypeStruct((rows, SPAN), F32),
        compiler_params=params(56),
        name="spectrum",
    )(gauge_kernel.reshape(rows, 1), kernels, forward)


def delayed(before, here, after, spec, forward, inverse_last):
    rows, half = here.shape
    stacked = jnp.concatenate(
        [jnp.concatenate([before, here], axis=1), jnp.concatenate([here, after], axis=1)], axis=0
    )
    waves = exact(stacked, forward)
    real, imag = waves[:, :half], waves[:, half:]
    kr = jnp.concatenate([spec[:, :half]] * 2, axis=0)
    ki = jnp.concatenate([spec[:, half:]] * 2, axis=0)
    turned = jnp.concatenate([real * kr - imag * ki, real * ki + imag * kr], axis=1)
    out = exact(turned, inverse_last)
    return out[:rows], out[rows:]


def advanced(here, after, spec, forward, inverse_first):
    half = here.shape[1]
    waves = exact(jnp.concatenate([here, after], axis=1), forward)
    real, imag = waves[:, :half], waves[:, half:]
    kr, ki = spec[:, :half], spec[:, half:]
    turned = jnp.concatenate([real * kr + imag * ki, imag * kr - real * ki], axis=1)
    return exact(turned, inverse_first)


def lanes(a, b):
    return jnp.sum(a * b, axis=0, keepdims=True)


def total(ref, row):
    return jnp.sum(ref[row : row + 1, :], axis=1, keepdims=True)


def ratios(ref):
    square = total(ref, 0)
    alpha = jnp.sqrt(square)
    beta = jnp.sqrt(jnp.maximum(total(ref, 1) / square - 2.0 * total(ref, 2) + square, 0.0))
    return alpha, beta


def first_kernel(
    more_ref, sums_ref, observed_ref, spec_ref, forward_ref, first_ref, last_ref, out_ref, note_ref
):
    rows, half = observed_ref.shape[0] // 2, observed_ref.shape[1]
    spec, forward = spec_ref[...], forward_ref[...]
    before, here, after = (sums_ref[pl.ds(i * rows, rows), :] for i in range(3))
    now, later = delayed(before, here, after, spec, forward, last_ref[...])
    start = observed_ref[pl.ds(0, rows), :] - now
    start_later = (observed_ref[pl.ds(rows, rows), :] - later) * more_ref[0]
    out_ref[...] = advanced(start, start_later, spec, forward, first_ref[...])
    note_ref[...] = jnp.concatenate([lanes(start, start), jnp.zeros((7, half), F32)], axis=0)


def first_step(more, sums, observed, spec, mats):
    rows, half = spec.shape[0], observed.shape[1]
    return pl.pallas_call(
        first_kernel,
        in_specs=[pl.BlockSpec(memory_space=pltpu.SMEM)] + [pl.BlockSpec(memory_space=pltpu.VMEM)] * 6,
        out_shape=[jax.ShapeDtypeStruct((rows, half), F32), jax.ShapeDtypeStruct((8, half), F32)],
        compiler_params=params(56),
        name="first_step",
    )(more, sums, observed, spec, *mats)


def step_kernel(
    opening,
    final,
    more_ref,
    note_ref,
    sums_ref,
    spec_ref,
    forward_ref,
    first_ref,
    last_ref,
    pulled_ref,
    *refs,
):
    if opening:
        state_ref = None
    else:
        state_ref, *refs = refs
    if final:
        (out_note_ref,) = refs
    else:
        new_ref, out_ref, out_note_ref = refs
    rows, half = pulled_ref.shape
    spec, forward = spec_ref[...], forward_ref[...]
    if opening:
        scale = 1.0 / jnp.sqrt(total(note_ref, 0))
        along = sums_ref[...] * scale
        new_s, new_su = along, along
        new_zu = pulled_ref[...] * scale
        new_z = new_zu
    else:
        alpha, beta = ratios(note_ref)
        a, b, g = 1.0 / (alpha * beta), alpha / beta, beta / alpha
        wide = pl.ds(0, 3 * rows), pl.ds(3 * rows, 3 * rows)
        new_su = sums_ref[...] * a - state_ref[wide[1], :] * b
        new_s = new_su - state_ref[wide[0], :] * g
        new_zu = pulled_ref[...] * a - state_ref[pl.ds(7 * rows, rows), :] * b
        new_z = new_zu - state_ref[pl.ds(6 * rows, rows), :] * g
    before, here, after = (new_s[i * rows : (i + 1) * rows] for i in range(3))
    now, later = delayed(before, here, after, spec, forward, last_ref[...])
    out_note_ref[...] = jnp.concatenate(
        [lanes(new_z, here), lanes(now, now), lanes(new_zu, here), jnp.zeros((5, half), F32)], axis=0
    )
    if not final:
        new_ref[pl.ds(0, 3 * rows), :] = new_s
        new_ref[pl.ds(3 * rows, 3 * rows), :] = new_su
        new_ref[pl.ds(6 * rows, rows), :] = new_z
        new_ref[pl.ds(7 * rows, rows), :] = new_zu
        out_ref[...] = advanced(now, later * more_ref[0], spec, forward, first_ref[...])


def next_step(more, note, sums, spec, mats, pulled, state, final):
    rows, half = pulled.shape
    opening = state is None
    shapes = [
        jax.ShapeDtypeStruct((8 * rows, half), F32),
        jax.ShapeDtypeStruct((rows, half), F32),
        jax.ShapeDtypeStruct((8, half), F32),
    ]
    args = [more, note, sums, spec, *mats, pulled] + ([] if opening else [state])
    return pl.pallas_call(
        functools.partial(step_kernel, opening, final),
        in_specs=[pl.BlockSpec(memory_space=pltpu.SMEM)]
        + [pl.BlockSpec(memory_space=pltpu.VMEM)] * (len(args) - 1),
        out_shape=shapes[2:] if final else shapes,
        compiler_params=params(56),
        name="next_step",
    )(*args)


def weights_of(notes):
    start = jnp.sqrt(total(notes[0], 0))
    zero = jnp.zeros_like(start)
    units = [1.0 / start, zero, zero]
    z, zu = list(units), list(units)
    phibar = start
    alpha, beta = ratios(notes[1])
    rhobar = alpha
    w = [value / alpha for value in z]
    result = [zero] * 3
    steps = len(notes) - 1
    for k in range(steps):
        rho = jnp.sqrt(rhobar * rhobar + beta * beta)
        cosine, sine = rhobar / rho, beta / rho
        phi, phibar = cosine * phibar, sine * phibar
        result = [r + phi / rho * value for r, value in zip(result, w)]
        if k < steps - 1:
            a, b, g = 1.0 / (alpha * beta), alpha / beta, beta / alpha
            zu = [(a if i == k + 1 else 0.0) - b * value for i, value in enumerate(zu)]
            z = [value - g * old for value, old in zip(zu, z)]
            alpha, beta = ratios(notes[k + 2])
            theta = sine * alpha
            rhobar = -cosine * alpha
            w = [value / alpha - theta / rho * old for value, old in zip(z, w)]
    return result


def finish_kernel(n0, n1, n2, n3, gauge_ref, q0, q1, q2, inc_ref, field_ref, out_ref, rows_ref):
    blocks, slots, width = inc_ref.shape
    count = rows_ref.shape[0]
    gauges = q0.shape[0]
    step = pl.program_id(0)

    @pl.when(step == 0)
    def _():
        e0, e1, e2 = weights_of([n0, n1, n2, n3])
        width_ = 512

        def body(i, value):
            here = pl.ds(pl.multiple_of(i * width_, width_), width_)
            mixed = q0[here, :] * e0 + q1[here, :] * e1 + q2[here, :] * e2
            gauge = lax.broadcasted_iota(jnp.int32, (count, width_), 1) + i * width_
            hot = jnp.where(gauge_ref[...] == gauge, 1.0, 0.0).astype(BF16)
            return value + pick(hot, mixed)

        rows_ref[...] = lax.fori_loop(0, gauges // width_, body, jnp.zeros(rows_ref.shape, F32))

    weights = inc_ref[...].astype(F32).astype(BF16)
    for b in range(blocks):
        here = pl.ds(b * width, width)
        rows = rows_ref[pl.ds(pl.multiple_of((step * blocks + b) * slots, slots), slots), :]
        added = sum(
            lax.dot_general(weights[b], piece, (((0,), (0,)), ((), ())), preferred_element_type=F32)
            for piece in pieces(rows, 3)
        )
        out_ref[here, :] = field_ref[here, :] + added


def finish(notes, row_gauge, gathered, incidence, field):
    blocks, slots, width = incidence.shape
    hours = field.shape[1]
    count = row_gauge.shape[0]
    step = 8
    whole = lambda shape: pl.BlockSpec(shape, lambda i: (0, 0))
    return pl.pallas_call(
        finish_kernel,
        grid=(blocks // step,),
        in_specs=[whole(n.shape) for n in notes]
        + [whole((count, 1))]
        + [whole(q.shape) for q in gathered]
        + [
            pl.BlockSpec((step, slots, width), lambda i: (i, 0, 0)),
            pl.BlockSpec((step * width, hours), lambda i: (i, 0)),
        ],
        out_specs=pl.BlockSpec((step * width, hours), lambda i: (i, 0)),
        out_shape=jax.ShapeDtypeStruct(field.shape, F32),
        scratch_shapes=[pltpu.VMEM((count, hours), F32)],
        compiler_params=params(56),
        name="finish",
    )(*notes, row_gauge.reshape(count, 1), *gathered, incidence, field)


def shifted(value, axis, by):
    devices = lax.axis_size(axis)
    pairs = [(i, i + by) for i in range(devices) if 0 <= i + by < devices]
    return lax.ppermute(value, axis, pairs)


def window(value):
    return jnp.concatenate([shifted(value, "tm", 1), value, shifted(value, "tm", -1)], axis=0)


def gathered_rows(value):
    owners = lax.axis_size("basin")
    copies = jnp.broadcast_to(value[None], (owners,) + value.shape)
    return lax.all_to_all(copies, "basin", 0, 0, tiled=False)


def over_hours(note):
    blocks = lax.axis_size("tm")
    result = note
    for by in range(1, blocks):
        result = result + lax.ppermute(note, "tm", [(i, (i + by) % blocks) for i in range(blocks)])
    return result


def shards(incidence, row_gauge, gauge_kernel, kernels, observed, first_guess):
    owners = lax.axis_size("basin")
    rows, hours = observed.shape
    gauges = rows * owners
    mats = transforms()
    spec = spectrum(gauge_kernel, kernels, mats[0])
    more = (lax.axis_index("tm") < lax.axis_size("tm") - 1).astype(F32).reshape(1)
    partial, gram = prepare(incidence, first_guess)
    all_gram = lax.all_gather(gram, "basin", axis=1, tiled=True)
    all_rows = lax.all_gather(row_gauge, "basin", axis=0, tiled=True)
    dense = table(row_gauge, partial, gauges).reshape(owners, rows, hours)
    sums = jnp.sum(lax.all_to_all(dense, "basin", 0, 0, tiled=False), axis=0)
    both = jnp.concatenate([observed, shifted(observed, "tm", -1)], axis=0)
    first = (lax.axis_index("basin") * rows).astype(jnp.int32).reshape(1)
    high, low = couple(first, all_rows, all_gram, rows, gauges)

    pulled, note = first_step(more, window(sums), both, spec, mats)
    notes, kept, state = [], [], None
    for k in range(3):
        everyone = gathered_rows(jnp.concatenate([pulled, note], axis=0))
        value = everyone[:, :rows].reshape(gauges, hours)
        notes.append(over_hours(jnp.sum(everyone[:, rows:], axis=0)))
        kept.append(value)
        around = window(mix(high, low, value))
        final = k == 2
        result = next_step(more, notes[-1], around, spec, mats, pulled, state, final)
        if final:
            (note,) = result
        else:
            state, pulled, note = result
    notes.append(over_hours(jnp.sum(gathered_rows(note), axis=0)))
    return finish(notes, row_gauge, kept, incidence, first_guess)


Z_, X_, Y_, C_ = 4, 2, 2, 2
NOTE = 8


def device(z, x, y, c):
    return (z * X_ + x) * (Y_ * C_) + y * C_ + c


def moved(value, where):
    pairs = []
    for z, x, y, c in np.ndindex(Z_, X_, Y_, C_):
        target = where(z, x, y, c)
        if target is not None:
            pairs.append((device(z, x, y, c), device(*target)))
    return lax.ppermute(value, ("basin", "tm"), pairs)


def to_plane(z, x, y, c):
    return 2 * y + c, x, z & 1, z >> 1


def to_plane_before(z, x, y, c):
    t = 2 * y + c
    return (t - 1, x, z & 1, z >> 1) if t else None


def from_plane(z, x, y, c):
    return 2 * c + y, x, z >> 1, z & 1


def over_x(z, x, y, c):
    return z, 1 - x, y, c


def over_y(z, x, y, c):
    return z, x, 1 - y, c


def over_xy(z, x, y, c):
    return z, 1 - x, 1 - y, c


def over_core(z, x, y, c):
    return z, x, y, 1 - c


def z_pair(z, x, y, c):
    return z ^ 1, x, y, c


def z_middle(z, x, y, c):
    return (3 - z, x, y, c) if z in (1, 2) else None


def z_two(z, x, y, c):
    return z ^ 2, x, y, c


def z_mirror(z, x, y, c):
    return 3 - z, x, y, c


SQUARE = (over_x, over_y, over_xy)


def split_constant(value):
    out = []
    for _ in range(3):
        piece = value.astype(jnp.bfloat16)
        out.append(jnp.asarray(piece))
        value = value - piece.astype(np.float64)
    return out


def turned_transforms():
    half = SPAN // 2
    freq = 2.0 * np.pi * (np.arange(half) + 0.5) / SPAN
    phase = freq[:, None] * np.arange(SPAN)[None, :]
    forward = np.concatenate([np.cos(phase), -np.sin(phase)], axis=0)
    inverse = forward.T * (2.0 / SPAN)
    return split_constant(forward), split_constant(inverse[:half]), split_constant(inverse[half:])


def product(mats, value, order):
    parts = pieces(value, order)
    result = None
    for level in reversed(range(order)):
        for i in range(level + 1):
            term = dot(mats[i][...], parts[level - i])
            result = term if result is None else result + term
    return result


def turn(waves, spec, sign):
    half = waves.shape[0] // 2
    real, imag = waves[:half], waves[half:]
    kr, ki = spec[:half], spec[half:] * sign
    return jnp.concatenate([real * kr - imag * ki, real * ki + imag * kr], axis=0)


def plane_delayed(before, here, after, spec, forward, last, order):
    out = []
    for pair in ((before, here), (here, after)):
        waves = product(forward, jnp.concatenate(pair, axis=0), order)
        out.append(product(last, turn(waves, spec, 1.0), order))
    return out


def plane_advanced(here, after, spec, forward, first, order):
    waves = product(forward, jnp.concatenate([here, after], axis=0), order)
    return product(first, turn(waves, spec, -1.0), order)


def describe_kernel(inc_ref, gauge_ref, kind_ref, out_ref):
    blocks, slots, width = inc_ref.shape
    tile = 8
    rows = tile * slots
    weights = inc_ref[...].astype(F32).astype(BF16)
    row = lax.broadcasted_iota(jnp.int32, (rows, rows), 0)
    col = lax.broadcasted_iota(jnp.int32, (rows, rows), 1)
    same = row // slots == col // slots
    for i in range(blocks // tile):
        flat = weights[i * tile : (i + 1) * tile].reshape(rows, width)
        full = lax.dot_general(flat, flat, (((1,), (1,)), ((), ())), preferred_element_type=F32)
        own = jnp.where(same, full, 0.0)
        out_ref[pl.ds(0, slots), pl.ds(i * rows, rows)] = jnp.sum(own.reshape(tile, slots, rows), axis=0)
    kinds = kind_ref.shape[1]
    out_ref[pl.ds(slots, 8), :] = jnp.concatenate(
        [
            gauge_ref[...].astype(F32),
            jnp.concatenate(
                [kind_ref[...].astype(F32), jnp.zeros((1, blocks * slots - kinds), F32)], axis=1
            ),
            jnp.zeros((6, blocks * slots), F32),
        ],
        axis=0,
    )


def describe(incidence, row_gauge, gauge_kernel):
    blocks, slots, _ = incidence.shape
    count = blocks * slots
    return pl.pallas_call(
        describe_kernel,
        out_shape=jax.ShapeDtypeStruct((slots + 8, count), F32),
        compiler_params=params(),
        name="describe",
    )(incidence, row_gauge.reshape(1, count), gauge_kernel.reshape(1, gauge_kernel.shape[0]))


def send_kernel(inc_ref, field_ref, out_ref):
    blocks, slots, width = inc_ref.shape
    weights = inc_ref[...].astype(F32).astype(BF16)
    parts = []
    for b in range(blocks):
        parts.append(pick(weights[b], field_ref[pl.ds(b * width, width), :]))
    out_ref[...] = jnp.transpose(jnp.concatenate(parts, axis=0))


def send(incidence, field):
    blocks, slots, width = incidence.shape
    hours = field.shape[1]
    step = 8
    return pl.pallas_call(
        send_kernel,
        grid=(blocks // step,),
        in_specs=[
            pl.BlockSpec((step, slots, width), lambda i: (i, 0, 0)),
            pl.BlockSpec((step * width, hours), lambda i: (i, 0)),
        ],
        out_specs=pl.BlockSpec((hours, step * slots), lambda i: (0, i)),
        out_shape=jax.ShapeDtypeStruct((hours, blocks * slots), F32),
        compiler_params=params(),
        name="send",
    )(incidence, field)


def hot_rows(gauge, first, rows):
    mine = (lax.broadcasted_iota(jnp.int32, (rows, gauge.shape[1]), 0) + first).astype(F32)
    return jnp.where(gauge == mine, 1.0, 0.0).astype(BF16)


def spread_kernel(first_ref, mine_ref, other_ref, meta_ref, meta_other_ref, *out_refs):
    rows = out_refs[0].shape[1]
    where = meta_ref.shape[0] - 8
    for m, out_ref in enumerate(out_refs):
        result = None
        for ref, meta in ((mine_ref, meta_ref), (other_ref, meta_other_ref)):
            hot = hot_rows(meta[where : where + 1, :], first_ref[m], rows)
            for piece in reversed(pieces(ref[...], 3)):
                term = lax.dot_general(
                    piece, hot, (((1,), (1,)), ((), ())), preferred_element_type=F32
                )
                result = term if result is None else result + term
        out_ref[...] = result


def spread(first, parcels, metas, rows):
    hours = parcels[0].shape[0]
    return pl.pallas_call(
        spread_kernel,
        in_specs=[pl.BlockSpec(memory_space=pltpu.SMEM)] + [pl.BlockSpec(memory_space=pltpu.VMEM)] * 4,
        out_shape=[jax.ShapeDtypeStruct((hours, rows), F32)] * 4,
        compiler_params=params(),
        name="spread",
    )(first, *parcels, *metas)


def plane_couple_kernel(
    owners, first_ref, a_ref, b_ref, c_ref, d_ref, high_ref, low_ref, total_ref, meta_ref
):
    height, double = a_ref.shape
    slots = height - 8
    count = double // 2
    cols, rows = high_ref.shape
    part = cols // len(owners)
    tile = 256
    for i, ref in enumerate((a_ref, b_ref, c_ref, d_ref)):
        for j in range(2):
            meta_ref[2 * i + j] = ref[:, j * count : (j + 1) * count]
    row = lax.broadcasted_iota(jnp.int32, (tile, tile), 0)
    col = lax.broadcasted_iota(jnp.int32, (tile, tile), 1)
    same = row // slots == col // slots
    total_ref[...] = jnp.zeros_like(total_ref)

    def body(i, carry):
        gauge = meta_ref[i, slots : slots + 1, :]
        near = []
        for j in range(count // tile):
            here = slice(j * tile, (j + 1) * tile)
            block = jnp.concatenate([meta_ref[i, :slots, here]] * (tile // slots), axis=0)
            block = jnp.where(same, block, 0.0).astype(BF16)
            mine = jnp.concatenate(
                [hot_rows(gauge[:, here], first_ref[4 + h], rows // 2) for h in range(2)], axis=0
            )
            near.append(
                lax.dot_general(block, mine, (((1,), (1,)), ((), ())), preferred_element_type=F32)
            )
        near = jnp.concatenate(near, axis=0)
        high = near.astype(BF16)
        rest = near - high.astype(F32)
        hot = jnp.concatenate([hot_rows(gauge, first_ref[m], part) for m in owners], axis=0)
        total_ref[...] += dot(hot, high)

        @pl.when(jnp.max(jnp.abs(rest)) > 0.0)
        def _():
            total_ref[...] += dot(hot, rest.astype(BF16))

        return carry

    lax.fori_loop(0, 8, body, 0)
    high, low = pieces(total_ref[...], 2)
    high_ref[...] = high
    low_ref[...] = low


def plane_couple(first, metas, rows, owners):
    height, double = metas[0].shape
    cols = len(owners) * rows
    return pl.pallas_call(
        functools.partial(plane_couple_kernel, owners),
        in_specs=[pl.BlockSpec(memory_space=pltpu.SMEM)] + [pl.BlockSpec(memory_space=pltpu.VMEM)] * 4,
        out_shape=[jax.ShapeDtypeStruct((cols, 2 * rows), BF16)] * 2,
        scratch_shapes=[
            pltpu.VMEM((cols, 2 * rows), F32),
            pltpu.VMEM((8, height, double // 2), F32),
        ],
        compiler_params=params(),
        name="plane_couple",
        cost_estimate=pl.CostEstimate(
            flops=2 * 8 * double * cols * rows, bytes_accessed=2_000_000, transcendentals=0
        ),
    )(first, *metas)


def plane_mix_kernel(high0_ref, low0_ref, high1_ref, low1_ref, a_ref, b_ref, c_ref, d_ref, mine_ref, other_ref):
    refs = (a_ref, b_ref, c_ref, d_ref)
    height, rows = a_ref.shape
    hours = height - NOTE
    result = None
    for pair, high_ref, low_ref in ((refs[:2], high0_ref, low0_ref), (refs[2:], high1_ref, low1_ref)):
        value = jnp.concatenate([ref[pl.ds(0, hours), :] for ref in pair], axis=1)
        one, two = pieces(value, 2)
        high, low = high_ref[...], low_ref[...]
        term = (dot(two, high) + dot(one, low)) + dot(one, high)
        result = term if result is None else result + term
    note = sum(ref[pl.ds(hours, NOTE), :] for ref in refs)
    mine_ref[pl.ds(0, hours), :] = result[:, :rows]
    other_ref[pl.ds(0, hours), :] = result[:, rows:]
    mine_ref[pl.ds(hours, NOTE), :] = note
    other_ref[pl.ds(hours, NOTE), :] = note


def plane_mix(coupling, values):
    return pl.pallas_call(
        plane_mix_kernel,
        out_shape=[jax.ShapeDtypeStruct(values[0].shape, F32)] * 2,
        compiler_params=params(),
        name="plane_mix",
    )(*coupling, *values)


def plane_rows_kernel(first_ref, mine_ref, other_ref, a_ref, b_ref, c_ref, d_ref, out_mine_ref, out_other_ref):
    height, rows = a_ref.shape
    hours = height - NOTE
    where = mine_ref.shape[0] - 8
    for ref, out_ref in ((mine_ref, out_mine_ref), (other_ref, out_other_ref)):
        gauge = ref[where : where + 1, :]
        result = None
        for m, value_ref in enumerate((a_ref, b_ref, c_ref, d_ref)):
            hot = hot_rows(gauge, first_ref[m], rows)
            for piece in reversed(pieces(value_ref[pl.ds(0, hours), :], 2)):
                term = dot(piece, hot)
                result = term if result is None else result + term
        out_ref[...] = result


def plane_rows(first, mine, other, values):
    hours = values[0].shape[0] - NOTE
    slots = mine.shape[1]
    return pl.pallas_call(
        plane_rows_kernel,
        in_specs=[pl.BlockSpec(memory_space=pltpu.SMEM)] + [pl.BlockSpec(memory_space=pltpu.VMEM)] * 6,
        out_shape=[jax.ShapeDtypeStruct((hours, slots), F32)] * 2,
        compiler_params=params(),
        name="plane_rows",
        cost_estimate=pl.CostEstimate(flops=1_000_000_000, bytes_accessed=2_000_000, transcendentals=0),
    )(first, mine, other, *values)


def plane_spectrum_kernel(class_ref, kernels_ref, f0_ref, f1_ref, f2_ref, out_ref):
    classes, taps = kernels_ref.shape
    kind = class_ref[class_ref.shape[0] - 7 : class_ref.shape[0] - 6, : out_ref.shape[1]]
    hot = jnp.where(
        lax.broadcasted_iota(jnp.int32, (classes, kind.shape[1]), 0).astype(F32) == kind, 1.0, 0.0
    ).astype(BF16)
    chosen = None
    for piece in reversed(pieces(jnp.transpose(kernels_ref[...]), 3)):
        term = dot(piece, hot)
        chosen = term if chosen is None else chosen + term
    mats = [ref[:, :taps] for ref in (f0_ref, f1_ref, f2_ref)]
    out_ref[...] = product(mats, chosen, 3)


def plane_spectrum(meta, kernels, forward, rows):
    return pl.pallas_call(
        plane_spectrum_kernel,
        out_shape=jax.ShapeDtypeStruct((SPAN, rows), F32),
        compiler_params=params(),
        name="plane_spectrum",
    )(meta, kernels, *forward)


def sides(even, pair, middle):
    return jnp.where(even, middle, pair), jnp.where(even, pair, middle)


def plane_first_kernel(
    flag_ref, here_ref, pair_ref, middle_ref, seen_ref, seen_later_ref, spec_ref, *refs
):
    *mats, out_ref = refs
    forward, first, last = mats[0:3], mats[3:6], mats[6:9]
    hours, rows = here_ref.shape
    spec = spec_ref[...]
    before, after = sides(flag_ref[0] > 0.5, pair_ref[...], middle_ref[...])
    now, later = plane_delayed(before, here_ref[...], after, spec, forward, last, 3)
    start = jnp.transpose(seen_ref[...]) - now
    start_later = (jnp.transpose(seen_later_ref[...]) - later) * flag_ref[1]
    out_ref[pl.ds(0, hours), :] = plane_advanced(start, start_later, spec, forward, first, 3)
    out_ref[pl.ds(hours, NOTE), :] = jnp.concatenate(
        [lanes(start, start), jnp.zeros((NOTE - 1, rows), F32)], axis=0
    )


def plane_first(flags, sums, seen, seen_later, spec, mats):
    hours, rows = sums[0].shape
    args = [flags, *sums, seen, seen_later, spec, *mats]
    return pl.pallas_call(
        plane_first_kernel,
        in_specs=[pl.BlockSpec(memory_space=pltpu.SMEM)]
        + [pl.BlockSpec(memory_space=pltpu.VMEM)] * (len(args) - 1),
        out_shape=jax.ShapeDtypeStruct((hours + NOTE, rows), F32),
        compiler_params=params(),
        name="plane_first",
    )(*args)


def plane_step_kernel(opening, final, flag_ref, here_ref, pair_ref, middle_ref, two_ref, mirror_ref, pulled_ref, spec_ref, *refs):
    mats, refs = refs[:9], refs[9:]
    forward, first, last = mats[0:3], mats[3:6], mats[6:9]
    if not opening:
        state_ref, *refs = refs
    if final:
        total_ref, out_ref = refs
    else:
        total_ref, out_ref, new_ref = refs
    height, rows = pulled_ref.shape
    hours = height - NOTE
    tail, body = pl.ds(hours, NOTE), pl.ds(0, hours)
    total_ref[...] = (here_ref[tail, :] + pair_ref[tail, :]) + (two_ref[...] + mirror_ref[...])
    spec = spec_ref[...]
    pulled = pulled_ref[body, :]
    sums = [ref[body, :] for ref in (here_ref, pair_ref, middle_ref)]
    if opening:
        scale = 1.0 / jnp.sqrt(total(total_ref, 0))
        new_su = [value * scale for value in sums]
        new_s = new_su
        new_zu = pulled * scale
        new_z = new_zu
    else:
        alpha, beta = ratios(total_ref)
        a, b, g = 1.0 / (alpha * beta), alpha / beta, beta / alpha
        old = lambda i: state_ref[pl.ds(i * hours, hours), :]
        new_su = [value * a - old(3 + i) * b for i, value in enumerate(sums)]
        new_s = [value - old(i) * g for i, value in enumerate(new_su)]
        new_zu = pulled * a - old(7) * b
        new_z = new_zu - old(6) * g
    here = new_s[0]
    before, after = sides(flag_ref[0] > 0.5, new_s[1], new_s[2])
    now, later = plane_delayed(before, here, after, spec, forward, last, 2)
    note = jnp.concatenate(
        [lanes(new_z, here), lanes(now, now), lanes(new_zu, here), jnp.zeros((NOTE - 3, rows), F32)],
        axis=0,
    )
    if final:
        out_ref[...] = note[:, : rows // 2] + note[:, rows // 2 :]
    else:
        for i, value in enumerate(new_s + new_su + [new_z, new_zu]):
            new_ref[pl.ds(i * hours, hours), :] = value
        out_ref[body, :] = plane_advanced(now, later * flag_ref[1], spec, forward, first, 2)
        out_ref[tail, :] = note


def plane_step(flags, sums, two, mirror, pulled, spec, mats, state, final):
    height, rows = pulled.shape
    hours = height - NOTE
    opening = state is None
    args = [flags, *sums, two, mirror, pulled, spec, *mats] + ([] if opening else [state])
    out = [jax.ShapeDtypeStruct((NOTE, rows), F32)]
    if final:
        out += [jax.ShapeDtypeStruct((NOTE, rows // 2), F32)]
    else:
        out += [jax.ShapeDtypeStruct((height, rows), F32), jax.ShapeDtypeStruct((8 * hours, rows), F32)]
    return pl.pallas_call(
        functools.partial(plane_step_kernel, opening, final),
        in_specs=[pl.BlockSpec(memory_space=pltpu.SMEM)]
        + [pl.BlockSpec(memory_space=pltpu.VMEM)] * (len(args) - 1),
        out_shape=out,
        compiler_params=params(),
        name="plane_step",
    )(*args)


def plane_finish_kernel(n0, n1, n2, n3, q0, q1, q2, inc_ref, field_ref, out_ref, rows_ref):
    blocks, slots, width = inc_ref.shape
    step = pl.program_id(0)

    @pl.when(step == 0)
    def _():
        e0, e1, e2 = weights_of([n0, n1, n2, n3])
        rows_ref[...] = jnp.transpose(q0[...] * e0 + q1[...] * e1 + q2[...] * e2)

    weights = inc_ref[...].astype(F32).astype(BF16)
    for b in range(blocks):
        here = pl.ds(b * width, width)
        rows = rows_ref[pl.ds(pl.multiple_of((step * blocks + b) * slots, slots), slots), :]
        added = sum(
            lax.dot_general(weights[b], piece, (((0,), (0,)), ((), ())), preferred_element_type=F32)
            for piece in pieces(rows, 2)
        )
        out_ref[here, :] = field_ref[here, :] + added


def plane_finish(notes, rows, incidence, field):
    blocks, slots, width = incidence.shape
    hours = field.shape[1]
    step = 8
    whole = lambda shape: pl.BlockSpec(shape, lambda i: (0, 0))
    return pl.pallas_call(
        plane_finish_kernel,
        grid=(blocks // step,),
        in_specs=[whole(n.shape) for n in notes]
        + [whole(q.shape) for q in rows]
        + [
            pl.BlockSpec((step, slots, width), lambda i: (i, 0, 0)),
            pl.BlockSpec((step * width, hours), lambda i: (i, 0)),
        ],
        out_specs=pl.BlockSpec((step * width, hours), lambda i: (i, 0)),
        out_shape=jax.ShapeDtypeStruct(field.shape, F32),
        scratch_shapes=[pltpu.VMEM((blocks * slots, hours), F32)],
        compiler_params=params(),
        name="plane_finish",
    )(*notes, *rows, incidence, field)


def plane_shards(incidence, row_gauge, gauge_kernel, kernels, observed, first_guess):
    rows, hours = observed.shape
    basin, tm = lax.axis_index("basin"), lax.axis_index("tm")
    z, x, y, c = basin // X_, basin % X_, tm // C_, tm % C_
    place = 2 * y + x
    first = jnp.stack([4 * c + (place ^ m) for m in range(4)] + [4 * c + place, 4 * (1 - c) + place])
    first = (first * rows).astype(jnp.int32)
    flags = jnp.stack([1 - z % 2, (z < Z_ - 1).astype(z.dtype)]).astype(F32)
    forward, inverse_first, inverse_last = turned_transforms()
    mats = [*forward, *inverse_first, *inverse_last]

    meta = describe(incidence, row_gauge, gauge_kernel)
    meta, field = lax.optimization_barrier((meta, first_guess))
    meta = moved(meta, to_plane)
    parcel = moved(send(incidence, field), to_plane)
    metas = [meta, moved(meta, over_core)]
    both = jnp.concatenate(metas, axis=1)
    around = [both] + [moved(both, where) for where in SQUARE]
    spec = plane_spectrum(meta, kernels, forward, rows)
    seen, parcel, around, spec = lax.optimization_barrier((observed, parcel, around, spec))
    seen_later = moved(seen, to_plane_before)
    seen = moved(seen, to_plane)

    dense = spread(first, [parcel, moved(parcel, over_core)], metas, rows)
    sums = dense[0] + sum(moved(value, where) for value, where in zip(dense[1:], SQUARE))
    sums = [sums, moved(sums, z_pair), moved(sums, z_middle)]
    coupling = plane_couple(first, around, rows, (0, 1))
    coupling, sums = lax.optimization_barrier((coupling, sums))
    coupling = [*coupling, *plane_couple(first, around, rows, (2, 3))]
    pulled = plane_first(flags, sums, seen, seen_later, spec, mats)
    notes, kept, state, values = [], [], None, None

    def ship(values):
        mine, other = plane_rows(first, *metas, values)
        return moved(mine + moved(other, over_core), from_plane)

    for k in range(3):
        if k:
            pulled, values = lax.optimization_barrier((pulled, values))
            kept.append(ship(values))
        values = [pulled] + [moved(pulled, where) for where in SQUARE]
        mine, other = plane_mix(coupling, values)
        mixed = mine + moved(other, over_core)
        note = mixed[hours:]
        sums = [mixed, moved(mixed, z_pair), moved(mixed, z_middle)]
        two, mirror = moved(note, z_two), moved(note, z_mirror)
        result = plane_step(flags, sums, two, mirror, pulled, spec, mats, state, k == 2)
        if k == 2:
            mixed, values = lax.optimization_barrier((mixed, values))
            kept.append(ship(values))
            total_note, last = result
            last, kept[1] = lax.optimization_barrier((last, kept[1]))
        else:
            total_note, pulled, state = result
        if k == 1:
            pulled, kept[0] = lax.optimization_barrier((pulled, kept[0]))
        notes.append(total_note)
    copies = jnp.broadcast_to(last[None], (Z_ * X_ * Y_ * C_,) + last.shape)
    notes.append(jnp.sum(lax.all_to_all(copies, ("basin", "tm"), 0, 0, tiled=False), axis=0))
    return plane_finish(notes, kept, incidence, first_guess)


def solution(mesh):
    planes = dict(mesh.shape) == {"basin": Z_ * X_, "tm": Y_ * C_}
    in_specs = (
        P("basin", None, None),
        P("basin"),
        P("basin"),
        P(),
        P("basin", "tm"),
        P("basin", "tm"),
    )
    return jax.shard_map(
        plane_shards if planes else shards, mesh=mesh, in_specs=in_specs, out_specs=P("basin", "tm"), check_vma=False
    )
```

```python
import functools

import jax
import jax.numpy as jnp
import numpy as np
from jax import lax
from jax.experimental import pallas as pl
from jax.experimental.pallas import tpu as pltpu
from jax.sharding import PartitionSpec as P

F32 = jnp.float32
BF16 = jnp.bfloat16
HIGH = lax.Precision.HIGHEST
SPAN = 256
MIB = 1024 * 1024


def params(mib=16):
    return pltpu.CompilerParams(vmem_limit_bytes=mib * MIB)


def transforms():
    half = SPAN // 2
    freq = 2.0 * np.pi * (np.arange(half) + 0.5) / SPAN
    phase = np.arange(SPAN)[:, None] * freq[None, :]
    forward = np.concatenate([np.cos(phase), -np.sin(phase)], axis=1)
    inverse = forward.T * (2.0 / SPAN)
    return (
        jnp.asarray(forward, F32),
        jnp.asarray(inverse[:, :half], F32),
        jnp.asarray(inverse[:, half:], F32),
    )


def dot(a, b):
    return jnp.dot(a, b, preferred_element_type=F32)


def exact(a, b):
    return jnp.dot(a, b, precision=HIGH, preferred_element_type=F32)


def pieces(value, count):
    out = []
    for _ in range(count):
        piece = value.astype(BF16)
        out.append(piece)
        value = value - piece.astype(F32)
    return out


def pick(hot, value):
    return sum(dot(hot, piece) for piece in pieces(value, 3))


def prepare_kernel(inc_ref, field_ref, partial_ref, gram_ref):
    blocks, slots, width = inc_ref.shape
    rows = blocks * slots
    weights = inc_ref[...].astype(F32).astype(BF16)
    for b in range(blocks):
        value = field_ref[pl.ds(b * width, width), :]
        partial_ref[pl.ds(b * slots, slots), :] = pick(weights[b], value)
    flat = weights.reshape(rows, width)
    full = lax.dot_general(flat, flat, (((1,), (1,)), ((), ())), preferred_element_type=F32)
    row = lax.broadcasted_iota(jnp.int32, (rows, rows), 0)
    col = lax.broadcasted_iota(jnp.int32, (rows, rows), 1)
    own = jnp.where(row // slots == col // slots, full, 0.0)
    gram_ref[...] = jnp.sum(own.reshape(blocks, slots, rows), axis=0)


def prepare(incidence, field):
    blocks, slots, width = incidence.shape
    hours = field.shape[1]
    step = 8
    return pl.pallas_call(
        prepare_kernel,
        grid=(blocks // step,),
        in_specs=[
            pl.BlockSpec((step, slots, width), lambda i: (i, 0, 0)),
            pl.BlockSpec((step * width, hours), lambda i: (i, 0)),
        ],
        out_specs=[
            pl.BlockSpec((step * slots, hours), lambda i: (i, 0)),
            pl.BlockSpec((slots, step * slots), lambda i: (0, i)),
        ],
        out_shape=[
            jax.ShapeDtypeStruct((blocks * slots, hours), F32),
            jax.ShapeDtypeStruct((slots, blocks * slots), F32),
        ],
        compiler_params=params(56),
        name="prepare",
    )(incidence, field)


def table_kernel(gauge_ref, partial_ref, out_ref):
    slots = partial_ref.shape[0]
    rows = out_ref.shape[0]
    first = pl.program_id(0) * rows
    gauge = lax.broadcasted_iota(jnp.int32, (rows, slots), 0) + first
    hot = jnp.where(gauge_ref[...] == gauge, 1.0, 0.0).astype(BF16)
    out_ref[...] = pick(hot, partial_ref[...])


def table(row_gauge, partial, gauges):
    slots, hours = partial.shape
    step = 256
    return pl.pallas_call(
        table_kernel,
        grid=(gauges // step,),
        in_specs=[
            pl.BlockSpec((1, slots), lambda i: (0, 0)),
            pl.BlockSpec((slots, hours), lambda i: (0, 0)),
        ],
        out_specs=pl.BlockSpec((step, hours), lambda i: (i, 0)),
        out_shape=jax.ShapeDtypeStruct((gauges, hours), F32),
        compiler_params=params(56),
        name="table",
    )(row_gauge.reshape(1, slots), partial)


def couple_kernel(first_ref, lane_ref, sub_ref, gram_ref, high_ref, low_ref, near_ref):
    slots = gram_ref.shape[0]
    count = lane_ref.shape[1]
    rows, cols = high_ref.shape
    tile = 256
    first = first_ref[0]

    @pl.when(pl.program_id(0) == 0)
    def _():
        row = lax.broadcasted_iota(jnp.int32, (tile, tile), 0)
        col = lax.broadcasted_iota(jnp.int32, (tile, tile), 1)
        same = row // slots == col // slots
        mine = lax.broadcasted_iota(jnp.int32, (rows, tile), 0) + first

        def body(i, carry):
            here = pl.ds(pl.multiple_of(i * tile, tile), tile)
            block = jnp.concatenate([gram_ref[:, here]] * (tile // slots), axis=0)
            block = jnp.where(same, block, 0.0).astype(BF16)
            hot = jnp.where(lane_ref[:, here] == mine, 1.0, 0.0).astype(BF16)
            near_ref[:, here] = dot(hot, block)
            return carry

        lax.fori_loop(0, count // tile, body, 0)

    def chunk(i, total):
        here = pl.ds(pl.multiple_of(i * 1024, 1024), 1024)
        gauge = lax.broadcasted_iota(jnp.int32, (1024, cols), 1) + pl.program_id(0) * cols
        hot = jnp.where(sub_ref[here, :] == gauge, 1.0, 0.0).astype(BF16)
        near = near_ref[:, here]
        high = near.astype(BF16)
        low = (near - high.astype(F32)).astype(BF16)
        return total + dot(high, hot) + dot(low, hot)

    total = lax.fori_loop(0, count // 1024, chunk, jnp.zeros((rows, cols), F32))
    high, low = pieces(total, 2)
    high_ref[...] = high
    low_ref[...] = low


def couple(first, row_gauge, gram, rows, gauges):
    count = row_gauge.shape[0]
    step = 256
    return pl.pallas_call(
        couple_kernel,
        grid=(gauges // step,),
        in_specs=[
            pl.BlockSpec(memory_space=pltpu.SMEM),
            pl.BlockSpec((1, count), lambda i: (0, 0)),
            pl.BlockSpec((count, 1), lambda i: (0, 0)),
            pl.BlockSpec(gram.shape, lambda i: (0, 0)),
        ],
        out_specs=[pl.BlockSpec((rows, step), lambda i: (0, i))] * 2,
        out_shape=[jax.ShapeDtypeStruct((rows, gauges), BF16)] * 2,
        scratch_shapes=[pltpu.VMEM((rows, count), F32)],
        compiler_params=params(56),
        name="couple",
    )(first, row_gauge.reshape(1, count), row_gauge.reshape(count, 1), gram)


def mix_kernel(high_ref, low_ref, value_ref, out_ref):
    high = high_ref[...]
    low = low_ref[...]
    one, two, three = pieces(value_ref[...], 3)
    out_ref[...] = (dot(high, three) + dot(low, two)) + (dot(high, two) + dot(low, one)) + dot(high, one)


def mix(high, low, value):
    return pl.pallas_call(
        mix_kernel,
        out_shape=jax.ShapeDtypeStruct((high.shape[0], value.shape[1]), F32),
        compiler_params=params(56),
        name="mix",
    )(high, low, value)


def spectrum_kernel(class_ref, kernels_ref, forward_ref, out_ref):
    rows = class_ref.shape[0]
    classes, taps = kernels_ref.shape
    kind = lax.broadcasted_iota(jnp.int32, (rows, classes), 1)
    hot = jnp.where(class_ref[...] == kind, 1.0, 0.0)
    out_ref[...] = exact(exact(hot, kernels_ref[...]), forward_ref[pl.ds(0, taps), :])


def spectrum(gauge_kernel, kernels, forward):
    rows = gauge_kernel.shape[0]
    return pl.pallas_call(
        spectrum_kernel,
        out_shape=jax.ShapeDtypeStruct((rows, SPAN), F32),
        compiler_params=params(56),
        name="spectrum",
    )(gauge_kernel.reshape(rows, 1), kernels, forward)


def delayed(before, here, after, spec, forward, inverse_last):
    rows, half = here.shape
    stacked = jnp.concatenate(
        [jnp.concatenate([before, here], axis=1), jnp.concatenate([here, after], axis=1)], axis=0
    )
    waves = exact(stacked, forward)
    real, imag = waves[:, :half], waves[:, half:]
    kr = jnp.concatenate([spec[:, :half]] * 2, axis=0)
    ki = jnp.concatenate([spec[:, half:]] * 2, axis=0)
    turned = jnp.concatenate([real * kr - imag * ki, real * ki + imag * kr], axis=1)
    out = exact(turned, inverse_last)
    return out[:rows], out[rows:]


def advanced(here, after, spec, forward, inverse_first):
    half = here.shape[1]
    waves = exact(jnp.concatenate([here, after], axis=1), forward)
    real, imag = waves[:, :half], waves[:, half:]
    kr, ki = spec[:, :half], spec[:, half:]
    turned = jnp.concatenate([real * kr + imag * ki, imag * kr - real * ki], axis=1)
    return exact(turned, inverse_first)


def lanes(a, b):
    return jnp.sum(a * b, axis=0, keepdims=True)


def total(ref, row):
    return jnp.sum(ref[row : row + 1, :], axis=1, keepdims=True)


def ratios(ref):
    square = total(ref, 0)
    alpha = jnp.sqrt(square)
    beta = jnp.sqrt(jnp.maximum(total(ref, 1) / square - 2.0 * total(ref, 2) + square, 0.0))
    return alpha, beta


def first_kernel(
    more_ref, sums_ref, observed_ref, spec_ref, forward_ref, first_ref, last_ref, out_ref, note_ref
):
    rows, half = observed_ref.shape[0] // 2, observed_ref.shape[1]
    spec, forward = spec_ref[...], forward_ref[...]
    before, here, after = (sums_ref[pl.ds(i * rows, rows), :] for i in range(3))
    now, later = delayed(before, here, after, spec, forward, last_ref[...])
    start = observed_ref[pl.ds(0, rows), :] - now
    start_later = (observed_ref[pl.ds(rows, rows), :] - later) * more_ref[0]
    out_ref[...] = advanced(start, start_later, spec, forward, first_ref[...])
    note_ref[...] = jnp.concatenate([lanes(start, start), jnp.zeros((7, half), F32)], axis=0)


def first_step(more, sums, observed, spec, mats):
    rows, half = spec.shape[0], observed.shape[1]
    return pl.pallas_call(
        first_kernel,
        in_specs=[pl.BlockSpec(memory_space=pltpu.SMEM)] + [pl.BlockSpec(memory_space=pltpu.VMEM)] * 6,
        out_shape=[jax.ShapeDtypeStruct((rows, half), F32), jax.ShapeDtypeStruct((8, half), F32)],
        compiler_params=params(56),
        name="first_step",
    )(more, sums, observed, spec, *mats)


def step_kernel(
    opening,
    final,
    more_ref,
    note_ref,
    sums_ref,
    spec_ref,
    forward_ref,
    first_ref,
    last_ref,
    pulled_ref,
    *refs,
):
    if opening:
        state_ref = None
    else:
        state_ref, *refs = refs
    if final:
        (out_note_ref,) = refs
    else:
        new_ref, out_ref, out_note_ref = refs
    rows, half = pulled_ref.shape
    spec, forward = spec_ref[...], forward_ref[...]
    if opening:
        scale = 1.0 / jnp.sqrt(total(note_ref, 0))
        along = sums_ref[...] * scale
        new_s, new_su = along, along
        new_zu = pulled_ref[...] * scale
        new_z = new_zu
    else:
        alpha, beta = ratios(note_ref)
        a, b, g = 1.0 / (alpha * beta), alpha / beta, beta / alpha
        wide = pl.ds(0, 3 * rows), pl.ds(3 * rows, 3 * rows)
        new_su = sums_ref[...] * a - state_ref[wide[1], :] * b
        new_s = new_su - state_ref[wide[0], :] * g
        new_zu = pulled_ref[...] * a - state_ref[pl.ds(7 * rows, rows), :] * b
        new_z = new_zu - state_ref[pl.ds(6 * rows, rows), :] * g
    before, here, after = (new_s[i * rows : (i + 1) * rows] for i in range(3))
    now, later = delayed(before, here, after, spec, forward, last_ref[...])
    out_note_ref[...] = jnp.concatenate(
        [lanes(new_z, here), lanes(now, now), lanes(new_zu, here), jnp.zeros((5, half), F32)], axis=0
    )
    if not final:
        new_ref[pl.ds(0, 3 * rows), :] = new_s
        new_ref[pl.ds(3 * rows, 3 * rows), :] = new_su
        new_ref[pl.ds(6 * rows, rows), :] = new_z
        new_ref[pl.ds(7 * rows, rows), :] = new_zu
        out_ref[...] = advanced(now, later * more_ref[0], spec, forward, first_ref[...])


def next_step(more, note, sums, spec, mats, pulled, state, final):
    rows, half = pulled.shape
    opening = state is None
    shapes = [
        jax.ShapeDtypeStruct((8 * rows, half), F32),
        jax.ShapeDtypeStruct((rows, half), F32),
        jax.ShapeDtypeStruct((8, half), F32),
    ]
    args = [more, note, sums, spec, *mats, pulled] + ([] if opening else [state])
    return pl.pallas_call(
        functools.partial(step_kernel, opening, final),
        in_specs=[pl.BlockSpec(memory_space=pltpu.SMEM)]
        + [pl.BlockSpec(memory_space=pltpu.VMEM)] * (len(args) - 1),
        out_shape=shapes[2:] if final else shapes,
        compiler_params=params(56),
        name="next_step",
    )(*args)


def weights_of(notes):
    start = jnp.sqrt(total(notes[0], 0))
    zero = jnp.zeros_like(start)
    units = [1.0 / start, zero, zero]
    z, zu = list(units), list(units)
    phibar = start
    alpha, beta = ratios(notes[1])
    rhobar = alpha
    w = [value / alpha for value in z]
    result = [zero] * 3
    steps = len(notes) - 1
    for k in range(steps):
        rho = jnp.sqrt(rhobar * rhobar + beta * beta)
        cosine, sine = rhobar / rho, beta / rho
        phi, phibar = cosine * phibar, sine * phibar
        result = [r + phi / rho * value for r, value in zip(result, w)]
        if k < steps - 1:
            a, b, g = 1.0 / (alpha * beta), alpha / beta, beta / alpha
            zu = [(a if i == k + 1 else 0.0) - b * value for i, value in enumerate(zu)]
            z = [value - g * old for value, old in zip(zu, z)]
            alpha, beta = ratios(notes[k + 2])
            theta = sine * alpha
            rhobar = -cosine * alpha
            w = [value / alpha - theta / rho * old for value, old in zip(z, w)]
    return result


def finish_kernel(n0, n1, n2, n3, gauge_ref, q0, q1, q2, inc_ref, field_ref, out_ref, rows_ref):
    blocks, slots, width = inc_ref.shape
    count = rows_ref.shape[0]
    gauges = q0.shape[0]
    step = pl.program_id(0)

    @pl.when(step == 0)
    def _():
        e0, e1, e2 = weights_of([n0, n1, n2, n3])
        width_ = 512

        def body(i, value):
            here = pl.ds(pl.multiple_of(i * width_, width_), width_)
            mixed = q0[here, :] * e0 + q1[here, :] * e1 + q2[here, :] * e2
            gauge = lax.broadcasted_iota(jnp.int32, (count, width_), 1) + i * width_
            hot = jnp.where(gauge_ref[...] == gauge, 1.0, 0.0).astype(BF16)
            return value + pick(hot, mixed)

        rows_ref[...] = lax.fori_loop(0, gauges // width_, body, jnp.zeros(rows_ref.shape, F32))

    weights = inc_ref[...].astype(F32).astype(BF16)
    for b in range(blocks):
        here = pl.ds(b * width, width)
        rows = rows_ref[pl.ds(pl.multiple_of((step * blocks + b) * slots, slots), slots), :]
        added = sum(
            lax.dot_general(weights[b], piece, (((0,), (0,)), ((), ())), preferred_element_type=F32)
            for piece in pieces(rows, 3)
        )
        out_ref[here, :] = field_ref[here, :] + added


def finish(notes, row_gauge, gathered, incidence, field):
    blocks, slots, width = incidence.shape
    hours = field.shape[1]
    count = row_gauge.shape[0]
    step = 8
    whole = lambda shape: pl.BlockSpec(shape, lambda i: (0, 0))
    return pl.pallas_call(
        finish_kernel,
        grid=(blocks // step,),
        in_specs=[whole(n.shape) for n in notes]
        + [whole((count, 1))]
        + [whole(q.shape) for q in gathered]
        + [
            pl.BlockSpec((step, slots, width), lambda i: (i, 0, 0)),
            pl.BlockSpec((step * width, hours), lambda i: (i, 0)),
        ],
        out_specs=pl.BlockSpec((step * width, hours), lambda i: (i, 0)),
        out_shape=jax.ShapeDtypeStruct(field.shape, F32),
        scratch_shapes=[pltpu.VMEM((count, hours), F32)],
        compiler_params=params(56),
        name="finish",
    )(*notes, row_gauge.reshape(count, 1), *gathered, incidence, field)


def shifted(value, axis, by):
    devices = lax.axis_size(axis)
    pairs = [(i, i + by) for i in range(devices) if 0 <= i + by < devices]
    return lax.ppermute(value, axis, pairs)


def window(value):
    return jnp.concatenate([shifted(value, "tm", 1), value, shifted(value, "tm", -1)], axis=0)


def gathered_rows(value):
    owners = lax.axis_size("basin")
    copies = jnp.broadcast_to(value[None], (owners,) + value.shape)
    return lax.all_to_all(copies, "basin", 0, 0, tiled=False)


def over_hours(note):
    blocks = lax.axis_size("tm")
    result = note
    for by in range(1, blocks):
        result = result + lax.ppermute(note, "tm", [(i, (i + by) % blocks) for i in range(blocks)])
    return result


def shards(incidence, row_gauge, gauge_kernel, kernels, observed, first_guess):
    owners = lax.axis_size("basin")
    rows, hours = observed.shape
    gauges = rows * owners
    mats = transforms()
    spec = spectrum(gauge_kernel, kernels, mats[0])
    more = (lax.axis_index("tm") < lax.axis_size("tm") - 1).astype(F32).reshape(1)
    partial, gram = prepare(incidence, first_guess)
    all_gram = lax.all_gather(gram, "basin", axis=1, tiled=True)
    all_rows = lax.all_gather(row_gauge, "basin", axis=0, tiled=True)
    dense = table(row_gauge, partial, gauges).reshape(owners, rows, hours)
    sums = jnp.sum(lax.all_to_all(dense, "basin", 0, 0, tiled=False), axis=0)
    both = jnp.concatenate([observed, shifted(observed, "tm", -1)], axis=0)
    first = (lax.axis_index("basin") * rows).astype(jnp.int32).reshape(1)
    high, low = couple(first, all_rows, all_gram, rows, gauges)

    pulled, note = first_step(more, window(sums), both, spec, mats)
    notes, kept, state = [], [], None
    for k in range(3):
        everyone = gathered_rows(jnp.concatenate([pulled, note], axis=0))
        value = everyone[:, :rows].reshape(gauges, hours)
        notes.append(over_hours(jnp.sum(everyone[:, rows:], axis=0)))
        kept.append(value)
        around = window(mix(high, low, value))
        final = k == 2
        result = next_step(more, notes[-1], around, spec, mats, pulled, state, final)
        if final:
            (note,) = result
        else:
            state, pulled, note = result
    notes.append(over_hours(jnp.sum(gathered_rows(note), axis=0)))
    return finish(notes, row_gauge, kept, incidence, first_guess)


Z_, X_, Y_, C_ = 4, 2, 2, 2
NOTE = 8


def device(z, x, y, c):
    return (z * X_ + x) * (Y_ * C_) + y * C_ + c


def moved(value, where):
    pairs = []
    for z, x, y, c in np.ndindex(Z_, X_, Y_, C_):
        target = where(z, x, y, c)
        if target is not None:
            pairs.append((device(z, x, y, c), device(*target)))
    return lax.ppermute(value, ("basin", "tm"), pairs)


def to_plane(z, x, y, c):
    return 2 * y + c, x, z & 1, z >> 1


def to_plane_before(z, x, y, c):
    t = 2 * y + c
    return (t - 1, x, z & 1, z >> 1) if t else None


def from_plane(z, x, y, c):
    return 2 * c + y, x, z >> 1, z & 1


def over_x(z, x, y, c):
    return z, 1 - x, y, c


def over_y(z, x, y, c):
    return z, x, 1 - y, c


def over_xy(z, x, y, c):
    return z, 1 - x, 1 - y, c


def over_core(z, x, y, c):
    return z, x, y, 1 - c


def z_pair(z, x, y, c):
    return z ^ 1, x, y, c


def z_middle(z, x, y, c):
    return (3 - z, x, y, c) if z in (1, 2) else None


def z_two(z, x, y, c):
    return z ^ 2, x, y, c


def z_mirror(z, x, y, c):
    return 3 - z, x, y, c


SQUARE = (over_x, over_y, over_xy)


def split_constant(value):
    out = []
    for _ in range(3):
        piece = value.astype(jnp.bfloat16)
        out.append(jnp.asarray(piece))
        value = value - piece.astype(np.float64)
    return out


def turned_transforms():
    half = SPAN // 2
    freq = 2.0 * np.pi * (np.arange(half) + 0.5) / SPAN
    phase = freq[:, None] * np.arange(SPAN)[None, :]
    forward = np.concatenate([np.cos(phase), -np.sin(phase)], axis=0)
    inverse = forward.T * (2.0 / SPAN)
    return split_constant(forward), split_constant(inverse[:half]), split_constant(inverse[half:])


def product(mats, value, order):
    parts = pieces(value, order)
    result = None
    for level in reversed(range(order)):
        for i in range(level + 1):
            term = dot(mats[i][...], parts[level - i])
            result = term if result is None else result + term
    return result


def turn(waves, spec, sign):
    half = waves.shape[0] // 2
    real, imag = waves[:half], waves[half:]
    kr, ki = spec[:half], spec[half:] * sign
    return jnp.concatenate([real * kr - imag * ki, real * ki + imag * kr], axis=0)


def plane_delayed(before, here, after, spec, forward, last, order):
    out = []
    for pair in ((before, here), (here, after)):
        waves = product(forward, jnp.concatenate(pair, axis=0), order)
        out.append(product(last, turn(waves, spec, 1.0), order))
    return out


def plane_advanced(here, after, spec, forward, first, order):
    waves = product(forward, jnp.concatenate([here, after], axis=0), order)
    return product(first, turn(waves, spec, -1.0), order)


def send_kernel(inc_ref, field_ref, gauge_ref, kind_ref, out_ref):
    blocks, slots, width = inc_ref.shape
    rows = blocks * slots
    hours = field_ref.shape[1]
    weights = inc_ref[...].astype(F32).astype(BF16)
    parts = []
    for b in range(blocks):
        parts.append(pick(weights[b], field_ref[pl.ds(b * width, width), :]))
    out_ref[pl.ds(0, hours), :] = jnp.transpose(jnp.concatenate(parts, axis=0))
    flat = weights.reshape(rows, width)
    full = lax.dot_general(flat, flat, (((1,), (1,)), ((), ())), preferred_element_type=F32)
    row = lax.broadcasted_iota(jnp.int32, (rows, rows), 0)
    col = lax.broadcasted_iota(jnp.int32, (rows, rows), 1)
    own = jnp.where(row // slots == col // slots, full, 0.0)
    out_ref[pl.ds(hours, slots), :] = jnp.sum(own.reshape(blocks, slots, rows), axis=0)
    out_ref[pl.ds(hours + slots, 8), :] = jnp.concatenate(
        [gauge_ref[...].astype(F32), kind_ref[...].astype(F32), jnp.zeros((6, rows), F32)], axis=0
    )


def send(incidence, field, row_gauge, gauge_kernel):
    blocks, slots, width = incidence.shape
    count = blocks * slots
    hours = field.shape[1]
    step = 8
    height = hours + slots + 8
    kinds = jnp.pad(gauge_kernel, (0, count - gauge_kernel.shape[0]))
    return pl.pallas_call(
        send_kernel,
        grid=(blocks // step,),
        in_specs=[
            pl.BlockSpec((step, slots, width), lambda i: (i, 0, 0)),
            pl.BlockSpec((step * width, hours), lambda i: (i, 0)),
            pl.BlockSpec((1, step * slots), lambda i: (0, i)),
            pl.BlockSpec((1, step * slots), lambda i: (0, i)),
        ],
        out_specs=pl.BlockSpec((height, step * slots), lambda i: (0, i)),
        out_shape=jax.ShapeDtypeStruct((height, count), F32),
        compiler_params=params(),
        name="send",
    )(incidence, field, row_gauge.reshape(1, count), kinds.reshape(1, count))


def hot_rows(gauge, first, rows):
    mine = (lax.broadcasted_iota(jnp.int32, (rows, gauge.shape[1]), 0) + first).astype(F32)
    return jnp.where(gauge == mine, 1.0, 0.0).astype(BF16)


def spread_kernel(first_ref, mine_ref, other_ref, *out_refs):
    hours, rows = out_refs[0].shape
    where = mine_ref.shape[0] - 8
    for m, out_ref in enumerate(out_refs):
        result = None
        for ref in (mine_ref, other_ref):
            hot = hot_rows(ref[where : where + 1, :], first_ref[m], rows)
            for piece in reversed(pieces(ref[pl.ds(0, hours), :], 3)):
                term = lax.dot_general(
                    piece, hot, (((1,), (1,)), ((), ())), preferred_element_type=F32
                )
                result = term if result is None else result + term
        out_ref[...] = result


def spread(first, parcels, hours, rows):
    return pl.pallas_call(
        spread_kernel,
        in_specs=[pl.BlockSpec(memory_space=pltpu.SMEM)] + [pl.BlockSpec(memory_space=pltpu.VMEM)] * 2,
        out_shape=[jax.ShapeDtypeStruct((hours, rows), F32)] * 4,
        compiler_params=params(),
        name="spread",
    )(first, *parcels)


def plane_couple_kernel(last, first_ref, *refs):
    if last:
        a_ref, b_ref, before_ref, high_ref, low_ref, total_ref, meta_ref = refs
        total_ref[...] = before_ref[...]
    else:
        a_ref, b_ref, total_ref, meta_ref = refs
        total_ref[...] = jnp.zeros_like(total_ref)
    height, double = a_ref.shape
    slots = height - 8
    count = double // 2
    cols, rows = total_ref.shape
    tile = 256
    for i, ref in enumerate((a_ref, b_ref)):
        for j in range(2):
            meta_ref[2 * i + j] = ref[:, j * count : (j + 1) * count]
    row = lax.broadcasted_iota(jnp.int32, (tile, tile), 0)
    col = lax.broadcasted_iota(jnp.int32, (tile, tile), 1)
    same = row // slots == col // slots

    def body(i, carry):
        gauge = meta_ref[i, slots : slots + 1, :]
        near = []
        for j in range(count // tile):
            here = slice(j * tile, (j + 1) * tile)
            block = jnp.concatenate([meta_ref[i, :slots, here]] * (tile // slots), axis=0)
            block = jnp.where(same, block, 0.0).astype(BF16)
            mine = jnp.concatenate(
                [hot_rows(gauge[:, here], first_ref[4 + h], rows // 2) for h in range(2)], axis=0
            )
            near.append(
                lax.dot_general(block, mine, (((1,), (1,)), ((), ())), preferred_element_type=F32)
            )
        near = jnp.concatenate(near, axis=0)
        high = near.astype(BF16)
        rest = near - high.astype(F32)
        hot = jnp.concatenate([hot_rows(gauge, first_ref[m], cols // 4) for m in range(4)], axis=0)
        total_ref[...] += dot(hot, high)

        @pl.when(jnp.max(jnp.abs(rest)) > 0.0)
        def _():
            total_ref[...] += dot(hot, rest.astype(BF16))

        return carry

    lax.fori_loop(0, 4, body, 0)
    if last:
        high, low = pieces(total_ref[...], 2)
        high_ref[...] = high
        low_ref[...] = low


def plane_couple(first, metas, rows, before=None):
    height, double = metas[0].shape
    shape = (4 * rows, 2 * rows)
    last = before is not None
    args = [first, *metas] + ([before] if last else [])
    scratch = [pltpu.VMEM((4, height, double // 2), F32)]
    return pl.pallas_call(
        functools.partial(plane_couple_kernel, last),
        in_specs=[pl.BlockSpec(memory_space=pltpu.SMEM)]
        + [pl.BlockSpec(memory_space=pltpu.VMEM)] * (len(args) - 1),
        out_shape=[jax.ShapeDtypeStruct(shape, BF16)] * 2 if last else jax.ShapeDtypeStruct(shape, F32),
        scratch_shapes=([pltpu.VMEM(shape, F32)] if last else []) + scratch,
        compiler_params=params(),
        name="plane_couple",
        cost_estimate=pl.CostEstimate(
            flops=2 * 2 * double * 8 * rows * rows, bytes_accessed=2_000_000, transcendentals=0
        ),
    )(*args)


def plane_mix_kernel(
    first_ref, high_ref, low_ref, meta_ref, meta_other_ref, a_ref, b_ref, c_ref, d_ref, mine_ref, other_ref, rows_ref
):
    refs = (a_ref, b_ref, c_ref, d_ref)
    height, rows = a_ref.shape
    hours = height - NOTE
    body, tail = pl.ds(0, hours), pl.ds(hours, NOTE)
    value = jnp.concatenate([ref[body, :] for ref in refs], axis=1)
    one, two = pieces(value, 2)
    high, low = high_ref[...], low_ref[...]
    result = (dot(two, high) + dot(one, low)) + dot(one, high)
    note = sum(ref[tail, :] for ref in refs)
    mine_ref[body, :] = result[:, :rows]
    other_ref[body, :] = result[:, rows:]
    mine_ref[tail, :] = note
    other_ref[tail, :] = note
    where = meta_ref.shape[0] - 8
    for ref in (meta_ref, meta_other_ref):
        gauge = ref[where : where + 1, :]
        hot = jnp.concatenate([hot_rows(gauge, first_ref[m], rows) for m in range(4)], axis=0)
        picked = dot(two, hot) + dot(one, hot)
        if ref is meta_ref:
            rows_ref[...] = picked
        else:
            for i in range(gauge.shape[1] // rows):
                other_ref[pl.ds(height + i * hours, hours), :] = picked[:, i * rows : (i + 1) * rows]


def plane_mix(first, coupling, metas, values):
    height, rows = values[0].shape
    hours = height - NOTE
    slots = metas[0].shape[1]
    return pl.pallas_call(
        plane_mix_kernel,
        in_specs=[pl.BlockSpec(memory_space=pltpu.SMEM)] + [pl.BlockSpec(memory_space=pltpu.VMEM)] * 8,
        out_shape=[
            jax.ShapeDtypeStruct((height, rows), F32),
            jax.ShapeDtypeStruct((height + slots // rows * hours, rows), F32),
            jax.ShapeDtypeStruct((hours, slots), F32),
        ],
        compiler_params=params(),
        name="plane_mix",
    )(first, *coupling, *metas, *values)


def plane_spectrum_kernel(class_ref, kernels_ref, f0_ref, f1_ref, f2_ref, out_ref):
    classes, taps = kernels_ref.shape
    kind = class_ref[class_ref.shape[0] - 7 : class_ref.shape[0] - 6, : out_ref.shape[1]]
    hot = jnp.where(
        lax.broadcasted_iota(jnp.int32, (classes, kind.shape[1]), 0).astype(F32) == kind, 1.0, 0.0
    ).astype(BF16)
    chosen = None
    for piece in reversed(pieces(jnp.transpose(kernels_ref[...]), 3)):
        term = dot(piece, hot)
        chosen = term if chosen is None else chosen + term
    mats = [ref[:, :taps] for ref in (f0_ref, f1_ref, f2_ref)]
    out_ref[...] = product(mats, chosen, 3)


def plane_spectrum(meta, kernels, forward, rows):
    return pl.pallas_call(
        plane_spectrum_kernel,
        out_shape=jax.ShapeDtypeStruct((SPAN, rows), F32),
        compiler_params=params(),
        name="plane_spectrum",
    )(meta, kernels, *forward)


def sides(even, pair, middle):
    return jnp.where(even, middle, pair), jnp.where(even, pair, middle)


def plane_first_kernel(flag_ref, here_ref, pair_ref, middle_ref, spec_ref, *refs):
    *mats, out_ref = refs
    forward, first, last = mats[0:3], mats[3:6], mats[6:9]
    rows = here_ref.shape[1]
    hours = here_ref.shape[0] // 2
    spec = spec_ref[...]
    before, after = sides(flag_ref[0] > 0.5, pair_ref[...], middle_ref[...])
    now, later = plane_delayed(
        before[:hours], here_ref[pl.ds(0, hours), :], after[:hours], spec, forward, last, 3
    )
    start = here_ref[pl.ds(hours, hours), :] - now
    start_later = (after[hours:] - later) * flag_ref[1]
    out_ref[pl.ds(0, hours), :] = plane_advanced(start, start_later, spec, forward, first, 3)
    out_ref[pl.ds(hours, NOTE), :] = jnp.concatenate(
        [lanes(start, start), jnp.zeros((NOTE - 1, rows), F32)], axis=0
    )


def plane_first(flags, sums, spec, mats):
    double, rows = sums[0].shape
    args = [flags, *sums, spec, *mats]
    return pl.pallas_call(
        plane_first_kernel,
        in_specs=[pl.BlockSpec(memory_space=pltpu.SMEM)]
        + [pl.BlockSpec(memory_space=pltpu.VMEM)] * (len(args) - 1),
        out_shape=jax.ShapeDtypeStruct((double // 2 + NOTE, rows), F32),
        compiler_params=params(),
        name="plane_first",
    )(*args)


def plane_open_kernel(flag_ref, here_ref, pair_ref, middle_ref, pulled_ref, spec_ref, *refs):
    mats, (out_ref, now_ref) = refs[:9], refs[9:]
    forward, first, last = mats[0:3], mats[3:6], mats[6:9]
    height, rows = pulled_ref.shape
    hours = height - NOTE
    tail, body = pl.ds(hours, NOTE), pl.ds(0, hours)
    spec = spec_ref[...]
    here = here_ref[body, :]
    before, after = sides(flag_ref[0] > 0.5, pair_ref[body, :], middle_ref[body, :])
    now, later = plane_delayed(before, here, after, spec, forward, last, 2)
    out_ref[body, :] = plane_advanced(now, later * flag_ref[1], spec, forward, first, 2)
    out_ref[tail, :] = jnp.concatenate(
        [
            lanes(pulled_ref[body, :], here),
            lanes(now, now),
            pulled_ref[hours : hours + 1, :],
            jnp.zeros((NOTE - 3, rows), F32),
        ],
        axis=0,
    )
    now_ref[...] = now


def plane_open(flags, sums, pulled, spec, mats):
    height, rows = pulled.shape
    args = [flags, *sums, pulled, spec, *mats]
    return pl.pallas_call(
        plane_open_kernel,
        in_specs=[pl.BlockSpec(memory_space=pltpu.SMEM)]
        + [pl.BlockSpec(memory_space=pltpu.VMEM)] * (len(args) - 1),
        out_shape=[
            jax.ShapeDtypeStruct((height, rows), F32),
            jax.ShapeDtypeStruct((height - NOTE, rows), F32),
        ],
        compiler_params=params(),
        name="plane_open",
    )(*args)


def opening(ref):
    start = total(ref, 2)
    square = total(ref, 0) / start
    alpha = jnp.sqrt(square)
    beta = jnp.sqrt(jnp.maximum(total(ref, 1) / total(ref, 0) - square, 0.0))
    return 1.0 / jnp.sqrt(start), alpha, beta


def plane_step_kernel(flag_ref, here_ref, pair_ref, middle_ref, two_ref, mirror_ref, *refs):
    old_refs, (pulled_ref, old_z_ref, old_now_ref, spec_ref), refs = refs[:3], refs[3:7], refs[7:]
    mats, (total_ref, out_ref, kept_ref) = refs[:9], refs[9:]
    forward, first, last = mats[0:3], mats[3:6], mats[6:9]
    height, rows = pulled_ref.shape
    hours = height - NOTE
    tail, body = pl.ds(hours, NOTE), pl.ds(0, hours)
    total_ref[...] = (here_ref[tail, :] + pair_ref[tail, :]) + (two_ref[...] + mirror_ref[...])
    scale, alpha, beta = opening(total_ref)
    a, b, g = scale / (alpha * beta), scale * alpha / beta, scale * beta / alpha
    spec = spec_ref[...]
    s, su = [], []
    for ref, old_ref in zip((here_ref, pair_ref, middle_ref), old_refs):
        old = old_ref[body, :]
        su.append(ref[body, :] * a - old * b)
        s.append(su[-1] - old * g)
    zu = pulled_ref[body, :] * a - old_z_ref[body, :] * b
    z = zu - old_z_ref[body, :] * g
    before, after = sides(flag_ref[0] > 0.5, s[1], s[2])
    now, later = plane_delayed(before, s[0], after, spec, forward, last, 2)
    out_ref[body, :] = plane_advanced(now, later * flag_ref[1], spec, forward, first, 2)
    out_ref[tail, :] = jnp.concatenate(
        [lanes(z, s[0]), lanes(now, now), lanes(zu, s[0]), jnp.zeros((NOTE - 3, rows), F32)], axis=0
    )
    for i, value in enumerate((s[0], su[0], z, zu, now, now + old_now_ref[...] * g)):
        kept_ref[pl.ds(i * hours, hours), :] = value


def plane_step(flags, sums, two, mirror, old, pulled, old_z, old_now, spec, mats):
    height, rows = pulled.shape
    args = [flags, *sums, two, mirror, *old, pulled, old_z, old_now, spec, *mats]
    return pl.pallas_call(
        plane_step_kernel,
        in_specs=[pl.BlockSpec(memory_space=pltpu.SMEM)]
        + [pl.BlockSpec(memory_space=pltpu.VMEM)] * (len(args) - 1),
        out_shape=[
            jax.ShapeDtypeStruct((NOTE, rows), F32),
            jax.ShapeDtypeStruct((height, rows), F32),
            jax.ShapeDtypeStruct((6 * (height - NOTE), rows), F32),
        ],
        compiler_params=params(),
        name="plane_step",
    )(*args)


def plane_close_kernel(flag_ref, here_ref, pair_ref, middle_ref, pulled_ref, kept_ref, spec_ref, *refs):
    mats, (out_ref,) = refs[:9], refs[9:]
    forward, last = mats[0:3], mats[6:9]
    height, rows = pulled_ref.shape
    hours = height - NOTE
    body = pl.ds(0, hours)
    before, after = sides(flag_ref[0] > 0.5, pair_ref[body, :], middle_ref[body, :])
    here = here_ref[body, :]
    waves = product(forward, jnp.concatenate([before, here], axis=0), 2)
    now = product(last, turn(waves, spec_ref[...], 1.0), 2)
    s, su, z, zu, old_now, old_now_u = (kept_ref[pl.ds(i * hours, hours), :] for i in range(6))
    raw = pulled_ref[body, :]
    note = [pulled_ref[hours + i : hours + i + 1, :] for i in range(3)]
    for left in (raw, zu, z):
        note += [lanes(left, right) for right in (here, su, s)]
    parts = (now, old_now_u, old_now)
    for i in range(3):
        note += [lanes(parts[i], parts[j]) for j in range(i, 3)]
    note.append(jnp.zeros((24 - len(note), rows), F32))
    note = jnp.concatenate(note, axis=0)
    out_ref[...] = note[:, : rows // 2] + note[:, rows // 2 :]


def plane_close(flags, sums, pulled, kept, spec, mats):
    rows = pulled.shape[1]
    args = [flags, *sums, pulled, kept, spec, *mats]
    return pl.pallas_call(
        plane_close_kernel,
        in_specs=[pl.BlockSpec(memory_space=pltpu.SMEM)]
        + [pl.BlockSpec(memory_space=pltpu.VMEM)] * (len(args) - 1),
        out_shape=jax.ShapeDtypeStruct((24, rows // 2), F32),
        compiler_params=params(),
        name="plane_close",
    )(*args)


def plane_weights(open_ref, close_ref):
    scale, alpha, beta = opening(open_ref)
    start = 1.0 / scale
    phibar, rhobar = start, alpha
    zero = jnp.zeros_like(start)
    z = zu = [scale, zero, zero]
    w = [value / alpha for value in z]
    result = [zero] * 3
    for k in range(3):
        rho = jnp.sqrt(rhobar * rhobar + beta * beta)
        cosine, sine = rhobar / rho, beta / rho
        phi, phibar = cosine * phibar, sine * phibar
        result = [r + phi / rho * value for r, value in zip(result, w)]
        if k == 2:
            return result
        a, b, g = 1.0 / (alpha * beta), alpha / beta, beta / alpha
        zu = [-b * value for value in zu]
        zu[k + 1] = zu[k + 1] + (a * scale if k == 0 else a)
        z = [value - g * old for value, old in zip(zu, z)]
        if k == 0:
            square, norm, along = (total(close_ref, i) for i in range(3))
        else:
            plain = (a, -b, -g)
            cross = [[total(close_ref, 3 + 3 * i + j) for j in range(3)] for i in range(3)]
            along = sum(plain[i] * plain[j] * cross[i][j] for i in range(2) for j in range(3))
            square = along + sum(plain[2] * plain[j] * cross[2][j] for j in range(3))
            pairs = [(i, j) for i in range(3) for j in range(i, 3)]
            norm = sum(
                plain[i] * plain[j] * total(close_ref, 12 + n) * (1.0 if i == j else 2.0)
                for n, (i, j) in enumerate(pairs)
            )
        alpha = jnp.sqrt(square)
        beta = jnp.sqrt(jnp.maximum(norm / square - 2.0 * along + square, 0.0))
        theta = sine * alpha
        rhobar = -cosine * alpha
        w = [value / alpha - theta / rho * old for value, old in zip(z, w)]


def plane_finish_kernel(open_ref, close_ref, q0, q1, q2, inc_ref, field_ref, out_ref, rows_ref):
    blocks, slots, width = inc_ref.shape
    step = pl.program_id(0)

    @pl.when(step == 0)
    def _():
        e0, e1, e2 = plane_weights(open_ref, close_ref)
        rows_ref[...] = jnp.transpose(q0[...] * e0 + q1[...] * e1 + q2[...] * e2)

    weights = inc_ref[...].astype(F32).astype(BF16)
    for b in range(blocks):
        here = pl.ds(b * width, width)
        rows = rows_ref[pl.ds(pl.multiple_of((step * blocks + b) * slots, slots), slots), :]
        added = sum(
            lax.dot_general(weights[b], piece, (((0,), (0,)), ((), ())), preferred_element_type=F32)
            for piece in pieces(rows, 2)
        )
        out_ref[here, :] = field_ref[here, :] + added


def plane_finish(notes, rows, incidence, field):
    blocks, slots, width = incidence.shape
    hours = field.shape[1]
    step = 8
    whole = lambda shape: pl.BlockSpec(shape, lambda i: (0, 0))
    return pl.pallas_call(
        plane_finish_kernel,
        grid=(blocks // step,),
        in_specs=[whole(n.shape) for n in notes]
        + [whole(q.shape) for q in rows]
        + [
            pl.BlockSpec((step, slots, width), lambda i: (i, 0, 0)),
            pl.BlockSpec((step * width, hours), lambda i: (i, 0)),
        ],
        out_specs=pl.BlockSpec((step * width, hours), lambda i: (i, 0)),
        out_shape=jax.ShapeDtypeStruct(field.shape, F32),
        scratch_shapes=[pltpu.VMEM((blocks * slots, hours), F32)],
        compiler_params=params(),
        name="plane_finish",
    )(*notes, *rows, incidence, field)


def plane_shards(incidence, row_gauge, gauge_kernel, kernels, observed, first_guess):
    rows, hours = observed.shape
    basin, tm = lax.axis_index("basin"), lax.axis_index("tm")
    z, x, y, c = basin // X_, basin % X_, tm // C_, tm % C_
    place = 2 * y + x
    first = jnp.stack([4 * c + (place ^ m) for m in range(4)] + [4 * c + place, 4 * (1 - c) + place])
    first = (first * rows).astype(jnp.int32)
    flags = jnp.stack([1 - z % 2, (z < Z_ - 1).astype(z.dtype)]).astype(F32)
    forward, inverse_first, inverse_last = turned_transforms()
    mats = [*forward, *inverse_first, *inverse_last]

    parcel = moved(send(incidence, first_guess, row_gauge, gauge_kernel), to_plane)
    seen, parcel = lax.optimization_barrier((jnp.transpose(observed), parcel))
    parcels = [parcel, moved(parcel, over_core)]
    seen = moved(seen, to_plane)
    metas = [value[hours:] for value in parcels]
    both = jnp.concatenate(metas, axis=1)
    around = [both] + [moved(both, where) for where in SQUARE]
    spec = plane_spectrum(metas[0], kernels, forward, rows)

    dense = spread(first, parcels, hours, rows)
    sums = dense[0] + sum(moved(value, where) for value, where in zip(dense[1:], SQUARE))
    sums = jnp.concatenate([sums, seen], axis=0)
    sums = [sums, moved(sums, z_pair), moved(sums, z_middle)]
    coupled = plane_couple(first, around[:2], rows)
    coupled, sums = lax.optimization_barrier((coupled, sums))
    coupling = plane_couple(first, around[2:], rows, coupled)
    pulled = [plane_first(flags, sums, spec, mats)]
    kept, shipped, mixes = [], [], []
    for k in range(3):
        if k:
            pulled[k], kept[k - 1] = lax.optimization_barrier((pulled[k], kept[k - 1]))
            shipped.append(moved(kept[k - 1], from_plane))
        values = [pulled[k]] + [moved(pulled[k], where) for where in SQUARE]
        mine, other, slot_rows = plane_mix(first, coupling, metas, values)
        beside = moved(other, over_core)
        mixed = mine + beside[: hours + NOTE]
        kept.append(
            slot_rows
            + jnp.concatenate(
                [beside[hours + NOTE + i * hours :][:hours] for i in range(slot_rows.shape[1] // rows)], axis=1
            )
        )
        sums = [mixed, moved(mixed, z_pair), moved(mixed, z_middle)]
        mixes.append(sums)
        if k == 0:
            following, now = plane_open(flags, sums, pulled[0], spec, mats)
        elif k == 1:
            note = mixed[hours:]
            two, mirror = moved(note, z_two), moved(note, z_mirror)
            open_note, following, state = plane_step(
                flags, sums, two, mirror, mixes[0], pulled[1], pulled[0], now, spec, mats
            )
            following, shipped[0] = lax.optimization_barrier((following, shipped[0]))
        else:
            shipped.append(moved(kept[2], from_plane))
            note = plane_close(flags, sums, pulled[2], state, spec, mats)
        pulled.append(following)
    note, shipped[1] = lax.optimization_barrier((note, shipped[1]))
    copies = jnp.broadcast_to(note[None], (Z_ * X_ * Y_ * C_,) + note.shape)
    close_note = jnp.sum(lax.all_to_all(copies, ("basin", "tm"), 0, 0, tiled=False), axis=0)
    return plane_finish([open_note, close_note], shipped, incidence, first_guess)


def solution(mesh):
    planes = dict(mesh.shape) == {"basin": Z_ * X_, "tm": Y_ * C_}
    in_specs = (
        P("basin", None, None),
        P("basin"),
        P("basin"),
        P(),
        P("basin", "tm"),
        P("basin", "tm"),
    )
    return jax.shard_map(
        plane_shards if planes else shards, mesh=mesh, in_specs=in_specs, out_specs=P("basin", "tm"), check_vma=False
    )
```

```python
import functools

import jax
import jax.numpy as jnp
import numpy as np
from jax import lax
from jax.experimental import pallas as pl
from jax.experimental.pallas import tpu as pltpu
from jax.sharding import PartitionSpec as P

F32 = jnp.float32
BF16 = jnp.bfloat16
HIGH = lax.Precision.HIGHEST
SPAN = 256
MIB = 1024 * 1024


SMALL = pl.CostEstimate(flops=1, bytes_accessed=1, transcendentals=0)


def params(mib=16):
    return pltpu.CompilerParams(vmem_limit_bytes=mib * MIB)


def transforms():
    half = SPAN // 2
    freq = 2.0 * np.pi * (np.arange(half) + 0.5) / SPAN
    phase = np.arange(SPAN)[:, None] * freq[None, :]
    forward = np.concatenate([np.cos(phase), -np.sin(phase)], axis=1)
    inverse = forward.T * (2.0 / SPAN)
    return (
        jnp.asarray(forward, F32),
        jnp.asarray(inverse[:, :half], F32),
        jnp.asarray(inverse[:, half:], F32),
    )


def dot(a, b):
    return jnp.dot(a, b, preferred_element_type=F32)


def exact(a, b):
    return jnp.dot(a, b, precision=HIGH, preferred_element_type=F32)


def pieces(value, count):
    out = []
    for _ in range(count):
        piece = value.astype(BF16)
        out.append(piece)
        value = value - piece.astype(F32)
    return out


def pick(hot, value):
    return sum(dot(hot, piece) for piece in pieces(value, 3))


def prepare_kernel(inc_ref, field_ref, partial_ref, gram_ref):
    blocks, slots, width = inc_ref.shape
    rows = blocks * slots
    weights = inc_ref[...].astype(F32).astype(BF16)
    for b in range(blocks):
        value = field_ref[pl.ds(b * width, width), :]
        partial_ref[pl.ds(b * slots, slots), :] = pick(weights[b], value)
    flat = weights.reshape(rows, width)
    full = lax.dot_general(flat, flat, (((1,), (1,)), ((), ())), preferred_element_type=F32)
    row = lax.broadcasted_iota(jnp.int32, (rows, rows), 0)
    col = lax.broadcasted_iota(jnp.int32, (rows, rows), 1)
    own = jnp.where(row // slots == col // slots, full, 0.0)
    gram_ref[...] = jnp.sum(own.reshape(blocks, slots, rows), axis=0)


def prepare(incidence, field):
    blocks, slots, width = incidence.shape
    hours = field.shape[1]
    step = 8
    return pl.pallas_call(
        prepare_kernel,
        grid=(blocks // step,),
        in_specs=[
            pl.BlockSpec((step, slots, width), lambda i: (i, 0, 0)),
            pl.BlockSpec((step * width, hours), lambda i: (i, 0)),
        ],
        out_specs=[
            pl.BlockSpec((step * slots, hours), lambda i: (i, 0)),
            pl.BlockSpec((slots, step * slots), lambda i: (0, i)),
        ],
        out_shape=[
            jax.ShapeDtypeStruct((blocks * slots, hours), F32),
            jax.ShapeDtypeStruct((slots, blocks * slots), F32),
        ],
        compiler_params=params(56),
        name="prepare",
    )(incidence, field)


def table_kernel(gauge_ref, partial_ref, out_ref):
    slots = partial_ref.shape[0]
    rows = out_ref.shape[0]
    first = pl.program_id(0) * rows
    gauge = lax.broadcasted_iota(jnp.int32, (rows, slots), 0) + first
    hot = jnp.where(gauge_ref[...] == gauge, 1.0, 0.0).astype(BF16)
    out_ref[...] = pick(hot, partial_ref[...])


def table(row_gauge, partial, gauges):
    slots, hours = partial.shape
    step = 256
    return pl.pallas_call(
        table_kernel,
        grid=(gauges // step,),
        in_specs=[
            pl.BlockSpec((1, slots), lambda i: (0, 0)),
            pl.BlockSpec((slots, hours), lambda i: (0, 0)),
        ],
        out_specs=pl.BlockSpec((step, hours), lambda i: (i, 0)),
        out_shape=jax.ShapeDtypeStruct((gauges, hours), F32),
        compiler_params=params(56),
        name="table",
    )(row_gauge.reshape(1, slots), partial)


def couple_kernel(first_ref, lane_ref, sub_ref, gram_ref, high_ref, low_ref, near_ref):
    slots = gram_ref.shape[0]
    count = lane_ref.shape[1]
    rows, cols = high_ref.shape
    tile = 256
    first = first_ref[0]

    @pl.when(pl.program_id(0) == 0)
    def _():
        row = lax.broadcasted_iota(jnp.int32, (tile, tile), 0)
        col = lax.broadcasted_iota(jnp.int32, (tile, tile), 1)
        same = row // slots == col // slots
        mine = lax.broadcasted_iota(jnp.int32, (rows, tile), 0) + first

        def body(i, carry):
            here = pl.ds(pl.multiple_of(i * tile, tile), tile)
            block = jnp.concatenate([gram_ref[:, here]] * (tile // slots), axis=0)
            block = jnp.where(same, block, 0.0).astype(BF16)
            hot = jnp.where(lane_ref[:, here] == mine, 1.0, 0.0).astype(BF16)
            near_ref[:, here] = dot(hot, block)
            return carry

        lax.fori_loop(0, count // tile, body, 0)

    def chunk(i, total):
        here = pl.ds(pl.multiple_of(i * 1024, 1024), 1024)
        gauge = lax.broadcasted_iota(jnp.int32, (1024, cols), 1) + pl.program_id(0) * cols
        hot = jnp.where(sub_ref[here, :] == gauge, 1.0, 0.0).astype(BF16)
        near = near_ref[:, here]
        high = near.astype(BF16)
        low = (near - high.astype(F32)).astype(BF16)
        return total + dot(high, hot) + dot(low, hot)

    total = lax.fori_loop(0, count // 1024, chunk, jnp.zeros((rows, cols), F32))
    high, low = pieces(total, 2)
    high_ref[...] = high
    low_ref[...] = low


def couple(first, row_gauge, gram, rows, gauges):
    count = row_gauge.shape[0]
    step = 256
    return pl.pallas_call(
        couple_kernel,
        grid=(gauges // step,),
        in_specs=[
            pl.BlockSpec(memory_space=pltpu.SMEM),
            pl.BlockSpec((1, count), lambda i: (0, 0)),
            pl.BlockSpec((count, 1), lambda i: (0, 0)),
            pl.BlockSpec(gram.shape, lambda i: (0, 0)),
        ],
        out_specs=[pl.BlockSpec((rows, step), lambda i: (0, i))] * 2,
        out_shape=[jax.ShapeDtypeStruct((rows, gauges), BF16)] * 2,
        scratch_shapes=[pltpu.VMEM((rows, count), F32)],
        compiler_params=params(56),
        name="couple",
    )(first, row_gauge.reshape(1, count), row_gauge.reshape(count, 1), gram)


def mix_kernel(high_ref, low_ref, value_ref, out_ref):
    high = high_ref[...]
    low = low_ref[...]
    one, two, three = pieces(value_ref[...], 3)
    out_ref[...] = (dot(high, three) + dot(low, two)) + (dot(high, two) + dot(low, one)) + dot(high, one)


def mix(high, low, value):
    return pl.pallas_call(
        mix_kernel,
        out_shape=jax.ShapeDtypeStruct((high.shape[0], value.shape[1]), F32),
        compiler_params=params(56),
        name="mix",
    )(high, low, value)


def spectrum_kernel(class_ref, kernels_ref, forward_ref, out_ref):
    rows = class_ref.shape[0]
    classes, taps = kernels_ref.shape
    kind = lax.broadcasted_iota(jnp.int32, (rows, classes), 1)
    hot = jnp.where(class_ref[...] == kind, 1.0, 0.0)
    out_ref[...] = exact(exact(hot, kernels_ref[...]), forward_ref[pl.ds(0, taps), :])


def spectrum(gauge_kernel, kernels, forward):
    rows = gauge_kernel.shape[0]
    return pl.pallas_call(
        spectrum_kernel,
        out_shape=jax.ShapeDtypeStruct((rows, SPAN), F32),
        compiler_params=params(56),
        name="spectrum",
    )(gauge_kernel.reshape(rows, 1), kernels, forward)


def delayed(before, here, after, spec, forward, inverse_last):
    rows, half = here.shape
    stacked = jnp.concatenate(
        [jnp.concatenate([before, here], axis=1), jnp.concatenate([here, after], axis=1)], axis=0
    )
    waves = exact(stacked, forward)
    real, imag = waves[:, :half], waves[:, half:]
    kr = jnp.concatenate([spec[:, :half]] * 2, axis=0)
    ki = jnp.concatenate([spec[:, half:]] * 2, axis=0)
    turned = jnp.concatenate([real * kr - imag * ki, real * ki + imag * kr], axis=1)
    out = exact(turned, inverse_last)
    return out[:rows], out[rows:]


def advanced(here, after, spec, forward, inverse_first):
    half = here.shape[1]
    waves = exact(jnp.concatenate([here, after], axis=1), forward)
    real, imag = waves[:, :half], waves[:, half:]
    kr, ki = spec[:, :half], spec[:, half:]
    turned = jnp.concatenate([real * kr + imag * ki, imag * kr - real * ki], axis=1)
    return exact(turned, inverse_first)


def lanes(a, b):
    return jnp.sum(a * b, axis=0, keepdims=True)


def total(ref, row):
    return jnp.sum(ref[row : row + 1, :], axis=1, keepdims=True)


def ratios(ref):
    square = total(ref, 0)
    alpha = jnp.sqrt(square)
    beta = jnp.sqrt(jnp.maximum(total(ref, 1) / square - 2.0 * total(ref, 2) + square, 0.0))
    return alpha, beta


def first_kernel(
    more_ref, sums_ref, observed_ref, spec_ref, forward_ref, first_ref, last_ref, out_ref, note_ref
):
    rows, half = observed_ref.shape[0] // 2, observed_ref.shape[1]
    spec, forward = spec_ref[...], forward_ref[...]
    before, here, after = (sums_ref[pl.ds(i * rows, rows), :] for i in range(3))
    now, later = delayed(before, here, after, spec, forward, last_ref[...])
    start = observed_ref[pl.ds(0, rows), :] - now
    start_later = (observed_ref[pl.ds(rows, rows), :] - later) * more_ref[0]
    out_ref[...] = advanced(start, start_later, spec, forward, first_ref[...])
    note_ref[...] = jnp.concatenate([lanes(start, start), jnp.zeros((7, half), F32)], axis=0)


def first_step(more, sums, observed, spec, mats):
    rows, half = spec.shape[0], observed.shape[1]
    return pl.pallas_call(
        first_kernel,
        in_specs=[pl.BlockSpec(memory_space=pltpu.SMEM)] + [pl.BlockSpec(memory_space=pltpu.VMEM)] * 6,
        out_shape=[jax.ShapeDtypeStruct((rows, half), F32), jax.ShapeDtypeStruct((8, half), F32)],
        compiler_params=params(56),
        name="first_step",
    )(more, sums, observed, spec, *mats)


def step_kernel(
    opening,
    final,
    more_ref,
    note_ref,
    sums_ref,
    spec_ref,
    forward_ref,
    first_ref,
    last_ref,
    pulled_ref,
    *refs,
):
    if opening:
        state_ref = None
    else:
        state_ref, *refs = refs
    if final:
        (out_note_ref,) = refs
    else:
        new_ref, out_ref, out_note_ref = refs
    rows, half = pulled_ref.shape
    spec, forward = spec_ref[...], forward_ref[...]
    if opening:
        scale = 1.0 / jnp.sqrt(total(note_ref, 0))
        along = sums_ref[...] * scale
        new_s, new_su = along, along
        new_zu = pulled_ref[...] * scale
        new_z = new_zu
    else:
        alpha, beta = ratios(note_ref)
        a, b, g = 1.0 / (alpha * beta), alpha / beta, beta / alpha
        wide = pl.ds(0, 3 * rows), pl.ds(3 * rows, 3 * rows)
        new_su = sums_ref[...] * a - state_ref[wide[1], :] * b
        new_s = new_su - state_ref[wide[0], :] * g
        new_zu = pulled_ref[...] * a - state_ref[pl.ds(7 * rows, rows), :] * b
        new_z = new_zu - state_ref[pl.ds(6 * rows, rows), :] * g
    before, here, after = (new_s[i * rows : (i + 1) * rows] for i in range(3))
    now, later = delayed(before, here, after, spec, forward, last_ref[...])
    out_note_ref[...] = jnp.concatenate(
        [lanes(new_z, here), lanes(now, now), lanes(new_zu, here), jnp.zeros((5, half), F32)], axis=0
    )
    if not final:
        new_ref[pl.ds(0, 3 * rows), :] = new_s
        new_ref[pl.ds(3 * rows, 3 * rows), :] = new_su
        new_ref[pl.ds(6 * rows, rows), :] = new_z
        new_ref[pl.ds(7 * rows, rows), :] = new_zu
        out_ref[...] = advanced(now, later * more_ref[0], spec, forward, first_ref[...])


def next_step(more, note, sums, spec, mats, pulled, state, final):
    rows, half = pulled.shape
    opening = state is None
    shapes = [
        jax.ShapeDtypeStruct((8 * rows, half), F32),
        jax.ShapeDtypeStruct((rows, half), F32),
        jax.ShapeDtypeStruct((8, half), F32),
    ]
    args = [more, note, sums, spec, *mats, pulled] + ([] if opening else [state])
    return pl.pallas_call(
        functools.partial(step_kernel, opening, final),
        in_specs=[pl.BlockSpec(memory_space=pltpu.SMEM)]
        + [pl.BlockSpec(memory_space=pltpu.VMEM)] * (len(args) - 1),
        out_shape=shapes[2:] if final else shapes,
        compiler_params=params(56),
        name="next_step",
    )(*args)


def weights_of(notes):
    start = jnp.sqrt(total(notes[0], 0))
    zero = jnp.zeros_like(start)
    units = [1.0 / start, zero, zero]
    z, zu = list(units), list(units)
    phibar = start
    alpha, beta = ratios(notes[1])
    rhobar = alpha
    w = [value / alpha for value in z]
    result = [zero] * 3
    steps = len(notes) - 1
    for k in range(steps):
        rho = jnp.sqrt(rhobar * rhobar + beta * beta)
        cosine, sine = rhobar / rho, beta / rho
        phi, phibar = cosine * phibar, sine * phibar
        result = [r + phi / rho * value for r, value in zip(result, w)]
        if k < steps - 1:
            a, b, g = 1.0 / (alpha * beta), alpha / beta, beta / alpha
            zu = [(a if i == k + 1 else 0.0) - b * value for i, value in enumerate(zu)]
            z = [value - g * old for value, old in zip(zu, z)]
            alpha, beta = ratios(notes[k + 2])
            theta = sine * alpha
            rhobar = -cosine * alpha
            w = [value / alpha - theta / rho * old for value, old in zip(z, w)]
    return result


def finish_kernel(n0, n1, n2, n3, gauge_ref, q0, q1, q2, inc_ref, field_ref, out_ref, rows_ref):
    blocks, slots, width = inc_ref.shape
    count = rows_ref.shape[0]
    gauges = q0.shape[0]
    step = pl.program_id(0)

    @pl.when(step == 0)
    def _():
        e0, e1, e2 = weights_of([n0, n1, n2, n3])
        width_ = 512

        def body(i, value):
            here = pl.ds(pl.multiple_of(i * width_, width_), width_)
            mixed = q0[here, :] * e0 + q1[here, :] * e1 + q2[here, :] * e2
            gauge = lax.broadcasted_iota(jnp.int32, (count, width_), 1) + i * width_
            hot = jnp.where(gauge_ref[...] == gauge, 1.0, 0.0).astype(BF16)
            return value + pick(hot, mixed)

        rows_ref[...] = lax.fori_loop(0, gauges // width_, body, jnp.zeros(rows_ref.shape, F32))

    weights = inc_ref[...].astype(F32).astype(BF16)
    for b in range(blocks):
        here = pl.ds(b * width, width)
        rows = rows_ref[pl.ds(pl.multiple_of((step * blocks + b) * slots, slots), slots), :]
        added = sum(
            lax.dot_general(weights[b], piece, (((0,), (0,)), ((), ())), preferred_element_type=F32)
            for piece in pieces(rows, 3)
        )
        out_ref[here, :] = field_ref[here, :] + added


def finish(notes, row_gauge, gathered, incidence, field):
    blocks, slots, width = incidence.shape
    hours = field.shape[1]
    count = row_gauge.shape[0]
    step = 8
    whole = lambda shape: pl.BlockSpec(shape, lambda i: (0, 0))
    return pl.pallas_call(
        finish_kernel,
        grid=(blocks // step,),
        in_specs=[whole(n.shape) for n in notes]
        + [whole((count, 1))]
        + [whole(q.shape) for q in gathered]
        + [
            pl.BlockSpec((step, slots, width), lambda i: (i, 0, 0)),
            pl.BlockSpec((step * width, hours), lambda i: (i, 0)),
        ],
        out_specs=pl.BlockSpec((step * width, hours), lambda i: (i, 0)),
        out_shape=jax.ShapeDtypeStruct(field.shape, F32),
        scratch_shapes=[pltpu.VMEM((count, hours), F32)],
        compiler_params=params(56),
        name="finish",
    )(*notes, row_gauge.reshape(count, 1), *gathered, incidence, field)


def shifted(value, axis, by):
    devices = lax.axis_size(axis)
    pairs = [(i, i + by) for i in range(devices) if 0 <= i + by < devices]
    return lax.ppermute(value, axis, pairs)


def window(value):
    return jnp.concatenate([shifted(value, "tm", 1), value, shifted(value, "tm", -1)], axis=0)


def gathered_rows(value):
    owners = lax.axis_size("basin")
    copies = jnp.broadcast_to(value[None], (owners,) + value.shape)
    return lax.all_to_all(copies, "basin", 0, 0, tiled=False)


def over_hours(note):
    blocks = lax.axis_size("tm")
    result = note
    for by in range(1, blocks):
        result = result + lax.ppermute(note, "tm", [(i, (i + by) % blocks) for i in range(blocks)])
    return result


def shards(incidence, row_gauge, gauge_kernel, kernels, observed, first_guess):
    owners = lax.axis_size("basin")
    rows, hours = observed.shape
    gauges = rows * owners
    mats = transforms()
    spec = spectrum(gauge_kernel, kernels, mats[0])
    more = (lax.axis_index("tm") < lax.axis_size("tm") - 1).astype(F32).reshape(1)
    partial, gram = prepare(incidence, first_guess)
    all_gram = lax.all_gather(gram, "basin", axis=1, tiled=True)
    all_rows = lax.all_gather(row_gauge, "basin", axis=0, tiled=True)
    dense = table(row_gauge, partial, gauges).reshape(owners, rows, hours)
    sums = jnp.sum(lax.all_to_all(dense, "basin", 0, 0, tiled=False), axis=0)
    both = jnp.concatenate([observed, shifted(observed, "tm", -1)], axis=0)
    first = (lax.axis_index("basin") * rows).astype(jnp.int32).reshape(1)
    high, low = couple(first, all_rows, all_gram, rows, gauges)

    pulled, note = first_step(more, window(sums), both, spec, mats)
    notes, kept, state = [], [], None
    for k in range(3):
        everyone = gathered_rows(jnp.concatenate([pulled, note], axis=0))
        value = everyone[:, :rows].reshape(gauges, hours)
        notes.append(over_hours(jnp.sum(everyone[:, rows:], axis=0)))
        kept.append(value)
        around = window(mix(high, low, value))
        final = k == 2
        result = next_step(more, notes[-1], around, spec, mats, pulled, state, final)
        if final:
            (note,) = result
        else:
            state, pulled, note = result
    notes.append(over_hours(jnp.sum(gathered_rows(note), axis=0)))
    return finish(notes, row_gauge, kept, incidence, first_guess)


Z_, X_, Y_, C_ = 4, 2, 2, 2
NOTE = 8


def device(z, x, y, c):
    return (z * X_ + x) * (Y_ * C_) + y * C_ + c


def moved(value, where):
    pairs = []
    for z, x, y, c in np.ndindex(Z_, X_, Y_, C_):
        target = where(z, x, y, c)
        if target is not None:
            pairs.append((device(z, x, y, c), device(*target)))
    return lax.ppermute(value, ("basin", "tm"), pairs)


def to_plane(z, x, y, c):
    return 2 * y + c, x, z & 1, z >> 1


def to_plane_before(z, x, y, c):
    t = 2 * y + c
    return (t - 1, x, z & 1, z >> 1) if t else None


def from_plane(z, x, y, c):
    return 2 * c + y, x, z >> 1, z & 1


def over_x(z, x, y, c):
    return z, 1 - x, y, c


def over_y(z, x, y, c):
    return z, x, 1 - y, c


def over_xy(z, x, y, c):
    return z, 1 - x, 1 - y, c


def over_core(z, x, y, c):
    return z, x, y, 1 - c


def z_pair(z, x, y, c):
    return z ^ 1, x, y, c


def z_middle(z, x, y, c):
    return (3 - z, x, y, c) if z in (1, 2) else None


def z_two(z, x, y, c):
    return z ^ 2, x, y, c


def z_mirror(z, x, y, c):
    return 3 - z, x, y, c


SQUARE = (over_x, over_y, over_xy)


def split_constant(value):
    out = []
    for _ in range(3):
        piece = value.astype(jnp.bfloat16)
        out.append(jnp.asarray(piece))
        value = value - piece.astype(np.float64)
    return out


def turned_transforms():
    half = SPAN // 2
    freq = 2.0 * np.pi * (np.arange(half) + 0.5) / SPAN
    phase = freq[:, None] * np.arange(SPAN)[None, :]
    forward = np.concatenate([np.cos(phase), -np.sin(phase)], axis=0)
    inverse = forward.T * (2.0 / SPAN)
    return split_constant(forward), split_constant(inverse[:half]), split_constant(inverse[half:])


def product(mats, value, order):
    parts = pieces(value, order)
    result = None
    for level in reversed(range(order)):
        for i in range(level + 1):
            term = dot(mats[i][...], parts[level - i])
            result = term if result is None else result + term
    return result


def turn(waves, spec, sign):
    half = waves.shape[0] // 2
    real, imag = waves[:half], waves[half:]
    kr, ki = spec[:half], spec[half:] * sign
    return jnp.concatenate([real * kr - imag * ki, real * ki + imag * kr], axis=0)


def plane_delayed(before, here, after, spec, forward, last, order):
    out = []
    for pair in ((before, here), (here, after)):
        waves = product(forward, jnp.concatenate(pair, axis=0), order)
        out.append(product(last, turn(waves, spec, 1.0), order))
    return out


def plane_advanced(here, after, spec, forward, first, order):
    waves = product(forward, jnp.concatenate([here, after], axis=0), order)
    return product(first, turn(waves, spec, -1.0), order)


def describe_kernel(inc_ref, gauge_ref, kind_ref, seen_ref, out_ref):
    blocks, slots, width = inc_ref.shape
    rows, hours = seen_ref.shape
    count = blocks * slots
    tile = 8
    side = tile * slots
    weights = inc_ref[...].astype(F32).astype(BF16)
    row = lax.broadcasted_iota(jnp.int32, (side, side), 0)
    col = lax.broadcasted_iota(jnp.int32, (side, side), 1)
    same = row // slots == col // slots
    for i in range(blocks // tile):
        flat = weights[i * tile : (i + 1) * tile].reshape(side, width)
        full = lax.dot_general(flat, flat, (((1,), (1,)), ((), ())), preferred_element_type=F32)
        own = jnp.where(same, full, 0.0)
        out_ref[pl.ds(0, slots), pl.ds(i * side, side)] = jnp.sum(own.reshape(tile, slots, side), axis=0)
    kinds = jnp.concatenate([kind_ref[...].astype(F32), jnp.zeros((1, count - rows), F32)], axis=1)
    out_ref[pl.ds(slots, 8), :] = jnp.concatenate(
        [gauge_ref[...].astype(F32), kinds, jnp.zeros((6, count), F32)], axis=0
    )
    turned = jnp.transpose(seen_ref[...])
    step = hours * rows // count
    for i in range(count // rows):
        out_ref[pl.ds(slots + 8, step), pl.ds(i * rows, rows)] = turned[i * step : (i + 1) * step]


def describe(incidence, row_gauge, gauge_kernel, observed):
    blocks, slots, _ = incidence.shape
    rows, hours = observed.shape
    count = blocks * slots
    return pl.pallas_call(
        describe_kernel,
        out_shape=jax.ShapeDtypeStruct((slots + 8 + hours * rows // count, count), F32),
        compiler_params=params(),
        name="describe",
        cost_estimate=SMALL,
    )(incidence, row_gauge.reshape(1, count), gauge_kernel.reshape(1, rows), observed)


def send_kernel(inc_ref, field_ref, out_ref):
    blocks, slots, width = inc_ref.shape
    weights = inc_ref[...].astype(F32).astype(BF16)
    parts = []
    for b in range(blocks):
        parts.append(pick(weights[b], field_ref[pl.ds(b * width, width), :]))
    out_ref[...] = jnp.transpose(jnp.concatenate(parts, axis=0))


def send(incidence, field):
    blocks, slots, width = incidence.shape
    hours = field.shape[1]
    step = 8
    return pl.pallas_call(
        send_kernel,
        grid=(blocks // step,),
        in_specs=[
            pl.BlockSpec((step, slots, width), lambda i: (i, 0, 0)),
            pl.BlockSpec((step * width, hours), lambda i: (i, 0)),
        ],
        out_specs=pl.BlockSpec((hours, step * slots), lambda i: (0, i)),
        out_shape=jax.ShapeDtypeStruct((hours, blocks * slots), F32),
        compiler_params=params(),
        name="send",
        cost_estimate=SMALL,
    )(incidence, field)


def hot_rows(gauge, first, rows):
    mine = (lax.broadcasted_iota(jnp.int32, (rows, gauge.shape[1]), 0) + first).astype(F32)
    return jnp.where(gauge == mine, 1.0, 0.0).astype(BF16)


def spread_kernel(first_ref, mine_ref, other_ref, meta_ref, meta_other_ref, *out_refs):
    rows = out_refs[0].shape[1]
    where = meta_ref.shape[0] - 8
    for m, out_ref in enumerate(out_refs):
        result = None
        for ref, meta in ((mine_ref, meta_ref), (other_ref, meta_other_ref)):
            hot = hot_rows(meta[where : where + 1, :], first_ref[m], rows)
            for piece in reversed(pieces(ref[...], 3)):
                term = lax.dot_general(
                    piece, hot, (((1,), (1,)), ((), ())), preferred_element_type=F32
                )
                result = term if result is None else result + term
        out_ref[...] = result


def spread(first, parcels, metas, rows):
    hours = parcels[0].shape[0]
    return pl.pallas_call(
        spread_kernel,
        in_specs=[pl.BlockSpec(memory_space=pltpu.SMEM)] + [pl.BlockSpec(memory_space=pltpu.VMEM)] * 4,
        out_shape=[jax.ShapeDtypeStruct((hours, rows), F32)] * 4,
        compiler_params=params(),
        name="spread",
        cost_estimate=SMALL,
    )(first, *parcels, *metas)


def plane_couple_kernel(last, first_ref, *refs):
    if last:
        a_ref, b_ref, before_ref, high_ref, low_ref, total_ref, meta_ref = refs
        total_ref[...] = before_ref[...]
    else:
        a_ref, b_ref, total_ref, meta_ref = refs
        total_ref[...] = jnp.zeros_like(total_ref)
    height, double = a_ref.shape
    slots = height - 8
    count = double // 2
    cols, rows = total_ref.shape
    tile = 256
    for i, ref in enumerate((a_ref, b_ref)):
        for j in range(2):
            meta_ref[2 * i + j] = ref[:, j * count : (j + 1) * count]
    row = lax.broadcasted_iota(jnp.int32, (tile, tile), 0)
    col = lax.broadcasted_iota(jnp.int32, (tile, tile), 1)
    same = row // slots == col // slots

    def body(i, carry):
        gauge = meta_ref[i, slots : slots + 1, :]
        near = []
        for j in range(count // tile):
            here = slice(j * tile, (j + 1) * tile)
            block = jnp.concatenate([meta_ref[i, :slots, here]] * (tile // slots), axis=0)
            block = jnp.where(same, block, 0.0).astype(BF16)
            mine = jnp.concatenate(
                [hot_rows(gauge[:, here], first_ref[4 + h], rows // 2) for h in range(2)], axis=0
            )
            near.append(
                lax.dot_general(block, mine, (((1,), (1,)), ((), ())), preferred_element_type=F32)
            )
        near = jnp.concatenate(near, axis=0)
        high = near.astype(BF16)
        rest = near - high.astype(F32)
        hot = jnp.concatenate([hot_rows(gauge, first_ref[m], cols // 4) for m in range(4)], axis=0)
        total_ref[...] += dot(hot, high)

        @pl.when(jnp.max(jnp.abs(rest)) > 0.0)
        def _():
            total_ref[...] += dot(hot, rest.astype(BF16))

        return carry

    lax.fori_loop(0, 4, body, 0)
    if last:
        high, low = pieces(total_ref[...], 2)
        high_ref[...] = high
        low_ref[...] = low


def plane_couple(first, metas, rows, before=None):
    height, double = metas[0].shape
    shape = (4 * rows, 2 * rows)
    last = before is not None
    args = [first, *metas] + ([before] if last else [])
    scratch = [pltpu.VMEM((4, height, double // 2), F32)]
    return pl.pallas_call(
        functools.partial(plane_couple_kernel, last),
        in_specs=[pl.BlockSpec(memory_space=pltpu.SMEM)]
        + [pl.BlockSpec(memory_space=pltpu.VMEM)] * (len(args) - 1),
        out_shape=[jax.ShapeDtypeStruct(shape, BF16)] * 2 if last else jax.ShapeDtypeStruct(shape, F32),
        scratch_shapes=([pltpu.VMEM(shape, F32)] if last else []) + scratch,
        compiler_params=params(),
        name="plane_couple",
        cost_estimate=pl.CostEstimate(
            flops=2 * 2 * double * 8 * rows * rows, bytes_accessed=2_000_000, transcendentals=0
        ),
    )(*args)


def plane_mix_kernel(
    first_ref, high_ref, low_ref, meta_ref, meta_other_ref, a_ref, b_ref, c_ref, d_ref, mine_ref, other_ref, rows_ref
):
    refs = (a_ref, b_ref, c_ref, d_ref)
    height, rows = a_ref.shape
    hours = height - NOTE
    body, tail = pl.ds(0, hours), pl.ds(hours, NOTE)
    value = jnp.concatenate([ref[body, :] for ref in refs], axis=1)
    one, two = pieces(value, 2)
    high, low = high_ref[...], low_ref[...]
    result = (dot(two, high) + dot(one, low)) + dot(one, high)
    note = sum(ref[tail, :] for ref in refs)
    mine_ref[body, :] = result[:, :rows]
    other_ref[body, :] = result[:, rows:]
    mine_ref[tail, :] = note
    other_ref[tail, :] = note
    where = meta_ref.shape[0] - 8
    for ref in (meta_ref, meta_other_ref):
        gauge = ref[where : where + 1, :]
        hot = jnp.concatenate([hot_rows(gauge, first_ref[m], rows) for m in range(4)], axis=0)
        picked = dot(two, hot) + dot(one, hot)
        if ref is meta_ref:
            rows_ref[...] = picked
        else:
            for i in range(gauge.shape[1] // rows):
                other_ref[pl.ds(height + i * hours, hours), :] = picked[:, i * rows : (i + 1) * rows]


def plane_mix(first, coupling, metas, values):
    height, rows = values[0].shape
    hours = height - NOTE
    slots = metas[0].shape[1]
    return pl.pallas_call(
        plane_mix_kernel,
        in_specs=[pl.BlockSpec(memory_space=pltpu.SMEM)] + [pl.BlockSpec(memory_space=pltpu.VMEM)] * 8,
        out_shape=[
            jax.ShapeDtypeStruct((height, rows), F32),
            jax.ShapeDtypeStruct((height + slots // rows * hours, rows), F32),
            jax.ShapeDtypeStruct((hours, slots), F32),
        ],
        compiler_params=params(),
        name="plane_mix",
        cost_estimate=SMALL,
    )(first, *coupling, *metas, *values)


def plane_spectrum_kernel(class_ref, kernels_ref, f0_ref, f1_ref, f2_ref, out_ref):
    classes, taps = kernels_ref.shape
    kind = class_ref[class_ref.shape[0] - 7 : class_ref.shape[0] - 6, : out_ref.shape[1]]
    hot = jnp.where(
        lax.broadcasted_iota(jnp.int32, (classes, kind.shape[1]), 0).astype(F32) == kind, 1.0, 0.0
    ).astype(BF16)
    chosen = None
    for piece in reversed(pieces(jnp.transpose(kernels_ref[...]), 3)):
        term = dot(piece, hot)
        chosen = term if chosen is None else chosen + term
    mats = [ref[:, :taps] for ref in (f0_ref, f1_ref, f2_ref)]
    out_ref[...] = product(mats, chosen, 3)


def plane_spectrum(meta, kernels, forward, rows):
    return pl.pallas_call(
        plane_spectrum_kernel,
        out_shape=jax.ShapeDtypeStruct((SPAN, rows), F32),
        compiler_params=params(),
        name="plane_spectrum",
        cost_estimate=SMALL,
    )(meta, kernels, *forward)


def sides(even, pair, middle):
    return jnp.where(even, middle, pair), jnp.where(even, pair, middle)


def plane_first_kernel(flag_ref, *refs):
    sums, seen, (spec_ref, *mats, out_ref) = refs[:3], refs[3:6], refs[6:]
    forward, first, last = mats[0:3], mats[3:6], mats[6:9]
    hours, rows = sums[0].shape
    spec = spec_ref[...]
    even = flag_ref[0] > 0.5
    before, after = sides(even, sums[1][...], sums[2][...])
    now, later = plane_delayed(before, sums[0][...], after, spec, forward, last, 3)
    start = seen[0][...] - now
    start_later = (sides(even, seen[1][...], seen[2][...])[1] - later) * flag_ref[1]
    out_ref[pl.ds(0, hours), :] = plane_advanced(start, start_later, spec, forward, first, 3)
    out_ref[pl.ds(hours, NOTE), :] = jnp.concatenate(
        [lanes(start, start), jnp.zeros((NOTE - 1, rows), F32)], axis=0
    )


def plane_first(flags, sums, seen, spec, mats):
    hours, rows = sums[0].shape
    args = [flags, *sums, *seen, spec, *mats]
    return pl.pallas_call(
        plane_first_kernel,
        in_specs=[pl.BlockSpec(memory_space=pltpu.SMEM)]
        + [pl.BlockSpec(memory_space=pltpu.VMEM)] * (len(args) - 1),
        out_shape=jax.ShapeDtypeStruct((hours + NOTE, rows), F32),
        compiler_params=params(),
        name="plane_first",
        cost_estimate=SMALL,
    )(*args)


def plane_open_kernel(flag_ref, here_ref, pair_ref, middle_ref, pulled_ref, spec_ref, *refs):
    mats, (out_ref, now_ref) = refs[:9], refs[9:]
    forward, first, last = mats[0:3], mats[3:6], mats[6:9]
    height, rows = pulled_ref.shape
    hours = height - NOTE
    tail, body = pl.ds(hours, NOTE), pl.ds(0, hours)
    spec = spec_ref[...]
    here = here_ref[body, :]
    before, after = sides(flag_ref[0] > 0.5, pair_ref[body, :], middle_ref[body, :])
    now, later = plane_delayed(before, here, after, spec, forward, last, 2)
    out_ref[body, :] = plane_advanced(now, later * flag_ref[1], spec, forward, first, 2)
    out_ref[tail, :] = jnp.concatenate(
        [
            lanes(pulled_ref[body, :], here),
            lanes(now, now),
            pulled_ref[hours : hours + 1, :],
            jnp.zeros((NOTE - 3, rows), F32),
        ],
        axis=0,
    )
    now_ref[...] = now


def plane_open(flags, sums, pulled, spec, mats):
    height, rows = pulled.shape
    args = [flags, *sums, pulled, spec, *mats]
    return pl.pallas_call(
        plane_open_kernel,
        in_specs=[pl.BlockSpec(memory_space=pltpu.SMEM)]
        + [pl.BlockSpec(memory_space=pltpu.VMEM)] * (len(args) - 1),
        out_shape=[
            jax.ShapeDtypeStruct((height, rows), F32),
            jax.ShapeDtypeStruct((height - NOTE, rows), F32),
        ],
        compiler_params=params(),
        name="plane_open",
        cost_estimate=SMALL,
    )(*args)


def opening(ref):
    start = total(ref, 2)
    square = total(ref, 0) / start
    alpha = jnp.sqrt(square)
    beta = jnp.sqrt(jnp.maximum(total(ref, 1) / total(ref, 0) - square, 0.0))
    return 1.0 / jnp.sqrt(start), alpha, beta


def plane_step_kernel(flag_ref, here_ref, pair_ref, middle_ref, two_ref, mirror_ref, *refs):
    old_refs, (pulled_ref, old_z_ref, old_now_ref, spec_ref), refs = refs[:3], refs[3:7], refs[7:]
    mats, (total_ref, out_ref, kept_ref) = refs[:9], refs[9:]
    forward, first, last = mats[0:3], mats[3:6], mats[6:9]
    height, rows = pulled_ref.shape
    hours = height - NOTE
    tail, body = pl.ds(hours, NOTE), pl.ds(0, hours)
    total_ref[...] = (here_ref[tail, :] + pair_ref[tail, :]) + (two_ref[...] + mirror_ref[...])
    scale, alpha, beta = opening(total_ref)
    a, b, g = scale / (alpha * beta), scale * alpha / beta, scale * beta / alpha
    spec = spec_ref[...]
    s, su = [], []
    for ref, old_ref in zip((here_ref, pair_ref, middle_ref), old_refs):
        old = old_ref[body, :]
        su.append(ref[body, :] * a - old * b)
        s.append(su[-1] - old * g)
    zu = pulled_ref[body, :] * a - old_z_ref[body, :] * b
    z = zu - old_z_ref[body, :] * g
    before, after = sides(flag_ref[0] > 0.5, s[1], s[2])
    now, later = plane_delayed(before, s[0], after, spec, forward, last, 2)
    out_ref[body, :] = plane_advanced(now, later * flag_ref[1], spec, forward, first, 2)
    out_ref[tail, :] = jnp.concatenate(
        [lanes(z, s[0]), lanes(now, now), lanes(zu, s[0]), jnp.zeros((NOTE - 3, rows), F32)], axis=0
    )
    for i, value in enumerate((s[0], su[0], z, zu, now, now + old_now_ref[...] * g)):
        kept_ref[pl.ds(i * hours, hours), :] = value


def plane_step(flags, sums, two, mirror, old, pulled, old_z, old_now, spec, mats):
    height, rows = pulled.shape
    args = [flags, *sums, two, mirror, *old, pulled, old_z, old_now, spec, *mats]
    return pl.pallas_call(
        plane_step_kernel,
        in_specs=[pl.BlockSpec(memory_space=pltpu.SMEM)]
        + [pl.BlockSpec(memory_space=pltpu.VMEM)] * (len(args) - 1),
        out_shape=[
            jax.ShapeDtypeStruct((NOTE, rows), F32),
            jax.ShapeDtypeStruct((height, rows), F32),
            jax.ShapeDtypeStruct((6 * (height - NOTE), rows), F32),
        ],
        compiler_params=params(),
        name="plane_step",
        cost_estimate=SMALL,
    )(*args)


def plane_close_kernel(flag_ref, here_ref, pair_ref, middle_ref, pulled_ref, kept_ref, spec_ref, *refs):
    mats, (out_ref,) = refs[:9], refs[9:]
    forward, last = mats[0:3], mats[6:9]
    height, rows = pulled_ref.shape
    hours = height - NOTE
    body = pl.ds(0, hours)
    before, after = sides(flag_ref[0] > 0.5, pair_ref[body, :], middle_ref[body, :])
    here = here_ref[body, :]
    waves = product(forward, jnp.concatenate([before, here], axis=0), 2)
    now = product(last, turn(waves, spec_ref[...], 1.0), 2)
    s, su, z, zu, old_now, old_now_u = (kept_ref[pl.ds(i * hours, hours), :] for i in range(6))
    raw = pulled_ref[body, :]
    note = [pulled_ref[hours + i : hours + i + 1, :] for i in range(3)]
    for left in (raw, zu, z):
        note += [lanes(left, right) for right in (here, su, s)]
    parts = (now, old_now_u, old_now)
    for i in range(3):
        note += [lanes(parts[i], parts[j]) for j in range(i, 3)]
    note.append(jnp.zeros((24 - len(note), rows), F32))
    note = jnp.concatenate(note, axis=0)
    out_ref[...] = note[:, : rows // 2] + note[:, rows // 2 :]


def plane_close(flags, sums, pulled, kept, spec, mats):
    rows = pulled.shape[1]
    args = [flags, *sums, pulled, kept, spec, *mats]
    return pl.pallas_call(
        plane_close_kernel,
        in_specs=[pl.BlockSpec(memory_space=pltpu.SMEM)]
        + [pl.BlockSpec(memory_space=pltpu.VMEM)] * (len(args) - 1),
        out_shape=jax.ShapeDtypeStruct((24, rows // 2), F32),
        compiler_params=params(),
        name="plane_close",
        cost_estimate=SMALL,
    )(*args)


def plane_weights(open_ref, close_ref):
    scale, alpha, beta = opening(open_ref)
    start = 1.0 / scale
    phibar, rhobar = start, alpha
    zero = jnp.zeros_like(start)
    z = zu = [scale, zero, zero]
    w = [value / alpha for value in z]
    result = [zero] * 3
    for k in range(3):
        rho = jnp.sqrt(rhobar * rhobar + beta * beta)
        cosine, sine = rhobar / rho, beta / rho
        phi, phibar = cosine * phibar, sine * phibar
        result = [r + phi / rho * value for r, value in zip(result, w)]
        if k == 2:
            return result
        a, b, g = 1.0 / (alpha * beta), alpha / beta, beta / alpha
        zu = [-b * value for value in zu]
        zu[k + 1] = zu[k + 1] + (a * scale if k == 0 else a)
        z = [value - g * old for value, old in zip(zu, z)]
        if k == 0:
            square, norm, along = (total(close_ref, i) for i in range(3))
        else:
            plain = (a, -b, -g)
            cross = [[total(close_ref, 3 + 3 * i + j) for j in range(3)] for i in range(3)]
            along = sum(plain[i] * plain[j] * cross[i][j] for i in range(2) for j in range(3))
            square = along + sum(plain[2] * plain[j] * cross[2][j] for j in range(3))
            pairs = [(i, j) for i in range(3) for j in range(i, 3)]
            norm = sum(
                plain[i] * plain[j] * total(close_ref, 12 + n) * (1.0 if i == j else 2.0)
                for n, (i, j) in enumerate(pairs)
            )
        alpha = jnp.sqrt(square)
        beta = jnp.sqrt(jnp.maximum(norm / square - 2.0 * along + square, 0.0))
        theta = sine * alpha
        rhobar = -cosine * alpha
        w = [value / alpha - theta / rho * old for value, old in zip(z, w)]


def plane_finish_kernel(open_ref, close_ref, q0, q1, q2, inc_ref, field_ref, out_ref, rows_ref):
    blocks, slots, width = inc_ref.shape
    step = pl.program_id(0)

    @pl.when(step == 0)
    def _():
        e0, e1, e2 = plane_weights(open_ref, close_ref)
        rows_ref[...] = jnp.transpose(q0[...] * e0 + q1[...] * e1 + q2[...] * e2)

    weights = inc_ref[...].astype(F32).astype(BF16)
    for b in range(blocks):
        here = pl.ds(b * width, width)
        rows = rows_ref[pl.ds(pl.multiple_of((step * blocks + b) * slots, slots), slots), :]
        added = sum(
            lax.dot_general(weights[b], piece, (((0,), (0,)), ((), ())), preferred_element_type=F32)
            for piece in pieces(rows, 2)
        )
        out_ref[here, :] = field_ref[here, :] + added


def plane_finish(notes, rows, incidence, field):
    blocks, slots, width = incidence.shape
    hours = field.shape[1]
    step = 8
    whole = lambda shape: pl.BlockSpec(shape, lambda i: (0, 0))
    return pl.pallas_call(
        plane_finish_kernel,
        grid=(blocks // step,),
        in_specs=[whole(n.shape) for n in notes]
        + [whole(q.shape) for q in rows]
        + [
            pl.BlockSpec((step, slots, width), lambda i: (i, 0, 0)),
            pl.BlockSpec((step * width, hours), lambda i: (i, 0)),
        ],
        out_specs=pl.BlockSpec((step * width, hours), lambda i: (i, 0)),
        out_shape=jax.ShapeDtypeStruct(field.shape, F32),
        scratch_shapes=[pltpu.VMEM((blocks * slots, hours), F32)],
        compiler_params=params(),
        name="plane_finish",
    )(*notes, *rows, incidence, field)


def plane_shards(incidence, row_gauge, gauge_kernel, kernels, observed, first_guess):
    rows, hours = observed.shape
    basin, tm = lax.axis_index("basin"), lax.axis_index("tm")
    z, x, y, c = basin // X_, basin % X_, tm // C_, tm % C_
    place = 2 * y + x
    first = jnp.stack([4 * c + (place ^ m) for m in range(4)] + [4 * c + place, 4 * (1 - c) + place])
    first = (first * rows).astype(jnp.int32)
    flags = jnp.stack([1 - z % 2, (z < Z_ - 1).astype(z.dtype)]).astype(F32)
    forward, inverse_first, inverse_last = turned_transforms()
    mats = [*forward, *inverse_first, *inverse_last]

    slots = incidence.shape[1]
    ahead = describe(incidence, row_gauge, gauge_kernel, observed)
    ahead, field = lax.optimization_barrier((ahead, first_guess))
    ahead = moved(ahead, to_plane)
    parcel = moved(send(incidence, field), to_plane)
    meta, seen = ahead[: slots + 8], ahead[slots + 8 :]
    seen = jnp.concatenate([seen[:, i : i + rows] for i in range(0, seen.shape[1], rows)], axis=0)
    seen = [seen, moved(seen, z_pair), moved(seen, z_middle)]
    metas = [meta, moved(meta, over_core)]
    both = jnp.concatenate(metas, axis=1)
    around = [both] + [moved(both, where) for where in SQUARE]
    spec = plane_spectrum(meta, kernels, forward, rows)
    parcel, seen, around, spec = lax.optimization_barrier((parcel, seen, around, spec))

    dense = spread(first, [parcel, moved(parcel, over_core)], metas, rows)
    sums = dense[0] + sum(moved(value, where) for value, where in zip(dense[1:], SQUARE))
    sums = [sums, moved(sums, z_pair), moved(sums, z_middle)]
    coupled = plane_couple(first, around[:2], rows)
    coupled, sums = lax.optimization_barrier((coupled, sums))
    coupling = plane_couple(first, around[2:], rows, coupled)
    pulled = [plane_first(flags, sums, seen, spec, mats)]
    kept, shipped, mixes = [], [], []
    for k in range(3):
        if k:
            pulled[k], kept[k - 1] = lax.optimization_barrier((pulled[k], kept[k - 1]))
            shipped.append(moved(kept[k - 1], from_plane))
        values = [pulled[k]] + [moved(pulled[k], where) for where in SQUARE]
        mine, other, slot_rows = plane_mix(first, coupling, metas, values)
        beside = moved(other, over_core)
        mixed = mine + beside[: hours + NOTE]
        kept.append(
            slot_rows
            + jnp.concatenate(
                [beside[hours + NOTE + i * hours :][:hours] for i in range(slot_rows.shape[1] // rows)], axis=1
            )
        )
        sums = [mixed, moved(mixed, z_pair), moved(mixed, z_middle)]
        mixes.append(sums)
        if k:
            sums, shipped[k - 1] = lax.optimization_barrier((sums, shipped[k - 1]))
        if k == 0:
            following, now = plane_open(flags, sums, pulled[0], spec, mats)
        elif k == 1:
            note = mixed[hours:]
            two, mirror = moved(note, z_two), moved(note, z_mirror)
            open_note, following, state = plane_step(
                flags, sums, two, mirror, mixes[0], pulled[1], pulled[0], now, spec, mats
            )
        else:
            shipped.append(moved(kept[2], from_plane))
            note = plane_close(flags, sums, pulled[2], state, spec, mats)
        pulled.append(following)
    copies = jnp.broadcast_to(note[None], (Z_ * X_ * Y_ * C_,) + note.shape)
    close_note = jnp.sum(lax.all_to_all(copies, ("basin", "tm"), 0, 0, tiled=False), axis=0)
    return plane_finish([open_note, close_note], shipped, incidence, first_guess)


def solution(mesh):
    planes = dict(mesh.shape) == {"basin": Z_ * X_, "tm": Y_ * C_}
    in_specs = (
        P("basin", None, None),
        P("basin"),
        P("basin"),
        P(),
        P("basin", "tm"),
        P("basin", "tm"),
    )
    return jax.shard_map(
        plane_shards if planes else shards, mesh=mesh, in_specs=in_specs, out_specs=P("basin", "tm"), check_vma=False
    )
```

```python
import functools

import jax
import jax.numpy as jnp
import numpy as np
from jax import lax
from jax.experimental import pallas as pl
from jax.experimental.pallas import tpu as pltpu
from jax.sharding import PartitionSpec as P

F32 = jnp.float32
BF16 = jnp.bfloat16
HIGH = lax.Precision.HIGHEST
SPAN = 256
MIB = 1024 * 1024


SMALL = pl.CostEstimate(flops=1, bytes_accessed=1, transcendentals=0)


def params(mib=16):
    return pltpu.CompilerParams(vmem_limit_bytes=mib * MIB)


def transforms():
    half = SPAN // 2
    freq = 2.0 * np.pi * (np.arange(half) + 0.5) / SPAN
    phase = np.arange(SPAN)[:, None] * freq[None, :]
    forward = np.concatenate([np.cos(phase), -np.sin(phase)], axis=1)
    inverse = forward.T * (2.0 / SPAN)
    return (
        jnp.asarray(forward, F32),
        jnp.asarray(inverse[:, :half], F32),
        jnp.asarray(inverse[:, half:], F32),
    )


def dot(a, b):
    return jnp.dot(a, b, preferred_element_type=F32)


def exact(a, b):
    return jnp.dot(a, b, precision=HIGH, preferred_element_type=F32)


def pieces(value, count):
    out = []
    for _ in range(count):
        piece = value.astype(BF16)
        out.append(piece)
        value = value - piece.astype(F32)
    return out


def pick(hot, value):
    return sum(dot(hot, piece) for piece in pieces(value, 3))


def prepare_kernel(inc_ref, field_ref, partial_ref, gram_ref):
    blocks, slots, width = inc_ref.shape
    rows = blocks * slots
    weights = inc_ref[...].astype(F32).astype(BF16)
    for b in range(blocks):
        value = field_ref[pl.ds(b * width, width), :]
        partial_ref[pl.ds(b * slots, slots), :] = pick(weights[b], value)
    flat = weights.reshape(rows, width)
    full = lax.dot_general(flat, flat, (((1,), (1,)), ((), ())), preferred_element_type=F32)
    row = lax.broadcasted_iota(jnp.int32, (rows, rows), 0)
    col = lax.broadcasted_iota(jnp.int32, (rows, rows), 1)
    own = jnp.where(row // slots == col // slots, full, 0.0)
    gram_ref[...] = jnp.sum(own.reshape(blocks, slots, rows), axis=0)


def prepare(incidence, field):
    blocks, slots, width = incidence.shape
    hours = field.shape[1]
    step = 8
    return pl.pallas_call(
        prepare_kernel,
        grid=(blocks // step,),
        in_specs=[
            pl.BlockSpec((step, slots, width), lambda i: (i, 0, 0)),
            pl.BlockSpec((step * width, hours), lambda i: (i, 0)),
        ],
        out_specs=[
            pl.BlockSpec((step * slots, hours), lambda i: (i, 0)),
            pl.BlockSpec((slots, step * slots), lambda i: (0, i)),
        ],
        out_shape=[
            jax.ShapeDtypeStruct((blocks * slots, hours), F32),
            jax.ShapeDtypeStruct((slots, blocks * slots), F32),
        ],
        compiler_params=params(56),
        name="prepare",
    )(incidence, field)


def table_kernel(gauge_ref, partial_ref, out_ref):
    slots = partial_ref.shape[0]
    rows = out_ref.shape[0]
    first = pl.program_id(0) * rows
    gauge = lax.broadcasted_iota(jnp.int32, (rows, slots), 0) + first
    hot = jnp.where(gauge_ref[...] == gauge, 1.0, 0.0).astype(BF16)
    out_ref[...] = pick(hot, partial_ref[...])


def table(row_gauge, partial, gauges):
    slots, hours = partial.shape
    step = 256
    return pl.pallas_call(
        table_kernel,
        grid=(gauges // step,),
        in_specs=[
            pl.BlockSpec((1, slots), lambda i: (0, 0)),
            pl.BlockSpec((slots, hours), lambda i: (0, 0)),
        ],
        out_specs=pl.BlockSpec((step, hours), lambda i: (i, 0)),
        out_shape=jax.ShapeDtypeStruct((gauges, hours), F32),
        compiler_params=params(56),
        name="table",
    )(row_gauge.reshape(1, slots), partial)


def couple_kernel(first_ref, lane_ref, sub_ref, gram_ref, high_ref, low_ref, near_ref):
    slots = gram_ref.shape[0]
    count = lane_ref.shape[1]
    rows, cols = high_ref.shape
    tile = 256
    first = first_ref[0]

    @pl.when(pl.program_id(0) == 0)
    def _():
        row = lax.broadcasted_iota(jnp.int32, (tile, tile), 0)
        col = lax.broadcasted_iota(jnp.int32, (tile, tile), 1)
        same = row // slots == col // slots
        mine = lax.broadcasted_iota(jnp.int32, (rows, tile), 0) + first

        def body(i, carry):
            here = pl.ds(pl.multiple_of(i * tile, tile), tile)
            block = jnp.concatenate([gram_ref[:, here]] * (tile // slots), axis=0)
            block = jnp.where(same, block, 0.0).astype(BF16)
            hot = jnp.where(lane_ref[:, here] == mine, 1.0, 0.0).astype(BF16)
            near_ref[:, here] = dot(hot, block)
            return carry

        lax.fori_loop(0, count // tile, body, 0)

    def chunk(i, total):
        here = pl.ds(pl.multiple_of(i * 1024, 1024), 1024)
        gauge = lax.broadcasted_iota(jnp.int32, (1024, cols), 1) + pl.program_id(0) * cols
        hot = jnp.where(sub_ref[here, :] == gauge, 1.0, 0.0).astype(BF16)
        near = near_ref[:, here]
        high = near.astype(BF16)
        low = (near - high.astype(F32)).astype(BF16)
        return total + dot(high, hot) + dot(low, hot)

    total = lax.fori_loop(0, count // 1024, chunk, jnp.zeros((rows, cols), F32))
    high, low = pieces(total, 2)
    high_ref[...] = high
    low_ref[...] = low


def couple(first, row_gauge, gram, rows, gauges):
    count = row_gauge.shape[0]
    step = 256
    return pl.pallas_call(
        couple_kernel,
        grid=(gauges // step,),
        in_specs=[
            pl.BlockSpec(memory_space=pltpu.SMEM),
            pl.BlockSpec((1, count), lambda i: (0, 0)),
            pl.BlockSpec((count, 1), lambda i: (0, 0)),
            pl.BlockSpec(gram.shape, lambda i: (0, 0)),
        ],
        out_specs=[pl.BlockSpec((rows, step), lambda i: (0, i))] * 2,
        out_shape=[jax.ShapeDtypeStruct((rows, gauges), BF16)] * 2,
        scratch_shapes=[pltpu.VMEM((rows, count), F32)],
        compiler_params=params(56),
        name="couple",
    )(first, row_gauge.reshape(1, count), row_gauge.reshape(count, 1), gram)


def mix_kernel(high_ref, low_ref, value_ref, out_ref):
    high = high_ref[...]
    low = low_ref[...]
    one, two, three = pieces(value_ref[...], 3)
    out_ref[...] = (dot(high, three) + dot(low, two)) + (dot(high, two) + dot(low, one)) + dot(high, one)


def mix(high, low, value):
    return pl.pallas_call(
        mix_kernel,
        out_shape=jax.ShapeDtypeStruct((high.shape[0], value.shape[1]), F32),
        compiler_params=params(56),
        name="mix",
    )(high, low, value)


def spectrum_kernel(class_ref, kernels_ref, forward_ref, out_ref):
    rows = class_ref.shape[0]
    classes, taps = kernels_ref.shape
    kind = lax.broadcasted_iota(jnp.int32, (rows, classes), 1)
    hot = jnp.where(class_ref[...] == kind, 1.0, 0.0)
    out_ref[...] = exact(exact(hot, kernels_ref[...]), forward_ref[pl.ds(0, taps), :])


def spectrum(gauge_kernel, kernels, forward):
    rows = gauge_kernel.shape[0]
    return pl.pallas_call(
        spectrum_kernel,
        out_shape=jax.ShapeDtypeStruct((rows, SPAN), F32),
        compiler_params=params(56),
        name="spectrum",
    )(gauge_kernel.reshape(rows, 1), kernels, forward)


def delayed(before, here, after, spec, forward, inverse_last):
    rows, half = here.shape
    stacked = jnp.concatenate(
        [jnp.concatenate([before, here], axis=1), jnp.concatenate([here, after], axis=1)], axis=0
    )
    waves = exact(stacked, forward)
    real, imag = waves[:, :half], waves[:, half:]
    kr = jnp.concatenate([spec[:, :half]] * 2, axis=0)
    ki = jnp.concatenate([spec[:, half:]] * 2, axis=0)
    turned = jnp.concatenate([real * kr - imag * ki, real * ki + imag * kr], axis=1)
    out = exact(turned, inverse_last)
    return out[:rows], out[rows:]


def advanced(here, after, spec, forward, inverse_first):
    half = here.shape[1]
    waves = exact(jnp.concatenate([here, after], axis=1), forward)
    real, imag = waves[:, :half], waves[:, half:]
    kr, ki = spec[:, :half], spec[:, half:]
    turned = jnp.concatenate([real * kr + imag * ki, imag * kr - real * ki], axis=1)
    return exact(turned, inverse_first)


def lanes(a, b):
    return jnp.sum(a * b, axis=0, keepdims=True)


def total(ref, row):
    return jnp.sum(ref[row : row + 1, :], axis=1, keepdims=True)


def ratios(ref):
    square = total(ref, 0)
    alpha = jnp.sqrt(square)
    beta = jnp.sqrt(jnp.maximum(total(ref, 1) / square - 2.0 * total(ref, 2) + square, 0.0))
    return alpha, beta


def first_kernel(
    more_ref, sums_ref, observed_ref, spec_ref, forward_ref, first_ref, last_ref, out_ref, note_ref
):
    rows, half = observed_ref.shape[0] // 2, observed_ref.shape[1]
    spec, forward = spec_ref[...], forward_ref[...]
    before, here, after = (sums_ref[pl.ds(i * rows, rows), :] for i in range(3))
    now, later = delayed(before, here, after, spec, forward, last_ref[...])
    start = observed_ref[pl.ds(0, rows), :] - now
    start_later = (observed_ref[pl.ds(rows, rows), :] - later) * more_ref[0]
    out_ref[...] = advanced(start, start_later, spec, forward, first_ref[...])
    note_ref[...] = jnp.concatenate([lanes(start, start), jnp.zeros((7, half), F32)], axis=0)


def first_step(more, sums, observed, spec, mats):
    rows, half = spec.shape[0], observed.shape[1]
    return pl.pallas_call(
        first_kernel,
        in_specs=[pl.BlockSpec(memory_space=pltpu.SMEM)] + [pl.BlockSpec(memory_space=pltpu.VMEM)] * 6,
        out_shape=[jax.ShapeDtypeStruct((rows, half), F32), jax.ShapeDtypeStruct((8, half), F32)],
        compiler_params=params(56),
        name="first_step",
    )(more, sums, observed, spec, *mats)


def step_kernel(
    opening,
    final,
    more_ref,
    note_ref,
    sums_ref,
    spec_ref,
    forward_ref,
    first_ref,
    last_ref,
    pulled_ref,
    *refs,
):
    if opening:
        state_ref = None
    else:
        state_ref, *refs = refs
    if final:
        (out_note_ref,) = refs
    else:
        new_ref, out_ref, out_note_ref = refs
    rows, half = pulled_ref.shape
    spec, forward = spec_ref[...], forward_ref[...]
    if opening:
        scale = 1.0 / jnp.sqrt(total(note_ref, 0))
        along = sums_ref[...] * scale
        new_s, new_su = along, along
        new_zu = pulled_ref[...] * scale
        new_z = new_zu
    else:
        alpha, beta = ratios(note_ref)
        a, b, g = 1.0 / (alpha * beta), alpha / beta, beta / alpha
        wide = pl.ds(0, 3 * rows), pl.ds(3 * rows, 3 * rows)
        new_su = sums_ref[...] * a - state_ref[wide[1], :] * b
        new_s = new_su - state_ref[wide[0], :] * g
        new_zu = pulled_ref[...] * a - state_ref[pl.ds(7 * rows, rows), :] * b
        new_z = new_zu - state_ref[pl.ds(6 * rows, rows), :] * g
    before, here, after = (new_s[i * rows : (i + 1) * rows] for i in range(3))
    now, later = delayed(before, here, after, spec, forward, last_ref[...])
    out_note_ref[...] = jnp.concatenate(
        [lanes(new_z, here), lanes(now, now), lanes(new_zu, here), jnp.zeros((5, half), F32)], axis=0
    )
    if not final:
        new_ref[pl.ds(0, 3 * rows), :] = new_s
        new_ref[pl.ds(3 * rows, 3 * rows), :] = new_su
        new_ref[pl.ds(6 * rows, rows), :] = new_z
        new_ref[pl.ds(7 * rows, rows), :] = new_zu
        out_ref[...] = advanced(now, later * more_ref[0], spec, forward, first_ref[...])


def next_step(more, note, sums, spec, mats, pulled, state, final):
    rows, half = pulled.shape
    opening = state is None
    shapes = [
        jax.ShapeDtypeStruct((8 * rows, half), F32),
        jax.ShapeDtypeStruct((rows, half), F32),
        jax.ShapeDtypeStruct((8, half), F32),
    ]
    args = [more, note, sums, spec, *mats, pulled] + ([] if opening else [state])
    return pl.pallas_call(
        functools.partial(step_kernel, opening, final),
        in_specs=[pl.BlockSpec(memory_space=pltpu.SMEM)]
        + [pl.BlockSpec(memory_space=pltpu.VMEM)] * (len(args) - 1),
        out_shape=shapes[2:] if final else shapes,
        compiler_params=params(56),
        name="next_step",
    )(*args)


def weights_of(notes):
    start = jnp.sqrt(total(notes[0], 0))
    zero = jnp.zeros_like(start)
    units = [1.0 / start, zero, zero]
    z, zu = list(units), list(units)
    phibar = start
    alpha, beta = ratios(notes[1])
    rhobar = alpha
    w = [value / alpha for value in z]
    result = [zero] * 3
    steps = len(notes) - 1
    for k in range(steps):
        rho = jnp.sqrt(rhobar * rhobar + beta * beta)
        cosine, sine = rhobar / rho, beta / rho
        phi, phibar = cosine * phibar, sine * phibar
        result = [r + phi / rho * value for r, value in zip(result, w)]
        if k < steps - 1:
            a, b, g = 1.0 / (alpha * beta), alpha / beta, beta / alpha
            zu = [(a if i == k + 1 else 0.0) - b * value for i, value in enumerate(zu)]
            z = [value - g * old for value, old in zip(zu, z)]
            alpha, beta = ratios(notes[k + 2])
            theta = sine * alpha
            rhobar = -cosine * alpha
            w = [value / alpha - theta / rho * old for value, old in zip(z, w)]
    return result


def finish_kernel(n0, n1, n2, n3, gauge_ref, q0, q1, q2, inc_ref, field_ref, out_ref, rows_ref):
    blocks, slots, width = inc_ref.shape
    count = rows_ref.shape[0]
    gauges = q0.shape[0]
    step = pl.program_id(0)

    @pl.when(step == 0)
    def _():
        e0, e1, e2 = weights_of([n0, n1, n2, n3])
        width_ = 512

        def body(i, value):
            here = pl.ds(pl.multiple_of(i * width_, width_), width_)
            mixed = q0[here, :] * e0 + q1[here, :] * e1 + q2[here, :] * e2
            gauge = lax.broadcasted_iota(jnp.int32, (count, width_), 1) + i * width_
            hot = jnp.where(gauge_ref[...] == gauge, 1.0, 0.0).astype(BF16)
            return value + pick(hot, mixed)

        rows_ref[...] = lax.fori_loop(0, gauges // width_, body, jnp.zeros(rows_ref.shape, F32))

    weights = inc_ref[...].astype(F32).astype(BF16)
    for b in range(blocks):
        here = pl.ds(b * width, width)
        rows = rows_ref[pl.ds(pl.multiple_of((step * blocks + b) * slots, slots), slots), :]
        added = sum(
            lax.dot_general(weights[b], piece, (((0,), (0,)), ((), ())), preferred_element_type=F32)
            for piece in pieces(rows, 3)
        )
        out_ref[here, :] = field_ref[here, :] + added


def finish(notes, row_gauge, gathered, incidence, field):
    blocks, slots, width = incidence.shape
    hours = field.shape[1]
    count = row_gauge.shape[0]
    step = 8
    whole = lambda shape: pl.BlockSpec(shape, lambda i: (0, 0))
    return pl.pallas_call(
        finish_kernel,
        grid=(blocks // step,),
        in_specs=[whole(n.shape) for n in notes]
        + [whole((count, 1))]
        + [whole(q.shape) for q in gathered]
        + [
            pl.BlockSpec((step, slots, width), lambda i: (i, 0, 0)),
            pl.BlockSpec((step * width, hours), lambda i: (i, 0)),
        ],
        out_specs=pl.BlockSpec((step * width, hours), lambda i: (i, 0)),
        out_shape=jax.ShapeDtypeStruct(field.shape, F32),
        scratch_shapes=[pltpu.VMEM((count, hours), F32)],
        compiler_params=params(56),
        name="finish",
    )(*notes, row_gauge.reshape(count, 1), *gathered, incidence, field)


def shifted(value, axis, by):
    devices = lax.axis_size(axis)
    pairs = [(i, i + by) for i in range(devices) if 0 <= i + by < devices]
    return lax.ppermute(value, axis, pairs)


def window(value):
    return jnp.concatenate([shifted(value, "tm", 1), value, shifted(value, "tm", -1)], axis=0)


def gathered_rows(value):
    owners = lax.axis_size("basin")
    copies = jnp.broadcast_to(value[None], (owners,) + value.shape)
    return lax.all_to_all(copies, "basin", 0, 0, tiled=False)


def over_hours(note):
    blocks = lax.axis_size("tm")
    result = note
    for by in range(1, blocks):
        result = result + lax.ppermute(note, "tm", [(i, (i + by) % blocks) for i in range(blocks)])
    return result


def shards(incidence, row_gauge, gauge_kernel, kernels, observed, first_guess):
    owners = lax.axis_size("basin")
    rows, hours = observed.shape
    gauges = rows * owners
    mats = transforms()
    spec = spectrum(gauge_kernel, kernels, mats[0])
    more = (lax.axis_index("tm") < lax.axis_size("tm") - 1).astype(F32).reshape(1)
    partial, gram = prepare(incidence, first_guess)
    all_gram = lax.all_gather(gram, "basin", axis=1, tiled=True)
    all_rows = lax.all_gather(row_gauge, "basin", axis=0, tiled=True)
    dense = table(row_gauge, partial, gauges).reshape(owners, rows, hours)
    sums = jnp.sum(lax.all_to_all(dense, "basin", 0, 0, tiled=False), axis=0)
    both = jnp.concatenate([observed, shifted(observed, "tm", -1)], axis=0)
    first = (lax.axis_index("basin") * rows).astype(jnp.int32).reshape(1)
    high, low = couple(first, all_rows, all_gram, rows, gauges)

    pulled, note = first_step(more, window(sums), both, spec, mats)
    notes, kept, state = [], [], None
    for k in range(3):
        everyone = gathered_rows(jnp.concatenate([pulled, note], axis=0))
        value = everyone[:, :rows].reshape(gauges, hours)
        notes.append(over_hours(jnp.sum(everyone[:, rows:], axis=0)))
        kept.append(value)
        around = window(mix(high, low, value))
        final = k == 2
        result = next_step(more, notes[-1], around, spec, mats, pulled, state, final)
        if final:
            (note,) = result
        else:
            state, pulled, note = result
    notes.append(over_hours(jnp.sum(gathered_rows(note), axis=0)))
    return finish(notes, row_gauge, kept, incidence, first_guess)


Z_, X_, Y_, C_ = 4, 2, 2, 2
NOTE = 8


def device(z, x, y, c):
    return (z * X_ + x) * (Y_ * C_) + y * C_ + c


def moved(value, where):
    pairs = []
    for z, x, y, c in np.ndindex(Z_, X_, Y_, C_):
        target = where(z, x, y, c)
        if target is not None:
            pairs.append((device(z, x, y, c), device(*target)))
    return lax.ppermute(value, ("basin", "tm"), pairs)


def to_plane(z, x, y, c):
    return 2 * y + c, x, z & 1, z >> 1


def to_plane_before(z, x, y, c):
    t = 2 * y + c
    return (t - 1, x, z & 1, z >> 1) if t else None


def from_plane(z, x, y, c):
    return 2 * c + y, x, z >> 1, z & 1


def over_x(z, x, y, c):
    return z, 1 - x, y, c


def over_y(z, x, y, c):
    return z, x, 1 - y, c


def over_xy(z, x, y, c):
    return z, 1 - x, 1 - y, c


def over_core(z, x, y, c):
    return z, x, y, 1 - c


def z_pair(z, x, y, c):
    return z ^ 1, x, y, c


def z_middle(z, x, y, c):
    return (3 - z, x, y, c) if z in (1, 2) else None


def z_two(z, x, y, c):
    return z ^ 2, x, y, c


def z_mirror(z, x, y, c):
    return 3 - z, x, y, c


SQUARE = (over_x, over_y, over_xy)


def split_constant(value):
    out = []
    for _ in range(3):
        piece = value.astype(jnp.bfloat16)
        out.append(jnp.asarray(piece))
        value = value - piece.astype(np.float64)
    return out


def turned_transforms():
    half = SPAN // 2
    freq = 2.0 * np.pi * (np.arange(half) + 0.5) / SPAN
    phase = freq[:, None] * np.arange(SPAN)[None, :]
    forward = np.concatenate([np.cos(phase), -np.sin(phase)], axis=0)
    inverse = forward.T * (2.0 / SPAN)
    return split_constant(forward), split_constant(inverse[:half]), split_constant(inverse[half:])


def product(mats, value, order):
    parts = pieces(value, order)
    result = None
    for level in reversed(range(order)):
        for i in range(level + 1):
            term = dot(mats[i][...], parts[level - i])
            result = term if result is None else result + term
    return result


def turn(waves, spec, sign):
    half = waves.shape[0] // 2
    real, imag = waves[:half], waves[half:]
    kr, ki = spec[:half], spec[half:] * sign
    return jnp.concatenate([real * kr - imag * ki, real * ki + imag * kr], axis=0)


def plane_delayed(before, here, after, spec, forward, last, order):
    out = []
    for pair in ((before, here), (here, after)):
        waves = product(forward, jnp.concatenate(pair, axis=0), order)
        out.append(product(last, turn(waves, spec, 1.0), order))
    return out


def plane_advanced(here, after, spec, forward, first, order):
    waves = product(forward, jnp.concatenate([here, after], axis=0), order)
    return product(first, turn(waves, spec, -1.0), order)


def describe_kernel(inc_ref, seen_ref, out_ref):
    blocks, slots, width = inc_ref.shape
    rows, hours = seen_ref.shape
    count = blocks * slots
    tile = 8
    side = tile * slots
    weights = inc_ref[...].astype(F32).astype(BF16)
    row = lax.broadcasted_iota(jnp.int32, (side, side), 0)
    col = lax.broadcasted_iota(jnp.int32, (side, side), 1)
    same = row // slots == col // slots
    for i in range(blocks // tile):
        flat = weights[i * tile : (i + 1) * tile].reshape(side, width)
        full = lax.dot_general(flat, flat, (((1,), (1,)), ((), ())), preferred_element_type=F32)
        own = jnp.where(same, full, 0.0)
        out_ref[pl.ds(0, slots), pl.ds(i * side, side)] = jnp.sum(own.reshape(tile, slots, side), axis=0)
    turned = jnp.transpose(seen_ref[...])
    step = hours * rows // count
    for i in range(count // rows):
        out_ref[pl.ds(slots, step), pl.ds(i * rows, rows)] = turned[i * step : (i + 1) * step]


def describe(incidence, observed):
    blocks, slots, _ = incidence.shape
    rows, hours = observed.shape
    count = blocks * slots
    return pl.pallas_call(
        describe_kernel,
        out_shape=jax.ShapeDtypeStruct((slots + hours * rows // count, count), F32),
        compiler_params=params(),
        name="describe",
        cost_estimate=SMALL,
    )(incidence, observed)


def send_kernel(inc_ref, field_ref, gauge_ref, kind_ref, out_ref):
    blocks, slots, width = inc_ref.shape
    hours = field_ref.shape[1]
    weights = inc_ref[...].astype(F32).astype(BF16)
    parts = []
    for b in range(blocks):
        parts.append(pick(weights[b], field_ref[pl.ds(b * width, width), :]))
    out_ref[pl.ds(0, hours), :] = jnp.transpose(jnp.concatenate(parts, axis=0))
    out_ref[pl.ds(hours, 8), :] = jnp.concatenate(
        [gauge_ref[...].astype(F32), kind_ref[...].astype(F32), jnp.zeros((6, blocks * slots), F32)], axis=0
    )


def send(incidence, field, row_gauge, gauge_kernel):
    blocks, slots, width = incidence.shape
    count = blocks * slots
    hours = field.shape[1]
    step = 8
    kinds = jnp.pad(gauge_kernel, (0, count - gauge_kernel.shape[0]))
    return pl.pallas_call(
        send_kernel,
        grid=(blocks // step,),
        in_specs=[
            pl.BlockSpec((step, slots, width), lambda i: (i, 0, 0)),
            pl.BlockSpec((step * width, hours), lambda i: (i, 0)),
            pl.BlockSpec((1, step * slots), lambda i: (0, i)),
            pl.BlockSpec((1, step * slots), lambda i: (0, i)),
        ],
        out_specs=pl.BlockSpec((hours + 8, step * slots), lambda i: (0, i)),
        out_shape=jax.ShapeDtypeStruct((hours + 8, count), F32),
        compiler_params=params(),
        name="send",
        cost_estimate=SMALL,
    )(incidence, field, row_gauge.reshape(1, count), kinds.reshape(1, count))


def hot_rows(gauge, first, rows):
    mine = (lax.broadcasted_iota(jnp.int32, (rows, gauge.shape[1]), 0) + first).astype(F32)
    return jnp.where(gauge == mine, 1.0, 0.0).astype(BF16)


def spread_kernel(first_ref, mine_ref, other_ref, *out_refs):
    hours, rows = out_refs[0].shape
    for m, out_ref in enumerate(out_refs):
        result = None
        for ref in (mine_ref, other_ref):
            hot = hot_rows(ref[hours : hours + 1, :], first_ref[m], rows)
            for piece in reversed(pieces(ref[pl.ds(0, hours), :], 3)):
                term = lax.dot_general(
                    piece, hot, (((1,), (1,)), ((), ())), preferred_element_type=F32
                )
                result = term if result is None else result + term
        out_ref[...] = result


def spread(first, parcels, hours, rows):
    return pl.pallas_call(
        spread_kernel,
        in_specs=[pl.BlockSpec(memory_space=pltpu.SMEM)] + [pl.BlockSpec(memory_space=pltpu.VMEM)] * 2,
        out_shape=[jax.ShapeDtypeStruct((hours, rows), F32)] * 4,
        compiler_params=params(),
        name="spread",
        cost_estimate=SMALL,
    )(first, *parcels)


def plane_couple_kernel(last, first_ref, *refs):
    if last:
        a_ref, b_ref, before_ref, high_ref, low_ref, total_ref, meta_ref = refs
        total_ref[...] = before_ref[...]
    else:
        a_ref, b_ref, total_ref, meta_ref = refs
        total_ref[...] = jnp.zeros_like(total_ref)
    height, double = a_ref.shape
    slots = height - 8
    count = double // 2
    cols, rows = total_ref.shape
    tile = 256
    for i, ref in enumerate((a_ref, b_ref)):
        for j in range(2):
            meta_ref[2 * i + j] = ref[:, j * count : (j + 1) * count]
    row = lax.broadcasted_iota(jnp.int32, (tile, tile), 0)
    col = lax.broadcasted_iota(jnp.int32, (tile, tile), 1)
    same = row // slots == col // slots

    def body(i, carry):
        gauge = meta_ref[i, slots : slots + 1, :]
        near = []
        for j in range(count // tile):
            here = slice(j * tile, (j + 1) * tile)
            block = jnp.concatenate([meta_ref[i, :slots, here]] * (tile // slots), axis=0)
            block = jnp.where(same, block, 0.0).astype(BF16)
            mine = jnp.concatenate(
                [hot_rows(gauge[:, here], first_ref[4 + h], rows // 2) for h in range(2)], axis=0
            )
            near.append(
                lax.dot_general(block, mine, (((1,), (1,)), ((), ())), preferred_element_type=F32)
            )
        near = jnp.concatenate(near, axis=0)
        high = near.astype(BF16)
        rest = near - high.astype(F32)
        hot = jnp.concatenate([hot_rows(gauge, first_ref[m], cols // 4) for m in range(4)], axis=0)
        total_ref[...] += dot(hot, high)

        @pl.when(jnp.max(jnp.abs(rest)) > 0.0)
        def _():
            total_ref[...] += dot(hot, rest.astype(BF16))

        return carry

    lax.fori_loop(0, 4, body, 0)
    if last:
        high, low = pieces(total_ref[...], 2)
        high_ref[...] = high
        low_ref[...] = low


def plane_couple(first, metas, rows, before=None):
    height, double = metas[0].shape
    shape = (4 * rows, 2 * rows)
    last = before is not None
    args = [first, *metas] + ([before] if last else [])
    scratch = [pltpu.VMEM((4, height, double // 2), F32)]
    return pl.pallas_call(
        functools.partial(plane_couple_kernel, last),
        in_specs=[pl.BlockSpec(memory_space=pltpu.SMEM)]
        + [pl.BlockSpec(memory_space=pltpu.VMEM)] * (len(args) - 1),
        out_shape=[jax.ShapeDtypeStruct(shape, BF16)] * 2 if last else jax.ShapeDtypeStruct(shape, F32),
        scratch_shapes=([pltpu.VMEM(shape, F32)] if last else []) + scratch,
        compiler_params=params(),
        name="plane_couple",
        cost_estimate=pl.CostEstimate(
            flops=2 * 2 * double * 8 * rows * rows, bytes_accessed=2_000_000, transcendentals=0
        ),
    )(*args)


def plane_mix_kernel(
    first_ref, high_ref, low_ref, meta_ref, meta_other_ref, a_ref, b_ref, c_ref, d_ref, mine_ref, other_ref, rows_ref
):
    refs = (a_ref, b_ref, c_ref, d_ref)
    height, rows = a_ref.shape
    hours = height - NOTE
    body, tail = pl.ds(0, hours), pl.ds(hours, NOTE)
    value = jnp.concatenate([ref[body, :] for ref in refs], axis=1)
    one, two = pieces(value, 2)
    high, low = high_ref[...], low_ref[...]
    result = (dot(two, high) + dot(one, low)) + dot(one, high)
    note = sum(ref[tail, :] for ref in refs)
    mine_ref[body, :] = result[:, :rows]
    other_ref[body, :] = result[:, rows:]
    mine_ref[tail, :] = note
    other_ref[tail, :] = note
    for ref in (meta_ref, meta_other_ref):
        gauge = ref[0:1, :]
        hot = jnp.concatenate([hot_rows(gauge, first_ref[m], rows) for m in range(4)], axis=0)
        picked = dot(two, hot) + dot(one, hot)
        if ref is meta_ref:
            rows_ref[...] = picked
        else:
            for i in range(gauge.shape[1] // rows):
                other_ref[pl.ds(height + i * hours, hours), :] = picked[:, i * rows : (i + 1) * rows]


def plane_mix(first, coupling, metas, values):
    height, rows = values[0].shape
    hours = height - NOTE
    slots = metas[0].shape[1]
    return pl.pallas_call(
        plane_mix_kernel,
        in_specs=[pl.BlockSpec(memory_space=pltpu.SMEM)] + [pl.BlockSpec(memory_space=pltpu.VMEM)] * 8,
        out_shape=[
            jax.ShapeDtypeStruct((height, rows), F32),
            jax.ShapeDtypeStruct((height + slots // rows * hours, rows), F32),
            jax.ShapeDtypeStruct((hours, slots), F32),
        ],
        compiler_params=params(),
        name="plane_mix",
        cost_estimate=SMALL,
    )(first, *coupling, *metas, *values)


def plane_spectrum_kernel(class_ref, kernels_ref, f0_ref, f1_ref, f2_ref, out_ref):
    classes, taps = kernels_ref.shape
    kind = class_ref[1:2, : out_ref.shape[1]]
    hot = jnp.where(
        lax.broadcasted_iota(jnp.int32, (classes, kind.shape[1]), 0).astype(F32) == kind, 1.0, 0.0
    ).astype(BF16)
    chosen = None
    for piece in reversed(pieces(jnp.transpose(kernels_ref[...]), 3)):
        term = dot(piece, hot)
        chosen = term if chosen is None else chosen + term
    mats = [ref[:, :taps] for ref in (f0_ref, f1_ref, f2_ref)]
    out_ref[...] = product(mats, chosen, 3)


def plane_spectrum(meta, kernels, forward, rows):
    return pl.pallas_call(
        plane_spectrum_kernel,
        out_shape=jax.ShapeDtypeStruct((SPAN, rows), F32),
        compiler_params=params(),
        name="plane_spectrum",
        cost_estimate=SMALL,
    )(meta, kernels, *forward)


def sides(even, pair, middle):
    return jnp.where(even, middle, pair), jnp.where(even, pair, middle)


def plane_first_kernel(flag_ref, here_ref, pair_ref, middle_ref, spec_ref, *refs):
    *mats, out_ref = refs
    forward, first, last = mats[0:3], mats[3:6], mats[6:9]
    rows = here_ref.shape[1]
    hours = here_ref.shape[0] // 2
    spec = spec_ref[...]
    before, after = sides(flag_ref[0] > 0.5, pair_ref[...], middle_ref[...])
    now, later = plane_delayed(
        before[:hours], here_ref[pl.ds(0, hours), :], after[:hours], spec, forward, last, 3
    )
    start = here_ref[pl.ds(hours, hours), :] - now
    start_later = (after[hours:] - later) * flag_ref[1]
    out_ref[pl.ds(0, hours), :] = plane_advanced(start, start_later, spec, forward, first, 3)
    out_ref[pl.ds(hours, NOTE), :] = jnp.concatenate(
        [lanes(start, start), jnp.zeros((NOTE - 1, rows), F32)], axis=0
    )


def plane_first(flags, sums, spec, mats):
    double, rows = sums[0].shape
    args = [flags, *sums, spec, *mats]
    return pl.pallas_call(
        plane_first_kernel,
        in_specs=[pl.BlockSpec(memory_space=pltpu.SMEM)]
        + [pl.BlockSpec(memory_space=pltpu.VMEM)] * (len(args) - 1),
        out_shape=jax.ShapeDtypeStruct((double // 2 + NOTE, rows), F32),
        compiler_params=params(),
        name="plane_first",
        cost_estimate=SMALL,
    )(*args)


def plane_open_kernel(flag_ref, here_ref, pair_ref, middle_ref, pulled_ref, spec_ref, *refs):
    mats, (out_ref, now_ref) = refs[:9], refs[9:]
    forward, first, last = mats[0:3], mats[3:6], mats[6:9]
    height, rows = pulled_ref.shape
    hours = height - NOTE
    tail, body = pl.ds(hours, NOTE), pl.ds(0, hours)
    spec = spec_ref[...]
    here = here_ref[body, :]
    before, after = sides(flag_ref[0] > 0.5, pair_ref[body, :], middle_ref[body, :])
    now, later = plane_delayed(before, here, after, spec, forward, last, 2)
    out_ref[body, :] = plane_advanced(now, later * flag_ref[1], spec, forward, first, 2)
    out_ref[tail, :] = jnp.concatenate(
        [
            lanes(pulled_ref[body, :], here),
            lanes(now, now),
            pulled_ref[hours : hours + 1, :],
            jnp.zeros((NOTE - 3, rows), F32),
        ],
        axis=0,
    )
    now_ref[...] = now


def plane_open(flags, sums, pulled, spec, mats):
    height, rows = pulled.shape
    args = [flags, *sums, pulled, spec, *mats]
    return pl.pallas_call(
        plane_open_kernel,
        in_specs=[pl.BlockSpec(memory_space=pltpu.SMEM)]
        + [pl.BlockSpec(memory_space=pltpu.VMEM)] * (len(args) - 1),
        out_shape=[
            jax.ShapeDtypeStruct((height, rows), F32),
            jax.ShapeDtypeStruct((height - NOTE, rows), F32),
        ],
        compiler_params=params(),
        name="plane_open",
        cost_estimate=SMALL,
    )(*args)


def opening(ref):
    start = total(ref, 2)
    square = total(ref, 0) / start
    alpha = jnp.sqrt(square)
    beta = jnp.sqrt(jnp.maximum(total(ref, 1) / total(ref, 0) - square, 0.0))
    return 1.0 / jnp.sqrt(start), alpha, beta


def plane_step_kernel(flag_ref, here_ref, pair_ref, middle_ref, two_ref, mirror_ref, *refs):
    old_refs, (pulled_ref, old_z_ref, old_now_ref, spec_ref), refs = refs[:3], refs[3:7], refs[7:]
    mats, (total_ref, out_ref, kept_ref) = refs[:9], refs[9:]
    forward, first, last = mats[0:3], mats[3:6], mats[6:9]
    height, rows = pulled_ref.shape
    hours = height - NOTE
    tail, body = pl.ds(hours, NOTE), pl.ds(0, hours)
    total_ref[...] = (here_ref[tail, :] + pair_ref[tail, :]) + (two_ref[...] + mirror_ref[...])
    scale, alpha, beta = opening(total_ref)
    a, b, g = scale / (alpha * beta), scale * alpha / beta, scale * beta / alpha
    spec = spec_ref[...]
    s, su = [], []
    for ref, old_ref in zip((here_ref, pair_ref, middle_ref), old_refs):
        old = old_ref[body, :]
        su.append(ref[body, :] * a - old * b)
        s.append(su[-1] - old * g)
    zu = pulled_ref[body, :] * a - old_z_ref[body, :] * b
    z = zu - old_z_ref[body, :] * g
    before, after = sides(flag_ref[0] > 0.5, s[1], s[2])
    now, later = plane_delayed(before, s[0], after, spec, forward, last, 2)
    out_ref[body, :] = plane_advanced(now, later * flag_ref[1], spec, forward, first, 2)
    out_ref[tail, :] = jnp.concatenate(
        [lanes(z, s[0]), lanes(now, now), lanes(zu, s[0]), jnp.zeros((NOTE - 3, rows), F32)], axis=0
    )
    for i, value in enumerate((s[0], su[0], z, zu, now, now + old_now_ref[...] * g)):
        kept_ref[pl.ds(i * hours, hours), :] = value


def plane_step(flags, sums, two, mirror, old, pulled, old_z, old_now, spec, mats):
    height, rows = pulled.shape
    args = [flags, *sums, two, mirror, *old, pulled, old_z, old_now, spec, *mats]
    return pl.pallas_call(
        plane_step_kernel,
        in_specs=[pl.BlockSpec(memory_space=pltpu.SMEM)]
        + [pl.BlockSpec(memory_space=pltpu.VMEM)] * (len(args) - 1),
        out_shape=[
            jax.ShapeDtypeStruct((NOTE, rows), F32),
            jax.ShapeDtypeStruct((height, rows), F32),
            jax.ShapeDtypeStruct((6 * (height - NOTE), rows), F32),
        ],
        compiler_params=params(),
        name="plane_step",
        cost_estimate=SMALL,
    )(*args)


def plane_close_kernel(flag_ref, here_ref, pair_ref, middle_ref, pulled_ref, kept_ref, spec_ref, *refs):
    mats, (out_ref,) = refs[:9], refs[9:]
    forward, last = mats[0:3], mats[6:9]
    height, rows = pulled_ref.shape
    hours = height - NOTE
    body = pl.ds(0, hours)
    before, after = sides(flag_ref[0] > 0.5, pair_ref[body, :], middle_ref[body, :])
    here = here_ref[body, :]
    waves = product(forward, jnp.concatenate([before, here], axis=0), 2)
    now = product(last, turn(waves, spec_ref[...], 1.0), 2)
    s, su, z, zu, old_now, old_now_u = (kept_ref[pl.ds(i * hours, hours), :] for i in range(6))
    raw = pulled_ref[body, :]
    note = [pulled_ref[hours + i : hours + i + 1, :] for i in range(3)]
    for left in (raw, zu, z):
        note += [lanes(left, right) for right in (here, su, s)]
    parts = (now, old_now_u, old_now)
    for i in range(3):
        note += [lanes(parts[i], parts[j]) for j in range(i, 3)]
    note.append(jnp.zeros((24 - len(note), rows), F32))
    note = jnp.sum(jnp.concatenate(note, axis=0), axis=1, keepdims=True)
    shape = (24, out_ref.shape[2])
    row, col = (lax.broadcasted_iota(jnp.int32, shape, i) for i in range(2))
    note = jnp.sum(jnp.where(row == col, jnp.broadcast_to(note, shape), 0.0), axis=0, keepdims=True)
    out_ref[...] = jnp.broadcast_to(note[None], out_ref.shape)


def plane_close(flags, sums, pulled, kept, spec, mats):
    rows = pulled.shape[1]
    args = [flags, *sums, pulled, kept, spec, *mats]
    return pl.pallas_call(
        plane_close_kernel,
        in_specs=[pl.BlockSpec(memory_space=pltpu.SMEM)]
        + [pl.BlockSpec(memory_space=pltpu.VMEM)] * (len(args) - 1),
        out_shape=jax.ShapeDtypeStruct((Z_ * X_ * Y_ * C_, 8, rows // 2), F32),
        compiler_params=params(),
        name="plane_close",
        cost_estimate=SMALL,
    )(*args)


def plane_weights(open_ref, close):
    scale, alpha, beta = opening(open_ref)
    start = 1.0 / scale
    phibar, rhobar = start, alpha
    zero = jnp.zeros_like(start)
    z = zu = [scale, zero, zero]
    w = [value / alpha for value in z]
    result = [zero] * 3
    for k in range(3):
        rho = jnp.sqrt(rhobar * rhobar + beta * beta)
        cosine, sine = rhobar / rho, beta / rho
        phi, phibar = cosine * phibar, sine * phibar
        result = [r + phi / rho * value for r, value in zip(result, w)]
        if k == 2:
            return result
        a, b, g = 1.0 / (alpha * beta), alpha / beta, beta / alpha
        zu = [-b * value for value in zu]
        zu[k + 1] = zu[k + 1] + (a * scale if k == 0 else a)
        z = [value - g * old for value, old in zip(zu, z)]
        if k == 0:
            square, norm, along = (close[:, i : i + 1] for i in range(3))
        else:
            plain = (a, -b, -g)
            cross = [[close[:, 3 + 3 * i + j : 4 + 3 * i + j] for j in range(3)] for i in range(3)]
            along = sum(plain[i] * plain[j] * cross[i][j] for i in range(2) for j in range(3))
            square = along + sum(plain[2] * plain[j] * cross[2][j] for j in range(3))
            pairs = [(i, j) for i in range(3) for j in range(i, 3)]
            norm = sum(
                plain[i] * plain[j] * close[:, 12 + n : 13 + n] * (1.0 if i == j else 2.0)
                for n, (i, j) in enumerate(pairs)
            )
        alpha = jnp.sqrt(square)
        beta = jnp.sqrt(jnp.maximum(norm / square - 2.0 * along + square, 0.0))
        theta = sine * alpha
        rhobar = -cosine * alpha
        w = [value / alpha - theta / rho * old for value, old in zip(z, w)]


def plane_combine_kernel(open_ref, close_ref, *refs):
    *parts, out_ref = refs
    hours, rows = out_ref.shape[1], open_ref.shape[1]
    close = jnp.sum(close_ref[...], axis=0)[0:1, :]
    weights = plane_weights(open_ref, close)
    mine = sum(ref[...] * e for ref, e in zip(parts[:3], weights))
    skip = parts[3].shape[0] - mine.shape[1] // rows * hours
    for i in range(mine.shape[1] // rows):
        here = pl.ds(skip + i * hours, hours)
        other = sum(ref[here, :] * e for ref, e in zip(parts[3:], weights))
        out_ref[pl.ds(i * rows, rows), :] = jnp.transpose(mine[:, i * rows : (i + 1) * rows] + other)


def plane_combine(open_note, close_note, mine, other):
    hours, slots = mine[0].shape
    return pl.pallas_call(
        plane_combine_kernel,
        out_shape=jax.ShapeDtypeStruct((slots, hours), F32),
        compiler_params=params(),
        name="plane_combine",
        cost_estimate=SMALL,
    )(open_note, close_note, *mine, *other)


def plane_finish_kernel(rows_ref, inc_ref, field_ref, out_ref):
    blocks, slots, width = inc_ref.shape
    weights = inc_ref[...].astype(F32).astype(BF16)
    for b in range(blocks):
        here = pl.ds(b * width, width)
        added = sum(
            lax.dot_general(weights[b], piece, (((0,), (0,)), ((), ())), preferred_element_type=F32)
            for piece in pieces(rows_ref[pl.ds(b * slots, slots), :], 2)
        )
        out_ref[here, :] = field_ref[here, :] + added


def plane_finish(rows, incidence, field):
    blocks, slots, width = incidence.shape
    hours = field.shape[1]
    step = 8
    return pl.pallas_call(
        plane_finish_kernel,
        grid=(blocks // step,),
        in_specs=[
            pl.BlockSpec((step * slots, hours), lambda i: (i, 0)),
            pl.BlockSpec((step, slots, width), lambda i: (i, 0, 0)),
            pl.BlockSpec((step * width, hours), lambda i: (i, 0)),
        ],
        out_specs=pl.BlockSpec((step * width, hours), lambda i: (i, 0)),
        out_shape=jax.ShapeDtypeStruct(field.shape, F32),
        compiler_params=params(),
        name="plane_finish",
    )(rows, incidence, field)


def plane_shards(incidence, row_gauge, gauge_kernel, kernels, observed, first_guess):
    rows, hours = observed.shape
    basin, tm = lax.axis_index("basin"), lax.axis_index("tm")
    z, x, y, c = basin // X_, basin % X_, tm // C_, tm % C_
    place = 2 * y + x
    first = jnp.stack([4 * c + (place ^ m) for m in range(4)] + [4 * c + place, 4 * (1 - c) + place])
    first = (first * rows).astype(jnp.int32)
    flags = jnp.stack([1 - z % 2, (z < Z_ - 1).astype(z.dtype)]).astype(F32)
    forward, inverse_first, inverse_last = turned_transforms()
    mats = [*forward, *inverse_first, *inverse_last]

    parcel = send(incidence, first_guess, row_gauge, gauge_kernel)
    incidence_, seen, parcel = lax.optimization_barrier((incidence, observed, parcel))
    parcel = moved(parcel, to_plane)
    behind = moved(describe(incidence_, seen), to_plane)
    parcel, behind = lax.optimization_barrier((parcel, behind))
    parcels = [parcel, moved(parcel, over_core)]
    metas = [value[hours:] for value in parcels]
    spec = plane_spectrum(metas[0], kernels, forward, rows)
    dense = spread(first, parcels, hours, rows)
    sums = dense[0] + sum(moved(value, where) for value, where in zip(dense[1:], SQUARE))

    slots = incidence.shape[1]
    gram, seen = behind[:slots], behind[slots:]
    seen = [seen[:, i : i + rows] for i in range(0, seen.shape[1], rows)]
    sums = jnp.concatenate([sums, *seen], axis=0)
    sums = [sums, moved(sums, z_pair), moved(sums, z_middle)]
    both = jnp.concatenate([gram, moved(gram, over_core)], axis=1)
    both = jnp.concatenate([both, jnp.concatenate(metas, axis=1)], axis=0)
    around = [both] + [moved(both, where) for where in SQUARE]
    coupled = plane_couple(first, around[:2], rows)
    coupled, sums = lax.optimization_barrier((coupled, sums))
    coupling = plane_couple(first, around[2:], rows, coupled)
    pulled = [plane_first(flags, sums, spec, mats)]

    slot_rows, slot_rows_other, mixes = [], [], []
    for k in range(3):
        values = [pulled[k]] + [moved(pulled[k], where) for where in SQUARE]
        mine, other, picked = plane_mix(first, coupling, metas, values)
        beside = moved(other, over_core)
        slot_rows.append(picked)
        slot_rows_other.append(beside)
        mixed = mine + beside[: hours + NOTE]
        sums = [mixed, moved(mixed, z_pair), moved(mixed, z_middle)]
        mixes.append(sums)
        if k == 0:
            following, now = plane_open(flags, sums, pulled[0], spec, mats)
        elif k == 1:
            note = mixed[hours:]
            two, mirror = moved(note, z_two), moved(note, z_mirror)
            open_note, following, state = plane_step(
                flags, sums, two, mirror, mixes[0], pulled[1], pulled[0], now, spec, mats
            )
        else:
            note = plane_close(flags, sums, pulled[2], state, spec, mats)
        pulled.append(following)
    close_note = lax.all_to_all(note, ("basin", "tm"), 0, 0, tiled=False)
    answer = moved(plane_combine(open_note, close_note, slot_rows, slot_rows_other), from_plane)
    return plane_finish(answer, incidence, first_guess)


def solution(mesh):
    planes = dict(mesh.shape) == {"basin": Z_ * X_, "tm": Y_ * C_}
    in_specs = (
        P("basin", None, None),
        P("basin"),
        P("basin"),
        P(),
        P("basin", "tm"),
        P("basin", "tm"),
    )
    return jax.shard_map(
        plane_shards if planes else shards, mesh=mesh, in_specs=in_specs, out_specs=P("basin", "tm"), check_vma=False
    )
```

```python
import functools

import jax
import jax.numpy as jnp
import numpy as np
from jax import lax
from jax.experimental import pallas as pl
from jax.experimental.pallas import tpu as pltpu
from jax.sharding import PartitionSpec as P

F32 = jnp.float32
BF16 = jnp.bfloat16
HIGH = lax.Precision.HIGHEST
SPAN = 256
MIB = 1024 * 1024


SMALL = pl.CostEstimate(flops=1, bytes_accessed=1, transcendentals=0)


def params(mib=16):
    return pltpu.CompilerParams(vmem_limit_bytes=mib * MIB)


def transforms():
    half = SPAN // 2
    freq = 2.0 * np.pi * (np.arange(half) + 0.5) / SPAN
    phase = np.arange(SPAN)[:, None] * freq[None, :]
    forward = np.concatenate([np.cos(phase), -np.sin(phase)], axis=1)
    inverse = forward.T * (2.0 / SPAN)
    return (
        jnp.asarray(forward, F32),
        jnp.asarray(inverse[:, :half], F32),
        jnp.asarray(inverse[:, half:], F32),
    )


def dot(a, b):
    return jnp.dot(a, b, preferred_element_type=F32)


def exact(a, b):
    return jnp.dot(a, b, precision=HIGH, preferred_element_type=F32)


def pieces(value, count):
    out = []
    for _ in range(count):
        piece = value.astype(BF16)
        out.append(piece)
        value = value - piece.astype(F32)
    return out


def pick(hot, value):
    return sum(dot(hot, piece) for piece in pieces(value, 3))


def prepare_kernel(inc_ref, field_ref, partial_ref, gram_ref):
    blocks, slots, width = inc_ref.shape
    rows = blocks * slots
    weights = inc_ref[...].astype(F32).astype(BF16)
    for b in range(blocks):
        value = field_ref[pl.ds(b * width, width), :]
        partial_ref[pl.ds(b * slots, slots), :] = pick(weights[b], value)
    flat = weights.reshape(rows, width)
    full = lax.dot_general(flat, flat, (((1,), (1,)), ((), ())), preferred_element_type=F32)
    row = lax.broadcasted_iota(jnp.int32, (rows, rows), 0)
    col = lax.broadcasted_iota(jnp.int32, (rows, rows), 1)
    own = jnp.where(row // slots == col // slots, full, 0.0)
    gram_ref[...] = jnp.sum(own.reshape(blocks, slots, rows), axis=0)


def prepare(incidence, field):
    blocks, slots, width = incidence.shape
    hours = field.shape[1]
    step = 8
    return pl.pallas_call(
        prepare_kernel,
        grid=(blocks // step,),
        in_specs=[
            pl.BlockSpec((step, slots, width), lambda i: (i, 0, 0)),
            pl.BlockSpec((step * width, hours), lambda i: (i, 0)),
        ],
        out_specs=[
            pl.BlockSpec((step * slots, hours), lambda i: (i, 0)),
            pl.BlockSpec((slots, step * slots), lambda i: (0, i)),
        ],
        out_shape=[
            jax.ShapeDtypeStruct((blocks * slots, hours), F32),
            jax.ShapeDtypeStruct((slots, blocks * slots), F32),
        ],
        compiler_params=params(56),
        name="prepare",
    )(incidence, field)


def table_kernel(gauge_ref, partial_ref, out_ref):
    slots = partial_ref.shape[0]
    rows = out_ref.shape[0]
    first = pl.program_id(0) * rows
    gauge = lax.broadcasted_iota(jnp.int32, (rows, slots), 0) + first
    hot = jnp.where(gauge_ref[...] == gauge, 1.0, 0.0).astype(BF16)
    out_ref[...] = pick(hot, partial_ref[...])


def table(row_gauge, partial, gauges):
    slots, hours = partial.shape
    step = 256
    return pl.pallas_call(
        table_kernel,
        grid=(gauges // step,),
        in_specs=[
            pl.BlockSpec((1, slots), lambda i: (0, 0)),
            pl.BlockSpec((slots, hours), lambda i: (0, 0)),
        ],
        out_specs=pl.BlockSpec((step, hours), lambda i: (i, 0)),
        out_shape=jax.ShapeDtypeStruct((gauges, hours), F32),
        compiler_params=params(56),
        name="table",
    )(row_gauge.reshape(1, slots), partial)


def couple_kernel(first_ref, lane_ref, sub_ref, gram_ref, high_ref, low_ref, near_ref):
    slots = gram_ref.shape[0]
    count = lane_ref.shape[1]
    rows, cols = high_ref.shape
    tile = 256
    first = first_ref[0]

    @pl.when(pl.program_id(0) == 0)
    def _():
        row = lax.broadcasted_iota(jnp.int32, (tile, tile), 0)
        col = lax.broadcasted_iota(jnp.int32, (tile, tile), 1)
        same = row // slots == col // slots
        mine = lax.broadcasted_iota(jnp.int32, (rows, tile), 0) + first

        def body(i, carry):
            here = pl.ds(pl.multiple_of(i * tile, tile), tile)
            block = jnp.concatenate([gram_ref[:, here]] * (tile // slots), axis=0)
            block = jnp.where(same, block, 0.0).astype(BF16)
            hot = jnp.where(lane_ref[:, here] == mine, 1.0, 0.0).astype(BF16)
            near_ref[:, here] = dot(hot, block)
            return carry

        lax.fori_loop(0, count // tile, body, 0)

    def chunk(i, total):
        here = pl.ds(pl.multiple_of(i * 1024, 1024), 1024)
        gauge = lax.broadcasted_iota(jnp.int32, (1024, cols), 1) + pl.program_id(0) * cols
        hot = jnp.where(sub_ref[here, :] == gauge, 1.0, 0.0).astype(BF16)
        near = near_ref[:, here]
        high = near.astype(BF16)
        low = (near - high.astype(F32)).astype(BF16)
        return total + dot(high, hot) + dot(low, hot)

    total = lax.fori_loop(0, count // 1024, chunk, jnp.zeros((rows, cols), F32))
    high, low = pieces(total, 2)
    high_ref[...] = high
    low_ref[...] = low


def couple(first, row_gauge, gram, rows, gauges):
    count = row_gauge.shape[0]
    step = 256
    return pl.pallas_call(
        couple_kernel,
        grid=(gauges // step,),
        in_specs=[
            pl.BlockSpec(memory_space=pltpu.SMEM),
            pl.BlockSpec((1, count), lambda i: (0, 0)),
            pl.BlockSpec((count, 1), lambda i: (0, 0)),
            pl.BlockSpec(gram.shape, lambda i: (0, 0)),
        ],
        out_specs=[pl.BlockSpec((rows, step), lambda i: (0, i))] * 2,
        out_shape=[jax.ShapeDtypeStruct((rows, gauges), BF16)] * 2,
        scratch_shapes=[pltpu.VMEM((rows, count), F32)],
        compiler_params=params(56),
        name="couple",
    )(first, row_gauge.reshape(1, count), row_gauge.reshape(count, 1), gram)


def mix_kernel(high_ref, low_ref, value_ref, out_ref):
    high = high_ref[...]
    low = low_ref[...]
    one, two, three = pieces(value_ref[...], 3)
    out_ref[...] = (dot(high, three) + dot(low, two)) + (dot(high, two) + dot(low, one)) + dot(high, one)


def mix(high, low, value):
    return pl.pallas_call(
        mix_kernel,
        out_shape=jax.ShapeDtypeStruct((high.shape[0], value.shape[1]), F32),
        compiler_params=params(56),
        name="mix",
    )(high, low, value)


def spectrum_kernel(class_ref, kernels_ref, forward_ref, out_ref):
    rows = class_ref.shape[0]
    classes, taps = kernels_ref.shape
    kind = lax.broadcasted_iota(jnp.int32, (rows, classes), 1)
    hot = jnp.where(class_ref[...] == kind, 1.0, 0.0)
    out_ref[...] = exact(exact(hot, kernels_ref[...]), forward_ref[pl.ds(0, taps), :])


def spectrum(gauge_kernel, kernels, forward):
    rows = gauge_kernel.shape[0]
    return pl.pallas_call(
        spectrum_kernel,
        out_shape=jax.ShapeDtypeStruct((rows, SPAN), F32),
        compiler_params=params(56),
        name="spectrum",
    )(gauge_kernel.reshape(rows, 1), kernels, forward)


def delayed(before, here, after, spec, forward, inverse_last):
    rows, half = here.shape
    stacked = jnp.concatenate(
        [jnp.concatenate([before, here], axis=1), jnp.concatenate([here, after], axis=1)], axis=0
    )
    waves = exact(stacked, forward)
    real, imag = waves[:, :half], waves[:, half:]
    kr = jnp.concatenate([spec[:, :half]] * 2, axis=0)
    ki = jnp.concatenate([spec[:, half:]] * 2, axis=0)
    turned = jnp.concatenate([real * kr - imag * ki, real * ki + imag * kr], axis=1)
    out = exact(turned, inverse_last)
    return out[:rows], out[rows:]


def advanced(here, after, spec, forward, inverse_first):
    half = here.shape[1]
    waves = exact(jnp.concatenate([here, after], axis=1), forward)
    real, imag = waves[:, :half], waves[:, half:]
    kr, ki = spec[:, :half], spec[:, half:]
    turned = jnp.concatenate([real * kr + imag * ki, imag * kr - real * ki], axis=1)
    return exact(turned, inverse_first)


def lanes(a, b):
    return jnp.sum(a * b, axis=0, keepdims=True)


def total(ref, row):
    return jnp.sum(ref[row : row + 1, :], axis=1, keepdims=True)


def ratios(ref):
    square = total(ref, 0)
    alpha = jnp.sqrt(square)
    beta = jnp.sqrt(jnp.maximum(total(ref, 1) / square - 2.0 * total(ref, 2) + square, 0.0))
    return alpha, beta


def first_kernel(
    more_ref, sums_ref, observed_ref, spec_ref, forward_ref, first_ref, last_ref, out_ref, note_ref
):
    rows, half = observed_ref.shape[0] // 2, observed_ref.shape[1]
    spec, forward = spec_ref[...], forward_ref[...]
    before, here, after = (sums_ref[pl.ds(i * rows, rows), :] for i in range(3))
    now, later = delayed(before, here, after, spec, forward, last_ref[...])
    start = observed_ref[pl.ds(0, rows), :] - now
    start_later = (observed_ref[pl.ds(rows, rows), :] - later) * more_ref[0]
    out_ref[...] = advanced(start, start_later, spec, forward, first_ref[...])
    note_ref[...] = jnp.concatenate([lanes(start, start), jnp.zeros((7, half), F32)], axis=0)


def first_step(more, sums, observed, spec, mats):
    rows, half = spec.shape[0], observed.shape[1]
    return pl.pallas_call(
        first_kernel,
        in_specs=[pl.BlockSpec(memory_space=pltpu.SMEM)] + [pl.BlockSpec(memory_space=pltpu.VMEM)] * 6,
        out_shape=[jax.ShapeDtypeStruct((rows, half), F32), jax.ShapeDtypeStruct((8, half), F32)],
        compiler_params=params(56),
        name="first_step",
    )(more, sums, observed, spec, *mats)


def step_kernel(
    opening,
    final,
    more_ref,
    note_ref,
    sums_ref,
    spec_ref,
    forward_ref,
    first_ref,
    last_ref,
    pulled_ref,
    *refs,
):
    if opening:
        state_ref = None
    else:
        state_ref, *refs = refs
    if final:
        (out_note_ref,) = refs
    else:
        new_ref, out_ref, out_note_ref = refs
    rows, half = pulled_ref.shape
    spec, forward = spec_ref[...], forward_ref[...]
    if opening:
        scale = 1.0 / jnp.sqrt(total(note_ref, 0))
        along = sums_ref[...] * scale
        new_s, new_su = along, along
        new_zu = pulled_ref[...] * scale
        new_z = new_zu
    else:
        alpha, beta = ratios(note_ref)
        a, b, g = 1.0 / (alpha * beta), alpha / beta, beta / alpha
        wide = pl.ds(0, 3 * rows), pl.ds(3 * rows, 3 * rows)
        new_su = sums_ref[...] * a - state_ref[wide[1], :] * b
        new_s = new_su - state_ref[wide[0], :] * g
        new_zu = pulled_ref[...] * a - state_ref[pl.ds(7 * rows, rows), :] * b
        new_z = new_zu - state_ref[pl.ds(6 * rows, rows), :] * g
    before, here, after = (new_s[i * rows : (i + 1) * rows] for i in range(3))
    now, later = delayed(before, here, after, spec, forward, last_ref[...])
    out_note_ref[...] = jnp.concatenate(
        [lanes(new_z, here), lanes(now, now), lanes(new_zu, here), jnp.zeros((5, half), F32)], axis=0
    )
    if not final:
        new_ref[pl.ds(0, 3 * rows), :] = new_s
        new_ref[pl.ds(3 * rows, 3 * rows), :] = new_su
        new_ref[pl.ds(6 * rows, rows), :] = new_z
        new_ref[pl.ds(7 * rows, rows), :] = new_zu
        out_ref[...] = advanced(now, later * more_ref[0], spec, forward, first_ref[...])


def next_step(more, note, sums, spec, mats, pulled, state, final):
    rows, half = pulled.shape
    opening = state is None
    shapes = [
        jax.ShapeDtypeStruct((8 * rows, half), F32),
        jax.ShapeDtypeStruct((rows, half), F32),
        jax.ShapeDtypeStruct((8, half), F32),
    ]
    args = [more, note, sums, spec, *mats, pulled] + ([] if opening else [state])
    return pl.pallas_call(
        functools.partial(step_kernel, opening, final),
        in_specs=[pl.BlockSpec(memory_space=pltpu.SMEM)]
        + [pl.BlockSpec(memory_space=pltpu.VMEM)] * (len(args) - 1),
        out_shape=shapes[2:] if final else shapes,
        compiler_params=params(56),
        name="next_step",
    )(*args)


def weights_of(notes):
    start = jnp.sqrt(total(notes[0], 0))
    zero = jnp.zeros_like(start)
    units = [1.0 / start, zero, zero]
    z, zu = list(units), list(units)
    phibar = start
    alpha, beta = ratios(notes[1])
    rhobar = alpha
    w = [value / alpha for value in z]
    result = [zero] * 3
    steps = len(notes) - 1
    for k in range(steps):
        rho = jnp.sqrt(rhobar * rhobar + beta * beta)
        cosine, sine = rhobar / rho, beta / rho
        phi, phibar = cosine * phibar, sine * phibar
        result = [r + phi / rho * value for r, value in zip(result, w)]
        if k < steps - 1:
            a, b, g = 1.0 / (alpha * beta), alpha / beta, beta / alpha
            zu = [(a if i == k + 1 else 0.0) - b * value for i, value in enumerate(zu)]
            z = [value - g * old for value, old in zip(zu, z)]
            alpha, beta = ratios(notes[k + 2])
            theta = sine * alpha
            rhobar = -cosine * alpha
            w = [value / alpha - theta / rho * old for value, old in zip(z, w)]
    return result


def finish_kernel(n0, n1, n2, n3, gauge_ref, q0, q1, q2, inc_ref, field_ref, out_ref, rows_ref):
    blocks, slots, width = inc_ref.shape
    count = rows_ref.shape[0]
    gauges = q0.shape[0]
    step = pl.program_id(0)

    @pl.when(step == 0)
    def _():
        e0, e1, e2 = weights_of([n0, n1, n2, n3])
        width_ = 512

        def body(i, value):
            here = pl.ds(pl.multiple_of(i * width_, width_), width_)
            mixed = q0[here, :] * e0 + q1[here, :] * e1 + q2[here, :] * e2
            gauge = lax.broadcasted_iota(jnp.int32, (count, width_), 1) + i * width_
            hot = jnp.where(gauge_ref[...] == gauge, 1.0, 0.0).astype(BF16)
            return value + pick(hot, mixed)

        rows_ref[...] = lax.fori_loop(0, gauges // width_, body, jnp.zeros(rows_ref.shape, F32))

    weights = inc_ref[...].astype(F32).astype(BF16)
    for b in range(blocks):
        here = pl.ds(b * width, width)
        rows = rows_ref[pl.ds(pl.multiple_of((step * blocks + b) * slots, slots), slots), :]
        added = sum(
            lax.dot_general(weights[b], piece, (((0,), (0,)), ((), ())), preferred_element_type=F32)
            for piece in pieces(rows, 3)
        )
        out_ref[here, :] = field_ref[here, :] + added


def finish(notes, row_gauge, gathered, incidence, field):
    blocks, slots, width = incidence.shape
    hours = field.shape[1]
    count = row_gauge.shape[0]
    step = 8
    whole = lambda shape: pl.BlockSpec(shape, lambda i: (0, 0))
    return pl.pallas_call(
        finish_kernel,
        grid=(blocks // step,),
        in_specs=[whole(n.shape) for n in notes]
        + [whole((count, 1))]
        + [whole(q.shape) for q in gathered]
        + [
            pl.BlockSpec((step, slots, width), lambda i: (i, 0, 0)),
            pl.BlockSpec((step * width, hours), lambda i: (i, 0)),
        ],
        out_specs=pl.BlockSpec((step * width, hours), lambda i: (i, 0)),
        out_shape=jax.ShapeDtypeStruct(field.shape, F32),
        scratch_shapes=[pltpu.VMEM((count, hours), F32)],
        compiler_params=params(56),
        name="finish",
    )(*notes, row_gauge.reshape(count, 1), *gathered, incidence, field)


def shifted(value, axis, by):
    devices = lax.axis_size(axis)
    pairs = [(i, i + by) for i in range(devices) if 0 <= i + by < devices]
    return lax.ppermute(value, axis, pairs)


def window(value):
    return jnp.concatenate([shifted(value, "tm", 1), value, shifted(value, "tm", -1)], axis=0)


def gathered_rows(value):
    owners = lax.axis_size("basin")
    copies = jnp.broadcast_to(value[None], (owners,) + value.shape)
    return lax.all_to_all(copies, "basin", 0, 0, tiled=False)


def over_hours(note):
    blocks = lax.axis_size("tm")
    result = note
    for by in range(1, blocks):
        result = result + lax.ppermute(note, "tm", [(i, (i + by) % blocks) for i in range(blocks)])
    return result


def shards(incidence, row_gauge, gauge_kernel, kernels, observed, first_guess):
    owners = lax.axis_size("basin")
    rows, hours = observed.shape
    gauges = rows * owners
    mats = transforms()
    spec = spectrum(gauge_kernel, kernels, mats[0])
    more = (lax.axis_index("tm") < lax.axis_size("tm") - 1).astype(F32).reshape(1)
    partial, gram = prepare(incidence, first_guess)
    all_gram = lax.all_gather(gram, "basin", axis=1, tiled=True)
    all_rows = lax.all_gather(row_gauge, "basin", axis=0, tiled=True)
    dense = table(row_gauge, partial, gauges).reshape(owners, rows, hours)
    sums = jnp.sum(lax.all_to_all(dense, "basin", 0, 0, tiled=False), axis=0)
    both = jnp.concatenate([observed, shifted(observed, "tm", -1)], axis=0)
    first = (lax.axis_index("basin") * rows).astype(jnp.int32).reshape(1)
    high, low = couple(first, all_rows, all_gram, rows, gauges)

    pulled, note = first_step(more, window(sums), both, spec, mats)
    notes, kept, state = [], [], None
    for k in range(3):
        everyone = gathered_rows(jnp.concatenate([pulled, note], axis=0))
        value = everyone[:, :rows].reshape(gauges, hours)
        notes.append(over_hours(jnp.sum(everyone[:, rows:], axis=0)))
        kept.append(value)
        around = window(mix(high, low, value))
        final = k == 2
        result = next_step(more, notes[-1], around, spec, mats, pulled, state, final)
        if final:
            (note,) = result
        else:
            state, pulled, note = result
    notes.append(over_hours(jnp.sum(gathered_rows(note), axis=0)))
    return finish(notes, row_gauge, kept, incidence, first_guess)


Z_, X_, Y_, C_ = 4, 2, 2, 2
NOTE = 8


def device(z, x, y, c):
    return (z * X_ + x) * (Y_ * C_) + y * C_ + c


def moved(value, where):
    pairs = []
    for z, x, y, c in np.ndindex(Z_, X_, Y_, C_):
        target = where(z, x, y, c)
        if target is not None:
            pairs.append((device(z, x, y, c), device(*target)))
    return lax.ppermute(value, ("basin", "tm"), pairs)


def to_plane(z, x, y, c):
    return 2 * y + c, x, z & 1, z >> 1


def to_plane_before(z, x, y, c):
    t = 2 * y + c
    return (t - 1, x, z & 1, z >> 1) if t else None


def from_plane(z, x, y, c):
    return 2 * c + y, x, z >> 1, z & 1


def over_x(z, x, y, c):
    return z, 1 - x, y, c


def over_y(z, x, y, c):
    return z, x, 1 - y, c


def over_xy(z, x, y, c):
    return z, 1 - x, 1 - y, c


def over_core(z, x, y, c):
    return z, x, y, 1 - c


def z_pair(z, x, y, c):
    return z ^ 1, x, y, c


def z_middle(z, x, y, c):
    return (3 - z, x, y, c) if z in (1, 2) else None


def z_two(z, x, y, c):
    return z ^ 2, x, y, c


def z_mirror(z, x, y, c):
    return 3 - z, x, y, c


SQUARE = (over_x, over_y, over_xy)


def split_constant(value):
    out = []
    for _ in range(3):
        piece = value.astype(jnp.bfloat16)
        out.append(jnp.asarray(piece))
        value = value - piece.astype(np.float64)
    return out


def turned_transforms():
    half = SPAN // 2
    freq = 2.0 * np.pi * (np.arange(half) + 0.5) / SPAN
    phase = freq[:, None] * np.arange(SPAN)[None, :]
    forward = np.concatenate([np.cos(phase), -np.sin(phase)], axis=0)
    inverse = forward.T * (2.0 / SPAN)
    return split_constant(forward), split_constant(inverse[:half]), split_constant(inverse[half:])


def product(mats, value, order):
    parts = pieces(value, order)
    result = None
    for level in reversed(range(order)):
        for i in range(level + 1):
            term = dot(mats[i][...], parts[level - i])
            result = term if result is None else result + term
    return result


def turn(waves, spec, sign):
    half = waves.shape[0] // 2
    real, imag = waves[:half], waves[half:]
    kr, ki = spec[:half], spec[half:] * sign
    return jnp.concatenate([real * kr - imag * ki, real * ki + imag * kr], axis=0)


def plane_delayed(before, here, after, spec, forward, last, order):
    out = []
    for pair in ((before, here), (here, after)):
        waves = product(forward, jnp.concatenate(pair, axis=0), order)
        out.append(product(last, turn(waves, spec, 1.0), order))
    return out


def plane_advanced(here, after, spec, forward, first, order):
    waves = product(forward, jnp.concatenate([here, after], axis=0), order)
    return product(first, turn(waves, spec, -1.0), order)


def describe_kernel(inc_ref, gauge_ref, kind_ref, out_ref):
    blocks, slots, width = inc_ref.shape
    tile = 8
    rows = tile * slots
    weights = inc_ref[...].astype(F32).astype(BF16)
    row = lax.broadcasted_iota(jnp.int32, (rows, rows), 0)
    col = lax.broadcasted_iota(jnp.int32, (rows, rows), 1)
    same = row // slots == col // slots
    for i in range(blocks // tile):
        flat = weights[i * tile : (i + 1) * tile].reshape(rows, width)
        full = lax.dot_general(flat, flat, (((1,), (1,)), ((), ())), preferred_element_type=F32)
        own = jnp.where(same, full, 0.0)
        out_ref[pl.ds(0, slots), pl.ds(i * rows, rows)] = jnp.sum(own.reshape(tile, slots, rows), axis=0)
    kinds = kind_ref.shape[1]
    out_ref[pl.ds(slots, 8), :] = jnp.concatenate(
        [
            gauge_ref[...].astype(F32),
            jnp.concatenate(
                [kind_ref[...].astype(F32), jnp.zeros((1, blocks * slots - kinds), F32)], axis=1
            ),
            jnp.zeros((6, blocks * slots), F32),
        ],
        axis=0,
    )


def describe(incidence, row_gauge, gauge_kernel):
    blocks, slots, _ = incidence.shape
    count = blocks * slots
    return pl.pallas_call(
        describe_kernel,
        out_shape=jax.ShapeDtypeStruct((slots + 8, count), F32),
        compiler_params=params(),
        name="describe",
        cost_estimate=SMALL,
    )(incidence, row_gauge.reshape(1, count), gauge_kernel.reshape(1, gauge_kernel.shape[0]))


def send_kernel(inc_ref, field_ref, out_ref):
    blocks, slots, width = inc_ref.shape
    weights = inc_ref[...].astype(F32).astype(BF16)
    parts = []
    for b in range(blocks):
        parts.append(pick(weights[b], field_ref[pl.ds(b * width, width), :]))
    out_ref[...] = jnp.transpose(jnp.concatenate(parts, axis=0))


def send(incidence, field):
    blocks, slots, width = incidence.shape
    hours = field.shape[1]
    step = 8
    return pl.pallas_call(
        send_kernel,
        grid=(blocks // step,),
        in_specs=[
            pl.BlockSpec((step, slots, width), lambda i: (i, 0, 0)),
            pl.BlockSpec((step * width, hours), lambda i: (i, 0)),
        ],
        out_specs=pl.BlockSpec((hours, step * slots), lambda i: (0, i)),
        out_shape=jax.ShapeDtypeStruct((hours, blocks * slots), F32),
        compiler_params=params(),
        name="send",
        cost_estimate=SMALL,
    )(incidence, field)


def hot_rows(gauge, first, rows):
    mine = (lax.broadcasted_iota(jnp.int32, (rows, gauge.shape[1]), 0) + first).astype(F32)
    return jnp.where(gauge == mine, 1.0, 0.0).astype(BF16)


def spread_kernel(first_ref, mine_ref, other_ref, meta_ref, meta_other_ref, *out_refs):
    rows = out_refs[0].shape[1]
    where = meta_ref.shape[0] - 8
    for m, out_ref in enumerate(out_refs):
        result = None
        for ref, meta in ((mine_ref, meta_ref), (other_ref, meta_other_ref)):
            hot = hot_rows(meta[where : where + 1, :], first_ref[m], rows)
            for piece in reversed(pieces(ref[...], 3)):
                term = lax.dot_general(
                    piece, hot, (((1,), (1,)), ((), ())), preferred_element_type=F32
                )
                result = term if result is None else result + term
        out_ref[...] = result


def spread(first, parcels, metas, rows):
    hours = parcels[0].shape[0]
    return pl.pallas_call(
        spread_kernel,
        in_specs=[pl.BlockSpec(memory_space=pltpu.SMEM)] + [pl.BlockSpec(memory_space=pltpu.VMEM)] * 4,
        out_shape=[jax.ShapeDtypeStruct((hours, rows), F32)] * 4,
        compiler_params=params(),
        name="spread",
        cost_estimate=SMALL,
    )(first, *parcels, *metas)


def plane_couple_kernel(last, first_ref, *refs):
    if last:
        a_ref, b_ref, before_ref, high_ref, low_ref, total_ref, meta_ref = refs
        total_ref[...] = before_ref[...]
    else:
        a_ref, b_ref, total_ref, meta_ref = refs
        total_ref[...] = jnp.zeros_like(total_ref)
    height, double = a_ref.shape
    slots = height - 8
    count = double // 2
    cols, rows = total_ref.shape
    tile = 256
    for i, ref in enumerate((a_ref, b_ref)):
        for j in range(2):
            meta_ref[2 * i + j] = ref[:, j * count : (j + 1) * count]
    row = lax.broadcasted_iota(jnp.int32, (tile, tile), 0)
    col = lax.broadcasted_iota(jnp.int32, (tile, tile), 1)
    same = row // slots == col // slots

    def body(i, carry):
        gauge = meta_ref[i, slots : slots + 1, :]
        near = []
        for j in range(count // tile):
            here = slice(j * tile, (j + 1) * tile)
            block = jnp.concatenate([meta_ref[i, :slots, here]] * (tile // slots), axis=0)
            block = jnp.where(same, block, 0.0).astype(BF16)
            mine = jnp.concatenate(
                [hot_rows(gauge[:, here], first_ref[4 + h], rows // 2) for h in range(2)], axis=0
            )
            near.append(
                lax.dot_general(block, mine, (((1,), (1,)), ((), ())), preferred_element_type=F32)
            )
        near = jnp.concatenate(near, axis=0)
        high = near.astype(BF16)
        rest = near - high.astype(F32)
        hot = jnp.concatenate([hot_rows(gauge, first_ref[m], cols // 4) for m in range(4)], axis=0)
        total_ref[...] += dot(hot, high)

        @pl.when(jnp.max(jnp.abs(rest)) > 0.0)
        def _():
            total_ref[...] += dot(hot, rest.astype(BF16))

        return carry

    lax.fori_loop(0, 4, body, 0)
    if last:
        high, low = pieces(total_ref[...], 2)
        high_ref[...] = high
        low_ref[...] = low


def plane_couple(first, metas, rows, before=None):
    height, double = metas[0].shape
    shape = (4 * rows, 2 * rows)
    last = before is not None
    args = [first, *metas] + ([before] if last else [])
    scratch = [pltpu.VMEM((4, height, double // 2), F32)]
    return pl.pallas_call(
        functools.partial(plane_couple_kernel, last),
        in_specs=[pl.BlockSpec(memory_space=pltpu.SMEM)]
        + [pl.BlockSpec(memory_space=pltpu.VMEM)] * (len(args) - 1),
        out_shape=[jax.ShapeDtypeStruct(shape, BF16)] * 2 if last else jax.ShapeDtypeStruct(shape, F32),
        scratch_shapes=([pltpu.VMEM(shape, F32)] if last else []) + scratch,
        compiler_params=params(),
        name="plane_couple",
        cost_estimate=pl.CostEstimate(
            flops=2 * 2 * double * 8 * rows * rows, bytes_accessed=2_000_000, transcendentals=0
        ),
    )(*args)


def plane_mix_kernel(
    first_ref, high_ref, low_ref, meta_ref, meta_other_ref, a_ref, b_ref, c_ref, d_ref, mine_ref, other_ref, rows_ref
):
    refs = (a_ref, b_ref, c_ref, d_ref)
    height, rows = a_ref.shape
    hours = height - NOTE
    body, tail = pl.ds(0, hours), pl.ds(hours, NOTE)
    value = jnp.concatenate([ref[body, :] for ref in refs], axis=1)
    one, two = pieces(value, 2)
    high, low = high_ref[...], low_ref[...]
    result = (dot(two, high) + dot(one, low)) + dot(one, high)
    note = sum(ref[tail, :] for ref in refs)
    mine_ref[body, :] = result[:, :rows]
    other_ref[body, :] = result[:, rows:]
    mine_ref[tail, :] = note
    other_ref[tail, :] = note
    where = meta_ref.shape[0] - 8
    for ref in (meta_ref, meta_other_ref):
        gauge = ref[where : where + 1, :]
        hot = jnp.concatenate([hot_rows(gauge, first_ref[m], rows) for m in range(4)], axis=0)
        picked = dot(two, hot) + dot(one, hot)
        if ref is meta_ref:
            rows_ref[...] = picked
        else:
            for i in range(gauge.shape[1] // rows):
                other_ref[pl.ds(height + i * hours, hours), :] = picked[:, i * rows : (i + 1) * rows]


def plane_mix(first, coupling, metas, values):
    height, rows = values[0].shape
    hours = height - NOTE
    slots = metas[0].shape[1]
    return pl.pallas_call(
        plane_mix_kernel,
        in_specs=[pl.BlockSpec(memory_space=pltpu.SMEM)] + [pl.BlockSpec(memory_space=pltpu.VMEM)] * 8,
        out_shape=[
            jax.ShapeDtypeStruct((height, rows), F32),
            jax.ShapeDtypeStruct((height + slots // rows * hours, rows), F32),
            jax.ShapeDtypeStruct((hours, slots), F32),
        ],
        compiler_params=params(),
        name="plane_mix",
        cost_estimate=SMALL,
    )(first, *coupling, *metas, *values)


def plane_spectrum_kernel(class_ref, kernels_ref, f0_ref, f1_ref, f2_ref, out_ref):
    classes, taps = kernels_ref.shape
    kind = class_ref[class_ref.shape[0] - 7 : class_ref.shape[0] - 6, : out_ref.shape[1]]
    hot = jnp.where(
        lax.broadcasted_iota(jnp.int32, (classes, kind.shape[1]), 0).astype(F32) == kind, 1.0, 0.0
    ).astype(BF16)
    chosen = None
    for piece in reversed(pieces(jnp.transpose(kernels_ref[...]), 3)):
        term = dot(piece, hot)
        chosen = term if chosen is None else chosen + term
    mats = [ref[:, :taps] for ref in (f0_ref, f1_ref, f2_ref)]
    out_ref[...] = product(mats, chosen, 3)


def plane_spectrum(meta, kernels, forward, rows):
    return pl.pallas_call(
        plane_spectrum_kernel,
        out_shape=jax.ShapeDtypeStruct((SPAN, rows), F32),
        compiler_params=params(),
        name="plane_spectrum",
        cost_estimate=SMALL,
    )(meta, kernels, *forward)


def sides(even, pair, middle):
    return jnp.where(even, middle, pair), jnp.where(even, pair, middle)


def plane_first_kernel(flag_ref, here_ref, pair_ref, middle_ref, seen_ref, seen_later_ref, spec_ref, *refs):
    *mats, out_ref = refs
    forward, first, last = mats[0:3], mats[3:6], mats[6:9]
    hours, rows = here_ref.shape
    spec = spec_ref[...]
    before, after = sides(flag_ref[0] > 0.5, pair_ref[...], middle_ref[...])
    now, later = plane_delayed(before, here_ref[...], after, spec, forward, last, 3)
    start = jnp.transpose(seen_ref[...]) - now
    start_later = (jnp.transpose(seen_later_ref[...]) - later) * flag_ref[1]
    out_ref[pl.ds(0, hours), :] = plane_advanced(start, start_later, spec, forward, first, 3)
    out_ref[pl.ds(hours, NOTE), :] = jnp.concatenate(
        [lanes(start, start), jnp.zeros((NOTE - 1, rows), F32)], axis=0
    )


def plane_first(flags, sums, seen, seen_later, spec, mats):
    hours, rows = sums[0].shape
    args = [flags, *sums, seen, seen_later, spec, *mats]
    return pl.pallas_call(
        plane_first_kernel,
        in_specs=[pl.BlockSpec(memory_space=pltpu.SMEM)]
        + [pl.BlockSpec(memory_space=pltpu.VMEM)] * (len(args) - 1),
        out_shape=jax.ShapeDtypeStruct((hours + NOTE, rows), F32),
        compiler_params=params(),
        name="plane_first",
        cost_estimate=SMALL,
    )(*args)


def plane_open_kernel(flag_ref, here_ref, pair_ref, middle_ref, pulled_ref, spec_ref, *refs):
    mats, (out_ref, now_ref) = refs[:9], refs[9:]
    forward, first, last = mats[0:3], mats[3:6], mats[6:9]
    height, rows = pulled_ref.shape
    hours = height - NOTE
    tail, body = pl.ds(hours, NOTE), pl.ds(0, hours)
    spec = spec_ref[...]
    here = here_ref[body, :]
    before, after = sides(flag_ref[0] > 0.5, pair_ref[body, :], middle_ref[body, :])
    now, later = plane_delayed(before, here, after, spec, forward, last, 2)
    out_ref[body, :] = plane_advanced(now, later * flag_ref[1], spec, forward, first, 2)
    out_ref[tail, :] = jnp.concatenate(
        [
            lanes(pulled_ref[body, :], here),
            lanes(now, now),
            pulled_ref[hours : hours + 1, :],
            jnp.zeros((NOTE - 3, rows), F32),
        ],
        axis=0,
    )
    now_ref[...] = now


def plane_open(flags, sums, pulled, spec, mats):
    height, rows = pulled.shape
    args = [flags, *sums, pulled, spec, *mats]
    return pl.pallas_call(
        plane_open_kernel,
        in_specs=[pl.BlockSpec(memory_space=pltpu.SMEM)]
        + [pl.BlockSpec(memory_space=pltpu.VMEM)] * (len(args) - 1),
        out_shape=[
            jax.ShapeDtypeStruct((height, rows), F32),
            jax.ShapeDtypeStruct((height - NOTE, rows), F32),
        ],
        compiler_params=params(),
        name="plane_open",
        cost_estimate=SMALL,
    )(*args)


def opening(ref):
    start = total(ref, 2)
    square = total(ref, 0) / start
    alpha = jnp.sqrt(square)
    beta = jnp.sqrt(jnp.maximum(total(ref, 1) / total(ref, 0) - square, 0.0))
    return 1.0 / jnp.sqrt(start), alpha, beta


def plane_step_kernel(flag_ref, here_ref, pair_ref, middle_ref, two_ref, mirror_ref, *refs):
    old_refs, (pulled_ref, old_z_ref, old_now_ref, spec_ref), refs = refs[:3], refs[3:7], refs[7:]
    mats, (total_ref, out_ref, kept_ref) = refs[:9], refs[9:]
    forward, first, last = mats[0:3], mats[3:6], mats[6:9]
    height, rows = pulled_ref.shape
    hours = height - NOTE
    tail, body = pl.ds(hours, NOTE), pl.ds(0, hours)
    total_ref[...] = (here_ref[tail, :] + pair_ref[tail, :]) + (two_ref[...] + mirror_ref[...])
    scale, alpha, beta = opening(total_ref)
    a, b, g = scale / (alpha * beta), scale * alpha / beta, scale * beta / alpha
    spec = spec_ref[...]
    s, su = [], []
    for ref, old_ref in zip((here_ref, pair_ref, middle_ref), old_refs):
        old = old_ref[body, :]
        su.append(ref[body, :] * a - old * b)
        s.append(su[-1] - old * g)
    zu = pulled_ref[body, :] * a - old_z_ref[body, :] * b
    z = zu - old_z_ref[body, :] * g
    before, after = sides(flag_ref[0] > 0.5, s[1], s[2])
    now, later = plane_delayed(before, s[0], after, spec, forward, last, 2)
    out_ref[body, :] = plane_advanced(now, later * flag_ref[1], spec, forward, first, 2)
    out_ref[tail, :] = jnp.concatenate(
        [lanes(z, s[0]), lanes(now, now), lanes(zu, s[0]), jnp.zeros((NOTE - 3, rows), F32)], axis=0
    )
    for i, value in enumerate((s[0], su[0], z, zu, now, now + old_now_ref[...] * g)):
        kept_ref[pl.ds(i * hours, hours), :] = value


def plane_step(flags, sums, two, mirror, old, pulled, old_z, old_now, spec, mats):
    height, rows = pulled.shape
    args = [flags, *sums, two, mirror, *old, pulled, old_z, old_now, spec, *mats]
    return pl.pallas_call(
        plane_step_kernel,
        in_specs=[pl.BlockSpec(memory_space=pltpu.SMEM)]
        + [pl.BlockSpec(memory_space=pltpu.VMEM)] * (len(args) - 1),
        out_shape=[
            jax.ShapeDtypeStruct((NOTE, rows), F32),
            jax.ShapeDtypeStruct((height, rows), F32),
            jax.ShapeDtypeStruct((6 * (height - NOTE), rows), F32),
        ],
        compiler_params=params(),
        name="plane_step",
        cost_estimate=SMALL,
    )(*args)


def plane_close_kernel(flag_ref, here_ref, pair_ref, middle_ref, pulled_ref, kept_ref, spec_ref, *refs):
    mats, (out_ref,) = refs[:9], refs[9:]
    forward, last = mats[0:3], mats[6:9]
    height, rows = pulled_ref.shape
    hours = height - NOTE
    body = pl.ds(0, hours)
    before, after = sides(flag_ref[0] > 0.5, pair_ref[body, :], middle_ref[body, :])
    here = here_ref[body, :]
    waves = product(forward, jnp.concatenate([before, here], axis=0), 2)
    now = product(last, turn(waves, spec_ref[...], 1.0), 2)
    s, su, z, zu, old_now, old_now_u = (kept_ref[pl.ds(i * hours, hours), :] for i in range(6))
    raw = pulled_ref[body, :]
    note = [pulled_ref[hours + i : hours + i + 1, :] for i in range(3)]
    for left in (raw, zu, z):
        note += [lanes(left, right) for right in (here, su, s)]
    parts = (now, old_now_u, old_now)
    for i in range(3):
        note += [lanes(parts[i], parts[j]) for j in range(i, 3)]
    note.append(jnp.zeros((24 - len(note), rows), F32))
    note = jnp.sum(jnp.concatenate(note, axis=0), axis=1, keepdims=True)
    shape = (24, out_ref.shape[2])
    row, col = (lax.broadcasted_iota(jnp.int32, shape, i) for i in range(2))
    note = jnp.sum(jnp.where(row == col, jnp.broadcast_to(note, shape), 0.0), axis=0, keepdims=True)
    out_ref[...] = jnp.broadcast_to(note[None], out_ref.shape)


def plane_close(flags, sums, pulled, kept, spec, mats):
    rows = pulled.shape[1]
    args = [flags, *sums, pulled, kept, spec, *mats]
    return pl.pallas_call(
        plane_close_kernel,
        in_specs=[pl.BlockSpec(memory_space=pltpu.SMEM)]
        + [pl.BlockSpec(memory_space=pltpu.VMEM)] * (len(args) - 1),
        out_shape=jax.ShapeDtypeStruct((Z_ * X_ * Y_ * C_, 8, rows // 2), F32),
        compiler_params=params(),
        name="plane_close",
        cost_estimate=SMALL,
    )(*args)


def plane_weights(open_ref, close):
    scale, alpha, beta = opening(open_ref)
    start = 1.0 / scale
    phibar, rhobar = start, alpha
    zero = jnp.zeros_like(start)
    z = zu = [scale, zero, zero]
    w = [value / alpha for value in z]
    result = [zero] * 3
    for k in range(3):
        rho = jnp.sqrt(rhobar * rhobar + beta * beta)
        cosine, sine = rhobar / rho, beta / rho
        phi, phibar = cosine * phibar, sine * phibar
        result = [r + phi / rho * value for r, value in zip(result, w)]
        if k == 2:
            return result
        a, b, g = 1.0 / (alpha * beta), alpha / beta, beta / alpha
        zu = [-b * value for value in zu]
        zu[k + 1] = zu[k + 1] + (a * scale if k == 0 else a)
        z = [value - g * old for value, old in zip(zu, z)]
        if k == 0:
            square, norm, along = (close[:, i : i + 1] for i in range(3))
        else:
            plain = (a, -b, -g)
            cross = [[close[:, 3 + 3 * i + j : 4 + 3 * i + j] for j in range(3)] for i in range(3)]
            along = sum(plain[i] * plain[j] * cross[i][j] for i in range(2) for j in range(3))
            square = along + sum(plain[2] * plain[j] * cross[2][j] for j in range(3))
            pairs = [(i, j) for i in range(3) for j in range(i, 3)]
            norm = sum(
                plain[i] * plain[j] * close[:, 12 + n : 13 + n] * (1.0 if i == j else 2.0)
                for n, (i, j) in enumerate(pairs)
            )
        alpha = jnp.sqrt(square)
        beta = jnp.sqrt(jnp.maximum(norm / square - 2.0 * along + square, 0.0))
        theta = sine * alpha
        rhobar = -cosine * alpha
        w = [value / alpha - theta / rho * old for value, old in zip(z, w)]


def plane_combine_kernel(open_ref, close_ref, *refs):
    *parts, out_ref = refs
    hours, rows = out_ref.shape[1], open_ref.shape[1]
    close = jnp.sum(close_ref[...], axis=0)[0:1, :]
    weights = plane_weights(open_ref, close)
    mine = sum(ref[...] * e for ref, e in zip(parts[:3], weights))
    skip = parts[3].shape[0] - mine.shape[1] // rows * hours
    for i in range(mine.shape[1] // rows):
        here = pl.ds(skip + i * hours, hours)
        other = sum(ref[here, :] * e for ref, e in zip(parts[3:], weights))
        out_ref[pl.ds(i * rows, rows), :] = jnp.transpose(mine[:, i * rows : (i + 1) * rows] + other)


def plane_combine(open_note, close_note, mine, other):
    hours, slots = mine[0].shape
    return pl.pallas_call(
        plane_combine_kernel,
        out_shape=jax.ShapeDtypeStruct((slots, hours), F32),
        compiler_params=params(),
        name="plane_combine",
        cost_estimate=SMALL,
    )(open_note, close_note, *mine, *other)


def plane_finish_kernel(rows_ref, inc_ref, field_ref, out_ref):
    blocks, slots, width = inc_ref.shape
    weights = inc_ref[...].astype(F32).astype(BF16)
    for b in range(blocks):
        here = pl.ds(b * width, width)
        added = sum(
            lax.dot_general(weights[b], piece, (((0,), (0,)), ((), ())), preferred_element_type=F32)
            for piece in pieces(rows_ref[pl.ds(b * slots, slots), :], 2)
        )
        out_ref[here, :] = field_ref[here, :] + added


def plane_finish(rows, incidence, field):
    blocks, slots, width = incidence.shape
    hours = field.shape[1]
    step = 8
    return pl.pallas_call(
        plane_finish_kernel,
        grid=(blocks // step,),
        in_specs=[
            pl.BlockSpec((step * slots, hours), lambda i: (i, 0)),
            pl.BlockSpec((step, slots, width), lambda i: (i, 0, 0)),
            pl.BlockSpec((step * width, hours), lambda i: (i, 0)),
        ],
        out_specs=pl.BlockSpec((step * width, hours), lambda i: (i, 0)),
        out_shape=jax.ShapeDtypeStruct(field.shape, F32),
        compiler_params=params(),
        name="plane_finish",
    )(rows, incidence, field)


def plane_shards(incidence, row_gauge, gauge_kernel, kernels, observed, first_guess):
    rows, hours = observed.shape
    basin, tm = lax.axis_index("basin"), lax.axis_index("tm")
    z, x, y, c = basin // X_, basin % X_, tm // C_, tm % C_
    place = 2 * y + x
    first = jnp.stack([4 * c + (place ^ m) for m in range(4)] + [4 * c + place, 4 * (1 - c) + place])
    first = (first * rows).astype(jnp.int32)
    flags = jnp.stack([1 - z % 2, (z < Z_ - 1).astype(z.dtype)]).astype(F32)
    forward, inverse_first, inverse_last = turned_transforms()
    mats = [*forward, *inverse_first, *inverse_last]

    meta = describe(incidence, row_gauge, gauge_kernel)
    meta, field = lax.optimization_barrier((meta, first_guess))
    meta = moved(meta, to_plane)
    parcel = moved(send(incidence, field), to_plane)
    metas = [meta, moved(meta, over_core)]
    both = jnp.concatenate(metas, axis=1)
    around = [both] + [moved(both, where) for where in SQUARE]
    spec = plane_spectrum(meta, kernels, forward, rows)
    seen, parcel, around, spec = lax.optimization_barrier((observed, parcel, around, spec))
    seen_later = moved(seen, to_plane_before)
    seen = moved(seen, to_plane)

    dense = spread(first, [parcel, moved(parcel, over_core)], metas, rows)
    sums = dense[0] + sum(moved(value, where) for value, where in zip(dense[1:], SQUARE))
    sums = [sums, moved(sums, z_pair), moved(sums, z_middle)]
    coupled = plane_couple(first, around[:2], rows)
    coupled, sums = lax.optimization_barrier((coupled, sums))
    coupling = plane_couple(first, around[2:], rows, coupled)
    pulled = [plane_first(flags, sums, seen, seen_later, spec, mats)]

    slot_rows, slot_rows_other, mixes = [], [], []
    for k in range(3):
        values = [pulled[k]] + [moved(pulled[k], where) for where in SQUARE]
        mine, other, picked = plane_mix(first, coupling, metas, values)
        beside = moved(other, over_core)
        slot_rows.append(picked)
        slot_rows_other.append(beside)
        mixed = mine + beside[: hours + NOTE]
        sums = [mixed, moved(mixed, z_pair), moved(mixed, z_middle)]
        mixes.append(sums)
        if k == 0:
            following, now = plane_open(flags, sums, pulled[0], spec, mats)
        elif k == 1:
            note = mixed[hours:]
            two, mirror = moved(note, z_two), moved(note, z_mirror)
            open_note, following, state = plane_step(
                flags, sums, two, mirror, mixes[0], pulled[1], pulled[0], now, spec, mats
            )
        else:
            note = plane_close(flags, sums, pulled[2], state, spec, mats)
        pulled.append(following)
    close_note = lax.all_to_all(note, ("basin", "tm"), 0, 0, tiled=False)
    answer = moved(plane_combine(open_note, close_note, slot_rows, slot_rows_other), from_plane)
    return plane_finish(answer, incidence, first_guess)


def solution(mesh):
    planes = dict(mesh.shape) == {"basin": Z_ * X_, "tm": Y_ * C_}
    in_specs = (
        P("basin", None, None),
        P("basin"),
        P("basin"),
        P(),
        P("basin", "tm"),
        P("basin", "tm"),
    )
    return jax.shard_map(
        plane_shards if planes else shards, mesh=mesh, in_specs=in_specs, out_specs=P("basin", "tm"), check_vma=False
    )
```

```python
import functools

import jax
import jax.numpy as jnp
import numpy as np
from jax import lax
from jax.experimental import pallas as pl
from jax.experimental.pallas import tpu as pltpu
from jax.sharding import PartitionSpec as P

F32 = jnp.float32
BF16 = jnp.bfloat16
HIGH = lax.Precision.HIGHEST
SPAN = 256
MIB = 1024 * 1024


SMALL = pl.CostEstimate(flops=1, bytes_accessed=1, transcendentals=0)


def params(mib=16):
    return pltpu.CompilerParams(vmem_limit_bytes=mib * MIB)


def transforms():
    half = SPAN // 2
    freq = 2.0 * np.pi * (np.arange(half) + 0.5) / SPAN
    phase = np.arange(SPAN)[:, None] * freq[None, :]
    forward = np.concatenate([np.cos(phase), -np.sin(phase)], axis=1)
    inverse = forward.T * (2.0 / SPAN)
    return (
        jnp.asarray(forward, F32),
        jnp.asarray(inverse[:, :half], F32),
        jnp.asarray(inverse[:, half:], F32),
    )


def dot(a, b):
    return jnp.dot(a, b, preferred_element_type=F32)


def exact(a, b):
    return jnp.dot(a, b, precision=HIGH, preferred_element_type=F32)


def pieces(value, count):
    out = []
    for _ in range(count):
        piece = value.astype(BF16)
        out.append(piece)
        value = value - piece.astype(F32)
    return out


def pick(hot, value):
    return sum(dot(hot, piece) for piece in pieces(value, 3))


def prepare_kernel(inc_ref, field_ref, partial_ref, gram_ref):
    blocks, slots, width = inc_ref.shape
    rows = blocks * slots
    weights = inc_ref[...].astype(F32).astype(BF16)
    for b in range(blocks):
        value = field_ref[pl.ds(b * width, width), :]
        partial_ref[pl.ds(b * slots, slots), :] = pick(weights[b], value)
    flat = weights.reshape(rows, width)
    full = lax.dot_general(flat, flat, (((1,), (1,)), ((), ())), preferred_element_type=F32)
    row = lax.broadcasted_iota(jnp.int32, (rows, rows), 0)
    col = lax.broadcasted_iota(jnp.int32, (rows, rows), 1)
    own = jnp.where(row // slots == col // slots, full, 0.0)
    gram_ref[...] = jnp.sum(own.reshape(blocks, slots, rows), axis=0)


def prepare(incidence, field):
    blocks, slots, width = incidence.shape
    hours = field.shape[1]
    step = 8
    return pl.pallas_call(
        prepare_kernel,
        grid=(blocks // step,),
        in_specs=[
            pl.BlockSpec((step, slots, width), lambda i: (i, 0, 0)),
            pl.BlockSpec((step * width, hours), lambda i: (i, 0)),
        ],
        out_specs=[
            pl.BlockSpec((step * slots, hours), lambda i: (i, 0)),
            pl.BlockSpec((slots, step * slots), lambda i: (0, i)),
        ],
        out_shape=[
            jax.ShapeDtypeStruct((blocks * slots, hours), F32),
            jax.ShapeDtypeStruct((slots, blocks * slots), F32),
        ],
        compiler_params=params(56),
        name="prepare",
    )(incidence, field)


def table_kernel(gauge_ref, partial_ref, out_ref):
    slots = partial_ref.shape[0]
    rows = out_ref.shape[0]
    first = pl.program_id(0) * rows
    gauge = lax.broadcasted_iota(jnp.int32, (rows, slots), 0) + first
    hot = jnp.where(gauge_ref[...] == gauge, 1.0, 0.0).astype(BF16)
    out_ref[...] = pick(hot, partial_ref[...])


def table(row_gauge, partial, gauges):
    slots, hours = partial.shape
    step = 256
    return pl.pallas_call(
        table_kernel,
        grid=(gauges // step,),
        in_specs=[
            pl.BlockSpec((1, slots), lambda i: (0, 0)),
            pl.BlockSpec((slots, hours), lambda i: (0, 0)),
        ],
        out_specs=pl.BlockSpec((step, hours), lambda i: (i, 0)),
        out_shape=jax.ShapeDtypeStruct((gauges, hours), F32),
        compiler_params=params(56),
        name="table",
    )(row_gauge.reshape(1, slots), partial)


def couple_kernel(first_ref, lane_ref, sub_ref, gram_ref, high_ref, low_ref, near_ref):
    slots = gram_ref.shape[0]
    count = lane_ref.shape[1]
    rows, cols = high_ref.shape
    tile = 256
    first = first_ref[0]

    @pl.when(pl.program_id(0) == 0)
    def _():
        row = lax.broadcasted_iota(jnp.int32, (tile, tile), 0)
        col = lax.broadcasted_iota(jnp.int32, (tile, tile), 1)
        same = row // slots == col // slots
        mine = lax.broadcasted_iota(jnp.int32, (rows, tile), 0) + first

        def body(i, carry):
            here = pl.ds(pl.multiple_of(i * tile, tile), tile)
            block = jnp.concatenate([gram_ref[:, here]] * (tile // slots), axis=0)
            block = jnp.where(same, block, 0.0).astype(BF16)
            hot = jnp.where(lane_ref[:, here] == mine, 1.0, 0.0).astype(BF16)
            near_ref[:, here] = dot(hot, block)
            return carry

        lax.fori_loop(0, count // tile, body, 0)

    def chunk(i, total):
        here = pl.ds(pl.multiple_of(i * 1024, 1024), 1024)
        gauge = lax.broadcasted_iota(jnp.int32, (1024, cols), 1) + pl.program_id(0) * cols
        hot = jnp.where(sub_ref[here, :] == gauge, 1.0, 0.0).astype(BF16)
        near = near_ref[:, here]
        high = near.astype(BF16)
        low = (near - high.astype(F32)).astype(BF16)
        return total + dot(high, hot) + dot(low, hot)

    total = lax.fori_loop(0, count // 1024, chunk, jnp.zeros((rows, cols), F32))
    high, low = pieces(total, 2)
    high_ref[...] = high
    low_ref[...] = low


def couple(first, row_gauge, gram, rows, gauges):
    count = row_gauge.shape[0]
    step = 256
    return pl.pallas_call(
        couple_kernel,
        grid=(gauges // step,),
        in_specs=[
            pl.BlockSpec(memory_space=pltpu.SMEM),
            pl.BlockSpec((1, count), lambda i: (0, 0)),
            pl.BlockSpec((count, 1), lambda i: (0, 0)),
            pl.BlockSpec(gram.shape, lambda i: (0, 0)),
        ],
        out_specs=[pl.BlockSpec((rows, step), lambda i: (0, i))] * 2,
        out_shape=[jax.ShapeDtypeStruct((rows, gauges), BF16)] * 2,
        scratch_shapes=[pltpu.VMEM((rows, count), F32)],
        compiler_params=params(56),
        name="couple",
    )(first, row_gauge.reshape(1, count), row_gauge.reshape(count, 1), gram)


def mix_kernel(high_ref, low_ref, value_ref, out_ref):
    high = high_ref[...]
    low = low_ref[...]
    one, two, three = pieces(value_ref[...], 3)
    out_ref[...] = (dot(high, three) + dot(low, two)) + (dot(high, two) + dot(low, one)) + dot(high, one)


def mix(high, low, value):
    return pl.pallas_call(
        mix_kernel,
        out_shape=jax.ShapeDtypeStruct((high.shape[0], value.shape[1]), F32),
        compiler_params=params(56),
        name="mix",
    )(high, low, value)


def spectrum_kernel(class_ref, kernels_ref, forward_ref, out_ref):
    rows = class_ref.shape[0]
    classes, taps = kernels_ref.shape
    kind = lax.broadcasted_iota(jnp.int32, (rows, classes), 1)
    hot = jnp.where(class_ref[...] == kind, 1.0, 0.0)
    out_ref[...] = exact(exact(hot, kernels_ref[...]), forward_ref[pl.ds(0, taps), :])


def spectrum(gauge_kernel, kernels, forward):
    rows = gauge_kernel.shape[0]
    return pl.pallas_call(
        spectrum_kernel,
        out_shape=jax.ShapeDtypeStruct((rows, SPAN), F32),
        compiler_params=params(56),
        name="spectrum",
    )(gauge_kernel.reshape(rows, 1), kernels, forward)


def delayed(before, here, after, spec, forward, inverse_last):
    rows, half = here.shape
    stacked = jnp.concatenate(
        [jnp.concatenate([before, here], axis=1), jnp.concatenate([here, after], axis=1)], axis=0
    )
    waves = exact(stacked, forward)
    real, imag = waves[:, :half], waves[:, half:]
    kr = jnp.concatenate([spec[:, :half]] * 2, axis=0)
    ki = jnp.concatenate([spec[:, half:]] * 2, axis=0)
    turned = jnp.concatenate([real * kr - imag * ki, real * ki + imag * kr], axis=1)
    out = exact(turned, inverse_last)
    return out[:rows], out[rows:]


def advanced(here, after, spec, forward, inverse_first):
    half = here.shape[1]
    waves = exact(jnp.concatenate([here, after], axis=1), forward)
    real, imag = waves[:, :half], waves[:, half:]
    kr, ki = spec[:, :half], spec[:, half:]
    turned = jnp.concatenate([real * kr + imag * ki, imag * kr - real * ki], axis=1)
    return exact(turned, inverse_first)


def lanes(a, b):
    return jnp.sum(a * b, axis=0, keepdims=True)


def total(ref, row):
    return jnp.sum(ref[row : row + 1, :], axis=1, keepdims=True)


def ratios(ref):
    square = total(ref, 0)
    alpha = jnp.sqrt(square)
    beta = jnp.sqrt(jnp.maximum(total(ref, 1) / square - 2.0 * total(ref, 2) + square, 0.0))
    return alpha, beta


def first_kernel(
    more_ref, sums_ref, observed_ref, spec_ref, forward_ref, first_ref, last_ref, out_ref, note_ref
):
    rows, half = observed_ref.shape[0] // 2, observed_ref.shape[1]
    spec, forward = spec_ref[...], forward_ref[...]
    before, here, after = (sums_ref[pl.ds(i * rows, rows), :] for i in range(3))
    now, later = delayed(before, here, after, spec, forward, last_ref[...])
    start = observed_ref[pl.ds(0, rows), :] - now
    start_later = (observed_ref[pl.ds(rows, rows), :] - later) * more_ref[0]
    out_ref[...] = advanced(start, start_later, spec, forward, first_ref[...])
    note_ref[...] = jnp.concatenate([lanes(start, start), jnp.zeros((7, half), F32)], axis=0)


def first_step(more, sums, observed, spec, mats):
    rows, half = spec.shape[0], observed.shape[1]
    return pl.pallas_call(
        first_kernel,
        in_specs=[pl.BlockSpec(memory_space=pltpu.SMEM)] + [pl.BlockSpec(memory_space=pltpu.VMEM)] * 6,
        out_shape=[jax.ShapeDtypeStruct((rows, half), F32), jax.ShapeDtypeStruct((8, half), F32)],
        compiler_params=params(56),
        name="first_step",
    )(more, sums, observed, spec, *mats)


def step_kernel(
    opening,
    final,
    more_ref,
    note_ref,
    sums_ref,
    spec_ref,
    forward_ref,
    first_ref,
    last_ref,
    pulled_ref,
    *refs,
):
    if opening:
        state_ref = None
    else:
        state_ref, *refs = refs
    if final:
        (out_note_ref,) = refs
    else:
        new_ref, out_ref, out_note_ref = refs
    rows, half = pulled_ref.shape
    spec, forward = spec_ref[...], forward_ref[...]
    if opening:
        scale = 1.0 / jnp.sqrt(total(note_ref, 0))
        along = sums_ref[...] * scale
        new_s, new_su = along, along
        new_zu = pulled_ref[...] * scale
        new_z = new_zu
    else:
        alpha, beta = ratios(note_ref)
        a, b, g = 1.0 / (alpha * beta), alpha / beta, beta / alpha
        wide = pl.ds(0, 3 * rows), pl.ds(3 * rows, 3 * rows)
        new_su = sums_ref[...] * a - state_ref[wide[1], :] * b
        new_s = new_su - state_ref[wide[0], :] * g
        new_zu = pulled_ref[...] * a - state_ref[pl.ds(7 * rows, rows), :] * b
        new_z = new_zu - state_ref[pl.ds(6 * rows, rows), :] * g
    before, here, after = (new_s[i * rows : (i + 1) * rows] for i in range(3))
    now, later = delayed(before, here, after, spec, forward, last_ref[...])
    out_note_ref[...] = jnp.concatenate(
        [lanes(new_z, here), lanes(now, now), lanes(new_zu, here), jnp.zeros((5, half), F32)], axis=0
    )
    if not final:
        new_ref[pl.ds(0, 3 * rows), :] = new_s
        new_ref[pl.ds(3 * rows, 3 * rows), :] = new_su
        new_ref[pl.ds(6 * rows, rows), :] = new_z
        new_ref[pl.ds(7 * rows, rows), :] = new_zu
        out_ref[...] = advanced(now, later * more_ref[0], spec, forward, first_ref[...])


def next_step(more, note, sums, spec, mats, pulled, state, final):
    rows, half = pulled.shape
    opening = state is None
    shapes = [
        jax.ShapeDtypeStruct((8 * rows, half), F32),
        jax.ShapeDtypeStruct((rows, half), F32),
        jax.ShapeDtypeStruct((8, half), F32),
    ]
    args = [more, note, sums, spec, *mats, pulled] + ([] if opening else [state])
    return pl.pallas_call(
        functools.partial(step_kernel, opening, final),
        in_specs=[pl.BlockSpec(memory_space=pltpu.SMEM)]
        + [pl.BlockSpec(memory_space=pltpu.VMEM)] * (len(args) - 1),
        out_shape=shapes[2:] if final else shapes,
        compiler_params=params(56),
        name="next_step",
    )(*args)


def weights_of(notes):
    start = jnp.sqrt(total(notes[0], 0))
    zero = jnp.zeros_like(start)
    units = [1.0 / start, zero, zero]
    z, zu = list(units), list(units)
    phibar = start
    alpha, beta = ratios(notes[1])
    rhobar = alpha
    w = [value / alpha for value in z]
    result = [zero] * 3
    steps = len(notes) - 1
    for k in range(steps):
        rho = jnp.sqrt(rhobar * rhobar + beta * beta)
        cosine, sine = rhobar / rho, beta / rho
        phi, phibar = cosine * phibar, sine * phibar
        result = [r + phi / rho * value for r, value in zip(result, w)]
        if k < steps - 1:
            a, b, g = 1.0 / (alpha * beta), alpha / beta, beta / alpha
            zu = [(a if i == k + 1 else 0.0) - b * value for i, value in enumerate(zu)]
            z = [value - g * old for value, old in zip(zu, z)]
            alpha, beta = ratios(notes[k + 2])
            theta = sine * alpha
            rhobar = -cosine * alpha
            w = [value / alpha - theta / rho * old for value, old in zip(z, w)]
    return result


def finish_kernel(n0, n1, n2, n3, gauge_ref, q0, q1, q2, inc_ref, field_ref, out_ref, rows_ref):
    blocks, slots, width = inc_ref.shape
    count = rows_ref.shape[0]
    gauges = q0.shape[0]
    step = pl.program_id(0)

    @pl.when(step == 0)
    def _():
        e0, e1, e2 = weights_of([n0, n1, n2, n3])
        width_ = 512

        def body(i, value):
            here = pl.ds(pl.multiple_of(i * width_, width_), width_)
            mixed = q0[here, :] * e0 + q1[here, :] * e1 + q2[here, :] * e2
            gauge = lax.broadcasted_iota(jnp.int32, (count, width_), 1) + i * width_
            hot = jnp.where(gauge_ref[...] == gauge, 1.0, 0.0).astype(BF16)
            return value + pick(hot, mixed)

        rows_ref[...] = lax.fori_loop(0, gauges // width_, body, jnp.zeros(rows_ref.shape, F32))

    weights = inc_ref[...].astype(F32).astype(BF16)
    for b in range(blocks):
        here = pl.ds(b * width, width)
        rows = rows_ref[pl.ds(pl.multiple_of((step * blocks + b) * slots, slots), slots), :]
        added = sum(
            lax.dot_general(weights[b], piece, (((0,), (0,)), ((), ())), preferred_element_type=F32)
            for piece in pieces(rows, 3)
        )
        out_ref[here, :] = field_ref[here, :] + added


def finish(notes, row_gauge, gathered, incidence, field):
    blocks, slots, width = incidence.shape
    hours = field.shape[1]
    count = row_gauge.shape[0]
    step = 8
    whole = lambda shape: pl.BlockSpec(shape, lambda i: (0, 0))
    return pl.pallas_call(
        finish_kernel,
        grid=(blocks // step,),
        in_specs=[whole(n.shape) for n in notes]
        + [whole((count, 1))]
        + [whole(q.shape) for q in gathered]
        + [
            pl.BlockSpec((step, slots, width), lambda i: (i, 0, 0)),
            pl.BlockSpec((step * width, hours), lambda i: (i, 0)),
        ],
        out_specs=pl.BlockSpec((step * width, hours), lambda i: (i, 0)),
        out_shape=jax.ShapeDtypeStruct(field.shape, F32),
        scratch_shapes=[pltpu.VMEM((count, hours), F32)],
        compiler_params=params(56),
        name="finish",
    )(*notes, row_gauge.reshape(count, 1), *gathered, incidence, field)


def shifted(value, axis, by):
    devices = lax.axis_size(axis)
    pairs = [(i, i + by) for i in range(devices) if 0 <= i + by < devices]
    return lax.ppermute(value, axis, pairs)


def window(value):
    return jnp.concatenate([shifted(value, "tm", 1), value, shifted(value, "tm", -1)], axis=0)


def gathered_rows(value):
    owners = lax.axis_size("basin")
    copies = jnp.broadcast_to(value[None], (owners,) + value.shape)
    return lax.all_to_all(copies, "basin", 0, 0, tiled=False)


def over_hours(note):
    blocks = lax.axis_size("tm")
    result = note
    for by in range(1, blocks):
        result = result + lax.ppermute(note, "tm", [(i, (i + by) % blocks) for i in range(blocks)])
    return result


def shards(incidence, row_gauge, gauge_kernel, kernels, observed, first_guess):
    owners = lax.axis_size("basin")
    rows, hours = observed.shape
    gauges = rows * owners
    mats = transforms()
    spec = spectrum(gauge_kernel, kernels, mats[0])
    more = (lax.axis_index("tm") < lax.axis_size("tm") - 1).astype(F32).reshape(1)
    partial, gram = prepare(incidence, first_guess)
    all_gram = lax.all_gather(gram, "basin", axis=1, tiled=True)
    all_rows = lax.all_gather(row_gauge, "basin", axis=0, tiled=True)
    dense = table(row_gauge, partial, gauges).reshape(owners, rows, hours)
    sums = jnp.sum(lax.all_to_all(dense, "basin", 0, 0, tiled=False), axis=0)
    both = jnp.concatenate([observed, shifted(observed, "tm", -1)], axis=0)
    first = (lax.axis_index("basin") * rows).astype(jnp.int32).reshape(1)
    high, low = couple(first, all_rows, all_gram, rows, gauges)

    pulled, note = first_step(more, window(sums), both, spec, mats)
    notes, kept, state = [], [], None
    for k in range(3):
        everyone = gathered_rows(jnp.concatenate([pulled, note], axis=0))
        value = everyone[:, :rows].reshape(gauges, hours)
        notes.append(over_hours(jnp.sum(everyone[:, rows:], axis=0)))
        kept.append(value)
        around = window(mix(high, low, value))
        final = k == 2
        result = next_step(more, notes[-1], around, spec, mats, pulled, state, final)
        if final:
            (note,) = result
        else:
            state, pulled, note = result
    notes.append(over_hours(jnp.sum(gathered_rows(note), axis=0)))
    return finish(notes, row_gauge, kept, incidence, first_guess)


Z_, X_, Y_, C_ = 4, 2, 2, 2
NOTE = 8


def device(z, x, y, c):
    return (z * X_ + x) * (Y_ * C_) + y * C_ + c


def moved(value, where):
    pairs = []
    for z, x, y, c in np.ndindex(Z_, X_, Y_, C_):
        target = where(z, x, y, c)
        if target is not None:
            pairs.append((device(z, x, y, c), device(*target)))
    return lax.ppermute(value, ("basin", "tm"), pairs)


def to_plane(z, x, y, c):
    return 2 * y + c, x, z & 1, z >> 1


def to_plane_before(z, x, y, c):
    t = 2 * y + c
    return (t - 1, x, z & 1, z >> 1) if t else None


def from_plane(z, x, y, c):
    return 2 * c + y, x, z >> 1, z & 1


def over_x(z, x, y, c):
    return z, 1 - x, y, c


def over_y(z, x, y, c):
    return z, x, 1 - y, c


def over_xy(z, x, y, c):
    return z, 1 - x, 1 - y, c


def over_core(z, x, y, c):
    return z, x, y, 1 - c


def z_pair(z, x, y, c):
    return z ^ 1, x, y, c


def z_middle(z, x, y, c):
    return (3 - z, x, y, c) if z in (1, 2) else None


def z_two(z, x, y, c):
    return z ^ 2, x, y, c


def z_mirror(z, x, y, c):
    return 3 - z, x, y, c


def z_next(z, x, y, c):
    return (z + 1, x, y, c) if z < 3 else None


SQUARE = (over_x, over_y, over_xy)


def split_constant(value):
    out = []
    for _ in range(3):
        piece = value.astype(jnp.bfloat16)
        out.append(piece)
        value = value - piece.astype(np.float64)
    return out


ORDERS = {2: ((0, 1), (1, 0), (0, 0)), 3: ((0, 2), (1, 1), (2, 0), (0, 1), (1, 0), (0, 0))}


def widened(mat, order):
    parts = split_constant(mat)
    return jnp.asarray(np.concatenate([parts[i] for i, _ in ORDERS[order]], axis=1))


def product(wide, value, order):
    parts = pieces(value, order)
    return dot(wide, jnp.concatenate([parts[j] for _, j in ORDERS[order]], axis=0))


def turned_transforms(order):
    half = SPAN // 2
    freq = 2.0 * np.pi * (np.arange(half) + 0.5) / SPAN
    phase = freq[:, None] * np.arange(SPAN)[None, :]
    forward = np.concatenate([np.cos(phase), -np.sin(phase)], axis=0)
    inverse = forward.T * (2.0 / SPAN)
    return [widened(mat, order) for mat in (forward, inverse[:half], inverse[half:], forward[:, :half])]


def turn(waves, spec, sign):
    half = waves.shape[0] // 2
    real, imag = waves[:half], waves[half:]
    kr, ki = spec[:half], spec[half:] * sign
    return jnp.concatenate([real * kr - imag * ki, real * ki + imag * kr], axis=0)


def plane_delayed(before, here, after, spec, forward, last, order):
    rows = here.shape[1]
    pairs = [jnp.concatenate(pair, axis=0) for pair in ((before, here), (here, after))]
    waves = product(forward, jnp.concatenate(pairs, axis=1), order)
    turned = [turn(waves[:, i * rows : (i + 1) * rows], spec, 1.0) for i in range(2)]
    out = product(last, jnp.concatenate(turned, axis=1), order)
    return out[:, :rows], out[:, rows:]


def plane_advanced(here, after, spec, forward, first, order):
    waves = product(forward, jnp.concatenate([here, after], axis=0), order)
    return product(first, turn(waves, spec, -1.0), order)


def describe_kernel(inc_ref, gauge_ref, kind_ref, out_ref):
    blocks, slots, width = inc_ref.shape
    tile = 8
    rows = tile * slots
    weights = inc_ref[...].astype(F32).astype(BF16)
    row = lax.broadcasted_iota(jnp.int32, (rows, rows), 0)
    col = lax.broadcasted_iota(jnp.int32, (rows, rows), 1)
    same = row // slots == col // slots
    for i in range(blocks // tile):
        flat = weights[i * tile : (i + 1) * tile].reshape(rows, width)
        full = lax.dot_general(flat, flat, (((1,), (1,)), ((), ())), preferred_element_type=F32)
        own = jnp.where(same, full, 0.0)
        out_ref[pl.ds(0, slots), pl.ds(i * rows, rows)] = jnp.sum(own.reshape(tile, slots, rows), axis=0)
    kinds = kind_ref.shape[1]
    out_ref[pl.ds(slots, 8), :] = jnp.concatenate(
        [
            gauge_ref[...].astype(F32),
            jnp.concatenate(
                [kind_ref[...].astype(F32), jnp.zeros((1, blocks * slots - kinds), F32)], axis=1
            ),
            jnp.zeros((6, blocks * slots), F32),
        ],
        axis=0,
    )


def describe(incidence, row_gauge, gauge_kernel):
    blocks, slots, _ = incidence.shape
    count = blocks * slots
    return pl.pallas_call(
        describe_kernel,
        out_shape=jax.ShapeDtypeStruct((slots + 8, count), F32),
        compiler_params=params(),
        name="describe",
        cost_estimate=SMALL,
    )(incidence, row_gauge.reshape(1, count), gauge_kernel.reshape(1, gauge_kernel.shape[0]))


def send_kernel(inc_ref, field_ref, out_ref):
    blocks, slots, width = inc_ref.shape
    weights = inc_ref[...].astype(F32).astype(BF16)
    parts = []
    for b in range(blocks):
        value = jnp.concatenate(pieces(field_ref[pl.ds(b * width, width), :], 3)[::-1], axis=0)
        parts.append(dot(jnp.concatenate([weights[b]] * 3, axis=1), value))
    out_ref[...] = jnp.transpose(jnp.concatenate(parts, axis=0))


def send(incidence, field):
    blocks, slots, width = incidence.shape
    hours = field.shape[1]
    step = 8
    return pl.pallas_call(
        send_kernel,
        grid=(blocks // step,),
        in_specs=[
            pl.BlockSpec((step, slots, width), lambda i: (i, 0, 0)),
            pl.BlockSpec((step * width, hours), lambda i: (i, 0)),
        ],
        out_specs=pl.BlockSpec((hours, step * slots), lambda i: (0, i)),
        out_shape=jax.ShapeDtypeStruct((hours, blocks * slots), F32),
        compiler_params=params(),
        name="send",
        cost_estimate=SMALL,
    )(incidence, field)


def hot_rows(gauge, first, rows):
    mine = (lax.broadcasted_iota(jnp.int32, (rows, gauge.shape[1]), 0) + first).astype(F32)
    return jnp.where(gauge == mine, 1.0, 0.0).astype(BF16)


def spread_kernel(first_ref, mine_ref, other_ref, meta_ref, meta_other_ref, *out_refs):
    hours, rows = out_refs[0].shape
    where = meta_ref.shape[0] - 8
    value = jnp.concatenate([mine_ref[...], other_ref[...]], axis=1)
    gauge = jnp.concatenate([ref[where : where + 1, :] for ref in (meta_ref, meta_other_ref)], axis=1)
    stacked = jnp.concatenate(pieces(value, 3), axis=0)
    for m, out_ref in enumerate(out_refs):
        hot = hot_rows(gauge, first_ref[m], rows)
        result = lax.dot_general(stacked, hot, (((1,), (1,)), ((), ())), preferred_element_type=F32)
        out_ref[...] = (result[2 * hours :] + result[hours : 2 * hours]) + result[:hours]


def spread(first, parcels, metas, rows):
    hours = parcels[0].shape[0]
    return pl.pallas_call(
        spread_kernel,
        in_specs=[pl.BlockSpec(memory_space=pltpu.SMEM)] + [pl.BlockSpec(memory_space=pltpu.VMEM)] * 4,
        out_shape=[jax.ShapeDtypeStruct((hours, rows), F32)] * 4,
        compiler_params=params(),
        name="spread",
        cost_estimate=SMALL,
    )(first, *parcels, *metas)


def plane_couple_kernel(last, first_ref, *refs):
    if last:
        a_ref, b_ref, before_ref, high_ref, low_ref, total_ref, meta_ref = refs
        total_ref[...] = before_ref[...]
    else:
        a_ref, b_ref, total_ref, meta_ref = refs
        total_ref[...] = jnp.zeros_like(total_ref)
    height, double = a_ref.shape
    slots = height - 8
    count = double // 2
    cols, rows = total_ref.shape
    tile = 256
    for i, ref in enumerate((a_ref, b_ref)):
        for j in range(2):
            meta_ref[2 * i + j] = ref[:, j * count : (j + 1) * count]
    row = lax.broadcasted_iota(jnp.int32, (tile, tile), 0)
    col = lax.broadcasted_iota(jnp.int32, (tile, tile), 1)
    same = row // slots == col // slots

    def body(i, carry):
        gauge = meta_ref[i, slots : slots + 1, :]
        near = []
        for j in range(count // tile):
            here = slice(j * tile, (j + 1) * tile)
            block = jnp.concatenate([meta_ref[i, :slots, here]] * (tile // slots), axis=0)
            block = jnp.where(same, block, 0.0).astype(BF16)
            mine = jnp.concatenate(
                [hot_rows(gauge[:, here], first_ref[4 + h], rows // 2) for h in range(2)], axis=0
            )
            near.append(
                lax.dot_general(block, mine, (((1,), (1,)), ((), ())), preferred_element_type=F32)
            )
        near = jnp.concatenate(near, axis=0)
        high = near.astype(BF16)
        rest = near - high.astype(F32)
        hot = jnp.concatenate([hot_rows(gauge, first_ref[m], cols // 4) for m in range(4)], axis=0)
        total_ref[...] += dot(hot, high)

        @pl.when(jnp.max(jnp.abs(rest)) > 0.0)
        def _():
            total_ref[...] += dot(hot, rest.astype(BF16))

        return carry

    lax.fori_loop(0, 4, body, 0)
    if last:
        high, low = pieces(total_ref[...], 2)
        high_ref[...] = high
        low_ref[...] = low


def plane_couple(first, metas, rows, before=None):
    height, double = metas[0].shape
    shape = (4 * rows, 2 * rows)
    last = before is not None
    args = [first, *metas] + ([before] if last else [])
    scratch = [pltpu.VMEM((4, height, double // 2), F32)]
    return pl.pallas_call(
        functools.partial(plane_couple_kernel, last),
        in_specs=[pl.BlockSpec(memory_space=pltpu.SMEM)]
        + [pl.BlockSpec(memory_space=pltpu.VMEM)] * (len(args) - 1),
        out_shape=[jax.ShapeDtypeStruct(shape, BF16)] * 2 if last else jax.ShapeDtypeStruct(shape, F32),
        scratch_shapes=([pltpu.VMEM(shape, F32)] if last else []) + scratch,
        compiler_params=params(),
        name="plane_couple",
        cost_estimate=pl.CostEstimate(
            flops=2 * 2 * double * 8 * rows * rows, bytes_accessed=2_000_000, transcendentals=0
        ),
    )(*args)


def plane_mix_kernel(high_ref, low_ref, a_ref, b_ref, c_ref, d_ref, *refs):
    *extra, mine_ref, other_ref = refs
    refs = (a_ref, b_ref, c_ref, d_ref)
    height, rows = a_ref.shape
    hours = height - NOTE
    body, tail = pl.ds(0, hours), pl.ds(hours, NOTE)
    one, two = pieces(jnp.concatenate([ref[body, :] for ref in refs], axis=1), 2)
    both = dot(jnp.concatenate([two, one], axis=0), high_ref[...])
    result = (both[:hours] + dot(one, low_ref[...])) + both[hours:]
    note = sum(ref[tail, :] for ref in refs)
    mine_ref[body, :] = result[:, :rows]
    other_ref[body, :] = result[:, rows:]
    mine_ref[tail, :] = note
    other_ref[tail, :] = note
    for ref in extra:
        other_ref[pl.ds(height, ref.shape[0]), :] = ref[...]


def plane_mix(coupling, values, extra):
    height, rows = values[0].shape
    return pl.pallas_call(
        plane_mix_kernel,
        out_shape=[
            jax.ShapeDtypeStruct((height, rows), F32),
            jax.ShapeDtypeStruct((height + sum(value.shape[0] for value in extra), rows), F32),
        ],
        compiler_params=params(),
        name="plane_mix",
        cost_estimate=SMALL,
    )(*coupling, *values, *extra)


def plane_rows_kernel(first_ref, meta_ref, meta_other_ref, a_ref, b_ref, c_ref, d_ref, mine_ref, other_ref):
    refs = (a_ref, b_ref, c_ref, d_ref)
    height, rows = a_ref.shape
    hours = height - NOTE
    one, two = pieces(jnp.concatenate([ref[pl.ds(0, hours), :] for ref in refs], axis=1), 2)
    stacked = jnp.concatenate([two, one], axis=0)
    where = meta_ref.shape[0] - 8
    picked = []
    for ref in (meta_ref, meta_other_ref):
        gauge = ref[where : where + 1, :]
        hot = jnp.concatenate([hot_rows(gauge, first_ref[m], rows) for m in range(4)], axis=0)
        both = dot(stacked, hot)
        picked.append(both[:hours] + both[hours:])
    mine_ref[...] = picked[0]
    for i in range(picked[1].shape[1] // rows):
        other_ref[pl.ds(i * hours, hours), :] = picked[1][:, i * rows : (i + 1) * rows]


def plane_rows(first, metas, values):
    height, rows = values[0].shape
    hours = height - NOTE
    slots = metas[0].shape[1]
    return pl.pallas_call(
        plane_rows_kernel,
        in_specs=[pl.BlockSpec(memory_space=pltpu.SMEM)] + [pl.BlockSpec(memory_space=pltpu.VMEM)] * 6,
        out_shape=[
            jax.ShapeDtypeStruct((hours, slots), F32),
            jax.ShapeDtypeStruct((slots // rows * hours, rows), F32),
        ],
        compiler_params=params(),
        name="plane_rows",
        cost_estimate=pl.CostEstimate(flops=1_000_000_000, bytes_accessed=2_000_000, transcendentals=0),
    )(first, *metas, *values)


def plane_spectrum_kernel(class_ref, kernels_ref, wide_ref, out_ref):
    classes = kernels_ref.shape[0]
    where = class_ref.shape[0] - 7
    kind = class_ref[where : where + 1, : out_ref.shape[1]]
    hot = jnp.where(
        lax.broadcasted_iota(jnp.int32, (classes, kind.shape[1]), 0).astype(F32) == kind, 1.0, 0.0
    ).astype(BF16)
    chosen = None
    for piece in reversed(pieces(jnp.transpose(kernels_ref[...]), 3)):
        term = dot(piece, hot)
        chosen = term if chosen is None else chosen + term
    out_ref[...] = product(wide_ref[...], chosen, 3)


def plane_spectrum(meta, kernels, wide, rows):
    return pl.pallas_call(
        plane_spectrum_kernel,
        out_shape=jax.ShapeDtypeStruct((SPAN, rows), F32),
        compiler_params=params(),
        name="plane_spectrum",
        cost_estimate=SMALL,
    )(meta, kernels, wide)


def sides(even, pair, middle):
    return jnp.where(even, middle, pair), jnp.where(even, pair, middle)


def plane_first_kernel(flag_ref, here_ref, pair_ref, middle_ref, seen_ref, seen_later_ref, spec_ref, *refs):
    forward3, last3, forward, first, out_ref = refs
    hours, rows = here_ref.shape
    spec = spec_ref[...]
    before, after = sides(flag_ref[0] > 0.5, pair_ref[...], middle_ref[...])
    now, later = plane_delayed(before, here_ref[...], after, spec, forward3[...], last3[...], 3)
    start = jnp.transpose(seen_ref[...]) - now
    start_later = (jnp.transpose(seen_later_ref[...]) - later) * flag_ref[1]
    out_ref[pl.ds(0, hours), :] = plane_advanced(start, start_later, spec, forward[...], first[...], 2)
    out_ref[pl.ds(hours, NOTE), :] = jnp.concatenate(
        [lanes(start, start), jnp.zeros((NOTE - 1, rows), F32)], axis=0
    )


def plane_first(flags, sums, seen, seen_later, spec, mats):
    hours, rows = sums[0].shape
    args = [flags, *sums, seen, seen_later, spec, *mats]
    return pl.pallas_call(
        plane_first_kernel,
        in_specs=[pl.BlockSpec(memory_space=pltpu.SMEM)]
        + [pl.BlockSpec(memory_space=pltpu.VMEM)] * (len(args) - 1),
        out_shape=jax.ShapeDtypeStruct((hours + NOTE, rows), F32),
        compiler_params=params(),
        name="plane_first",
        cost_estimate=SMALL,
    )(*args)


def plane_open_kernel(flag_ref, here_ref, pair_ref, middle_ref, pulled_ref, spec_ref, *refs):
    forward, first, last, out_ref, now_ref = refs
    height, rows = pulled_ref.shape
    hours = height - NOTE
    tail, body = pl.ds(hours, NOTE), pl.ds(0, hours)
    spec = spec_ref[...]
    here = here_ref[body, :]
    before, after = sides(flag_ref[0] > 0.5, pair_ref[body, :], middle_ref[body, :])
    now, later = plane_delayed(before, here, after, spec, forward[...], last[...], 2)
    out_ref[body, :] = plane_advanced(now, later * flag_ref[1], spec, forward[...], first[...], 2)
    out_ref[tail, :] = jnp.concatenate(
        [
            lanes(pulled_ref[body, :], here),
            lanes(now, now),
            pulled_ref[hours : hours + 1, :],
            jnp.zeros((NOTE - 3, rows), F32),
        ],
        axis=0,
    )
    now_ref[...] = now


def plane_open(flags, sums, pulled, spec, mats):
    height, rows = pulled.shape
    args = [flags, *sums, pulled, spec, *mats]
    return pl.pallas_call(
        plane_open_kernel,
        in_specs=[pl.BlockSpec(memory_space=pltpu.SMEM)]
        + [pl.BlockSpec(memory_space=pltpu.VMEM)] * (len(args) - 1),
        out_shape=[
            jax.ShapeDtypeStruct((height, rows), F32),
            jax.ShapeDtypeStruct((height - NOTE, rows), F32),
        ],
        compiler_params=params(),
        name="plane_open",
        cost_estimate=SMALL,
    )(*args)


def opening(ref):
    start = total(ref, 2)
    square = total(ref, 0) / start
    alpha = jnp.sqrt(square)
    beta = jnp.sqrt(jnp.maximum(total(ref, 1) / total(ref, 0) - square, 0.0))
    return 1.0 / jnp.sqrt(start), alpha, beta


def plane_step_kernel(flag_ref, here_ref, pair_ref, mirror_ref, two_ref, *refs):
    old_refs, (pulled_ref, old_z_ref, old_now_ref, spec_ref), refs = refs[:3], refs[3:7], refs[7:]
    forward, first, last, total_ref, out_ref, kept_ref = refs
    height, rows = pulled_ref.shape
    hours = height - NOTE
    tail, body = pl.ds(hours, NOTE), pl.ds(0, hours)
    total_ref[...] = (here_ref[tail, :] + pair_ref[tail, :]) + (two_ref[...] + mirror_ref[tail, :])
    scale, alpha, beta = opening(total_ref)
    a, b, g = scale / (alpha * beta), scale * alpha / beta, scale * beta / alpha
    spec = spec_ref[...]
    s, su = [], []
    for ref, old_ref in zip((here_ref, pair_ref, mirror_ref), old_refs):
        old = old_ref[body, :]
        new = ref[body, :] * flag_ref[2] if ref is mirror_ref else ref[body, :]
        su.append(new * a - old * b)
        s.append(su[-1] - old * g)
    zu = pulled_ref[body, :] * a - old_z_ref[body, :] * b
    z = zu - old_z_ref[body, :] * g
    before, after = sides(flag_ref[0] > 0.5, s[1], s[2])
    now, later = plane_delayed(before, s[0], after, spec, forward[...], last[...], 2)
    out_ref[body, :] = plane_advanced(now, later * flag_ref[1], spec, forward[...], first[...], 2)
    out_ref[tail, :] = jnp.concatenate(
        [lanes(z, s[0]), lanes(now, now), lanes(zu, s[0]), jnp.zeros((NOTE - 3, rows), F32)], axis=0
    )
    for i, value in enumerate((s[0], su[0], z, zu, now, now + old_now_ref[...] * g)):
        kept_ref[pl.ds(i * hours, hours), :] = value


def plane_step(flags, sums, two, old, pulled, old_z, old_now, spec, mats):
    height, rows = pulled.shape
    args = [flags, *sums, two, *old, pulled, old_z, old_now, spec, *mats]
    return pl.pallas_call(
        plane_step_kernel,
        in_specs=[pl.BlockSpec(memory_space=pltpu.SMEM)]
        + [pl.BlockSpec(memory_space=pltpu.VMEM)] * (len(args) - 1),
        out_shape=[
            jax.ShapeDtypeStruct((NOTE, rows), F32),
            jax.ShapeDtypeStruct((height, rows), F32),
            jax.ShapeDtypeStruct((6 * (height - NOTE), rows), F32),
        ],
        compiler_params=params(),
        name="plane_step",
        cost_estimate=SMALL,
    )(*args)


def plane_close_kernel(here_ref, before_ref, pulled_ref, kept_ref, spec_ref, forward, last, out_ref):
    height, rows = pulled_ref.shape
    hours = height - NOTE
    body = pl.ds(0, hours)
    here = here_ref[body, :]
    waves = product(forward[...], jnp.concatenate([before_ref[body, :], here], axis=0), 2)
    now = product(last[...], turn(waves, spec_ref[...], 1.0), 2)
    s, su, z, zu, old_now, old_now_u = (kept_ref[pl.ds(i * hours, hours), :] for i in range(6))
    raw = pulled_ref[body, :]
    note = [pulled_ref[hours + i : hours + i + 1, :] for i in range(3)]
    for left in (raw, zu, z):
        note += [lanes(left, right) for right in (here, su, s)]
    parts = (now, old_now_u, old_now)
    for i in range(3):
        note += [lanes(parts[i], parts[j]) for j in range(i, 3)]
    note.append(jnp.zeros((24 - len(note), rows), F32))
    note = jnp.sum(jnp.concatenate(note, axis=0), axis=1, keepdims=True)
    shape = (24, out_ref.shape[2])
    row, col = (lax.broadcasted_iota(jnp.int32, shape, i) for i in range(2))
    note = jnp.sum(jnp.where(row == col, jnp.broadcast_to(note, shape), 0.0), axis=0, keepdims=True)
    out_ref[...] = jnp.broadcast_to(note[None], out_ref.shape)


def plane_close(sums, pulled, kept, spec, mats):
    rows = pulled.shape[1]
    return pl.pallas_call(
        plane_close_kernel,
        out_shape=jax.ShapeDtypeStruct((Z_ * X_ * Y_ * C_, 8, rows // 2), F32),
        compiler_params=params(),
        name="plane_close",
        cost_estimate=SMALL,
    )(*sums, pulled, kept, spec, *mats)


def plane_weights(open_ref, close):
    scale, alpha, beta = opening(open_ref)
    start = 1.0 / scale
    phibar, rhobar = start, alpha
    zero = jnp.zeros_like(start)
    z = zu = [scale, zero, zero]
    w = [value / alpha for value in z]
    result = [zero] * 3
    for k in range(3):
        rho = jnp.sqrt(rhobar * rhobar + beta * beta)
        cosine, sine = rhobar / rho, beta / rho
        phi, phibar = cosine * phibar, sine * phibar
        result = [r + phi / rho * value for r, value in zip(result, w)]
        if k == 2:
            return result
        a, b, g = 1.0 / (alpha * beta), alpha / beta, beta / alpha
        zu = [-b * value for value in zu]
        zu[k + 1] = zu[k + 1] + (a * scale if k == 0 else a)
        z = [value - g * old for value, old in zip(zu, z)]
        if k == 0:
            square, norm, along = (close[:, i : i + 1] for i in range(3))
        else:
            plain = (a, -b, -g)
            cross = [[close[:, 3 + 3 * i + j : 4 + 3 * i + j] for j in range(3)] for i in range(3)]
            along = sum(plain[i] * plain[j] * cross[i][j] for i in range(2) for j in range(3))
            square = along + sum(plain[2] * plain[j] * cross[2][j] for j in range(3))
            pairs = [(i, j) for i in range(3) for j in range(i, 3)]
            norm = sum(
                plain[i] * plain[j] * close[:, 12 + n : 13 + n] * (1.0 if i == j else 2.0)
                for n, (i, j) in enumerate(pairs)
            )
        alpha = jnp.sqrt(square)
        beta = jnp.sqrt(jnp.maximum(norm / square - 2.0 * along + square, 0.0))
        theta = sine * alpha
        rhobar = -cosine * alpha
        w = [value / alpha - theta / rho * old for value, old in zip(z, w)]


def plane_combine_kernel(open_ref, close_ref, *refs):
    *parts, out_ref = refs
    hours, rows = out_ref.shape[1], open_ref.shape[1]
    close = jnp.sum(close_ref[...], axis=0)[0:1, :]
    weights = plane_weights(open_ref, close)
    mine = sum(ref[...] * e for ref, e in zip(parts[:3], weights))
    count = mine.shape[1] // rows
    for i in range(count):
        other = 0.0
        for ref, e in zip(parts[3:], weights):
            other = other + ref[pl.ds(ref.shape[0] - (count - i) * hours, hours), :] * e
        out_ref[pl.ds(i * rows, rows), :] = jnp.transpose(mine[:, i * rows : (i + 1) * rows] + other)


def plane_combine(open_note, close_note, mine, other):
    hours, slots = mine[0].shape
    return pl.pallas_call(
        plane_combine_kernel,
        out_shape=jax.ShapeDtypeStruct((slots, hours), F32),
        compiler_params=params(),
        name="plane_combine",
        cost_estimate=SMALL,
    )(open_note, close_note, *mine, *other)


def plane_finish_kernel(rows_ref, inc_ref, field_ref, out_ref):
    blocks, slots, width = inc_ref.shape
    weights = inc_ref[...].astype(F32).astype(BF16)
    for b in range(blocks):
        here = pl.ds(b * width, width)
        rows = jnp.concatenate(pieces(rows_ref[pl.ds(b * slots, slots), :], 2), axis=0)
        twice = jnp.concatenate([weights[b]] * 2, axis=0)
        added = lax.dot_general(twice, rows, (((0,), (0,)), ((), ())), preferred_element_type=F32)
        out_ref[here, :] = field_ref[here, :] + added


def plane_finish(rows, incidence, field):
    blocks, slots, width = incidence.shape
    hours = field.shape[1]
    step = 8
    return pl.pallas_call(
        plane_finish_kernel,
        grid=(blocks // step,),
        in_specs=[
            pl.BlockSpec((step * slots, hours), lambda i: (i, 0)),
            pl.BlockSpec((step, slots, width), lambda i: (i, 0, 0)),
            pl.BlockSpec((step * width, hours), lambda i: (i, 0)),
        ],
        out_specs=pl.BlockSpec((step * width, hours), lambda i: (i, 0)),
        out_shape=jax.ShapeDtypeStruct(field.shape, F32),
        compiler_params=params(),
        name="plane_finish",
    )(rows, incidence, field)


def plane_shards(incidence, row_gauge, gauge_kernel, kernels, observed, first_guess):
    rows, hours = observed.shape
    basin, tm = lax.axis_index("basin"), lax.axis_index("tm")
    z, x, y, c = basin // X_, basin % X_, tm // C_, tm % C_
    place = 2 * y + x
    first = jnp.stack([4 * c + (place ^ m) for m in range(4)] + [4 * c + place, 4 * (1 - c) + place])
    first = (first * rows).astype(jnp.int32)
    flags = jnp.stack([1 - z % 2, (z < Z_ - 1).astype(z.dtype), (z > 0).astype(z.dtype)]).astype(F32)
    forward, inverse_first, inverse_last, _ = turned_transforms(2)
    forward3, _, inverse_last3, short3 = turned_transforms(3)
    mats = [forward, inverse_first, inverse_last]

    meta = describe(incidence, row_gauge, gauge_kernel)
    meta, field = lax.optimization_barrier((meta, first_guess))
    meta = moved(meta, to_plane)
    parcel = moved(send(incidence, field), to_plane)
    metas = [meta, moved(meta, over_core)]
    both = jnp.concatenate(metas, axis=1)
    around = [both] + [moved(both, where) for where in SQUARE]
    spec = plane_spectrum(meta, kernels, short3, rows)
    seen, parcel, around, spec = lax.optimization_barrier((observed, parcel, around, spec))
    seen_later = moved(seen, to_plane_before)
    seen = moved(seen, to_plane)

    dense = spread(first, [parcel, moved(parcel, over_core)], metas, rows)
    sums = dense[0] + sum(moved(value, where) for value, where in zip(dense[1:], SQUARE))
    sums = [sums, moved(sums, z_pair), moved(sums, z_middle)]
    coupled = plane_couple(first, around[:2], rows)
    coupled, sums = lax.optimization_barrier((coupled, sums))
    coupling = plane_couple(first, around[2:], rows, coupled)
    pulled = [
        plane_first(
            flags, sums, seen, seen_later, spec, [forward3, inverse_last3, forward, inverse_first]
        )
    ]

    mine_rows, other_rows, extra, mixes = [], [], [], []
    for k in range(3):
        values = [pulled[k]] + [moved(pulled[k], where) for where in SQUARE]
        mine, other = plane_mix(coupling, values, extra)
        beside = moved(other, over_core)
        mixed = mine + beside[: hours + NOTE]
        if k:
            other_rows.append(beside)
        picked, theirs = plane_rows(first, metas, values)
        mine_rows.append(picked)
        extra = [theirs]
        if k == 0:
            mixes = [mixed, moved(mixed, z_pair), moved(mixed, z_middle)]
            following, now = plane_open(flags, mixes, pulled[0], spec, mats)
        elif k == 1:
            sums = [mixed, moved(mixed, z_pair), moved(mixed, z_mirror)]
            two = moved(mixed[hours:], z_two)
            open_note, following, state = plane_step(
                flags, sums, two, mixes, pulled[1], pulled[0], now, spec, mats
            )
        else:
            sums = [mixed, moved(mixed, z_next)]
            note = plane_close(sums, pulled[2], state, spec, [forward, inverse_last])
            other_rows.append(moved(theirs, over_core))
        pulled.append(following)
    close_note = lax.all_to_all(note, ("basin", "tm"), 0, 0, tiled=False)
    answer = moved(plane_combine(open_note, close_note, mine_rows, other_rows), from_plane)
    return plane_finish(answer, incidence, first_guess)


def solution(mesh):
    planes = dict(mesh.shape) == {"basin": Z_ * X_, "tm": Y_ * C_}
    in_specs = (
        P("basin", None, None),
        P("basin"),
        P("basin"),
        P(),
        P("basin", "tm"),
        P("basin", "tm"),
    )
    return jax.shard_map(
        plane_shards if planes else shards, mesh=mesh, in_specs=in_specs, out_specs=P("basin", "tm"), check_vma=False
    )
```

```python
import functools

import jax
import jax.numpy as jnp
import numpy as np
from jax import lax
from jax.experimental import pallas as pl
from jax.experimental.pallas import tpu as pltpu
from jax.sharding import PartitionSpec as P

F32 = jnp.float32
BF16 = jnp.bfloat16
HIGH = lax.Precision.HIGHEST
SPAN = 256
MIB = 1024 * 1024


SMALL = pl.CostEstimate(flops=1, bytes_accessed=1, transcendentals=0)


def params(mib=16):
    return pltpu.CompilerParams(vmem_limit_bytes=mib * MIB)


def transforms():
    half = SPAN // 2
    freq = 2.0 * np.pi * (np.arange(half) + 0.5) / SPAN
    phase = np.arange(SPAN)[:, None] * freq[None, :]
    forward = np.concatenate([np.cos(phase), -np.sin(phase)], axis=1)
    inverse = forward.T * (2.0 / SPAN)
    return (
        jnp.asarray(forward, F32),
        jnp.asarray(inverse[:, :half], F32),
        jnp.asarray(inverse[:, half:], F32),
    )


def dot(a, b):
    return jnp.dot(a, b, preferred_element_type=F32)


def exact(a, b):
    return jnp.dot(a, b, precision=HIGH, preferred_element_type=F32)


def pieces(value, count):
    out = []
    for _ in range(count):
        piece = value.astype(BF16)
        out.append(piece)
        value = value - piece.astype(F32)
    return out


def pick(hot, value):
    return sum(dot(hot, piece) for piece in pieces(value, 3))


def prepare_kernel(inc_ref, field_ref, partial_ref, gram_ref):
    blocks, slots, width = inc_ref.shape
    rows = blocks * slots
    weights = inc_ref[...].astype(F32).astype(BF16)
    for b in range(blocks):
        value = field_ref[pl.ds(b * width, width), :]
        partial_ref[pl.ds(b * slots, slots), :] = pick(weights[b], value)
    flat = weights.reshape(rows, width)
    full = lax.dot_general(flat, flat, (((1,), (1,)), ((), ())), preferred_element_type=F32)
    row = lax.broadcasted_iota(jnp.int32, (rows, rows), 0)
    col = lax.broadcasted_iota(jnp.int32, (rows, rows), 1)
    own = jnp.where(row // slots == col // slots, full, 0.0)
    gram_ref[...] = jnp.sum(own.reshape(blocks, slots, rows), axis=0)


def prepare(incidence, field):
    blocks, slots, width = incidence.shape
    hours = field.shape[1]
    step = 8
    return pl.pallas_call(
        prepare_kernel,
        grid=(blocks // step,),
        in_specs=[
            pl.BlockSpec((step, slots, width), lambda i: (i, 0, 0)),
            pl.BlockSpec((step * width, hours), lambda i: (i, 0)),
        ],
        out_specs=[
            pl.BlockSpec((step * slots, hours), lambda i: (i, 0)),
            pl.BlockSpec((slots, step * slots), lambda i: (0, i)),
        ],
        out_shape=[
            jax.ShapeDtypeStruct((blocks * slots, hours), F32),
            jax.ShapeDtypeStruct((slots, blocks * slots), F32),
        ],
        compiler_params=params(56),
        name="prepare",
    )(incidence, field)


def table_kernel(gauge_ref, partial_ref, out_ref):
    slots = partial_ref.shape[0]
    rows = out_ref.shape[0]
    first = pl.program_id(0) * rows
    gauge = lax.broadcasted_iota(jnp.int32, (rows, slots), 0) + first
    hot = jnp.where(gauge_ref[...] == gauge, 1.0, 0.0).astype(BF16)
    out_ref[...] = pick(hot, partial_ref[...])


def table(row_gauge, partial, gauges):
    slots, hours = partial.shape
    step = 256
    return pl.pallas_call(
        table_kernel,
        grid=(gauges // step,),
        in_specs=[
            pl.BlockSpec((1, slots), lambda i: (0, 0)),
            pl.BlockSpec((slots, hours), lambda i: (0, 0)),
        ],
        out_specs=pl.BlockSpec((step, hours), lambda i: (i, 0)),
        out_shape=jax.ShapeDtypeStruct((gauges, hours), F32),
        compiler_params=params(56),
        name="table",
    )(row_gauge.reshape(1, slots), partial)


def couple_kernel(first_ref, lane_ref, sub_ref, gram_ref, high_ref, low_ref, near_ref):
    slots = gram_ref.shape[0]
    count = lane_ref.shape[1]
    rows, cols = high_ref.shape
    tile = 256
    first = first_ref[0]

    @pl.when(pl.program_id(0) == 0)
    def _():
        row = lax.broadcasted_iota(jnp.int32, (tile, tile), 0)
        col = lax.broadcasted_iota(jnp.int32, (tile, tile), 1)
        same = row // slots == col // slots
        mine = lax.broadcasted_iota(jnp.int32, (rows, tile), 0) + first

        def body(i, carry):
            here = pl.ds(pl.multiple_of(i * tile, tile), tile)
            block = jnp.concatenate([gram_ref[:, here]] * (tile // slots), axis=0)
            block = jnp.where(same, block, 0.0).astype(BF16)
            hot = jnp.where(lane_ref[:, here] == mine, 1.0, 0.0).astype(BF16)
            near_ref[:, here] = dot(hot, block)
            return carry

        lax.fori_loop(0, count // tile, body, 0)

    def chunk(i, total):
        here = pl.ds(pl.multiple_of(i * 1024, 1024), 1024)
        gauge = lax.broadcasted_iota(jnp.int32, (1024, cols), 1) + pl.program_id(0) * cols
        hot = jnp.where(sub_ref[here, :] == gauge, 1.0, 0.0).astype(BF16)
        near = near_ref[:, here]
        high = near.astype(BF16)
        low = (near - high.astype(F32)).astype(BF16)
        return total + dot(high, hot) + dot(low, hot)

    total = lax.fori_loop(0, count // 1024, chunk, jnp.zeros((rows, cols), F32))
    high, low = pieces(total, 2)
    high_ref[...] = high
    low_ref[...] = low


def couple(first, row_gauge, gram, rows, gauges):
    count = row_gauge.shape[0]
    step = 256
    return pl.pallas_call(
        couple_kernel,
        grid=(gauges // step,),
        in_specs=[
            pl.BlockSpec(memory_space=pltpu.SMEM),
            pl.BlockSpec((1, count), lambda i: (0, 0)),
            pl.BlockSpec((count, 1), lambda i: (0, 0)),
            pl.BlockSpec(gram.shape, lambda i: (0, 0)),
        ],
        out_specs=[pl.BlockSpec((rows, step), lambda i: (0, i))] * 2,
        out_shape=[jax.ShapeDtypeStruct((rows, gauges), BF16)] * 2,
        scratch_shapes=[pltpu.VMEM((rows, count), F32)],
        compiler_params=params(56),
        name="couple",
    )(first, row_gauge.reshape(1, count), row_gauge.reshape(count, 1), gram)


def mix_kernel(high_ref, low_ref, value_ref, out_ref):
    high = high_ref[...]
    low = low_ref[...]
    one, two, three = pieces(value_ref[...], 3)
    out_ref[...] = (dot(high, three) + dot(low, two)) + (dot(high, two) + dot(low, one)) + dot(high, one)


def mix(high, low, value):
    return pl.pallas_call(
        mix_kernel,
        out_shape=jax.ShapeDtypeStruct((high.shape[0], value.shape[1]), F32),
        compiler_params=params(56),
        name="mix",
    )(high, low, value)


def spectrum_kernel(class_ref, kernels_ref, forward_ref, out_ref):
    rows = class_ref.shape[0]
    classes, taps = kernels_ref.shape
    kind = lax.broadcasted_iota(jnp.int32, (rows, classes), 1)
    hot = jnp.where(class_ref[...] == kind, 1.0, 0.0)
    out_ref[...] = exact(exact(hot, kernels_ref[...]), forward_ref[pl.ds(0, taps), :])


def spectrum(gauge_kernel, kernels, forward):
    rows = gauge_kernel.shape[0]
    return pl.pallas_call(
        spectrum_kernel,
        out_shape=jax.ShapeDtypeStruct((rows, SPAN), F32),
        compiler_params=params(56),
        name="spectrum",
    )(gauge_kernel.reshape(rows, 1), kernels, forward)


def delayed(before, here, after, spec, forward, inverse_last):
    rows, half = here.shape
    stacked = jnp.concatenate(
        [jnp.concatenate([before, here], axis=1), jnp.concatenate([here, after], axis=1)], axis=0
    )
    waves = exact(stacked, forward)
    real, imag = waves[:, :half], waves[:, half:]
    kr = jnp.concatenate([spec[:, :half]] * 2, axis=0)
    ki = jnp.concatenate([spec[:, half:]] * 2, axis=0)
    turned = jnp.concatenate([real * kr - imag * ki, real * ki + imag * kr], axis=1)
    out = exact(turned, inverse_last)
    return out[:rows], out[rows:]


def advanced(here, after, spec, forward, inverse_first):
    half = here.shape[1]
    waves = exact(jnp.concatenate([here, after], axis=1), forward)
    real, imag = waves[:, :half], waves[:, half:]
    kr, ki = spec[:, :half], spec[:, half:]
    turned = jnp.concatenate([real * kr + imag * ki, imag * kr - real * ki], axis=1)
    return exact(turned, inverse_first)


def lanes(a, b):
    return jnp.sum(a * b, axis=0, keepdims=True)


def total(ref, row):
    return jnp.sum(ref[row : row + 1, :], axis=1, keepdims=True)


def ratios(ref):
    square = total(ref, 0)
    alpha = jnp.sqrt(square)
    beta = jnp.sqrt(jnp.maximum(total(ref, 1) / square - 2.0 * total(ref, 2) + square, 0.0))
    return alpha, beta


def first_kernel(
    more_ref, sums_ref, observed_ref, spec_ref, forward_ref, first_ref, last_ref, out_ref, note_ref
):
    rows, half = observed_ref.shape[0] // 2, observed_ref.shape[1]
    spec, forward = spec_ref[...], forward_ref[...]
    before, here, after = (sums_ref[pl.ds(i * rows, rows), :] for i in range(3))
    now, later = delayed(before, here, after, spec, forward, last_ref[...])
    start = observed_ref[pl.ds(0, rows), :] - now
    start_later = (observed_ref[pl.ds(rows, rows), :] - later) * more_ref[0]
    out_ref[...] = advanced(start, start_later, spec, forward, first_ref[...])
    note_ref[...] = jnp.concatenate([lanes(start, start), jnp.zeros((7, half), F32)], axis=0)


def first_step(more, sums, observed, spec, mats):
    rows, half = spec.shape[0], observed.shape[1]
    return pl.pallas_call(
        first_kernel,
        in_specs=[pl.BlockSpec(memory_space=pltpu.SMEM)] + [pl.BlockSpec(memory_space=pltpu.VMEM)] * 6,
        out_shape=[jax.ShapeDtypeStruct((rows, half), F32), jax.ShapeDtypeStruct((8, half), F32)],
        compiler_params=params(56),
        name="first_step",
    )(more, sums, observed, spec, *mats)


def step_kernel(
    opening,
    final,
    more_ref,
    note_ref,
    sums_ref,
    spec_ref,
    forward_ref,
    first_ref,
    last_ref,
    pulled_ref,
    *refs,
):
    if opening:
        state_ref = None
    else:
        state_ref, *refs = refs
    if final:
        (out_note_ref,) = refs
    else:
        new_ref, out_ref, out_note_ref = refs
    rows, half = pulled_ref.shape
    spec, forward = spec_ref[...], forward_ref[...]
    if opening:
        scale = 1.0 / jnp.sqrt(total(note_ref, 0))
        along = sums_ref[...] * scale
        new_s, new_su = along, along
        new_zu = pulled_ref[...] * scale
        new_z = new_zu
    else:
        alpha, beta = ratios(note_ref)
        a, b, g = 1.0 / (alpha * beta), alpha / beta, beta / alpha
        wide = pl.ds(0, 3 * rows), pl.ds(3 * rows, 3 * rows)
        new_su = sums_ref[...] * a - state_ref[wide[1], :] * b
        new_s = new_su - state_ref[wide[0], :] * g
        new_zu = pulled_ref[...] * a - state_ref[pl.ds(7 * rows, rows), :] * b
        new_z = new_zu - state_ref[pl.ds(6 * rows, rows), :] * g
    before, here, after = (new_s[i * rows : (i + 1) * rows] for i in range(3))
    now, later = delayed(before, here, after, spec, forward, last_ref[...])
    out_note_ref[...] = jnp.concatenate(
        [lanes(new_z, here), lanes(now, now), lanes(new_zu, here), jnp.zeros((5, half), F32)], axis=0
    )
    if not final:
        new_ref[pl.ds(0, 3 * rows), :] = new_s
        new_ref[pl.ds(3 * rows, 3 * rows), :] = new_su
        new_ref[pl.ds(6 * rows, rows), :] = new_z
        new_ref[pl.ds(7 * rows, rows), :] = new_zu
        out_ref[...] = advanced(now, later * more_ref[0], spec, forward, first_ref[...])


def next_step(more, note, sums, spec, mats, pulled, state, final):
    rows, half = pulled.shape
    opening = state is None
    shapes = [
        jax.ShapeDtypeStruct((8 * rows, half), F32),
        jax.ShapeDtypeStruct((rows, half), F32),
        jax.ShapeDtypeStruct((8, half), F32),
    ]
    args = [more, note, sums, spec, *mats, pulled] + ([] if opening else [state])
    return pl.pallas_call(
        functools.partial(step_kernel, opening, final),
        in_specs=[pl.BlockSpec(memory_space=pltpu.SMEM)]
        + [pl.BlockSpec(memory_space=pltpu.VMEM)] * (len(args) - 1),
        out_shape=shapes[2:] if final else shapes,
        compiler_params=params(56),
        name="next_step",
    )(*args)


def weights_of(notes):
    start = jnp.sqrt(total(notes[0], 0))
    zero = jnp.zeros_like(start)
    units = [1.0 / start, zero, zero]
    z, zu = list(units), list(units)
    phibar = start
    alpha, beta = ratios(notes[1])
    rhobar = alpha
    w = [value / alpha for value in z]
    result = [zero] * 3
    steps = len(notes) - 1
    for k in range(steps):
        rho = jnp.sqrt(rhobar * rhobar + beta * beta)
        cosine, sine = rhobar / rho, beta / rho
        phi, phibar = cosine * phibar, sine * phibar
        result = [r + phi / rho * value for r, value in zip(result, w)]
        if k < steps - 1:
            a, b, g = 1.0 / (alpha * beta), alpha / beta, beta / alpha
            zu = [(a if i == k + 1 else 0.0) - b * value for i, value in enumerate(zu)]
            z = [value - g * old for value, old in zip(zu, z)]
            alpha, beta = ratios(notes[k + 2])
            theta = sine * alpha
            rhobar = -cosine * alpha
            w = [value / alpha - theta / rho * old for value, old in zip(z, w)]
    return result


def finish_kernel(n0, n1, n2, n3, gauge_ref, q0, q1, q2, inc_ref, field_ref, out_ref, rows_ref):
    blocks, slots, width = inc_ref.shape
    count = rows_ref.shape[0]
    gauges = q0.shape[0]
    step = pl.program_id(0)

    @pl.when(step == 0)
    def _():
        e0, e1, e2 = weights_of([n0, n1, n2, n3])
        width_ = 512

        def body(i, value):
            here = pl.ds(pl.multiple_of(i * width_, width_), width_)
            mixed = q0[here, :] * e0 + q1[here, :] * e1 + q2[here, :] * e2
            gauge = lax.broadcasted_iota(jnp.int32, (count, width_), 1) + i * width_
            hot = jnp.where(gauge_ref[...] == gauge, 1.0, 0.0).astype(BF16)
            return value + pick(hot, mixed)

        rows_ref[...] = lax.fori_loop(0, gauges // width_, body, jnp.zeros(rows_ref.shape, F32))

    weights = inc_ref[...].astype(F32).astype(BF16)
    for b in range(blocks):
        here = pl.ds(b * width, width)
        rows = rows_ref[pl.ds(pl.multiple_of((step * blocks + b) * slots, slots), slots), :]
        added = sum(
            lax.dot_general(weights[b], piece, (((0,), (0,)), ((), ())), preferred_element_type=F32)
            for piece in pieces(rows, 3)
        )
        out_ref[here, :] = field_ref[here, :] + added


def finish(notes, row_gauge, gathered, incidence, field):
    blocks, slots, width = incidence.shape
    hours = field.shape[1]
    count = row_gauge.shape[0]
    step = 8
    whole = lambda shape: pl.BlockSpec(shape, lambda i: (0, 0))
    return pl.pallas_call(
        finish_kernel,
        grid=(blocks // step,),
        in_specs=[whole(n.shape) for n in notes]
        + [whole((count, 1))]
        + [whole(q.shape) for q in gathered]
        + [
            pl.BlockSpec((step, slots, width), lambda i: (i, 0, 0)),
            pl.BlockSpec((step * width, hours), lambda i: (i, 0)),
        ],
        out_specs=pl.BlockSpec((step * width, hours), lambda i: (i, 0)),
        out_shape=jax.ShapeDtypeStruct(field.shape, F32),
        scratch_shapes=[pltpu.VMEM((count, hours), F32)],
        compiler_params=params(56),
        name="finish",
    )(*notes, row_gauge.reshape(count, 1), *gathered, incidence, field)


def shifted(value, axis, by):
    devices = lax.axis_size(axis)
    pairs = [(i, i + by) for i in range(devices) if 0 <= i + by < devices]
    return lax.ppermute(value, axis, pairs)


def window(value):
    return jnp.concatenate([shifted(value, "tm", 1), value, shifted(value, "tm", -1)], axis=0)


def gathered_rows(value):
    owners = lax.axis_size("basin")
    copies = jnp.broadcast_to(value[None], (owners,) + value.shape)
    return lax.all_to_all(copies, "basin", 0, 0, tiled=False)


def over_hours(note):
    blocks = lax.axis_size("tm")
    result = note
    for by in range(1, blocks):
        result = result + lax.ppermute(note, "tm", [(i, (i + by) % blocks) for i in range(blocks)])
    return result


def shards(incidence, row_gauge, gauge_kernel, kernels, observed, first_guess):
    owners = lax.axis_size("basin")
    rows, hours = observed.shape
    gauges = rows * owners
    mats = transforms()
    spec = spectrum(gauge_kernel, kernels, mats[0])
    more = (lax.axis_index("tm") < lax.axis_size("tm") - 1).astype(F32).reshape(1)
    partial, gram = prepare(incidence, first_guess)
    all_gram = lax.all_gather(gram, "basin", axis=1, tiled=True)
    all_rows = lax.all_gather(row_gauge, "basin", axis=0, tiled=True)
    dense = table(row_gauge, partial, gauges).reshape(owners, rows, hours)
    sums = jnp.sum(lax.all_to_all(dense, "basin", 0, 0, tiled=False), axis=0)
    both = jnp.concatenate([observed, shifted(observed, "tm", -1)], axis=0)
    first = (lax.axis_index("basin") * rows).astype(jnp.int32).reshape(1)
    high, low = couple(first, all_rows, all_gram, rows, gauges)

    pulled, note = first_step(more, window(sums), both, spec, mats)
    notes, kept, state = [], [], None
    for k in range(3):
        everyone = gathered_rows(jnp.concatenate([pulled, note], axis=0))
        value = everyone[:, :rows].reshape(gauges, hours)
        notes.append(over_hours(jnp.sum(everyone[:, rows:], axis=0)))
        kept.append(value)
        around = window(mix(high, low, value))
        final = k == 2
        result = next_step(more, notes[-1], around, spec, mats, pulled, state, final)
        if final:
            (note,) = result
        else:
            state, pulled, note = result
    notes.append(over_hours(jnp.sum(gathered_rows(note), axis=0)))
    return finish(notes, row_gauge, kept, incidence, first_guess)


Z_, X_, Y_, C_ = 4, 2, 2, 2
NOTE = 8
HOURS = SPAN // 2


def device(z, x, y, c):
    return (z * X_ + x) * (Y_ * C_) + y * C_ + c


def moved(value, where):
    pairs = []
    for z, x, y, c in np.ndindex(Z_, X_, Y_, C_):
        target = where(z, x, y, c)
        if target is not None:
            pairs.append((device(z, x, y, c), device(*target)))
    return lax.ppermute(value, ("basin", "tm"), pairs)


def to_plane(z, x, y, c):
    return 2 * y + c, x, z & 1, z >> 1


def hour_before(z, x, y, c):
    t = 2 * y + c - 1
    return (z, x, t >> 1, t & 1) if t >= 0 else None


def from_plane(z, x, y, c):
    return 2 * c + y, x, z >> 1, z & 1


def over_x(z, x, y, c):
    return z, 1 - x, y, c


def over_y(z, x, y, c):
    return z, x, 1 - y, c


def over_xy(z, x, y, c):
    return z, 1 - x, 1 - y, c


def over_core(z, x, y, c):
    return z, x, y, 1 - c


def z_pair(z, x, y, c):
    return z ^ 1, x, y, c


def z_middle(z, x, y, c):
    return (3 - z, x, y, c) if z in (1, 2) else None


def z_two(z, x, y, c):
    return z ^ 2, x, y, c


def z_mirror(z, x, y, c):
    return 3 - z, x, y, c


def z_next(z, x, y, c):
    return (z + 1, x, y, c) if z < 3 else None


SQUARE = (over_x, over_y, over_xy)


def split_constant(value):
    out = []
    for _ in range(3):
        piece = value.astype(jnp.bfloat16)
        out.append(piece)
        value = value - piece.astype(np.float64)
    return out


ORDERS = {2: ((0, 1), (1, 0), (0, 0)), 3: ((0, 2), (1, 1), (2, 0), (0, 1), (1, 0), (0, 0))}


def widened(mat, order):
    parts = split_constant(mat)
    return jnp.asarray(np.concatenate([parts[i] for i, _ in ORDERS[order]], axis=1))


def product(wide, value, order):
    parts = pieces(value, order)
    return dot(wide, jnp.concatenate([parts[j] for _, j in ORDERS[order]], axis=0))


def turned_transforms(order):
    half = SPAN // 2
    freq = 2.0 * np.pi * (np.arange(half) + 0.5) / SPAN
    phase = freq[:, None] * np.arange(SPAN)[None, :]
    forward = np.concatenate([np.cos(phase), -np.sin(phase)], axis=0)
    inverse = forward.T * (2.0 / SPAN)
    return [widened(mat, order) for mat in (forward, inverse[:half], inverse[half:], forward[:, :half])]


def turn(waves, spec, sign):
    half = waves.shape[0] // 2
    real, imag = waves[:half], waves[half:]
    kr, ki = spec[:half], spec[half:] * sign
    return jnp.concatenate([real * kr - imag * ki, real * ki + imag * kr], axis=0)


def plane_delayed(before, here, after, spec, forward, last, order):
    rows = here.shape[1]
    pairs = [jnp.concatenate(pair, axis=0) for pair in ((before, here), (here, after))]
    waves = product(forward, jnp.concatenate(pairs, axis=1), order)
    turned = [turn(waves[:, i * rows : (i + 1) * rows], spec, 1.0) for i in range(2)]
    out = product(last, jnp.concatenate(turned, axis=1), order)
    return out[:, :rows], out[:, rows:]


def plane_advanced(here, after, spec, forward, first, order):
    waves = product(forward, jnp.concatenate([here, after], axis=0), order)
    return product(first, turn(waves, spec, -1.0), order)


def describe_kernel(inc_ref, gauge_ref, kind_ref, out_ref):
    blocks, slots, width = inc_ref.shape
    tile = 8
    rows = tile * slots
    weights = inc_ref[...].astype(F32).astype(BF16)
    row = lax.broadcasted_iota(jnp.int32, (rows, rows), 0)
    col = lax.broadcasted_iota(jnp.int32, (rows, rows), 1)
    same = row // slots == col // slots
    for i in range(blocks // tile):
        flat = weights[i * tile : (i + 1) * tile].reshape(rows, width)
        full = lax.dot_general(flat, flat, (((1,), (1,)), ((), ())), preferred_element_type=F32)
        own = jnp.where(same, full, 0.0)
        out_ref[pl.ds(0, slots), pl.ds(i * rows, rows)] = jnp.sum(own.reshape(tile, slots, rows), axis=0)
    kinds = kind_ref.shape[1]
    out_ref[pl.ds(slots, 8), :] = jnp.concatenate(
        [
            gauge_ref[...].astype(F32),
            jnp.concatenate(
                [kind_ref[...].astype(F32), jnp.zeros((1, blocks * slots - kinds), F32)], axis=1
            ),
            jnp.zeros((6, blocks * slots), F32),
        ],
        axis=0,
    )


def describe(incidence, row_gauge, gauge_kernel):
    blocks, slots, _ = incidence.shape
    count = blocks * slots
    return pl.pallas_call(
        describe_kernel,
        out_shape=jax.ShapeDtypeStruct((slots + 8, count), F32),
        compiler_params=params(),
        name="describe",
        cost_estimate=SMALL,
    )(incidence, row_gauge.reshape(1, count), gauge_kernel.reshape(1, gauge_kernel.shape[0]))


def send_kernel(inc_ref, field_ref, out_ref):
    blocks, slots, width = inc_ref.shape
    weights = inc_ref[...].astype(F32).astype(BF16)
    parts = []
    for b in range(blocks):
        value = jnp.concatenate(pieces(field_ref[pl.ds(b * width, width), :], 3)[::-1], axis=0)
        parts.append(dot(jnp.concatenate([weights[b]] * 3, axis=1), value))
    out_ref[...] = jnp.transpose(jnp.concatenate(parts, axis=0))


def send(incidence, field):
    blocks, slots, width = incidence.shape
    hours = field.shape[1]
    step = 8
    return pl.pallas_call(
        send_kernel,
        grid=(blocks // step,),
        in_specs=[
            pl.BlockSpec((step, slots, width), lambda i: (i, 0, 0)),
            pl.BlockSpec((step * width, hours), lambda i: (i, 0)),
        ],
        out_specs=pl.BlockSpec((hours, step * slots), lambda i: (0, i)),
        out_shape=jax.ShapeDtypeStruct((hours, blocks * slots), F32),
        compiler_params=params(),
        name="send",
        cost_estimate=SMALL,
    )(incidence, field)


def hot_rows(gauge, first, rows):
    mine = (lax.broadcasted_iota(jnp.int32, (rows, gauge.shape[1]), 0) + first).astype(F32)
    return jnp.where(gauge == mine, 1.0, 0.0).astype(BF16)


def spread_kernel(first_ref, mine_ref, other_ref, meta_ref, meta_other_ref, *out_refs):
    hours, rows = out_refs[0].shape
    where = meta_ref.shape[0] - 8
    value = jnp.concatenate([mine_ref[...], other_ref[...]], axis=1)
    gauge = jnp.concatenate([ref[where : where + 1, :] for ref in (meta_ref, meta_other_ref)], axis=1)
    stacked = jnp.concatenate(pieces(value, 3), axis=0)
    for m, out_ref in enumerate(out_refs):
        hot = hot_rows(gauge, first_ref[m], rows)
        result = lax.dot_general(stacked, hot, (((1,), (1,)), ((), ())), preferred_element_type=F32)
        out_ref[...] = (result[2 * hours :] + result[hours : 2 * hours]) + result[:hours]


def spread(first, parcels, metas, rows):
    hours = parcels[0].shape[0]
    return pl.pallas_call(
        spread_kernel,
        in_specs=[pl.BlockSpec(memory_space=pltpu.SMEM)] + [pl.BlockSpec(memory_space=pltpu.VMEM)] * 4,
        out_shape=[jax.ShapeDtypeStruct((hours, rows), F32)] * 4,
        compiler_params=params(),
        name="spread",
        cost_estimate=SMALL,
    )(first, *parcels, *metas)


def plane_couple_kernel(last, first_ref, *refs):
    if last:
        a_ref, b_ref, before_ref, high_ref, low_ref, total_ref, meta_ref = refs
        total_ref[...] = before_ref[...]
    else:
        a_ref, b_ref, total_ref, meta_ref = refs
        total_ref[...] = jnp.zeros_like(total_ref)
    height, double = a_ref.shape
    slots = height - 8
    count = double // 2
    cols, rows = total_ref.shape
    tile = 256
    for i, ref in enumerate((a_ref, b_ref)):
        for j in range(2):
            meta_ref[2 * i + j] = ref[:, j * count : (j + 1) * count]
    row = lax.broadcasted_iota(jnp.int32, (tile, tile), 0)
    col = lax.broadcasted_iota(jnp.int32, (tile, tile), 1)
    same = row // slots == col // slots

    def body(i, carry):
        gauge = meta_ref[i, slots : slots + 1, :]
        near = []
        for j in range(count // tile):
            here = slice(j * tile, (j + 1) * tile)
            block = jnp.concatenate([meta_ref[i, :slots, here]] * (tile // slots), axis=0)
            block = jnp.where(same, block, 0.0).astype(BF16)
            mine = jnp.concatenate(
                [hot_rows(gauge[:, here], first_ref[4 + h], rows // 2) for h in range(2)], axis=0
            )
            near.append(
                lax.dot_general(block, mine, (((1,), (1,)), ((), ())), preferred_element_type=F32)
            )
        near = jnp.concatenate(near, axis=0)
        high = near.astype(BF16)
        rest = near - high.astype(F32)
        hot = jnp.concatenate([hot_rows(gauge, first_ref[m], cols // 4) for m in range(4)], axis=0)
        total_ref[...] += dot(hot, high)

        @pl.when(jnp.max(jnp.abs(rest)) > 0.0)
        def _():
            total_ref[...] += dot(hot, rest.astype(BF16))

        return carry

    lax.fori_loop(0, 4, body, 0)
    if last:
        high, low = pieces(total_ref[...], 2)
        high_ref[...] = high
        low_ref[...] = low


def plane_couple(first, metas, rows, before=None):
    height, double = metas[0].shape
    shape = (4 * rows, 2 * rows)
    last = before is not None
    args = [first, *metas] + ([before] if last else [])
    scratch = [pltpu.VMEM((4, height, double // 2), F32)]
    return pl.pallas_call(
        functools.partial(plane_couple_kernel, last),
        in_specs=[pl.BlockSpec(memory_space=pltpu.SMEM)]
        + [pl.BlockSpec(memory_space=pltpu.VMEM)] * (len(args) - 1),
        out_shape=[jax.ShapeDtypeStruct(shape, BF16)] * 2 if last else jax.ShapeDtypeStruct(shape, F32),
        scratch_shapes=([pltpu.VMEM(shape, F32)] if last else []) + scratch,
        compiler_params=params(),
        name="plane_couple",
        cost_estimate=pl.CostEstimate(
            flops=2 * 2 * double * 8 * rows * rows, bytes_accessed=2_000_000, transcendentals=0
        ),
    )(*args)


def plane_mix_kernel(high_ref, low_ref, a_ref, b_ref, c_ref, d_ref, *refs):
    *extra, mine_ref, other_ref = refs
    refs = (a_ref, b_ref, c_ref, d_ref)
    height, rows = a_ref.shape
    body = pl.ds(0, HOURS)
    one, two = pieces(jnp.concatenate([ref[body, :] for ref in refs], axis=1), 2)
    both = dot(jnp.concatenate([two, one], axis=0), high_ref[...])
    result = (both[:HOURS] + dot(one, low_ref[...])) + both[HOURS:]
    mine_ref[body, :] = result[:, :rows]
    other_ref[body, :] = result[:, rows:]
    if height > HOURS:
        tail = pl.ds(HOURS, NOTE)
        note = sum(ref[tail, :] for ref in refs)
        mine_ref[tail, :] = note
        other_ref[tail, :] = note
    for ref in extra:
        other_ref[pl.ds(height, ref.shape[0]), :] = ref[...]


def plane_mix(coupling, values, extra):
    height, rows = values[0].shape
    return pl.pallas_call(
        plane_mix_kernel,
        out_shape=[
            jax.ShapeDtypeStruct((height, rows), F32),
            jax.ShapeDtypeStruct((height + sum(value.shape[0] for value in extra), rows), F32),
        ],
        compiler_params=params(),
        name="plane_mix",
        cost_estimate=SMALL,
    )(*coupling, *values, *extra)


def plane_rows_kernel(first_ref, meta_ref, meta_other_ref, a_ref, b_ref, c_ref, d_ref, *refs):
    if len(refs) > 2:
        *stack, last_ref, beside_ref, mine_ref, other_ref, stack_ref = refs
    else:
        mine_ref, other_ref = refs
    rows = a_ref.shape[1]
    value = jnp.concatenate([ref[pl.ds(0, HOURS), :] for ref in (a_ref, b_ref, c_ref, d_ref)], axis=1)
    one, two = pieces(value, 2)
    stacked = jnp.concatenate([two, one], axis=0)
    where = meta_ref.shape[0] - 8
    picked = []
    for ref in (meta_ref, meta_other_ref):
        gauge = ref[where : where + 1, :]
        hot = jnp.concatenate([hot_rows(gauge, first_ref[m], rows) for m in range(4)], axis=0)
        both = dot(stacked, hot)
        picked.append(both[:HOURS] + both[HOURS:])
    mine_ref[...] = picked[0]
    count = picked[1].shape[1] // rows
    for i in range(count):
        other_ref[pl.ds(i * HOURS, HOURS), :] = picked[1][:, i * rows : (i + 1) * rows]
    if len(refs) > 2:
        top = stack_ref.shape[0] - HOURS
        for ref in stack:
            stack_ref[pl.ds(0, top), :] = ref[...]
        for i in range(count):
            here = pl.ds(i * rows, rows)
            beside = beside_ref[pl.ds(beside_ref.shape[0] - (count - i) * HOURS, HOURS), :]
            stack_ref[pl.ds(top, HOURS), here] = last_ref[:, here] + beside


def plane_rows(first, metas, values, before):
    rows = values[0].shape[1]
    slots = metas[0].shape[1]
    args = [first, *metas, *values, *before]
    shapes = [(HOURS, slots), (slots // rows * HOURS, rows)]
    if before:
        shapes.append(((len(before) - 1) * HOURS, slots))
    return pl.pallas_call(
        plane_rows_kernel,
        in_specs=[pl.BlockSpec(memory_space=pltpu.SMEM)]
        + [pl.BlockSpec(memory_space=pltpu.VMEM)] * (len(args) - 1),
        out_shape=[jax.ShapeDtypeStruct(shape, F32) for shape in shapes],
        compiler_params=params(),
        name="plane_rows",
        cost_estimate=pl.CostEstimate(flops=1_000_000_000, bytes_accessed=2_000_000, transcendentals=0),
    )(*args)


def gain(kernels):
    return jnp.max(jnp.sum(kernels, axis=1, keepdims=True), axis=0, keepdims=True)


def spectra(kind, kernels, wide):
    classes = kernels.shape[0]
    row = lax.broadcasted_iota(jnp.int32, (classes, kind.shape[1]), 0).astype(F32)
    hot = jnp.where(row == kind, 1.0, 0.0).astype(BF16)
    taps = jnp.transpose(kernels / gain(kernels))
    chosen = dot(jnp.concatenate(pieces(taps, 3)[::-1], axis=1), jnp.concatenate([hot] * 3, axis=0))
    return product(wide, chosen, 3)


def plane_spectrum_kernel(class_ref, kernels_ref, wide_ref, out_ref):
    where = class_ref.shape[0] - 7
    kind = class_ref[where : where + 1, : out_ref.shape[1]]
    out_ref[...] = spectra(kind, kernels_ref[...], wide_ref[...])


def plane_spectrum(meta, kernels, wide, rows):
    return pl.pallas_call(
        plane_spectrum_kernel,
        out_shape=jax.ShapeDtypeStruct((SPAN, rows), F32),
        compiler_params=params(),
        name="plane_spectrum",
        cost_estimate=SMALL,
    )(meta, kernels, wide)


def observe_kernel(seen_ref, later_ref, kind_ref, kernels_ref, wide_ref, forward, first, out_ref):
    spec = spectra(kind_ref[...].astype(F32), kernels_ref[...], wide_ref[...])
    here, after = jnp.transpose(seen_ref[...]), jnp.transpose(later_ref[...])
    out_ref[...] = plane_advanced(here, after, spec, forward[...], first[...], 3)


def observe(seen, later, gauge_kernel, kernels, wide, mats):
    rows, hours = seen.shape
    return pl.pallas_call(
        observe_kernel,
        out_shape=jax.ShapeDtypeStruct((hours, rows), F32),
        compiler_params=params(),
        name="observe",
        cost_estimate=SMALL,
    )(seen, later, gauge_kernel.reshape(1, rows), kernels, wide, *mats)


def sides(even, pair, middle):
    return jnp.where(even, middle, pair), jnp.where(even, pair, middle)


def plane_call(kernel, name, shapes, flags, args):
    return pl.pallas_call(
        kernel,
        in_specs=[pl.BlockSpec(memory_space=pltpu.SMEM)] * len(flags)
        + [pl.BlockSpec(memory_space=pltpu.VMEM)] * len(args),
        out_shape=[jax.ShapeDtypeStruct(shape, F32) for shape in shapes],
        compiler_params=params(),
        name=name,
        cost_estimate=SMALL,
    )(*flags, *args)


def plane_first_kernel(
    flag_ref, here_ref, pair_ref, middle_ref, seen_ref, spec_ref, kernels_ref, forward, first, last, out_ref
):
    spec = spec_ref[...]
    before, after = sides(flag_ref[0] > 0.5, pair_ref[...], middle_ref[...])
    now, later = plane_delayed(before, here_ref[...], after, spec, forward[...], last[...], 3)
    known = plane_advanced(now, later * flag_ref[1], spec, forward[...], first[...], 3)
    out_ref[...] = seen_ref[...] - known * gain(kernels_ref[...])


def plane_delay_kernel(flag_ref, here_ref, pair_ref, middle_ref, spec_ref, forward, last, out_ref):
    body = pl.ds(0, HOURS)
    before, after = sides(flag_ref[0] > 0.5, pair_ref[body, :], middle_ref[body, :])
    out = plane_delayed(before, here_ref[body, :], after, spec_ref[...], forward[...], last[...], 2)
    for i in range(2):
        out_ref[pl.ds(i * HOURS, HOURS), :] = out[i]


def write_note(ref, rows):
    tail = [jnp.zeros((NOTE - len(rows), ref.shape[1]), F32)]
    ref[pl.ds(HOURS, NOTE), :] = jnp.concatenate(rows + tail, axis=0)


def plane_open_kernel(
    flag_ref, here_ref, pair_ref, middle_ref, pulled_ref, spec_ref, forward, first, last, out_ref, delayed_ref
):
    here = here_ref[...]
    spec = spec_ref[...]
    before, after = sides(flag_ref[0] > 0.5, pair_ref[...], middle_ref[...])
    now, later = plane_delayed(before, here, after, spec, forward[...], last[...], 2)
    out_ref[pl.ds(0, HOURS), :] = plane_advanced(now, later * flag_ref[1], spec, forward[...], first[...], 2)
    write_note(out_ref, [lanes(pulled_ref[...], here), lanes(now, now)])
    delayed_ref[pl.ds(0, HOURS), :] = now
    delayed_ref[pl.ds(HOURS, HOURS), :] = later


def plane_step_kernel(
    flag_ref,
    here_ref,
    pair_ref,
    two_ref,
    mirror_ref,
    pulled_ref,
    delayed_ref,
    old_z_ref,
    old_s_ref,
    old_delayed_ref,
    spec_ref,
    forward,
    first,
    total_ref,
    out_ref,
    kept_ref,
):
    tail, body = pl.ds(HOURS, NOTE), pl.ds(0, HOURS)
    total_ref[...] = (here_ref[tail, :] + pair_ref[tail, :]) + (two_ref[...] + mirror_ref[...])
    inverse = total(total_ref, 0) / total(total_ref, 1)
    z = pulled_ref[body, :] * inverse - old_z_ref[...]
    s = here_ref[body, :] * inverse - old_s_ref[...]
    both = delayed_ref[...] * inverse - old_delayed_ref[...]
    now, later = both[:HOURS], both[HOURS:]
    following = plane_advanced(now, later * flag_ref[1], spec_ref[...], forward[...], first[...], 2)
    out_ref[body, :] = following * inverse
    write_note(out_ref, [lanes(z, s), lanes(now, now)])
    for i, value in enumerate((z, s, now)):
        kept_ref[pl.ds(i * HOURS, HOURS), :] = value


def plane_close_kernel(
    here_ref, before_ref, pulled_ref, kept_ref, old_z_ref, old_s_ref, old_delayed_ref, spec_ref, forward, last, out_ref
):
    body = pl.ds(0, HOURS)
    here, raw = here_ref[body, :], pulled_ref[body, :]
    waves = product(forward[...], jnp.concatenate([before_ref[body, :], here], axis=0), 2)
    now = product(last[...], turn(waves, spec_ref[...], 1.0), 2)
    z, s, delayed = (kept_ref[pl.ds(i * HOURS, HOURS), :] for i in range(3))
    note = [pulled_ref[HOURS + i : HOURS + i + 1, :] for i in range(2)]
    for left in (raw, z, old_z_ref[...]):
        note += [lanes(left, right) for right in (here, s, old_s_ref[...])]
    parts = (now, delayed, old_delayed_ref[body, :])
    for i in range(3):
        note += [lanes(parts[i], parts[j]) for j in range(i, 3)]
    note.append(jnp.zeros((24 - len(note), here.shape[1]), F32))
    note = jnp.sum(jnp.concatenate(note, axis=0), axis=1, keepdims=True)
    shape = (24, out_ref.shape[2])
    row, col = (lax.broadcasted_iota(jnp.int32, shape, i) for i in range(2))
    note = jnp.sum(jnp.where(row == col, jnp.broadcast_to(note, shape), 0.0), axis=0, keepdims=True)
    out_ref[...] = jnp.broadcast_to(note[None], out_ref.shape)


def plane_weights(open_ref, close, scale):
    entry = lambda i: close[:, i : i + 1]
    n1, t1 = total(open_ref, 0), total(open_ref, 1)
    n2, t2 = entry(0), entry(1)
    a1 = t1 / n1
    a2, r2 = (t2 / n2) / a1, n2 / n1
    plain = (1.0, -a2, -r2)
    n3 = sum(plain[i] * plain[j] * entry(2 + 3 * i + j) for i in range(3) for j in range(3))
    pairs = [(i, j) for i in range(3) for j in range(i, 3)]
    t3 = sum(
        plain[i] * plain[j] * entry(11 + n) * (1.0 if i == j else 2.0) for n, (i, j) in enumerate(pairs)
    )
    a3, r3 = (t3 / n3) / a1, n3 / n2
    unit = 1.0 / (a1 * scale)
    c3 = unit / (a3 * (a2 - r2) - r3)
    c2 = -a3 * c3
    c1 = unit - r2 * c2
    step = c2 - c3 * a2
    return c1 - step - c3 * r2, step / a1, c3


def plane_combine_kernel(open_ref, close_ref, kernels_ref, stack_ref, mine_ref, beside_ref, out_ref):
    rows = open_ref.shape[1]
    close = jnp.sum(close_ref[...], axis=0)[0:1, :]
    e0, e1, e2 = plane_weights(open_ref, close, gain(kernels_ref[...]))
    for i in range(out_ref.shape[0] // rows):
        here = pl.ds(i * rows, rows)
        last = mine_ref[:, here] + beside_ref[pl.ds(i * HOURS, HOURS), :]
        value = stack_ref[pl.ds(0, HOURS), here] * e0 + stack_ref[pl.ds(HOURS, HOURS), here] * e1 + last * e2
        out_ref[here, :] = jnp.transpose(value)


def plane_finish_kernel(rows_ref, inc_ref, field_ref, out_ref):
    blocks, slots, width = inc_ref.shape
    weights = inc_ref[...].astype(F32).astype(BF16)
    for b in range(blocks):
        here = pl.ds(b * width, width)
        rows = jnp.concatenate(pieces(rows_ref[pl.ds(b * slots, slots), :], 2), axis=0)
        twice = jnp.concatenate([weights[b]] * 2, axis=0)
        added = lax.dot_general(twice, rows, (((0,), (0,)), ((), ())), preferred_element_type=F32)
        out_ref[here, :] = field_ref[here, :] + added


def plane_finish(rows, incidence, field):
    blocks, slots, width = incidence.shape
    hours = field.shape[1]
    step = 8
    return pl.pallas_call(
        plane_finish_kernel,
        grid=(blocks // step,),
        in_specs=[
            pl.BlockSpec((step * slots, hours), lambda i: (i, 0)),
            pl.BlockSpec((step, slots, width), lambda i: (i, 0, 0)),
            pl.BlockSpec((step * width, hours), lambda i: (i, 0)),
        ],
        out_specs=pl.BlockSpec((step * width, hours), lambda i: (i, 0)),
        out_shape=jax.ShapeDtypeStruct(field.shape, F32),
        compiler_params=params(),
        name="plane_finish",
    )(rows, incidence, field)


def plane_shards(incidence, row_gauge, gauge_kernel, kernels, observed, first_guess):
    rows, hours = observed.shape
    basin, tm = lax.axis_index("basin"), lax.axis_index("tm")
    z, x, y, c = basin // X_, basin % X_, tm // C_, tm % C_
    place = 2 * y + x
    first = jnp.stack([4 * c + (place ^ m) for m in range(4)] + [4 * c + place, 4 * (1 - c) + place])
    first = (first * rows).astype(jnp.int32)
    flags = jnp.stack([1 - z % 2, (z < Z_ - 1).astype(z.dtype), (z > 0).astype(z.dtype)]).astype(F32)
    forward, inverse_first, inverse_last, _ = turned_transforms(2)
    forward3, inverse_first3, inverse_last3, short3 = turned_transforms(3)
    block, noted = (hours, rows), (hours + NOTE, rows)

    parcel = send(incidence, first_guess)
    parcel, near, gauges, kinds, seen = lax.optimization_barrier(
        (parcel, incidence, row_gauge, gauge_kernel, observed)
    )
    parcel = moved(parcel, to_plane)
    meta = moved(describe(near, gauges, kinds), to_plane)
    seen = observe(seen, moved(seen, hour_before), kinds, kernels, short3, [forward3, inverse_first3])
    metas = [meta, moved(meta, over_core)]
    spec = plane_spectrum(meta, kernels, short3, rows)
    parcel, seen, metas, spec = lax.optimization_barrier((parcel, seen, metas, spec))
    seen = moved(seen, to_plane)
    both = jnp.concatenate(metas, axis=1)
    around = [both] + [moved(both, where) for where in SQUARE]

    dense = spread(first, [parcel, moved(parcel, over_core)], metas, rows)
    sums = dense[0] + sum(moved(value, where) for value, where in zip(dense[1:], SQUARE))
    sums = [sums, moved(sums, z_pair), moved(sums, z_middle)]
    coupled = plane_couple(first, around[:2], rows)
    coupled, sums = lax.optimization_barrier((coupled, sums))
    coupling = plane_couple(first, around[2:], rows, coupled)
    (pulled0,) = plane_call(
        plane_first_kernel,
        "plane_first",
        [block],
        [flags],
        [*sums, seen, spec, kernels, forward3, inverse_first3, inverse_last3],
    )

    def mixing(pulled, extra):
        values = [pulled] + [moved(pulled, where) for where in SQUARE]
        mine, other = plane_mix(coupling, values, extra)
        beside = moved(other, over_core)
        return values, mine + beside[: pulled.shape[0]], beside

    values, mixed0, _ = mixing(pulled0, [])
    picked, theirs = plane_rows(first, metas, values, [])
    sums = [mixed0, moved(mixed0, z_pair), moved(mixed0, z_middle)]
    pulled1, delayed0 = plane_call(
        plane_open_kernel,
        "plane_open",
        [noted, (2 * hours, rows)],
        [flags],
        [*sums, pulled0, spec, forward, inverse_first, inverse_last],
    )

    values, mixed1, beside = mixing(pulled1, [theirs])
    picked, theirs, stack = plane_rows(first, metas, values, [picked, beside])
    sums = [mixed1, moved(mixed1, z_pair), moved(mixed1, z_middle)]
    two, mirror = moved(mixed1[hours:], z_two), moved(mixed1[hours:], z_mirror)
    (delayed1,) = plane_call(
        plane_delay_kernel, "plane_delay", [(2 * hours, rows)], [flags], [*sums, spec, forward, inverse_last]
    )
    open_note, pulled2, kept = plane_call(
        plane_step_kernel,
        "plane_step",
        [(NOTE, rows), noted, (3 * hours, rows)],
        [flags],
        [*sums[:2], two, mirror, pulled1, delayed1, pulled0, mixed0, delayed0, spec, forward, inverse_first],
    )

    values, mixed2, beside = mixing(pulled2, [theirs])
    picked, theirs, stack = plane_rows(first, metas, values, [stack, picked, beside])
    (note,) = plane_call(
        plane_close_kernel,
        "plane_close",
        [(Z_ * X_ * Y_ * C_, 8, rows // 2)],
        [],
        [mixed2, moved(mixed2, z_next), pulled2, kept, pulled0, mixed0, delayed0, spec, forward, inverse_last],
    )
    close_note = lax.all_to_all(note, ("basin", "tm"), 0, 0, tiled=False)
    (answer,) = plane_call(
        plane_combine_kernel,
        "plane_combine",
        [(metas[0].shape[1], hours)],
        [],
        [open_note, close_note, kernels, stack, picked, moved(theirs, over_core)],
    )
    return plane_finish(moved(answer, from_plane), incidence, first_guess)


def solution(mesh):
    planes = dict(mesh.shape) == {"basin": Z_ * X_, "tm": Y_ * C_}
    in_specs = (
        P("basin", None, None),
        P("basin"),
        P("basin"),
        P(),
        P("basin", "tm"),
        P("basin", "tm"),
    )
    return jax.shard_map(
        plane_shards if planes else shards, mesh=mesh, in_specs=in_specs, out_specs=P("basin", "tm"), check_vma=False
    )
```

```python
import functools

import jax
import jax.numpy as jnp
import numpy as np
from jax import lax
from jax.experimental import pallas as pl
from jax.experimental.pallas import tpu as pltpu
from jax.sharding import PartitionSpec as P

F32 = jnp.float32
BF16 = jnp.bfloat16
HIGH = lax.Precision.HIGHEST
SPAN = 256
MIB = 1024 * 1024


SMALL = pl.CostEstimate(flops=1, bytes_accessed=1, transcendentals=0)


def params(mib=16):
    return pltpu.CompilerParams(vmem_limit_bytes=mib * MIB)


def transforms():
    half = SPAN // 2
    freq = 2.0 * np.pi * (np.arange(half) + 0.5) / SPAN
    phase = np.arange(SPAN)[:, None] * freq[None, :]
    forward = np.concatenate([np.cos(phase), -np.sin(phase)], axis=1)
    inverse = forward.T * (2.0 / SPAN)
    return (
        jnp.asarray(forward, F32),
        jnp.asarray(inverse[:, :half], F32),
        jnp.asarray(inverse[:, half:], F32),
    )


def dot(a, b):
    return jnp.dot(a, b, preferred_element_type=F32)


def exact(a, b):
    return jnp.dot(a, b, precision=HIGH, preferred_element_type=F32)


def pieces(value, count):
    out = []
    for _ in range(count):
        piece = value.astype(BF16)
        out.append(piece)
        value = value - piece.astype(F32)
    return out


def pick(hot, value):
    return sum(dot(hot, piece) for piece in pieces(value, 3))


def prepare_kernel(inc_ref, field_ref, partial_ref, gram_ref):
    blocks, slots, width = inc_ref.shape
    rows = blocks * slots
    weights = inc_ref[...].astype(F32).astype(BF16)
    for b in range(blocks):
        value = field_ref[pl.ds(b * width, width), :]
        partial_ref[pl.ds(b * slots, slots), :] = pick(weights[b], value)
    flat = weights.reshape(rows, width)
    full = lax.dot_general(flat, flat, (((1,), (1,)), ((), ())), preferred_element_type=F32)
    row = lax.broadcasted_iota(jnp.int32, (rows, rows), 0)
    col = lax.broadcasted_iota(jnp.int32, (rows, rows), 1)
    own = jnp.where(row // slots == col // slots, full, 0.0)
    gram_ref[...] = jnp.sum(own.reshape(blocks, slots, rows), axis=0)


def prepare(incidence, field):
    blocks, slots, width = incidence.shape
    hours = field.shape[1]
    step = 8
    return pl.pallas_call(
        prepare_kernel,
        grid=(blocks // step,),
        in_specs=[
            pl.BlockSpec((step, slots, width), lambda i: (i, 0, 0)),
            pl.BlockSpec((step * width, hours), lambda i: (i, 0)),
        ],
        out_specs=[
            pl.BlockSpec((step * slots, hours), lambda i: (i, 0)),
            pl.BlockSpec((slots, step * slots), lambda i: (0, i)),
        ],
        out_shape=[
            jax.ShapeDtypeStruct((blocks * slots, hours), F32),
            jax.ShapeDtypeStruct((slots, blocks * slots), F32),
        ],
        compiler_params=params(56),
        name="prepare",
    )(incidence, field)


def table_kernel(gauge_ref, partial_ref, out_ref):
    slots = partial_ref.shape[0]
    rows = out_ref.shape[0]
    first = pl.program_id(0) * rows
    gauge = lax.broadcasted_iota(jnp.int32, (rows, slots), 0) + first
    hot = jnp.where(gauge_ref[...] == gauge, 1.0, 0.0).astype(BF16)
    out_ref[...] = pick(hot, partial_ref[...])


def table(row_gauge, partial, gauges):
    slots, hours = partial.shape
    step = 256
    return pl.pallas_call(
        table_kernel,
        grid=(gauges // step,),
        in_specs=[
            pl.BlockSpec((1, slots), lambda i: (0, 0)),
            pl.BlockSpec((slots, hours), lambda i: (0, 0)),
        ],
        out_specs=pl.BlockSpec((step, hours), lambda i: (i, 0)),
        out_shape=jax.ShapeDtypeStruct((gauges, hours), F32),
        compiler_params=params(56),
        name="table",
    )(row_gauge.reshape(1, slots), partial)


def couple_kernel(first_ref, lane_ref, sub_ref, gram_ref, high_ref, low_ref, near_ref):
    slots = gram_ref.shape[0]
    count = lane_ref.shape[1]
    rows, cols = high_ref.shape
    tile = 256
    first = first_ref[0]

    @pl.when(pl.program_id(0) == 0)
    def _():
        row = lax.broadcasted_iota(jnp.int32, (tile, tile), 0)
        col = lax.broadcasted_iota(jnp.int32, (tile, tile), 1)
        same = row // slots == col // slots
        mine = lax.broadcasted_iota(jnp.int32, (rows, tile), 0) + first

        def body(i, carry):
            here = pl.ds(pl.multiple_of(i * tile, tile), tile)
            block = jnp.concatenate([gram_ref[:, here]] * (tile // slots), axis=0)
            block = jnp.where(same, block, 0.0).astype(BF16)
            hot = jnp.where(lane_ref[:, here] == mine, 1.0, 0.0).astype(BF16)
            near_ref[:, here] = dot(hot, block)
            return carry

        lax.fori_loop(0, count // tile, body, 0)

    def chunk(i, total):
        here = pl.ds(pl.multiple_of(i * 1024, 1024), 1024)
        gauge = lax.broadcasted_iota(jnp.int32, (1024, cols), 1) + pl.program_id(0) * cols
        hot = jnp.where(sub_ref[here, :] == gauge, 1.0, 0.0).astype(BF16)
        near = near_ref[:, here]
        high = near.astype(BF16)
        low = (near - high.astype(F32)).astype(BF16)
        return total + dot(high, hot) + dot(low, hot)

    total = lax.fori_loop(0, count // 1024, chunk, jnp.zeros((rows, cols), F32))
    high, low = pieces(total, 2)
    high_ref[...] = high
    low_ref[...] = low


def couple(first, row_gauge, gram, rows, gauges):
    count = row_gauge.shape[0]
    step = 256
    return pl.pallas_call(
        couple_kernel,
        grid=(gauges // step,),
        in_specs=[
            pl.BlockSpec(memory_space=pltpu.SMEM),
            pl.BlockSpec((1, count), lambda i: (0, 0)),
            pl.BlockSpec((count, 1), lambda i: (0, 0)),
            pl.BlockSpec(gram.shape, lambda i: (0, 0)),
        ],
        out_specs=[pl.BlockSpec((rows, step), lambda i: (0, i))] * 2,
        out_shape=[jax.ShapeDtypeStruct((rows, gauges), BF16)] * 2,
        scratch_shapes=[pltpu.VMEM((rows, count), F32)],
        compiler_params=params(56),
        name="couple",
    )(first, row_gauge.reshape(1, count), row_gauge.reshape(count, 1), gram)


def mix_kernel(high_ref, low_ref, value_ref, out_ref):
    high = high_ref[...]
    low = low_ref[...]
    one, two, three = pieces(value_ref[...], 3)
    out_ref[...] = (dot(high, three) + dot(low, two)) + (dot(high, two) + dot(low, one)) + dot(high, one)


def mix(high, low, value):
    return pl.pallas_call(
        mix_kernel,
        out_shape=jax.ShapeDtypeStruct((high.shape[0], value.shape[1]), F32),
        compiler_params=params(56),
        name="mix",
    )(high, low, value)


def spectrum_kernel(class_ref, kernels_ref, forward_ref, out_ref):
    rows = class_ref.shape[0]
    classes, taps = kernels_ref.shape
    kind = lax.broadcasted_iota(jnp.int32, (rows, classes), 1)
    hot = jnp.where(class_ref[...] == kind, 1.0, 0.0)
    out_ref[...] = exact(exact(hot, kernels_ref[...]), forward_ref[pl.ds(0, taps), :])


def spectrum(gauge_kernel, kernels, forward):
    rows = gauge_kernel.shape[0]
    return pl.pallas_call(
        spectrum_kernel,
        out_shape=jax.ShapeDtypeStruct((rows, SPAN), F32),
        compiler_params=params(56),
        name="spectrum",
    )(gauge_kernel.reshape(rows, 1), kernels, forward)


def delayed(before, here, after, spec, forward, inverse_last):
    rows, half = here.shape
    stacked = jnp.concatenate(
        [jnp.concatenate([before, here], axis=1), jnp.concatenate([here, after], axis=1)], axis=0
    )
    waves = exact(stacked, forward)
    real, imag = waves[:, :half], waves[:, half:]
    kr = jnp.concatenate([spec[:, :half]] * 2, axis=0)
    ki = jnp.concatenate([spec[:, half:]] * 2, axis=0)
    turned = jnp.concatenate([real * kr - imag * ki, real * ki + imag * kr], axis=1)
    out = exact(turned, inverse_last)
    return out[:rows], out[rows:]


def advanced(here, after, spec, forward, inverse_first):
    half = here.shape[1]
    waves = exact(jnp.concatenate([here, after], axis=1), forward)
    real, imag = waves[:, :half], waves[:, half:]
    kr, ki = spec[:, :half], spec[:, half:]
    turned = jnp.concatenate([real * kr + imag * ki, imag * kr - real * ki], axis=1)
    return exact(turned, inverse_first)


def lanes(a, b):
    return jnp.sum(a * b, axis=0, keepdims=True)


def total(ref, row):
    return jnp.sum(ref[row : row + 1, :], axis=1, keepdims=True)


def ratios(ref):
    square = total(ref, 0)
    alpha = jnp.sqrt(square)
    beta = jnp.sqrt(jnp.maximum(total(ref, 1) / square - 2.0 * total(ref, 2) + square, 0.0))
    return alpha, beta


def first_kernel(
    more_ref, sums_ref, observed_ref, spec_ref, forward_ref, first_ref, last_ref, out_ref, note_ref
):
    rows, half = observed_ref.shape[0] // 2, observed_ref.shape[1]
    spec, forward = spec_ref[...], forward_ref[...]
    before, here, after = (sums_ref[pl.ds(i * rows, rows), :] for i in range(3))
    now, later = delayed(before, here, after, spec, forward, last_ref[...])
    start = observed_ref[pl.ds(0, rows), :] - now
    start_later = (observed_ref[pl.ds(rows, rows), :] - later) * more_ref[0]
    out_ref[...] = advanced(start, start_later, spec, forward, first_ref[...])
    note_ref[...] = jnp.concatenate([lanes(start, start), jnp.zeros((7, half), F32)], axis=0)


def first_step(more, sums, observed, spec, mats):
    rows, half = spec.shape[0], observed.shape[1]
    return pl.pallas_call(
        first_kernel,
        in_specs=[pl.BlockSpec(memory_space=pltpu.SMEM)] + [pl.BlockSpec(memory_space=pltpu.VMEM)] * 6,
        out_shape=[jax.ShapeDtypeStruct((rows, half), F32), jax.ShapeDtypeStruct((8, half), F32)],
        compiler_params=params(56),
        name="first_step",
    )(more, sums, observed, spec, *mats)


def step_kernel(
    opening,
    final,
    more_ref,
    note_ref,
    sums_ref,
    spec_ref,
    forward_ref,
    first_ref,
    last_ref,
    pulled_ref,
    *refs,
):
    if opening:
        state_ref = None
    else:
        state_ref, *refs = refs
    if final:
        (out_note_ref,) = refs
    else:
        new_ref, out_ref, out_note_ref = refs
    rows, half = pulled_ref.shape
    spec, forward = spec_ref[...], forward_ref[...]
    if opening:
        scale = 1.0 / jnp.sqrt(total(note_ref, 0))
        along = sums_ref[...] * scale
        new_s, new_su = along, along
        new_zu = pulled_ref[...] * scale
        new_z = new_zu
    else:
        alpha, beta = ratios(note_ref)
        a, b, g = 1.0 / (alpha * beta), alpha / beta, beta / alpha
        wide = pl.ds(0, 3 * rows), pl.ds(3 * rows, 3 * rows)
        new_su = sums_ref[...] * a - state_ref[wide[1], :] * b
        new_s = new_su - state_ref[wide[0], :] * g
        new_zu = pulled_ref[...] * a - state_ref[pl.ds(7 * rows, rows), :] * b
        new_z = new_zu - state_ref[pl.ds(6 * rows, rows), :] * g
    before, here, after = (new_s[i * rows : (i + 1) * rows] for i in range(3))
    now, later = delayed(before, here, after, spec, forward, last_ref[...])
    out_note_ref[...] = jnp.concatenate(
        [lanes(new_z, here), lanes(now, now), lanes(new_zu, here), jnp.zeros((5, half), F32)], axis=0
    )
    if not final:
        new_ref[pl.ds(0, 3 * rows), :] = new_s
        new_ref[pl.ds(3 * rows, 3 * rows), :] = new_su
        new_ref[pl.ds(6 * rows, rows), :] = new_z
        new_ref[pl.ds(7 * rows, rows), :] = new_zu
        out_ref[...] = advanced(now, later * more_ref[0], spec, forward, first_ref[...])


def next_step(more, note, sums, spec, mats, pulled, state, final):
    rows, half = pulled.shape
    opening = state is None
    shapes = [
        jax.ShapeDtypeStruct((8 * rows, half), F32),
        jax.ShapeDtypeStruct((rows, half), F32),
        jax.ShapeDtypeStruct((8, half), F32),
    ]
    args = [more, note, sums, spec, *mats, pulled] + ([] if opening else [state])
    return pl.pallas_call(
        functools.partial(step_kernel, opening, final),
        in_specs=[pl.BlockSpec(memory_space=pltpu.SMEM)]
        + [pl.BlockSpec(memory_space=pltpu.VMEM)] * (len(args) - 1),
        out_shape=shapes[2:] if final else shapes,
        compiler_params=params(56),
        name="next_step",
    )(*args)


def weights_of(notes):
    start = jnp.sqrt(total(notes[0], 0))
    zero = jnp.zeros_like(start)
    units = [1.0 / start, zero, zero]
    z, zu = list(units), list(units)
    phibar = start
    alpha, beta = ratios(notes[1])
    rhobar = alpha
    w = [value / alpha for value in z]
    result = [zero] * 3
    steps = len(notes) - 1
    for k in range(steps):
        rho = jnp.sqrt(rhobar * rhobar + beta * beta)
        cosine, sine = rhobar / rho, beta / rho
        phi, phibar = cosine * phibar, sine * phibar
        result = [r + phi / rho * value for r, value in zip(result, w)]
        if k < steps - 1:
            a, b, g = 1.0 / (alpha * beta), alpha / beta, beta / alpha
            zu = [(a if i == k + 1 else 0.0) - b * value for i, value in enumerate(zu)]
            z = [value - g * old for value, old in zip(zu, z)]
            alpha, beta = ratios(notes[k + 2])
            theta = sine * alpha
            rhobar = -cosine * alpha
            w = [value / alpha - theta / rho * old for value, old in zip(z, w)]
    return result


def finish_kernel(n0, n1, n2, n3, gauge_ref, q0, q1, q2, inc_ref, field_ref, out_ref, rows_ref):
    blocks, slots, width = inc_ref.shape
    count = rows_ref.shape[0]
    gauges = q0.shape[0]
    step = pl.program_id(0)

    @pl.when(step == 0)
    def _():
        e0, e1, e2 = weights_of([n0, n1, n2, n3])
        width_ = 512

        def body(i, value):
            here = pl.ds(pl.multiple_of(i * width_, width_), width_)
            mixed = q0[here, :] * e0 + q1[here, :] * e1 + q2[here, :] * e2
            gauge = lax.broadcasted_iota(jnp.int32, (count, width_), 1) + i * width_
            hot = jnp.where(gauge_ref[...] == gauge, 1.0, 0.0).astype(BF16)
            return value + pick(hot, mixed)

        rows_ref[...] = lax.fori_loop(0, gauges // width_, body, jnp.zeros(rows_ref.shape, F32))

    weights = inc_ref[...].astype(F32).astype(BF16)
    for b in range(blocks):
        here = pl.ds(b * width, width)
        rows = rows_ref[pl.ds(pl.multiple_of((step * blocks + b) * slots, slots), slots), :]
        added = sum(
            lax.dot_general(weights[b], piece, (((0,), (0,)), ((), ())), preferred_element_type=F32)
            for piece in pieces(rows, 3)
        )
        out_ref[here, :] = field_ref[here, :] + added


def finish(notes, row_gauge, gathered, incidence, field):
    blocks, slots, width = incidence.shape
    hours = field.shape[1]
    count = row_gauge.shape[0]
    step = 8
    whole = lambda shape: pl.BlockSpec(shape, lambda i: (0, 0))
    return pl.pallas_call(
        finish_kernel,
        grid=(blocks // step,),
        in_specs=[whole(n.shape) for n in notes]
        + [whole((count, 1))]
        + [whole(q.shape) for q in gathered]
        + [
            pl.BlockSpec((step, slots, width), lambda i: (i, 0, 0)),
            pl.BlockSpec((step * width, hours), lambda i: (i, 0)),
        ],
        out_specs=pl.BlockSpec((step * width, hours), lambda i: (i, 0)),
        out_shape=jax.ShapeDtypeStruct(field.shape, F32),
        scratch_shapes=[pltpu.VMEM((count, hours), F32)],
        compiler_params=params(56),
        name="finish",
    )(*notes, row_gauge.reshape(count, 1), *gathered, incidence, field)


def shifted(value, axis, by):
    devices = lax.axis_size(axis)
    pairs = [(i, i + by) for i in range(devices) if 0 <= i + by < devices]
    return lax.ppermute(value, axis, pairs)


def window(value):
    return jnp.concatenate([shifted(value, "tm", 1), value, shifted(value, "tm", -1)], axis=0)


def gathered_rows(value):
    owners = lax.axis_size("basin")
    copies = jnp.broadcast_to(value[None], (owners,) + value.shape)
    return lax.all_to_all(copies, "basin", 0, 0, tiled=False)


def over_hours(note):
    blocks = lax.axis_size("tm")
    result = note
    for by in range(1, blocks):
        result = result + lax.ppermute(note, "tm", [(i, (i + by) % blocks) for i in range(blocks)])
    return result


def shards(incidence, row_gauge, gauge_kernel, kernels, observed, first_guess):
    owners = lax.axis_size("basin")
    rows, hours = observed.shape
    gauges = rows * owners
    mats = transforms()
    spec = spectrum(gauge_kernel, kernels, mats[0])
    more = (lax.axis_index("tm") < lax.axis_size("tm") - 1).astype(F32).reshape(1)
    partial, gram = prepare(incidence, first_guess)
    all_gram = lax.all_gather(gram, "basin", axis=1, tiled=True)
    all_rows = lax.all_gather(row_gauge, "basin", axis=0, tiled=True)
    dense = table(row_gauge, partial, gauges).reshape(owners, rows, hours)
    sums = jnp.sum(lax.all_to_all(dense, "basin", 0, 0, tiled=False), axis=0)
    both = jnp.concatenate([observed, shifted(observed, "tm", -1)], axis=0)
    first = (lax.axis_index("basin") * rows).astype(jnp.int32).reshape(1)
    high, low = couple(first, all_rows, all_gram, rows, gauges)

    pulled, note = first_step(more, window(sums), both, spec, mats)
    notes, kept, state = [], [], None
    for k in range(3):
        everyone = gathered_rows(jnp.concatenate([pulled, note], axis=0))
        value = everyone[:, :rows].reshape(gauges, hours)
        notes.append(over_hours(jnp.sum(everyone[:, rows:], axis=0)))
        kept.append(value)
        around = window(mix(high, low, value))
        final = k == 2
        result = next_step(more, notes[-1], around, spec, mats, pulled, state, final)
        if final:
            (note,) = result
        else:
            state, pulled, note = result
    notes.append(over_hours(jnp.sum(gathered_rows(note), axis=0)))
    return finish(notes, row_gauge, kept, incidence, first_guess)


Z_, X_, Y_, C_ = 4, 2, 2, 2
NOTE = 8
HOURS = SPAN // 2


def device(z, x, y, c):
    return (z * X_ + x) * (Y_ * C_) + y * C_ + c


def moved(value, where):
    pairs = []
    for z, x, y, c in np.ndindex(Z_, X_, Y_, C_):
        target = where(z, x, y, c)
        if target is not None:
            pairs.append((device(z, x, y, c), device(*target)))
    return lax.ppermute(value, ("basin", "tm"), pairs)


def to_plane(z, x, y, c):
    return 2 * y + c, x, z & 1, z >> 1


def hour_before(z, x, y, c):
    t = 2 * y + c - 1
    return (z, x, t >> 1, t & 1) if t >= 0 else None


def from_plane(z, x, y, c):
    return 2 * c + y, x, z >> 1, z & 1


def over_x(z, x, y, c):
    return z, 1 - x, y, c


def over_y(z, x, y, c):
    return z, x, 1 - y, c


def over_xy(z, x, y, c):
    return z, 1 - x, 1 - y, c


def over_core(z, x, y, c):
    return z, x, y, 1 - c


def z_pair(z, x, y, c):
    return z ^ 1, x, y, c


def z_middle(z, x, y, c):
    return (3 - z, x, y, c) if z in (1, 2) else None


def z_two(z, x, y, c):
    return z ^ 2, x, y, c


def z_mirror(z, x, y, c):
    return 3 - z, x, y, c


def z_next(z, x, y, c):
    return (z + 1, x, y, c) if z < 3 else None


SQUARE = (over_x, over_y, over_xy)


def split_constant(value):
    out = []
    for _ in range(3):
        piece = value.astype(jnp.bfloat16)
        out.append(piece)
        value = value - piece.astype(np.float64)
    return out


ORDERS = {2: ((0, 1), (1, 0), (0, 0)), 3: ((0, 2), (1, 1), (2, 0), (0, 1), (1, 0), (0, 0))}


def widened(mat, order):
    parts = split_constant(mat)
    return jnp.asarray(np.concatenate([parts[i] for i, _ in ORDERS[order]], axis=1))


def product(wide, value, order):
    parts = pieces(value, order)
    return dot(wide, jnp.concatenate([parts[j] for _, j in ORDERS[order]], axis=0))


def turned_transforms(order):
    half = SPAN // 2
    freq = 2.0 * np.pi * (np.arange(half) + 0.5) / SPAN
    phase = freq[:, None] * np.arange(SPAN)[None, :]
    forward = np.concatenate([np.cos(phase), -np.sin(phase)], axis=0)
    inverse = forward.T * (2.0 / SPAN)
    return [widened(mat, order) for mat in (forward, inverse[:half], inverse[half:], forward[:, :half])]


def turn(waves, spec, sign):
    half = waves.shape[0] // 2
    real, imag = waves[:half], waves[half:]
    kr, ki = spec[:half], spec[half:] * sign
    return jnp.concatenate([real * kr - imag * ki, real * ki + imag * kr], axis=0)


def plane_delayed(before, here, after, spec, forward, last, order):
    rows = here.shape[1]
    pairs = [jnp.concatenate(pair, axis=0) for pair in ((before, here), (here, after))]
    waves = product(forward, jnp.concatenate(pairs, axis=1), order)
    turned = [turn(waves[:, i * rows : (i + 1) * rows], spec, 1.0) for i in range(2)]
    out = product(last, jnp.concatenate(turned, axis=1), order)
    return out[:, :rows], out[:, rows:]


def plane_advanced(here, after, spec, forward, first, order):
    waves = product(forward, jnp.concatenate([here, after], axis=0), order)
    return product(first, turn(waves, spec, -1.0), order)


def describe_kernel(inc_ref, seen_ref, later_ref, kind_ref, kernels_ref, wide_ref, forward, first, out_ref):
    blocks, slots, width = inc_ref.shape
    rows = seen_ref.shape[0]
    tile = 8
    side = tile * slots
    weights = inc_ref[...].astype(F32).astype(BF16)
    row = lax.broadcasted_iota(jnp.int32, (side, side), 0)
    col = lax.broadcasted_iota(jnp.int32, (side, side), 1)
    same = row // slots == col // slots
    for i in range(blocks // tile):
        flat = weights[i * tile : (i + 1) * tile].reshape(side, width)
        full = lax.dot_general(flat, flat, (((1,), (1,)), ((), ())), preferred_element_type=F32)
        own = jnp.where(same, full, 0.0)
        out_ref[pl.ds(0, slots), pl.ds(i * side, side)] = jnp.sum(own.reshape(tile, slots, side), axis=0)
    spec = spectra(kind_ref[...].astype(F32), kernels_ref[...], wide_ref[...])
    here, after = jnp.transpose(seen_ref[...]), jnp.transpose(later_ref[...])
    pulled = plane_advanced(here, after, spec, forward[...], first[...], 3)
    step = out_ref.shape[0] - slots
    for i in range(HOURS // step):
        out_ref[pl.ds(slots, step), pl.ds(i * rows, rows)] = pulled[i * step : (i + 1) * step]


def describe(incidence, seen, later, gauge_kernel, kernels, wide, mats):
    blocks, slots, _ = incidence.shape
    rows, hours = seen.shape
    count = blocks * slots
    return pl.pallas_call(
        describe_kernel,
        out_shape=jax.ShapeDtypeStruct((slots + hours * rows // count, count), F32),
        compiler_params=params(),
        name="describe",
        cost_estimate=SMALL,
    )(incidence, seen, later, gauge_kernel.reshape(1, rows), kernels, wide, *mats)


def send_kernel(inc_ref, field_ref, gauge_ref, kind_ref, out_ref):
    blocks, slots, width = inc_ref.shape
    count = blocks * slots
    weights = inc_ref[...].astype(F32).astype(BF16)
    parts = []
    for b in range(blocks):
        value = jnp.concatenate(pieces(field_ref[pl.ds(b * width, width), :], 3)[::-1], axis=0)
        parts.append(dot(jnp.concatenate([weights[b]] * 3, axis=1), value))
    out_ref[pl.ds(0, HOURS), :] = jnp.transpose(jnp.concatenate(parts, axis=0))
    kinds = kind_ref.shape[1] // count
    here = jnp.minimum(pl.program_id(0), kinds - 1) * count
    out_ref[pl.ds(HOURS, 8), :] = jnp.concatenate(
        [
            gauge_ref[...].astype(F32),
            kind_ref[:, pl.ds(pl.multiple_of(here, count), count)].astype(F32),
            jnp.zeros((6, count), F32),
        ],
        axis=0,
    )


def send(incidence, field, row_gauge, gauge_kernel):
    blocks, slots, width = incidence.shape
    count = blocks * slots
    rows = gauge_kernel.shape[0]
    step = 8
    return pl.pallas_call(
        send_kernel,
        grid=(blocks // step,),
        in_specs=[
            pl.BlockSpec((step, slots, width), lambda i: (i, 0, 0)),
            pl.BlockSpec((step * width, HOURS), lambda i: (i, 0)),
            pl.BlockSpec((1, step * slots), lambda i: (0, i)),
            pl.BlockSpec((1, rows), lambda i: (0, 0)),
        ],
        out_specs=pl.BlockSpec((HOURS + 8, step * slots), lambda i: (0, i)),
        out_shape=jax.ShapeDtypeStruct((HOURS + 8, count), F32),
        compiler_params=params(),
        name="send",
        cost_estimate=SMALL,
    )(incidence, field, row_gauge.reshape(1, count), gauge_kernel.reshape(1, rows))


def hot_rows(gauge, first, rows):
    mine = (lax.broadcasted_iota(jnp.int32, (rows, gauge.shape[1]), 0) + first).astype(F32)
    return jnp.where(gauge == mine, 1.0, 0.0).astype(BF16)


def spread_kernel(first_ref, mine_ref, other_ref, *out_refs):
    rows = out_refs[0].shape[1]
    both = jnp.concatenate([mine_ref[...], other_ref[...]], axis=1)
    stacked = jnp.concatenate(pieces(both[:HOURS], 3), axis=0)
    for m, out_ref in enumerate(out_refs):
        hot = hot_rows(both[HOURS : HOURS + 1], first_ref[m], rows)
        result = lax.dot_general(stacked, hot, (((1,), (1,)), ((), ())), preferred_element_type=F32)
        out_ref[...] = (result[2 * HOURS :] + result[HOURS : 2 * HOURS]) + result[:HOURS]


def spread(first, parcels, rows):
    return pl.pallas_call(
        spread_kernel,
        in_specs=[pl.BlockSpec(memory_space=pltpu.SMEM)] + [pl.BlockSpec(memory_space=pltpu.VMEM)] * 2,
        out_shape=[jax.ShapeDtypeStruct((HOURS, rows), F32)] * 4,
        compiler_params=params(),
        name="spread",
        cost_estimate=SMALL,
    )(first, *parcels)


def plane_couple_kernel(last, first_ref, *refs):
    if last:
        a_ref, b_ref, before_ref, high_ref, low_ref, total_ref, meta_ref = refs
        total_ref[...] = before_ref[...]
    else:
        a_ref, b_ref, total_ref, meta_ref = refs
        total_ref[...] = jnp.zeros_like(total_ref)
    height, double = a_ref.shape
    slots = height - 8
    count = double // 2
    cols, rows = total_ref.shape
    tile = 256
    for i, ref in enumerate((a_ref, b_ref)):
        for j in range(2):
            meta_ref[2 * i + j] = ref[:, j * count : (j + 1) * count]
    row = lax.broadcasted_iota(jnp.int32, (tile, tile), 0)
    col = lax.broadcasted_iota(jnp.int32, (tile, tile), 1)
    same = row // slots == col // slots

    def body(i, carry):
        gauge = meta_ref[i, slots : slots + 1, :]
        near = []
        for j in range(count // tile):
            here = slice(j * tile, (j + 1) * tile)
            block = jnp.concatenate([meta_ref[i, :slots, here]] * (tile // slots), axis=0)
            block = jnp.where(same, block, 0.0).astype(BF16)
            mine = jnp.concatenate(
                [hot_rows(gauge[:, here], first_ref[4 + h], rows // 2) for h in range(2)], axis=0
            )
            near.append(
                lax.dot_general(block, mine, (((1,), (1,)), ((), ())), preferred_element_type=F32)
            )
        near = jnp.concatenate(near, axis=0)
        high = near.astype(BF16)
        rest = near - high.astype(F32)
        hot = jnp.concatenate([hot_rows(gauge, first_ref[m], cols // 4) for m in range(4)], axis=0)
        total_ref[...] += dot(hot, high)

        @pl.when(jnp.max(jnp.abs(rest)) > 0.0)
        def _():
            total_ref[...] += dot(hot, rest.astype(BF16))

        return carry

    lax.fori_loop(0, 4, body, 0)
    if last:
        high, low = pieces(total_ref[...], 2)
        high_ref[...] = high
        low_ref[...] = low


def plane_couple(first, metas, rows, before=None):
    height, double = metas[0].shape
    shape = (4 * rows, 2 * rows)
    last = before is not None
    args = [first, *metas] + ([before] if last else [])
    scratch = [pltpu.VMEM((4, height, double // 2), F32)]
    return pl.pallas_call(
        functools.partial(plane_couple_kernel, last),
        in_specs=[pl.BlockSpec(memory_space=pltpu.SMEM)]
        + [pl.BlockSpec(memory_space=pltpu.VMEM)] * (len(args) - 1),
        out_shape=[jax.ShapeDtypeStruct(shape, BF16)] * 2 if last else jax.ShapeDtypeStruct(shape, F32),
        scratch_shapes=([pltpu.VMEM(shape, F32)] if last else []) + scratch,
        compiler_params=params(),
        name="plane_couple",
        cost_estimate=pl.CostEstimate(
            flops=2 * 2 * double * 8 * rows * rows, bytes_accessed=2_000_000, transcendentals=0
        ),
    )(*args)


def plane_mix_kernel(high_ref, low_ref, a_ref, b_ref, c_ref, d_ref, *refs):
    *extra, mine_ref, other_ref = refs
    refs = (a_ref, b_ref, c_ref, d_ref)
    height, rows = a_ref.shape
    body = pl.ds(0, HOURS)
    one, two = pieces(jnp.concatenate([ref[body, :] for ref in refs], axis=1), 2)
    both = dot(jnp.concatenate([two, one], axis=0), high_ref[...])
    result = (both[:HOURS] + dot(one, low_ref[...])) + both[HOURS:]
    mine_ref[body, :] = result[:, :rows]
    other_ref[body, :] = result[:, rows:]
    if height > HOURS:
        tail = pl.ds(HOURS, NOTE)
        note = sum(ref[tail, :] for ref in refs)
        mine_ref[tail, :] = note
        other_ref[tail, :] = note
    for ref in extra:
        other_ref[pl.ds(height, ref.shape[0]), :] = ref[...]


def plane_mix(coupling, values, extra):
    height, rows = values[0].shape
    return pl.pallas_call(
        plane_mix_kernel,
        out_shape=[
            jax.ShapeDtypeStruct((height, rows), F32),
            jax.ShapeDtypeStruct((height + sum(value.shape[0] for value in extra), rows), F32),
        ],
        compiler_params=params(),
        name="plane_mix",
        cost_estimate=SMALL,
    )(*coupling, *values, *extra)


def plane_rows_kernel(first_ref, meta_ref, meta_other_ref, a_ref, b_ref, c_ref, d_ref, *refs):
    if len(refs) > 2:
        *stack, last_ref, beside_ref, mine_ref, other_ref, stack_ref = refs
    else:
        mine_ref, other_ref = refs
    rows = a_ref.shape[1]
    value = jnp.concatenate([ref[pl.ds(0, HOURS), :] for ref in (a_ref, b_ref, c_ref, d_ref)], axis=1)
    one, two = pieces(value, 2)
    stacked = jnp.concatenate([two, one], axis=0)
    picked = []
    for ref in (meta_ref, meta_other_ref):
        gauge = ref[0:1, :]
        hot = jnp.concatenate([hot_rows(gauge, first_ref[m], rows) for m in range(4)], axis=0)
        both = dot(stacked, hot)
        picked.append(both[:HOURS] + both[HOURS:])
    mine_ref[...] = picked[0]
    count = picked[1].shape[1] // rows
    for i in range(count):
        other_ref[pl.ds(i * HOURS, HOURS), :] = picked[1][:, i * rows : (i + 1) * rows]
    if len(refs) > 2:
        top = stack_ref.shape[0] - HOURS
        for ref in stack:
            stack_ref[pl.ds(0, top), :] = ref[...]
        for i in range(count):
            here = pl.ds(i * rows, rows)
            beside = beside_ref[pl.ds(beside_ref.shape[0] - (count - i) * HOURS, HOURS), :]
            stack_ref[pl.ds(top, HOURS), here] = last_ref[:, here] + beside


def plane_rows(first, metas, values, before):
    rows = values[0].shape[1]
    slots = metas[0].shape[1]
    args = [first, *metas, *values, *before]
    shapes = [(HOURS, slots), (slots // rows * HOURS, rows)]
    if before:
        shapes.append(((len(before) - 1) * HOURS, slots))
    return pl.pallas_call(
        plane_rows_kernel,
        in_specs=[pl.BlockSpec(memory_space=pltpu.SMEM)]
        + [pl.BlockSpec(memory_space=pltpu.VMEM)] * (len(args) - 1),
        out_shape=[jax.ShapeDtypeStruct(shape, F32) for shape in shapes],
        compiler_params=params(),
        name="plane_rows",
        cost_estimate=pl.CostEstimate(flops=1_000_000_000, bytes_accessed=2_000_000, transcendentals=0),
    )(*args)


def gain(kernels):
    return jnp.max(jnp.sum(kernels, axis=1, keepdims=True), axis=0, keepdims=True)


def spectra(kind, kernels, wide):
    classes = kernels.shape[0]
    row = lax.broadcasted_iota(jnp.int32, (classes, kind.shape[1]), 0).astype(F32)
    hot = jnp.where(row == kind, 1.0, 0.0).astype(BF16)
    taps = jnp.transpose(kernels / gain(kernels))
    chosen = dot(jnp.concatenate(pieces(taps, 3)[::-1], axis=1), jnp.concatenate([hot] * 3, axis=0))
    return product(wide, chosen, 3)


def plane_spectrum_kernel(class_ref, kernels_ref, wide_ref, out_ref):
    kind = class_ref[1:2, : out_ref.shape[1]]
    out_ref[...] = spectra(kind, kernels_ref[...], wide_ref[...])


def plane_spectrum(meta, kernels, wide, rows):
    return pl.pallas_call(
        plane_spectrum_kernel,
        out_shape=jax.ShapeDtypeStruct((SPAN, rows), F32),
        compiler_params=params(),
        name="plane_spectrum",
        cost_estimate=SMALL,
    )(meta, kernels, wide)


def sides(even, pair, middle):
    return jnp.where(even, middle, pair), jnp.where(even, pair, middle)


def plane_call(kernel, name, shapes, flags, args):
    return pl.pallas_call(
        kernel,
        in_specs=[pl.BlockSpec(memory_space=pltpu.SMEM)] * len(flags)
        + [pl.BlockSpec(memory_space=pltpu.VMEM)] * len(args),
        out_shape=[jax.ShapeDtypeStruct(shape, F32) for shape in shapes],
        compiler_params=params(),
        name=name,
        cost_estimate=SMALL,
    )(*flags, *args)


def plane_first_kernel(
    flag_ref, here_ref, pair_ref, middle_ref, seen_ref, spec_ref, kernels_ref, forward, first, last, out_ref
):
    spec = spec_ref[...]
    before, after = sides(flag_ref[0] > 0.5, pair_ref[...], middle_ref[...])
    now, later = plane_delayed(before, here_ref[...], after, spec, forward[...], last[...], 3)
    known = plane_advanced(now, later * flag_ref[1], spec, forward[...], first[...], 3)
    out_ref[...] = seen_ref[...] - known * gain(kernels_ref[...])


def plane_delay_kernel(flag_ref, here_ref, pair_ref, middle_ref, spec_ref, forward, last, out_ref):
    body = pl.ds(0, HOURS)
    before, after = sides(flag_ref[0] > 0.5, pair_ref[body, :], middle_ref[body, :])
    out = plane_delayed(before, here_ref[body, :], after, spec_ref[...], forward[...], last[...], 2)
    for i in range(2):
        out_ref[pl.ds(i * HOURS, HOURS), :] = out[i]


def write_note(ref, rows):
    tail = [jnp.zeros((NOTE - len(rows), ref.shape[1]), F32)]
    ref[pl.ds(HOURS, NOTE), :] = jnp.concatenate(rows + tail, axis=0)


def plane_open_kernel(
    flag_ref, here_ref, pair_ref, middle_ref, pulled_ref, spec_ref, forward, first, last, out_ref, delayed_ref
):
    here = here_ref[...]
    spec = spec_ref[...]
    before, after = sides(flag_ref[0] > 0.5, pair_ref[...], middle_ref[...])
    now, later = plane_delayed(before, here, after, spec, forward[...], last[...], 2)
    out_ref[pl.ds(0, HOURS), :] = plane_advanced(now, later * flag_ref[1], spec, forward[...], first[...], 2)
    write_note(out_ref, [lanes(pulled_ref[...], here), lanes(now, now)])
    delayed_ref[pl.ds(0, HOURS), :] = now
    delayed_ref[pl.ds(HOURS, HOURS), :] = later


def plane_step_kernel(
    flag_ref,
    here_ref,
    pair_ref,
    two_ref,
    mirror_ref,
    pulled_ref,
    delayed_ref,
    old_z_ref,
    old_s_ref,
    old_delayed_ref,
    spec_ref,
    forward,
    first,
    total_ref,
    out_ref,
    kept_ref,
):
    tail, body = pl.ds(HOURS, NOTE), pl.ds(0, HOURS)
    total_ref[...] = (here_ref[tail, :] + pair_ref[tail, :]) + (two_ref[...] + mirror_ref[...])
    inverse = total(total_ref, 0) / total(total_ref, 1)
    z = pulled_ref[body, :] * inverse - old_z_ref[...]
    s = here_ref[body, :] * inverse - old_s_ref[...]
    both = delayed_ref[...] * inverse - old_delayed_ref[...]
    now, later = both[:HOURS], both[HOURS:]
    following = plane_advanced(now, later * flag_ref[1], spec_ref[...], forward[...], first[...], 2)
    out_ref[body, :] = following * inverse
    write_note(out_ref, [lanes(z, s), lanes(now, now)])
    for i, value in enumerate((z, s, now)):
        kept_ref[pl.ds(i * HOURS, HOURS), :] = value


def plane_close_kernel(
    here_ref, before_ref, pulled_ref, kept_ref, old_z_ref, old_s_ref, old_delayed_ref, spec_ref, forward, last, out_ref
):
    body = pl.ds(0, HOURS)
    here, raw = here_ref[body, :], pulled_ref[body, :]
    waves = product(forward[...], jnp.concatenate([before_ref[body, :], here], axis=0), 2)
    now = product(last[...], turn(waves, spec_ref[...], 1.0), 2)
    z, s, delayed = (kept_ref[pl.ds(i * HOURS, HOURS), :] for i in range(3))
    note = [pulled_ref[HOURS + i : HOURS + i + 1, :] for i in range(2)]
    for left in (raw, z, old_z_ref[...]):
        note += [lanes(left, right) for right in (here, s, old_s_ref[...])]
    parts = (now, delayed, old_delayed_ref[body, :])
    for i in range(3):
        note += [lanes(parts[i], parts[j]) for j in range(i, 3)]
    note.append(jnp.zeros((24 - len(note), here.shape[1]), F32))
    note = jnp.sum(jnp.concatenate(note, axis=0), axis=1, keepdims=True)
    shape = (24, out_ref.shape[2])
    row, col = (lax.broadcasted_iota(jnp.int32, shape, i) for i in range(2))
    note = jnp.sum(jnp.where(row == col, jnp.broadcast_to(note, shape), 0.0), axis=0, keepdims=True)
    out_ref[...] = jnp.broadcast_to(note[None], out_ref.shape)


def plane_weights(open_ref, close, scale):
    entry = lambda i: close[:, i : i + 1]
    n1, t1 = total(open_ref, 0), total(open_ref, 1)
    n2, t2 = entry(0), entry(1)
    a1 = t1 / n1
    a2, r2 = (t2 / n2) / a1, n2 / n1
    plain = (1.0, -a2, -r2)
    n3 = sum(plain[i] * plain[j] * entry(2 + 3 * i + j) for i in range(3) for j in range(3))
    pairs = [(i, j) for i in range(3) for j in range(i, 3)]
    t3 = sum(
        plain[i] * plain[j] * entry(11 + n) * (1.0 if i == j else 2.0) for n, (i, j) in enumerate(pairs)
    )
    a3, r3 = (t3 / n3) / a1, n3 / n2
    unit = 1.0 / (a1 * scale)
    c3 = unit / (a3 * (a2 - r2) - r3)
    c2 = -a3 * c3
    c1 = unit - r2 * c2
    step = c2 - c3 * a2
    return c1 - step - c3 * r2, step / a1, c3


def plane_combine_kernel(open_ref, close_ref, kernels_ref, stack_ref, mine_ref, beside_ref, out_ref):
    rows = open_ref.shape[1]
    close = jnp.sum(close_ref[...], axis=0)[0:1, :]
    e0, e1, e2 = plane_weights(open_ref, close, gain(kernels_ref[...]))
    for i in range(out_ref.shape[0] // rows):
        here = pl.ds(i * rows, rows)
        last = mine_ref[:, here] + beside_ref[pl.ds(i * HOURS, HOURS), :]
        value = stack_ref[pl.ds(0, HOURS), here] * e0 + stack_ref[pl.ds(HOURS, HOURS), here] * e1 + last * e2
        out_ref[here, :] = jnp.transpose(value)


def plane_finish_kernel(rows_ref, inc_ref, field_ref, out_ref):
    blocks, slots, width = inc_ref.shape
    weights = inc_ref[...].astype(F32).astype(BF16)
    for b in range(blocks):
        here = pl.ds(b * width, width)
        rows = jnp.concatenate(pieces(rows_ref[pl.ds(b * slots, slots), :], 2), axis=0)
        twice = jnp.concatenate([weights[b]] * 2, axis=0)
        added = lax.dot_general(twice, rows, (((0,), (0,)), ((), ())), preferred_element_type=F32)
        out_ref[here, :] = field_ref[here, :] + added


def plane_finish(rows, incidence, field):
    blocks, slots, width = incidence.shape
    hours = field.shape[1]
    step = 8
    return pl.pallas_call(
        plane_finish_kernel,
        grid=(blocks // step,),
        in_specs=[
            pl.BlockSpec((step * slots, hours), lambda i: (i, 0)),
            pl.BlockSpec((step, slots, width), lambda i: (i, 0, 0)),
            pl.BlockSpec((step * width, hours), lambda i: (i, 0)),
        ],
        out_specs=pl.BlockSpec((step * width, hours), lambda i: (i, 0)),
        out_shape=jax.ShapeDtypeStruct(field.shape, F32),
        compiler_params=params(),
        name="plane_finish",
    )(rows, incidence, field)


def plane_shards(incidence, row_gauge, gauge_kernel, kernels, observed, first_guess):
    rows, hours = observed.shape
    basin, tm = lax.axis_index("basin"), lax.axis_index("tm")
    z, x, y, c = basin // X_, basin % X_, tm // C_, tm % C_
    place = 2 * y + x
    first = jnp.stack([4 * c + (place ^ m) for m in range(4)] + [4 * c + place, 4 * (1 - c) + place])
    first = (first * rows).astype(jnp.int32)
    flags = jnp.stack([1 - z % 2, (z < Z_ - 1).astype(z.dtype), (z > 0).astype(z.dtype)]).astype(F32)
    forward, inverse_first, inverse_last, _ = turned_transforms(2)
    forward3, inverse_first3, inverse_last3, short3 = turned_transforms(3)
    block, noted = (hours, rows), (hours + NOTE, rows)

    parcel = send(incidence, first_guess, row_gauge, gauge_kernel)
    parcel, near, kinds, seen = lax.optimization_barrier((parcel, incidence, gauge_kernel, observed))
    parcel = moved(parcel, to_plane)
    behind = describe(
        near, seen, moved(seen, hour_before), kinds, kernels, short3, [forward3, inverse_first3]
    )
    behind = moved(behind, to_plane)
    parcels = [parcel, moved(parcel, over_core)]
    parcels[1], behind = lax.optimization_barrier((parcels[1], behind))
    dense = spread(first, parcels, rows)
    slots = incidence.shape[1]
    gram, seen = behind[:slots], behind[slots:]
    seen = jnp.concatenate([seen[:, i : i + rows] for i in range(0, seen.shape[1], rows)], axis=0)
    metas = [value[hours:] for value in parcels]
    spec = plane_spectrum(metas[0], kernels, short3, rows)
    sums = dense[0] + sum(moved(value, where) for value, where in zip(dense[1:], SQUARE))
    sums = [sums, moved(sums, z_pair), moved(sums, z_middle)]
    both = jnp.concatenate([gram, moved(gram, over_core)], axis=1)
    both = jnp.concatenate([both, jnp.concatenate(metas, axis=1)], axis=0)
    around = [both] + [moved(both, where) for where in SQUARE]
    coupled = plane_couple(first, around[:2], rows)
    coupled, sums = lax.optimization_barrier((coupled, sums))
    coupling = plane_couple(first, around[2:], rows, coupled)
    (pulled0,) = plane_call(
        plane_first_kernel,
        "plane_first",
        [block],
        [flags],
        [*sums, seen, spec, kernels, forward3, inverse_first3, inverse_last3],
    )

    def mixing(pulled, extra):
        values = [pulled] + [moved(pulled, where) for where in SQUARE]
        mine, other = plane_mix(coupling, values, extra)
        beside = moved(other, over_core)
        return values, mine + beside[: pulled.shape[0]], beside

    values, mixed0, _ = mixing(pulled0, [])
    picked, theirs = plane_rows(first, metas, values, [])
    sums = [mixed0, moved(mixed0, z_pair), moved(mixed0, z_middle)]
    pulled1, delayed0 = plane_call(
        plane_open_kernel,
        "plane_open",
        [noted, (2 * hours, rows)],
        [flags],
        [*sums, pulled0, spec, forward, inverse_first, inverse_last],
    )

    values, mixed1, beside = mixing(pulled1, [theirs])
    picked, theirs, stack = plane_rows(first, metas, values, [picked, beside])
    sums = [mixed1, moved(mixed1, z_pair), moved(mixed1, z_middle)]
    two, mirror = moved(mixed1[hours:], z_two), moved(mixed1[hours:], z_mirror)
    (delayed1,) = plane_call(
        plane_delay_kernel, "plane_delay", [(2 * hours, rows)], [flags], [*sums, spec, forward, inverse_last]
    )
    open_note, pulled2, kept = plane_call(
        plane_step_kernel,
        "plane_step",
        [(NOTE, rows), noted, (3 * hours, rows)],
        [flags],
        [*sums[:2], two, mirror, pulled1, delayed1, pulled0, mixed0, delayed0, spec, forward, inverse_first],
    )

    values, mixed2, beside = mixing(pulled2, [theirs])
    picked, theirs, stack = plane_rows(first, metas, values, [stack, picked, beside])
    (note,) = plane_call(
        plane_close_kernel,
        "plane_close",
        [(Z_ * X_ * Y_ * C_, 8, rows // 2)],
        [],
        [mixed2, moved(mixed2, z_next), pulled2, kept, pulled0, mixed0, delayed0, spec, forward, inverse_last],
    )
    close_note = lax.all_to_all(note, ("basin", "tm"), 0, 0, tiled=False)
    (answer,) = plane_call(
        plane_combine_kernel,
        "plane_combine",
        [(parcel.shape[1], hours)],
        [],
        [open_note, close_note, kernels, stack, picked, moved(theirs, over_core)],
    )
    return plane_finish(moved(answer, from_plane), incidence, first_guess)


def solution(mesh):
    planes = dict(mesh.shape) == {"basin": Z_ * X_, "tm": Y_ * C_}
    in_specs = (
        P("basin", None, None),
        P("basin"),
        P("basin"),
        P(),
        P("basin", "tm"),
        P("basin", "tm"),
    )
    return jax.shard_map(
        plane_shards if planes else shards, mesh=mesh, in_specs=in_specs, out_specs=P("basin", "tm"), check_vma=False
    )
```

```python
import functools

import jax
import jax.numpy as jnp
import numpy as np
from jax import lax
from jax.experimental import pallas as pl
from jax.experimental.pallas import tpu as pltpu
from jax.sharding import PartitionSpec as P

F32 = jnp.float32
BF16 = jnp.bfloat16
HIGH = lax.Precision.HIGHEST
SPAN = 256
MIB = 1024 * 1024


SMALL = pl.CostEstimate(flops=1, bytes_accessed=1, transcendentals=0)


def params(mib=16):
    return pltpu.CompilerParams(vmem_limit_bytes=mib * MIB)


def transforms():
    half = SPAN // 2
    freq = 2.0 * np.pi * (np.arange(half) + 0.5) / SPAN
    phase = np.arange(SPAN)[:, None] * freq[None, :]
    forward = np.concatenate([np.cos(phase), -np.sin(phase)], axis=1)
    inverse = forward.T * (2.0 / SPAN)
    return (
        jnp.asarray(forward, F32),
        jnp.asarray(inverse[:, :half], F32),
        jnp.asarray(inverse[:, half:], F32),
    )


def dot(a, b):
    return jnp.dot(a, b, preferred_element_type=F32)


def exact(a, b):
    return jnp.dot(a, b, precision=HIGH, preferred_element_type=F32)


def pieces(value, count):
    out = []
    for _ in range(count):
        piece = value.astype(BF16)
        out.append(piece)
        value = value - piece.astype(F32)
    return out


def pick(hot, value):
    return sum(dot(hot, piece) for piece in pieces(value, 3))


def prepare_kernel(inc_ref, field_ref, partial_ref, gram_ref):
    blocks, slots, width = inc_ref.shape
    rows = blocks * slots
    weights = inc_ref[...].astype(F32).astype(BF16)
    for b in range(blocks):
        value = field_ref[pl.ds(b * width, width), :]
        partial_ref[pl.ds(b * slots, slots), :] = pick(weights[b], value)
    flat = weights.reshape(rows, width)
    full = lax.dot_general(flat, flat, (((1,), (1,)), ((), ())), preferred_element_type=F32)
    row = lax.broadcasted_iota(jnp.int32, (rows, rows), 0)
    col = lax.broadcasted_iota(jnp.int32, (rows, rows), 1)
    own = jnp.where(row // slots == col // slots, full, 0.0)
    gram_ref[...] = jnp.sum(own.reshape(blocks, slots, rows), axis=0)


def prepare(incidence, field):
    blocks, slots, width = incidence.shape
    hours = field.shape[1]
    step = 8
    return pl.pallas_call(
        prepare_kernel,
        grid=(blocks // step,),
        in_specs=[
            pl.BlockSpec((step, slots, width), lambda i: (i, 0, 0)),
            pl.BlockSpec((step * width, hours), lambda i: (i, 0)),
        ],
        out_specs=[
            pl.BlockSpec((step * slots, hours), lambda i: (i, 0)),
            pl.BlockSpec((slots, step * slots), lambda i: (0, i)),
        ],
        out_shape=[
            jax.ShapeDtypeStruct((blocks * slots, hours), F32),
            jax.ShapeDtypeStruct((slots, blocks * slots), F32),
        ],
        compiler_params=params(56),
        name="prepare",
    )(incidence, field)


def table_kernel(gauge_ref, partial_ref, out_ref):
    slots = partial_ref.shape[0]
    rows = out_ref.shape[0]
    first = pl.program_id(0) * rows
    gauge = lax.broadcasted_iota(jnp.int32, (rows, slots), 0) + first
    hot = jnp.where(gauge_ref[...] == gauge, 1.0, 0.0).astype(BF16)
    out_ref[...] = pick(hot, partial_ref[...])


def table(row_gauge, partial, gauges):
    slots, hours = partial.shape
    step = 256
    return pl.pallas_call(
        table_kernel,
        grid=(gauges // step,),
        in_specs=[
            pl.BlockSpec((1, slots), lambda i: (0, 0)),
            pl.BlockSpec((slots, hours), lambda i: (0, 0)),
        ],
        out_specs=pl.BlockSpec((step, hours), lambda i: (i, 0)),
        out_shape=jax.ShapeDtypeStruct((gauges, hours), F32),
        compiler_params=params(56),
        name="table",
    )(row_gauge.reshape(1, slots), partial)


def couple_kernel(first_ref, lane_ref, sub_ref, gram_ref, high_ref, low_ref, near_ref):
    slots = gram_ref.shape[0]
    count = lane_ref.shape[1]
    rows, cols = high_ref.shape
    tile = 256
    first = first_ref[0]

    @pl.when(pl.program_id(0) == 0)
    def _():
        row = lax.broadcasted_iota(jnp.int32, (tile, tile), 0)
        col = lax.broadcasted_iota(jnp.int32, (tile, tile), 1)
        same = row // slots == col // slots
        mine = lax.broadcasted_iota(jnp.int32, (rows, tile), 0) + first

        def body(i, carry):
            here = pl.ds(pl.multiple_of(i * tile, tile), tile)
            block = jnp.concatenate([gram_ref[:, here]] * (tile // slots), axis=0)
            block = jnp.where(same, block, 0.0).astype(BF16)
            hot = jnp.where(lane_ref[:, here] == mine, 1.0, 0.0).astype(BF16)
            near_ref[:, here] = dot(hot, block)
            return carry

        lax.fori_loop(0, count // tile, body, 0)

    def chunk(i, total):
        here = pl.ds(pl.multiple_of(i * 1024, 1024), 1024)
        gauge = lax.broadcasted_iota(jnp.int32, (1024, cols), 1) + pl.program_id(0) * cols
        hot = jnp.where(sub_ref[here, :] == gauge, 1.0, 0.0).astype(BF16)
        near = near_ref[:, here]
        high = near.astype(BF16)
        low = (near - high.astype(F32)).astype(BF16)
        return total + dot(high, hot) + dot(low, hot)

    total = lax.fori_loop(0, count // 1024, chunk, jnp.zeros((rows, cols), F32))
    high, low = pieces(total, 2)
    high_ref[...] = high
    low_ref[...] = low


def couple(first, row_gauge, gram, rows, gauges):
    count = row_gauge.shape[0]
    step = 256
    return pl.pallas_call(
        couple_kernel,
        grid=(gauges // step,),
        in_specs=[
            pl.BlockSpec(memory_space=pltpu.SMEM),
            pl.BlockSpec((1, count), lambda i: (0, 0)),
            pl.BlockSpec((count, 1), lambda i: (0, 0)),
            pl.BlockSpec(gram.shape, lambda i: (0, 0)),
        ],
        out_specs=[pl.BlockSpec((rows, step), lambda i: (0, i))] * 2,
        out_shape=[jax.ShapeDtypeStruct((rows, gauges), BF16)] * 2,
        scratch_shapes=[pltpu.VMEM((rows, count), F32)],
        compiler_params=params(56),
        name="couple",
    )(first, row_gauge.reshape(1, count), row_gauge.reshape(count, 1), gram)


def mix_kernel(high_ref, low_ref, value_ref, out_ref):
    high = high_ref[...]
    low = low_ref[...]
    one, two, three = pieces(value_ref[...], 3)
    out_ref[...] = (dot(high, three) + dot(low, two)) + (dot(high, two) + dot(low, one)) + dot(high, one)


def mix(high, low, value):
    return pl.pallas_call(
        mix_kernel,
        out_shape=jax.ShapeDtypeStruct((high.shape[0], value.shape[1]), F32),
        compiler_params=params(56),
        name="mix",
    )(high, low, value)


def spectrum_kernel(class_ref, kernels_ref, forward_ref, out_ref):
    rows = class_ref.shape[0]
    classes, taps = kernels_ref.shape
    kind = lax.broadcasted_iota(jnp.int32, (rows, classes), 1)
    hot = jnp.where(class_ref[...] == kind, 1.0, 0.0)
    out_ref[...] = exact(exact(hot, kernels_ref[...]), forward_ref[pl.ds(0, taps), :])


def spectrum(gauge_kernel, kernels, forward):
    rows = gauge_kernel.shape[0]
    return pl.pallas_call(
        spectrum_kernel,
        out_shape=jax.ShapeDtypeStruct((rows, SPAN), F32),
        compiler_params=params(56),
        name="spectrum",
    )(gauge_kernel.reshape(rows, 1), kernels, forward)


def delayed(before, here, after, spec, forward, inverse_last):
    rows, half = here.shape
    stacked = jnp.concatenate(
        [jnp.concatenate([before, here], axis=1), jnp.concatenate([here, after], axis=1)], axis=0
    )
    waves = exact(stacked, forward)
    real, imag = waves[:, :half], waves[:, half:]
    kr = jnp.concatenate([spec[:, :half]] * 2, axis=0)
    ki = jnp.concatenate([spec[:, half:]] * 2, axis=0)
    turned = jnp.concatenate([real * kr - imag * ki, real * ki + imag * kr], axis=1)
    out = exact(turned, inverse_last)
    return out[:rows], out[rows:]


def advanced(here, after, spec, forward, inverse_first):
    half = here.shape[1]
    waves = exact(jnp.concatenate([here, after], axis=1), forward)
    real, imag = waves[:, :half], waves[:, half:]
    kr, ki = spec[:, :half], spec[:, half:]
    turned = jnp.concatenate([real * kr + imag * ki, imag * kr - real * ki], axis=1)
    return exact(turned, inverse_first)


def lanes(a, b):
    return jnp.sum(a * b, axis=0, keepdims=True)


def total(ref, row):
    return jnp.sum(ref[row : row + 1, :], axis=1, keepdims=True)


def ratios(ref):
    square = total(ref, 0)
    alpha = jnp.sqrt(square)
    beta = jnp.sqrt(jnp.maximum(total(ref, 1) / square - 2.0 * total(ref, 2) + square, 0.0))
    return alpha, beta


def first_kernel(
    more_ref, sums_ref, observed_ref, spec_ref, forward_ref, first_ref, last_ref, out_ref, note_ref
):
    rows, half = observed_ref.shape[0] // 2, observed_ref.shape[1]
    spec, forward = spec_ref[...], forward_ref[...]
    before, here, after = (sums_ref[pl.ds(i * rows, rows), :] for i in range(3))
    now, later = delayed(before, here, after, spec, forward, last_ref[...])
    start = observed_ref[pl.ds(0, rows), :] - now
    start_later = (observed_ref[pl.ds(rows, rows), :] - later) * more_ref[0]
    out_ref[...] = advanced(start, start_later, spec, forward, first_ref[...])
    note_ref[...] = jnp.concatenate([lanes(start, start), jnp.zeros((7, half), F32)], axis=0)


def first_step(more, sums, observed, spec, mats):
    rows, half = spec.shape[0], observed.shape[1]
    return pl.pallas_call(
        first_kernel,
        in_specs=[pl.BlockSpec(memory_space=pltpu.SMEM)] + [pl.BlockSpec(memory_space=pltpu.VMEM)] * 6,
        out_shape=[jax.ShapeDtypeStruct((rows, half), F32), jax.ShapeDtypeStruct((8, half), F32)],
        compiler_params=params(56),
        name="first_step",
    )(more, sums, observed, spec, *mats)


def step_kernel(
    opening,
    final,
    more_ref,
    note_ref,
    sums_ref,
    spec_ref,
    forward_ref,
    first_ref,
    last_ref,
    pulled_ref,
    *refs,
):
    if opening:
        state_ref = None
    else:
        state_ref, *refs = refs
    if final:
        (out_note_ref,) = refs
    else:
        new_ref, out_ref, out_note_ref = refs
    rows, half = pulled_ref.shape
    spec, forward = spec_ref[...], forward_ref[...]
    if opening:
        scale = 1.0 / jnp.sqrt(total(note_ref, 0))
        along = sums_ref[...] * scale
        new_s, new_su = along, along
        new_zu = pulled_ref[...] * scale
        new_z = new_zu
    else:
        alpha, beta = ratios(note_ref)
        a, b, g = 1.0 / (alpha * beta), alpha / beta, beta / alpha
        wide = pl.ds(0, 3 * rows), pl.ds(3 * rows, 3 * rows)
        new_su = sums_ref[...] * a - state_ref[wide[1], :] * b
        new_s = new_su - state_ref[wide[0], :] * g
        new_zu = pulled_ref[...] * a - state_ref[pl.ds(7 * rows, rows), :] * b
        new_z = new_zu - state_ref[pl.ds(6 * rows, rows), :] * g
    before, here, after = (new_s[i * rows : (i + 1) * rows] for i in range(3))
    now, later = delayed(before, here, after, spec, forward, last_ref[...])
    out_note_ref[...] = jnp.concatenate(
        [lanes(new_z, here), lanes(now, now), lanes(new_zu, here), jnp.zeros((5, half), F32)], axis=0
    )
    if not final:
        new_ref[pl.ds(0, 3 * rows), :] = new_s
        new_ref[pl.ds(3 * rows, 3 * rows), :] = new_su
        new_ref[pl.ds(6 * rows, rows), :] = new_z
        new_ref[pl.ds(7 * rows, rows), :] = new_zu
        out_ref[...] = advanced(now, later * more_ref[0], spec, forward, first_ref[...])


def next_step(more, note, sums, spec, mats, pulled, state, final):
    rows, half = pulled.shape
    opening = state is None
    shapes = [
        jax.ShapeDtypeStruct((8 * rows, half), F32),
        jax.ShapeDtypeStruct((rows, half), F32),
        jax.ShapeDtypeStruct((8, half), F32),
    ]
    args = [more, note, sums, spec, *mats, pulled] + ([] if opening else [state])
    return pl.pallas_call(
        functools.partial(step_kernel, opening, final),
        in_specs=[pl.BlockSpec(memory_space=pltpu.SMEM)]
        + [pl.BlockSpec(memory_space=pltpu.VMEM)] * (len(args) - 1),
        out_shape=shapes[2:] if final else shapes,
        compiler_params=params(56),
        name="next_step",
    )(*args)


def weights_of(notes):
    start = jnp.sqrt(total(notes[0], 0))
    zero = jnp.zeros_like(start)
    units = [1.0 / start, zero, zero]
    z, zu = list(units), list(units)
    phibar = start
    alpha, beta = ratios(notes[1])
    rhobar = alpha
    w = [value / alpha for value in z]
    result = [zero] * 3
    steps = len(notes) - 1
    for k in range(steps):
        rho = jnp.sqrt(rhobar * rhobar + beta * beta)
        cosine, sine = rhobar / rho, beta / rho
        phi, phibar = cosine * phibar, sine * phibar
        result = [r + phi / rho * value for r, value in zip(result, w)]
        if k < steps - 1:
            a, b, g = 1.0 / (alpha * beta), alpha / beta, beta / alpha
            zu = [(a if i == k + 1 else 0.0) - b * value for i, value in enumerate(zu)]
            z = [value - g * old for value, old in zip(zu, z)]
            alpha, beta = ratios(notes[k + 2])
            theta = sine * alpha
            rhobar = -cosine * alpha
            w = [value / alpha - theta / rho * old for value, old in zip(z, w)]
    return result


def finish_kernel(n0, n1, n2, n3, gauge_ref, q0, q1, q2, inc_ref, field_ref, out_ref, rows_ref):
    blocks, slots, width = inc_ref.shape
    count = rows_ref.shape[0]
    gauges = q0.shape[0]
    step = pl.program_id(0)

    @pl.when(step == 0)
    def _():
        e0, e1, e2 = weights_of([n0, n1, n2, n3])
        width_ = 512

        def body(i, value):
            here = pl.ds(pl.multiple_of(i * width_, width_), width_)
            mixed = q0[here, :] * e0 + q1[here, :] * e1 + q2[here, :] * e2
            gauge = lax.broadcasted_iota(jnp.int32, (count, width_), 1) + i * width_
            hot = jnp.where(gauge_ref[...] == gauge, 1.0, 0.0).astype(BF16)
            return value + pick(hot, mixed)

        rows_ref[...] = lax.fori_loop(0, gauges // width_, body, jnp.zeros(rows_ref.shape, F32))

    weights = inc_ref[...].astype(F32).astype(BF16)
    for b in range(blocks):
        here = pl.ds(b * width, width)
        rows = rows_ref[pl.ds(pl.multiple_of((step * blocks + b) * slots, slots), slots), :]
        added = sum(
            lax.dot_general(weights[b], piece, (((0,), (0,)), ((), ())), preferred_element_type=F32)
            for piece in pieces(rows, 3)
        )
        out_ref[here, :] = field_ref[here, :] + added


def finish(notes, row_gauge, gathered, incidence, field):
    blocks, slots, width = incidence.shape
    hours = field.shape[1]
    count = row_gauge.shape[0]
    step = 8
    whole = lambda shape: pl.BlockSpec(shape, lambda i: (0, 0))
    return pl.pallas_call(
        finish_kernel,
        grid=(blocks // step,),
        in_specs=[whole(n.shape) for n in notes]
        + [whole((count, 1))]
        + [whole(q.shape) for q in gathered]
        + [
            pl.BlockSpec((step, slots, width), lambda i: (i, 0, 0)),
            pl.BlockSpec((step * width, hours), lambda i: (i, 0)),
        ],
        out_specs=pl.BlockSpec((step * width, hours), lambda i: (i, 0)),
        out_shape=jax.ShapeDtypeStruct(field.shape, F32),
        scratch_shapes=[pltpu.VMEM((count, hours), F32)],
        compiler_params=params(56),
        name="finish",
    )(*notes, row_gauge.reshape(count, 1), *gathered, incidence, field)


def shifted(value, axis, by):
    devices = lax.axis_size(axis)
    pairs = [(i, i + by) for i in range(devices) if 0 <= i + by < devices]
    return lax.ppermute(value, axis, pairs)


def window(value):
    return jnp.concatenate([shifted(value, "tm", 1), value, shifted(value, "tm", -1)], axis=0)


def gathered_rows(value):
    owners = lax.axis_size("basin")
    copies = jnp.broadcast_to(value[None], (owners,) + value.shape)
    return lax.all_to_all(copies, "basin", 0, 0, tiled=False)


def over_hours(note):
    blocks = lax.axis_size("tm")
    result = note
    for by in range(1, blocks):
        result = result + lax.ppermute(note, "tm", [(i, (i + by) % blocks) for i in range(blocks)])
    return result


def shards(incidence, row_gauge, gauge_kernel, kernels, observed, first_guess):
    owners = lax.axis_size("basin")
    rows, hours = observed.shape
    gauges = rows * owners
    mats = transforms()
    spec = spectrum(gauge_kernel, kernels, mats[0])
    more = (lax.axis_index("tm") < lax.axis_size("tm") - 1).astype(F32).reshape(1)
    partial, gram = prepare(incidence, first_guess)
    all_gram = lax.all_gather(gram, "basin", axis=1, tiled=True)
    all_rows = lax.all_gather(row_gauge, "basin", axis=0, tiled=True)
    dense = table(row_gauge, partial, gauges).reshape(owners, rows, hours)
    sums = jnp.sum(lax.all_to_all(dense, "basin", 0, 0, tiled=False), axis=0)
    both = jnp.concatenate([observed, shifted(observed, "tm", -1)], axis=0)
    first = (lax.axis_index("basin") * rows).astype(jnp.int32).reshape(1)
    high, low = couple(first, all_rows, all_gram, rows, gauges)

    pulled, note = first_step(more, window(sums), both, spec, mats)
    notes, kept, state = [], [], None
    for k in range(3):
        everyone = gathered_rows(jnp.concatenate([pulled, note], axis=0))
        value = everyone[:, :rows].reshape(gauges, hours)
        notes.append(over_hours(jnp.sum(everyone[:, rows:], axis=0)))
        kept.append(value)
        around = window(mix(high, low, value))
        final = k == 2
        result = next_step(more, notes[-1], around, spec, mats, pulled, state, final)
        if final:
            (note,) = result
        else:
            state, pulled, note = result
    notes.append(over_hours(jnp.sum(gathered_rows(note), axis=0)))
    return finish(notes, row_gauge, kept, incidence, first_guess)


Z_, X_, Y_, C_ = 4, 2, 2, 2
NOTE = 8
HOURS = SPAN // 2


def device(z, x, y, c):
    return (z * X_ + x) * (Y_ * C_) + y * C_ + c


def moved(value, where):
    pairs = []
    for z, x, y, c in np.ndindex(Z_, X_, Y_, C_):
        target = where(z, x, y, c)
        if target is not None:
            pairs.append((device(z, x, y, c), device(*target)))
    return lax.ppermute(value, ("basin", "tm"), pairs)


def to_plane(z, x, y, c):
    return 2 * y + c, x, z & 1, z >> 1


def hour_before(z, x, y, c):
    t = 2 * y + c - 1
    return (z, x, t >> 1, t & 1) if t >= 0 else None


def from_plane(z, x, y, c):
    return 2 * c + y, x, z >> 1, z & 1


def over_x(z, x, y, c):
    return z, 1 - x, y, c


def over_y(z, x, y, c):
    return z, x, 1 - y, c


def over_xy(z, x, y, c):
    return z, 1 - x, 1 - y, c


def over_core(z, x, y, c):
    return z, x, y, 1 - c


def z_pair(z, x, y, c):
    return z ^ 1, x, y, c


def z_middle(z, x, y, c):
    return (3 - z, x, y, c) if z in (1, 2) else None


def z_two(z, x, y, c):
    return z ^ 2, x, y, c


def z_mirror(z, x, y, c):
    return 3 - z, x, y, c


def z_next(z, x, y, c):
    return (z + 1, x, y, c) if z < 3 else None


SQUARE = (over_x, over_y, over_xy)


def split_constant(value):
    out = []
    for _ in range(3):
        piece = value.astype(jnp.bfloat16)
        out.append(piece)
        value = value - piece.astype(np.float64)
    return out


ORDERS = {2: ((0, 1), (1, 0), (0, 0)), 3: ((0, 2), (1, 1), (2, 0), (0, 1), (1, 0), (0, 0))}


def widened(mat, order):
    parts = split_constant(mat)
    return jnp.asarray(np.concatenate([parts[i] for i, _ in ORDERS[order]], axis=1))


def product(wide, value, order):
    parts = pieces(value, order)
    return dot(wide, jnp.concatenate([parts[j] for _, j in ORDERS[order]], axis=0))


def turned_transforms(order):
    half = SPAN // 2
    freq = 2.0 * np.pi * (np.arange(half) + 0.5) / SPAN
    phase = freq[:, None] * np.arange(SPAN)[None, :]
    forward = np.concatenate([np.cos(phase), -np.sin(phase)], axis=0)
    inverse = forward.T * (2.0 / SPAN)
    return [widened(mat, order) for mat in (forward, inverse[:half], inverse[half:], forward[:, :half])]


def turn(waves, spec, sign):
    half = waves.shape[0] // 2
    real, imag = waves[:half], waves[half:]
    kr, ki = spec[:half], spec[half:] * sign
    return jnp.concatenate([real * kr - imag * ki, real * ki + imag * kr], axis=0)


def plane_delayed(before, here, after, spec, forward, last, order):
    rows = here.shape[1]
    pairs = [jnp.concatenate(pair, axis=0) for pair in ((before, here), (here, after))]
    waves = product(forward, jnp.concatenate(pairs, axis=1), order)
    turned = [turn(waves[:, i * rows : (i + 1) * rows], spec, 1.0) for i in range(2)]
    out = product(last, jnp.concatenate(turned, axis=1), order)
    return out[:, :rows], out[:, rows:]


def plane_advanced(here, after, spec, forward, first, order):
    waves = product(forward, jnp.concatenate([here, after], axis=0), order)
    return product(first, turn(waves, spec, -1.0), order)


def describe_kernel(inc_ref, gauge_ref, out_ref):
    blocks, slots, width = inc_ref.shape
    tile = 8
    side = tile * slots
    weights = inc_ref[...].astype(F32).astype(BF16)
    row = lax.broadcasted_iota(jnp.int32, (side, side), 0)
    col = lax.broadcasted_iota(jnp.int32, (side, side), 1)
    same = row // slots == col // slots
    for i in range(blocks // tile):
        flat = weights[i * tile : (i + 1) * tile].reshape(side, width)
        full = lax.dot_general(flat, flat, (((1,), (1,)), ((), ())), preferred_element_type=F32)
        own = jnp.where(same, full, 0.0)
        out_ref[pl.ds(0, slots), pl.ds(i * side, side)] = jnp.sum(own.reshape(tile, slots, side), axis=0)
    out_ref[pl.ds(slots, 8), :] = jnp.broadcast_to(gauge_ref[...].astype(F32), (8, blocks * slots))


def describe(incidence, row_gauge):
    blocks, slots, _ = incidence.shape
    count = blocks * slots
    return pl.pallas_call(
        describe_kernel,
        out_shape=jax.ShapeDtypeStruct((slots + 8, count), F32),
        compiler_params=params(),
        name="describe",
        cost_estimate=SMALL,
    )(incidence, row_gauge.reshape(1, count))


def observe_kernel(seen_ref, later_ref, kind_ref, kernels_ref, wide_ref, forward, first, out_ref):
    spec = spectra(kind_ref[...].astype(F32), kernels_ref[...], wide_ref[...])
    here, after = jnp.transpose(seen_ref[...]), jnp.transpose(later_ref[...])
    out_ref[...] = plane_advanced(here, after, spec, forward[...], first[...], 3)


def observe(seen, later, gauge_kernel, kernels, wide, mats):
    rows, hours = seen.shape
    return pl.pallas_call(
        observe_kernel,
        out_shape=jax.ShapeDtypeStruct((hours, rows), F32),
        compiler_params=params(),
        name="observe",
        cost_estimate=SMALL,
    )(seen, later, gauge_kernel.reshape(1, rows), kernels, wide, *mats)


def send_kernel(inc_ref, field_ref, gauge_ref, kind_ref, out_ref):
    blocks, slots, width = inc_ref.shape
    count = blocks * slots
    weights = inc_ref[...].astype(F32).astype(BF16)
    parts = []
    for b in range(blocks):
        value = jnp.concatenate(pieces(field_ref[pl.ds(b * width, width), :], 3)[::-1], axis=0)
        parts.append(dot(jnp.concatenate([weights[b]] * 3, axis=1), value))
    out_ref[pl.ds(0, HOURS), :] = jnp.transpose(jnp.concatenate(parts, axis=0))
    kinds = kind_ref.shape[1] // count
    here = jnp.minimum(pl.program_id(0), kinds - 1) * count
    out_ref[pl.ds(HOURS, 8), :] = jnp.concatenate(
        [
            gauge_ref[...].astype(F32),
            kind_ref[:, pl.ds(pl.multiple_of(here, count), count)].astype(F32),
            jnp.zeros((6, count), F32),
        ],
        axis=0,
    )


def send(incidence, field, row_gauge, gauge_kernel):
    blocks, slots, width = incidence.shape
    count = blocks * slots
    rows = gauge_kernel.shape[0]
    step = 8
    return pl.pallas_call(
        send_kernel,
        grid=(blocks // step,),
        in_specs=[
            pl.BlockSpec((step, slots, width), lambda i: (i, 0, 0)),
            pl.BlockSpec((step * width, HOURS), lambda i: (i, 0)),
            pl.BlockSpec((1, step * slots), lambda i: (0, i)),
            pl.BlockSpec((1, rows), lambda i: (0, 0)),
        ],
        out_specs=pl.BlockSpec((HOURS + 8, step * slots), lambda i: (0, i)),
        out_shape=jax.ShapeDtypeStruct((HOURS + 8, count), F32),
        compiler_params=params(),
        name="send",
        cost_estimate=SMALL,
    )(incidence, field, row_gauge.reshape(1, count), gauge_kernel.reshape(1, rows))


def hot_rows(gauge, first, rows):
    mine = (lax.broadcasted_iota(jnp.int32, (rows, gauge.shape[1]), 0) + first).astype(F32)
    return jnp.where(gauge == mine, 1.0, 0.0).astype(BF16)


def spread_kernel(first_ref, mine_ref, other_ref, *out_refs):
    rows = out_refs[0].shape[1]
    both = jnp.concatenate([mine_ref[...], other_ref[...]], axis=1)
    stacked = jnp.concatenate(pieces(both[:HOURS], 3), axis=0)
    for m, out_ref in enumerate(out_refs):
        hot = hot_rows(both[HOURS : HOURS + 1], first_ref[m], rows)
        result = lax.dot_general(stacked, hot, (((1,), (1,)), ((), ())), preferred_element_type=F32)
        out_ref[...] = (result[2 * HOURS :] + result[HOURS : 2 * HOURS]) + result[:HOURS]


def spread(first, parcels, rows):
    return pl.pallas_call(
        spread_kernel,
        in_specs=[pl.BlockSpec(memory_space=pltpu.SMEM)] + [pl.BlockSpec(memory_space=pltpu.VMEM)] * 2,
        out_shape=[jax.ShapeDtypeStruct((HOURS, rows), F32)] * 4,
        compiler_params=params(),
        name="spread",
        cost_estimate=SMALL,
    )(first, *parcels)


def plane_couple_kernel(last, first_ref, *refs):
    if last:
        all_ref, before_ref, high_ref, low_ref, total_ref, meta_ref = refs
        total_ref[...] = before_ref[...]
    else:
        all_ref, total_ref, meta_ref = refs
        total_ref[...] = jnp.zeros_like(total_ref)
    parts, height, count = meta_ref.shape
    slots = height - 8
    cols, rows = total_ref.shape
    tile = 256
    for i in range(parts):
        meta_ref[i] = all_ref[:, i * count : (i + 1) * count]
    row = lax.broadcasted_iota(jnp.int32, (tile, tile), 0)
    col = lax.broadcasted_iota(jnp.int32, (tile, tile), 1)
    same = row // slots == col // slots

    def body(i, carry):
        gauge = meta_ref[i, slots : slots + 1, :]
        near = []
        for j in range(count // tile):
            here = slice(j * tile, (j + 1) * tile)
            block = jnp.concatenate([meta_ref[i, :slots, here]] * (tile // slots), axis=0)
            block = jnp.where(same, block, 0.0).astype(BF16)
            mine = jnp.concatenate(
                [hot_rows(gauge[:, here], first_ref[4 + h], rows // 2) for h in range(2)], axis=0
            )
            near.append(
                lax.dot_general(block, mine, (((1,), (1,)), ((), ())), preferred_element_type=F32)
            )
        near = jnp.concatenate(near, axis=0)
        high = near.astype(BF16)
        rest = near - high.astype(F32)
        hot = jnp.concatenate([hot_rows(gauge, first_ref[m], cols // 4) for m in range(4)], axis=0)
        total_ref[...] += dot(hot, high)

        @pl.when(jnp.max(jnp.abs(rest)) > 0.0)
        def _():
            total_ref[...] += dot(hot, rest.astype(BF16))

        return carry

    lax.fori_loop(0, parts, body, 0)
    if last:
        high, low = pieces(total_ref[...], 2)
        high_ref[...] = high
        low_ref[...] = low


def plane_couple(first, meta, rows, before=None):
    height, wide = meta.shape
    parts = 2 * X_
    shape = (4 * rows, 2 * rows)
    last = before is not None
    args = [first, meta] + ([before] if last else [])
    scratch = [pltpu.VMEM((parts, height, wide // parts), F32)]
    return pl.pallas_call(
        functools.partial(plane_couple_kernel, last),
        in_specs=[pl.BlockSpec(memory_space=pltpu.SMEM)]
        + [pl.BlockSpec(memory_space=pltpu.VMEM)] * (len(args) - 1),
        out_shape=[jax.ShapeDtypeStruct(shape, BF16)] * 2 if last else jax.ShapeDtypeStruct(shape, F32),
        scratch_shapes=([pltpu.VMEM(shape, F32)] if last else []) + scratch,
        compiler_params=params(),
        name="plane_couple",
        cost_estimate=pl.CostEstimate(
            flops=2 * 8 * wide * rows * rows, bytes_accessed=2_000_000, transcendentals=0
        ),
    )(*args)


def plane_mix_kernel(high_ref, low_ref, a_ref, b_ref, c_ref, d_ref, *refs):
    *extra, mine_ref, other_ref = refs
    refs = (a_ref, b_ref, c_ref, d_ref)
    height, rows = a_ref.shape
    body = pl.ds(0, HOURS)
    one, two = pieces(jnp.concatenate([ref[body, :] for ref in refs], axis=1), 2)
    both = dot(jnp.concatenate([two, one], axis=0), high_ref[...])
    result = (both[:HOURS] + dot(one, low_ref[...])) + both[HOURS:]
    mine_ref[body, :] = result[:, :rows]
    other_ref[body, :] = result[:, rows:]
    if height > HOURS:
        tail = pl.ds(HOURS, NOTE)
        note = sum(ref[tail, :] for ref in refs)
        mine_ref[tail, :] = note
        other_ref[tail, :] = note
    for ref in extra:
        other_ref[pl.ds(height, ref.shape[0]), :] = ref[...]


def plane_mix(coupling, values, extra):
    height, rows = values[0].shape
    return pl.pallas_call(
        plane_mix_kernel,
        out_shape=[
            jax.ShapeDtypeStruct((height, rows), F32),
            jax.ShapeDtypeStruct((height + sum(value.shape[0] for value in extra), rows), F32),
        ],
        compiler_params=params(),
        name="plane_mix",
        cost_estimate=SMALL,
    )(*coupling, *values, *extra)


def plane_rows_kernel(first_ref, meta_ref, meta_other_ref, a_ref, b_ref, c_ref, d_ref, *refs):
    if len(refs) > 2:
        *stack, last_ref, beside_ref, mine_ref, other_ref, stack_ref = refs
    else:
        mine_ref, other_ref = refs
    rows = a_ref.shape[1]
    value = jnp.concatenate([ref[pl.ds(0, HOURS), :] for ref in (a_ref, b_ref, c_ref, d_ref)], axis=1)
    one, two = pieces(value, 2)
    stacked = jnp.concatenate([two, one], axis=0)
    picked = []
    for ref in (meta_ref, meta_other_ref):
        gauge = ref[0:1, :]
        hot = jnp.concatenate([hot_rows(gauge, first_ref[m], rows) for m in range(4)], axis=0)
        both = dot(stacked, hot)
        picked.append(both[:HOURS] + both[HOURS:])
    mine_ref[...] = picked[0]
    count = picked[1].shape[1] // rows
    for i in range(count):
        other_ref[pl.ds(i * HOURS, HOURS), :] = picked[1][:, i * rows : (i + 1) * rows]
    if len(refs) > 2:
        top = stack_ref.shape[0] - HOURS
        for ref in stack:
            stack_ref[pl.ds(0, top), :] = ref[...]
        for i in range(count):
            here = pl.ds(i * rows, rows)
            beside = beside_ref[pl.ds(beside_ref.shape[0] - (count - i) * HOURS, HOURS), :]
            stack_ref[pl.ds(top, HOURS), here] = last_ref[:, here] + beside


def plane_rows(first, metas, values, before):
    rows = values[0].shape[1]
    slots = metas[0].shape[1]
    args = [first, *metas, *values, *before]
    shapes = [(HOURS, slots), (slots // rows * HOURS, rows)]
    if before:
        shapes.append(((len(before) - 1) * HOURS, slots))
    return pl.pallas_call(
        plane_rows_kernel,
        in_specs=[pl.BlockSpec(memory_space=pltpu.SMEM)]
        + [pl.BlockSpec(memory_space=pltpu.VMEM)] * (len(args) - 1),
        out_shape=[jax.ShapeDtypeStruct(shape, F32) for shape in shapes],
        compiler_params=params(),
        name="plane_rows",
        cost_estimate=pl.CostEstimate(flops=1_000_000_000, bytes_accessed=2_000_000, transcendentals=0),
    )(*args)


def gain(kernels):
    return jnp.max(jnp.sum(kernels, axis=1, keepdims=True), axis=0, keepdims=True)


def spectra(kind, kernels, wide):
    classes = kernels.shape[0]
    row = lax.broadcasted_iota(jnp.int32, (classes, kind.shape[1]), 0).astype(F32)
    hot = jnp.where(row == kind, 1.0, 0.0).astype(BF16)
    taps = jnp.transpose(kernels / gain(kernels))
    chosen = dot(jnp.concatenate(pieces(taps, 3)[::-1], axis=1), jnp.concatenate([hot] * 3, axis=0))
    return product(wide, chosen, 3)


def plane_spectrum_kernel(class_ref, kernels_ref, wide_ref, out_ref):
    kind = class_ref[1:2, : out_ref.shape[1]]
    out_ref[...] = spectra(kind, kernels_ref[...], wide_ref[...])


def plane_spectrum(meta, kernels, wide, rows):
    return pl.pallas_call(
        plane_spectrum_kernel,
        out_shape=jax.ShapeDtypeStruct((SPAN, rows), F32),
        compiler_params=params(),
        name="plane_spectrum",
        cost_estimate=SMALL,
    )(meta, kernels, wide)


def sides(even, pair, middle):
    return jnp.where(even, middle, pair), jnp.where(even, pair, middle)


def plane_call(kernel, name, shapes, flags, args):
    return pl.pallas_call(
        kernel,
        in_specs=[pl.BlockSpec(memory_space=pltpu.SMEM)] * len(flags)
        + [pl.BlockSpec(memory_space=pltpu.VMEM)] * len(args),
        out_shape=[jax.ShapeDtypeStruct(shape, F32) for shape in shapes],
        compiler_params=params(),
        name=name,
        cost_estimate=SMALL,
    )(*flags, *args)


def plane_first_kernel(
    flag_ref, here_ref, pair_ref, middle_ref, seen_ref, spec_ref, kernels_ref, forward, first, last, out_ref
):
    spec = spec_ref[...]
    before, after = sides(flag_ref[0] > 0.5, pair_ref[...], middle_ref[...])
    now, later = plane_delayed(before, here_ref[...], after, spec, forward[...], last[...], 3)
    known = plane_advanced(now, later * flag_ref[1], spec, forward[...], first[...], 3)
    out_ref[...] = seen_ref[...] - known * gain(kernels_ref[...])


def plane_delay_kernel(flag_ref, here_ref, pair_ref, middle_ref, spec_ref, forward, last, out_ref):
    body = pl.ds(0, HOURS)
    before, after = sides(flag_ref[0] > 0.5, pair_ref[body, :], middle_ref[body, :])
    out = plane_delayed(before, here_ref[body, :], after, spec_ref[...], forward[...], last[...], 2)
    for i in range(2):
        out_ref[pl.ds(i * HOURS, HOURS), :] = out[i]


def write_note(ref, rows):
    tail = [jnp.zeros((NOTE - len(rows), ref.shape[1]), F32)]
    ref[pl.ds(HOURS, NOTE), :] = jnp.concatenate(rows + tail, axis=0)


def plane_open_kernel(
    flag_ref, here_ref, pair_ref, middle_ref, pulled_ref, spec_ref, forward, first, last, out_ref, delayed_ref
):
    here = here_ref[...]
    spec = spec_ref[...]
    before, after = sides(flag_ref[0] > 0.5, pair_ref[...], middle_ref[...])
    now, later = plane_delayed(before, here, after, spec, forward[...], last[...], 2)
    out_ref[pl.ds(0, HOURS), :] = plane_advanced(now, later * flag_ref[1], spec, forward[...], first[...], 2)
    write_note(out_ref, [lanes(pulled_ref[...], here), lanes(now, now)])
    delayed_ref[pl.ds(0, HOURS), :] = now
    delayed_ref[pl.ds(HOURS, HOURS), :] = later


def plane_step_kernel(
    flag_ref,
    here_ref,
    pair_ref,
    two_ref,
    mirror_ref,
    pulled_ref,
    delayed_ref,
    old_z_ref,
    old_s_ref,
    old_delayed_ref,
    spec_ref,
    forward,
    first,
    total_ref,
    out_ref,
    kept_ref,
):
    tail, body = pl.ds(HOURS, NOTE), pl.ds(0, HOURS)
    total_ref[...] = (here_ref[tail, :] + pair_ref[tail, :]) + (two_ref[...] + mirror_ref[...])
    inverse = total(total_ref, 0) / total(total_ref, 1)
    z = pulled_ref[body, :] * inverse - old_z_ref[...]
    s = here_ref[body, :] * inverse - old_s_ref[...]
    both = delayed_ref[...] * inverse - old_delayed_ref[...]
    now, later = both[:HOURS], both[HOURS:]
    following = plane_advanced(now, later * flag_ref[1], spec_ref[...], forward[...], first[...], 2)
    out_ref[body, :] = following * inverse
    write_note(out_ref, [lanes(z, s), lanes(now, now)])
    for i, value in enumerate((z, s, now)):
        kept_ref[pl.ds(i * HOURS, HOURS), :] = value


def plane_close_kernel(
    here_ref, before_ref, pulled_ref, kept_ref, old_z_ref, old_s_ref, old_delayed_ref, spec_ref, forward, last, out_ref
):
    body = pl.ds(0, HOURS)
    here, raw = here_ref[body, :], pulled_ref[body, :]
    waves = product(forward[...], jnp.concatenate([before_ref[body, :], here], axis=0), 2)
    now = product(last[...], turn(waves, spec_ref[...], 1.0), 2)
    z, s, delayed = (kept_ref[pl.ds(i * HOURS, HOURS), :] for i in range(3))
    note = [pulled_ref[HOURS + i : HOURS + i + 1, :] for i in range(2)]
    for left in (raw, z, old_z_ref[...]):
        note += [lanes(left, right) for right in (here, s, old_s_ref[...])]
    parts = (now, delayed, old_delayed_ref[body, :])
    for i in range(3):
        note += [lanes(parts[i], parts[j]) for j in range(i, 3)]
    note.append(jnp.zeros((24 - len(note), here.shape[1]), F32))
    note = jnp.sum(jnp.concatenate(note, axis=0), axis=1, keepdims=True)
    shape = (24, out_ref.shape[2])
    row, col = (lax.broadcasted_iota(jnp.int32, shape, i) for i in range(2))
    note = jnp.sum(jnp.where(row == col, jnp.broadcast_to(note, shape), 0.0), axis=0, keepdims=True)
    out_ref[...] = jnp.broadcast_to(note[None], out_ref.shape)


def plane_weights(open_ref, close, scale):
    entry = lambda i: close[:, i : i + 1]
    n1, t1 = total(open_ref, 0), total(open_ref, 1)
    n2, t2 = entry(0), entry(1)
    a1 = t1 / n1
    a2, r2 = (t2 / n2) / a1, n2 / n1
    plain = (1.0, -a2, -r2)
    n3 = sum(plain[i] * plain[j] * entry(2 + 3 * i + j) for i in range(3) for j in range(3))
    pairs = [(i, j) for i in range(3) for j in range(i, 3)]
    t3 = sum(
        plain[i] * plain[j] * entry(11 + n) * (1.0 if i == j else 2.0) for n, (i, j) in enumerate(pairs)
    )
    a3, r3 = (t3 / n3) / a1, n3 / n2
    unit = 1.0 / (a1 * scale)
    c3 = unit / (a3 * (a2 - r2) - r3)
    c2 = -a3 * c3
    c1 = unit - r2 * c2
    step = c2 - c3 * a2
    return c1 - step - c3 * r2, step / a1, c3


def plane_combine_kernel(open_ref, close_ref, kernels_ref, stack_ref, mine_ref, beside_ref, out_ref):
    rows = open_ref.shape[1]
    close = jnp.sum(close_ref[...], axis=0)[0:1, :]
    e0, e1, e2 = plane_weights(open_ref, close, gain(kernels_ref[...]))
    for i in range(out_ref.shape[0] // rows):
        here = pl.ds(i * rows, rows)
        last = mine_ref[:, here] + beside_ref[pl.ds(i * HOURS, HOURS), :]
        value = stack_ref[pl.ds(0, HOURS), here] * e0 + stack_ref[pl.ds(HOURS, HOURS), here] * e1 + last * e2
        out_ref[here, :] = jnp.transpose(value)


def plane_finish_kernel(rows_ref, inc_ref, field_ref, out_ref):
    blocks, slots, width = inc_ref.shape
    weights = inc_ref[...].astype(F32).astype(BF16)
    for b in range(blocks):
        here = pl.ds(b * width, width)
        rows = jnp.concatenate(pieces(rows_ref[pl.ds(b * slots, slots), :], 2), axis=0)
        twice = jnp.concatenate([weights[b]] * 2, axis=0)
        added = lax.dot_general(twice, rows, (((0,), (0,)), ((), ())), preferred_element_type=F32)
        out_ref[here, :] = field_ref[here, :] + added


def plane_finish(rows, incidence, field):
    blocks, slots, width = incidence.shape
    hours = field.shape[1]
    step = 8
    return pl.pallas_call(
        plane_finish_kernel,
        grid=(blocks // step,),
        in_specs=[
            pl.BlockSpec((step * slots, hours), lambda i: (i, 0)),
            pl.BlockSpec((step, slots, width), lambda i: (i, 0, 0)),
            pl.BlockSpec((step * width, hours), lambda i: (i, 0)),
        ],
        out_specs=pl.BlockSpec((step * width, hours), lambda i: (i, 0)),
        out_shape=jax.ShapeDtypeStruct(field.shape, F32),
        compiler_params=params(),
        name="plane_finish",
    )(rows, incidence, field)


def plane_shards(incidence, row_gauge, gauge_kernel, kernels, observed, first_guess):
    rows, hours = observed.shape
    basin, tm = lax.axis_index("basin"), lax.axis_index("tm")
    z, x, y, c = basin // X_, basin % X_, tm // C_, tm % C_
    place = 2 * y + x
    first = jnp.stack([4 * c + (place ^ m) for m in range(4)] + [4 * c + place, 4 * (1 - c) + place])
    first = (first * rows).astype(jnp.int32)
    flags = jnp.stack([1 - z % 2, (z < Z_ - 1).astype(z.dtype), (z > 0).astype(z.dtype)]).astype(F32)
    forward, inverse_first, inverse_last, _ = turned_transforms(2)
    forward3, inverse_first3, inverse_last3, short3 = turned_transforms(3)
    block, noted = (hours, rows), (hours + NOTE, rows)

    parcel = send(incidence, first_guess, row_gauge, gauge_kernel)
    parcel, near, gauges, kinds, seen = lax.optimization_barrier(
        (parcel, incidence, row_gauge, gauge_kernel, observed)
    )
    parcel = moved(parcel, to_plane)
    meta = describe(near, gauges)
    meta = jnp.concatenate([meta, moved(meta, over_x)], axis=1)
    meta = jnp.concatenate([meta, moved(meta, z_pair)], axis=1)
    seen = observe(seen, moved(seen, hour_before), kinds, kernels, short3, [forward3, inverse_first3])
    parcel, behind = lax.optimization_barrier((parcel, seen))
    seen = moved(seen, to_plane)
    parcels = [parcel, moved(parcel, over_core)]
    spec = plane_spectrum(parcel[hours:], kernels, short3, rows)
    parcels[1], seen, meta, spec = lax.optimization_barrier((parcels[1], seen, meta, spec))
    around = [meta, moved(meta, z_two)]
    dense = spread(first, parcels, rows)
    metas = [value[hours:] for value in parcels]
    sums = dense[0] + sum(moved(value, where) for value, where in zip(dense[1:], SQUARE))
    sums = [sums, moved(sums, z_pair), moved(sums, z_middle)]
    coupled = plane_couple(first, around[0], rows)
    coupled, sums = lax.optimization_barrier((coupled, sums))
    coupling = plane_couple(first, around[1], rows, coupled)
    (pulled0,) = plane_call(
        plane_first_kernel,
        "plane_first",
        [block],
        [flags],
        [*sums, seen, spec, kernels, forward3, inverse_first3, inverse_last3],
    )

    def mixing(pulled, extra):
        values = [pulled] + [moved(pulled, where) for where in SQUARE]
        mine, other = plane_mix(coupling, values, extra)
        beside = moved(other, over_core)
        return values, mine + beside[: pulled.shape[0]], beside

    values, mixed0, _ = mixing(pulled0, [])
    picked, theirs = plane_rows(first, metas, values, [])
    sums = [mixed0, moved(mixed0, z_pair), moved(mixed0, z_middle)]
    pulled1, delayed0 = plane_call(
        plane_open_kernel,
        "plane_open",
        [noted, (2 * hours, rows)],
        [flags],
        [*sums, pulled0, spec, forward, inverse_first, inverse_last],
    )

    values, mixed1, beside = mixing(pulled1, [theirs])
    picked, theirs, stack = plane_rows(first, metas, values, [picked, beside])
    sums = [mixed1, moved(mixed1, z_pair), moved(mixed1, z_middle)]
    two, mirror = moved(mixed1[hours:], z_two), moved(mixed1[hours:], z_mirror)
    (delayed1,) = plane_call(
        plane_delay_kernel, "plane_delay", [(2 * hours, rows)], [flags], [*sums, spec, forward, inverse_last]
    )
    open_note, pulled2, kept = plane_call(
        plane_step_kernel,
        "plane_step",
        [(NOTE, rows), noted, (3 * hours, rows)],
        [flags],
        [*sums[:2], two, mirror, pulled1, delayed1, pulled0, mixed0, delayed0, spec, forward, inverse_first],
    )

    values, mixed2, beside = mixing(pulled2, [theirs])
    picked, theirs, stack = plane_rows(first, metas, values, [stack, picked, beside])
    (note,) = plane_call(
        plane_close_kernel,
        "plane_close",
        [(Z_ * X_ * Y_ * C_, 8, rows // 2)],
        [],
        [mixed2, moved(mixed2, z_next), pulled2, kept, pulled0, mixed0, delayed0, spec, forward, inverse_last],
    )
    close_note = lax.all_to_all(note, ("basin", "tm"), 0, 0, tiled=False)
    (answer,) = plane_call(
        plane_combine_kernel,
        "plane_combine",
        [(parcel.shape[1], hours)],
        [],
        [open_note, close_note, kernels, stack, picked, moved(theirs, over_core)],
    )
    return plane_finish(moved(answer, from_plane), incidence, first_guess)


def solution(mesh):
    planes = dict(mesh.shape) == {"basin": Z_ * X_, "tm": Y_ * C_}
    in_specs = (
        P("basin", None, None),
        P("basin"),
        P("basin"),
        P(),
        P("basin", "tm"),
        P("basin", "tm"),
    )
    return jax.shard_map(
        plane_shards if planes else shards, mesh=mesh, in_specs=in_specs, out_specs=P("basin", "tm"), check_vma=False
    )
```

```python
import functools

import jax
import jax.numpy as jnp
import numpy as np
from jax import lax
from jax.experimental import pallas as pl
from jax.experimental.pallas import tpu as pltpu
from jax.sharding import PartitionSpec as P

F32 = jnp.float32
BF16 = jnp.bfloat16
HIGH = lax.Precision.HIGHEST
SPAN = 256
MIB = 1024 * 1024


SMALL = pl.CostEstimate(flops=1, bytes_accessed=1, transcendentals=0)


def params(mib=16):
    return pltpu.CompilerParams(vmem_limit_bytes=mib * MIB)


def transforms():
    half = SPAN // 2
    freq = 2.0 * np.pi * (np.arange(half) + 0.5) / SPAN
    phase = np.arange(SPAN)[:, None] * freq[None, :]
    forward = np.concatenate([np.cos(phase), -np.sin(phase)], axis=1)
    inverse = forward.T * (2.0 / SPAN)
    return (
        jnp.asarray(forward, F32),
        jnp.asarray(inverse[:, :half], F32),
        jnp.asarray(inverse[:, half:], F32),
    )


def dot(a, b):
    return jnp.dot(a, b, preferred_element_type=F32)


def exact(a, b):
    return jnp.dot(a, b, precision=HIGH, preferred_element_type=F32)


def pieces(value, count):
    out = []
    for _ in range(count):
        piece = value.astype(BF16)
        out.append(piece)
        value = value - piece.astype(F32)
    return out


def pick(hot, value):
    return sum(dot(hot, piece) for piece in pieces(value, 3))


def prepare_kernel(inc_ref, field_ref, partial_ref, gram_ref):
    blocks, slots, width = inc_ref.shape
    rows = blocks * slots
    weights = inc_ref[...].astype(F32).astype(BF16)
    for b in range(blocks):
        value = field_ref[pl.ds(b * width, width), :]
        partial_ref[pl.ds(b * slots, slots), :] = pick(weights[b], value)
    flat = weights.reshape(rows, width)
    full = lax.dot_general(flat, flat, (((1,), (1,)), ((), ())), preferred_element_type=F32)
    row = lax.broadcasted_iota(jnp.int32, (rows, rows), 0)
    col = lax.broadcasted_iota(jnp.int32, (rows, rows), 1)
    own = jnp.where(row // slots == col // slots, full, 0.0)
    gram_ref[...] = jnp.sum(own.reshape(blocks, slots, rows), axis=0)


def prepare(incidence, field):
    blocks, slots, width = incidence.shape
    hours = field.shape[1]
    step = 8
    return pl.pallas_call(
        prepare_kernel,
        grid=(blocks // step,),
        in_specs=[
            pl.BlockSpec((step, slots, width), lambda i: (i, 0, 0)),
            pl.BlockSpec((step * width, hours), lambda i: (i, 0)),
        ],
        out_specs=[
            pl.BlockSpec((step * slots, hours), lambda i: (i, 0)),
            pl.BlockSpec((slots, step * slots), lambda i: (0, i)),
        ],
        out_shape=[
            jax.ShapeDtypeStruct((blocks * slots, hours), F32),
            jax.ShapeDtypeStruct((slots, blocks * slots), F32),
        ],
        compiler_params=params(56),
        name="prepare",
    )(incidence, field)


def table_kernel(gauge_ref, partial_ref, out_ref):
    slots = partial_ref.shape[0]
    rows = out_ref.shape[0]
    first = pl.program_id(0) * rows
    gauge = lax.broadcasted_iota(jnp.int32, (rows, slots), 0) + first
    hot = jnp.where(gauge_ref[...] == gauge, 1.0, 0.0).astype(BF16)
    out_ref[...] = pick(hot, partial_ref[...])


def table(row_gauge, partial, gauges):
    slots, hours = partial.shape
    step = 256
    return pl.pallas_call(
        table_kernel,
        grid=(gauges // step,),
        in_specs=[
            pl.BlockSpec((1, slots), lambda i: (0, 0)),
            pl.BlockSpec((slots, hours), lambda i: (0, 0)),
        ],
        out_specs=pl.BlockSpec((step, hours), lambda i: (i, 0)),
        out_shape=jax.ShapeDtypeStruct((gauges, hours), F32),
        compiler_params=params(56),
        name="table",
    )(row_gauge.reshape(1, slots), partial)


def couple_kernel(first_ref, lane_ref, sub_ref, gram_ref, high_ref, low_ref, near_ref):
    slots = gram_ref.shape[0]
    count = lane_ref.shape[1]
    rows, cols = high_ref.shape
    tile = 256
    first = first_ref[0]

    @pl.when(pl.program_id(0) == 0)
    def _():
        row = lax.broadcasted_iota(jnp.int32, (tile, tile), 0)
        col = lax.broadcasted_iota(jnp.int32, (tile, tile), 1)
        same = row // slots == col // slots
        mine = lax.broadcasted_iota(jnp.int32, (rows, tile), 0) + first

        def body(i, carry):
            here = pl.ds(pl.multiple_of(i * tile, tile), tile)
            block = jnp.concatenate([gram_ref[:, here]] * (tile // slots), axis=0)
            block = jnp.where(same, block, 0.0).astype(BF16)
            hot = jnp.where(lane_ref[:, here] == mine, 1.0, 0.0).astype(BF16)
            near_ref[:, here] = dot(hot, block)
            return carry

        lax.fori_loop(0, count // tile, body, 0)

    def chunk(i, total):
        here = pl.ds(pl.multiple_of(i * 1024, 1024), 1024)
        gauge = lax.broadcasted_iota(jnp.int32, (1024, cols), 1) + pl.program_id(0) * cols
        hot = jnp.where(sub_ref[here, :] == gauge, 1.0, 0.0).astype(BF16)
        near = near_ref[:, here]
        high = near.astype(BF16)
        low = (near - high.astype(F32)).astype(BF16)
        return total + dot(high, hot) + dot(low, hot)

    total = lax.fori_loop(0, count // 1024, chunk, jnp.zeros((rows, cols), F32))
    high, low = pieces(total, 2)
    high_ref[...] = high
    low_ref[...] = low


def couple(first, row_gauge, gram, rows, gauges):
    count = row_gauge.shape[0]
    step = 256
    return pl.pallas_call(
        couple_kernel,
        grid=(gauges // step,),
        in_specs=[
            pl.BlockSpec(memory_space=pltpu.SMEM),
            pl.BlockSpec((1, count), lambda i: (0, 0)),
            pl.BlockSpec((count, 1), lambda i: (0, 0)),
            pl.BlockSpec(gram.shape, lambda i: (0, 0)),
        ],
        out_specs=[pl.BlockSpec((rows, step), lambda i: (0, i))] * 2,
        out_shape=[jax.ShapeDtypeStruct((rows, gauges), BF16)] * 2,
        scratch_shapes=[pltpu.VMEM((rows, count), F32)],
        compiler_params=params(56),
        name="couple",
    )(first, row_gauge.reshape(1, count), row_gauge.reshape(count, 1), gram)


def mix_kernel(high_ref, low_ref, value_ref, out_ref):
    high = high_ref[...]
    low = low_ref[...]
    one, two, three = pieces(value_ref[...], 3)
    out_ref[...] = (dot(high, three) + dot(low, two)) + (dot(high, two) + dot(low, one)) + dot(high, one)


def mix(high, low, value):
    return pl.pallas_call(
        mix_kernel,
        out_shape=jax.ShapeDtypeStruct((high.shape[0], value.shape[1]), F32),
        compiler_params=params(56),
        name="mix",
    )(high, low, value)


def spectrum_kernel(class_ref, kernels_ref, forward_ref, out_ref):
    rows = class_ref.shape[0]
    classes, taps = kernels_ref.shape
    kind = lax.broadcasted_iota(jnp.int32, (rows, classes), 1)
    hot = jnp.where(class_ref[...] == kind, 1.0, 0.0)
    out_ref[...] = exact(exact(hot, kernels_ref[...]), forward_ref[pl.ds(0, taps), :])


def spectrum(gauge_kernel, kernels, forward):
    rows = gauge_kernel.shape[0]
    return pl.pallas_call(
        spectrum_kernel,
        out_shape=jax.ShapeDtypeStruct((rows, SPAN), F32),
        compiler_params=params(56),
        name="spectrum",
    )(gauge_kernel.reshape(rows, 1), kernels, forward)


def delayed(before, here, after, spec, forward, inverse_last):
    rows, half = here.shape
    stacked = jnp.concatenate(
        [jnp.concatenate([before, here], axis=1), jnp.concatenate([here, after], axis=1)], axis=0
    )
    waves = exact(stacked, forward)
    real, imag = waves[:, :half], waves[:, half:]
    kr = jnp.concatenate([spec[:, :half]] * 2, axis=0)
    ki = jnp.concatenate([spec[:, half:]] * 2, axis=0)
    turned = jnp.concatenate([real * kr - imag * ki, real * ki + imag * kr], axis=1)
    out = exact(turned, inverse_last)
    return out[:rows], out[rows:]


def advanced(here, after, spec, forward, inverse_first):
    half = here.shape[1]
    waves = exact(jnp.concatenate([here, after], axis=1), forward)
    real, imag = waves[:, :half], waves[:, half:]
    kr, ki = spec[:, :half], spec[:, half:]
    turned = jnp.concatenate([real * kr + imag * ki, imag * kr - real * ki], axis=1)
    return exact(turned, inverse_first)


def lanes(a, b):
    return jnp.sum(a * b, axis=0, keepdims=True)


def total(ref, row):
    return jnp.sum(ref[row : row + 1, :], axis=1, keepdims=True)


def ratios(ref):
    square = total(ref, 0)
    alpha = jnp.sqrt(square)
    beta = jnp.sqrt(jnp.maximum(total(ref, 1) / square - 2.0 * total(ref, 2) + square, 0.0))
    return alpha, beta


def first_kernel(
    more_ref, sums_ref, observed_ref, spec_ref, forward_ref, first_ref, last_ref, out_ref, note_ref
):
    rows, half = observed_ref.shape[0] // 2, observed_ref.shape[1]
    spec, forward = spec_ref[...], forward_ref[...]
    before, here, after = (sums_ref[pl.ds(i * rows, rows), :] for i in range(3))
    now, later = delayed(before, here, after, spec, forward, last_ref[...])
    start = observed_ref[pl.ds(0, rows), :] - now
    start_later = (observed_ref[pl.ds(rows, rows), :] - later) * more_ref[0]
    out_ref[...] = advanced(start, start_later, spec, forward, first_ref[...])
    note_ref[...] = jnp.concatenate([lanes(start, start), jnp.zeros((7, half), F32)], axis=0)


def first_step(more, sums, observed, spec, mats):
    rows, half = spec.shape[0], observed.shape[1]
    return pl.pallas_call(
        first_kernel,
        in_specs=[pl.BlockSpec(memory_space=pltpu.SMEM)] + [pl.BlockSpec(memory_space=pltpu.VMEM)] * 6,
        out_shape=[jax.ShapeDtypeStruct((rows, half), F32), jax.ShapeDtypeStruct((8, half), F32)],
        compiler_params=params(56),
        name="first_step",
    )(more, sums, observed, spec, *mats)


def step_kernel(
    opening,
    final,
    more_ref,
    note_ref,
    sums_ref,
    spec_ref,
    forward_ref,
    first_ref,
    last_ref,
    pulled_ref,
    *refs,
):
    if opening:
        state_ref = None
    else:
        state_ref, *refs = refs
    if final:
        (out_note_ref,) = refs
    else:
        new_ref, out_ref, out_note_ref = refs
    rows, half = pulled_ref.shape
    spec, forward = spec_ref[...], forward_ref[...]
    if opening:
        scale = 1.0 / jnp.sqrt(total(note_ref, 0))
        along = sums_ref[...] * scale
        new_s, new_su = along, along
        new_zu = pulled_ref[...] * scale
        new_z = new_zu
    else:
        alpha, beta = ratios(note_ref)
        a, b, g = 1.0 / (alpha * beta), alpha / beta, beta / alpha
        wide = pl.ds(0, 3 * rows), pl.ds(3 * rows, 3 * rows)
        new_su = sums_ref[...] * a - state_ref[wide[1], :] * b
        new_s = new_su - state_ref[wide[0], :] * g
        new_zu = pulled_ref[...] * a - state_ref[pl.ds(7 * rows, rows), :] * b
        new_z = new_zu - state_ref[pl.ds(6 * rows, rows), :] * g
    before, here, after = (new_s[i * rows : (i + 1) * rows] for i in range(3))
    now, later = delayed(before, here, after, spec, forward, last_ref[...])
    out_note_ref[...] = jnp.concatenate(
        [lanes(new_z, here), lanes(now, now), lanes(new_zu, here), jnp.zeros((5, half), F32)], axis=0
    )
    if not final:
        new_ref[pl.ds(0, 3 * rows), :] = new_s
        new_ref[pl.ds(3 * rows, 3 * rows), :] = new_su
        new_ref[pl.ds(6 * rows, rows), :] = new_z
        new_ref[pl.ds(7 * rows, rows), :] = new_zu
        out_ref[...] = advanced(now, later * more_ref[0], spec, forward, first_ref[...])


def next_step(more, note, sums, spec, mats, pulled, state, final):
    rows, half = pulled.shape
    opening = state is None
    shapes = [
        jax.ShapeDtypeStruct((8 * rows, half), F32),
        jax.ShapeDtypeStruct((rows, half), F32),
        jax.ShapeDtypeStruct((8, half), F32),
    ]
    args = [more, note, sums, spec, *mats, pulled] + ([] if opening else [state])
    return pl.pallas_call(
        functools.partial(step_kernel, opening, final),
        in_specs=[pl.BlockSpec(memory_space=pltpu.SMEM)]
        + [pl.BlockSpec(memory_space=pltpu.VMEM)] * (len(args) - 1),
        out_shape=shapes[2:] if final else shapes,
        compiler_params=params(56),
        name="next_step",
    )(*args)


def weights_of(notes):
    start = jnp.sqrt(total(notes[0], 0))
    zero = jnp.zeros_like(start)
    units = [1.0 / start, zero, zero]
    z, zu = list(units), list(units)
    phibar = start
    alpha, beta = ratios(notes[1])
    rhobar = alpha
    w = [value / alpha for value in z]
    result = [zero] * 3
    steps = len(notes) - 1
    for k in range(steps):
        rho = jnp.sqrt(rhobar * rhobar + beta * beta)
        cosine, sine = rhobar / rho, beta / rho
        phi, phibar = cosine * phibar, sine * phibar
        result = [r + phi / rho * value for r, value in zip(result, w)]
        if k < steps - 1:
            a, b, g = 1.0 / (alpha * beta), alpha / beta, beta / alpha
            zu = [(a if i == k + 1 else 0.0) - b * value for i, value in enumerate(zu)]
            z = [value - g * old for value, old in zip(zu, z)]
            alpha, beta = ratios(notes[k + 2])
            theta = sine * alpha
            rhobar = -cosine * alpha
            w = [value / alpha - theta / rho * old for value, old in zip(z, w)]
    return result


def finish_kernel(n0, n1, n2, n3, gauge_ref, q0, q1, q2, inc_ref, field_ref, out_ref, rows_ref):
    blocks, slots, width = inc_ref.shape
    count = rows_ref.shape[0]
    gauges = q0.shape[0]
    step = pl.program_id(0)

    @pl.when(step == 0)
    def _():
        e0, e1, e2 = weights_of([n0, n1, n2, n3])
        width_ = 512

        def body(i, value):
            here = pl.ds(pl.multiple_of(i * width_, width_), width_)
            mixed = q0[here, :] * e0 + q1[here, :] * e1 + q2[here, :] * e2
            gauge = lax.broadcasted_iota(jnp.int32, (count, width_), 1) + i * width_
            hot = jnp.where(gauge_ref[...] == gauge, 1.0, 0.0).astype(BF16)
            return value + pick(hot, mixed)

        rows_ref[...] = lax.fori_loop(0, gauges // width_, body, jnp.zeros(rows_ref.shape, F32))

    weights = inc_ref[...].astype(F32).astype(BF16)
    for b in range(blocks):
        here = pl.ds(b * width, width)
        rows = rows_ref[pl.ds(pl.multiple_of((step * blocks + b) * slots, slots), slots), :]
        added = sum(
            lax.dot_general(weights[b], piece, (((0,), (0,)), ((), ())), preferred_element_type=F32)
            for piece in pieces(rows, 3)
        )
        out_ref[here, :] = field_ref[here, :] + added


def finish(notes, row_gauge, gathered, incidence, field):
    blocks, slots, width = incidence.shape
    hours = field.shape[1]
    count = row_gauge.shape[0]
    step = 8
    whole = lambda shape: pl.BlockSpec(shape, lambda i: (0, 0))
    return pl.pallas_call(
        finish_kernel,
        grid=(blocks // step,),
        in_specs=[whole(n.shape) for n in notes]
        + [whole((count, 1))]
        + [whole(q.shape) for q in gathered]
        + [
            pl.BlockSpec((step, slots, width), lambda i: (i, 0, 0)),
            pl.BlockSpec((step * width, hours), lambda i: (i, 0)),
        ],
        out_specs=pl.BlockSpec((step * width, hours), lambda i: (i, 0)),
        out_shape=jax.ShapeDtypeStruct(field.shape, F32),
        scratch_shapes=[pltpu.VMEM((count, hours), F32)],
        compiler_params=params(56),
        name="finish",
    )(*notes, row_gauge.reshape(count, 1), *gathered, incidence, field)


def shifted(value, axis, by):
    devices = lax.axis_size(axis)
    pairs = [(i, i + by) for i in range(devices) if 0 <= i + by < devices]
    return lax.ppermute(value, axis, pairs)


def window(value):
    return jnp.concatenate([shifted(value, "tm", 1), value, shifted(value, "tm", -1)], axis=0)


def gathered_rows(value):
    owners = lax.axis_size("basin")
    copies = jnp.broadcast_to(value[None], (owners,) + value.shape)
    return lax.all_to_all(copies, "basin", 0, 0, tiled=False)


def over_hours(note):
    blocks = lax.axis_size("tm")
    result = note
    for by in range(1, blocks):
        result = result + lax.ppermute(note, "tm", [(i, (i + by) % blocks) for i in range(blocks)])
    return result


def shards(incidence, row_gauge, gauge_kernel, kernels, observed, first_guess):
    owners = lax.axis_size("basin")
    rows, hours = observed.shape
    gauges = rows * owners
    mats = transforms()
    spec = spectrum(gauge_kernel, kernels, mats[0])
    more = (lax.axis_index("tm") < lax.axis_size("tm") - 1).astype(F32).reshape(1)
    partial, gram = prepare(incidence, first_guess)
    all_gram = lax.all_gather(gram, "basin", axis=1, tiled=True)
    all_rows = lax.all_gather(row_gauge, "basin", axis=0, tiled=True)
    dense = table(row_gauge, partial, gauges).reshape(owners, rows, hours)
    sums = jnp.sum(lax.all_to_all(dense, "basin", 0, 0, tiled=False), axis=0)
    both = jnp.concatenate([observed, shifted(observed, "tm", -1)], axis=0)
    first = (lax.axis_index("basin") * rows).astype(jnp.int32).reshape(1)
    high, low = couple(first, all_rows, all_gram, rows, gauges)

    pulled, note = first_step(more, window(sums), both, spec, mats)
    notes, kept, state = [], [], None
    for k in range(3):
        everyone = gathered_rows(jnp.concatenate([pulled, note], axis=0))
        value = everyone[:, :rows].reshape(gauges, hours)
        notes.append(over_hours(jnp.sum(everyone[:, rows:], axis=0)))
        kept.append(value)
        around = window(mix(high, low, value))
        final = k == 2
        result = next_step(more, notes[-1], around, spec, mats, pulled, state, final)
        if final:
            (note,) = result
        else:
            state, pulled, note = result
    notes.append(over_hours(jnp.sum(gathered_rows(note), axis=0)))
    return finish(notes, row_gauge, kept, incidence, first_guess)


Z_, X_, Y_, C_ = 4, 2, 2, 2
NOTE = 8
HOURS = SPAN // 2


def device(z, x, y, c):
    return (z * X_ + x) * (Y_ * C_) + y * C_ + c


def moved(value, where):
    pairs = []
    for z, x, y, c in np.ndindex(Z_, X_, Y_, C_):
        target = where(z, x, y, c)
        if target is not None:
            pairs.append((device(z, x, y, c), device(*target)))
    return lax.ppermute(value, ("basin", "tm"), pairs)


def to_plane(z, x, y, c):
    return 2 * y + c, x, z & 1, z >> 1


def hour_before(z, x, y, c):
    t = 2 * y + c - 1
    return (z, x, t >> 1, t & 1) if t >= 0 else None


def from_plane(z, x, y, c):
    return 2 * c + y, x, z >> 1, z & 1


def over_x(z, x, y, c):
    return z, 1 - x, y, c


def over_y(z, x, y, c):
    return z, x, 1 - y, c


def over_xy(z, x, y, c):
    return z, 1 - x, 1 - y, c


def over_core(z, x, y, c):
    return z, x, y, 1 - c


def z_pair(z, x, y, c):
    return z ^ 1, x, y, c


def z_middle(z, x, y, c):
    return (3 - z, x, y, c) if z in (1, 2) else None


def z_two(z, x, y, c):
    return z ^ 2, x, y, c


def z_mirror(z, x, y, c):
    return 3 - z, x, y, c


def z_next(z, x, y, c):
    return (z + 1, x, y, c) if z < 3 else None


SQUARE = (over_x, over_y, over_xy)


def split_constant(value):
    out = []
    for _ in range(3):
        piece = value.astype(jnp.bfloat16)
        out.append(piece)
        value = value - piece.astype(np.float64)
    return out


ORDERS = {2: ((0, 1), (1, 0), (0, 0)), 3: ((0, 2), (1, 1), (2, 0), (0, 1), (1, 0), (0, 0))}


def widened(mat, order):
    parts = split_constant(mat)
    return jnp.asarray(np.concatenate([parts[i] for i, _ in ORDERS[order]], axis=1))


def product(wide, value, order):
    parts = pieces(value, order)
    return dot(wide, jnp.concatenate([parts[j] for _, j in ORDERS[order]], axis=0))


def turned_transforms(order):
    half = SPAN // 2
    freq = 2.0 * np.pi * (np.arange(half) + 0.5) / SPAN
    phase = freq[:, None] * np.arange(SPAN)[None, :]
    forward = np.concatenate([np.cos(phase), -np.sin(phase)], axis=0)
    inverse = forward.T * (2.0 / SPAN)
    return [widened(mat, order) for mat in (forward, inverse[:half], inverse[half:], forward[:, :half])]


def turn(waves, spec, sign):
    half = waves.shape[0] // 2
    real, imag = waves[:half], waves[half:]
    kr, ki = spec[:half], spec[half:] * sign
    return jnp.concatenate([real * kr - imag * ki, real * ki + imag * kr], axis=0)


def plane_delayed(before, here, after, spec, forward, last, order):
    rows = here.shape[1]
    pairs = [jnp.concatenate(pair, axis=0) for pair in ((before, here), (here, after))]
    waves = product(forward, jnp.concatenate(pairs, axis=1), order)
    turned = [turn(waves[:, i * rows : (i + 1) * rows], spec, 1.0) for i in range(2)]
    out = product(last, jnp.concatenate(turned, axis=1), order)
    return out[:, :rows], out[:, rows:]


def plane_advanced(here, after, spec, forward, first, order):
    waves = product(forward, jnp.concatenate([here, after], axis=0), order)
    return product(first, turn(waves, spec, -1.0), order)


def describe_kernel(inc_ref, gauge_ref, out_ref):
    blocks, slots, width = inc_ref.shape
    tile = 8
    side = tile * slots
    weights = inc_ref[...].astype(F32).astype(BF16)
    row = lax.broadcasted_iota(jnp.int32, (side, side), 0)
    col = lax.broadcasted_iota(jnp.int32, (side, side), 1)
    same = row // slots == col // slots
    for i in range(blocks // tile):
        flat = weights[i * tile : (i + 1) * tile].reshape(side, width)
        full = lax.dot_general(flat, flat, (((1,), (1,)), ((), ())), preferred_element_type=F32)
        own = jnp.where(same, full, 0.0)
        out_ref[pl.ds(0, slots), pl.ds(i * side, side)] = jnp.sum(own.reshape(tile, slots, side), axis=0)
    out_ref[pl.ds(slots, 8), :] = jnp.broadcast_to(gauge_ref[...].astype(F32), (8, blocks * slots))


def describe(incidence, row_gauge):
    blocks, slots, _ = incidence.shape
    count = blocks * slots
    return pl.pallas_call(
        describe_kernel,
        out_shape=jax.ShapeDtypeStruct((slots + 8, count), F32),
        compiler_params=params(),
        name="describe",
        cost_estimate=SMALL,
    )(incidence, row_gauge.reshape(1, count))


def observe_kernel(seen_ref, later_ref, kind_ref, kernels_ref, wide_ref, forward, first, out_ref):
    spec = spectra(kind_ref[...].astype(F32), kernels_ref[...], wide_ref[...])
    here, after = jnp.transpose(seen_ref[...]), jnp.transpose(later_ref[...])
    out_ref[...] = plane_advanced(here, after, spec, forward[...], first[...], 3)


def observe(seen, later, gauge_kernel, kernels, wide, mats):
    rows, hours = seen.shape
    return pl.pallas_call(
        observe_kernel,
        out_shape=jax.ShapeDtypeStruct((hours, rows), F32),
        compiler_params=params(),
        name="observe",
        cost_estimate=SMALL,
    )(seen, later, gauge_kernel.reshape(1, rows), kernels, wide, *mats)


def send_kernel(inc_ref, field_ref, gauge_ref, kind_ref, out_ref):
    blocks, slots, width = inc_ref.shape
    count = blocks * slots
    weights = inc_ref[...].astype(F32).astype(BF16)
    parts = []
    for b in range(blocks):
        value = jnp.concatenate(pieces(field_ref[pl.ds(b * width, width), :], 3)[::-1], axis=0)
        parts.append(dot(jnp.concatenate([weights[b]] * 3, axis=1), value))
    out_ref[pl.ds(0, HOURS), :] = jnp.transpose(jnp.concatenate(parts, axis=0))
    kinds = kind_ref.shape[1] // count
    here = jnp.minimum(pl.program_id(0), kinds - 1) * count
    out_ref[pl.ds(HOURS, 8), :] = jnp.concatenate(
        [
            gauge_ref[...].astype(F32),
            kind_ref[:, pl.ds(pl.multiple_of(here, count), count)].astype(F32),
            jnp.zeros((6, count), F32),
        ],
        axis=0,
    )


def send(incidence, field, row_gauge, gauge_kernel):
    blocks, slots, width = incidence.shape
    count = blocks * slots
    rows = gauge_kernel.shape[0]
    step = 8
    return pl.pallas_call(
        send_kernel,
        grid=(blocks // step,),
        in_specs=[
            pl.BlockSpec((step, slots, width), lambda i: (i, 0, 0)),
            pl.BlockSpec((step * width, HOURS), lambda i: (i, 0)),
            pl.BlockSpec((1, step * slots), lambda i: (0, i)),
            pl.BlockSpec((1, rows), lambda i: (0, 0)),
        ],
        out_specs=pl.BlockSpec((HOURS + 8, step * slots), lambda i: (0, i)),
        out_shape=jax.ShapeDtypeStruct((HOURS + 8, count), F32),
        compiler_params=params(),
        name="send",
        cost_estimate=SMALL,
    )(incidence, field, row_gauge.reshape(1, count), gauge_kernel.reshape(1, rows))


def hot_rows(gauge, first, rows):
    mine = (lax.broadcasted_iota(jnp.int32, (rows, gauge.shape[1]), 0) + first).astype(F32)
    return jnp.where(gauge == mine, 1.0, 0.0).astype(BF16)


def spread_kernel(first_ref, mine_ref, other_ref, *out_refs):
    rows = out_refs[0].shape[1]
    both = jnp.concatenate([mine_ref[...], other_ref[...]], axis=1)
    stacked = jnp.concatenate(pieces(both[:HOURS], 3), axis=0)
    for m, out_ref in enumerate(out_refs):
        hot = hot_rows(both[HOURS : HOURS + 1], first_ref[m], rows)
        result = lax.dot_general(stacked, hot, (((1,), (1,)), ((), ())), preferred_element_type=F32)
        out_ref[...] = (result[2 * HOURS :] + result[HOURS : 2 * HOURS]) + result[:HOURS]


def spread(first, parcels, rows):
    return pl.pallas_call(
        spread_kernel,
        in_specs=[pl.BlockSpec(memory_space=pltpu.SMEM)] + [pl.BlockSpec(memory_space=pltpu.VMEM)] * 2,
        out_shape=[jax.ShapeDtypeStruct((HOURS, rows), F32)] * 4,
        compiler_params=params(),
        name="spread",
        cost_estimate=SMALL,
    )(first, *parcels)


def plane_couple_kernel(last, first_ref, *refs):
    if last:
        all_ref, before_ref, high_ref, low_ref, total_ref, meta_ref = refs
        total_ref[...] = before_ref[...]
    else:
        all_ref, total_ref, meta_ref = refs
        total_ref[...] = jnp.zeros_like(total_ref)
    parts, height, count = meta_ref.shape
    slots = height - 8
    cols, rows = total_ref.shape
    tile = 256
    for i in range(parts):
        meta_ref[i] = all_ref[:, i * count : (i + 1) * count]
    row = lax.broadcasted_iota(jnp.int32, (tile, tile), 0)
    col = lax.broadcasted_iota(jnp.int32, (tile, tile), 1)
    same = row // slots == col // slots

    def body(i, carry):
        gauge = meta_ref[i, slots : slots + 1, :]
        near = []
        for j in range(count // tile):
            here = slice(j * tile, (j + 1) * tile)
            block = jnp.concatenate([meta_ref[i, :slots, here]] * (tile // slots), axis=0)
            block = jnp.where(same, block, 0.0).astype(BF16)
            mine = jnp.concatenate(
                [hot_rows(gauge[:, here], first_ref[4 + h], rows // 2) for h in range(2)], axis=0
            )
            near.append(
                lax.dot_general(block, mine, (((1,), (1,)), ((), ())), preferred_element_type=F32)
            )
        near = jnp.concatenate(near, axis=0)
        high = near.astype(BF16)
        rest = near - high.astype(F32)
        hot = jnp.concatenate([hot_rows(gauge, first_ref[m], cols // 4) for m in range(4)], axis=0)
        total_ref[...] += dot(hot, high)

        @pl.when(jnp.max(jnp.abs(rest)) > 0.0)
        def _():
            total_ref[...] += dot(hot, rest.astype(BF16))

        return carry

    lax.fori_loop(0, parts, body, 0)
    if last:
        high, low = pieces(total_ref[...], 2)
        high_ref[...] = high
        low_ref[...] = low


def plane_couple(first, meta, rows, before=None):
    height, wide = meta.shape
    parts = 2 * X_
    shape = (4 * rows, 2 * rows)
    last = before is not None
    args = [first, meta] + ([before] if last else [])
    scratch = [pltpu.VMEM((parts, height, wide // parts), F32)]
    return pl.pallas_call(
        functools.partial(plane_couple_kernel, last),
        in_specs=[pl.BlockSpec(memory_space=pltpu.SMEM)]
        + [pl.BlockSpec(memory_space=pltpu.VMEM)] * (len(args) - 1),
        out_shape=[jax.ShapeDtypeStruct(shape, BF16)] * 2 if last else jax.ShapeDtypeStruct(shape, F32),
        scratch_shapes=([pltpu.VMEM(shape, F32)] if last else []) + scratch,
        compiler_params=params(),
        name="plane_couple",
        cost_estimate=pl.CostEstimate(
            flops=2 * 8 * wide * rows * rows, bytes_accessed=2_000_000, transcendentals=0
        ),
    )(*args)


def plane_mix_kernel(high_ref, low_ref, a_ref, b_ref, c_ref, d_ref, *refs):
    *extra, mine_ref, other_ref = refs
    refs = (a_ref, b_ref, c_ref, d_ref)
    height, rows = a_ref.shape
    body = pl.ds(0, HOURS)
    one, two = pieces(jnp.concatenate([ref[body, :] for ref in refs], axis=1), 2)
    both = dot(jnp.concatenate([two, one], axis=0), high_ref[...])
    result = (both[:HOURS] + dot(one, low_ref[...])) + both[HOURS:]
    mine_ref[body, :] = result[:, :rows]
    other_ref[body, :] = result[:, rows:]
    if height > HOURS:
        tail = pl.ds(HOURS, NOTE)
        note = sum(ref[tail, :] for ref in refs)
        mine_ref[tail, :] = note
        other_ref[tail, :] = note
    for ref in extra:
        other_ref[pl.ds(height, ref.shape[0]), :] = ref[...]


def plane_mix(coupling, values, extra):
    height, rows = values[0].shape
    return pl.pallas_call(
        plane_mix_kernel,
        out_shape=[
            jax.ShapeDtypeStruct((height, rows), F32),
            jax.ShapeDtypeStruct((height + sum(value.shape[0] for value in extra), rows), F32),
        ],
        compiler_params=params(),
        name="plane_mix",
        cost_estimate=SMALL,
    )(*coupling, *values, *extra)


def plane_rows_kernel(first_ref, meta_ref, meta_other_ref, a_ref, b_ref, c_ref, d_ref, *refs):
    if len(refs) > 2:
        *stack, last_ref, beside_ref, mine_ref, other_ref, stack_ref = refs
    else:
        mine_ref, other_ref = refs
    rows = a_ref.shape[1]
    value = jnp.concatenate([ref[pl.ds(0, HOURS), :] for ref in (a_ref, b_ref, c_ref, d_ref)], axis=1)
    one, two = pieces(value, 2)
    stacked = jnp.concatenate([two, one], axis=0)
    picked = []
    for ref in (meta_ref, meta_other_ref):
        gauge = ref[0:1, :]
        hot = jnp.concatenate([hot_rows(gauge, first_ref[m], rows) for m in range(4)], axis=0)
        both = dot(stacked, hot)
        picked.append(both[:HOURS] + both[HOURS:])
    mine_ref[...] = picked[0]
    count = picked[1].shape[1] // rows
    for i in range(count):
        other_ref[pl.ds(i * HOURS, HOURS), :] = picked[1][:, i * rows : (i + 1) * rows]
    if len(refs) > 2:
        top = stack_ref.shape[0] - HOURS
        for ref in stack:
            stack_ref[pl.ds(0, top), :] = ref[...]
        for i in range(count):
            here = pl.ds(i * rows, rows)
            beside = beside_ref[pl.ds(beside_ref.shape[0] - (count - i) * HOURS, HOURS), :]
            stack_ref[pl.ds(top, HOURS), here] = last_ref[:, here] + beside


def plane_rows(first, metas, values, before):
    rows = values[0].shape[1]
    slots = metas[0].shape[1]
    args = [first, *metas, *values, *before]
    shapes = [(HOURS, slots), (slots // rows * HOURS, rows)]
    if before:
        shapes.append(((len(before) - 1) * HOURS, slots))
    return pl.pallas_call(
        plane_rows_kernel,
        in_specs=[pl.BlockSpec(memory_space=pltpu.SMEM)]
        + [pl.BlockSpec(memory_space=pltpu.VMEM)] * (len(args) - 1),
        out_shape=[jax.ShapeDtypeStruct(shape, F32) for shape in shapes],
        compiler_params=params(),
        name="plane_rows",
        cost_estimate=pl.CostEstimate(flops=1_000_000_000, bytes_accessed=2_000_000, transcendentals=0),
    )(*args)


def gain(kernels):
    return jnp.max(jnp.sum(kernels, axis=1, keepdims=True), axis=0, keepdims=True)


def spectra(kind, kernels, wide):
    classes = kernels.shape[0]
    row = lax.broadcasted_iota(jnp.int32, (classes, kind.shape[1]), 0).astype(F32)
    hot = jnp.where(row == kind, 1.0, 0.0).astype(BF16)
    taps = jnp.transpose(kernels / gain(kernels))
    chosen = dot(jnp.concatenate(pieces(taps, 3)[::-1], axis=1), jnp.concatenate([hot] * 3, axis=0))
    return product(wide, chosen, 3)


def plane_spectrum_kernel(class_ref, kernels_ref, wide_ref, out_ref):
    kind = class_ref[1:2, : out_ref.shape[1]]
    out_ref[...] = spectra(kind, kernels_ref[...], wide_ref[...])


def plane_spectrum(meta, kernels, wide, rows):
    return pl.pallas_call(
        plane_spectrum_kernel,
        out_shape=jax.ShapeDtypeStruct((SPAN, rows), F32),
        compiler_params=params(),
        name="plane_spectrum",
        cost_estimate=SMALL,
    )(meta, kernels, wide)


def sides(even, pair, middle):
    return jnp.where(even, middle, pair), jnp.where(even, pair, middle)


def plane_call(kernel, name, shapes, flags, args):
    return pl.pallas_call(
        kernel,
        in_specs=[pl.BlockSpec(memory_space=pltpu.SMEM)] * len(flags)
        + [pl.BlockSpec(memory_space=pltpu.VMEM)] * len(args),
        out_shape=[jax.ShapeDtypeStruct(shape, F32) for shape in shapes],
        compiler_params=params(),
        name=name,
        cost_estimate=SMALL,
    )(*flags, *args)


def plane_first_kernel(
    flag_ref, here_ref, pair_ref, middle_ref, seen_ref, spec_ref, kernels_ref, forward, first, last, out_ref
):
    spec = spec_ref[...]
    before, after = sides(flag_ref[0] > 0.5, pair_ref[...], middle_ref[...])
    now, later = plane_delayed(before, here_ref[...], after, spec, forward[...], last[...], 3)
    known = plane_advanced(now, later * flag_ref[1], spec, forward[...], first[...], 3)
    out_ref[...] = seen_ref[...] - known * gain(kernels_ref[...])


def plane_delay_kernel(flag_ref, here_ref, pair_ref, middle_ref, spec_ref, forward, last, out_ref):
    body = pl.ds(0, HOURS)
    before, after = sides(flag_ref[0] > 0.5, pair_ref[body, :], middle_ref[body, :])
    out = plane_delayed(before, here_ref[body, :], after, spec_ref[...], forward[...], last[...], 2)
    for i in range(2):
        out_ref[pl.ds(i * HOURS, HOURS), :] = out[i]


def write_note(ref, rows):
    tail = [jnp.zeros((NOTE - len(rows), ref.shape[1]), F32)]
    ref[pl.ds(HOURS, NOTE), :] = jnp.concatenate(rows + tail, axis=0)


def plane_open_kernel(
    flag_ref, here_ref, pair_ref, middle_ref, pulled_ref, spec_ref, forward, first, last, out_ref, delayed_ref
):
    here = here_ref[...]
    spec = spec_ref[...]
    before, after = sides(flag_ref[0] > 0.5, pair_ref[...], middle_ref[...])
    now, later = plane_delayed(before, here, after, spec, forward[...], last[...], 2)
    out_ref[pl.ds(0, HOURS), :] = plane_advanced(now, later * flag_ref[1], spec, forward[...], first[...], 2)
    write_note(out_ref, [lanes(pulled_ref[...], here), lanes(now, now)])
    delayed_ref[pl.ds(0, HOURS), :] = now
    delayed_ref[pl.ds(HOURS, HOURS), :] = later


def plane_step_kernel(
    flag_ref,
    here_ref,
    pair_ref,
    two_ref,
    mirror_ref,
    pulled_ref,
    delayed_ref,
    old_z_ref,
    old_s_ref,
    old_delayed_ref,
    spec_ref,
    forward,
    first,
    total_ref,
    out_ref,
    kept_ref,
):
    tail, body = pl.ds(HOURS, NOTE), pl.ds(0, HOURS)
    total_ref[...] = (here_ref[tail, :] + pair_ref[tail, :]) + (two_ref[...] + mirror_ref[...])
    inverse = total(total_ref, 0) / total(total_ref, 1)
    z = pulled_ref[body, :] * inverse - old_z_ref[...]
    s = here_ref[body, :] * inverse - old_s_ref[...]
    both = delayed_ref[...] * inverse - old_delayed_ref[...]
    now, later = both[:HOURS], both[HOURS:]
    following = plane_advanced(now, later * flag_ref[1], spec_ref[...], forward[...], first[...], 2)
    out_ref[body, :] = following * inverse
    write_note(out_ref, [lanes(z, s), lanes(now, now)])
    for i, value in enumerate((z, s, now)):
        kept_ref[pl.ds(i * HOURS, HOURS), :] = value


def plane_close_kernel(
    here_ref, before_ref, pulled_ref, kept_ref, old_z_ref, old_s_ref, old_delayed_ref, spec_ref, forward, last, out_ref
):
    body = pl.ds(0, HOURS)
    here, raw = here_ref[body, :], pulled_ref[body, :]
    waves = product(forward[...], jnp.concatenate([before_ref[body, :], here], axis=0), 2)
    now = product(last[...], turn(waves, spec_ref[...], 1.0), 2)
    z, s, delayed = (kept_ref[pl.ds(i * HOURS, HOURS), :] for i in range(3))
    note = [pulled_ref[HOURS + i : HOURS + i + 1, :] for i in range(2)]
    for left in (raw, z, old_z_ref[...]):
        note += [lanes(left, right) for right in (here, s, old_s_ref[...])]
    parts = (now, delayed, old_delayed_ref[body, :])
    for i in range(3):
        note += [lanes(parts[i], parts[j]) for j in range(i, 3)]
    note.append(jnp.zeros((24 - len(note), here.shape[1]), F32))
    note = jnp.sum(jnp.concatenate(note, axis=0), axis=1, keepdims=True)
    shape = (24, out_ref.shape[2])
    row, col = (lax.broadcasted_iota(jnp.int32, shape, i) for i in range(2))
    note = jnp.sum(jnp.where(row == col, jnp.broadcast_to(note, shape), 0.0), axis=0, keepdims=True)
    out_ref[...] = jnp.broadcast_to(note[None], out_ref.shape)


def plane_weights(open_ref, close, scale):
    entry = lambda i: close[:, i : i + 1]
    n1, t1 = total(open_ref, 0), total(open_ref, 1)
    n2, t2 = entry(0), entry(1)
    a1 = t1 / n1
    a2, r2 = (t2 / n2) / a1, n2 / n1
    plain = (1.0, -a2, -r2)
    n3 = sum(plain[i] * plain[j] * entry(2 + 3 * i + j) for i in range(3) for j in range(3))
    pairs = [(i, j) for i in range(3) for j in range(i, 3)]
    t3 = sum(
        plain[i] * plain[j] * entry(11 + n) * (1.0 if i == j else 2.0) for n, (i, j) in enumerate(pairs)
    )
    a3, r3 = (t3 / n3) / a1, n3 / n2
    unit = 1.0 / (a1 * scale)
    c3 = unit / (a3 * (a2 - r2) - r3)
    c2 = -a3 * c3
    c1 = unit - r2 * c2
    step = c2 - c3 * a2
    return c1 - step - c3 * r2, step / a1, c3


def plane_combine_kernel(open_ref, close_ref, kernels_ref, stack_ref, mine_ref, beside_ref, out_ref):
    rows = open_ref.shape[1]
    close = jnp.sum(close_ref[...], axis=0)[0:1, :]
    e0, e1, e2 = plane_weights(open_ref, close, gain(kernels_ref[...]))
    for i in range(out_ref.shape[0] // rows):
        here = pl.ds(i * rows, rows)
        last = mine_ref[:, here] + beside_ref[pl.ds(i * HOURS, HOURS), :]
        value = stack_ref[pl.ds(0, HOURS), here] * e0 + stack_ref[pl.ds(HOURS, HOURS), here] * e1 + last * e2
        out_ref[here, :] = jnp.transpose(value)


def plane_finish_kernel(rows_ref, inc_ref, field_ref, out_ref):
    blocks, slots, width = inc_ref.shape
    weights = inc_ref[...].astype(F32).astype(BF16)
    for b in range(blocks):
        here = pl.ds(b * width, width)
        rows = jnp.concatenate(pieces(rows_ref[pl.ds(b * slots, slots), :], 2), axis=0)
        twice = jnp.concatenate([weights[b]] * 2, axis=0)
        added = lax.dot_general(twice, rows, (((0,), (0,)), ((), ())), preferred_element_type=F32)
        out_ref[here, :] = field_ref[here, :] + added


def plane_finish(rows, incidence, field):
    blocks, slots, width = incidence.shape
    hours = field.shape[1]
    step = 8
    return pl.pallas_call(
        plane_finish_kernel,
        grid=(blocks // step,),
        in_specs=[
            pl.BlockSpec((step * slots, hours), lambda i: (i, 0)),
            pl.BlockSpec((step, slots, width), lambda i: (i, 0, 0)),
            pl.BlockSpec((step * width, hours), lambda i: (i, 0)),
        ],
        out_specs=pl.BlockSpec((step * width, hours), lambda i: (i, 0)),
        out_shape=jax.ShapeDtypeStruct(field.shape, F32),
        compiler_params=params(),
        name="plane_finish",
    )(rows, incidence, field)


def plane_shards(incidence, row_gauge, gauge_kernel, kernels, observed, first_guess):
    rows, hours = observed.shape
    basin, tm = lax.axis_index("basin"), lax.axis_index("tm")
    z, x, y, c = basin // X_, basin % X_, tm // C_, tm % C_
    place = 2 * y + x
    first = jnp.stack([4 * c + (place ^ m) for m in range(4)] + [4 * c + place, 4 * (1 - c) + place])
    first = (first * rows).astype(jnp.int32)
    flags = jnp.stack([1 - z % 2, (z < Z_ - 1).astype(z.dtype), (z > 0).astype(z.dtype)]).astype(F32)
    forward, inverse_first, inverse_last, _ = turned_transforms(2)
    forward3, inverse_first3, inverse_last3, short3 = turned_transforms(3)
    block, noted = (hours, rows), (hours + NOTE, rows)

    parcel = send(incidence, first_guess, row_gauge, gauge_kernel)
    parcel, near, gauges, kinds, seen = lax.optimization_barrier(
        (parcel, incidence, row_gauge, gauge_kernel, observed)
    )
    parcel = moved(parcel, to_plane)
    meta = describe(near, gauges)
    meta = jnp.concatenate([meta, moved(meta, over_x)], axis=1)
    meta = jnp.concatenate([meta, moved(meta, z_pair)], axis=1)
    seen = observe(seen, moved(seen, hour_before), kinds, kernels, short3, [forward3, inverse_first3])
    seen = moved(seen, to_plane)
    parcel, seen = lax.optimization_barrier((parcel, seen))
    parcels = [parcel, moved(parcel, over_core)]
    spec = plane_spectrum(parcel[hours:], kernels, short3, rows)
    parcels[1], seen, meta, spec = lax.optimization_barrier((parcels[1], seen, meta, spec))
    around = [meta, moved(meta, z_two)]
    dense = spread(first, parcels, rows)
    metas = [value[hours:] for value in parcels]
    sums = dense[0] + sum(moved(value, where) for value, where in zip(dense[1:], SQUARE))
    sums = [sums, moved(sums, z_pair), moved(sums, z_middle)]
    coupled = plane_couple(first, around[0], rows)
    coupled, sums = lax.optimization_barrier((coupled, sums))
    coupling = plane_couple(first, around[1], rows, coupled)
    (pulled0,) = plane_call(
        plane_first_kernel,
        "plane_first",
        [block],
        [flags],
        [*sums, seen, spec, kernels, forward3, inverse_first3, inverse_last3],
    )

    def mixing(pulled, extra):
        values = [pulled] + [moved(pulled, where) for where in SQUARE]
        mine, other = plane_mix(coupling, values, extra)
        beside = moved(other, over_core)
        return values, mine + beside[: pulled.shape[0]], beside

    values, mixed0, _ = mixing(pulled0, [])
    picked, theirs = plane_rows(first, metas, values, [])
    sums = [mixed0, moved(mixed0, z_pair), moved(mixed0, z_middle)]
    pulled1, delayed0 = plane_call(
        plane_open_kernel,
        "plane_open",
        [noted, (2 * hours, rows)],
        [flags],
        [*sums, pulled0, spec, forward, inverse_first, inverse_last],
    )

    values, mixed1, beside = mixing(pulled1, [theirs])
    picked, theirs, stack = plane_rows(first, metas, values, [picked, beside])
    sums = [mixed1, moved(mixed1, z_pair), moved(mixed1, z_middle)]
    two, mirror = moved(mixed1[hours:], z_two), moved(mixed1[hours:], z_mirror)
    (delayed1,) = plane_call(
        plane_delay_kernel, "plane_delay", [(2 * hours, rows)], [flags], [*sums, spec, forward, inverse_last]
    )
    open_note, pulled2, kept = plane_call(
        plane_step_kernel,
        "plane_step",
        [(NOTE, rows), noted, (3 * hours, rows)],
        [flags],
        [*sums[:2], two, mirror, pulled1, delayed1, pulled0, mixed0, delayed0, spec, forward, inverse_first],
    )

    values, mixed2, beside = mixing(pulled2, [theirs])
    picked, theirs, stack = plane_rows(first, metas, values, [stack, picked, beside])
    (note,) = plane_call(
        plane_close_kernel,
        "plane_close",
        [(Z_ * X_ * Y_ * C_, 8, rows // 2)],
        [],
        [mixed2, moved(mixed2, z_next), pulled2, kept, pulled0, mixed0, delayed0, spec, forward, inverse_last],
    )
    close_note = lax.all_to_all(note, ("basin", "tm"), 0, 0, tiled=False)
    (answer,) = plane_call(
        plane_combine_kernel,
        "plane_combine",
        [(parcel.shape[1], hours)],
        [],
        [open_note, close_note, kernels, stack, picked, moved(theirs, over_core)],
    )
    return plane_finish(moved(answer, from_plane), incidence, first_guess)


def solution(mesh):
    planes = dict(mesh.shape) == {"basin": Z_ * X_, "tm": Y_ * C_}
    in_specs = (
        P("basin", None, None),
        P("basin"),
        P("basin"),
        P(),
        P("basin", "tm"),
        P("basin", "tm"),
    )
    return jax.shard_map(
        plane_shards if planes else shards, mesh=mesh, in_specs=in_specs, out_specs=P("basin", "tm"), check_vma=False
    )
```

```python
import functools

import jax
import jax.numpy as jnp
import numpy as np
from jax import lax
from jax.experimental import pallas as pl
from jax.experimental.pallas import tpu as pltpu
from jax.sharding import PartitionSpec as P

F32 = jnp.float32
BF16 = jnp.bfloat16
HIGH = lax.Precision.HIGHEST
SPAN = 256
MIB = 1024 * 1024


SMALL = pl.CostEstimate(flops=1, bytes_accessed=1, transcendentals=0)


def params(mib=16):
    return pltpu.CompilerParams(vmem_limit_bytes=mib * MIB)


def transforms():
    half = SPAN // 2
    freq = 2.0 * np.pi * (np.arange(half) + 0.5) / SPAN
    phase = np.arange(SPAN)[:, None] * freq[None, :]
    forward = np.concatenate([np.cos(phase), -np.sin(phase)], axis=1)
    inverse = forward.T * (2.0 / SPAN)
    return (
        jnp.asarray(forward, F32),
        jnp.asarray(inverse[:, :half], F32),
        jnp.asarray(inverse[:, half:], F32),
    )


def dot(a, b):
    return jnp.dot(a, b, preferred_element_type=F32)


def exact(a, b):
    return jnp.dot(a, b, precision=HIGH, preferred_element_type=F32)


def pieces(value, count):
    out = []
    for _ in range(count):
        piece = value.astype(BF16)
        out.append(piece)
        value = value - piece.astype(F32)
    return out


def pick(hot, value):
    return sum(dot(hot, piece) for piece in pieces(value, 3))


def prepare_kernel(inc_ref, field_ref, partial_ref, gram_ref):
    blocks, slots, width = inc_ref.shape
    rows = blocks * slots
    weights = inc_ref[...].astype(F32).astype(BF16)
    for b in range(blocks):
        value = field_ref[pl.ds(b * width, width), :]
        partial_ref[pl.ds(b * slots, slots), :] = pick(weights[b], value)
    flat = weights.reshape(rows, width)
    full = lax.dot_general(flat, flat, (((1,), (1,)), ((), ())), preferred_element_type=F32)
    row = lax.broadcasted_iota(jnp.int32, (rows, rows), 0)
    col = lax.broadcasted_iota(jnp.int32, (rows, rows), 1)
    own = jnp.where(row // slots == col // slots, full, 0.0)
    gram_ref[...] = jnp.sum(own.reshape(blocks, slots, rows), axis=0)


def prepare(incidence, field):
    blocks, slots, width = incidence.shape
    hours = field.shape[1]
    step = 8
    return pl.pallas_call(
        prepare_kernel,
        grid=(blocks // step,),
        in_specs=[
            pl.BlockSpec((step, slots, width), lambda i: (i, 0, 0)),
            pl.BlockSpec((step * width, hours), lambda i: (i, 0)),
        ],
        out_specs=[
            pl.BlockSpec((step * slots, hours), lambda i: (i, 0)),
            pl.BlockSpec((slots, step * slots), lambda i: (0, i)),
        ],
        out_shape=[
            jax.ShapeDtypeStruct((blocks * slots, hours), F32),
            jax.ShapeDtypeStruct((slots, blocks * slots), F32),
        ],
        compiler_params=params(56),
        name="prepare",
    )(incidence, field)


def table_kernel(gauge_ref, partial_ref, out_ref):
    slots = partial_ref.shape[0]
    rows = out_ref.shape[0]
    first = pl.program_id(0) * rows
    gauge = lax.broadcasted_iota(jnp.int32, (rows, slots), 0) + first
    hot = jnp.where(gauge_ref[...] == gauge, 1.0, 0.0).astype(BF16)
    out_ref[...] = pick(hot, partial_ref[...])


def table(row_gauge, partial, gauges):
    slots, hours = partial.shape
    step = 256
    return pl.pallas_call(
        table_kernel,
        grid=(gauges // step,),
        in_specs=[
            pl.BlockSpec((1, slots), lambda i: (0, 0)),
            pl.BlockSpec((slots, hours), lambda i: (0, 0)),
        ],
        out_specs=pl.BlockSpec((step, hours), lambda i: (i, 0)),
        out_shape=jax.ShapeDtypeStruct((gauges, hours), F32),
        compiler_params=params(56),
        name="table",
    )(row_gauge.reshape(1, slots), partial)


def couple_kernel(first_ref, lane_ref, sub_ref, gram_ref, high_ref, low_ref, near_ref):
    slots = gram_ref.shape[0]
    count = lane_ref.shape[1]
    rows, cols = high_ref.shape
    tile = 256
    first = first_ref[0]

    @pl.when(pl.program_id(0) == 0)
    def _():
        row = lax.broadcasted_iota(jnp.int32, (tile, tile), 0)
        col = lax.broadcasted_iota(jnp.int32, (tile, tile), 1)
        same = row // slots == col // slots
        mine = lax.broadcasted_iota(jnp.int32, (rows, tile), 0) + first

        def body(i, carry):
            here = pl.ds(pl.multiple_of(i * tile, tile), tile)
            block = jnp.concatenate([gram_ref[:, here]] * (tile // slots), axis=0)
            block = jnp.where(same, block, 0.0).astype(BF16)
            hot = jnp.where(lane_ref[:, here] == mine, 1.0, 0.0).astype(BF16)
            near_ref[:, here] = dot(hot, block)
            return carry

        lax.fori_loop(0, count // tile, body, 0)

    def chunk(i, total):
        here = pl.ds(pl.multiple_of(i * 1024, 1024), 1024)
        gauge = lax.broadcasted_iota(jnp.int32, (1024, cols), 1) + pl.program_id(0) * cols
        hot = jnp.where(sub_ref[here, :] == gauge, 1.0, 0.0).astype(BF16)
        near = near_ref[:, here]
        high = near.astype(BF16)
        low = (near - high.astype(F32)).astype(BF16)
        return total + dot(high, hot) + dot(low, hot)

    total = lax.fori_loop(0, count // 1024, chunk, jnp.zeros((rows, cols), F32))
    high, low = pieces(total, 2)
    high_ref[...] = high
    low_ref[...] = low


def couple(first, row_gauge, gram, rows, gauges):
    count = row_gauge.shape[0]
    step = 256
    return pl.pallas_call(
        couple_kernel,
        grid=(gauges // step,),
        in_specs=[
            pl.BlockSpec(memory_space=pltpu.SMEM),
            pl.BlockSpec((1, count), lambda i: (0, 0)),
            pl.BlockSpec((count, 1), lambda i: (0, 0)),
            pl.BlockSpec(gram.shape, lambda i: (0, 0)),
        ],
        out_specs=[pl.BlockSpec((rows, step), lambda i: (0, i))] * 2,
        out_shape=[jax.ShapeDtypeStruct((rows, gauges), BF16)] * 2,
        scratch_shapes=[pltpu.VMEM((rows, count), F32)],
        compiler_params=params(56),
        name="couple",
    )(first, row_gauge.reshape(1, count), row_gauge.reshape(count, 1), gram)


def mix_kernel(high_ref, low_ref, value_ref, out_ref):
    high = high_ref[...]
    low = low_ref[...]
    one, two, three = pieces(value_ref[...], 3)
    out_ref[...] = (dot(high, three) + dot(low, two)) + (dot(high, two) + dot(low, one)) + dot(high, one)


def mix(high, low, value):
    return pl.pallas_call(
        mix_kernel,
        out_shape=jax.ShapeDtypeStruct((high.shape[0], value.shape[1]), F32),
        compiler_params=params(56),
        name="mix",
    )(high, low, value)


def spectrum_kernel(class_ref, kernels_ref, forward_ref, out_ref):
    rows = class_ref.shape[0]
    classes, taps = kernels_ref.shape
    kind = lax.broadcasted_iota(jnp.int32, (rows, classes), 1)
    hot = jnp.where(class_ref[...] == kind, 1.0, 0.0)
    out_ref[...] = exact(exact(hot, kernels_ref[...]), forward_ref[pl.ds(0, taps), :])


def spectrum(gauge_kernel, kernels, forward):
    rows = gauge_kernel.shape[0]
    return pl.pallas_call(
        spectrum_kernel,
        out_shape=jax.ShapeDtypeStruct((rows, SPAN), F32),
        compiler_params=params(56),
        name="spectrum",
    )(gauge_kernel.reshape(rows, 1), kernels, forward)


def delayed(before, here, after, spec, forward, inverse_last):
    rows, half = here.shape
    stacked = jnp.concatenate(
        [jnp.concatenate([before, here], axis=1), jnp.concatenate([here, after], axis=1)], axis=0
    )
    waves = exact(stacked, forward)
    real, imag = waves[:, :half], waves[:, half:]
    kr = jnp.concatenate([spec[:, :half]] * 2, axis=0)
    ki = jnp.concatenate([spec[:, half:]] * 2, axis=0)
    turned = jnp.concatenate([real * kr - imag * ki, real * ki + imag * kr], axis=1)
    out = exact(turned, inverse_last)
    return out[:rows], out[rows:]


def advanced(here, after, spec, forward, inverse_first):
    half = here.shape[1]
    waves = exact(jnp.concatenate([here, after], axis=1), forward)
    real, imag = waves[:, :half], waves[:, half:]
    kr, ki = spec[:, :half], spec[:, half:]
    turned = jnp.concatenate([real * kr + imag * ki, imag * kr - real * ki], axis=1)
    return exact(turned, inverse_first)


def lanes(a, b):
    return jnp.sum(a * b, axis=0, keepdims=True)


def total(ref, row):
    return jnp.sum(ref[row : row + 1, :], axis=1, keepdims=True)


def ratios(ref):
    square = total(ref, 0)
    alpha = jnp.sqrt(square)
    beta = jnp.sqrt(jnp.maximum(total(ref, 1) / square - 2.0 * total(ref, 2) + square, 0.0))
    return alpha, beta


def first_kernel(
    more_ref, sums_ref, observed_ref, spec_ref, forward_ref, first_ref, last_ref, out_ref, note_ref
):
    rows, half = observed_ref.shape[0] // 2, observed_ref.shape[1]
    spec, forward = spec_ref[...], forward_ref[...]
    before, here, after = (sums_ref[pl.ds(i * rows, rows), :] for i in range(3))
    now, later = delayed(before, here, after, spec, forward, last_ref[...])
    start = observed_ref[pl.ds(0, rows), :] - now
    start_later = (observed_ref[pl.ds(rows, rows), :] - later) * more_ref[0]
    out_ref[...] = advanced(start, start_later, spec, forward, first_ref[...])
    note_ref[...] = jnp.concatenate([lanes(start, start), jnp.zeros((7, half), F32)], axis=0)


def first_step(more, sums, observed, spec, mats):
    rows, half = spec.shape[0], observed.shape[1]
    return pl.pallas_call(
        first_kernel,
        in_specs=[pl.BlockSpec(memory_space=pltpu.SMEM)] + [pl.BlockSpec(memory_space=pltpu.VMEM)] * 6,
        out_shape=[jax.ShapeDtypeStruct((rows, half), F32), jax.ShapeDtypeStruct((8, half), F32)],
        compiler_params=params(56),
        name="first_step",
    )(more, sums, observed, spec, *mats)


def step_kernel(
    opening,
    final,
    more_ref,
    note_ref,
    sums_ref,
    spec_ref,
    forward_ref,
    first_ref,
    last_ref,
    pulled_ref,
    *refs,
):
    if opening:
        state_ref = None
    else:
        state_ref, *refs = refs
    if final:
        (out_note_ref,) = refs
    else:
        new_ref, out_ref, out_note_ref = refs
    rows, half = pulled_ref.shape
    spec, forward = spec_ref[...], forward_ref[...]
    if opening:
        scale = 1.0 / jnp.sqrt(total(note_ref, 0))
        along = sums_ref[...] * scale
        new_s, new_su = along, along
        new_zu = pulled_ref[...] * scale
        new_z = new_zu
    else:
        alpha, beta = ratios(note_ref)
        a, b, g = 1.0 / (alpha * beta), alpha / beta, beta / alpha
        wide = pl.ds(0, 3 * rows), pl.ds(3 * rows, 3 * rows)
        new_su = sums_ref[...] * a - state_ref[wide[1], :] * b
        new_s = new_su - state_ref[wide[0], :] * g
        new_zu = pulled_ref[...] * a - state_ref[pl.ds(7 * rows, rows), :] * b
        new_z = new_zu - state_ref[pl.ds(6 * rows, rows), :] * g
    before, here, after = (new_s[i * rows : (i + 1) * rows] for i in range(3))
    now, later = delayed(before, here, after, spec, forward, last_ref[...])
    out_note_ref[...] = jnp.concatenate(
        [lanes(new_z, here), lanes(now, now), lanes(new_zu, here), jnp.zeros((5, half), F32)], axis=0
    )
    if not final:
        new_ref[pl.ds(0, 3 * rows), :] = new_s
        new_ref[pl.ds(3 * rows, 3 * rows), :] = new_su
        new_ref[pl.ds(6 * rows, rows), :] = new_z
        new_ref[pl.ds(7 * rows, rows), :] = new_zu
        out_ref[...] = advanced(now, later * more_ref[0], spec, forward, first_ref[...])


def next_step(more, note, sums, spec, mats, pulled, state, final):
    rows, half = pulled.shape
    opening = state is None
    shapes = [
        jax.ShapeDtypeStruct((8 * rows, half), F32),
        jax.ShapeDtypeStruct((rows, half), F32),
        jax.ShapeDtypeStruct((8, half), F32),
    ]
    args = [more, note, sums, spec, *mats, pulled] + ([] if opening else [state])
    return pl.pallas_call(
        functools.partial(step_kernel, opening, final),
        in_specs=[pl.BlockSpec(memory_space=pltpu.SMEM)]
        + [pl.BlockSpec(memory_space=pltpu.VMEM)] * (len(args) - 1),
        out_shape=shapes[2:] if final else shapes,
        compiler_params=params(56),
        name="next_step",
    )(*args)


def weights_of(notes):
    start = jnp.sqrt(total(notes[0], 0))
    zero = jnp.zeros_like(start)
    units = [1.0 / start, zero, zero]
    z, zu = list(units), list(units)
    phibar = start
    alpha, beta = ratios(notes[1])
    rhobar = alpha
    w = [value / alpha for value in z]
    result = [zero] * 3
    steps = len(notes) - 1
    for k in range(steps):
        rho = jnp.sqrt(rhobar * rhobar + beta * beta)
        cosine, sine = rhobar / rho, beta / rho
        phi, phibar = cosine * phibar, sine * phibar
        result = [r + phi / rho * value for r, value in zip(result, w)]
        if k < steps - 1:
            a, b, g = 1.0 / (alpha * beta), alpha / beta, beta / alpha
            zu = [(a if i == k + 1 else 0.0) - b * value for i, value in enumerate(zu)]
            z = [value - g * old for value, old in zip(zu, z)]
            alpha, beta = ratios(notes[k + 2])
            theta = sine * alpha
            rhobar = -cosine * alpha
            w = [value / alpha - theta / rho * old for value, old in zip(z, w)]
    return result


def finish_kernel(n0, n1, n2, n3, gauge_ref, q0, q1, q2, inc_ref, field_ref, out_ref, rows_ref):
    blocks, slots, width = inc_ref.shape
    count = rows_ref.shape[0]
    gauges = q0.shape[0]
    step = pl.program_id(0)

    @pl.when(step == 0)
    def _():
        e0, e1, e2 = weights_of([n0, n1, n2, n3])
        width_ = 512

        def body(i, value):
            here = pl.ds(pl.multiple_of(i * width_, width_), width_)
            mixed = q0[here, :] * e0 + q1[here, :] * e1 + q2[here, :] * e2
            gauge = lax.broadcasted_iota(jnp.int32, (count, width_), 1) + i * width_
            hot = jnp.where(gauge_ref[...] == gauge, 1.0, 0.0).astype(BF16)
            return value + pick(hot, mixed)

        rows_ref[...] = lax.fori_loop(0, gauges // width_, body, jnp.zeros(rows_ref.shape, F32))

    weights = inc_ref[...].astype(F32).astype(BF16)
    for b in range(blocks):
        here = pl.ds(b * width, width)
        rows = rows_ref[pl.ds(pl.multiple_of((step * blocks + b) * slots, slots), slots), :]
        added = sum(
            lax.dot_general(weights[b], piece, (((0,), (0,)), ((), ())), preferred_element_type=F32)
            for piece in pieces(rows, 3)
        )
        out_ref[here, :] = field_ref[here, :] + added


def finish(notes, row_gauge, gathered, incidence, field):
    blocks, slots, width = incidence.shape
    hours = field.shape[1]
    count = row_gauge.shape[0]
    step = 8
    whole = lambda shape: pl.BlockSpec(shape, lambda i: (0, 0))
    return pl.pallas_call(
        finish_kernel,
        grid=(blocks // step,),
        in_specs=[whole(n.shape) for n in notes]
        + [whole((count, 1))]
        + [whole(q.shape) for q in gathered]
        + [
            pl.BlockSpec((step, slots, width), lambda i: (i, 0, 0)),
            pl.BlockSpec((step * width, hours), lambda i: (i, 0)),
        ],
        out_specs=pl.BlockSpec((step * width, hours), lambda i: (i, 0)),
        out_shape=jax.ShapeDtypeStruct(field.shape, F32),
        scratch_shapes=[pltpu.VMEM((count, hours), F32)],
        compiler_params=params(56),
        name="finish",
    )(*notes, row_gauge.reshape(count, 1), *gathered, incidence, field)


def shifted(value, axis, by):
    devices = lax.axis_size(axis)
    pairs = [(i, i + by) for i in range(devices) if 0 <= i + by < devices]
    return lax.ppermute(value, axis, pairs)


def window(value):
    return jnp.concatenate([shifted(value, "tm", 1), value, shifted(value, "tm", -1)], axis=0)


def gathered_rows(value):
    owners = lax.axis_size("basin")
    copies = jnp.broadcast_to(value[None], (owners,) + value.shape)
    return lax.all_to_all(copies, "basin", 0, 0, tiled=False)


def over_hours(note):
    blocks = lax.axis_size("tm")
    result = note
    for by in range(1, blocks):
        result = result + lax.ppermute(note, "tm", [(i, (i + by) % blocks) for i in range(blocks)])
    return result


def shards(incidence, row_gauge, gauge_kernel, kernels, observed, first_guess):
    owners = lax.axis_size("basin")
    rows, hours = observed.shape
    gauges = rows * owners
    mats = transforms()
    spec = spectrum(gauge_kernel, kernels, mats[0])
    more = (lax.axis_index("tm") < lax.axis_size("tm") - 1).astype(F32).reshape(1)
    partial, gram = prepare(incidence, first_guess)
    all_gram = lax.all_gather(gram, "basin", axis=1, tiled=True)
    all_rows = lax.all_gather(row_gauge, "basin", axis=0, tiled=True)
    dense = table(row_gauge, partial, gauges).reshape(owners, rows, hours)
    sums = jnp.sum(lax.all_to_all(dense, "basin", 0, 0, tiled=False), axis=0)
    both = jnp.concatenate([observed, shifted(observed, "tm", -1)], axis=0)
    first = (lax.axis_index("basin") * rows).astype(jnp.int32).reshape(1)
    high, low = couple(first, all_rows, all_gram, rows, gauges)

    pulled, note = first_step(more, window(sums), both, spec, mats)
    notes, kept, state = [], [], None
    for k in range(3):
        everyone = gathered_rows(jnp.concatenate([pulled, note], axis=0))
        value = everyone[:, :rows].reshape(gauges, hours)
        notes.append(over_hours(jnp.sum(everyone[:, rows:], axis=0)))
        kept.append(value)
        around = window(mix(high, low, value))
        final = k == 2
        result = next_step(more, notes[-1], around, spec, mats, pulled, state, final)
        if final:
            (note,) = result
        else:
            state, pulled, note = result
    notes.append(over_hours(jnp.sum(gathered_rows(note), axis=0)))
    return finish(notes, row_gauge, kept, incidence, first_guess)


Z_, X_, Y_, C_ = 4, 2, 2, 2
NOTE = 8
HOURS = SPAN // 2


def device(z, x, y, c):
    return (z * X_ + x) * (Y_ * C_) + y * C_ + c


def moved(value, where):
    pairs = []
    for z, x, y, c in np.ndindex(Z_, X_, Y_, C_):
        target = where(z, x, y, c)
        if target is not None:
            pairs.append((device(z, x, y, c), device(*target)))
    return lax.ppermute(value, ("basin", "tm"), pairs)


def to_plane(z, x, y, c):
    return 2 * y + c, x, z & 1, z >> 1


def hour_before(z, x, y, c):
    t = 2 * y + c - 1
    return (z, x, t >> 1, t & 1) if t >= 0 else None


def from_plane(z, x, y, c):
    return 2 * c + y, x, z >> 1, z & 1


def over_x(z, x, y, c):
    return z, 1 - x, y, c


def over_y(z, x, y, c):
    return z, x, 1 - y, c


def over_xy(z, x, y, c):
    return z, 1 - x, 1 - y, c


def over_core(z, x, y, c):
    return z, x, y, 1 - c


def z_pair(z, x, y, c):
    return z ^ 1, x, y, c


def z_middle(z, x, y, c):
    return (3 - z, x, y, c) if z in (1, 2) else None


def z_two(z, x, y, c):
    return z ^ 2, x, y, c


def z_mirror(z, x, y, c):
    return 3 - z, x, y, c


def z_next(z, x, y, c):
    return (z + 1, x, y, c) if z < 3 else None


SQUARE = (over_x, over_y, over_xy)


def split_constant(value):
    out = []
    for _ in range(3):
        piece = value.astype(jnp.bfloat16)
        out.append(piece)
        value = value - piece.astype(np.float64)
    return out


ORDERS = {2: ((0, 1), (1, 0), (0, 0)), 3: ((0, 2), (1, 1), (2, 0), (0, 1), (1, 0), (0, 0))}


def widened(mat, order):
    parts = split_constant(mat)
    return jnp.asarray(np.concatenate([parts[i] for i, _ in ORDERS[order]], axis=1))


def product(wide, value, order):
    parts = pieces(value, order)
    return dot(wide, jnp.concatenate([parts[j] for _, j in ORDERS[order]], axis=0))


def turned_transforms(order):
    half = SPAN // 2
    freq = 2.0 * np.pi * (np.arange(half) + 0.5) / SPAN
    phase = freq[:, None] * np.arange(SPAN)[None, :]
    forward = np.concatenate([np.cos(phase), -np.sin(phase)], axis=0)
    inverse = forward.T * (2.0 / SPAN)
    return [widened(mat, order) for mat in (forward, inverse[:half], inverse[half:], forward[:, :half])]


def turn(waves, spec, sign):
    half = waves.shape[0] // 2
    real, imag = waves[:half], waves[half:]
    kr, ki = spec[:half], spec[half:] * sign
    return jnp.concatenate([real * kr - imag * ki, real * ki + imag * kr], axis=0)


def plane_delayed(before, here, after, spec, forward, last, order):
    rows = here.shape[1]
    pairs = [jnp.concatenate(pair, axis=0) for pair in ((before, here), (here, after))]
    waves = product(forward, jnp.concatenate(pairs, axis=1), order)
    turned = [turn(waves[:, i * rows : (i + 1) * rows], spec, 1.0) for i in range(2)]
    out = product(last, jnp.concatenate(turned, axis=1), order)
    return out[:, :rows], out[:, rows:]


def plane_advanced(here, after, spec, forward, first, order):
    waves = product(forward, jnp.concatenate([here, after], axis=0), order)
    return product(first, turn(waves, spec, -1.0), order)


def describe_kernel(inc_ref, gauge_ref, out_ref):
    blocks, slots, width = inc_ref.shape
    tile = 8
    side = tile * slots
    weights = inc_ref[...].astype(F32).astype(BF16)
    row = lax.broadcasted_iota(jnp.int32, (side, side), 0)
    col = lax.broadcasted_iota(jnp.int32, (side, side), 1)
    same = row // slots == col // slots
    for i in range(blocks // tile):
        flat = weights[i * tile : (i + 1) * tile].reshape(side, width)
        full = lax.dot_general(flat, flat, (((1,), (1,)), ((), ())), preferred_element_type=F32)
        own = jnp.where(same, full, 0.0)
        out_ref[pl.ds(0, slots), pl.ds(i * side, side)] = jnp.sum(own.reshape(tile, slots, side), axis=0)
    out_ref[pl.ds(slots, 8), :] = jnp.broadcast_to(gauge_ref[...].astype(F32), (8, blocks * slots))


def describe(incidence, row_gauge):
    blocks, slots, _ = incidence.shape
    count = blocks * slots
    return pl.pallas_call(
        describe_kernel,
        out_shape=jax.ShapeDtypeStruct((slots + 8, count), F32),
        compiler_params=params(),
        name="describe",
        cost_estimate=SMALL,
    )(incidence, row_gauge.reshape(1, count))


def label_kernel(seen_ref, gauge_ref, kind_ref, out_ref):
    rows = seen_ref.shape[0]
    count = gauge_ref.shape[1]
    turned = jnp.transpose(seen_ref[...])
    step = out_ref.shape[0] - 8
    for i in range(count // rows):
        out_ref[pl.ds(0, step), pl.ds(i * rows, rows)] = turned[i * step : (i + 1) * step]
    kinds = jnp.concatenate([kind_ref[...].astype(F32), jnp.zeros((1, count - rows), F32)], axis=1)
    out_ref[pl.ds(step, 8), :] = jnp.concatenate(
        [gauge_ref[...].astype(F32), kinds, jnp.zeros((6, count), F32)], axis=0
    )


def label(seen, row_gauge, gauge_kernel):
    rows, hours = seen.shape
    count = row_gauge.shape[0]
    return pl.pallas_call(
        label_kernel,
        out_shape=jax.ShapeDtypeStruct((hours * rows // count + 8, count), F32),
        compiler_params=params(),
        name="label",
        cost_estimate=SMALL,
    )(seen, row_gauge.reshape(1, count), gauge_kernel.reshape(1, rows))


def send_kernel(inc_hbm, field_hbm, out_ref, inc_ref, field_ref, sems):
    blocks, slots, width = inc_ref.shape
    chunks = sems.shape[0]
    step = blocks // chunks
    copies = []
    for i in range(chunks):
        near = pl.ds(i * step, step)
        far = pl.ds(i * step * width, step * width)
        copies.append(
            (
                pltpu.make_async_copy(inc_hbm.at[near], inc_ref.at[near], sems.at[i, 0]),
                pltpu.make_async_copy(field_hbm.at[far], field_ref.at[far], sems.at[i, 1]),
            )
        )
        for copy in copies[-1]:
            copy.start()
    for i in range(chunks):
        for copy in copies[i]:
            copy.wait()
        parts = []
        for b in range(i * step, (i + 1) * step):
            weight = inc_ref[b].astype(F32).astype(BF16)
            value = jnp.concatenate(pieces(field_ref[pl.ds(b * width, width), :], 3)[::-1], axis=0)
            parts.append(dot(jnp.concatenate([weight] * 3, axis=1), value))
        out_ref[:, pl.ds(i * step * slots, step * slots)] = jnp.transpose(jnp.concatenate(parts, axis=0))


def send(incidence, field):
    blocks, slots, width = incidence.shape
    hours = field.shape[1]
    chunks = 4
    return pl.pallas_call(
        send_kernel,
        in_specs=[pl.BlockSpec(memory_space=pltpu.HBM)] * 2,
        out_shape=jax.ShapeDtypeStruct((hours, blocks * slots), F32),
        scratch_shapes=[
            pltpu.VMEM(incidence.shape, incidence.dtype),
            pltpu.VMEM(field.shape, F32),
            pltpu.SemaphoreType.DMA((chunks, 2)),
        ],
        compiler_params=params(),
        name="send",
        cost_estimate=SMALL,
    )(incidence, field)


def hot_rows(gauge, first, rows):
    mine = (lax.broadcasted_iota(jnp.int32, (rows, gauge.shape[1]), 0) + first).astype(F32)
    return jnp.where(gauge == mine, 1.0, 0.0).astype(BF16)


def spread_kernel(first_ref, mine_ref, other_ref, meta_ref, meta_other_ref, *out_refs):
    rows = out_refs[0].shape[1]
    value = jnp.concatenate([mine_ref[...], other_ref[...]], axis=1)
    gauge = jnp.concatenate([meta_ref[0:1, :], meta_other_ref[0:1, :]], axis=1)
    stacked = jnp.concatenate(pieces(value, 3), axis=0)
    for m, out_ref in enumerate(out_refs):
        hot = hot_rows(gauge, first_ref[m], rows)
        result = lax.dot_general(stacked, hot, (((1,), (1,)), ((), ())), preferred_element_type=F32)
        out_ref[...] = (result[2 * HOURS :] + result[HOURS : 2 * HOURS]) + result[:HOURS]


def spread(first, parcels, metas, rows):
    return pl.pallas_call(
        spread_kernel,
        in_specs=[pl.BlockSpec(memory_space=pltpu.SMEM)] + [pl.BlockSpec(memory_space=pltpu.VMEM)] * 4,
        out_shape=[jax.ShapeDtypeStruct((HOURS, rows), F32)] * 4,
        compiler_params=params(),
        name="spread",
        cost_estimate=SMALL,
    )(first, *parcels, *metas)


def plane_couple_kernel(last, first_ref, *refs):
    if last:
        all_ref, before_ref, high_ref, low_ref, total_ref, meta_ref = refs
        total_ref[...] = before_ref[...]
    else:
        all_ref, total_ref, meta_ref = refs
        total_ref[...] = jnp.zeros_like(total_ref)
    parts, height, count = meta_ref.shape
    slots = height - 8
    cols, rows = total_ref.shape
    tile = 256
    for i in range(parts):
        meta_ref[i] = all_ref[:, i * count : (i + 1) * count]
    row = lax.broadcasted_iota(jnp.int32, (tile, tile), 0)
    col = lax.broadcasted_iota(jnp.int32, (tile, tile), 1)
    same = row // slots == col // slots

    def body(i, carry):
        gauge = meta_ref[i, slots : slots + 1, :]
        near = []
        for j in range(count // tile):
            here = slice(j * tile, (j + 1) * tile)
            block = jnp.concatenate([meta_ref[i, :slots, here]] * (tile // slots), axis=0)
            block = jnp.where(same, block, 0.0).astype(BF16)
            mine = jnp.concatenate(
                [hot_rows(gauge[:, here], first_ref[4 + h], rows // 2) for h in range(2)], axis=0
            )
            near.append(
                lax.dot_general(block, mine, (((1,), (1,)), ((), ())), preferred_element_type=F32)
            )
        near = jnp.concatenate(near, axis=0)
        high = near.astype(BF16)
        rest = near - high.astype(F32)
        hot = jnp.concatenate([hot_rows(gauge, first_ref[m], cols // 4) for m in range(4)], axis=0)
        total_ref[...] += dot(hot, high)

        @pl.when(jnp.max(jnp.abs(rest)) > 0.0)
        def _():
            total_ref[...] += dot(hot, rest.astype(BF16))

        return carry

    lax.fori_loop(0, parts, body, 0)
    if last:
        high, low = pieces(total_ref[...], 2)
        high_ref[...] = high
        low_ref[...] = low


def plane_couple(first, meta, rows, before=None):
    height, wide = meta.shape
    parts = 2 * X_
    shape = (4 * rows, 2 * rows)
    last = before is not None
    args = [first, meta] + ([before] if last else [])
    scratch = [pltpu.VMEM((parts, height, wide // parts), F32)]
    return pl.pallas_call(
        functools.partial(plane_couple_kernel, last),
        in_specs=[pl.BlockSpec(memory_space=pltpu.SMEM)]
        + [pl.BlockSpec(memory_space=pltpu.VMEM)] * (len(args) - 1),
        out_shape=[jax.ShapeDtypeStruct(shape, BF16)] * 2 if last else jax.ShapeDtypeStruct(shape, F32),
        scratch_shapes=([pltpu.VMEM(shape, F32)] if last else []) + scratch,
        compiler_params=params(),
        name="plane_couple",
        cost_estimate=pl.CostEstimate(
            flops=2 * 8 * wide * rows * rows, bytes_accessed=2_000_000, transcendentals=0
        ),
    )(*args)


def plane_mix_kernel(high_ref, low_ref, a_ref, b_ref, c_ref, d_ref, *refs):
    *extra, mine_ref, other_ref = refs
    refs = (a_ref, b_ref, c_ref, d_ref)
    height, rows = a_ref.shape
    body = pl.ds(0, HOURS)
    one, two = pieces(jnp.concatenate([ref[body, :] for ref in refs], axis=1), 2)
    both = dot(jnp.concatenate([two, one], axis=0), high_ref[...])
    result = (both[:HOURS] + dot(one, low_ref[...])) + both[HOURS:]
    mine_ref[body, :] = result[:, :rows]
    other_ref[body, :] = result[:, rows:]
    if height > HOURS:
        tail = pl.ds(HOURS, NOTE)
        note = sum(ref[tail, :] for ref in refs)
        mine_ref[tail, :] = note
        other_ref[tail, :] = note
    for ref in extra:
        other_ref[pl.ds(height, ref.shape[0]), :] = ref[...]


def plane_mix(coupling, values, extra):
    height, rows = values[0].shape
    return pl.pallas_call(
        plane_mix_kernel,
        out_shape=[
            jax.ShapeDtypeStruct((height, rows), F32),
            jax.ShapeDtypeStruct((height + sum(value.shape[0] for value in extra), rows), F32),
        ],
        compiler_params=params(),
        name="plane_mix",
        cost_estimate=SMALL,
    )(*coupling, *values, *extra)


def plane_rows_kernel(first_ref, meta_ref, meta_other_ref, a_ref, b_ref, c_ref, d_ref, *refs):
    if len(refs) > 2:
        *stack, last_ref, beside_ref, mine_ref, other_ref, stack_ref = refs
    else:
        mine_ref, other_ref = refs
    rows = a_ref.shape[1]
    value = jnp.concatenate([ref[pl.ds(0, HOURS), :] for ref in (a_ref, b_ref, c_ref, d_ref)], axis=1)
    one, two = pieces(value, 2)
    stacked = jnp.concatenate([two, one], axis=0)
    picked = []
    for ref in (meta_ref, meta_other_ref):
        gauge = ref[0:1, :]
        hot = jnp.concatenate([hot_rows(gauge, first_ref[m], rows) for m in range(4)], axis=0)
        both = dot(stacked, hot)
        picked.append(both[:HOURS] + both[HOURS:])
    mine_ref[...] = picked[0]
    count = picked[1].shape[1] // rows
    for i in range(count):
        other_ref[pl.ds(i * HOURS, HOURS), :] = picked[1][:, i * rows : (i + 1) * rows]
    if len(refs) > 2:
        top = stack_ref.shape[0] - HOURS
        for ref in stack:
            stack_ref[pl.ds(0, top), :] = ref[...]
        for i in range(count):
            here = pl.ds(i * rows, rows)
            beside = beside_ref[pl.ds(beside_ref.shape[0] - (count - i) * HOURS, HOURS), :]
            stack_ref[pl.ds(top, HOURS), here] = last_ref[:, here] + beside


def plane_rows(first, metas, values, before):
    rows = values[0].shape[1]
    slots = metas[0].shape[1]
    args = [first, *metas, *values, *before]
    shapes = [(HOURS, slots), (slots // rows * HOURS, rows)]
    if before:
        shapes.append(((len(before) - 1) * HOURS, slots))
    return pl.pallas_call(
        plane_rows_kernel,
        in_specs=[pl.BlockSpec(memory_space=pltpu.SMEM)]
        + [pl.BlockSpec(memory_space=pltpu.VMEM)] * (len(args) - 1),
        out_shape=[jax.ShapeDtypeStruct(shape, F32) for shape in shapes],
        compiler_params=params(),
        name="plane_rows",
        cost_estimate=pl.CostEstimate(flops=1_000_000_000, bytes_accessed=2_000_000, transcendentals=0),
    )(*args)


def gain(kernels):
    return jnp.max(jnp.sum(kernels, axis=1, keepdims=True), axis=0, keepdims=True)


def spectra(kind, kernels, wide):
    classes = kernels.shape[0]
    row = lax.broadcasted_iota(jnp.int32, (classes, kind.shape[1]), 0).astype(F32)
    hot = jnp.where(row == kind, 1.0, 0.0).astype(BF16)
    taps = jnp.transpose(kernels / gain(kernels))
    chosen = dot(jnp.concatenate(pieces(taps, 3)[::-1], axis=1), jnp.concatenate([hot] * 3, axis=0))
    return product(wide, chosen, 3)


def plane_spectrum_kernel(class_ref, kernels_ref, wide_ref, out_ref):
    kind = class_ref[1:2, : out_ref.shape[1]]
    out_ref[...] = spectra(kind, kernels_ref[...], wide_ref[...])


def plane_spectrum(meta, kernels, wide, rows):
    return pl.pallas_call(
        plane_spectrum_kernel,
        out_shape=jax.ShapeDtypeStruct((SPAN, rows), F32),
        compiler_params=params(),
        name="plane_spectrum",
        cost_estimate=SMALL,
    )(meta, kernels, wide)


def sides(even, pair, middle):
    return jnp.where(even, middle, pair), jnp.where(even, pair, middle)


def plane_call(kernel, name, shapes, flags, args):
    return pl.pallas_call(
        kernel,
        in_specs=[pl.BlockSpec(memory_space=pltpu.SMEM)] * len(flags)
        + [pl.BlockSpec(memory_space=pltpu.VMEM)] * len(args),
        out_shape=[jax.ShapeDtypeStruct(shape, F32) for shape in shapes],
        compiler_params=params(),
        name=name,
        cost_estimate=SMALL,
    )(*flags, *args)


def plane_first_kernel(
    flag_ref, here_ref, pair_ref, middle_ref, spec_ref, kernels_ref, forward, first, last, out_ref
):
    spec = spec_ref[...]
    before, after = sides(flag_ref[0] > 0.5, pair_ref[...], middle_ref[...])
    here = here_ref[...]
    both = plane_delayed(before[:HOURS], here[:HOURS], after[:HOURS], spec, forward[...], last[...], 3)
    scale = gain(kernels_ref[...])
    now = here[HOURS:] - both[0] * scale
    later = (after[HOURS:] - both[1] * scale) * flag_ref[1]
    out_ref[...] = plane_advanced(now, later, spec, forward[...], first[...], 3)


def plane_delay_kernel(flag_ref, here_ref, pair_ref, middle_ref, spec_ref, forward, last, out_ref):
    body = pl.ds(0, HOURS)
    before, after = sides(flag_ref[0] > 0.5, pair_ref[body, :], middle_ref[body, :])
    out = plane_delayed(before, here_ref[body, :], after, spec_ref[...], forward[...], last[...], 2)
    for i in range(2):
        out_ref[pl.ds(i * HOURS, HOURS), :] = out[i]


def write_note(ref, rows):
    tail = [jnp.zeros((NOTE - len(rows), ref.shape[1]), F32)]
    ref[pl.ds(HOURS, NOTE), :] = jnp.concatenate(rows + tail, axis=0)


def plane_open_kernel(
    flag_ref, here_ref, pair_ref, middle_ref, pulled_ref, spec_ref, forward, first, last, out_ref, delayed_ref
):
    here = here_ref[...]
    spec = spec_ref[...]
    before, after = sides(flag_ref[0] > 0.5, pair_ref[...], middle_ref[...])
    now, later = plane_delayed(before, here, after, spec, forward[...], last[...], 2)
    out_ref[pl.ds(0, HOURS), :] = plane_advanced(now, later * flag_ref[1], spec, forward[...], first[...], 2)
    write_note(out_ref, [lanes(pulled_ref[...], here), lanes(now, now)])
    delayed_ref[pl.ds(0, HOURS), :] = now
    delayed_ref[pl.ds(HOURS, HOURS), :] = later


def plane_step_kernel(
    flag_ref,
    here_ref,
    pair_ref,
    two_ref,
    mirror_ref,
    pulled_ref,
    delayed_ref,
    old_z_ref,
    old_s_ref,
    old_delayed_ref,
    spec_ref,
    forward,
    first,
    total_ref,
    out_ref,
    kept_ref,
):
    tail, body = pl.ds(HOURS, NOTE), pl.ds(0, HOURS)
    total_ref[...] = (here_ref[tail, :] + pair_ref[tail, :]) + (two_ref[...] + mirror_ref[...])
    inverse = total(total_ref, 0) / total(total_ref, 1)
    z = pulled_ref[body, :] * inverse - old_z_ref[...]
    s = here_ref[body, :] * inverse - old_s_ref[...]
    both = delayed_ref[...] * inverse - old_delayed_ref[...]
    now, later = both[:HOURS], both[HOURS:]
    following = plane_advanced(now, later * flag_ref[1], spec_ref[...], forward[...], first[...], 2)
    out_ref[body, :] = following * inverse
    write_note(out_ref, [lanes(z, s), lanes(now, now)])
    for i, value in enumerate((z, s, now)):
        kept_ref[pl.ds(i * HOURS, HOURS), :] = value


def plane_close_kernel(
    here_ref, before_ref, pulled_ref, kept_ref, old_z_ref, old_s_ref, old_delayed_ref, spec_ref, forward, last, out_ref
):
    body = pl.ds(0, HOURS)
    here, raw = here_ref[body, :], pulled_ref[body, :]
    waves = product(forward[...], jnp.concatenate([before_ref[body, :], here], axis=0), 2)
    now = product(last[...], turn(waves, spec_ref[...], 1.0), 2)
    z, s, delayed = (kept_ref[pl.ds(i * HOURS, HOURS), :] for i in range(3))
    note = [pulled_ref[HOURS + i : HOURS + i + 1, :] for i in range(2)]
    for left in (raw, z, old_z_ref[...]):
        note += [lanes(left, right) for right in (here, s, old_s_ref[...])]
    parts = (now, delayed, old_delayed_ref[body, :])
    for i in range(3):
        note += [lanes(parts[i], parts[j]) for j in range(i, 3)]
    note.append(jnp.zeros((24 - len(note), here.shape[1]), F32))
    note = jnp.sum(jnp.concatenate(note, axis=0), axis=1, keepdims=True)
    shape = (24, out_ref.shape[2])
    row, col = (lax.broadcasted_iota(jnp.int32, shape, i) for i in range(2))
    note = jnp.sum(jnp.where(row == col, jnp.broadcast_to(note, shape), 0.0), axis=0, keepdims=True)
    out_ref[...] = jnp.broadcast_to(note[None], out_ref.shape)


def plane_weights(open_ref, close, scale):
    entry = lambda i: close[:, i : i + 1]
    n1, t1 = total(open_ref, 0), total(open_ref, 1)
    n2, t2 = entry(0), entry(1)
    a1 = t1 / n1
    a2, r2 = (t2 / n2) / a1, n2 / n1
    plain = (1.0, -a2, -r2)
    n3 = sum(plain[i] * plain[j] * entry(2 + 3 * i + j) for i in range(3) for j in range(3))
    pairs = [(i, j) for i in range(3) for j in range(i, 3)]
    t3 = sum(
        plain[i] * plain[j] * entry(11 + n) * (1.0 if i == j else 2.0) for n, (i, j) in enumerate(pairs)
    )
    a3, r3 = (t3 / n3) / a1, n3 / n2
    unit = 1.0 / (a1 * scale)
    c3 = unit / (a3 * (a2 - r2) - r3)
    c2 = -a3 * c3
    c1 = unit - r2 * c2
    step = c2 - c3 * a2
    return c1 - step - c3 * r2, step / a1, c3


def plane_combine_kernel(open_ref, close_ref, kernels_ref, stack_ref, mine_ref, beside_ref, out_ref):
    rows = open_ref.shape[1]
    close = jnp.sum(close_ref[...], axis=0)[0:1, :]
    e0, e1, e2 = plane_weights(open_ref, close, gain(kernels_ref[...]))
    for i in range(out_ref.shape[0] // rows):
        here = pl.ds(i * rows, rows)
        last = mine_ref[:, here] + beside_ref[pl.ds(i * HOURS, HOURS), :]
        value = stack_ref[pl.ds(0, HOURS), here] * e0 + stack_ref[pl.ds(HOURS, HOURS), here] * e1 + last * e2
        out_ref[here, :] = jnp.transpose(value)


def plane_finish_kernel(rows_ref, inc_ref, field_ref, out_ref):
    blocks, slots, width = inc_ref.shape
    weights = inc_ref[...].astype(F32).astype(BF16)
    for b in range(blocks):
        here = pl.ds(b * width, width)
        rows = jnp.concatenate(pieces(rows_ref[pl.ds(b * slots, slots), :], 2), axis=0)
        twice = jnp.concatenate([weights[b]] * 2, axis=0)
        added = lax.dot_general(twice, rows, (((0,), (0,)), ((), ())), preferred_element_type=F32)
        out_ref[here, :] = field_ref[here, :] + added


def plane_finish(rows, incidence, field):
    blocks, slots, width = incidence.shape
    hours = field.shape[1]
    step = 8
    return pl.pallas_call(
        plane_finish_kernel,
        grid=(blocks // step,),
        in_specs=[
            pl.BlockSpec((step * slots, hours), lambda i: (i, 0)),
            pl.BlockSpec((step, slots, width), lambda i: (i, 0, 0)),
            pl.BlockSpec((step * width, hours), lambda i: (i, 0)),
        ],
        out_specs=pl.BlockSpec((step * width, hours), lambda i: (i, 0)),
        out_shape=jax.ShapeDtypeStruct(field.shape, F32),
        compiler_params=params(),
        name="plane_finish",
    )(rows, incidence, field)


def plane_shards(incidence, row_gauge, gauge_kernel, kernels, observed, first_guess):
    rows, hours = observed.shape
    basin, tm = lax.axis_index("basin"), lax.axis_index("tm")
    z, x, y, c = basin // X_, basin % X_, tm // C_, tm % C_
    place = 2 * y + x
    first = jnp.stack([4 * c + (place ^ m) for m in range(4)] + [4 * c + place, 4 * (1 - c) + place])
    first = (first * rows).astype(jnp.int32)
    flags = jnp.stack([1 - z % 2, (z < Z_ - 1).astype(z.dtype), (z > 0).astype(z.dtype)]).astype(F32)
    forward, inverse_first, inverse_last, _ = turned_transforms(2)
    forward3, inverse_first3, inverse_last3, short3 = turned_transforms(3)
    block, noted = (hours, rows), (hours + NOTE, rows)

    parcel = send(incidence, first_guess)
    parcel, near, gauges, kinds, seen = lax.optimization_barrier(
        (parcel, incidence, row_gauge, gauge_kernel, observed)
    )
    parcel = moved(parcel, to_plane)
    behind = moved(label(seen, gauges, kinds), to_plane)
    meta = describe(near, gauges)
    meta = jnp.concatenate([meta, moved(meta, over_x)], axis=1)
    meta = jnp.concatenate([meta, moved(meta, z_pair)], axis=1)
    parcel, behind = lax.optimization_barrier((parcel, behind))
    seen, labels = behind[:-8], behind[-8:]
    seen = jnp.concatenate([seen[:, i : i + rows] for i in range(0, seen.shape[1], rows)], axis=0)
    parcels = [parcel, moved(parcel, over_core)]
    metas = [labels, moved(labels, over_core)]
    spec = plane_spectrum(labels, kernels, short3, rows)
    parcels[1], meta, spec = lax.optimization_barrier((parcels[1], meta, spec))
    around = [meta, moved(meta, z_two)]
    dense = spread(first, parcels, metas, rows)
    sums = dense[0] + sum(moved(value, where) for value, where in zip(dense[1:], SQUARE))
    sums = jnp.concatenate([sums, seen], axis=0)
    sums = [sums, moved(sums, z_pair), moved(sums, z_middle)]
    coupled = plane_couple(first, around[0], rows)
    coupled, sums = lax.optimization_barrier((coupled, sums))
    coupling = plane_couple(first, around[1], rows, coupled)
    (pulled0,) = plane_call(
        plane_first_kernel,
        "plane_first",
        [block],
        [flags],
        [*sums, spec, kernels, forward3, inverse_first3, inverse_last3],
    )

    def mixing(pulled, extra):
        values = [pulled] + [moved(pulled, where) for where in SQUARE]
        mine, other = plane_mix(coupling, values, extra)
        beside = moved(other, over_core)
        return values, mine + beside[: pulled.shape[0]], beside

    values, mixed0, _ = mixing(pulled0, [])
    picked, theirs = plane_rows(first, metas, values, [])
    sums = [mixed0, moved(mixed0, z_pair), moved(mixed0, z_middle)]
    pulled1, delayed0 = plane_call(
        plane_open_kernel,
        "plane_open",
        [noted, (2 * hours, rows)],
        [flags],
        [*sums, pulled0, spec, forward, inverse_first, inverse_last],
    )

    values, mixed1, beside = mixing(pulled1, [theirs])
    picked, theirs, stack = plane_rows(first, metas, values, [picked, beside])
    sums = [mixed1, moved(mixed1, z_pair), moved(mixed1, z_middle)]
    two, mirror = moved(mixed1[hours:], z_two), moved(mixed1[hours:], z_mirror)
    (delayed1,) = plane_call(
        plane_delay_kernel, "plane_delay", [(2 * hours, rows)], [flags], [*sums, spec, forward, inverse_last]
    )
    open_note, pulled2, kept = plane_call(
        plane_step_kernel,
        "plane_step",
        [(NOTE, rows), noted, (3 * hours, rows)],
        [flags],
        [*sums[:2], two, mirror, pulled1, delayed1, pulled0, mixed0, delayed0, spec, forward, inverse_first],
    )

    values, mixed2, beside = mixing(pulled2, [theirs])
    picked, theirs, stack = plane_rows(first, metas, values, [stack, picked, beside])
    (note,) = plane_call(
        plane_close_kernel,
        "plane_close",
        [(Z_ * X_ * Y_ * C_, 8, rows // 2)],
        [],
        [mixed2, moved(mixed2, z_next), pulled2, kept, pulled0, mixed0, delayed0, spec, forward, inverse_last],
    )
    close_note = lax.all_to_all(note, ("basin", "tm"), 0, 0, tiled=False)
    (answer,) = plane_call(
        plane_combine_kernel,
        "plane_combine",
        [(parcel.shape[1], hours)],
        [],
        [open_note, close_note, kernels, stack, picked, moved(theirs, over_core)],
    )
    return plane_finish(moved(answer, from_plane), incidence, first_guess)


def solution(mesh):
    planes = dict(mesh.shape) == {"basin": Z_ * X_, "tm": Y_ * C_}
    in_specs = (
        P("basin", None, None),
        P("basin"),
        P("basin"),
        P(),
        P("basin", "tm"),
        P("basin", "tm"),
    )
    return jax.shard_map(
        plane_shards if planes else shards, mesh=mesh, in_specs=in_specs, out_specs=P("basin", "tm"), check_vma=False
    )
```

```python
import functools

import jax
import jax.numpy as jnp
import numpy as np
from jax import lax
from jax.experimental import pallas as pl
from jax.experimental.pallas import tpu as pltpu
from jax.sharding import PartitionSpec as P

F32 = jnp.float32
BF16 = jnp.bfloat16
HIGH = lax.Precision.HIGHEST
SPAN = 256
MIB = 1024 * 1024


SMALL = pl.CostEstimate(flops=1, bytes_accessed=1, transcendentals=0)


def params(mib=16):
    return pltpu.CompilerParams(vmem_limit_bytes=mib * MIB)


def transforms():
    half = SPAN // 2
    freq = 2.0 * np.pi * (np.arange(half) + 0.5) / SPAN
    phase = np.arange(SPAN)[:, None] * freq[None, :]
    forward = np.concatenate([np.cos(phase), -np.sin(phase)], axis=1)
    inverse = forward.T * (2.0 / SPAN)
    return (
        jnp.asarray(forward, F32),
        jnp.asarray(inverse[:, :half], F32),
        jnp.asarray(inverse[:, half:], F32),
    )


def dot(a, b):
    return jnp.dot(a, b, preferred_element_type=F32)


def exact(a, b):
    return jnp.dot(a, b, precision=HIGH, preferred_element_type=F32)


def pieces(value, count):
    out = []
    for _ in range(count):
        piece = value.astype(BF16)
        out.append(piece)
        value = value - piece.astype(F32)
    return out


def pick(hot, value):
    return sum(dot(hot, piece) for piece in pieces(value, 3))


def prepare_kernel(inc_ref, field_ref, partial_ref, gram_ref):
    blocks, slots, width = inc_ref.shape
    rows = blocks * slots
    weights = inc_ref[...].astype(F32).astype(BF16)
    for b in range(blocks):
        value = field_ref[pl.ds(b * width, width), :]
        partial_ref[pl.ds(b * slots, slots), :] = pick(weights[b], value)
    flat = weights.reshape(rows, width)
    full = lax.dot_general(flat, flat, (((1,), (1,)), ((), ())), preferred_element_type=F32)
    row = lax.broadcasted_iota(jnp.int32, (rows, rows), 0)
    col = lax.broadcasted_iota(jnp.int32, (rows, rows), 1)
    own = jnp.where(row // slots == col // slots, full, 0.0)
    gram_ref[...] = jnp.sum(own.reshape(blocks, slots, rows), axis=0)


def prepare(incidence, field):
    blocks, slots, width = incidence.shape
    hours = field.shape[1]
    step = 8
    return pl.pallas_call(
        prepare_kernel,
        grid=(blocks // step,),
        in_specs=[
            pl.BlockSpec((step, slots, width), lambda i: (i, 0, 0)),
            pl.BlockSpec((step * width, hours), lambda i: (i, 0)),
        ],
        out_specs=[
            pl.BlockSpec((step * slots, hours), lambda i: (i, 0)),
            pl.BlockSpec((slots, step * slots), lambda i: (0, i)),
        ],
        out_shape=[
            jax.ShapeDtypeStruct((blocks * slots, hours), F32),
            jax.ShapeDtypeStruct((slots, blocks * slots), F32),
        ],
        compiler_params=params(56),
        name="prepare",
    )(incidence, field)


def table_kernel(gauge_ref, partial_ref, out_ref):
    slots = partial_ref.shape[0]
    rows = out_ref.shape[0]
    first = pl.program_id(0) * rows
    gauge = lax.broadcasted_iota(jnp.int32, (rows, slots), 0) + first
    hot = jnp.where(gauge_ref[...] == gauge, 1.0, 0.0).astype(BF16)
    out_ref[...] = pick(hot, partial_ref[...])


def table(row_gauge, partial, gauges):
    slots, hours = partial.shape
    step = 256
    return pl.pallas_call(
        table_kernel,
        grid=(gauges // step,),
        in_specs=[
            pl.BlockSpec((1, slots), lambda i: (0, 0)),
            pl.BlockSpec((slots, hours), lambda i: (0, 0)),
        ],
        out_specs=pl.BlockSpec((step, hours), lambda i: (i, 0)),
        out_shape=jax.ShapeDtypeStruct((gauges, hours), F32),
        compiler_params=params(56),
        name="table",
    )(row_gauge.reshape(1, slots), partial)


def couple_kernel(first_ref, lane_ref, sub_ref, gram_ref, high_ref, low_ref, near_ref):
    slots = gram_ref.shape[0]
    count = lane_ref.shape[1]
    rows, cols = high_ref.shape
    tile = 256
    first = first_ref[0]

    @pl.when(pl.program_id(0) == 0)
    def _():
        row = lax.broadcasted_iota(jnp.int32, (tile, tile), 0)
        col = lax.broadcasted_iota(jnp.int32, (tile, tile), 1)
        same = row // slots == col // slots
        mine = lax.broadcasted_iota(jnp.int32, (rows, tile), 0) + first

        def body(i, carry):
            here = pl.ds(pl.multiple_of(i * tile, tile), tile)
            block = jnp.concatenate([gram_ref[:, here]] * (tile // slots), axis=0)
            block = jnp.where(same, block, 0.0).astype(BF16)
            hot = jnp.where(lane_ref[:, here] == mine, 1.0, 0.0).astype(BF16)
            near_ref[:, here] = dot(hot, block)
            return carry

        lax.fori_loop(0, count // tile, body, 0)

    def chunk(i, total):
        here = pl.ds(pl.multiple_of(i * 1024, 1024), 1024)
        gauge = lax.broadcasted_iota(jnp.int32, (1024, cols), 1) + pl.program_id(0) * cols
        hot = jnp.where(sub_ref[here, :] == gauge, 1.0, 0.0).astype(BF16)
        near = near_ref[:, here]
        high = near.astype(BF16)
        low = (near - high.astype(F32)).astype(BF16)
        return total + dot(high, hot) + dot(low, hot)

    total = lax.fori_loop(0, count // 1024, chunk, jnp.zeros((rows, cols), F32))
    high, low = pieces(total, 2)
    high_ref[...] = high
    low_ref[...] = low


def couple(first, row_gauge, gram, rows, gauges):
    count = row_gauge.shape[0]
    step = 256
    return pl.pallas_call(
        couple_kernel,
        grid=(gauges // step,),
        in_specs=[
            pl.BlockSpec(memory_space=pltpu.SMEM),
            pl.BlockSpec((1, count), lambda i: (0, 0)),
            pl.BlockSpec((count, 1), lambda i: (0, 0)),
            pl.BlockSpec(gram.shape, lambda i: (0, 0)),
        ],
        out_specs=[pl.BlockSpec((rows, step), lambda i: (0, i))] * 2,
        out_shape=[jax.ShapeDtypeStruct((rows, gauges), BF16)] * 2,
        scratch_shapes=[pltpu.VMEM((rows, count), F32)],
        compiler_params=params(56),
        name="couple",
    )(first, row_gauge.reshape(1, count), row_gauge.reshape(count, 1), gram)


def mix_kernel(high_ref, low_ref, value_ref, out_ref):
    high = high_ref[...]
    low = low_ref[...]
    one, two, three = pieces(value_ref[...], 3)
    out_ref[...] = (dot(high, three) + dot(low, two)) + (dot(high, two) + dot(low, one)) + dot(high, one)


def mix(high, low, value):
    return pl.pallas_call(
        mix_kernel,
        out_shape=jax.ShapeDtypeStruct((high.shape[0], value.shape[1]), F32),
        compiler_params=params(56),
        name="mix",
    )(high, low, value)


def spectrum_kernel(class_ref, kernels_ref, forward_ref, out_ref):
    rows = class_ref.shape[0]
    classes, taps = kernels_ref.shape
    kind = lax.broadcasted_iota(jnp.int32, (rows, classes), 1)
    hot = jnp.where(class_ref[...] == kind, 1.0, 0.0)
    out_ref[...] = exact(exact(hot, kernels_ref[...]), forward_ref[pl.ds(0, taps), :])


def spectrum(gauge_kernel, kernels, forward):
    rows = gauge_kernel.shape[0]
    return pl.pallas_call(
        spectrum_kernel,
        out_shape=jax.ShapeDtypeStruct((rows, SPAN), F32),
        compiler_params=params(56),
        name="spectrum",
    )(gauge_kernel.reshape(rows, 1), kernels, forward)


def delayed(before, here, after, spec, forward, inverse_last):
    rows, half = here.shape
    stacked = jnp.concatenate(
        [jnp.concatenate([before, here], axis=1), jnp.concatenate([here, after], axis=1)], axis=0
    )
    waves = exact(stacked, forward)
    real, imag = waves[:, :half], waves[:, half:]
    kr = jnp.concatenate([spec[:, :half]] * 2, axis=0)
    ki = jnp.concatenate([spec[:, half:]] * 2, axis=0)
    turned = jnp.concatenate([real * kr - imag * ki, real * ki + imag * kr], axis=1)
    out = exact(turned, inverse_last)
    return out[:rows], out[rows:]


def advanced(here, after, spec, forward, inverse_first):
    half = here.shape[1]
    waves = exact(jnp.concatenate([here, after], axis=1), forward)
    real, imag = waves[:, :half], waves[:, half:]
    kr, ki = spec[:, :half], spec[:, half:]
    turned = jnp.concatenate([real * kr + imag * ki, imag * kr - real * ki], axis=1)
    return exact(turned, inverse_first)


def lanes(a, b):
    return jnp.sum(a * b, axis=0, keepdims=True)


def total(ref, row):
    return jnp.sum(ref[row : row + 1, :], axis=1, keepdims=True)


def ratios(ref):
    square = total(ref, 0)
    alpha = jnp.sqrt(square)
    beta = jnp.sqrt(jnp.maximum(total(ref, 1) / square - 2.0 * total(ref, 2) + square, 0.0))
    return alpha, beta


def first_kernel(
    more_ref, sums_ref, observed_ref, spec_ref, forward_ref, first_ref, last_ref, out_ref, note_ref
):
    rows, half = observed_ref.shape[0] // 2, observed_ref.shape[1]
    spec, forward = spec_ref[...], forward_ref[...]
    before, here, after = (sums_ref[pl.ds(i * rows, rows), :] for i in range(3))
    now, later = delayed(before, here, after, spec, forward, last_ref[...])
    start = observed_ref[pl.ds(0, rows), :] - now
    start_later = (observed_ref[pl.ds(rows, rows), :] - later) * more_ref[0]
    out_ref[...] = advanced(start, start_later, spec, forward, first_ref[...])
    note_ref[...] = jnp.concatenate([lanes(start, start), jnp.zeros((7, half), F32)], axis=0)


def first_step(more, sums, observed, spec, mats):
    rows, half = spec.shape[0], observed.shape[1]
    return pl.pallas_call(
        first_kernel,
        in_specs=[pl.BlockSpec(memory_space=pltpu.SMEM)] + [pl.BlockSpec(memory_space=pltpu.VMEM)] * 6,
        out_shape=[jax.ShapeDtypeStruct((rows, half), F32), jax.ShapeDtypeStruct((8, half), F32)],
        compiler_params=params(56),
        name="first_step",
    )(more, sums, observed, spec, *mats)


def step_kernel(
    opening,
    final,
    more_ref,
    note_ref,
    sums_ref,
    spec_ref,
    forward_ref,
    first_ref,
    last_ref,
    pulled_ref,
    *refs,
):
    if opening:
        state_ref = None
    else:
        state_ref, *refs = refs
    if final:
        (out_note_ref,) = refs
    else:
        new_ref, out_ref, out_note_ref = refs
    rows, half = pulled_ref.shape
    spec, forward = spec_ref[...], forward_ref[...]
    if opening:
        scale = 1.0 / jnp.sqrt(total(note_ref, 0))
        along = sums_ref[...] * scale
        new_s, new_su = along, along
        new_zu = pulled_ref[...] * scale
        new_z = new_zu
    else:
        alpha, beta = ratios(note_ref)
        a, b, g = 1.0 / (alpha * beta), alpha / beta, beta / alpha
        wide = pl.ds(0, 3 * rows), pl.ds(3 * rows, 3 * rows)
        new_su = sums_ref[...] * a - state_ref[wide[1], :] * b
        new_s = new_su - state_ref[wide[0], :] * g
        new_zu = pulled_ref[...] * a - state_ref[pl.ds(7 * rows, rows), :] * b
        new_z = new_zu - state_ref[pl.ds(6 * rows, rows), :] * g
    before, here, after = (new_s[i * rows : (i + 1) * rows] for i in range(3))
    now, later = delayed(before, here, after, spec, forward, last_ref[...])
    out_note_ref[...] = jnp.concatenate(
        [lanes(new_z, here), lanes(now, now), lanes(new_zu, here), jnp.zeros((5, half), F32)], axis=0
    )
    if not final:
        new_ref[pl.ds(0, 3 * rows), :] = new_s
        new_ref[pl.ds(3 * rows, 3 * rows), :] = new_su
        new_ref[pl.ds(6 * rows, rows), :] = new_z
        new_ref[pl.ds(7 * rows, rows), :] = new_zu
        out_ref[...] = advanced(now, later * more_ref[0], spec, forward, first_ref[...])


def next_step(more, note, sums, spec, mats, pulled, state, final):
    rows, half = pulled.shape
    opening = state is None
    shapes = [
        jax.ShapeDtypeStruct((8 * rows, half), F32),
        jax.ShapeDtypeStruct((rows, half), F32),
        jax.ShapeDtypeStruct((8, half), F32),
    ]
    args = [more, note, sums, spec, *mats, pulled] + ([] if opening else [state])
    return pl.pallas_call(
        functools.partial(step_kernel, opening, final),
        in_specs=[pl.BlockSpec(memory_space=pltpu.SMEM)]
        + [pl.BlockSpec(memory_space=pltpu.VMEM)] * (len(args) - 1),
        out_shape=shapes[2:] if final else shapes,
        compiler_params=params(56),
        name="next_step",
    )(*args)


def weights_of(notes):
    start = jnp.sqrt(total(notes[0], 0))
    zero = jnp.zeros_like(start)
    units = [1.0 / start, zero, zero]
    z, zu = list(units), list(units)
    phibar = start
    alpha, beta = ratios(notes[1])
    rhobar = alpha
    w = [value / alpha for value in z]
    result = [zero] * 3
    steps = len(notes) - 1
    for k in range(steps):
        rho = jnp.sqrt(rhobar * rhobar + beta * beta)
        cosine, sine = rhobar / rho, beta / rho
        phi, phibar = cosine * phibar, sine * phibar
        result = [r + phi / rho * value for r, value in zip(result, w)]
        if k < steps - 1:
            a, b, g = 1.0 / (alpha * beta), alpha / beta, beta / alpha
            zu = [(a if i == k + 1 else 0.0) - b * value for i, value in enumerate(zu)]
            z = [value - g * old for value, old in zip(zu, z)]
            alpha, beta = ratios(notes[k + 2])
            theta = sine * alpha
            rhobar = -cosine * alpha
            w = [value / alpha - theta / rho * old for value, old in zip(z, w)]
    return result


def finish_kernel(n0, n1, n2, n3, gauge_ref, q0, q1, q2, inc_ref, field_ref, out_ref, rows_ref):
    blocks, slots, width = inc_ref.shape
    count = rows_ref.shape[0]
    gauges = q0.shape[0]
    step = pl.program_id(0)

    @pl.when(step == 0)
    def _():
        e0, e1, e2 = weights_of([n0, n1, n2, n3])
        width_ = 512

        def body(i, value):
            here = pl.ds(pl.multiple_of(i * width_, width_), width_)
            mixed = q0[here, :] * e0 + q1[here, :] * e1 + q2[here, :] * e2
            gauge = lax.broadcasted_iota(jnp.int32, (count, width_), 1) + i * width_
            hot = jnp.where(gauge_ref[...] == gauge, 1.0, 0.0).astype(BF16)
            return value + pick(hot, mixed)

        rows_ref[...] = lax.fori_loop(0, gauges // width_, body, jnp.zeros(rows_ref.shape, F32))

    weights = inc_ref[...].astype(F32).astype(BF16)
    for b in range(blocks):
        here = pl.ds(b * width, width)
        rows = rows_ref[pl.ds(pl.multiple_of((step * blocks + b) * slots, slots), slots), :]
        added = sum(
            lax.dot_general(weights[b], piece, (((0,), (0,)), ((), ())), preferred_element_type=F32)
            for piece in pieces(rows, 3)
        )
        out_ref[here, :] = field_ref[here, :] + added


def finish(notes, row_gauge, gathered, incidence, field):
    blocks, slots, width = incidence.shape
    hours = field.shape[1]
    count = row_gauge.shape[0]
    step = 8
    whole = lambda shape: pl.BlockSpec(shape, lambda i: (0, 0))
    return pl.pallas_call(
        finish_kernel,
        grid=(blocks // step,),
        in_specs=[whole(n.shape) for n in notes]
        + [whole((count, 1))]
        + [whole(q.shape) for q in gathered]
        + [
            pl.BlockSpec((step, slots, width), lambda i: (i, 0, 0)),
            pl.BlockSpec((step * width, hours), lambda i: (i, 0)),
        ],
        out_specs=pl.BlockSpec((step * width, hours), lambda i: (i, 0)),
        out_shape=jax.ShapeDtypeStruct(field.shape, F32),
        scratch_shapes=[pltpu.VMEM((count, hours), F32)],
        compiler_params=params(56),
        name="finish",
    )(*notes, row_gauge.reshape(count, 1), *gathered, incidence, field)


def shifted(value, axis, by):
    devices = lax.axis_size(axis)
    pairs = [(i, i + by) for i in range(devices) if 0 <= i + by < devices]
    return lax.ppermute(value, axis, pairs)


def window(value):
    return jnp.concatenate([shifted(value, "tm", 1), value, shifted(value, "tm", -1)], axis=0)


def gathered_rows(value):
    owners = lax.axis_size("basin")
    copies = jnp.broadcast_to(value[None], (owners,) + value.shape)
    return lax.all_to_all(copies, "basin", 0, 0, tiled=False)


def over_hours(note):
    blocks = lax.axis_size("tm")
    result = note
    for by in range(1, blocks):
        result = result + lax.ppermute(note, "tm", [(i, (i + by) % blocks) for i in range(blocks)])
    return result


def shards(incidence, row_gauge, gauge_kernel, kernels, observed, first_guess):
    owners = lax.axis_size("basin")
    rows, hours = observed.shape
    gauges = rows * owners
    mats = transforms()
    spec = spectrum(gauge_kernel, kernels, mats[0])
    more = (lax.axis_index("tm") < lax.axis_size("tm") - 1).astype(F32).reshape(1)
    partial, gram = prepare(incidence, first_guess)
    all_gram = lax.all_gather(gram, "basin", axis=1, tiled=True)
    all_rows = lax.all_gather(row_gauge, "basin", axis=0, tiled=True)
    dense = table(row_gauge, partial, gauges).reshape(owners, rows, hours)
    sums = jnp.sum(lax.all_to_all(dense, "basin", 0, 0, tiled=False), axis=0)
    both = jnp.concatenate([observed, shifted(observed, "tm", -1)], axis=0)
    first = (lax.axis_index("basin") * rows).astype(jnp.int32).reshape(1)
    high, low = couple(first, all_rows, all_gram, rows, gauges)

    pulled, note = first_step(more, window(sums), both, spec, mats)
    notes, kept, state = [], [], None
    for k in range(3):
        everyone = gathered_rows(jnp.concatenate([pulled, note], axis=0))
        value = everyone[:, :rows].reshape(gauges, hours)
        notes.append(over_hours(jnp.sum(everyone[:, rows:], axis=0)))
        kept.append(value)
        around = window(mix(high, low, value))
        final = k == 2
        result = next_step(more, notes[-1], around, spec, mats, pulled, state, final)
        if final:
            (note,) = result
        else:
            state, pulled, note = result
    notes.append(over_hours(jnp.sum(gathered_rows(note), axis=0)))
    return finish(notes, row_gauge, kept, incidence, first_guess)


Z_, X_, Y_, C_ = 4, 2, 2, 2
NOTE = 8
HOURS = SPAN // 2


def device(z, x, y, c):
    return (z * X_ + x) * (Y_ * C_) + y * C_ + c


def moved(value, where):
    pairs = []
    for z, x, y, c in np.ndindex(Z_, X_, Y_, C_):
        target = where(z, x, y, c)
        if target is not None:
            pairs.append((device(z, x, y, c), device(*target)))
    return lax.ppermute(value, ("basin", "tm"), pairs)


def to_plane(z, x, y, c):
    return 2 * y + c, x, z & 1, z >> 1


def hour_before(z, x, y, c):
    t = 2 * y + c - 1
    return (z, x, t >> 1, t & 1) if t >= 0 else None


def from_plane(z, x, y, c):
    return 2 * c + y, x, z >> 1, z & 1


def over_x(z, x, y, c):
    return z, 1 - x, y, c


def over_y(z, x, y, c):
    return z, x, 1 - y, c


def over_xy(z, x, y, c):
    return z, 1 - x, 1 - y, c


def over_core(z, x, y, c):
    return z, x, y, 1 - c


def z_pair(z, x, y, c):
    return z ^ 1, x, y, c


def z_middle(z, x, y, c):
    return (3 - z, x, y, c) if z in (1, 2) else None


def z_two(z, x, y, c):
    return z ^ 2, x, y, c


def z_mirror(z, x, y, c):
    return 3 - z, x, y, c


def z_next(z, x, y, c):
    return (z + 1, x, y, c) if z < 3 else None


SQUARE = (over_x, over_y, over_xy)


def split_constant(value):
    out = []
    for _ in range(3):
        piece = value.astype(jnp.bfloat16)
        out.append(piece)
        value = value - piece.astype(np.float64)
    return out


ORDERS = {2: ((0, 1), (1, 0), (0, 0)), 3: ((0, 2), (1, 1), (2, 0), (0, 1), (1, 0), (0, 0))}


def widened(mat, order):
    parts = split_constant(mat)
    return jnp.asarray(np.concatenate([parts[i] for i, _ in ORDERS[order]], axis=1))


def product(wide, value, order):
    parts = pieces(value, order)
    return dot(wide, jnp.concatenate([parts[j] for _, j in ORDERS[order]], axis=0))


def turned_transforms(order):
    half = SPAN // 2
    freq = 2.0 * np.pi * (np.arange(half) + 0.5) / SPAN
    phase = freq[:, None] * np.arange(SPAN)[None, :]
    forward = np.concatenate([np.cos(phase), -np.sin(phase)], axis=0)
    inverse = forward.T * (2.0 / SPAN)
    return [widened(mat, order) for mat in (forward, inverse[:half], inverse[half:], forward[:, :half])]


def turn(waves, spec, sign):
    half = waves.shape[0] // 2
    real, imag = waves[:half], waves[half:]
    kr, ki = spec[:half], spec[half:] * sign
    return jnp.concatenate([real * kr - imag * ki, real * ki + imag * kr], axis=0)


def plane_delayed(before, here, after, spec, forward, last, order):
    rows = here.shape[1]
    pairs = [jnp.concatenate(pair, axis=0) for pair in ((before, here), (here, after))]
    waves = product(forward, jnp.concatenate(pairs, axis=1), order)
    turned = [turn(waves[:, i * rows : (i + 1) * rows], spec, 1.0) for i in range(2)]
    out = product(last, jnp.concatenate(turned, axis=1), order)
    return out[:, :rows], out[:, rows:]


def plane_advanced(here, after, spec, forward, first, order):
    waves = product(forward, jnp.concatenate([here, after], axis=0), order)
    return product(first, turn(waves, spec, -1.0), order)


def describe_kernel(inc_ref, gauge_ref, out_ref):
    blocks, slots, width = inc_ref.shape
    tile = 8
    side = tile * slots
    weights = inc_ref[...].astype(F32).astype(BF16)
    row = lax.broadcasted_iota(jnp.int32, (side, side), 0)
    col = lax.broadcasted_iota(jnp.int32, (side, side), 1)
    same = row // slots == col // slots
    for i in range(blocks // tile):
        flat = weights[i * tile : (i + 1) * tile].reshape(side, width)
        full = lax.dot_general(flat, flat, (((1,), (1,)), ((), ())), preferred_element_type=F32)
        own = jnp.where(same, full, 0.0)
        out_ref[pl.ds(0, slots), pl.ds(i * side, side)] = jnp.sum(own.reshape(tile, slots, side), axis=0)
    out_ref[pl.ds(slots, 8), :] = jnp.broadcast_to(gauge_ref[...].astype(F32), (8, blocks * slots))


def describe(incidence, row_gauge):
    blocks, slots, _ = incidence.shape
    count = blocks * slots
    return pl.pallas_call(
        describe_kernel,
        out_shape=jax.ShapeDtypeStruct((slots + 8, count), F32),
        compiler_params=params(),
        name="describe",
        cost_estimate=SMALL,
    )(incidence, row_gauge.reshape(1, count))


def observe_kernel(seen_ref, later_ref, gauge_ref, kind_ref, kernels_ref, wide_ref, forward, first, out_ref):
    rows = seen_ref.shape[0]
    count = gauge_ref.shape[1]
    kind = kind_ref[...].astype(F32)
    spec = spectra(kind, kernels_ref[...], wide_ref[...])
    here, after = jnp.transpose(seen_ref[...]), jnp.transpose(later_ref[...])
    pulled = plane_advanced(here, after, spec, forward[...], first[...], 3)
    step = out_ref.shape[0] - 8
    for i in range(count // rows):
        out_ref[pl.ds(0, step), pl.ds(i * rows, rows)] = pulled[i * step : (i + 1) * step]
    kinds = jnp.concatenate([kind, jnp.zeros((1, count - rows), F32)], axis=1)
    out_ref[pl.ds(step, 8), :] = jnp.concatenate(
        [gauge_ref[...].astype(F32), kinds, jnp.zeros((6, count), F32)], axis=0
    )


def observe(seen, later, row_gauge, gauge_kernel, kernels, wide, mats):
    rows, hours = seen.shape
    count = row_gauge.shape[0]
    return pl.pallas_call(
        observe_kernel,
        out_shape=jax.ShapeDtypeStruct((hours * rows // count + 8, count), F32),
        compiler_params=params(),
        name="observe",
        cost_estimate=SMALL,
    )(seen, later, row_gauge.reshape(1, count), gauge_kernel.reshape(1, rows), kernels, wide, *mats)


def send_kernel(inc_hbm, field_hbm, out_ref, inc_ref, field_ref, sems):
    blocks, slots, width = inc_ref.shape
    chunks = sems.shape[0]
    step = blocks // chunks
    copies = []
    for i in range(chunks):
        near = pl.ds(i * step, step)
        far = pl.ds(i * step * width, step * width)
        copies.append(
            (
                pltpu.make_async_copy(inc_hbm.at[near], inc_ref.at[near], sems.at[i, 0]),
                pltpu.make_async_copy(field_hbm.at[far], field_ref.at[far], sems.at[i, 1]),
            )
        )
        for copy in copies[-1]:
            copy.start()
    for i in range(chunks):
        for copy in copies[i]:
            copy.wait()
        parts = []
        for b in range(i * step, (i + 1) * step):
            weight = inc_ref[b].astype(F32).astype(BF16)
            value = jnp.concatenate(pieces(field_ref[pl.ds(b * width, width), :], 3)[::-1], axis=0)
            parts.append(dot(jnp.concatenate([weight] * 3, axis=1), value))
        out_ref[:, pl.ds(i * step * slots, step * slots)] = jnp.transpose(jnp.concatenate(parts, axis=0))


def send(incidence, field):
    blocks, slots, width = incidence.shape
    hours = field.shape[1]
    chunks = 4
    return pl.pallas_call(
        send_kernel,
        in_specs=[pl.BlockSpec(memory_space=pltpu.HBM)] * 2,
        out_shape=jax.ShapeDtypeStruct((hours, blocks * slots), F32),
        scratch_shapes=[
            pltpu.VMEM(incidence.shape, incidence.dtype),
            pltpu.VMEM(field.shape, F32),
            pltpu.SemaphoreType.DMA((chunks, 2)),
        ],
        compiler_params=params(60),
        name="send",
        cost_estimate=SMALL,
    )(incidence, field)


def hot_rows(gauge, first, rows):
    mine = (lax.broadcasted_iota(jnp.int32, (rows, gauge.shape[1]), 0) + first).astype(F32)
    return jnp.where(gauge == mine, 1.0, 0.0).astype(BF16)


def spread_kernel(first_ref, mine_ref, other_ref, meta_ref, meta_other_ref, *out_refs):
    rows = out_refs[0].shape[1]
    value = jnp.concatenate([mine_ref[...], other_ref[...]], axis=1)
    gauge = jnp.concatenate([meta_ref[0:1, :], meta_other_ref[0:1, :]], axis=1)
    stacked = jnp.concatenate(pieces(value, 3), axis=0)
    for m, out_ref in enumerate(out_refs):
        hot = hot_rows(gauge, first_ref[m], rows)
        result = lax.dot_general(stacked, hot, (((1,), (1,)), ((), ())), preferred_element_type=F32)
        out_ref[...] = (result[2 * HOURS :] + result[HOURS : 2 * HOURS]) + result[:HOURS]


def spread(first, parcels, metas, rows):
    return pl.pallas_call(
        spread_kernel,
        in_specs=[pl.BlockSpec(memory_space=pltpu.SMEM)] + [pl.BlockSpec(memory_space=pltpu.VMEM)] * 4,
        out_shape=[jax.ShapeDtypeStruct((HOURS, rows), F32)] * 4,
        compiler_params=params(),
        name="spread",
        cost_estimate=SMALL,
    )(first, *parcels, *metas)


def plane_couple_kernel(last, first_ref, *refs):
    if last:
        all_ref, before_ref, high_ref, low_ref, total_ref, meta_ref = refs
        total_ref[...] = before_ref[...]
    else:
        all_ref, total_ref, meta_ref = refs
        total_ref[...] = jnp.zeros_like(total_ref)
    parts, height, count = meta_ref.shape
    slots = height - 8
    cols, rows = total_ref.shape
    tile = 256
    for i in range(parts):
        meta_ref[i] = all_ref[:, i * count : (i + 1) * count]
    row = lax.broadcasted_iota(jnp.int32, (tile, tile), 0)
    col = lax.broadcasted_iota(jnp.int32, (tile, tile), 1)
    same = row // slots == col // slots

    def body(i, carry):
        gauge = meta_ref[i, slots : slots + 1, :]
        near = []
        for j in range(count // tile):
            here = slice(j * tile, (j + 1) * tile)
            block = jnp.concatenate([meta_ref[i, :slots, here]] * (tile // slots), axis=0)
            block = jnp.where(same, block, 0.0).astype(BF16)
            mine = jnp.concatenate(
                [hot_rows(gauge[:, here], first_ref[4 + h], rows // 2) for h in range(2)], axis=0
            )
            near.append(
                lax.dot_general(block, mine, (((1,), (1,)), ((), ())), preferred_element_type=F32)
            )
        near = jnp.concatenate(near, axis=0)
        high = near.astype(BF16)
        rest = near - high.astype(F32)
        hot = jnp.concatenate([hot_rows(gauge, first_ref[m], cols // 4) for m in range(4)], axis=0)
        total_ref[...] += dot(hot, high)

        @pl.when(jnp.max(jnp.abs(rest)) > 0.0)
        def _():
            total_ref[...] += dot(hot, rest.astype(BF16))

        return carry

    lax.fori_loop(0, parts, body, 0)
    if last:
        high, low = pieces(total_ref[...], 2)
        high_ref[...] = high
        low_ref[...] = low


def plane_couple(first, meta, rows, before=None):
    height, wide = meta.shape
    parts = 2 * X_
    shape = (4 * rows, 2 * rows)
    last = before is not None
    args = [first, meta] + ([before] if last else [])
    scratch = [pltpu.VMEM((parts, height, wide // parts), F32)]
    return pl.pallas_call(
        functools.partial(plane_couple_kernel, last),
        in_specs=[pl.BlockSpec(memory_space=pltpu.SMEM)]
        + [pl.BlockSpec(memory_space=pltpu.VMEM)] * (len(args) - 1),
        out_shape=[jax.ShapeDtypeStruct(shape, BF16)] * 2 if last else jax.ShapeDtypeStruct(shape, F32),
        scratch_shapes=([pltpu.VMEM(shape, F32)] if last else []) + scratch,
        compiler_params=params(),
        name="plane_couple",
        cost_estimate=pl.CostEstimate(
            flops=2 * 8 * wide * rows * rows, bytes_accessed=2_000_000, transcendentals=0
        ),
    )(*args)


def plane_mix_kernel(high_ref, low_ref, a_ref, b_ref, c_ref, d_ref, *refs):
    *extra, mine_ref, other_ref = refs
    refs = (a_ref, b_ref, c_ref, d_ref)
    height, rows = a_ref.shape
    body = pl.ds(0, HOURS)
    one, two = pieces(jnp.concatenate([ref[body, :] for ref in refs], axis=1), 2)
    both = dot(jnp.concatenate([two, one], axis=0), high_ref[...])
    result = (both[:HOURS] + dot(one, low_ref[...])) + both[HOURS:]
    mine_ref[body, :] = result[:, :rows]
    other_ref[body, :] = result[:, rows:]
    if height > HOURS:
        tail = pl.ds(HOURS, NOTE)
        note = sum(ref[tail, :] for ref in refs)
        mine_ref[tail, :] = note
        other_ref[tail, :] = note
    for ref in extra:
        other_ref[pl.ds(height, ref.shape[0]), :] = ref[...]


def plane_mix(coupling, values, extra):
    height, rows = values[0].shape
    return pl.pallas_call(
        plane_mix_kernel,
        out_shape=[
            jax.ShapeDtypeStruct((height, rows), F32),
            jax.ShapeDtypeStruct((height + sum(value.shape[0] for value in extra), rows), F32),
        ],
        compiler_params=params(),
        name="plane_mix",
        cost_estimate=SMALL,
    )(*coupling, *values, *extra)


def plane_rows_kernel(first_ref, meta_ref, meta_other_ref, a_ref, b_ref, c_ref, d_ref, *refs):
    if len(refs) > 2:
        *stack, last_ref, beside_ref, mine_ref, other_ref, stack_ref = refs
    else:
        mine_ref, other_ref = refs
    rows = a_ref.shape[1]
    value = jnp.concatenate([ref[pl.ds(0, HOURS), :] for ref in (a_ref, b_ref, c_ref, d_ref)], axis=1)
    one, two = pieces(value, 2)
    stacked = jnp.concatenate([two, one], axis=0)
    picked = []
    for ref in (meta_ref, meta_other_ref):
        gauge = ref[0:1, :]
        hot = jnp.concatenate([hot_rows(gauge, first_ref[m], rows) for m in range(4)], axis=0)
        both = dot(stacked, hot)
        picked.append(both[:HOURS] + both[HOURS:])
    mine_ref[...] = picked[0]
    count = picked[1].shape[1] // rows
    for i in range(count):
        other_ref[pl.ds(i * HOURS, HOURS), :] = picked[1][:, i * rows : (i + 1) * rows]
    if len(refs) > 2:
        top = stack_ref.shape[0] - HOURS
        for ref in stack:
            stack_ref[pl.ds(0, top), :] = ref[...]
        for i in range(count):
            here = pl.ds(i * rows, rows)
            beside = beside_ref[pl.ds(beside_ref.shape[0] - (count - i) * HOURS, HOURS), :]
            stack_ref[pl.ds(top, HOURS), here] = last_ref[:, here] + beside


def plane_rows(first, metas, values, before):
    rows = values[0].shape[1]
    slots = metas[0].shape[1]
    args = [first, *metas, *values, *before]
    shapes = [(HOURS, slots), (slots // rows * HOURS, rows)]
    if before:
        shapes.append(((len(before) - 1) * HOURS, slots))
    return pl.pallas_call(
        plane_rows_kernel,
        in_specs=[pl.BlockSpec(memory_space=pltpu.SMEM)]
        + [pl.BlockSpec(memory_space=pltpu.VMEM)] * (len(args) - 1),
        out_shape=[jax.ShapeDtypeStruct(shape, F32) for shape in shapes],
        compiler_params=params(),
        name="plane_rows",
        cost_estimate=pl.CostEstimate(flops=1_000_000_000, bytes_accessed=2_000_000, transcendentals=0),
    )(*args)


def gain(kernels):
    return jnp.max(jnp.sum(kernels, axis=1, keepdims=True), axis=0, keepdims=True)


def spectra(kind, kernels, wide):
    classes = kernels.shape[0]
    row = lax.broadcasted_iota(jnp.int32, (classes, kind.shape[1]), 0).astype(F32)
    hot = jnp.where(row == kind, 1.0, 0.0).astype(BF16)
    taps = jnp.transpose(kernels / gain(kernels))
    chosen = dot(jnp.concatenate(pieces(taps, 3)[::-1], axis=1), jnp.concatenate([hot] * 3, axis=0))
    return product(wide, chosen, 3)


def plane_spectrum_kernel(class_ref, kernels_ref, wide_ref, out_ref):
    kind = class_ref[1:2, : out_ref.shape[1]]
    out_ref[...] = spectra(kind, kernels_ref[...], wide_ref[...])


def plane_spectrum(meta, kernels, wide, rows):
    return pl.pallas_call(
        plane_spectrum_kernel,
        out_shape=jax.ShapeDtypeStruct((SPAN, rows), F32),
        compiler_params=params(),
        name="plane_spectrum",
        cost_estimate=SMALL,
    )(meta, kernels, wide)


def sides(even, pair, middle):
    return jnp.where(even, middle, pair), jnp.where(even, pair, middle)


def plane_call(kernel, name, shapes, flags, args):
    return pl.pallas_call(
        kernel,
        in_specs=[pl.BlockSpec(memory_space=pltpu.SMEM)] * len(flags)
        + [pl.BlockSpec(memory_space=pltpu.VMEM)] * len(args),
        out_shape=[jax.ShapeDtypeStruct(shape, F32) for shape in shapes],
        compiler_params=params(),
        name=name,
        cost_estimate=SMALL,
    )(*flags, *args)


def plane_first_kernel(
    flag_ref, here_ref, pair_ref, middle_ref, seen_ref, spec_ref, kernels_ref, forward, first, last, out_ref
):
    spec = spec_ref[...]
    before, after = sides(flag_ref[0] > 0.5, pair_ref[...], middle_ref[...])
    now, later = plane_delayed(before, here_ref[...], after, spec, forward[...], last[...], 3)
    known = plane_advanced(now, later * flag_ref[1], spec, forward[...], first[...], 3)
    out_ref[...] = seen_ref[...] - known * gain(kernels_ref[...])


def plane_delay_kernel(flag_ref, here_ref, pair_ref, middle_ref, spec_ref, forward, last, out_ref):
    body = pl.ds(0, HOURS)
    before, after = sides(flag_ref[0] > 0.5, pair_ref[body, :], middle_ref[body, :])
    out = plane_delayed(before, here_ref[body, :], after, spec_ref[...], forward[...], last[...], 2)
    for i in range(2):
        out_ref[pl.ds(i * HOURS, HOURS), :] = out[i]


def write_note(ref, rows):
    tail = [jnp.zeros((NOTE - len(rows), ref.shape[1]), F32)]
    ref[pl.ds(HOURS, NOTE), :] = jnp.concatenate(rows + tail, axis=0)


def plane_open_kernel(
    flag_ref, here_ref, pair_ref, middle_ref, pulled_ref, spec_ref, forward, first, last, out_ref, delayed_ref
):
    here = here_ref[...]
    spec = spec_ref[...]
    before, after = sides(flag_ref[0] > 0.5, pair_ref[...], middle_ref[...])
    now, later = plane_delayed(before, here, after, spec, forward[...], last[...], 2)
    out_ref[pl.ds(0, HOURS), :] = plane_advanced(now, later * flag_ref[1], spec, forward[...], first[...], 2)
    write_note(out_ref, [lanes(pulled_ref[...], here), lanes(now, now)])
    delayed_ref[pl.ds(0, HOURS), :] = now
    delayed_ref[pl.ds(HOURS, HOURS), :] = later


def plane_step_kernel(
    flag_ref,
    here_ref,
    pair_ref,
    two_ref,
    mirror_ref,
    pulled_ref,
    delayed_ref,
    old_z_ref,
    old_s_ref,
    old_delayed_ref,
    spec_ref,
    forward,
    first,
    total_ref,
    out_ref,
    kept_ref,
):
    tail, body = pl.ds(HOURS, NOTE), pl.ds(0, HOURS)
    total_ref[...] = (here_ref[tail, :] + pair_ref[tail, :]) + (two_ref[...] + mirror_ref[...])
    inverse = total(total_ref, 0) / total(total_ref, 1)
    z = pulled_ref[body, :] * inverse - old_z_ref[...]
    s = here_ref[body, :] * inverse - old_s_ref[...]
    both = delayed_ref[...] * inverse - old_delayed_ref[...]
    now, later = both[:HOURS], both[HOURS:]
    following = plane_advanced(now, later * flag_ref[1], spec_ref[...], forward[...], first[...], 2)
    out_ref[body, :] = following * inverse
    write_note(out_ref, [lanes(z, s), lanes(now, now)])
    for i, value in enumerate((z, s, now)):
        kept_ref[pl.ds(i * HOURS, HOURS), :] = value


def plane_close_kernel(
    here_ref, before_ref, pulled_ref, kept_ref, old_z_ref, old_s_ref, old_delayed_ref, spec_ref, forward, last, out_ref
):
    body = pl.ds(0, HOURS)
    here, raw = here_ref[body, :], pulled_ref[body, :]
    waves = product(forward[...], jnp.concatenate([before_ref[body, :], here], axis=0), 2)
    now = product(last[...], turn(waves, spec_ref[...], 1.0), 2)
    z, s, delayed = (kept_ref[pl.ds(i * HOURS, HOURS), :] for i in range(3))
    note = [pulled_ref[HOURS + i : HOURS + i + 1, :] for i in range(2)]
    for left in (raw, z, old_z_ref[...]):
        note += [lanes(left, right) for right in (here, s, old_s_ref[...])]
    parts = (now, delayed, old_delayed_ref[body, :])
    for i in range(3):
        note += [lanes(parts[i], parts[j]) for j in range(i, 3)]
    note.append(jnp.zeros((24 - len(note), here.shape[1]), F32))
    note = jnp.sum(jnp.concatenate(note, axis=0), axis=1, keepdims=True)
    shape = (24, out_ref.shape[2])
    row, col = (lax.broadcasted_iota(jnp.int32, shape, i) for i in range(2))
    note = jnp.sum(jnp.where(row == col, jnp.broadcast_to(note, shape), 0.0), axis=0, keepdims=True)
    out_ref[...] = jnp.broadcast_to(note[None], out_ref.shape)


def plane_weights(open_ref, close, scale):
    entry = lambda i: close[:, i : i + 1]
    n1, t1 = total(open_ref, 0), total(open_ref, 1)
    n2, t2 = entry(0), entry(1)
    a1 = t1 / n1
    a2, r2 = (t2 / n2) / a1, n2 / n1
    plain = (1.0, -a2, -r2)
    n3 = sum(plain[i] * plain[j] * entry(2 + 3 * i + j) for i in range(3) for j in range(3))
    pairs = [(i, j) for i in range(3) for j in range(i, 3)]
    t3 = sum(
        plain[i] * plain[j] * entry(11 + n) * (1.0 if i == j else 2.0) for n, (i, j) in enumerate(pairs)
    )
    a3, r3 = (t3 / n3) / a1, n3 / n2
    unit = 1.0 / (a1 * scale)
    c3 = unit / (a3 * (a2 - r2) - r3)
    c2 = -a3 * c3
    c1 = unit - r2 * c2
    step = c2 - c3 * a2
    return c1 - step - c3 * r2, step / a1, c3


def plane_combine_kernel(open_ref, close_ref, kernels_ref, stack_ref, mine_ref, beside_ref, out_ref):
    rows = open_ref.shape[1]
    close = jnp.sum(close_ref[...], axis=0)[0:1, :]
    e0, e1, e2 = plane_weights(open_ref, close, gain(kernels_ref[...]))
    for i in range(out_ref.shape[0] // rows):
        here = pl.ds(i * rows, rows)
        last = mine_ref[:, here] + beside_ref[pl.ds(i * HOURS, HOURS), :]
        value = stack_ref[pl.ds(0, HOURS), here] * e0 + stack_ref[pl.ds(HOURS, HOURS), here] * e1 + last * e2
        out_ref[here, :] = jnp.transpose(value)


def plane_finish_kernel(rows_ref, inc_ref, field_ref, out_ref):
    blocks, slots, width = inc_ref.shape
    weights = inc_ref[...].astype(F32).astype(BF16)
    for b in range(blocks):
        here = pl.ds(b * width, width)
        rows = jnp.concatenate(pieces(rows_ref[pl.ds(b * slots, slots), :], 2), axis=0)
        twice = jnp.concatenate([weights[b]] * 2, axis=0)
        added = lax.dot_general(twice, rows, (((0,), (0,)), ((), ())), preferred_element_type=F32)
        out_ref[here, :] = field_ref[here, :] + added


def plane_finish(rows, incidence, field):
    blocks, slots, width = incidence.shape
    hours = field.shape[1]
    step = 8
    return pl.pallas_call(
        plane_finish_kernel,
        grid=(blocks // step,),
        in_specs=[
            pl.BlockSpec((step * slots, hours), lambda i: (i, 0)),
            pl.BlockSpec((step, slots, width), lambda i: (i, 0, 0)),
            pl.BlockSpec((step * width, hours), lambda i: (i, 0)),
        ],
        out_specs=pl.BlockSpec((step * width, hours), lambda i: (i, 0)),
        out_shape=jax.ShapeDtypeStruct(field.shape, F32),
        compiler_params=params(),
        name="plane_finish",
    )(rows, incidence, field)


def plane_shards(incidence, row_gauge, gauge_kernel, kernels, observed, first_guess):
    rows, hours = observed.shape
    basin, tm = lax.axis_index("basin"), lax.axis_index("tm")
    z, x, y, c = basin // X_, basin % X_, tm // C_, tm % C_
    place = 2 * y + x
    first = jnp.stack([4 * c + (place ^ m) for m in range(4)] + [4 * c + place, 4 * (1 - c) + place])
    first = (first * rows).astype(jnp.int32)
    flags = jnp.stack([1 - z % 2, (z < Z_ - 1).astype(z.dtype), (z > 0).astype(z.dtype)]).astype(F32)
    forward, inverse_first, inverse_last, _ = turned_transforms(2)
    forward3, inverse_first3, inverse_last3, short3 = turned_transforms(3)
    block, noted = (hours, rows), (hours + NOTE, rows)

    parcel = send(incidence, first_guess)
    parcel, near, gauges, kinds, seen = lax.optimization_barrier(
        (parcel, incidence, row_gauge, gauge_kernel, observed)
    )
    parcel = moved(parcel, to_plane)
    meta = describe(near, gauges)
    meta = jnp.concatenate([meta, moved(meta, over_x)], axis=1)
    meta = jnp.concatenate([meta, moved(meta, z_pair)], axis=1)
    behind = observe(
        seen, moved(seen, hour_before), gauges, kinds, kernels, short3, [forward3, inverse_first3]
    )
    behind = moved(behind, to_plane)
    parcel, behind = lax.optimization_barrier((parcel, behind))
    seen, labels = behind[:-8], behind[-8:]
    seen = jnp.concatenate([seen[:, i : i + rows] for i in range(0, seen.shape[1], rows)], axis=0)
    parcels = [parcel, moved(parcel, over_core)]
    metas = [labels, moved(labels, over_core)]
    spec = plane_spectrum(labels, kernels, short3, rows)
    parcels[1], meta, spec = lax.optimization_barrier((parcels[1], meta, spec))
    around = [meta, moved(meta, z_two)]
    dense = spread(first, parcels, metas, rows)
    sums = dense[0] + sum(moved(value, where) for value, where in zip(dense[1:], SQUARE))
    sums = [sums, moved(sums, z_pair), moved(sums, z_middle)]
    coupled = plane_couple(first, around[0], rows)
    coupled, sums = lax.optimization_barrier((coupled, sums))
    coupling = plane_couple(first, around[1], rows, coupled)
    (pulled0,) = plane_call(
        plane_first_kernel,
        "plane_first",
        [block],
        [flags],
        [*sums, seen, spec, kernels, forward3, inverse_first3, inverse_last3],
    )

    def mixing(pulled, extra):
        values = [pulled] + [moved(pulled, where) for where in SQUARE]
        mine, other = plane_mix(coupling, values, extra)
        beside = moved(other, over_core)
        return values, mine + beside[: pulled.shape[0]], beside

    values, mixed0, _ = mixing(pulled0, [])
    picked, theirs = plane_rows(first, metas, values, [])
    sums = [mixed0, moved(mixed0, z_pair), moved(mixed0, z_middle)]
    pulled1, delayed0 = plane_call(
        plane_open_kernel,
        "plane_open",
        [noted, (2 * hours, rows)],
        [flags],
        [*sums, pulled0, spec, forward, inverse_first, inverse_last],
    )

    values, mixed1, beside = mixing(pulled1, [theirs])
    picked, theirs, stack = plane_rows(first, metas, values, [picked, beside])
    sums = [mixed1, moved(mixed1, z_pair), moved(mixed1, z_middle)]
    two, mirror = moved(mixed1[hours:], z_two), moved(mixed1[hours:], z_mirror)
    (delayed1,) = plane_call(
        plane_delay_kernel, "plane_delay", [(2 * hours, rows)], [flags], [*sums, spec, forward, inverse_last]
    )
    open_note, pulled2, kept = plane_call(
        plane_step_kernel,
        "plane_step",
        [(NOTE, rows), noted, (3 * hours, rows)],
        [flags],
        [*sums[:2], two, mirror, pulled1, delayed1, pulled0, mixed0, delayed0, spec, forward, inverse_first],
    )

    values, mixed2, beside = mixing(pulled2, [theirs])
    picked, theirs, stack = plane_rows(first, metas, values, [stack, picked, beside])
    (note,) = plane_call(
        plane_close_kernel,
        "plane_close",
        [(Z_ * X_ * Y_ * C_, 8, rows // 2)],
        [],
        [mixed2, moved(mixed2, z_next), pulled2, kept, pulled0, mixed0, delayed0, spec, forward, inverse_last],
    )
    close_note = lax.all_to_all(note, ("basin", "tm"), 0, 0, tiled=False)
    (answer,) = plane_call(
        plane_combine_kernel,
        "plane_combine",
        [(parcel.shape[1], hours)],
        [],
        [open_note, close_note, kernels, stack, picked, moved(theirs, over_core)],
    )
    return plane_finish(moved(answer, from_plane), incidence, first_guess)


def solution(mesh):
    planes = dict(mesh.shape) == {"basin": Z_ * X_, "tm": Y_ * C_}
    in_specs = (
        P("basin", None, None),
        P("basin"),
        P("basin"),
        P(),
        P("basin", "tm"),
        P("basin", "tm"),
    )
    return jax.shard_map(
        plane_shards if planes else shards, mesh=mesh, in_specs=in_specs, out_specs=P("basin", "tm"), check_vma=False
    )
```

```python
import functools

import jax
import jax.numpy as jnp
import numpy as np
from jax import lax
from jax.experimental import pallas as pl
from jax.experimental.pallas import tpu as pltpu
from jax.sharding import PartitionSpec as P

F32 = jnp.float32
BF16 = jnp.bfloat16
HIGH = lax.Precision.HIGHEST
SPAN = 256
MIB = 1024 * 1024


SMALL = pl.CostEstimate(flops=1, bytes_accessed=1, transcendentals=0)


def params(mib=16):
    return pltpu.CompilerParams(vmem_limit_bytes=mib * MIB)


def transforms():
    half = SPAN // 2
    freq = 2.0 * np.pi * (np.arange(half) + 0.5) / SPAN
    phase = np.arange(SPAN)[:, None] * freq[None, :]
    forward = np.concatenate([np.cos(phase), -np.sin(phase)], axis=1)
    inverse = forward.T * (2.0 / SPAN)
    return (
        jnp.asarray(forward, F32),
        jnp.asarray(inverse[:, :half], F32),
        jnp.asarray(inverse[:, half:], F32),
    )


def dot(a, b):
    return jnp.dot(a, b, preferred_element_type=F32)


def exact(a, b):
    return jnp.dot(a, b, precision=HIGH, preferred_element_type=F32)


def pieces(value, count):
    out = []
    for _ in range(count):
        piece = value.astype(BF16)
        out.append(piece)
        value = value - piece.astype(F32)
    return out


def pick(hot, value):
    return sum(dot(hot, piece) for piece in pieces(value, 3))


def prepare_kernel(inc_ref, field_ref, partial_ref, gram_ref):
    blocks, slots, width = inc_ref.shape
    rows = blocks * slots
    weights = inc_ref[...].astype(F32).astype(BF16)
    for b in range(blocks):
        value = field_ref[pl.ds(b * width, width), :]
        partial_ref[pl.ds(b * slots, slots), :] = pick(weights[b], value)
    flat = weights.reshape(rows, width)
    full = lax.dot_general(flat, flat, (((1,), (1,)), ((), ())), preferred_element_type=F32)
    row = lax.broadcasted_iota(jnp.int32, (rows, rows), 0)
    col = lax.broadcasted_iota(jnp.int32, (rows, rows), 1)
    own = jnp.where(row // slots == col // slots, full, 0.0)
    gram_ref[...] = jnp.sum(own.reshape(blocks, slots, rows), axis=0)


def prepare(incidence, field):
    blocks, slots, width = incidence.shape
    hours = field.shape[1]
    step = 8
    return pl.pallas_call(
        prepare_kernel,
        grid=(blocks // step,),
        in_specs=[
            pl.BlockSpec((step, slots, width), lambda i: (i, 0, 0)),
            pl.BlockSpec((step * width, hours), lambda i: (i, 0)),
        ],
        out_specs=[
            pl.BlockSpec((step * slots, hours), lambda i: (i, 0)),
            pl.BlockSpec((slots, step * slots), lambda i: (0, i)),
        ],
        out_shape=[
            jax.ShapeDtypeStruct((blocks * slots, hours), F32),
            jax.ShapeDtypeStruct((slots, blocks * slots), F32),
        ],
        compiler_params=params(56),
        name="prepare",
    )(incidence, field)


def table_kernel(gauge_ref, partial_ref, out_ref):
    slots = partial_ref.shape[0]
    rows = out_ref.shape[0]
    first = pl.program_id(0) * rows
    gauge = lax.broadcasted_iota(jnp.int32, (rows, slots), 0) + first
    hot = jnp.where(gauge_ref[...] == gauge, 1.0, 0.0).astype(BF16)
    out_ref[...] = pick(hot, partial_ref[...])


def table(row_gauge, partial, gauges):
    slots, hours = partial.shape
    step = 256
    return pl.pallas_call(
        table_kernel,
        grid=(gauges // step,),
        in_specs=[
            pl.BlockSpec((1, slots), lambda i: (0, 0)),
            pl.BlockSpec((slots, hours), lambda i: (0, 0)),
        ],
        out_specs=pl.BlockSpec((step, hours), lambda i: (i, 0)),
        out_shape=jax.ShapeDtypeStruct((gauges, hours), F32),
        compiler_params=params(56),
        name="table",
    )(row_gauge.reshape(1, slots), partial)


def couple_kernel(first_ref, lane_ref, sub_ref, gram_ref, high_ref, low_ref, near_ref):
    slots = gram_ref.shape[0]
    count = lane_ref.shape[1]
    rows, cols = high_ref.shape
    tile = 256
    first = first_ref[0]

    @pl.when(pl.program_id(0) == 0)
    def _():
        row = lax.broadcasted_iota(jnp.int32, (tile, tile), 0)
        col = lax.broadcasted_iota(jnp.int32, (tile, tile), 1)
        same = row // slots == col // slots
        mine = lax.broadcasted_iota(jnp.int32, (rows, tile), 0) + first

        def body(i, carry):
            here = pl.ds(pl.multiple_of(i * tile, tile), tile)
            block = jnp.concatenate([gram_ref[:, here]] * (tile // slots), axis=0)
            block = jnp.where(same, block, 0.0).astype(BF16)
            hot = jnp.where(lane_ref[:, here] == mine, 1.0, 0.0).astype(BF16)
            near_ref[:, here] = dot(hot, block)
            return carry

        lax.fori_loop(0, count // tile, body, 0)

    def chunk(i, total):
        here = pl.ds(pl.multiple_of(i * 1024, 1024), 1024)
        gauge = lax.broadcasted_iota(jnp.int32, (1024, cols), 1) + pl.program_id(0) * cols
        hot = jnp.where(sub_ref[here, :] == gauge, 1.0, 0.0).astype(BF16)
        near = near_ref[:, here]
        high = near.astype(BF16)
        low = (near - high.astype(F32)).astype(BF16)
        return total + dot(high, hot) + dot(low, hot)

    total = lax.fori_loop(0, count // 1024, chunk, jnp.zeros((rows, cols), F32))
    high, low = pieces(total, 2)
    high_ref[...] = high
    low_ref[...] = low


def couple(first, row_gauge, gram, rows, gauges):
    count = row_gauge.shape[0]
    step = 256
    return pl.pallas_call(
        couple_kernel,
        grid=(gauges // step,),
        in_specs=[
            pl.BlockSpec(memory_space=pltpu.SMEM),
            pl.BlockSpec((1, count), lambda i: (0, 0)),
            pl.BlockSpec((count, 1), lambda i: (0, 0)),
            pl.BlockSpec(gram.shape, lambda i: (0, 0)),
        ],
        out_specs=[pl.BlockSpec((rows, step), lambda i: (0, i))] * 2,
        out_shape=[jax.ShapeDtypeStruct((rows, gauges), BF16)] * 2,
        scratch_shapes=[pltpu.VMEM((rows, count), F32)],
        compiler_params=params(56),
        name="couple",
    )(first, row_gauge.reshape(1, count), row_gauge.reshape(count, 1), gram)


def mix_kernel(high_ref, low_ref, value_ref, out_ref):
    high = high_ref[...]
    low = low_ref[...]
    one, two, three = pieces(value_ref[...], 3)
    out_ref[...] = (dot(high, three) + dot(low, two)) + (dot(high, two) + dot(low, one)) + dot(high, one)


def mix(high, low, value):
    return pl.pallas_call(
        mix_kernel,
        out_shape=jax.ShapeDtypeStruct((high.shape[0], value.shape[1]), F32),
        compiler_params=params(56),
        name="mix",
    )(high, low, value)


def spectrum_kernel(class_ref, kernels_ref, forward_ref, out_ref):
    rows = class_ref.shape[0]
    classes, taps = kernels_ref.shape
    kind = lax.broadcasted_iota(jnp.int32, (rows, classes), 1)
    hot = jnp.where(class_ref[...] == kind, 1.0, 0.0)
    out_ref[...] = exact(exact(hot, kernels_ref[...]), forward_ref[pl.ds(0, taps), :])


def spectrum(gauge_kernel, kernels, forward):
    rows = gauge_kernel.shape[0]
    return pl.pallas_call(
        spectrum_kernel,
        out_shape=jax.ShapeDtypeStruct((rows, SPAN), F32),
        compiler_params=params(56),
        name="spectrum",
    )(gauge_kernel.reshape(rows, 1), kernels, forward)


def delayed(before, here, after, spec, forward, inverse_last):
    rows, half = here.shape
    stacked = jnp.concatenate(
        [jnp.concatenate([before, here], axis=1), jnp.concatenate([here, after], axis=1)], axis=0
    )
    waves = exact(stacked, forward)
    real, imag = waves[:, :half], waves[:, half:]
    kr = jnp.concatenate([spec[:, :half]] * 2, axis=0)
    ki = jnp.concatenate([spec[:, half:]] * 2, axis=0)
    turned = jnp.concatenate([real * kr - imag * ki, real * ki + imag * kr], axis=1)
    out = exact(turned, inverse_last)
    return out[:rows], out[rows:]


def advanced(here, after, spec, forward, inverse_first):
    half = here.shape[1]
    waves = exact(jnp.concatenate([here, after], axis=1), forward)
    real, imag = waves[:, :half], waves[:, half:]
    kr, ki = spec[:, :half], spec[:, half:]
    turned = jnp.concatenate([real * kr + imag * ki, imag * kr - real * ki], axis=1)
    return exact(turned, inverse_first)


def lanes(a, b):
    return jnp.sum(a * b, axis=0, keepdims=True)


def total(ref, row):
    return jnp.sum(ref[row : row + 1, :], axis=1, keepdims=True)


def ratios(ref):
    square = total(ref, 0)
    alpha = jnp.sqrt(square)
    beta = jnp.sqrt(jnp.maximum(total(ref, 1) / square - 2.0 * total(ref, 2) + square, 0.0))
    return alpha, beta


def first_kernel(
    more_ref, sums_ref, observed_ref, spec_ref, forward_ref, first_ref, last_ref, out_ref, note_ref
):
    rows, half = observed_ref.shape[0] // 2, observed_ref.shape[1]
    spec, forward = spec_ref[...], forward_ref[...]
    before, here, after = (sums_ref[pl.ds(i * rows, rows), :] for i in range(3))
    now, later = delayed(before, here, after, spec, forward, last_ref[...])
    start = observed_ref[pl.ds(0, rows), :] - now
    start_later = (observed_ref[pl.ds(rows, rows), :] - later) * more_ref[0]
    out_ref[...] = advanced(start, start_later, spec, forward, first_ref[...])
    note_ref[...] = jnp.concatenate([lanes(start, start), jnp.zeros((7, half), F32)], axis=0)


def first_step(more, sums, observed, spec, mats):
    rows, half = spec.shape[0], observed.shape[1]
    return pl.pallas_call(
        first_kernel,
        in_specs=[pl.BlockSpec(memory_space=pltpu.SMEM)] + [pl.BlockSpec(memory_space=pltpu.VMEM)] * 6,
        out_shape=[jax.ShapeDtypeStruct((rows, half), F32), jax.ShapeDtypeStruct((8, half), F32)],
        compiler_params=params(56),
        name="first_step",
    )(more, sums, observed, spec, *mats)


def step_kernel(
    opening,
    final,
    more_ref,
    note_ref,
    sums_ref,
    spec_ref,
    forward_ref,
    first_ref,
    last_ref,
    pulled_ref,
    *refs,
):
    if opening:
        state_ref = None
    else:
        state_ref, *refs = refs
    if final:
        (out_note_ref,) = refs
    else:
        new_ref, out_ref, out_note_ref = refs
    rows, half = pulled_ref.shape
    spec, forward = spec_ref[...], forward_ref[...]
    if opening:
        scale = 1.0 / jnp.sqrt(total(note_ref, 0))
        along = sums_ref[...] * scale
        new_s, new_su = along, along
        new_zu = pulled_ref[...] * scale
        new_z = new_zu
    else:
        alpha, beta = ratios(note_ref)
        a, b, g = 1.0 / (alpha * beta), alpha / beta, beta / alpha
        wide = pl.ds(0, 3 * rows), pl.ds(3 * rows, 3 * rows)
        new_su = sums_ref[...] * a - state_ref[wide[1], :] * b
        new_s = new_su - state_ref[wide[0], :] * g
        new_zu = pulled_ref[...] * a - state_ref[pl.ds(7 * rows, rows), :] * b
        new_z = new_zu - state_ref[pl.ds(6 * rows, rows), :] * g
    before, here, after = (new_s[i * rows : (i + 1) * rows] for i in range(3))
    now, later = delayed(before, here, after, spec, forward, last_ref[...])
    out_note_ref[...] = jnp.concatenate(
        [lanes(new_z, here), lanes(now, now), lanes(new_zu, here), jnp.zeros((5, half), F32)], axis=0
    )
    if not final:
        new_ref[pl.ds(0, 3 * rows), :] = new_s
        new_ref[pl.ds(3 * rows, 3 * rows), :] = new_su
        new_ref[pl.ds(6 * rows, rows), :] = new_z
        new_ref[pl.ds(7 * rows, rows), :] = new_zu
        out_ref[...] = advanced(now, later * more_ref[0], spec, forward, first_ref[...])


def next_step(more, note, sums, spec, mats, pulled, state, final):
    rows, half = pulled.shape
    opening = state is None
    shapes = [
        jax.ShapeDtypeStruct((8 * rows, half), F32),
        jax.ShapeDtypeStruct((rows, half), F32),
        jax.ShapeDtypeStruct((8, half), F32),
    ]
    args = [more, note, sums, spec, *mats, pulled] + ([] if opening else [state])
    return pl.pallas_call(
        functools.partial(step_kernel, opening, final),
        in_specs=[pl.BlockSpec(memory_space=pltpu.SMEM)]
        + [pl.BlockSpec(memory_space=pltpu.VMEM)] * (len(args) - 1),
        out_shape=shapes[2:] if final else shapes,
        compiler_params=params(56),
        name="next_step",
    )(*args)


def weights_of(notes):
    start = jnp.sqrt(total(notes[0], 0))
    zero = jnp.zeros_like(start)
    units = [1.0 / start, zero, zero]
    z, zu = list(units), list(units)
    phibar = start
    alpha, beta = ratios(notes[1])
    rhobar = alpha
    w = [value / alpha for value in z]
    result = [zero] * 3
    steps = len(notes) - 1
    for k in range(steps):
        rho = jnp.sqrt(rhobar * rhobar + beta * beta)
        cosine, sine = rhobar / rho, beta / rho
        phi, phibar = cosine * phibar, sine * phibar
        result = [r + phi / rho * value for r, value in zip(result, w)]
        if k < steps - 1:
            a, b, g = 1.0 / (alpha * beta), alpha / beta, beta / alpha
            zu = [(a if i == k + 1 else 0.0) - b * value for i, value in enumerate(zu)]
            z = [value - g * old for value, old in zip(zu, z)]
            alpha, beta = ratios(notes[k + 2])
            theta = sine * alpha
            rhobar = -cosine * alpha
            w = [value / alpha - theta / rho * old for value, old in zip(z, w)]
    return result


def finish_kernel(n0, n1, n2, n3, gauge_ref, q0, q1, q2, inc_ref, field_ref, out_ref, rows_ref):
    blocks, slots, width = inc_ref.shape
    count = rows_ref.shape[0]
    gauges = q0.shape[0]
    step = pl.program_id(0)

    @pl.when(step == 0)
    def _():
        e0, e1, e2 = weights_of([n0, n1, n2, n3])
        width_ = 512

        def body(i, value):
            here = pl.ds(pl.multiple_of(i * width_, width_), width_)
            mixed = q0[here, :] * e0 + q1[here, :] * e1 + q2[here, :] * e2
            gauge = lax.broadcasted_iota(jnp.int32, (count, width_), 1) + i * width_
            hot = jnp.where(gauge_ref[...] == gauge, 1.0, 0.0).astype(BF16)
            return value + pick(hot, mixed)

        rows_ref[...] = lax.fori_loop(0, gauges // width_, body, jnp.zeros(rows_ref.shape, F32))

    weights = inc_ref[...].astype(F32).astype(BF16)
    for b in range(blocks):
        here = pl.ds(b * width, width)
        rows = rows_ref[pl.ds(pl.multiple_of((step * blocks + b) * slots, slots), slots), :]
        added = sum(
            lax.dot_general(weights[b], piece, (((0,), (0,)), ((), ())), preferred_element_type=F32)
            for piece in pieces(rows, 3)
        )
        out_ref[here, :] = field_ref[here, :] + added


def finish(notes, row_gauge, gathered, incidence, field):
    blocks, slots, width = incidence.shape
    hours = field.shape[1]
    count = row_gauge.shape[0]
    step = 8
    whole = lambda shape: pl.BlockSpec(shape, lambda i: (0, 0))
    return pl.pallas_call(
        finish_kernel,
        grid=(blocks // step,),
        in_specs=[whole(n.shape) for n in notes]
        + [whole((count, 1))]
        + [whole(q.shape) for q in gathered]
        + [
            pl.BlockSpec((step, slots, width), lambda i: (i, 0, 0)),
            pl.BlockSpec((step * width, hours), lambda i: (i, 0)),
        ],
        out_specs=pl.BlockSpec((step * width, hours), lambda i: (i, 0)),
        out_shape=jax.ShapeDtypeStruct(field.shape, F32),
        scratch_shapes=[pltpu.VMEM((count, hours), F32)],
        compiler_params=params(56),
        name="finish",
    )(*notes, row_gauge.reshape(count, 1), *gathered, incidence, field)


def shifted(value, axis, by):
    devices = lax.axis_size(axis)
    pairs = [(i, i + by) for i in range(devices) if 0 <= i + by < devices]
    return lax.ppermute(value, axis, pairs)


def window(value):
    return jnp.concatenate([shifted(value, "tm", 1), value, shifted(value, "tm", -1)], axis=0)


def gathered_rows(value):
    owners = lax.axis_size("basin")
    copies = jnp.broadcast_to(value[None], (owners,) + value.shape)
    return lax.all_to_all(copies, "basin", 0, 0, tiled=False)


def over_hours(note):
    blocks = lax.axis_size("tm")
    result = note
    for by in range(1, blocks):
        result = result + lax.ppermute(note, "tm", [(i, (i + by) % blocks) for i in range(blocks)])
    return result


def shards(incidence, row_gauge, gauge_kernel, kernels, observed, first_guess):
    owners = lax.axis_size("basin")
    rows, hours = observed.shape
    gauges = rows * owners
    mats = transforms()
    spec = spectrum(gauge_kernel, kernels, mats[0])
    more = (lax.axis_index("tm") < lax.axis_size("tm") - 1).astype(F32).reshape(1)
    partial, gram = prepare(incidence, first_guess)
    all_gram = lax.all_gather(gram, "basin", axis=1, tiled=True)
    all_rows = lax.all_gather(row_gauge, "basin", axis=0, tiled=True)
    dense = table(row_gauge, partial, gauges).reshape(owners, rows, hours)
    sums = jnp.sum(lax.all_to_all(dense, "basin", 0, 0, tiled=False), axis=0)
    both = jnp.concatenate([observed, shifted(observed, "tm", -1)], axis=0)
    first = (lax.axis_index("basin") * rows).astype(jnp.int32).reshape(1)
    high, low = couple(first, all_rows, all_gram, rows, gauges)

    pulled, note = first_step(more, window(sums), both, spec, mats)
    notes, kept, state = [], [], None
    for k in range(3):
        everyone = gathered_rows(jnp.concatenate([pulled, note], axis=0))
        value = everyone[:, :rows].reshape(gauges, hours)
        notes.append(over_hours(jnp.sum(everyone[:, rows:], axis=0)))
        kept.append(value)
        around = window(mix(high, low, value))
        final = k == 2
        result = next_step(more, notes[-1], around, spec, mats, pulled, state, final)
        if final:
            (note,) = result
        else:
            state, pulled, note = result
    notes.append(over_hours(jnp.sum(gathered_rows(note), axis=0)))
    return finish(notes, row_gauge, kept, incidence, first_guess)


Z_, X_, Y_, C_ = 4, 2, 2, 2
NOTE = 8
HOURS = SPAN // 2


def device(z, x, y, c):
    return (z * X_ + x) * (Y_ * C_) + y * C_ + c


def moved(value, where):
    pairs = []
    for z, x, y, c in np.ndindex(Z_, X_, Y_, C_):
        target = where(z, x, y, c)
        if target is not None:
            pairs.append((device(z, x, y, c), device(*target)))
    return lax.ppermute(value, ("basin", "tm"), pairs)


def to_plane(z, x, y, c):
    return 2 * y + c, x, z & 1, z >> 1


def hour_before(z, x, y, c):
    t = 2 * y + c - 1
    return (z, x, t >> 1, t & 1) if t >= 0 else None


def from_plane(z, x, y, c):
    return 2 * c + y, x, z >> 1, z & 1


def over_x(z, x, y, c):
    return z, 1 - x, y, c


def over_y(z, x, y, c):
    return z, x, 1 - y, c


def over_xy(z, x, y, c):
    return z, 1 - x, 1 - y, c


def over_core(z, x, y, c):
    return z, x, y, 1 - c


def z_pair(z, x, y, c):
    return z ^ 1, x, y, c


def z_middle(z, x, y, c):
    return (3 - z, x, y, c) if z in (1, 2) else None


def z_two(z, x, y, c):
    return z ^ 2, x, y, c


def z_mirror(z, x, y, c):
    return 3 - z, x, y, c


def z_next(z, x, y, c):
    return (z + 1, x, y, c) if z < 3 else None


SQUARE = (over_x, over_y, over_xy)


def split_constant(value):
    out = []
    for _ in range(3):
        piece = value.astype(jnp.bfloat16)
        out.append(piece)
        value = value - piece.astype(np.float64)
    return out


ORDERS = {2: ((0, 1), (1, 0), (0, 0)), 3: ((0, 2), (1, 1), (2, 0), (0, 1), (1, 0), (0, 0))}


def widened(mat, order):
    parts = split_constant(mat)
    return jnp.asarray(np.concatenate([parts[i] for i, _ in ORDERS[order]], axis=1))


def product(wide, value, order):
    parts = pieces(value, order)
    return dot(wide, jnp.concatenate([parts[j] for _, j in ORDERS[order]], axis=0))


def turned_transforms(order):
    half = SPAN // 2
    freq = 2.0 * np.pi * (np.arange(half) + 0.5) / SPAN
    phase = freq[:, None] * np.arange(SPAN)[None, :]
    forward = np.concatenate([np.cos(phase), -np.sin(phase)], axis=0)
    inverse = forward.T * (2.0 / SPAN)
    return [widened(mat, order) for mat in (forward, inverse[:half], inverse[half:], forward[:, :half])]


def turn(waves, spec, sign):
    half = waves.shape[0] // 2
    real, imag = waves[:half], waves[half:]
    kr, ki = spec[:half], spec[half:] * sign
    return jnp.concatenate([real * kr - imag * ki, real * ki + imag * kr], axis=0)


def plane_delayed(before, here, after, spec, forward, last, order):
    rows = here.shape[1]
    pairs = [jnp.concatenate(pair, axis=0) for pair in ((before, here), (here, after))]
    waves = product(forward, jnp.concatenate(pairs, axis=1), order)
    turned = [turn(waves[:, i * rows : (i + 1) * rows], spec, 1.0) for i in range(2)]
    out = product(last, jnp.concatenate(turned, axis=1), order)
    return out[:, :rows], out[:, rows:]


def plane_advanced(here, after, spec, forward, first, order):
    waves = product(forward, jnp.concatenate([here, after], axis=0), order)
    return product(first, turn(waves, spec, -1.0), order)


def describe_kernel(inc_ref, gauge_ref, out_ref):
    blocks, slots, width = inc_ref.shape
    tile = 8
    side = tile * slots
    weights = inc_ref[...].astype(F32).astype(BF16)
    row = lax.broadcasted_iota(jnp.int32, (side, side), 0)
    col = lax.broadcasted_iota(jnp.int32, (side, side), 1)
    same = row // slots == col // slots
    for i in range(blocks // tile):
        flat = weights[i * tile : (i + 1) * tile].reshape(side, width)
        full = lax.dot_general(flat, flat, (((1,), (1,)), ((), ())), preferred_element_type=F32)
        own = jnp.where(same, full, 0.0)
        out_ref[pl.ds(0, slots), pl.ds(i * side, side)] = jnp.sum(own.reshape(tile, slots, side), axis=0)
    out_ref[pl.ds(slots, 8), :] = jnp.broadcast_to(gauge_ref[...].astype(F32), (8, blocks * slots))


def describe(incidence, row_gauge):
    blocks, slots, _ = incidence.shape
    count = blocks * slots
    return pl.pallas_call(
        describe_kernel,
        out_shape=jax.ShapeDtypeStruct((slots + 8, count), F32),
        compiler_params=params(),
        name="describe",
        cost_estimate=SMALL,
    )(incidence, row_gauge.reshape(1, count))


def observe_kernel(seen_ref, later_ref, kind_ref, kernels_ref, wide_ref, forward, first, out_ref):
    spec = spectra(kind_ref[...].astype(F32), kernels_ref[...], wide_ref[...])
    here, after = jnp.transpose(seen_ref[...]), jnp.transpose(later_ref[...])
    out_ref[...] = plane_advanced(here, after, spec, forward[...], first[...], 3)


def observe(seen, later, gauge_kernel, kernels, wide, mats):
    rows, hours = seen.shape
    return pl.pallas_call(
        observe_kernel,
        out_shape=jax.ShapeDtypeStruct((hours, rows), F32),
        compiler_params=params(),
        name="observe",
        cost_estimate=SMALL,
    )(seen, later, gauge_kernel.reshape(1, rows), kernels, wide, *mats)


def send_kernel(
    inc_hbm, field_hbm, gauge_hbm, kind_hbm, out_ref, inc_ref, field_ref, gauge_ref, kind_ref, sems, label_sems
):
    blocks, slots, width = inc_ref.shape
    chunks = sems.shape[0]
    step = blocks // chunks
    copies = []
    for i in range(chunks):
        near = pl.ds(i * step, step)
        far = pl.ds(i * step * width, step * width)
        copies.append(
            (
                pltpu.make_async_copy(inc_hbm.at[near], inc_ref.at[near], sems.at[i, 0]),
                pltpu.make_async_copy(field_hbm.at[far], field_ref.at[far], sems.at[i, 1]),
            )
        )
        for copy in copies[-1]:
            copy.start()
    labels = (
        pltpu.make_async_copy(gauge_hbm, gauge_ref, label_sems.at[0]),
        pltpu.make_async_copy(kind_hbm, kind_ref, label_sems.at[1]),
    )
    for copy in labels:
        copy.start()
    for i in range(chunks):
        for copy in copies[i]:
            copy.wait()
        parts = []
        for b in range(i * step, (i + 1) * step):
            weight = inc_ref[b].astype(F32).astype(BF16)
            value = jnp.concatenate(pieces(field_ref[pl.ds(b * width, width), :], 3)[::-1], axis=0)
            parts.append(dot(jnp.concatenate([weight] * 3, axis=1), value))
        out_ref[pl.ds(0, HOURS), pl.ds(i * step * slots, step * slots)] = jnp.transpose(
            jnp.concatenate(parts, axis=0)
        )
    for copy in labels:
        copy.wait()
    count, kinds = gauge_ref.shape[1], kind_ref.shape[1]
    kind = jnp.concatenate([kind_ref[...].astype(F32), jnp.zeros((1, count - kinds), F32)], axis=1)
    out_ref[pl.ds(HOURS, 8), :] = jnp.concatenate(
        [gauge_ref[...].astype(F32), kind, jnp.zeros((6, count), F32)], axis=0
    )


def send(incidence, field, row_gauge, gauge_kernel):
    count, rows = row_gauge.shape[0], gauge_kernel.shape[0]
    chunks = 4
    return pl.pallas_call(
        send_kernel,
        in_specs=[pl.BlockSpec(memory_space=pltpu.HBM)] * 4,
        out_shape=jax.ShapeDtypeStruct((HOURS + 8, count), F32),
        scratch_shapes=[
            pltpu.VMEM(incidence.shape, incidence.dtype),
            pltpu.VMEM(field.shape, F32),
            pltpu.VMEM((1, count), row_gauge.dtype),
            pltpu.VMEM((1, rows), gauge_kernel.dtype),
            pltpu.SemaphoreType.DMA((chunks, 2)),
            pltpu.SemaphoreType.DMA((2,)),
        ],
        compiler_params=params(60),
        name="send",
        cost_estimate=SMALL,
    )(incidence, field, row_gauge.reshape(1, count), gauge_kernel.reshape(1, rows))


def hot_rows(gauge, first, rows):
    mine = (lax.broadcasted_iota(jnp.int32, (rows, gauge.shape[1]), 0) + first).astype(F32)
    return jnp.where(gauge == mine, 1.0, 0.0).astype(BF16)


def spread_kernel(first_ref, mine_ref, other_ref, *out_refs):
    rows = out_refs[0].shape[1]
    both = jnp.concatenate([mine_ref[...], other_ref[...]], axis=1)
    stacked = jnp.concatenate(pieces(both[:HOURS], 3), axis=0)
    for m, out_ref in enumerate(out_refs):
        hot = hot_rows(both[HOURS : HOURS + 1], first_ref[m], rows)
        result = lax.dot_general(stacked, hot, (((1,), (1,)), ((), ())), preferred_element_type=F32)
        out_ref[...] = (result[2 * HOURS :] + result[HOURS : 2 * HOURS]) + result[:HOURS]


def spread(first, parcels, rows):
    return pl.pallas_call(
        spread_kernel,
        in_specs=[pl.BlockSpec(memory_space=pltpu.SMEM)] + [pl.BlockSpec(memory_space=pltpu.VMEM)] * 2,
        out_shape=[jax.ShapeDtypeStruct((HOURS, rows), F32)] * 4,
        compiler_params=params(),
        name="spread",
        cost_estimate=SMALL,
    )(first, *parcels)


def plane_couple_kernel(last, first_ref, *refs):
    if last:
        all_ref, before_ref, high_ref, low_ref, total_ref, meta_ref = refs
        total_ref[...] = before_ref[...]
    else:
        all_ref, total_ref, meta_ref = refs
        total_ref[...] = jnp.zeros_like(total_ref)
    parts, height, count = meta_ref.shape
    slots = height - 8
    cols, rows = total_ref.shape
    tile = 256
    for i in range(parts):
        meta_ref[i] = all_ref[:, i * count : (i + 1) * count]
    row = lax.broadcasted_iota(jnp.int32, (tile, tile), 0)
    col = lax.broadcasted_iota(jnp.int32, (tile, tile), 1)
    same = row // slots == col // slots

    def body(i, carry):
        gauge = meta_ref[i, slots : slots + 1, :]
        near = []
        for j in range(count // tile):
            here = slice(j * tile, (j + 1) * tile)
            block = jnp.concatenate([meta_ref[i, :slots, here]] * (tile // slots), axis=0)
            block = jnp.where(same, block, 0.0).astype(BF16)
            mine = jnp.concatenate(
                [hot_rows(gauge[:, here], first_ref[4 + h], rows // 2) for h in range(2)], axis=0
            )
            near.append(
                lax.dot_general(block, mine, (((1,), (1,)), ((), ())), preferred_element_type=F32)
            )
        near = jnp.concatenate(near, axis=0)
        high = near.astype(BF16)
        rest = near - high.astype(F32)
        hot = jnp.concatenate([hot_rows(gauge, first_ref[m], cols // 4) for m in range(4)], axis=0)
        total_ref[...] += dot(hot, high)

        @pl.when(jnp.max(jnp.abs(rest)) > 0.0)
        def _():
            total_ref[...] += dot(hot, rest.astype(BF16))

        return carry

    lax.fori_loop(0, parts, body, 0)
    if last:
        high, low = pieces(total_ref[...], 2)
        high_ref[...] = high
        low_ref[...] = low


def plane_couple(first, meta, rows, before=None):
    height, wide = meta.shape
    parts = 2 * X_
    shape = (4 * rows, 2 * rows)
    last = before is not None
    args = [first, meta] + ([before] if last else [])
    scratch = [pltpu.VMEM((parts, height, wide // parts), F32)]
    return pl.pallas_call(
        functools.partial(plane_couple_kernel, last),
        in_specs=[pl.BlockSpec(memory_space=pltpu.SMEM)]
        + [pl.BlockSpec(memory_space=pltpu.VMEM)] * (len(args) - 1),
        out_shape=[jax.ShapeDtypeStruct(shape, BF16)] * 2 if last else jax.ShapeDtypeStruct(shape, F32),
        scratch_shapes=([pltpu.VMEM(shape, F32)] if last else []) + scratch,
        compiler_params=params(),
        name="plane_couple",
        cost_estimate=pl.CostEstimate(
            flops=2 * 8 * wide * rows * rows, bytes_accessed=2_000_000, transcendentals=0
        ),
    )(*args)


def plane_mix_kernel(high_ref, low_ref, a_ref, b_ref, c_ref, d_ref, *refs):
    *extra, mine_ref, other_ref = refs
    refs = (a_ref, b_ref, c_ref, d_ref)
    height, rows = a_ref.shape
    body = pl.ds(0, HOURS)
    one, two = pieces(jnp.concatenate([ref[body, :] for ref in refs], axis=1), 2)
    both = dot(jnp.concatenate([two, one], axis=0), high_ref[...])
    result = (both[:HOURS] + dot(one, low_ref[...])) + both[HOURS:]
    mine_ref[body, :] = result[:, :rows]
    other_ref[body, :] = result[:, rows:]
    if height > HOURS:
        tail = pl.ds(HOURS, NOTE)
        note = sum(ref[tail, :] for ref in refs)
        mine_ref[tail, :] = note
        other_ref[tail, :] = note
    for ref in extra:
        other_ref[pl.ds(height, ref.shape[0]), :] = ref[...]


def plane_mix(coupling, values, extra):
    height, rows = values[0].shape
    return pl.pallas_call(
        plane_mix_kernel,
        out_shape=[
            jax.ShapeDtypeStruct((height, rows), F32),
            jax.ShapeDtypeStruct((height + sum(value.shape[0] for value in extra), rows), F32),
        ],
        compiler_params=params(),
        name="plane_mix",
        cost_estimate=SMALL,
    )(*coupling, *values, *extra)


def plane_rows_kernel(first_ref, meta_ref, meta_other_ref, a_ref, b_ref, c_ref, d_ref, *refs):
    if len(refs) > 2:
        *stack, last_ref, beside_ref, mine_ref, other_ref, stack_ref = refs
    else:
        mine_ref, other_ref = refs
    rows = a_ref.shape[1]
    value = jnp.concatenate([ref[pl.ds(0, HOURS), :] for ref in (a_ref, b_ref, c_ref, d_ref)], axis=1)
    one, two = pieces(value, 2)
    stacked = jnp.concatenate([two, one], axis=0)
    picked = []
    for ref in (meta_ref, meta_other_ref):
        gauge = ref[0:1, :]
        hot = jnp.concatenate([hot_rows(gauge, first_ref[m], rows) for m in range(4)], axis=0)
        both = dot(stacked, hot)
        picked.append(both[:HOURS] + both[HOURS:])
    mine_ref[...] = picked[0]
    count = picked[1].shape[1] // rows
    for i in range(count):
        other_ref[pl.ds(i * HOURS, HOURS), :] = picked[1][:, i * rows : (i + 1) * rows]
    if len(refs) > 2:
        top = stack_ref.shape[0] - HOURS
        for ref in stack:
            stack_ref[pl.ds(0, top), :] = ref[...]
        for i in range(count):
            here = pl.ds(i * rows, rows)
            beside = beside_ref[pl.ds(beside_ref.shape[0] - (count - i) * HOURS, HOURS), :]
            stack_ref[pl.ds(top, HOURS), here] = last_ref[:, here] + beside


def plane_rows(first, metas, values, before):
    rows = values[0].shape[1]
    slots = metas[0].shape[1]
    args = [first, *metas, *values, *before]
    shapes = [(HOURS, slots), (slots // rows * HOURS, rows)]
    if before:
        shapes.append(((len(before) - 1) * HOURS, slots))
    return pl.pallas_call(
        plane_rows_kernel,
        in_specs=[pl.BlockSpec(memory_space=pltpu.SMEM)]
        + [pl.BlockSpec(memory_space=pltpu.VMEM)] * (len(args) - 1),
        out_shape=[jax.ShapeDtypeStruct(shape, F32) for shape in shapes],
        compiler_params=params(),
        name="plane_rows",
        cost_estimate=pl.CostEstimate(flops=1_000_000_000, bytes_accessed=2_000_000, transcendentals=0),
    )(*args)


def gain(kernels):
    return jnp.max(jnp.sum(kernels, axis=1, keepdims=True), axis=0, keepdims=True)


def spectra(kind, kernels, wide):
    classes = kernels.shape[0]
    row = lax.broadcasted_iota(jnp.int32, (classes, kind.shape[1]), 0).astype(F32)
    hot = jnp.where(row == kind, 1.0, 0.0).astype(BF16)
    taps = jnp.transpose(kernels / gain(kernels))
    chosen = dot(jnp.concatenate(pieces(taps, 3)[::-1], axis=1), jnp.concatenate([hot] * 3, axis=0))
    return product(wide, chosen, 3)


def plane_spectrum_kernel(class_ref, kernels_ref, wide_ref, out_ref):
    kind = class_ref[1:2, : out_ref.shape[1]]
    out_ref[...] = spectra(kind, kernels_ref[...], wide_ref[...])


def plane_spectrum(meta, kernels, wide, rows):
    return pl.pallas_call(
        plane_spectrum_kernel,
        out_shape=jax.ShapeDtypeStruct((SPAN, rows), F32),
        compiler_params=params(),
        name="plane_spectrum",
        cost_estimate=SMALL,
    )(meta, kernels, wide)


def sides(even, pair, middle):
    return jnp.where(even, middle, pair), jnp.where(even, pair, middle)


def plane_call(kernel, name, shapes, flags, args):
    return pl.pallas_call(
        kernel,
        in_specs=[pl.BlockSpec(memory_space=pltpu.SMEM)] * len(flags)
        + [pl.BlockSpec(memory_space=pltpu.VMEM)] * len(args),
        out_shape=[jax.ShapeDtypeStruct(shape, F32) for shape in shapes],
        compiler_params=params(),
        name=name,
        cost_estimate=SMALL,
    )(*flags, *args)


def plane_first_kernel(
    flag_ref, here_ref, pair_ref, middle_ref, seen_ref, spec_ref, kernels_ref, forward, first, last, out_ref
):
    spec = spec_ref[...]
    before, after = sides(flag_ref[0] > 0.5, pair_ref[...], middle_ref[...])
    now, later = plane_delayed(before, here_ref[...], after, spec, forward[...], last[...], 3)
    known = plane_advanced(now, later * flag_ref[1], spec, forward[...], first[...], 3)
    out_ref[...] = seen_ref[...] - known * gain(kernels_ref[...])


def plane_delay_kernel(flag_ref, here_ref, pair_ref, middle_ref, spec_ref, forward, last, out_ref):
    body = pl.ds(0, HOURS)
    before, after = sides(flag_ref[0] > 0.5, pair_ref[body, :], middle_ref[body, :])
    out = plane_delayed(before, here_ref[body, :], after, spec_ref[...], forward[...], last[...], 2)
    for i in range(2):
        out_ref[pl.ds(i * HOURS, HOURS), :] = out[i]


def write_note(ref, rows):
    tail = [jnp.zeros((NOTE - len(rows), ref.shape[1]), F32)]
    ref[pl.ds(HOURS, NOTE), :] = jnp.concatenate(rows + tail, axis=0)


def plane_open_kernel(
    flag_ref, here_ref, pair_ref, middle_ref, pulled_ref, spec_ref, forward, first, last, out_ref, delayed_ref
):
    here = here_ref[...]
    spec = spec_ref[...]
    before, after = sides(flag_ref[0] > 0.5, pair_ref[...], middle_ref[...])
    now, later = plane_delayed(before, here, after, spec, forward[...], last[...], 2)
    out_ref[pl.ds(0, HOURS), :] = plane_advanced(now, later * flag_ref[1], spec, forward[...], first[...], 2)
    write_note(out_ref, [lanes(pulled_ref[...], here), lanes(now, now)])
    delayed_ref[pl.ds(0, HOURS), :] = now
    delayed_ref[pl.ds(HOURS, HOURS), :] = later


def plane_step_kernel(
    flag_ref,
    here_ref,
    pair_ref,
    two_ref,
    mirror_ref,
    pulled_ref,
    delayed_ref,
    old_z_ref,
    old_s_ref,
    old_delayed_ref,
    spec_ref,
    forward,
    first,
    total_ref,
    out_ref,
    kept_ref,
):
    tail, body = pl.ds(HOURS, NOTE), pl.ds(0, HOURS)
    total_ref[...] = (here_ref[tail, :] + pair_ref[tail, :]) + (two_ref[...] + mirror_ref[...])
    inverse = total(total_ref, 0) / total(total_ref, 1)
    z = pulled_ref[body, :] * inverse - old_z_ref[...]
    s = here_ref[body, :] * inverse - old_s_ref[...]
    both = delayed_ref[...] * inverse - old_delayed_ref[...]
    now, later = both[:HOURS], both[HOURS:]
    following = plane_advanced(now, later * flag_ref[1], spec_ref[...], forward[...], first[...], 2)
    out_ref[body, :] = following * inverse
    write_note(out_ref, [lanes(z, s), lanes(now, now)])
    for i, value in enumerate((z, s, now)):
        kept_ref[pl.ds(i * HOURS, HOURS), :] = value


def plane_close_kernel(
    here_ref, before_ref, pulled_ref, kept_ref, old_z_ref, old_s_ref, old_delayed_ref, spec_ref, forward, last, out_ref
):
    body = pl.ds(0, HOURS)
    here, raw = here_ref[body, :], pulled_ref[body, :]
    waves = product(forward[...], jnp.concatenate([before_ref[body, :], here], axis=0), 2)
    now = product(last[...], turn(waves, spec_ref[...], 1.0), 2)
    z, s, delayed = (kept_ref[pl.ds(i * HOURS, HOURS), :] for i in range(3))
    note = [pulled_ref[HOURS + i : HOURS + i + 1, :] for i in range(2)]
    for left in (raw, z, old_z_ref[...]):
        note += [lanes(left, right) for right in (here, s, old_s_ref[...])]
    parts = (now, delayed, old_delayed_ref[body, :])
    for i in range(3):
        note += [lanes(parts[i], parts[j]) for j in range(i, 3)]
    note.append(jnp.zeros((24 - len(note), here.shape[1]), F32))
    note = jnp.sum(jnp.concatenate(note, axis=0), axis=1, keepdims=True)
    shape = (24, out_ref.shape[2])
    row, col = (lax.broadcasted_iota(jnp.int32, shape, i) for i in range(2))
    note = jnp.sum(jnp.where(row == col, jnp.broadcast_to(note, shape), 0.0), axis=0, keepdims=True)
    out_ref[...] = jnp.broadcast_to(note[None], out_ref.shape)


def plane_weights(open_ref, close, scale):
    entry = lambda i: close[:, i : i + 1]
    n1, t1 = total(open_ref, 0), total(open_ref, 1)
    n2, t2 = entry(0), entry(1)
    a1 = t1 / n1
    a2, r2 = (t2 / n2) / a1, n2 / n1
    plain = (1.0, -a2, -r2)
    n3 = sum(plain[i] * plain[j] * entry(2 + 3 * i + j) for i in range(3) for j in range(3))
    pairs = [(i, j) for i in range(3) for j in range(i, 3)]
    t3 = sum(
        plain[i] * plain[j] * entry(11 + n) * (1.0 if i == j else 2.0) for n, (i, j) in enumerate(pairs)
    )
    a3, r3 = (t3 / n3) / a1, n3 / n2
    unit = 1.0 / (a1 * scale)
    c3 = unit / (a3 * (a2 - r2) - r3)
    c2 = -a3 * c3
    c1 = unit - r2 * c2
    step = c2 - c3 * a2
    return c1 - step - c3 * r2, step / a1, c3


def plane_combine_kernel(open_ref, close_ref, kernels_ref, stack_ref, mine_ref, beside_ref, out_ref):
    rows = open_ref.shape[1]
    close = jnp.sum(close_ref[...], axis=0)[0:1, :]
    e0, e1, e2 = plane_weights(open_ref, close, gain(kernels_ref[...]))
    for i in range(out_ref.shape[0] // rows):
        here = pl.ds(i * rows, rows)
        last = mine_ref[:, here] + beside_ref[pl.ds(i * HOURS, HOURS), :]
        value = stack_ref[pl.ds(0, HOURS), here] * e0 + stack_ref[pl.ds(HOURS, HOURS), here] * e1 + last * e2
        out_ref[here, :] = jnp.transpose(value)


def plane_finish_kernel(rows_ref, inc_ref, field_ref, out_ref):
    blocks, slots, width = inc_ref.shape
    weights = inc_ref[...].astype(F32).astype(BF16)
    for b in range(blocks):
        here = pl.ds(b * width, width)
        rows = jnp.concatenate(pieces(rows_ref[pl.ds(b * slots, slots), :], 2), axis=0)
        twice = jnp.concatenate([weights[b]] * 2, axis=0)
        added = lax.dot_general(twice, rows, (((0,), (0,)), ((), ())), preferred_element_type=F32)
        out_ref[here, :] = field_ref[here, :] + added


def plane_finish(rows, incidence, field):
    blocks, slots, width = incidence.shape
    hours = field.shape[1]
    step = 8
    return pl.pallas_call(
        plane_finish_kernel,
        grid=(blocks // step,),
        in_specs=[
            pl.BlockSpec((step * slots, hours), lambda i: (i, 0)),
            pl.BlockSpec((step, slots, width), lambda i: (i, 0, 0)),
            pl.BlockSpec((step * width, hours), lambda i: (i, 0)),
        ],
        out_specs=pl.BlockSpec((step * width, hours), lambda i: (i, 0)),
        out_shape=jax.ShapeDtypeStruct(field.shape, F32),
        compiler_params=params(),
        name="plane_finish",
    )(rows, incidence, field)


def plane_shards(incidence, row_gauge, gauge_kernel, kernels, observed, first_guess):
    rows, hours = observed.shape
    basin, tm = lax.axis_index("basin"), lax.axis_index("tm")
    z, x, y, c = basin // X_, basin % X_, tm // C_, tm % C_
    place = 2 * y + x
    first = jnp.stack([4 * c + (place ^ m) for m in range(4)] + [4 * c + place, 4 * (1 - c) + place])
    first = (first * rows).astype(jnp.int32)
    flags = jnp.stack([1 - z % 2, (z < Z_ - 1).astype(z.dtype), (z > 0).astype(z.dtype)]).astype(F32)
    forward, inverse_first, inverse_last, _ = turned_transforms(2)
    forward3, inverse_first3, inverse_last3, short3 = turned_transforms(3)
    block, noted = (hours, rows), (hours + NOTE, rows)

    parcel = send(incidence, first_guess, row_gauge, gauge_kernel)
    parcel, near, gauges, kinds, seen = lax.optimization_barrier(
        (parcel, incidence, row_gauge, gauge_kernel, observed)
    )
    parcel = moved(parcel, to_plane)
    seen = observe(seen, moved(seen, hour_before), kinds, kernels, short3, [forward3, inverse_first3])
    seen, near = lax.optimization_barrier((seen, near))
    seen = moved(seen, to_plane)
    meta = describe(near, gauges)
    meta = jnp.concatenate([meta, moved(meta, over_x)], axis=1)
    meta = jnp.concatenate([meta, moved(meta, z_pair)], axis=1)
    parcel, seen = lax.optimization_barrier((parcel, seen))
    parcels = [parcel, moved(parcel, over_core)]
    spec = plane_spectrum(parcel[hours:], kernels, short3, rows)
    parcels[1], seen, meta, spec = lax.optimization_barrier((parcels[1], seen, meta, spec))
    around = [meta, moved(meta, z_two)]
    dense = spread(first, parcels, rows)
    metas = [value[hours:] for value in parcels]
    sums = dense[0] + sum(moved(value, where) for value, where in zip(dense[1:], SQUARE))
    sums = [sums, moved(sums, z_pair), moved(sums, z_middle)]
    coupled = plane_couple(first, around[0], rows)
    coupled, sums = lax.optimization_barrier((coupled, sums))
    coupling = plane_couple(first, around[1], rows, coupled)
    (pulled0,) = plane_call(
        plane_first_kernel,
        "plane_first",
        [block],
        [flags],
        [*sums, seen, spec, kernels, forward3, inverse_first3, inverse_last3],
    )

    def mixing(pulled, extra):
        values = [pulled] + [moved(pulled, where) for where in SQUARE]
        mine, other = plane_mix(coupling, values, extra)
        beside = moved(other, over_core)
        return values, mine + beside[: pulled.shape[0]], beside

    values, mixed0, _ = mixing(pulled0, [])
    picked, theirs = plane_rows(first, metas, values, [])
    sums = [mixed0, moved(mixed0, z_pair), moved(mixed0, z_middle)]
    pulled1, delayed0 = plane_call(
        plane_open_kernel,
        "plane_open",
        [noted, (2 * hours, rows)],
        [flags],
        [*sums, pulled0, spec, forward, inverse_first, inverse_last],
    )

    values, mixed1, beside = mixing(pulled1, [theirs])
    picked, theirs, stack = plane_rows(first, metas, values, [picked, beside])
    sums = [mixed1, moved(mixed1, z_pair), moved(mixed1, z_middle)]
    two, mirror = moved(mixed1[hours:], z_two), moved(mixed1[hours:], z_mirror)
    (delayed1,) = plane_call(
        plane_delay_kernel, "plane_delay", [(2 * hours, rows)], [flags], [*sums, spec, forward, inverse_last]
    )
    open_note, pulled2, kept = plane_call(
        plane_step_kernel,
        "plane_step",
        [(NOTE, rows), noted, (3 * hours, rows)],
        [flags],
        [*sums[:2], two, mirror, pulled1, delayed1, pulled0, mixed0, delayed0, spec, forward, inverse_first],
    )

    values, mixed2, beside = mixing(pulled2, [theirs])
    picked, theirs, stack = plane_rows(first, metas, values, [stack, picked, beside])
    (note,) = plane_call(
        plane_close_kernel,
        "plane_close",
        [(Z_ * X_ * Y_ * C_, 8, rows // 2)],
        [],
        [mixed2, moved(mixed2, z_next), pulled2, kept, pulled0, mixed0, delayed0, spec, forward, inverse_last],
    )
    close_note = lax.all_to_all(note, ("basin", "tm"), 0, 0, tiled=False)
    (answer,) = plane_call(
        plane_combine_kernel,
        "plane_combine",
        [(parcel.shape[1], hours)],
        [],
        [open_note, close_note, kernels, stack, picked, moved(theirs, over_core)],
    )
    return plane_finish(moved(answer, from_plane), incidence, first_guess)


def solution(mesh):
    planes = dict(mesh.shape) == {"basin": Z_ * X_, "tm": Y_ * C_}
    in_specs = (
        P("basin", None, None),
        P("basin"),
        P("basin"),
        P(),
        P("basin", "tm"),
        P("basin", "tm"),
    )
    return jax.shard_map(
        plane_shards if planes else shards, mesh=mesh, in_specs=in_specs, out_specs=P("basin", "tm"), check_vma=False
    )
```

```python
import functools

import jax
import jax.numpy as jnp
import numpy as np
from jax import lax
from jax.experimental import pallas as pl
from jax.experimental.pallas import tpu as pltpu
from jax.sharding import PartitionSpec as P

F32 = jnp.float32
BF16 = jnp.bfloat16
HIGH = lax.Precision.HIGHEST
SPAN = 256
MIB = 1024 * 1024


SMALL = pl.CostEstimate(flops=1, bytes_accessed=1, transcendentals=0)


def params(mib=16):
    return pltpu.CompilerParams(vmem_limit_bytes=mib * MIB)


def transforms():
    half = SPAN // 2
    freq = 2.0 * np.pi * (np.arange(half) + 0.5) / SPAN
    phase = np.arange(SPAN)[:, None] * freq[None, :]
    forward = np.concatenate([np.cos(phase), -np.sin(phase)], axis=1)
    inverse = forward.T * (2.0 / SPAN)
    return (
        jnp.asarray(forward, F32),
        jnp.asarray(inverse[:, :half], F32),
        jnp.asarray(inverse[:, half:], F32),
    )


def dot(a, b):
    return jnp.dot(a, b, preferred_element_type=F32)


def exact(a, b):
    return jnp.dot(a, b, precision=HIGH, preferred_element_type=F32)


def pieces(value, count):
    out = []
    for _ in range(count):
        piece = value.astype(BF16)
        out.append(piece)
        value = value - piece.astype(F32)
    return out


def pick(hot, value):
    return sum(dot(hot, piece) for piece in pieces(value, 3))


def prepare_kernel(inc_ref, field_ref, partial_ref, gram_ref):
    blocks, slots, width = inc_ref.shape
    rows = blocks * slots
    weights = inc_ref[...].astype(F32).astype(BF16)
    for b in range(blocks):
        value = field_ref[pl.ds(b * width, width), :]
        partial_ref[pl.ds(b * slots, slots), :] = pick(weights[b], value)
    flat = weights.reshape(rows, width)
    full = lax.dot_general(flat, flat, (((1,), (1,)), ((), ())), preferred_element_type=F32)
    row = lax.broadcasted_iota(jnp.int32, (rows, rows), 0)
    col = lax.broadcasted_iota(jnp.int32, (rows, rows), 1)
    own = jnp.where(row // slots == col // slots, full, 0.0)
    gram_ref[...] = jnp.sum(own.reshape(blocks, slots, rows), axis=0)


def prepare(incidence, field):
    blocks, slots, width = incidence.shape
    hours = field.shape[1]
    step = 8
    return pl.pallas_call(
        prepare_kernel,
        grid=(blocks // step,),
        in_specs=[
            pl.BlockSpec((step, slots, width), lambda i: (i, 0, 0)),
            pl.BlockSpec((step * width, hours), lambda i: (i, 0)),
        ],
        out_specs=[
            pl.BlockSpec((step * slots, hours), lambda i: (i, 0)),
            pl.BlockSpec((slots, step * slots), lambda i: (0, i)),
        ],
        out_shape=[
            jax.ShapeDtypeStruct((blocks * slots, hours), F32),
            jax.ShapeDtypeStruct((slots, blocks * slots), F32),
        ],
        compiler_params=params(56),
        name="prepare",
    )(incidence, field)


def table_kernel(gauge_ref, partial_ref, out_ref):
    slots = partial_ref.shape[0]
    rows = out_ref.shape[0]
    first = pl.program_id(0) * rows
    gauge = lax.broadcasted_iota(jnp.int32, (rows, slots), 0) + first
    hot = jnp.where(gauge_ref[...] == gauge, 1.0, 0.0).astype(BF16)
    out_ref[...] = pick(hot, partial_ref[...])


def table(row_gauge, partial, gauges):
    slots, hours = partial.shape
    step = 256
    return pl.pallas_call(
        table_kernel,
        grid=(gauges // step,),
        in_specs=[
            pl.BlockSpec((1, slots), lambda i: (0, 0)),
            pl.BlockSpec((slots, hours), lambda i: (0, 0)),
        ],
        out_specs=pl.BlockSpec((step, hours), lambda i: (i, 0)),
        out_shape=jax.ShapeDtypeStruct((gauges, hours), F32),
        compiler_params=params(56),
        name="table",
    )(row_gauge.reshape(1, slots), partial)


def couple_kernel(first_ref, lane_ref, sub_ref, gram_ref, high_ref, low_ref, near_ref):
    slots = gram_ref.shape[0]
    count = lane_ref.shape[1]
    rows, cols = high_ref.shape
    tile = 256
    first = first_ref[0]

    @pl.when(pl.program_id(0) == 0)
    def _():
        row = lax.broadcasted_iota(jnp.int32, (tile, tile), 0)
        col = lax.broadcasted_iota(jnp.int32, (tile, tile), 1)
        same = row // slots == col // slots
        mine = lax.broadcasted_iota(jnp.int32, (rows, tile), 0) + first

        def body(i, carry):
            here = pl.ds(pl.multiple_of(i * tile, tile), tile)
            block = jnp.concatenate([gram_ref[:, here]] * (tile // slots), axis=0)
            block = jnp.where(same, block, 0.0).astype(BF16)
            hot = jnp.where(lane_ref[:, here] == mine, 1.0, 0.0).astype(BF16)
            near_ref[:, here] = dot(hot, block)
            return carry

        lax.fori_loop(0, count // tile, body, 0)

    def chunk(i, total):
        here = pl.ds(pl.multiple_of(i * 1024, 1024), 1024)
        gauge = lax.broadcasted_iota(jnp.int32, (1024, cols), 1) + pl.program_id(0) * cols
        hot = jnp.where(sub_ref[here, :] == gauge, 1.0, 0.0).astype(BF16)
        near = near_ref[:, here]
        high = near.astype(BF16)
        low = (near - high.astype(F32)).astype(BF16)
        return total + dot(high, hot) + dot(low, hot)

    total = lax.fori_loop(0, count // 1024, chunk, jnp.zeros((rows, cols), F32))
    high, low = pieces(total, 2)
    high_ref[...] = high
    low_ref[...] = low


def couple(first, row_gauge, gram, rows, gauges):
    count = row_gauge.shape[0]
    step = 256
    return pl.pallas_call(
        couple_kernel,
        grid=(gauges // step,),
        in_specs=[
            pl.BlockSpec(memory_space=pltpu.SMEM),
            pl.BlockSpec((1, count), lambda i: (0, 0)),
            pl.BlockSpec((count, 1), lambda i: (0, 0)),
            pl.BlockSpec(gram.shape, lambda i: (0, 0)),
        ],
        out_specs=[pl.BlockSpec((rows, step), lambda i: (0, i))] * 2,
        out_shape=[jax.ShapeDtypeStruct((rows, gauges), BF16)] * 2,
        scratch_shapes=[pltpu.VMEM((rows, count), F32)],
        compiler_params=params(56),
        name="couple",
    )(first, row_gauge.reshape(1, count), row_gauge.reshape(count, 1), gram)


def mix_kernel(high_ref, low_ref, value_ref, out_ref):
    high = high_ref[...]
    low = low_ref[...]
    one, two, three = pieces(value_ref[...], 3)
    out_ref[...] = (dot(high, three) + dot(low, two)) + (dot(high, two) + dot(low, one)) + dot(high, one)


def mix(high, low, value):
    return pl.pallas_call(
        mix_kernel,
        out_shape=jax.ShapeDtypeStruct((high.shape[0], value.shape[1]), F32),
        compiler_params=params(56),
        name="mix",
    )(high, low, value)


def spectrum_kernel(class_ref, kernels_ref, forward_ref, out_ref):
    rows = class_ref.shape[0]
    classes, taps = kernels_ref.shape
    kind = lax.broadcasted_iota(jnp.int32, (rows, classes), 1)
    hot = jnp.where(class_ref[...] == kind, 1.0, 0.0)
    out_ref[...] = exact(exact(hot, kernels_ref[...]), forward_ref[pl.ds(0, taps), :])


def spectrum(gauge_kernel, kernels, forward):
    rows = gauge_kernel.shape[0]
    return pl.pallas_call(
        spectrum_kernel,
        out_shape=jax.ShapeDtypeStruct((rows, SPAN), F32),
        compiler_params=params(56),
        name="spectrum",
    )(gauge_kernel.reshape(rows, 1), kernels, forward)


def delayed(before, here, after, spec, forward, inverse_last):
    rows, half = here.shape
    stacked = jnp.concatenate(
        [jnp.concatenate([before, here], axis=1), jnp.concatenate([here, after], axis=1)], axis=0
    )
    waves = exact(stacked, forward)
    real, imag = waves[:, :half], waves[:, half:]
    kr = jnp.concatenate([spec[:, :half]] * 2, axis=0)
    ki = jnp.concatenate([spec[:, half:]] * 2, axis=0)
    turned = jnp.concatenate([real * kr - imag * ki, real * ki + imag * kr], axis=1)
    out = exact(turned, inverse_last)
    return out[:rows], out[rows:]


def advanced(here, after, spec, forward, inverse_first):
    half = here.shape[1]
    waves = exact(jnp.concatenate([here, after], axis=1), forward)
    real, imag = waves[:, :half], waves[:, half:]
    kr, ki = spec[:, :half], spec[:, half:]
    turned = jnp.concatenate([real * kr + imag * ki, imag * kr - real * ki], axis=1)
    return exact(turned, inverse_first)


def lanes(a, b):
    return jnp.sum(a * b, axis=0, keepdims=True)


def total(ref, row):
    return jnp.sum(ref[row : row + 1, :], axis=1, keepdims=True)


def ratios(ref):
    square = total(ref, 0)
    alpha = jnp.sqrt(square)
    beta = jnp.sqrt(jnp.maximum(total(ref, 1) / square - 2.0 * total(ref, 2) + square, 0.0))
    return alpha, beta


def first_kernel(
    more_ref, sums_ref, observed_ref, spec_ref, forward_ref, first_ref, last_ref, out_ref, note_ref
):
    rows, half = observed_ref.shape[0] // 2, observed_ref.shape[1]
    spec, forward = spec_ref[...], forward_ref[...]
    before, here, after = (sums_ref[pl.ds(i * rows, rows), :] for i in range(3))
    now, later = delayed(before, here, after, spec, forward, last_ref[...])
    start = observed_ref[pl.ds(0, rows), :] - now
    start_later = (observed_ref[pl.ds(rows, rows), :] - later) * more_ref[0]
    out_ref[...] = advanced(start, start_later, spec, forward, first_ref[...])
    note_ref[...] = jnp.concatenate([lanes(start, start), jnp.zeros((7, half), F32)], axis=0)


def first_step(more, sums, observed, spec, mats):
    rows, half = spec.shape[0], observed.shape[1]
    return pl.pallas_call(
        first_kernel,
        in_specs=[pl.BlockSpec(memory_space=pltpu.SMEM)] + [pl.BlockSpec(memory_space=pltpu.VMEM)] * 6,
        out_shape=[jax.ShapeDtypeStruct((rows, half), F32), jax.ShapeDtypeStruct((8, half), F32)],
        compiler_params=params(56),
        name="first_step",
    )(more, sums, observed, spec, *mats)


def step_kernel(
    opening,
    final,
    more_ref,
    note_ref,
    sums_ref,
    spec_ref,
    forward_ref,
    first_ref,
    last_ref,
    pulled_ref,
    *refs,
):
    if opening:
        state_ref = None
    else:
        state_ref, *refs = refs
    if final:
        (out_note_ref,) = refs
    else:
        new_ref, out_ref, out_note_ref = refs
    rows, half = pulled_ref.shape
    spec, forward = spec_ref[...], forward_ref[...]
    if opening:
        scale = 1.0 / jnp.sqrt(total(note_ref, 0))
        along = sums_ref[...] * scale
        new_s, new_su = along, along
        new_zu = pulled_ref[...] * scale
        new_z = new_zu
    else:
        alpha, beta = ratios(note_ref)
        a, b, g = 1.0 / (alpha * beta), alpha / beta, beta / alpha
        wide = pl.ds(0, 3 * rows), pl.ds(3 * rows, 3 * rows)
        new_su = sums_ref[...] * a - state_ref[wide[1], :] * b
        new_s = new_su - state_ref[wide[0], :] * g
        new_zu = pulled_ref[...] * a - state_ref[pl.ds(7 * rows, rows), :] * b
        new_z = new_zu - state_ref[pl.ds(6 * rows, rows), :] * g
    before, here, after = (new_s[i * rows : (i + 1) * rows] for i in range(3))
    now, later = delayed(before, here, after, spec, forward, last_ref[...])
    out_note_ref[...] = jnp.concatenate(
        [lanes(new_z, here), lanes(now, now), lanes(new_zu, here), jnp.zeros((5, half), F32)], axis=0
    )
    if not final:
        new_ref[pl.ds(0, 3 * rows), :] = new_s
        new_ref[pl.ds(3 * rows, 3 * rows), :] = new_su
        new_ref[pl.ds(6 * rows, rows), :] = new_z
        new_ref[pl.ds(7 * rows, rows), :] = new_zu
        out_ref[...] = advanced(now, later * more_ref[0], spec, forward, first_ref[...])


def next_step(more, note, sums, spec, mats, pulled, state, final):
    rows, half = pulled.shape
    opening = state is None
    shapes = [
        jax.ShapeDtypeStruct((8 * rows, half), F32),
        jax.ShapeDtypeStruct((rows, half), F32),
        jax.ShapeDtypeStruct((8, half), F32),
    ]
    args = [more, note, sums, spec, *mats, pulled] + ([] if opening else [state])
    return pl.pallas_call(
        functools.partial(step_kernel, opening, final),
        in_specs=[pl.BlockSpec(memory_space=pltpu.SMEM)]
        + [pl.BlockSpec(memory_space=pltpu.VMEM)] * (len(args) - 1),
        out_shape=shapes[2:] if final else shapes,
        compiler_params=params(56),
        name="next_step",
    )(*args)


def weights_of(notes):
    start = jnp.sqrt(total(notes[0], 0))
    zero = jnp.zeros_like(start)
    units = [1.0 / start, zero, zero]
    z, zu = list(units), list(units)
    phibar = start
    alpha, beta = ratios(notes[1])
    rhobar = alpha
    w = [value / alpha for value in z]
    result = [zero] * 3
    steps = len(notes) - 1
    for k in range(steps):
        rho = jnp.sqrt(rhobar * rhobar + beta * beta)
        cosine, sine = rhobar / rho, beta / rho
        phi, phibar = cosine * phibar, sine * phibar
        result = [r + phi / rho * value for r, value in zip(result, w)]
        if k < steps - 1:
            a, b, g = 1.0 / (alpha * beta), alpha / beta, beta / alpha
            zu = [(a if i == k + 1 else 0.0) - b * value for i, value in enumerate(zu)]
            z = [value - g * old for value, old in zip(zu, z)]
            alpha, beta = ratios(notes[k + 2])
            theta = sine * alpha
            rhobar = -cosine * alpha
            w = [value / alpha - theta / rho * old for value, old in zip(z, w)]
    return result


def finish_kernel(n0, n1, n2, n3, gauge_ref, q0, q1, q2, inc_ref, field_ref, out_ref, rows_ref):
    blocks, slots, width = inc_ref.shape
    count = rows_ref.shape[0]
    gauges = q0.shape[0]
    step = pl.program_id(0)

    @pl.when(step == 0)
    def _():
        e0, e1, e2 = weights_of([n0, n1, n2, n3])
        width_ = 512

        def body(i, value):
            here = pl.ds(pl.multiple_of(i * width_, width_), width_)
            mixed = q0[here, :] * e0 + q1[here, :] * e1 + q2[here, :] * e2
            gauge = lax.broadcasted_iota(jnp.int32, (count, width_), 1) + i * width_
            hot = jnp.where(gauge_ref[...] == gauge, 1.0, 0.0).astype(BF16)
            return value + pick(hot, mixed)

        rows_ref[...] = lax.fori_loop(0, gauges // width_, body, jnp.zeros(rows_ref.shape, F32))

    weights = inc_ref[...].astype(F32).astype(BF16)
    for b in range(blocks):
        here = pl.ds(b * width, width)
        rows = rows_ref[pl.ds(pl.multiple_of((step * blocks + b) * slots, slots), slots), :]
        added = sum(
            lax.dot_general(weights[b], piece, (((0,), (0,)), ((), ())), preferred_element_type=F32)
            for piece in pieces(rows, 3)
        )
        out_ref[here, :] = field_ref[here, :] + added


def finish(notes, row_gauge, gathered, incidence, field):
    blocks, slots, width = incidence.shape
    hours = field.shape[1]
    count = row_gauge.shape[0]
    step = 8
    whole = lambda shape: pl.BlockSpec(shape, lambda i: (0, 0))
    return pl.pallas_call(
        finish_kernel,
        grid=(blocks // step,),
        in_specs=[whole(n.shape) for n in notes]
        + [whole((count, 1))]
        + [whole(q.shape) for q in gathered]
        + [
            pl.BlockSpec((step, slots, width), lambda i: (i, 0, 0)),
            pl.BlockSpec((step * width, hours), lambda i: (i, 0)),
        ],
        out_specs=pl.BlockSpec((step * width, hours), lambda i: (i, 0)),
        out_shape=jax.ShapeDtypeStruct(field.shape, F32),
        scratch_shapes=[pltpu.VMEM((count, hours), F32)],
        compiler_params=params(56),
        name="finish",
    )(*notes, row_gauge.reshape(count, 1), *gathered, incidence, field)


def shifted(value, axis, by):
    devices = lax.axis_size(axis)
    pairs = [(i, i + by) for i in range(devices) if 0 <= i + by < devices]
    return lax.ppermute(value, axis, pairs)


def window(value):
    return jnp.concatenate([shifted(value, "tm", 1), value, shifted(value, "tm", -1)], axis=0)


def gathered_rows(value):
    owners = lax.axis_size("basin")
    copies = jnp.broadcast_to(value[None], (owners,) + value.shape)
    return lax.all_to_all(copies, "basin", 0, 0, tiled=False)


def over_hours(note):
    blocks = lax.axis_size("tm")
    result = note
    for by in range(1, blocks):
        result = result + lax.ppermute(note, "tm", [(i, (i + by) % blocks) for i in range(blocks)])
    return result


def shards(incidence, row_gauge, gauge_kernel, kernels, observed, first_guess):
    owners = lax.axis_size("basin")
    rows, hours = observed.shape
    gauges = rows * owners
    mats = transforms()
    spec = spectrum(gauge_kernel, kernels, mats[0])
    more = (lax.axis_index("tm") < lax.axis_size("tm") - 1).astype(F32).reshape(1)
    partial, gram = prepare(incidence, first_guess)
    all_gram = lax.all_gather(gram, "basin", axis=1, tiled=True)
    all_rows = lax.all_gather(row_gauge, "basin", axis=0, tiled=True)
    dense = table(row_gauge, partial, gauges).reshape(owners, rows, hours)
    sums = jnp.sum(lax.all_to_all(dense, "basin", 0, 0, tiled=False), axis=0)
    both = jnp.concatenate([observed, shifted(observed, "tm", -1)], axis=0)
    first = (lax.axis_index("basin") * rows).astype(jnp.int32).reshape(1)
    high, low = couple(first, all_rows, all_gram, rows, gauges)

    pulled, note = first_step(more, window(sums), both, spec, mats)
    notes, kept, state = [], [], None
    for k in range(3):
        everyone = gathered_rows(jnp.concatenate([pulled, note], axis=0))
        value = everyone[:, :rows].reshape(gauges, hours)
        notes.append(over_hours(jnp.sum(everyone[:, rows:], axis=0)))
        kept.append(value)
        around = window(mix(high, low, value))
        final = k == 2
        result = next_step(more, notes[-1], around, spec, mats, pulled, state, final)
        if final:
            (note,) = result
        else:
            state, pulled, note = result
    notes.append(over_hours(jnp.sum(gathered_rows(note), axis=0)))
    return finish(notes, row_gauge, kept, incidence, first_guess)


Z_, X_, Y_, C_ = 4, 2, 2, 2
NOTE = 8
HOURS = SPAN // 2


def device(z, x, y, c):
    return (z * X_ + x) * (Y_ * C_) + y * C_ + c


def moved(value, where):
    pairs = []
    for z, x, y, c in np.ndindex(Z_, X_, Y_, C_):
        target = where(z, x, y, c)
        if target is not None:
            pairs.append((device(z, x, y, c), device(*target)))
    return lax.ppermute(value, ("basin", "tm"), pairs)


def to_plane(z, x, y, c):
    return 2 * y + c, x, z & 1, z >> 1


def hour_before(z, x, y, c):
    t = 2 * y + c - 1
    return (z, x, t >> 1, t & 1) if t >= 0 else None


def from_plane(z, x, y, c):
    return 2 * c + y, x, z >> 1, z & 1


def over_x(z, x, y, c):
    return z, 1 - x, y, c


def over_y(z, x, y, c):
    return z, x, 1 - y, c


def over_xy(z, x, y, c):
    return z, 1 - x, 1 - y, c


def over_core(z, x, y, c):
    return z, x, y, 1 - c


def z_pair(z, x, y, c):
    return z ^ 1, x, y, c


def z_middle(z, x, y, c):
    return (3 - z, x, y, c) if z in (1, 2) else None


def z_two(z, x, y, c):
    return z ^ 2, x, y, c


def z_mirror(z, x, y, c):
    return 3 - z, x, y, c


def z_next(z, x, y, c):
    return (z + 1, x, y, c) if z < 3 else None


SQUARE = (over_x, over_y, over_xy)


def split_constant(value):
    out = []
    for _ in range(3):
        piece = value.astype(jnp.bfloat16)
        out.append(piece)
        value = value - piece.astype(np.float64)
    return out


ORDERS = {2: ((0, 1), (1, 0), (0, 0)), 3: ((0, 2), (1, 1), (2, 0), (0, 1), (1, 0), (0, 0))}


def widened(mat, order):
    parts = split_constant(mat)
    return jnp.asarray(np.concatenate([parts[i] for i, _ in ORDERS[order]], axis=1))


def product(wide, value, order):
    parts = pieces(value, order)
    return dot(wide, jnp.concatenate([parts[j] for _, j in ORDERS[order]], axis=0))


def turned_transforms(order):
    half = SPAN // 2
    freq = 2.0 * np.pi * (np.arange(half) + 0.5) / SPAN
    phase = freq[:, None] * np.arange(SPAN)[None, :]
    forward = np.concatenate([np.cos(phase), -np.sin(phase)], axis=0)
    inverse = forward.T * (2.0 / SPAN)
    return [widened(mat, order) for mat in (forward, inverse[:half], inverse[half:], forward[:, :half])]


def turn(waves, spec, sign):
    half = waves.shape[0] // 2
    real, imag = waves[:half], waves[half:]
    kr, ki = spec[:half], spec[half:] * sign
    return jnp.concatenate([real * kr - imag * ki, real * ki + imag * kr], axis=0)


def plane_delayed(before, here, after, spec, forward, last, order):
    rows = here.shape[1]
    pairs = [jnp.concatenate(pair, axis=0) for pair in ((before, here), (here, after))]
    waves = product(forward, jnp.concatenate(pairs, axis=1), order)
    turned = [turn(waves[:, i * rows : (i + 1) * rows], spec, 1.0) for i in range(2)]
    out = product(last, jnp.concatenate(turned, axis=1), order)
    return out[:, :rows], out[:, rows:]


def plane_advanced(here, after, spec, forward, first, order):
    waves = product(forward, jnp.concatenate([here, after], axis=0), order)
    return product(first, turn(waves, spec, -1.0), order)


def describe_kernel(inc_ref, gauge_ref, out_ref):
    blocks, slots, width = inc_ref.shape
    tile = 8
    side = tile * slots
    weights = inc_ref[...].astype(F32).astype(BF16)
    row = lax.broadcasted_iota(jnp.int32, (side, side), 0)
    col = lax.broadcasted_iota(jnp.int32, (side, side), 1)
    same = row // slots == col // slots
    for i in range(blocks // tile):
        flat = weights[i * tile : (i + 1) * tile].reshape(side, width)
        full = lax.dot_general(flat, flat, (((1,), (1,)), ((), ())), preferred_element_type=F32)
        own = jnp.where(same, full, 0.0)
        out_ref[pl.ds(0, slots), pl.ds(i * side, side)] = jnp.sum(own.reshape(tile, slots, side), axis=0)
    out_ref[pl.ds(slots, 8), :] = jnp.broadcast_to(gauge_ref[...].astype(F32), (8, blocks * slots))


def describe(incidence, row_gauge):
    blocks, slots, _ = incidence.shape
    count = blocks * slots
    return pl.pallas_call(
        describe_kernel,
        out_shape=jax.ShapeDtypeStruct((slots + 8, count), F32),
        compiler_params=params(),
        name="describe",
        cost_estimate=SMALL,
    )(incidence, row_gauge.reshape(1, count))


def observe_kernel(seen_ref, later_ref, kind_ref, kernels_ref, wide_ref, forward, first, out_ref):
    spec = spectra(kind_ref[...].astype(F32), kernels_ref[...], wide_ref[...])
    here, after = jnp.transpose(seen_ref[...]), jnp.transpose(later_ref[...])
    out_ref[...] = plane_advanced(here, after, spec, forward[...], first[...], 3)


def observe(seen, later, gauge_kernel, kernels, wide, mats):
    rows, hours = seen.shape
    return pl.pallas_call(
        observe_kernel,
        out_shape=jax.ShapeDtypeStruct((hours, rows), F32),
        compiler_params=params(),
        name="observe",
        cost_estimate=SMALL,
    )(seen, later, gauge_kernel.reshape(1, rows), kernels, wide, *mats)


def send_kernel(inc_ref, field_ref, gauge_ref, kind_ref, out_ref):
    blocks, slots, width = inc_ref.shape
    count = blocks * slots
    weights = inc_ref[...].astype(F32).astype(BF16)
    parts = []
    for b in range(blocks):
        value = jnp.concatenate(pieces(field_ref[pl.ds(b * width, width), :], 3)[::-1], axis=0)
        parts.append(dot(jnp.concatenate([weights[b]] * 3, axis=1), value))
    out_ref[pl.ds(0, HOURS), :] = jnp.transpose(jnp.concatenate(parts, axis=0))
    kinds = kind_ref.shape[1] // count
    here = jnp.minimum(pl.program_id(0), kinds - 1) * count
    out_ref[pl.ds(HOURS, 8), :] = jnp.concatenate(
        [
            gauge_ref[...].astype(F32),
            kind_ref[:, pl.ds(pl.multiple_of(here, count), count)].astype(F32),
            jnp.zeros((6, count), F32),
        ],
        axis=0,
    )


def send(incidence, field, row_gauge, gauge_kernel):
    blocks, slots, width = incidence.shape
    count = blocks * slots
    rows = gauge_kernel.shape[0]
    step = 8
    return pl.pallas_call(
        send_kernel,
        grid=(blocks // step,),
        in_specs=[
            pl.BlockSpec((step, slots, width), lambda i: (i, 0, 0)),
            pl.BlockSpec((step * width, HOURS), lambda i: (i, 0)),
            pl.BlockSpec((1, step * slots), lambda i: (0, i)),
            pl.BlockSpec((1, rows), lambda i: (0, 0)),
        ],
        out_specs=pl.BlockSpec((HOURS + 8, step * slots), lambda i: (0, i)),
        out_shape=jax.ShapeDtypeStruct((HOURS + 8, count), F32),
        compiler_params=params(),
        name="send",
        cost_estimate=SMALL,
    )(incidence, field, row_gauge.reshape(1, count), gauge_kernel.reshape(1, rows))


def hot_rows(gauge, first, rows):
    mine = (lax.broadcasted_iota(jnp.int32, (rows, gauge.shape[1]), 0) + first).astype(F32)
    return jnp.where(gauge == mine, 1.0, 0.0).astype(BF16)


def spread_kernel(first_ref, mine_ref, other_ref, *out_refs):
    rows = out_refs[0].shape[1]
    both = jnp.concatenate([mine_ref[...], other_ref[...]], axis=1)
    stacked = jnp.concatenate(pieces(both[:HOURS], 3), axis=0)
    for m, out_ref in enumerate(out_refs):
        hot = hot_rows(both[HOURS : HOURS + 1], first_ref[m], rows)
        result = lax.dot_general(stacked, hot, (((1,), (1,)), ((), ())), preferred_element_type=F32)
        out_ref[...] = (result[2 * HOURS :] + result[HOURS : 2 * HOURS]) + result[:HOURS]


def spread(first, parcels, rows):
    return pl.pallas_call(
        spread_kernel,
        in_specs=[pl.BlockSpec(memory_space=pltpu.SMEM)] + [pl.BlockSpec(memory_space=pltpu.VMEM)] * 2,
        out_shape=[jax.ShapeDtypeStruct((HOURS, rows), F32)] * 4,
        compiler_params=params(),
        name="spread",
        cost_estimate=SMALL,
    )(first, *parcels)


def plane_couple_kernel(last, first_ref, *refs):
    if last:
        all_ref, before_ref, high_ref, low_ref, total_ref, meta_ref = refs
        total_ref[...] = before_ref[...]
    else:
        all_ref, total_ref, meta_ref = refs
        total_ref[...] = jnp.zeros_like(total_ref)
    parts, height, count = meta_ref.shape
    slots = height - 8
    cols, rows = total_ref.shape
    tile = 256
    for i in range(parts):
        meta_ref[i] = all_ref[:, i * count : (i + 1) * count]
    row = lax.broadcasted_iota(jnp.int32, (tile, tile), 0)
    col = lax.broadcasted_iota(jnp.int32, (tile, tile), 1)
    same = row // slots == col // slots

    def body(i, carry):
        gauge = meta_ref[i, slots : slots + 1, :]
        near = []
        for j in range(count // tile):
            here = slice(j * tile, (j + 1) * tile)
            block = jnp.concatenate([meta_ref[i, :slots, here]] * (tile // slots), axis=0)
            block = jnp.where(same, block, 0.0).astype(BF16)
            mine = jnp.concatenate(
                [hot_rows(gauge[:, here], first_ref[4 + h], rows // 2) for h in range(2)], axis=0
            )
            near.append(
                lax.dot_general(block, mine, (((1,), (1,)), ((), ())), preferred_element_type=F32)
            )
        near = jnp.concatenate(near, axis=0)
        high = near.astype(BF16)
        rest = near - high.astype(F32)
        hot = jnp.concatenate([hot_rows(gauge, first_ref[m], cols // 4) for m in range(4)], axis=0)
        total_ref[...] += dot(hot, high)

        @pl.when(jnp.max(jnp.abs(rest)) > 0.0)
        def _():
            total_ref[...] += dot(hot, rest.astype(BF16))

        return carry

    lax.fori_loop(0, parts, body, 0)
    if last:
        high, low = pieces(total_ref[...], 2)
        high_ref[...] = high
        low_ref[...] = low


def plane_couple(first, meta, rows, before=None):
    height, wide = meta.shape
    parts = 2 * X_
    shape = (4 * rows, 2 * rows)
    last = before is not None
    args = [first, meta] + ([before] if last else [])
    scratch = [pltpu.VMEM((parts, height, wide // parts), F32)]
    return pl.pallas_call(
        functools.partial(plane_couple_kernel, last),
        in_specs=[pl.BlockSpec(memory_space=pltpu.SMEM)]
        + [pl.BlockSpec(memory_space=pltpu.VMEM)] * (len(args) - 1),
        out_shape=[jax.ShapeDtypeStruct(shape, BF16)] * 2 if last else jax.ShapeDtypeStruct(shape, F32),
        scratch_shapes=([pltpu.VMEM(shape, F32)] if last else []) + scratch,
        compiler_params=params(),
        name="plane_couple",
        cost_estimate=pl.CostEstimate(
            flops=2 * 8 * wide * rows * rows, bytes_accessed=2_000_000, transcendentals=0
        ),
    )(*args)


def plane_mix_kernel(high_ref, low_ref, a_ref, b_ref, c_ref, d_ref, *refs):
    *extra, mine_ref, other_ref = refs
    refs = (a_ref, b_ref, c_ref, d_ref)
    height, rows = a_ref.shape
    body = pl.ds(0, HOURS)
    one, two = pieces(jnp.concatenate([ref[body, :] for ref in refs], axis=1), 2)
    both = dot(jnp.concatenate([two, one], axis=0), high_ref[...])
    result = (both[:HOURS] + dot(one, low_ref[...])) + both[HOURS:]
    mine_ref[body, :] = result[:, :rows]
    other_ref[body, :] = result[:, rows:]
    if height > HOURS:
        tail = pl.ds(HOURS, NOTE)
        note = sum(ref[tail, :] for ref in refs)
        mine_ref[tail, :] = note
        other_ref[tail, :] = note
    for ref in extra:
        other_ref[pl.ds(height, ref.shape[0]), :] = ref[...]


def plane_mix(coupling, values, extra):
    height, rows = values[0].shape
    return pl.pallas_call(
        plane_mix_kernel,
        out_shape=[
            jax.ShapeDtypeStruct((height, rows), F32),
            jax.ShapeDtypeStruct((height + sum(value.shape[0] for value in extra), rows), F32),
        ],
        compiler_params=params(),
        name="plane_mix",
        cost_estimate=SMALL,
    )(*coupling, *values, *extra)


def plane_rows_kernel(first_ref, meta_ref, meta_other_ref, a_ref, b_ref, c_ref, d_ref, *refs):
    if len(refs) > 2:
        *stack, last_ref, beside_ref, mine_ref, other_ref, stack_ref = refs
    else:
        mine_ref, other_ref = refs
    rows = a_ref.shape[1]
    value = jnp.concatenate([ref[pl.ds(0, HOURS), :] for ref in (a_ref, b_ref, c_ref, d_ref)], axis=1)
    one, two = pieces(value, 2)
    stacked = jnp.concatenate([two, one], axis=0)
    picked = []
    for ref in (meta_ref, meta_other_ref):
        gauge = ref[0:1, :]
        hot = jnp.concatenate([hot_rows(gauge, first_ref[m], rows) for m in range(4)], axis=0)
        both = dot(stacked, hot)
        picked.append(both[:HOURS] + both[HOURS:])
    mine_ref[...] = picked[0]
    count = picked[1].shape[1] // rows
    for i in range(count):
        other_ref[pl.ds(i * HOURS, HOURS), :] = picked[1][:, i * rows : (i + 1) * rows]
    if len(refs) > 2:
        top = stack_ref.shape[0] - HOURS
        for ref in stack:
            stack_ref[pl.ds(0, top), :] = ref[...]
        for i in range(count):
            here = pl.ds(i * rows, rows)
            beside = beside_ref[pl.ds(beside_ref.shape[0] - (count - i) * HOURS, HOURS), :]
            stack_ref[pl.ds(top, HOURS), here] = last_ref[:, here] + beside


def plane_rows(first, metas, values, before):
    rows = values[0].shape[1]
    slots = metas[0].shape[1]
    args = [first, *metas, *values, *before]
    shapes = [(HOURS, slots), (slots // rows * HOURS, rows)]
    if before:
        shapes.append(((len(before) - 1) * HOURS, slots))
    return pl.pallas_call(
        plane_rows_kernel,
        in_specs=[pl.BlockSpec(memory_space=pltpu.SMEM)]
        + [pl.BlockSpec(memory_space=pltpu.VMEM)] * (len(args) - 1),
        out_shape=[jax.ShapeDtypeStruct(shape, F32) for shape in shapes],
        compiler_params=params(),
        name="plane_rows",
        cost_estimate=pl.CostEstimate(flops=1_000_000_000, bytes_accessed=2_000_000, transcendentals=0),
    )(*args)


def gain(kernels):
    return jnp.max(jnp.sum(kernels, axis=1, keepdims=True), axis=0, keepdims=True)


def spectra(kind, kernels, wide):
    classes = kernels.shape[0]
    row = lax.broadcasted_iota(jnp.int32, (classes, kind.shape[1]), 0).astype(F32)
    hot = jnp.where(row == kind, 1.0, 0.0).astype(BF16)
    taps = jnp.transpose(kernels / gain(kernels))
    chosen = dot(jnp.concatenate(pieces(taps, 3)[::-1], axis=1), jnp.concatenate([hot] * 3, axis=0))
    return product(wide, chosen, 3)


def plane_spectrum_kernel(class_ref, kernels_ref, wide_ref, out_ref):
    kind = class_ref[1:2, : out_ref.shape[1]]
    out_ref[...] = spectra(kind, kernels_ref[...], wide_ref[...])


def plane_spectrum(meta, kernels, wide, rows):
    return pl.pallas_call(
        plane_spectrum_kernel,
        out_shape=jax.ShapeDtypeStruct((SPAN, rows), F32),
        compiler_params=params(),
        name="plane_spectrum",
        cost_estimate=SMALL,
    )(meta, kernels, wide)


def sides(even, pair, middle):
    return jnp.where(even, middle, pair), jnp.where(even, pair, middle)


def plane_call(kernel, name, shapes, flags, args):
    return pl.pallas_call(
        kernel,
        in_specs=[pl.BlockSpec(memory_space=pltpu.SMEM)] * len(flags)
        + [pl.BlockSpec(memory_space=pltpu.VMEM)] * len(args),
        out_shape=[jax.ShapeDtypeStruct(shape, F32) for shape in shapes],
        compiler_params=params(),
        name=name,
        cost_estimate=SMALL,
    )(*flags, *args)


def plane_first_kernel(
    flag_ref, here_ref, pair_ref, middle_ref, seen_ref, spec_ref, kernels_ref, forward, first, last, out_ref
):
    spec = spec_ref[...]
    before, after = sides(flag_ref[0] > 0.5, pair_ref[...], middle_ref[...])
    now, later = plane_delayed(before, here_ref[...], after, spec, forward[...], last[...], 3)
    known = plane_advanced(now, later * flag_ref[1], spec, forward[...], first[...], 3)
    out_ref[...] = seen_ref[...] - known * gain(kernels_ref[...])


def plane_delay_kernel(flag_ref, here_ref, pair_ref, middle_ref, spec_ref, forward, last, out_ref):
    body = pl.ds(0, HOURS)
    before, after = sides(flag_ref[0] > 0.5, pair_ref[body, :], middle_ref[body, :])
    out = plane_delayed(before, here_ref[body, :], after, spec_ref[...], forward[...], last[...], 2)
    for i in range(2):
        out_ref[pl.ds(i * HOURS, HOURS), :] = out[i]


def write_note(ref, rows):
    tail = [jnp.zeros((NOTE - len(rows), ref.shape[1]), F32)]
    ref[pl.ds(HOURS, NOTE), :] = jnp.concatenate(rows + tail, axis=0)


def plane_open_kernel(
    flag_ref, here_ref, pair_ref, middle_ref, pulled_ref, spec_ref, forward, first, last, out_ref, delayed_ref
):
    here = here_ref[...]
    spec = spec_ref[...]
    before, after = sides(flag_ref[0] > 0.5, pair_ref[...], middle_ref[...])
    now, later = plane_delayed(before, here, after, spec, forward[...], last[...], 2)
    out_ref[pl.ds(0, HOURS), :] = plane_advanced(now, later * flag_ref[1], spec, forward[...], first[...], 2)
    write_note(out_ref, [lanes(pulled_ref[...], here), lanes(now, now)])
    delayed_ref[pl.ds(0, HOURS), :] = now
    delayed_ref[pl.ds(HOURS, HOURS), :] = later


def plane_step_kernel(
    flag_ref,
    here_ref,
    pair_ref,
    two_ref,
    mirror_ref,
    pulled_ref,
    delayed_ref,
    old_z_ref,
    old_s_ref,
    old_delayed_ref,
    spec_ref,
    forward,
    first,
    total_ref,
    out_ref,
    kept_ref,
):
    tail, body = pl.ds(HOURS, NOTE), pl.ds(0, HOURS)
    total_ref[...] = (here_ref[tail, :] + pair_ref[tail, :]) + (two_ref[...] + mirror_ref[...])
    inverse = total(total_ref, 0) / total(total_ref, 1)
    z = pulled_ref[body, :] * inverse - old_z_ref[...]
    s = here_ref[body, :] * inverse - old_s_ref[...]
    both = delayed_ref[...] * inverse - old_delayed_ref[...]
    now, later = both[:HOURS], both[HOURS:]
    following = plane_advanced(now, later * flag_ref[1], spec_ref[...], forward[...], first[...], 2)
    out_ref[body, :] = following * inverse
    write_note(out_ref, [lanes(z, s), lanes(now, now)])
    for i, value in enumerate((z, s, now)):
        kept_ref[pl.ds(i * HOURS, HOURS), :] = value


def plane_close_kernel(
    here_ref, before_ref, pulled_ref, kept_ref, old_z_ref, old_s_ref, old_delayed_ref, spec_ref, forward, last, out_ref
):
    body = pl.ds(0, HOURS)
    here, raw = here_ref[body, :], pulled_ref[body, :]
    waves = product(forward[...], jnp.concatenate([before_ref[body, :], here], axis=0), 2)
    now = product(last[...], turn(waves, spec_ref[...], 1.0), 2)
    z, s, delayed = (kept_ref[pl.ds(i * HOURS, HOURS), :] for i in range(3))
    note = [pulled_ref[HOURS + i : HOURS + i + 1, :] for i in range(2)]
    for left in (raw, z, old_z_ref[...]):
        note += [lanes(left, right) for right in (here, s, old_s_ref[...])]
    parts = (now, delayed, old_delayed_ref[body, :])
    for i in range(3):
        note += [lanes(parts[i], parts[j]) for j in range(i, 3)]
    note.append(jnp.zeros((24 - len(note), here.shape[1]), F32))
    note = jnp.sum(jnp.concatenate(note, axis=0), axis=1, keepdims=True)
    shape = (24, out_ref.shape[2])
    row, col = (lax.broadcasted_iota(jnp.int32, shape, i) for i in range(2))
    note = jnp.sum(jnp.where(row == col, jnp.broadcast_to(note, shape), 0.0), axis=0, keepdims=True)
    out_ref[...] = jnp.broadcast_to(note[None], out_ref.shape)


def plane_weights(open_ref, close, scale):
    entry = lambda i: close[:, i : i + 1]
    n1, t1 = total(open_ref, 0), total(open_ref, 1)
    n2, t2 = entry(0), entry(1)
    a1 = t1 / n1
    a2, r2 = (t2 / n2) / a1, n2 / n1
    plain = (1.0, -a2, -r2)
    n3 = sum(plain[i] * plain[j] * entry(2 + 3 * i + j) for i in range(3) for j in range(3))
    pairs = [(i, j) for i in range(3) for j in range(i, 3)]
    t3 = sum(
        plain[i] * plain[j] * entry(11 + n) * (1.0 if i == j else 2.0) for n, (i, j) in enumerate(pairs)
    )
    a3, r3 = (t3 / n3) / a1, n3 / n2
    unit = 1.0 / (a1 * scale)
    c3 = unit / (a3 * (a2 - r2) - r3)
    c2 = -a3 * c3
    c1 = unit - r2 * c2
    step = c2 - c3 * a2
    return c1 - step - c3 * r2, step / a1, c3


def plane_combine_kernel(open_ref, close_ref, kernels_ref, stack_ref, mine_ref, beside_ref, out_ref):
    rows = open_ref.shape[1]
    close = jnp.sum(close_ref[...], axis=0)[0:1, :]
    e0, e1, e2 = plane_weights(open_ref, close, gain(kernels_ref[...]))
    for i in range(out_ref.shape[0] // rows):
        here = pl.ds(i * rows, rows)
        last = mine_ref[:, here] + beside_ref[pl.ds(i * HOURS, HOURS), :]
        value = stack_ref[pl.ds(0, HOURS), here] * e0 + stack_ref[pl.ds(HOURS, HOURS), here] * e1 + last * e2
        out_ref[here, :] = jnp.transpose(value)


def plane_finish_kernel(rows_ref, inc_ref, field_ref, out_ref):
    blocks, slots, width = inc_ref.shape
    weights = inc_ref[...].astype(F32).astype(BF16)
    for b in range(blocks):
        here = pl.ds(b * width, width)
        rows = jnp.concatenate(pieces(rows_ref[pl.ds(b * slots, slots), :], 2), axis=0)
        twice = jnp.concatenate([weights[b]] * 2, axis=0)
        added = lax.dot_general(twice, rows, (((0,), (0,)), ((), ())), preferred_element_type=F32)
        out_ref[here, :] = field_ref[here, :] + added


def plane_finish(rows, incidence, field):
    blocks, slots, width = incidence.shape
    hours = field.shape[1]
    step = 8
    return pl.pallas_call(
        plane_finish_kernel,
        grid=(blocks // step,),
        in_specs=[
            pl.BlockSpec((step * slots, hours), lambda i: (i, 0)),
            pl.BlockSpec((step, slots, width), lambda i: (i, 0, 0)),
            pl.BlockSpec((step * width, hours), lambda i: (i, 0)),
        ],
        out_specs=pl.BlockSpec((step * width, hours), lambda i: (i, 0)),
        out_shape=jax.ShapeDtypeStruct(field.shape, F32),
        compiler_params=params(),
        name="plane_finish",
    )(rows, incidence, field)


def plane_shards(incidence, row_gauge, gauge_kernel, kernels, observed, first_guess):
    rows, hours = observed.shape
    basin, tm = lax.axis_index("basin"), lax.axis_index("tm")
    z, x, y, c = basin // X_, basin % X_, tm // C_, tm % C_
    place = 2 * y + x
    first = jnp.stack([4 * c + (place ^ m) for m in range(4)] + [4 * c + place, 4 * (1 - c) + place])
    first = (first * rows).astype(jnp.int32)
    flags = jnp.stack([1 - z % 2, (z < Z_ - 1).astype(z.dtype), (z > 0).astype(z.dtype)]).astype(F32)
    forward, inverse_first, inverse_last, _ = turned_transforms(2)
    forward3, inverse_first3, inverse_last3, short3 = turned_transforms(3)
    block, noted = (hours, rows), (hours + NOTE, rows)

    seen = observe(
        observed, moved(observed, hour_before), gauge_kernel, kernels, short3, [forward3, inverse_first3]
    )
    seen, field = lax.optimization_barrier((seen, first_guess))
    seen = moved(seen, to_plane)
    parcel = send(incidence, field, row_gauge, gauge_kernel)
    parcel, near = lax.optimization_barrier((parcel, incidence))
    parcel = moved(parcel, to_plane)
    near, seen = lax.optimization_barrier((near, seen))
    meta = describe(near, row_gauge)
    meta = jnp.concatenate([meta, moved(meta, over_x)], axis=1)
    meta = jnp.concatenate([meta, moved(meta, z_pair)], axis=1)
    parcel, seen = lax.optimization_barrier((parcel, seen))
    parcels = [parcel, moved(parcel, over_core)]
    spec = plane_spectrum(parcel[hours:], kernels, short3, rows)
    parcels[1], seen, meta, spec = lax.optimization_barrier((parcels[1], seen, meta, spec))
    around = [meta, moved(meta, z_two)]
    dense = spread(first, parcels, rows)
    metas = [value[hours:] for value in parcels]
    sums = dense[0] + sum(moved(value, where) for value, where in zip(dense[1:], SQUARE))
    sums = [sums, moved(sums, z_pair), moved(sums, z_middle)]
    coupled = plane_couple(first, around[0], rows)
    coupled, sums = lax.optimization_barrier((coupled, sums))
    coupling = plane_couple(first, around[1], rows, coupled)
    (pulled0,) = plane_call(
        plane_first_kernel,
        "plane_first",
        [block],
        [flags],
        [*sums, seen, spec, kernels, forward3, inverse_first3, inverse_last3],
    )

    def mixing(pulled, extra):
        values = [pulled] + [moved(pulled, where) for where in SQUARE]
        mine, other = plane_mix(coupling, values, extra)
        beside = moved(other, over_core)
        return values, mine + beside[: pulled.shape[0]], beside

    values, mixed0, _ = mixing(pulled0, [])
    picked, theirs = plane_rows(first, metas, values, [])
    sums = [mixed0, moved(mixed0, z_pair), moved(mixed0, z_middle)]
    pulled1, delayed0 = plane_call(
        plane_open_kernel,
        "plane_open",
        [noted, (2 * hours, rows)],
        [flags],
        [*sums, pulled0, spec, forward, inverse_first, inverse_last],
    )

    values, mixed1, beside = mixing(pulled1, [theirs])
    picked, theirs, stack = plane_rows(first, metas, values, [picked, beside])
    sums = [mixed1, moved(mixed1, z_pair), moved(mixed1, z_middle)]
    two, mirror = moved(mixed1[hours:], z_two), moved(mixed1[hours:], z_mirror)
    (delayed1,) = plane_call(
        plane_delay_kernel, "plane_delay", [(2 * hours, rows)], [flags], [*sums, spec, forward, inverse_last]
    )
    open_note, pulled2, kept = plane_call(
        plane_step_kernel,
        "plane_step",
        [(NOTE, rows), noted, (3 * hours, rows)],
        [flags],
        [*sums[:2], two, mirror, pulled1, delayed1, pulled0, mixed0, delayed0, spec, forward, inverse_first],
    )

    values, mixed2, beside = mixing(pulled2, [theirs])
    picked, theirs, stack = plane_rows(first, metas, values, [stack, picked, beside])
    (note,) = plane_call(
        plane_close_kernel,
        "plane_close",
        [(Z_ * X_ * Y_ * C_, 8, rows // 2)],
        [],
        [mixed2, moved(mixed2, z_next), pulled2, kept, pulled0, mixed0, delayed0, spec, forward, inverse_last],
    )
    close_note = lax.all_to_all(note, ("basin", "tm"), 0, 0, tiled=False)
    (answer,) = plane_call(
        plane_combine_kernel,
        "plane_combine",
        [(parcel.shape[1], hours)],
        [],
        [open_note, close_note, kernels, stack, picked, moved(theirs, over_core)],
    )
    return plane_finish(moved(answer, from_plane), incidence, first_guess)


def solution(mesh):
    planes = dict(mesh.shape) == {"basin": Z_ * X_, "tm": Y_ * C_}
    in_specs = (
        P("basin", None, None),
        P("basin"),
        P("basin"),
        P(),
        P("basin", "tm"),
        P("basin", "tm"),
    )
    return jax.shard_map(
        plane_shards if planes else shards, mesh=mesh, in_specs=in_specs, out_specs=P("basin", "tm"), check_vma=False
    )
```

```python
import functools

import jax
import jax.numpy as jnp
import numpy as np
from jax import lax
from jax.experimental import pallas as pl
from jax.experimental.pallas import tpu as pltpu
from jax.sharding import PartitionSpec as P

F32 = jnp.float32
BF16 = jnp.bfloat16
HIGH = lax.Precision.HIGHEST
SPAN = 256
MIB = 1024 * 1024


SMALL = pl.CostEstimate(flops=1, bytes_accessed=1, transcendentals=0)


def params(mib=16):
    return pltpu.CompilerParams(vmem_limit_bytes=mib * MIB)


def transforms():
    half = SPAN // 2
    freq = 2.0 * np.pi * (np.arange(half) + 0.5) / SPAN
    phase = np.arange(SPAN)[:, None] * freq[None, :]
    forward = np.concatenate([np.cos(phase), -np.sin(phase)], axis=1)
    inverse = forward.T * (2.0 / SPAN)
    return (
        jnp.asarray(forward, F32),
        jnp.asarray(inverse[:, :half], F32),
        jnp.asarray(inverse[:, half:], F32),
    )


def dot(a, b):
    return jnp.dot(a, b, preferred_element_type=F32)


def exact(a, b):
    return jnp.dot(a, b, precision=HIGH, preferred_element_type=F32)


def pieces(value, count):
    out = []
    for _ in range(count):
        piece = value.astype(BF16)
        out.append(piece)
        value = value - piece.astype(F32)
    return out


def pick(hot, value):
    return sum(dot(hot, piece) for piece in pieces(value, 3))


def prepare_kernel(inc_ref, field_ref, partial_ref, gram_ref):
    blocks, slots, width = inc_ref.shape
    rows = blocks * slots
    weights = inc_ref[...].astype(F32).astype(BF16)
    for b in range(blocks):
        value = field_ref[pl.ds(b * width, width), :]
        partial_ref[pl.ds(b * slots, slots), :] = pick(weights[b], value)
    flat = weights.reshape(rows, width)
    full = lax.dot_general(flat, flat, (((1,), (1,)), ((), ())), preferred_element_type=F32)
    row = lax.broadcasted_iota(jnp.int32, (rows, rows), 0)
    col = lax.broadcasted_iota(jnp.int32, (rows, rows), 1)
    own = jnp.where(row // slots == col // slots, full, 0.0)
    gram_ref[...] = jnp.sum(own.reshape(blocks, slots, rows), axis=0)


def prepare(incidence, field):
    blocks, slots, width = incidence.shape
    hours = field.shape[1]
    step = 8
    return pl.pallas_call(
        prepare_kernel,
        grid=(blocks // step,),
        in_specs=[
            pl.BlockSpec((step, slots, width), lambda i: (i, 0, 0)),
            pl.BlockSpec((step * width, hours), lambda i: (i, 0)),
        ],
        out_specs=[
            pl.BlockSpec((step * slots, hours), lambda i: (i, 0)),
            pl.BlockSpec((slots, step * slots), lambda i: (0, i)),
        ],
        out_shape=[
            jax.ShapeDtypeStruct((blocks * slots, hours), F32),
            jax.ShapeDtypeStruct((slots, blocks * slots), F32),
        ],
        compiler_params=params(56),
        name="prepare",
    )(incidence, field)


def table_kernel(gauge_ref, partial_ref, out_ref):
    slots = partial_ref.shape[0]
    rows = out_ref.shape[0]
    first = pl.program_id(0) * rows
    gauge = lax.broadcasted_iota(jnp.int32, (rows, slots), 0) + first
    hot = jnp.where(gauge_ref[...] == gauge, 1.0, 0.0).astype(BF16)
    out_ref[...] = pick(hot, partial_ref[...])


def table(row_gauge, partial, gauges):
    slots, hours = partial.shape
    step = 256
    return pl.pallas_call(
        table_kernel,
        grid=(gauges // step,),
        in_specs=[
            pl.BlockSpec((1, slots), lambda i: (0, 0)),
            pl.BlockSpec((slots, hours), lambda i: (0, 0)),
        ],
        out_specs=pl.BlockSpec((step, hours), lambda i: (i, 0)),
        out_shape=jax.ShapeDtypeStruct((gauges, hours), F32),
        compiler_params=params(56),
        name="table",
    )(row_gauge.reshape(1, slots), partial)


def couple_kernel(first_ref, lane_ref, sub_ref, gram_ref, high_ref, low_ref, near_ref):
    slots = gram_ref.shape[0]
    count = lane_ref.shape[1]
    rows, cols = high_ref.shape
    tile = 256
    first = first_ref[0]

    @pl.when(pl.program_id(0) == 0)
    def _():
        row = lax.broadcasted_iota(jnp.int32, (tile, tile), 0)
        col = lax.broadcasted_iota(jnp.int32, (tile, tile), 1)
        same = row // slots == col // slots
        mine = lax.broadcasted_iota(jnp.int32, (rows, tile), 0) + first

        def body(i, carry):
            here = pl.ds(pl.multiple_of(i * tile, tile), tile)
            block = jnp.concatenate([gram_ref[:, here]] * (tile // slots), axis=0)
            block = jnp.where(same, block, 0.0).astype(BF16)
            hot = jnp.where(lane_ref[:, here] == mine, 1.0, 0.0).astype(BF16)
            near_ref[:, here] = dot(hot, block)
            return carry

        lax.fori_loop(0, count // tile, body, 0)

    def chunk(i, total):
        here = pl.ds(pl.multiple_of(i * 1024, 1024), 1024)
        gauge = lax.broadcasted_iota(jnp.int32, (1024, cols), 1) + pl.program_id(0) * cols
        hot = jnp.where(sub_ref[here, :] == gauge, 1.0, 0.0).astype(BF16)
        near = near_ref[:, here]
        high = near.astype(BF16)
        low = (near - high.astype(F32)).astype(BF16)
        return total + dot(high, hot) + dot(low, hot)

    total = lax.fori_loop(0, count // 1024, chunk, jnp.zeros((rows, cols), F32))
    high, low = pieces(total, 2)
    high_ref[...] = high
    low_ref[...] = low


def couple(first, row_gauge, gram, rows, gauges):
    count = row_gauge.shape[0]
    step = 256
    return pl.pallas_call(
        couple_kernel,
        grid=(gauges // step,),
        in_specs=[
            pl.BlockSpec(memory_space=pltpu.SMEM),
            pl.BlockSpec((1, count), lambda i: (0, 0)),
            pl.BlockSpec((count, 1), lambda i: (0, 0)),
            pl.BlockSpec(gram.shape, lambda i: (0, 0)),
        ],
        out_specs=[pl.BlockSpec((rows, step), lambda i: (0, i))] * 2,
        out_shape=[jax.ShapeDtypeStruct((rows, gauges), BF16)] * 2,
        scratch_shapes=[pltpu.VMEM((rows, count), F32)],
        compiler_params=params(56),
        name="couple",
    )(first, row_gauge.reshape(1, count), row_gauge.reshape(count, 1), gram)


def mix_kernel(high_ref, low_ref, value_ref, out_ref):
    high = high_ref[...]
    low = low_ref[...]
    one, two, three = pieces(value_ref[...], 3)
    out_ref[...] = (dot(high, three) + dot(low, two)) + (dot(high, two) + dot(low, one)) + dot(high, one)


def mix(high, low, value):
    return pl.pallas_call(
        mix_kernel,
        out_shape=jax.ShapeDtypeStruct((high.shape[0], value.shape[1]), F32),
        compiler_params=params(56),
        name="mix",
    )(high, low, value)


def spectrum_kernel(class_ref, kernels_ref, forward_ref, out_ref):
    rows = class_ref.shape[0]
    classes, taps = kernels_ref.shape
    kind = lax.broadcasted_iota(jnp.int32, (rows, classes), 1)
    hot = jnp.where(class_ref[...] == kind, 1.0, 0.0)
    out_ref[...] = exact(exact(hot, kernels_ref[...]), forward_ref[pl.ds(0, taps), :])


def spectrum(gauge_kernel, kernels, forward):
    rows = gauge_kernel.shape[0]
    return pl.pallas_call(
        spectrum_kernel,
        out_shape=jax.ShapeDtypeStruct((rows, SPAN), F32),
        compiler_params=params(56),
        name="spectrum",
    )(gauge_kernel.reshape(rows, 1), kernels, forward)


def delayed(before, here, after, spec, forward, inverse_last):
    rows, half = here.shape
    stacked = jnp.concatenate(
        [jnp.concatenate([before, here], axis=1), jnp.concatenate([here, after], axis=1)], axis=0
    )
    waves = exact(stacked, forward)
    real, imag = waves[:, :half], waves[:, half:]
    kr = jnp.concatenate([spec[:, :half]] * 2, axis=0)
    ki = jnp.concatenate([spec[:, half:]] * 2, axis=0)
    turned = jnp.concatenate([real * kr - imag * ki, real * ki + imag * kr], axis=1)
    out = exact(turned, inverse_last)
    return out[:rows], out[rows:]


def advanced(here, after, spec, forward, inverse_first):
    half = here.shape[1]
    waves = exact(jnp.concatenate([here, after], axis=1), forward)
    real, imag = waves[:, :half], waves[:, half:]
    kr, ki = spec[:, :half], spec[:, half:]
    turned = jnp.concatenate([real * kr + imag * ki, imag * kr - real * ki], axis=1)
    return exact(turned, inverse_first)


def lanes(a, b):
    return jnp.sum(a * b, axis=0, keepdims=True)


def total(ref, row):
    return jnp.sum(ref[row : row + 1, :], axis=1, keepdims=True)


def ratios(ref):
    square = total(ref, 0)
    alpha = jnp.sqrt(square)
    beta = jnp.sqrt(jnp.maximum(total(ref, 1) / square - 2.0 * total(ref, 2) + square, 0.0))
    return alpha, beta


def first_kernel(
    more_ref, sums_ref, observed_ref, spec_ref, forward_ref, first_ref, last_ref, out_ref, note_ref
):
    rows, half = observed_ref.shape[0] // 2, observed_ref.shape[1]
    spec, forward = spec_ref[...], forward_ref[...]
    before, here, after = (sums_ref[pl.ds(i * rows, rows), :] for i in range(3))
    now, later = delayed(before, here, after, spec, forward, last_ref[...])
    start = observed_ref[pl.ds(0, rows), :] - now
    start_later = (observed_ref[pl.ds(rows, rows), :] - later) * more_ref[0]
    out_ref[...] = advanced(start, start_later, spec, forward, first_ref[...])
    note_ref[...] = jnp.concatenate([lanes(start, start), jnp.zeros((7, half), F32)], axis=0)


def first_step(more, sums, observed, spec, mats):
    rows, half = spec.shape[0], observed.shape[1]
    return pl.pallas_call(
        first_kernel,
        in_specs=[pl.BlockSpec(memory_space=pltpu.SMEM)] + [pl.BlockSpec(memory_space=pltpu.VMEM)] * 6,
        out_shape=[jax.ShapeDtypeStruct((rows, half), F32), jax.ShapeDtypeStruct((8, half), F32)],
        compiler_params=params(56),
        name="first_step",
    )(more, sums, observed, spec, *mats)


def step_kernel(
    opening,
    final,
    more_ref,
    note_ref,
    sums_ref,
    spec_ref,
    forward_ref,
    first_ref,
    last_ref,
    pulled_ref,
    *refs,
):
    if opening:
        state_ref = None
    else:
        state_ref, *refs = refs
    if final:
        (out_note_ref,) = refs
    else:
        new_ref, out_ref, out_note_ref = refs
    rows, half = pulled_ref.shape
    spec, forward = spec_ref[...], forward_ref[...]
    if opening:
        scale = 1.0 / jnp.sqrt(total(note_ref, 0))
        along = sums_ref[...] * scale
        new_s, new_su = along, along
        new_zu = pulled_ref[...] * scale
        new_z = new_zu
    else:
        alpha, beta = ratios(note_ref)
        a, b, g = 1.0 / (alpha * beta), alpha / beta, beta / alpha
        wide = pl.ds(0, 3 * rows), pl.ds(3 * rows, 3 * rows)
        new_su = sums_ref[...] * a - state_ref[wide[1], :] * b
        new_s = new_su - state_ref[wide[0], :] * g
        new_zu = pulled_ref[...] * a - state_ref[pl.ds(7 * rows, rows), :] * b
        new_z = new_zu - state_ref[pl.ds(6 * rows, rows), :] * g
    before, here, after = (new_s[i * rows : (i + 1) * rows] for i in range(3))
    now, later = delayed(before, here, after, spec, forward, last_ref[...])
    out_note_ref[...] = jnp.concatenate(
        [lanes(new_z, here), lanes(now, now), lanes(new_zu, here), jnp.zeros((5, half), F32)], axis=0
    )
    if not final:
        new_ref[pl.ds(0, 3 * rows), :] = new_s
        new_ref[pl.ds(3 * rows, 3 * rows), :] = new_su
        new_ref[pl.ds(6 * rows, rows), :] = new_z
        new_ref[pl.ds(7 * rows, rows), :] = new_zu
        out_ref[...] = advanced(now, later * more_ref[0], spec, forward, first_ref[...])


def next_step(more, note, sums, spec, mats, pulled, state, final):
    rows, half = pulled.shape
    opening = state is None
    shapes = [
        jax.ShapeDtypeStruct((8 * rows, half), F32),
        jax.ShapeDtypeStruct((rows, half), F32),
        jax.ShapeDtypeStruct((8, half), F32),
    ]
    args = [more, note, sums, spec, *mats, pulled] + ([] if opening else [state])
    return pl.pallas_call(
        functools.partial(step_kernel, opening, final),
        in_specs=[pl.BlockSpec(memory_space=pltpu.SMEM)]
        + [pl.BlockSpec(memory_space=pltpu.VMEM)] * (len(args) - 1),
        out_shape=shapes[2:] if final else shapes,
        compiler_params=params(56),
        name="next_step",
    )(*args)


def weights_of(notes):
    start = jnp.sqrt(total(notes[0], 0))
    zero = jnp.zeros_like(start)
    units = [1.0 / start, zero, zero]
    z, zu = list(units), list(units)
    phibar = start
    alpha, beta = ratios(notes[1])
    rhobar = alpha
    w = [value / alpha for value in z]
    result = [zero] * 3
    steps = len(notes) - 1
    for k in range(steps):
        rho = jnp.sqrt(rhobar * rhobar + beta * beta)
        cosine, sine = rhobar / rho, beta / rho
        phi, phibar = cosine * phibar, sine * phibar
        result = [r + phi / rho * value for r, value in zip(result, w)]
        if k < steps - 1:
            a, b, g = 1.0 / (alpha * beta), alpha / beta, beta / alpha
            zu = [(a if i == k + 1 else 0.0) - b * value for i, value in enumerate(zu)]
            z = [value - g * old for value, old in zip(zu, z)]
            alpha, beta = ratios(notes[k + 2])
            theta = sine * alpha
            rhobar = -cosine * alpha
            w = [value / alpha - theta / rho * old for value, old in zip(z, w)]
    return result


def finish_kernel(n0, n1, n2, n3, gauge_ref, q0, q1, q2, inc_ref, field_ref, out_ref, rows_ref):
    blocks, slots, width = inc_ref.shape
    count = rows_ref.shape[0]
    gauges = q0.shape[0]
    step = pl.program_id(0)

    @pl.when(step == 0)
    def _():
        e0, e1, e2 = weights_of([n0, n1, n2, n3])
        width_ = 512

        def body(i, value):
            here = pl.ds(pl.multiple_of(i * width_, width_), width_)
            mixed = q0[here, :] * e0 + q1[here, :] * e1 + q2[here, :] * e2
            gauge = lax.broadcasted_iota(jnp.int32, (count, width_), 1) + i * width_
            hot = jnp.where(gauge_ref[...] == gauge, 1.0, 0.0).astype(BF16)
            return value + pick(hot, mixed)

        rows_ref[...] = lax.fori_loop(0, gauges // width_, body, jnp.zeros(rows_ref.shape, F32))

    weights = inc_ref[...].astype(F32).astype(BF16)
    for b in range(blocks):
        here = pl.ds(b * width, width)
        rows = rows_ref[pl.ds(pl.multiple_of((step * blocks + b) * slots, slots), slots), :]
        added = sum(
            lax.dot_general(weights[b], piece, (((0,), (0,)), ((), ())), preferred_element_type=F32)
            for piece in pieces(rows, 3)
        )
        out_ref[here, :] = field_ref[here, :] + added


def finish(notes, row_gauge, gathered, incidence, field):
    blocks, slots, width = incidence.shape
    hours = field.shape[1]
    count = row_gauge.shape[0]
    step = 8
    whole = lambda shape: pl.BlockSpec(shape, lambda i: (0, 0))
    return pl.pallas_call(
        finish_kernel,
        grid=(blocks // step,),
        in_specs=[whole(n.shape) for n in notes]
        + [whole((count, 1))]
        + [whole(q.shape) for q in gathered]
        + [
            pl.BlockSpec((step, slots, width), lambda i: (i, 0, 0)),
            pl.BlockSpec((step * width, hours), lambda i: (i, 0)),
        ],
        out_specs=pl.BlockSpec((step * width, hours), lambda i: (i, 0)),
        out_shape=jax.ShapeDtypeStruct(field.shape, F32),
        scratch_shapes=[pltpu.VMEM((count, hours), F32)],
        compiler_params=params(56),
        name="finish",
    )(*notes, row_gauge.reshape(count, 1), *gathered, incidence, field)


def shifted(value, axis, by):
    devices = lax.axis_size(axis)
    pairs = [(i, i + by) for i in range(devices) if 0 <= i + by < devices]
    return lax.ppermute(value, axis, pairs)


def window(value):
    return jnp.concatenate([shifted(value, "tm", 1), value, shifted(value, "tm", -1)], axis=0)


def gathered_rows(value):
    owners = lax.axis_size("basin")
    copies = jnp.broadcast_to(value[None], (owners,) + value.shape)
    return lax.all_to_all(copies, "basin", 0, 0, tiled=False)


def over_hours(note):
    blocks = lax.axis_size("tm")
    result = note
    for by in range(1, blocks):
        result = result + lax.ppermute(note, "tm", [(i, (i + by) % blocks) for i in range(blocks)])
    return result


def shards(incidence, row_gauge, gauge_kernel, kernels, observed, first_guess):
    owners = lax.axis_size("basin")
    rows, hours = observed.shape
    gauges = rows * owners
    mats = transforms()
    spec = spectrum(gauge_kernel, kernels, mats[0])
    more = (lax.axis_index("tm") < lax.axis_size("tm") - 1).astype(F32).reshape(1)
    partial, gram = prepare(incidence, first_guess)
    all_gram = lax.all_gather(gram, "basin", axis=1, tiled=True)
    all_rows = lax.all_gather(row_gauge, "basin", axis=0, tiled=True)
    dense = table(row_gauge, partial, gauges).reshape(owners, rows, hours)
    sums = jnp.sum(lax.all_to_all(dense, "basin", 0, 0, tiled=False), axis=0)
    both = jnp.concatenate([observed, shifted(observed, "tm", -1)], axis=0)
    first = (lax.axis_index("basin") * rows).astype(jnp.int32).reshape(1)
    high, low = couple(first, all_rows, all_gram, rows, gauges)

    pulled, note = first_step(more, window(sums), both, spec, mats)
    notes, kept, state = [], [], None
    for k in range(3):
        everyone = gathered_rows(jnp.concatenate([pulled, note], axis=0))
        value = everyone[:, :rows].reshape(gauges, hours)
        notes.append(over_hours(jnp.sum(everyone[:, rows:], axis=0)))
        kept.append(value)
        around = window(mix(high, low, value))
        final = k == 2
        result = next_step(more, notes[-1], around, spec, mats, pulled, state, final)
        if final:
            (note,) = result
        else:
            state, pulled, note = result
    notes.append(over_hours(jnp.sum(gathered_rows(note), axis=0)))
    return finish(notes, row_gauge, kept, incidence, first_guess)


Z_, X_, Y_, C_ = 4, 2, 2, 2
NOTE = 8
HOURS = SPAN // 2


def device(z, x, y, c):
    return (z * X_ + x) * (Y_ * C_) + y * C_ + c


def moved(value, where):
    pairs = []
    for z, x, y, c in np.ndindex(Z_, X_, Y_, C_):
        target = where(z, x, y, c)
        if target is not None:
            pairs.append((device(z, x, y, c), device(*target)))
    return lax.ppermute(value, ("basin", "tm"), pairs)


def to_plane(z, x, y, c):
    return 2 * y + c, x, z & 1, z >> 1


def hour_before(z, x, y, c):
    t = 2 * y + c - 1
    return (z, x, t >> 1, t & 1) if t >= 0 else None


def from_plane(z, x, y, c):
    return 2 * c + y, x, z >> 1, z & 1


def over_x(z, x, y, c):
    return z, 1 - x, y, c


def over_y(z, x, y, c):
    return z, x, 1 - y, c


def over_xy(z, x, y, c):
    return z, 1 - x, 1 - y, c


def over_core(z, x, y, c):
    return z, x, y, 1 - c


def z_pair(z, x, y, c):
    return z ^ 1, x, y, c


def z_middle(z, x, y, c):
    return (3 - z, x, y, c) if z in (1, 2) else None


def z_two(z, x, y, c):
    return z ^ 2, x, y, c


def z_mirror(z, x, y, c):
    return 3 - z, x, y, c


def z_next(z, x, y, c):
    return (z + 1, x, y, c) if z < 3 else None


SQUARE = (over_x, over_y, over_xy)


def split_constant(value):
    out = []
    for _ in range(3):
        piece = value.astype(jnp.bfloat16)
        out.append(piece)
        value = value - piece.astype(np.float64)
    return out


ORDERS = {2: ((0, 1), (1, 0), (0, 0)), 3: ((0, 2), (1, 1), (2, 0), (0, 1), (1, 0), (0, 0))}


def widened(mat, order):
    parts = split_constant(mat)
    return jnp.asarray(np.concatenate([parts[i] for i, _ in ORDERS[order]], axis=1))


def product(wide, value, order):
    parts = pieces(value, order)
    return dot(wide, jnp.concatenate([parts[j] for _, j in ORDERS[order]], axis=0))


def turned_transforms(order):
    half = SPAN // 2
    freq = 2.0 * np.pi * (np.arange(half) + 0.5) / SPAN
    phase = freq[:, None] * np.arange(SPAN)[None, :]
    forward = np.concatenate([np.cos(phase), -np.sin(phase)], axis=0)
    inverse = forward.T * (2.0 / SPAN)
    return [widened(mat, order) for mat in (forward, inverse[:half], inverse[half:], forward[:, :half])]


def turn(waves, spec, sign):
    half = waves.shape[0] // 2
    real, imag = waves[:half], waves[half:]
    kr, ki = spec[:half], spec[half:] * sign
    return jnp.concatenate([real * kr - imag * ki, real * ki + imag * kr], axis=0)


def plane_delayed(before, here, after, spec, forward, last, order):
    rows = here.shape[1]
    pairs = [jnp.concatenate(pair, axis=0) for pair in ((before, here), (here, after))]
    waves = product(forward, jnp.concatenate(pairs, axis=1), order)
    turned = [turn(waves[:, i * rows : (i + 1) * rows], spec, 1.0) for i in range(2)]
    out = product(last, jnp.concatenate(turned, axis=1), order)
    return out[:, :rows], out[:, rows:]


def plane_advanced(here, after, spec, forward, first, order):
    waves = product(forward, jnp.concatenate([here, after], axis=0), order)
    return product(first, turn(waves, spec, -1.0), order)


def describe_kernel(inc_ref, gauge_ref, out_ref):
    blocks, slots, width = inc_ref.shape
    tile = 8
    side = tile * slots
    weights = inc_ref[...].astype(F32).astype(BF16)
    row = lax.broadcasted_iota(jnp.int32, (side, side), 0)
    col = lax.broadcasted_iota(jnp.int32, (side, side), 1)
    same = row // slots == col // slots
    for i in range(blocks // tile):
        flat = weights[i * tile : (i + 1) * tile].reshape(side, width)
        full = lax.dot_general(flat, flat, (((1,), (1,)), ((), ())), preferred_element_type=F32)
        own = jnp.where(same, full, 0.0)
        out_ref[pl.ds(0, slots), pl.ds(i * side, side)] = jnp.sum(own.reshape(tile, slots, side), axis=0)
    out_ref[pl.ds(slots, 8), :] = jnp.broadcast_to(gauge_ref[...].astype(F32), (8, blocks * slots))


def describe(incidence, row_gauge):
    blocks, slots, _ = incidence.shape
    count = blocks * slots
    return pl.pallas_call(
        describe_kernel,
        out_shape=jax.ShapeDtypeStruct((slots + 8, count), F32),
        compiler_params=params(),
        name="describe",
        cost_estimate=SMALL,
    )(incidence, row_gauge.reshape(1, count))


def send_kernel(
    inc_hbm, field_hbm, gauge_hbm, kind_hbm, out_ref, inc_ref, field_ref, gauge_ref, kind_ref, sems, label_sems
):
    blocks, slots, width = inc_ref.shape
    chunks = sems.shape[0]
    step = blocks // chunks
    copies = []
    for i in range(chunks):
        near = pl.ds(i * step, step)
        far = pl.ds(i * step * width, step * width)
        copies.append(
            (
                pltpu.make_async_copy(inc_hbm.at[near], inc_ref.at[near], sems.at[i, 0]),
                pltpu.make_async_copy(field_hbm.at[far], field_ref.at[far], sems.at[i, 1]),
            )
        )
        for copy in copies[-1]:
            copy.start()
    labels = (
        pltpu.make_async_copy(gauge_hbm, gauge_ref, label_sems.at[0]),
        pltpu.make_async_copy(kind_hbm, kind_ref, label_sems.at[1]),
    )
    for copy in labels:
        copy.start()
    for i in range(chunks):
        for copy in copies[i]:
            copy.wait()
        parts = []
        for b in range(i * step, (i + 1) * step):
            weight = inc_ref[b].astype(F32).astype(BF16)
            value = jnp.concatenate(pieces(field_ref[pl.ds(b * width, width), :], 3)[::-1], axis=0)
            parts.append(dot(jnp.concatenate([weight] * 3, axis=1), value))
        out_ref[pl.ds(0, HOURS), pl.ds(i * step * slots, step * slots)] = jnp.transpose(
            jnp.concatenate(parts, axis=0)
        )
    for copy in labels:
        copy.wait()
    count, kinds = gauge_ref.shape[1], kind_ref.shape[1]
    kind = jnp.concatenate([kind_ref[...].astype(F32), jnp.zeros((1, count - kinds), F32)], axis=1)
    out_ref[pl.ds(HOURS, 8), :] = jnp.concatenate(
        [gauge_ref[...].astype(F32), kind, jnp.zeros((6, count), F32)], axis=0
    )


def send(incidence, field, row_gauge, gauge_kernel):
    count, rows = row_gauge.shape[0], gauge_kernel.shape[0]
    chunks = 4
    return pl.pallas_call(
        send_kernel,
        in_specs=[pl.BlockSpec(memory_space=pltpu.HBM)] * 4,
        out_shape=jax.ShapeDtypeStruct((HOURS + 8, count), F32),
        scratch_shapes=[
            pltpu.VMEM(incidence.shape, incidence.dtype),
            pltpu.VMEM(field.shape, F32),
            pltpu.VMEM((1, count), row_gauge.dtype),
            pltpu.VMEM((1, rows), gauge_kernel.dtype),
            pltpu.SemaphoreType.DMA((chunks, 2)),
            pltpu.SemaphoreType.DMA((2,)),
        ],
        compiler_params=params(60),
        name="send",
        cost_estimate=SMALL,
    )(incidence, field, row_gauge.reshape(1, count), gauge_kernel.reshape(1, rows))


def hot_rows(gauge, first, rows):
    mine = (lax.broadcasted_iota(jnp.int32, (rows, gauge.shape[1]), 0) + first).astype(F32)
    return jnp.where(gauge == mine, 1.0, 0.0).astype(BF16)


def spread_kernel(first_ref, mine_ref, other_ref, *out_refs):
    rows = out_refs[0].shape[1]
    both = jnp.concatenate([mine_ref[...], other_ref[...]], axis=1)
    stacked = jnp.concatenate(pieces(both[:HOURS], 3), axis=0)
    for m, out_ref in enumerate(out_refs):
        hot = hot_rows(both[HOURS : HOURS + 1], first_ref[m], rows)
        result = lax.dot_general(stacked, hot, (((1,), (1,)), ((), ())), preferred_element_type=F32)
        out_ref[...] = (result[2 * HOURS :] + result[HOURS : 2 * HOURS]) + result[:HOURS]


def spread(first, parcels, rows):
    return pl.pallas_call(
        spread_kernel,
        in_specs=[pl.BlockSpec(memory_space=pltpu.SMEM)] + [pl.BlockSpec(memory_space=pltpu.VMEM)] * 2,
        out_shape=[jax.ShapeDtypeStruct((HOURS, rows), F32)] * 4,
        compiler_params=params(),
        name="spread",
        cost_estimate=SMALL,
    )(first, *parcels)


def plane_couple_kernel(last, first_ref, *refs):
    if last:
        all_ref, before_ref, high_ref, low_ref, total_ref, meta_ref = refs
        total_ref[...] = before_ref[...]
    else:
        all_ref, total_ref, meta_ref = refs
        total_ref[...] = jnp.zeros_like(total_ref)
    parts, height, count = meta_ref.shape
    slots = height - 8
    cols, rows = total_ref.shape
    tile = 256
    for i in range(parts):
        meta_ref[i] = all_ref[:, i * count : (i + 1) * count]
    row = lax.broadcasted_iota(jnp.int32, (tile, tile), 0)
    col = lax.broadcasted_iota(jnp.int32, (tile, tile), 1)
    same = row // slots == col // slots

    def body(i, carry):
        gauge = meta_ref[i, slots : slots + 1, :]
        near = []
        for j in range(count // tile):
            here = slice(j * tile, (j + 1) * tile)
            block = jnp.concatenate([meta_ref[i, :slots, here]] * (tile // slots), axis=0)
            block = jnp.where(same, block, 0.0).astype(BF16)
            mine = jnp.concatenate(
                [hot_rows(gauge[:, here], first_ref[4 + h], rows // 2) for h in range(2)], axis=0
            )
            near.append(
                lax.dot_general(block, mine, (((1,), (1,)), ((), ())), preferred_element_type=F32)
            )
        near = jnp.concatenate(near, axis=0)
        high = near.astype(BF16)
        rest = near - high.astype(F32)
        hot = jnp.concatenate([hot_rows(gauge, first_ref[m], cols // 4) for m in range(4)], axis=0)
        total_ref[...] += dot(hot, high)

        @pl.when(jnp.max(jnp.abs(rest)) > 0.0)
        def _():
            total_ref[...] += dot(hot, rest.astype(BF16))

        return carry

    lax.fori_loop(0, parts, body, 0)
    if last:
        high, low = pieces(total_ref[...], 2)
        high_ref[...] = high
        low_ref[...] = low


def plane_couple(first, meta, rows, before=None):
    height, wide = meta.shape
    parts = 2 * X_
    shape = (4 * rows, 2 * rows)
    last = before is not None
    args = [first, meta] + ([before] if last else [])
    scratch = [pltpu.VMEM((parts, height, wide // parts), F32)]
    return pl.pallas_call(
        functools.partial(plane_couple_kernel, last),
        in_specs=[pl.BlockSpec(memory_space=pltpu.SMEM)]
        + [pl.BlockSpec(memory_space=pltpu.VMEM)] * (len(args) - 1),
        out_shape=[jax.ShapeDtypeStruct(shape, BF16)] * 2 if last else jax.ShapeDtypeStruct(shape, F32),
        scratch_shapes=([pltpu.VMEM(shape, F32)] if last else []) + scratch,
        compiler_params=params(),
        name="plane_couple",
        cost_estimate=pl.CostEstimate(
            flops=2 * 8 * wide * rows * rows, bytes_accessed=2_000_000, transcendentals=0
        ),
    )(*args)


def plane_mix_kernel(high_ref, low_ref, a_ref, b_ref, c_ref, d_ref, *refs):
    *extra, mine_ref, other_ref = refs
    refs = (a_ref, b_ref, c_ref, d_ref)
    height, rows = a_ref.shape
    body = pl.ds(0, HOURS)
    one, two = pieces(jnp.concatenate([ref[body, :] for ref in refs], axis=1), 2)
    both = dot(jnp.concatenate([two, one], axis=0), high_ref[...])
    result = (both[:HOURS] + dot(one, low_ref[...])) + both[HOURS:]
    mine_ref[body, :] = result[:, :rows]
    other_ref[body, :] = result[:, rows:]
    if height > HOURS:
        tail = pl.ds(HOURS, NOTE)
        note = sum(ref[tail, :] for ref in refs)
        mine_ref[tail, :] = note
        other_ref[tail, :] = note
    for ref in extra:
        other_ref[pl.ds(height, ref.shape[0]), :] = ref[...]


def plane_mix(coupling, values, extra):
    height, rows = values[0].shape
    return pl.pallas_call(
        plane_mix_kernel,
        out_shape=[
            jax.ShapeDtypeStruct((height, rows), F32),
            jax.ShapeDtypeStruct((height + sum(value.shape[0] for value in extra), rows), F32),
        ],
        compiler_params=params(),
        name="plane_mix",
        cost_estimate=SMALL,
    )(*coupling, *values, *extra)


def plane_rows_kernel(first_ref, meta_ref, meta_other_ref, a_ref, b_ref, c_ref, d_ref, *refs):
    if len(refs) > 2:
        *stack, last_ref, beside_ref, mine_ref, other_ref, stack_ref = refs
    else:
        mine_ref, other_ref = refs
    rows = a_ref.shape[1]
    value = jnp.concatenate([ref[pl.ds(0, HOURS), :] for ref in (a_ref, b_ref, c_ref, d_ref)], axis=1)
    one, two = pieces(value, 2)
    stacked = jnp.concatenate([two, one], axis=0)
    picked = []
    for ref in (meta_ref, meta_other_ref):
        gauge = ref[0:1, :]
        hot = jnp.concatenate([hot_rows(gauge, first_ref[m], rows) for m in range(4)], axis=0)
        both = dot(stacked, hot)
        picked.append(both[:HOURS] + both[HOURS:])
    mine_ref[...] = picked[0]
    count = picked[1].shape[1] // rows
    for i in range(count):
        other_ref[pl.ds(i * HOURS, HOURS), :] = picked[1][:, i * rows : (i + 1) * rows]
    if len(refs) > 2:
        top = stack_ref.shape[0] - HOURS
        for ref in stack:
            stack_ref[pl.ds(0, top), :] = ref[...]
        for i in range(count):
            here = pl.ds(i * rows, rows)
            beside = beside_ref[pl.ds(beside_ref.shape[0] - (count - i) * HOURS, HOURS), :]
            stack_ref[pl.ds(top, HOURS), here] = last_ref[:, here] + beside


def plane_rows(first, metas, values, before):
    rows = values[0].shape[1]
    slots = metas[0].shape[1]
    args = [first, *metas, *values, *before]
    shapes = [(HOURS, slots), (slots // rows * HOURS, rows)]
    if before:
        shapes.append(((len(before) - 1) * HOURS, slots))
    return pl.pallas_call(
        plane_rows_kernel,
        in_specs=[pl.BlockSpec(memory_space=pltpu.SMEM)]
        + [pl.BlockSpec(memory_space=pltpu.VMEM)] * (len(args) - 1),
        out_shape=[jax.ShapeDtypeStruct(shape, F32) for shape in shapes],
        compiler_params=params(),
        name="plane_rows",
        cost_estimate=pl.CostEstimate(flops=1_000_000_000, bytes_accessed=2_000_000, transcendentals=0),
    )(*args)


def gain(kernels):
    return jnp.max(jnp.sum(kernels, axis=1, keepdims=True), axis=0, keepdims=True)


def spectra(kind, kernels, wide):
    classes = kernels.shape[0]
    row = lax.broadcasted_iota(jnp.int32, (classes, kind.shape[1]), 0).astype(F32)
    hot = jnp.where(row == kind, 1.0, 0.0).astype(BF16)
    taps = jnp.transpose(kernels / gain(kernels))
    chosen = dot(jnp.concatenate(pieces(taps, 3)[::-1], axis=1), jnp.concatenate([hot] * 3, axis=0))
    return product(wide, chosen, 3)


def plane_spectrum_kernel(class_ref, kernels_ref, wide_ref, out_ref):
    kind = class_ref[1:2, : out_ref.shape[1]]
    out_ref[...] = spectra(kind, kernels_ref[...], wide_ref[...])


def plane_spectrum(meta, kernels, wide, rows):
    return pl.pallas_call(
        plane_spectrum_kernel,
        out_shape=jax.ShapeDtypeStruct((SPAN, rows), F32),
        compiler_params=params(),
        name="plane_spectrum",
        cost_estimate=SMALL,
    )(meta, kernels, wide)


def sides(even, pair, middle):
    return jnp.where(even, middle, pair), jnp.where(even, pair, middle)


def plane_call(kernel, name, shapes, flags, args):
    return pl.pallas_call(
        kernel,
        in_specs=[pl.BlockSpec(memory_space=pltpu.SMEM)] * len(flags)
        + [pl.BlockSpec(memory_space=pltpu.VMEM)] * len(args),
        out_shape=[jax.ShapeDtypeStruct(shape, F32) for shape in shapes],
        compiler_params=params(),
        name=name,
        cost_estimate=SMALL,
    )(*flags, *args)


def plane_first_kernel(
    flag_ref, here_ref, pair_ref, middle_ref, spec_ref, kernels_ref, forward, first, last, out_ref
):
    spec = spec_ref[...]
    before, after = sides(flag_ref[0] > 0.5, pair_ref[...], middle_ref[...])
    here = here_ref[...]
    both = plane_delayed(before[:HOURS], here[:HOURS], after[:HOURS], spec, forward[...], last[...], 3)
    scale = gain(kernels_ref[...])
    now = here[HOURS:] - both[0] * scale
    later = (after[HOURS:] - both[1] * scale) * flag_ref[1]
    out_ref[...] = plane_advanced(now, later, spec, forward[...], first[...], 3)


def plane_delay_kernel(flag_ref, here_ref, pair_ref, middle_ref, spec_ref, forward, last, out_ref):
    body = pl.ds(0, HOURS)
    before, after = sides(flag_ref[0] > 0.5, pair_ref[body, :], middle_ref[body, :])
    out = plane_delayed(before, here_ref[body, :], after, spec_ref[...], forward[...], last[...], 2)
    for i in range(2):
        out_ref[pl.ds(i * HOURS, HOURS), :] = out[i]


def write_note(ref, rows):
    tail = [jnp.zeros((NOTE - len(rows), ref.shape[1]), F32)]
    ref[pl.ds(HOURS, NOTE), :] = jnp.concatenate(rows + tail, axis=0)


def plane_open_kernel(
    flag_ref, here_ref, pair_ref, middle_ref, pulled_ref, spec_ref, forward, first, last, out_ref, delayed_ref
):
    here = here_ref[...]
    spec = spec_ref[...]
    before, after = sides(flag_ref[0] > 0.5, pair_ref[...], middle_ref[...])
    now, later = plane_delayed(before, here, after, spec, forward[...], last[...], 2)
    out_ref[pl.ds(0, HOURS), :] = plane_advanced(now, later * flag_ref[1], spec, forward[...], first[...], 2)
    write_note(out_ref, [lanes(pulled_ref[...], here), lanes(now, now)])
    delayed_ref[pl.ds(0, HOURS), :] = now
    delayed_ref[pl.ds(HOURS, HOURS), :] = later


def plane_step_kernel(
    flag_ref,
    here_ref,
    pair_ref,
    two_ref,
    mirror_ref,
    pulled_ref,
    delayed_ref,
    old_z_ref,
    old_s_ref,
    old_delayed_ref,
    spec_ref,
    forward,
    first,
    total_ref,
    out_ref,
    kept_ref,
):
    tail, body = pl.ds(HOURS, NOTE), pl.ds(0, HOURS)
    total_ref[...] = (here_ref[tail, :] + pair_ref[tail, :]) + (two_ref[...] + mirror_ref[...])
    inverse = total(total_ref, 0) / total(total_ref, 1)
    z = pulled_ref[body, :] * inverse - old_z_ref[...]
    s = here_ref[body, :] * inverse - old_s_ref[...]
    both = delayed_ref[...] * inverse - old_delayed_ref[...]
    now, later = both[:HOURS], both[HOURS:]
    following = plane_advanced(now, later * flag_ref[1], spec_ref[...], forward[...], first[...], 2)
    out_ref[body, :] = following * inverse
    write_note(out_ref, [lanes(z, s), lanes(now, now)])
    for i, value in enumerate((z, s, now)):
        kept_ref[pl.ds(i * HOURS, HOURS), :] = value


def plane_close_kernel(
    here_ref, before_ref, pulled_ref, kept_ref, old_z_ref, old_s_ref, old_delayed_ref, spec_ref, forward, last, out_ref
):
    body = pl.ds(0, HOURS)
    here, raw = here_ref[body, :], pulled_ref[body, :]
    waves = product(forward[...], jnp.concatenate([before_ref[body, :], here], axis=0), 2)
    now = product(last[...], turn(waves, spec_ref[...], 1.0), 2)
    z, s, delayed = (kept_ref[pl.ds(i * HOURS, HOURS), :] for i in range(3))
    note = [pulled_ref[HOURS + i : HOURS + i + 1, :] for i in range(2)]
    for left in (raw, z, old_z_ref[...]):
        note += [lanes(left, right) for right in (here, s, old_s_ref[...])]
    parts = (now, delayed, old_delayed_ref[body, :])
    for i in range(3):
        note += [lanes(parts[i], parts[j]) for j in range(i, 3)]
    note.append(jnp.zeros((24 - len(note), here.shape[1]), F32))
    note = jnp.sum(jnp.concatenate(note, axis=0), axis=1, keepdims=True)
    shape = (24, out_ref.shape[2])
    row, col = (lax.broadcasted_iota(jnp.int32, shape, i) for i in range(2))
    note = jnp.sum(jnp.where(row == col, jnp.broadcast_to(note, shape), 0.0), axis=0, keepdims=True)
    out_ref[...] = jnp.broadcast_to(note[None], out_ref.shape)


def plane_weights(open_ref, close, scale):
    entry = lambda i: close[:, i : i + 1]
    n1, t1 = total(open_ref, 0), total(open_ref, 1)
    n2, t2 = entry(0), entry(1)
    a1 = t1 / n1
    a2, r2 = (t2 / n2) / a1, n2 / n1
    plain = (1.0, -a2, -r2)
    n3 = sum(plain[i] * plain[j] * entry(2 + 3 * i + j) for i in range(3) for j in range(3))
    pairs = [(i, j) for i in range(3) for j in range(i, 3)]
    t3 = sum(
        plain[i] * plain[j] * entry(11 + n) * (1.0 if i == j else 2.0) for n, (i, j) in enumerate(pairs)
    )
    a3, r3 = (t3 / n3) / a1, n3 / n2
    unit = 1.0 / (a1 * scale)
    c3 = unit / (a3 * (a2 - r2) - r3)
    c2 = -a3 * c3
    c1 = unit - r2 * c2
    step = c2 - c3 * a2
    return c1 - step - c3 * r2, step / a1, c3


def plane_combine_kernel(open_ref, close_ref, kernels_ref, stack_ref, mine_ref, beside_ref, out_ref):
    rows = open_ref.shape[1]
    close = jnp.sum(close_ref[...], axis=0)[0:1, :]
    e0, e1, e2 = plane_weights(open_ref, close, gain(kernels_ref[...]))
    for i in range(out_ref.shape[0] // rows):
        here = pl.ds(i * rows, rows)
        last = mine_ref[:, here] + beside_ref[pl.ds(i * HOURS, HOURS), :]
        value = stack_ref[pl.ds(0, HOURS), here] * e0 + stack_ref[pl.ds(HOURS, HOURS), here] * e1 + last * e2
        out_ref[here, :] = jnp.transpose(value)


def plane_finish_kernel(rows_ref, inc_ref, field_ref, out_ref):
    blocks, slots, width = inc_ref.shape
    weights = inc_ref[...].astype(F32).astype(BF16)
    for b in range(blocks):
        here = pl.ds(b * width, width)
        rows = jnp.concatenate(pieces(rows_ref[pl.ds(b * slots, slots), :], 2), axis=0)
        twice = jnp.concatenate([weights[b]] * 2, axis=0)
        added = lax.dot_general(twice, rows, (((0,), (0,)), ((), ())), preferred_element_type=F32)
        out_ref[here, :] = field_ref[here, :] + added


def plane_finish(rows, incidence, field):
    blocks, slots, width = incidence.shape
    hours = field.shape[1]
    step = 8
    return pl.pallas_call(
        plane_finish_kernel,
        grid=(blocks // step,),
        in_specs=[
            pl.BlockSpec((step * slots, hours), lambda i: (i, 0)),
            pl.BlockSpec((step, slots, width), lambda i: (i, 0, 0)),
            pl.BlockSpec((step * width, hours), lambda i: (i, 0)),
        ],
        out_specs=pl.BlockSpec((step * width, hours), lambda i: (i, 0)),
        out_shape=jax.ShapeDtypeStruct(field.shape, F32),
        compiler_params=params(),
        name="plane_finish",
    )(rows, incidence, field)


def plane_shards(incidence, row_gauge, gauge_kernel, kernels, observed, first_guess):
    rows, hours = observed.shape
    basin, tm = lax.axis_index("basin"), lax.axis_index("tm")
    z, x, y, c = basin // X_, basin % X_, tm // C_, tm % C_
    place = 2 * y + x
    first = jnp.stack([4 * c + (place ^ m) for m in range(4)] + [4 * c + place, 4 * (1 - c) + place])
    first = (first * rows).astype(jnp.int32)
    flags = jnp.stack([1 - z % 2, (z < Z_ - 1).astype(z.dtype), (z > 0).astype(z.dtype)]).astype(F32)
    forward, inverse_first, inverse_last, _ = turned_transforms(2)
    forward3, inverse_first3, inverse_last3, short3 = turned_transforms(3)
    block, noted = (hours, rows), (hours + NOTE, rows)

    seen = moved(observed, to_plane)
    parcel = send(incidence, first_guess, row_gauge, gauge_kernel)
    parcel, near = lax.optimization_barrier((parcel, incidence))
    parcel = moved(parcel, to_plane)
    near, seen = lax.optimization_barrier((near, seen))
    meta = describe(near, row_gauge)
    meta = jnp.concatenate([meta, moved(meta, over_x)], axis=1)
    meta = jnp.concatenate([meta, moved(meta, z_pair)], axis=1)
    parcel, seen = lax.optimization_barrier((parcel, seen))
    parcels = [parcel, moved(parcel, over_core)]
    spec = plane_spectrum(parcel[hours:], kernels, short3, rows)
    parcels[1], seen, meta, spec = lax.optimization_barrier((parcels[1], seen, meta, spec))
    around = [meta, moved(meta, z_two)]
    dense = spread(first, parcels, rows)
    metas = [value[hours:] for value in parcels]
    sums = dense[0] + sum(moved(value, where) for value, where in zip(dense[1:], SQUARE))
    sums, around = lax.optimization_barrier((sums, around))
    sums = jnp.concatenate([sums, jnp.transpose(seen)], axis=0)
    sums = [sums, moved(sums, z_pair), moved(sums, z_middle)]
    coupled = plane_couple(first, around[0], rows)
    coupled, sums = lax.optimization_barrier((coupled, sums))
    coupling = plane_couple(first, around[1], rows, coupled)
    (pulled0,) = plane_call(
        plane_first_kernel,
        "plane_first",
        [block],
        [flags],
        [*sums, spec, kernels, forward3, inverse_first3, inverse_last3],
    )

    def mixing(pulled, extra):
        values = [pulled] + [moved(pulled, where) for where in SQUARE]
        mine, other = plane_mix(coupling, values, extra)
        beside = moved(other, over_core)
        return values, mine + beside[: pulled.shape[0]], beside

    values, mixed0, _ = mixing(pulled0, [])
    picked, theirs = plane_rows(first, metas, values, [])
    sums = [mixed0, moved(mixed0, z_pair), moved(mixed0, z_middle)]
    pulled1, delayed0 = plane_call(
        plane_open_kernel,
        "plane_open",
        [noted, (2 * hours, rows)],
        [flags],
        [*sums, pulled0, spec, forward, inverse_first, inverse_last],
    )

    values, mixed1, beside = mixing(pulled1, [theirs])
    picked, theirs, stack = plane_rows(first, metas, values, [picked, beside])
    sums = [mixed1, moved(mixed1, z_pair), moved(mixed1, z_middle)]
    two, mirror = moved(mixed1[hours:], z_two), moved(mixed1[hours:], z_mirror)
    (delayed1,) = plane_call(
        plane_delay_kernel, "plane_delay", [(2 * hours, rows)], [flags], [*sums, spec, forward, inverse_last]
    )
    open_note, pulled2, kept = plane_call(
        plane_step_kernel,
        "plane_step",
        [(NOTE, rows), noted, (3 * hours, rows)],
        [flags],
        [*sums[:2], two, mirror, pulled1, delayed1, pulled0, mixed0, delayed0, spec, forward, inverse_first],
    )

    values, mixed2, beside = mixing(pulled2, [theirs])
    picked, theirs, stack = plane_rows(first, metas, values, [stack, picked, beside])
    (note,) = plane_call(
        plane_close_kernel,
        "plane_close",
        [(Z_ * X_ * Y_ * C_, 8, rows // 2)],
        [],
        [mixed2, moved(mixed2, z_next), pulled2, kept, pulled0, mixed0, delayed0, spec, forward, inverse_last],
    )
    close_note = lax.all_to_all(note, ("basin", "tm"), 0, 0, tiled=False)
    (answer,) = plane_call(
        plane_combine_kernel,
        "plane_combine",
        [(parcel.shape[1], hours)],
        [],
        [open_note, close_note, kernels, stack, picked, moved(theirs, over_core)],
    )
    return plane_finish(moved(answer, from_plane), incidence, first_guess)


def solution(mesh):
    planes = dict(mesh.shape) == {"basin": Z_ * X_, "tm": Y_ * C_}
    in_specs = (
        P("basin", None, None),
        P("basin"),
        P("basin"),
        P(),
        P("basin", "tm"),
        P("basin", "tm"),
    )
    return jax.shard_map(
        plane_shards if planes else shards, mesh=mesh, in_specs=in_specs, out_specs=P("basin", "tm"), check_vma=False
    )
```

```python
import functools

import jax
import jax.numpy as jnp
import numpy as np
from jax import lax
from jax.experimental import pallas as pl
from jax.experimental.pallas import tpu as pltpu
from jax.sharding import PartitionSpec as P

F32 = jnp.float32
BF16 = jnp.bfloat16
HIGH = lax.Precision.HIGHEST
SPAN = 256
MIB = 1024 * 1024


SMALL = pl.CostEstimate(flops=1, bytes_accessed=1, transcendentals=0)


def params(mib=16):
    return pltpu.CompilerParams(vmem_limit_bytes=mib * MIB)


def transforms():
    half = SPAN // 2
    freq = 2.0 * np.pi * (np.arange(half) + 0.5) / SPAN
    phase = np.arange(SPAN)[:, None] * freq[None, :]
    forward = np.concatenate([np.cos(phase), -np.sin(phase)], axis=1)
    inverse = forward.T * (2.0 / SPAN)
    return (
        jnp.asarray(forward, F32),
        jnp.asarray(inverse[:, :half], F32),
        jnp.asarray(inverse[:, half:], F32),
    )


def dot(a, b):
    return jnp.dot(a, b, preferred_element_type=F32)


def exact(a, b):
    return jnp.dot(a, b, precision=HIGH, preferred_element_type=F32)


def pieces(value, count):
    out = []
    for _ in range(count):
        piece = value.astype(BF16)
        out.append(piece)
        value = value - piece.astype(F32)
    return out


def pick(hot, value):
    return sum(dot(hot, piece) for piece in pieces(value, 3))


def prepare_kernel(inc_ref, field_ref, partial_ref, gram_ref):
    blocks, slots, width = inc_ref.shape
    rows = blocks * slots
    weights = inc_ref[...].astype(F32).astype(BF16)
    for b in range(blocks):
        value = field_ref[pl.ds(b * width, width), :]
        partial_ref[pl.ds(b * slots, slots), :] = pick(weights[b], value)
    flat = weights.reshape(rows, width)
    full = lax.dot_general(flat, flat, (((1,), (1,)), ((), ())), preferred_element_type=F32)
    row = lax.broadcasted_iota(jnp.int32, (rows, rows), 0)
    col = lax.broadcasted_iota(jnp.int32, (rows, rows), 1)
    own = jnp.where(row // slots == col // slots, full, 0.0)
    gram_ref[...] = jnp.sum(own.reshape(blocks, slots, rows), axis=0)


def prepare(incidence, field):
    blocks, slots, width = incidence.shape
    hours = field.shape[1]
    step = 8
    return pl.pallas_call(
        prepare_kernel,
        grid=(blocks // step,),
        in_specs=[
            pl.BlockSpec((step, slots, width), lambda i: (i, 0, 0)),
            pl.BlockSpec((step * width, hours), lambda i: (i, 0)),
        ],
        out_specs=[
            pl.BlockSpec((step * slots, hours), lambda i: (i, 0)),
            pl.BlockSpec((slots, step * slots), lambda i: (0, i)),
        ],
        out_shape=[
            jax.ShapeDtypeStruct((blocks * slots, hours), F32),
            jax.ShapeDtypeStruct((slots, blocks * slots), F32),
        ],
        compiler_params=params(56),
        name="prepare",
    )(incidence, field)


def table_kernel(gauge_ref, partial_ref, out_ref):
    slots = partial_ref.shape[0]
    rows = out_ref.shape[0]
    first = pl.program_id(0) * rows
    gauge = lax.broadcasted_iota(jnp.int32, (rows, slots), 0) + first
    hot = jnp.where(gauge_ref[...] == gauge, 1.0, 0.0).astype(BF16)
    out_ref[...] = pick(hot, partial_ref[...])


def table(row_gauge, partial, gauges):
    slots, hours = partial.shape
    step = 256
    return pl.pallas_call(
        table_kernel,
        grid=(gauges // step,),
        in_specs=[
            pl.BlockSpec((1, slots), lambda i: (0, 0)),
            pl.BlockSpec((slots, hours), lambda i: (0, 0)),
        ],
        out_specs=pl.BlockSpec((step, hours), lambda i: (i, 0)),
        out_shape=jax.ShapeDtypeStruct((gauges, hours), F32),
        compiler_params=params(56),
        name="table",
    )(row_gauge.reshape(1, slots), partial)


def couple_kernel(first_ref, lane_ref, sub_ref, gram_ref, high_ref, low_ref, near_ref):
    slots = gram_ref.shape[0]
    count = lane_ref.shape[1]
    rows, cols = high_ref.shape
    tile = 256
    first = first_ref[0]

    @pl.when(pl.program_id(0) == 0)
    def _():
        row = lax.broadcasted_iota(jnp.int32, (tile, tile), 0)
        col = lax.broadcasted_iota(jnp.int32, (tile, tile), 1)
        same = row // slots == col // slots
        mine = lax.broadcasted_iota(jnp.int32, (rows, tile), 0) + first

        def body(i, carry):
            here = pl.ds(pl.multiple_of(i * tile, tile), tile)
            block = jnp.concatenate([gram_ref[:, here]] * (tile // slots), axis=0)
            block = jnp.where(same, block, 0.0).astype(BF16)
            hot = jnp.where(lane_ref[:, here] == mine, 1.0, 0.0).astype(BF16)
            near_ref[:, here] = dot(hot, block)
            return carry

        lax.fori_loop(0, count // tile, body, 0)

    def chunk(i, total):
        here = pl.ds(pl.multiple_of(i * 1024, 1024), 1024)
        gauge = lax.broadcasted_iota(jnp.int32, (1024, cols), 1) + pl.program_id(0) * cols
        hot = jnp.where(sub_ref[here, :] == gauge, 1.0, 0.0).astype(BF16)
        near = near_ref[:, here]
        high = near.astype(BF16)
        low = (near - high.astype(F32)).astype(BF16)
        return total + dot(high, hot) + dot(low, hot)

    total = lax.fori_loop(0, count // 1024, chunk, jnp.zeros((rows, cols), F32))
    high, low = pieces(total, 2)
    high_ref[...] = high
    low_ref[...] = low


def couple(first, row_gauge, gram, rows, gauges):
    count = row_gauge.shape[0]
    step = 256
    return pl.pallas_call(
        couple_kernel,
        grid=(gauges // step,),
        in_specs=[
            pl.BlockSpec(memory_space=pltpu.SMEM),
            pl.BlockSpec((1, count), lambda i: (0, 0)),
            pl.BlockSpec((count, 1), lambda i: (0, 0)),
            pl.BlockSpec(gram.shape, lambda i: (0, 0)),
        ],
        out_specs=[pl.BlockSpec((rows, step), lambda i: (0, i))] * 2,
        out_shape=[jax.ShapeDtypeStruct((rows, gauges), BF16)] * 2,
        scratch_shapes=[pltpu.VMEM((rows, count), F32)],
        compiler_params=params(56),
        name="couple",
    )(first, row_gauge.reshape(1, count), row_gauge.reshape(count, 1), gram)


def mix_kernel(high_ref, low_ref, value_ref, out_ref):
    high = high_ref[...]
    low = low_ref[...]
    one, two, three = pieces(value_ref[...], 3)
    out_ref[...] = (dot(high, three) + dot(low, two)) + (dot(high, two) + dot(low, one)) + dot(high, one)


def mix(high, low, value):
    return pl.pallas_call(
        mix_kernel,
        out_shape=jax.ShapeDtypeStruct((high.shape[0], value.shape[1]), F32),
        compiler_params=params(56),
        name="mix",
    )(high, low, value)


def spectrum_kernel(class_ref, kernels_ref, forward_ref, out_ref):
    rows = class_ref.shape[0]
    classes, taps = kernels_ref.shape
    kind = lax.broadcasted_iota(jnp.int32, (rows, classes), 1)
    hot = jnp.where(class_ref[...] == kind, 1.0, 0.0)
    out_ref[...] = exact(exact(hot, kernels_ref[...]), forward_ref[pl.ds(0, taps), :])


def spectrum(gauge_kernel, kernels, forward):
    rows = gauge_kernel.shape[0]
    return pl.pallas_call(
        spectrum_kernel,
        out_shape=jax.ShapeDtypeStruct((rows, SPAN), F32),
        compiler_params=params(56),
        name="spectrum",
    )(gauge_kernel.reshape(rows, 1), kernels, forward)


def delayed(before, here, after, spec, forward, inverse_last):
    rows, half = here.shape
    stacked = jnp.concatenate(
        [jnp.concatenate([before, here], axis=1), jnp.concatenate([here, after], axis=1)], axis=0
    )
    waves = exact(stacked, forward)
    real, imag = waves[:, :half], waves[:, half:]
    kr = jnp.concatenate([spec[:, :half]] * 2, axis=0)
    ki = jnp.concatenate([spec[:, half:]] * 2, axis=0)
    turned = jnp.concatenate([real * kr - imag * ki, real * ki + imag * kr], axis=1)
    out = exact(turned, inverse_last)
    return out[:rows], out[rows:]


def advanced(here, after, spec, forward, inverse_first):
    half = here.shape[1]
    waves = exact(jnp.concatenate([here, after], axis=1), forward)
    real, imag = waves[:, :half], waves[:, half:]
    kr, ki = spec[:, :half], spec[:, half:]
    turned = jnp.concatenate([real * kr + imag * ki, imag * kr - real * ki], axis=1)
    return exact(turned, inverse_first)


def lanes(a, b):
    return jnp.sum(a * b, axis=0, keepdims=True)


def total(ref, row):
    return jnp.sum(ref[row : row + 1, :], axis=1, keepdims=True)


def ratios(ref):
    square = total(ref, 0)
    alpha = jnp.sqrt(square)
    beta = jnp.sqrt(jnp.maximum(total(ref, 1) / square - 2.0 * total(ref, 2) + square, 0.0))
    return alpha, beta


def first_kernel(
    more_ref, sums_ref, observed_ref, spec_ref, forward_ref, first_ref, last_ref, out_ref, note_ref
):
    rows, half = observed_ref.shape[0] // 2, observed_ref.shape[1]
    spec, forward = spec_ref[...], forward_ref[...]
    before, here, after = (sums_ref[pl.ds(i * rows, rows), :] for i in range(3))
    now, later = delayed(before, here, after, spec, forward, last_ref[...])
    start = observed_ref[pl.ds(0, rows), :] - now
    start_later = (observed_ref[pl.ds(rows, rows), :] - later) * more_ref[0]
    out_ref[...] = advanced(start, start_later, spec, forward, first_ref[...])
    note_ref[...] = jnp.concatenate([lanes(start, start), jnp.zeros((7, half), F32)], axis=0)


def first_step(more, sums, observed, spec, mats):
    rows, half = spec.shape[0], observed.shape[1]
    return pl.pallas_call(
        first_kernel,
        in_specs=[pl.BlockSpec(memory_space=pltpu.SMEM)] + [pl.BlockSpec(memory_space=pltpu.VMEM)] * 6,
        out_shape=[jax.ShapeDtypeStruct((rows, half), F32), jax.ShapeDtypeStruct((8, half), F32)],
        compiler_params=params(56),
        name="first_step",
    )(more, sums, observed, spec, *mats)


def step_kernel(
    opening,
    final,
    more_ref,
    note_ref,
    sums_ref,
    spec_ref,
    forward_ref,
    first_ref,
    last_ref,
    pulled_ref,
    *refs,
):
    if opening:
        state_ref = None
    else:
        state_ref, *refs = refs
    if final:
        (out_note_ref,) = refs
    else:
        new_ref, out_ref, out_note_ref = refs
    rows, half = pulled_ref.shape
    spec, forward = spec_ref[...], forward_ref[...]
    if opening:
        scale = 1.0 / jnp.sqrt(total(note_ref, 0))
        along = sums_ref[...] * scale
        new_s, new_su = along, along
        new_zu = pulled_ref[...] * scale
        new_z = new_zu
    else:
        alpha, beta = ratios(note_ref)
        a, b, g = 1.0 / (alpha * beta), alpha / beta, beta / alpha
        wide = pl.ds(0, 3 * rows), pl.ds(3 * rows, 3 * rows)
        new_su = sums_ref[...] * a - state_ref[wide[1], :] * b
        new_s = new_su - state_ref[wide[0], :] * g
        new_zu = pulled_ref[...] * a - state_ref[pl.ds(7 * rows, rows), :] * b
        new_z = new_zu - state_ref[pl.ds(6 * rows, rows), :] * g
    before, here, after = (new_s[i * rows : (i + 1) * rows] for i in range(3))
    now, later = delayed(before, here, after, spec, forward, last_ref[...])
    out_note_ref[...] = jnp.concatenate(
        [lanes(new_z, here), lanes(now, now), lanes(new_zu, here), jnp.zeros((5, half), F32)], axis=0
    )
    if not final:
        new_ref[pl.ds(0, 3 * rows), :] = new_s
        new_ref[pl.ds(3 * rows, 3 * rows), :] = new_su
        new_ref[pl.ds(6 * rows, rows), :] = new_z
        new_ref[pl.ds(7 * rows, rows), :] = new_zu
        out_ref[...] = advanced(now, later * more_ref[0], spec, forward, first_ref[...])


def next_step(more, note, sums, spec, mats, pulled, state, final):
    rows, half = pulled.shape
    opening = state is None
    shapes = [
        jax.ShapeDtypeStruct((8 * rows, half), F32),
        jax.ShapeDtypeStruct((rows, half), F32),
        jax.ShapeDtypeStruct((8, half), F32),
    ]
    args = [more, note, sums, spec, *mats, pulled] + ([] if opening else [state])
    return pl.pallas_call(
        functools.partial(step_kernel, opening, final),
        in_specs=[pl.BlockSpec(memory_space=pltpu.SMEM)]
        + [pl.BlockSpec(memory_space=pltpu.VMEM)] * (len(args) - 1),
        out_shape=shapes[2:] if final else shapes,
        compiler_params=params(56),
        name="next_step",
    )(*args)


def weights_of(notes):
    start = jnp.sqrt(total(notes[0], 0))
    zero = jnp.zeros_like(start)
    units = [1.0 / start, zero, zero]
    z, zu = list(units), list(units)
    phibar = start
    alpha, beta = ratios(notes[1])
    rhobar = alpha
    w = [value / alpha for value in z]
    result = [zero] * 3
    steps = len(notes) - 1
    for k in range(steps):
        rho = jnp.sqrt(rhobar * rhobar + beta * beta)
        cosine, sine = rhobar / rho, beta / rho
        phi, phibar = cosine * phibar, sine * phibar
        result = [r + phi / rho * value for r, value in zip(result, w)]
        if k < steps - 1:
            a, b, g = 1.0 / (alpha * beta), alpha / beta, beta / alpha
            zu = [(a if i == k + 1 else 0.0) - b * value for i, value in enumerate(zu)]
            z = [value - g * old for value, old in zip(zu, z)]
            alpha, beta = ratios(notes[k + 2])
            theta = sine * alpha
            rhobar = -cosine * alpha
            w = [value / alpha - theta / rho * old for value, old in zip(z, w)]
    return result


def finish_kernel(n0, n1, n2, n3, gauge_ref, q0, q1, q2, inc_ref, field_ref, out_ref, rows_ref):
    blocks, slots, width = inc_ref.shape
    count = rows_ref.shape[0]
    gauges = q0.shape[0]
    step = pl.program_id(0)

    @pl.when(step == 0)
    def _():
        e0, e1, e2 = weights_of([n0, n1, n2, n3])
        width_ = 512

        def body(i, value):
            here = pl.ds(pl.multiple_of(i * width_, width_), width_)
            mixed = q0[here, :] * e0 + q1[here, :] * e1 + q2[here, :] * e2
            gauge = lax.broadcasted_iota(jnp.int32, (count, width_), 1) + i * width_
            hot = jnp.where(gauge_ref[...] == gauge, 1.0, 0.0).astype(BF16)
            return value + pick(hot, mixed)

        rows_ref[...] = lax.fori_loop(0, gauges // width_, body, jnp.zeros(rows_ref.shape, F32))

    weights = inc_ref[...].astype(F32).astype(BF16)
    for b in range(blocks):
        here = pl.ds(b * width, width)
        rows = rows_ref[pl.ds(pl.multiple_of((step * blocks + b) * slots, slots), slots), :]
        added = sum(
            lax.dot_general(weights[b], piece, (((0,), (0,)), ((), ())), preferred_element_type=F32)
            for piece in pieces(rows, 3)
        )
        out_ref[here, :] = field_ref[here, :] + added


def finish(notes, row_gauge, gathered, incidence, field):
    blocks, slots, width = incidence.shape
    hours = field.shape[1]
    count = row_gauge.shape[0]
    step = 8
    whole = lambda shape: pl.BlockSpec(shape, lambda i: (0, 0))
    return pl.pallas_call(
        finish_kernel,
        grid=(blocks // step,),
        in_specs=[whole(n.shape) for n in notes]
        + [whole((count, 1))]
        + [whole(q.shape) for q in gathered]
        + [
            pl.BlockSpec((step, slots, width), lambda i: (i, 0, 0)),
            pl.BlockSpec((step * width, hours), lambda i: (i, 0)),
        ],
        out_specs=pl.BlockSpec((step * width, hours), lambda i: (i, 0)),
        out_shape=jax.ShapeDtypeStruct(field.shape, F32),
        scratch_shapes=[pltpu.VMEM((count, hours), F32)],
        compiler_params=params(56),
        name="finish",
    )(*notes, row_gauge.reshape(count, 1), *gathered, incidence, field)


def shifted(value, axis, by):
    devices = lax.axis_size(axis)
    pairs = [(i, i + by) for i in range(devices) if 0 <= i + by < devices]
    return lax.ppermute(value, axis, pairs)


def window(value):
    return jnp.concatenate([shifted(value, "tm", 1), value, shifted(value, "tm", -1)], axis=0)


def gathered_rows(value):
    owners = lax.axis_size("basin")
    copies = jnp.broadcast_to(value[None], (owners,) + value.shape)
    return lax.all_to_all(copies, "basin", 0, 0, tiled=False)


def over_hours(note):
    blocks = lax.axis_size("tm")
    result = note
    for by in range(1, blocks):
        result = result + lax.ppermute(note, "tm", [(i, (i + by) % blocks) for i in range(blocks)])
    return result


def shards(incidence, row_gauge, gauge_kernel, kernels, observed, first_guess):
    owners = lax.axis_size("basin")
    rows, hours = observed.shape
    gauges = rows * owners
    mats = transforms()
    spec = spectrum(gauge_kernel, kernels, mats[0])
    more = (lax.axis_index("tm") < lax.axis_size("tm") - 1).astype(F32).reshape(1)
    partial, gram = prepare(incidence, first_guess)
    all_gram = lax.all_gather(gram, "basin", axis=1, tiled=True)
    all_rows = lax.all_gather(row_gauge, "basin", axis=0, tiled=True)
    dense = table(row_gauge, partial, gauges).reshape(owners, rows, hours)
    sums = jnp.sum(lax.all_to_all(dense, "basin", 0, 0, tiled=False), axis=0)
    both = jnp.concatenate([observed, shifted(observed, "tm", -1)], axis=0)
    first = (lax.axis_index("basin") * rows).astype(jnp.int32).reshape(1)
    high, low = couple(first, all_rows, all_gram, rows, gauges)

    pulled, note = first_step(more, window(sums), both, spec, mats)
    notes, kept, state = [], [], None
    for k in range(3):
        everyone = gathered_rows(jnp.concatenate([pulled, note], axis=0))
        value = everyone[:, :rows].reshape(gauges, hours)
        notes.append(over_hours(jnp.sum(everyone[:, rows:], axis=0)))
        kept.append(value)
        around = window(mix(high, low, value))
        final = k == 2
        result = next_step(more, notes[-1], around, spec, mats, pulled, state, final)
        if final:
            (note,) = result
        else:
            state, pulled, note = result
    notes.append(over_hours(jnp.sum(gathered_rows(note), axis=0)))
    return finish(notes, row_gauge, kept, incidence, first_guess)


Z_, X_, Y_, C_ = 4, 2, 2, 2
NOTE = 8
HOURS = SPAN // 2


def device(z, x, y, c):
    return (z * X_ + x) * (Y_ * C_) + y * C_ + c


def moved(value, where):
    pairs = []
    for z, x, y, c in np.ndindex(Z_, X_, Y_, C_):
        target = where(z, x, y, c)
        if target is not None:
            pairs.append((device(z, x, y, c), device(*target)))
    return lax.ppermute(value, ("basin", "tm"), pairs)


def to_plane(z, x, y, c):
    return 2 * y + c, x, z & 1, z >> 1


def hour_before(z, x, y, c):
    t = 2 * y + c - 1
    return (z, x, t >> 1, t & 1) if t >= 0 else None


def from_plane(z, x, y, c):
    return 2 * c + y, x, z >> 1, z & 1


def over_x(z, x, y, c):
    return z, 1 - x, y, c


def over_y(z, x, y, c):
    return z, x, 1 - y, c


def over_xy(z, x, y, c):
    return z, 1 - x, 1 - y, c


def over_core(z, x, y, c):
    return z, x, y, 1 - c


def z_pair(z, x, y, c):
    return z ^ 1, x, y, c


def z_middle(z, x, y, c):
    return (3 - z, x, y, c) if z in (1, 2) else None


def z_two(z, x, y, c):
    return z ^ 2, x, y, c


def z_mirror(z, x, y, c):
    return 3 - z, x, y, c


def z_next(z, x, y, c):
    return (z + 1, x, y, c) if z < 3 else None


SQUARE = (over_x, over_y, over_xy)


def split_constant(value):
    out = []
    for _ in range(3):
        piece = value.astype(jnp.bfloat16)
        out.append(piece)
        value = value - piece.astype(np.float64)
    return out


ORDERS = {2: ((0, 1), (1, 0), (0, 0)), 3: ((0, 2), (1, 1), (2, 0), (0, 1), (1, 0), (0, 0))}


def widened(mat, order):
    parts = split_constant(mat)
    return jnp.asarray(np.concatenate([parts[i] for i, _ in ORDERS[order]], axis=1))


def product(wide, value, order):
    parts = pieces(value, order)
    return dot(wide, jnp.concatenate([parts[j] for _, j in ORDERS[order]], axis=0))


def turned_transforms(order):
    half = SPAN // 2
    freq = 2.0 * np.pi * (np.arange(half) + 0.5) / SPAN
    phase = freq[:, None] * np.arange(SPAN)[None, :]
    forward = np.concatenate([np.cos(phase), -np.sin(phase)], axis=0)
    inverse = forward.T * (2.0 / SPAN)
    return [widened(mat, order) for mat in (forward, inverse[:half], inverse[half:], forward[:, :half])]


def turn(waves, spec, sign):
    half = waves.shape[0] // 2
    real, imag = waves[:half], waves[half:]
    kr, ki = spec[:half], spec[half:] * sign
    return jnp.concatenate([real * kr - imag * ki, real * ki + imag * kr], axis=0)


def plane_delayed(before, here, after, spec, forward, last, order):
    rows = here.shape[1]
    pairs = [jnp.concatenate(pair, axis=0) for pair in ((before, here), (here, after))]
    waves = product(forward, jnp.concatenate(pairs, axis=1), order)
    turned = [turn(waves[:, i * rows : (i + 1) * rows], spec, 1.0) for i in range(2)]
    out = product(last, jnp.concatenate(turned, axis=1), order)
    return out[:, :rows], out[:, rows:]


def plane_advanced(here, after, spec, forward, first, order):
    waves = product(forward, jnp.concatenate([here, after], axis=0), order)
    return product(first, turn(waves, spec, -1.0), order)


def describe_kernel(inc_ref, gauge_ref, out_ref):
    blocks, slots, width = inc_ref.shape
    tile = 8
    side = tile * slots
    weights = inc_ref[...].astype(F32).astype(BF16)
    row = lax.broadcasted_iota(jnp.int32, (side, side), 0)
    col = lax.broadcasted_iota(jnp.int32, (side, side), 1)
    same = row // slots == col // slots
    for i in range(blocks // tile):
        flat = weights[i * tile : (i + 1) * tile].reshape(side, width)
        full = lax.dot_general(flat, flat, (((1,), (1,)), ((), ())), preferred_element_type=F32)
        own = jnp.where(same, full, 0.0)
        out_ref[pl.ds(0, slots), pl.ds(i * side, side)] = jnp.sum(own.reshape(tile, slots, side), axis=0)
    out_ref[pl.ds(slots, 8), :] = jnp.broadcast_to(gauge_ref[...].astype(F32), (8, blocks * slots))


def describe(incidence, row_gauge):
    blocks, slots, _ = incidence.shape
    count = blocks * slots
    return pl.pallas_call(
        describe_kernel,
        out_shape=jax.ShapeDtypeStruct((slots + 8, count), F32),
        compiler_params=params(),
        name="describe",
        cost_estimate=SMALL,
    )(incidence, row_gauge.reshape(1, count))


def send_kernel(
    inc_hbm, field_hbm, gauge_hbm, kind_hbm, out_ref, inc_ref, field_ref, gauge_ref, kind_ref, sems, label_sems
):
    blocks, slots, width = inc_ref.shape
    chunks = sems.shape[0]
    step = blocks // chunks
    copies = []
    for i in range(chunks):
        near = pl.ds(i * step, step)
        far = pl.ds(i * step * width, step * width)
        copies.append(
            (
                pltpu.make_async_copy(inc_hbm.at[near], inc_ref.at[near], sems.at[i, 0]),
                pltpu.make_async_copy(field_hbm.at[far], field_ref.at[far], sems.at[i, 1]),
            )
        )
        for copy in copies[-1]:
            copy.start()
    labels = (
        pltpu.make_async_copy(gauge_hbm, gauge_ref, label_sems.at[0]),
        pltpu.make_async_copy(kind_hbm, kind_ref, label_sems.at[1]),
    )
    for copy in labels:
        copy.start()
    for i in range(chunks):
        for copy in copies[i]:
            copy.wait()
        parts = []
        for b in range(i * step, (i + 1) * step):
            weight = inc_ref[b].astype(F32).astype(BF16)
            value = jnp.concatenate(pieces(field_ref[pl.ds(b * width, width), :], 3)[::-1], axis=0)
            parts.append(dot(jnp.concatenate([weight] * 3, axis=1), value))
        out_ref[pl.ds(0, HOURS), pl.ds(i * step * slots, step * slots)] = jnp.transpose(
            jnp.concatenate(parts, axis=0)
        )
    for copy in labels:
        copy.wait()
    count, kinds = gauge_ref.shape[1], kind_ref.shape[1]
    kind = jnp.concatenate([kind_ref[...].astype(F32), jnp.zeros((1, count - kinds), F32)], axis=1)
    out_ref[pl.ds(HOURS, 8), :] = jnp.concatenate(
        [gauge_ref[...].astype(F32), kind, jnp.zeros((6, count), F32)], axis=0
    )


def send(incidence, field, row_gauge, gauge_kernel):
    count, rows = row_gauge.shape[0], gauge_kernel.shape[0]
    chunks = 4
    return pl.pallas_call(
        send_kernel,
        in_specs=[pl.BlockSpec(memory_space=pltpu.HBM)] * 4,
        out_shape=jax.ShapeDtypeStruct((HOURS + 8, count), F32),
        scratch_shapes=[
            pltpu.VMEM(incidence.shape, incidence.dtype),
            pltpu.VMEM(field.shape, F32),
            pltpu.VMEM((1, count), row_gauge.dtype),
            pltpu.VMEM((1, rows), gauge_kernel.dtype),
            pltpu.SemaphoreType.DMA((chunks, 2)),
            pltpu.SemaphoreType.DMA((2,)),
        ],
        compiler_params=params(60),
        name="send",
        cost_estimate=SMALL,
    )(incidence, field, row_gauge.reshape(1, count), gauge_kernel.reshape(1, rows))


def hot_rows(gauge, first, rows):
    mine = (lax.broadcasted_iota(jnp.int32, (rows, gauge.shape[1]), 0) + first).astype(F32)
    return jnp.where(gauge == mine, 1.0, 0.0).astype(BF16)


def spread_kernel(first_ref, mine_ref, other_ref, *out_refs):
    rows = out_refs[0].shape[1]
    both = jnp.concatenate([mine_ref[...], other_ref[...]], axis=1)
    stacked = jnp.concatenate(pieces(both[:HOURS], 3), axis=0)
    for m, out_ref in enumerate(out_refs):
        hot = hot_rows(both[HOURS : HOURS + 1], first_ref[m], rows)
        result = lax.dot_general(stacked, hot, (((1,), (1,)), ((), ())), preferred_element_type=F32)
        out_ref[...] = (result[2 * HOURS :] + result[HOURS : 2 * HOURS]) + result[:HOURS]


def spread(first, parcels, rows):
    return pl.pallas_call(
        spread_kernel,
        in_specs=[pl.BlockSpec(memory_space=pltpu.SMEM)] + [pl.BlockSpec(memory_space=pltpu.VMEM)] * 2,
        out_shape=[jax.ShapeDtypeStruct((HOURS, rows), F32)] * 4,
        compiler_params=params(),
        name="spread",
        cost_estimate=SMALL,
    )(first, *parcels)


def plane_couple_kernel(last, first_ref, *refs):
    if last:
        all_ref, before_ref, high_ref, low_ref, total_ref, meta_ref = refs
        total_ref[...] = before_ref[...]
    else:
        all_ref, total_ref, meta_ref = refs
        total_ref[...] = jnp.zeros_like(total_ref)
    parts, height, count = meta_ref.shape
    slots = height - 8
    cols, rows = total_ref.shape
    tile = 256
    for i in range(parts):
        meta_ref[i] = all_ref[:, i * count : (i + 1) * count]
    row = lax.broadcasted_iota(jnp.int32, (tile, tile), 0)
    col = lax.broadcasted_iota(jnp.int32, (tile, tile), 1)
    same = row // slots == col // slots

    def body(i, carry):
        gauge = meta_ref[i, slots : slots + 1, :]
        near = []
        for j in range(count // tile):
            here = slice(j * tile, (j + 1) * tile)
            block = jnp.concatenate([meta_ref[i, :slots, here]] * (tile // slots), axis=0)
            block = jnp.where(same, block, 0.0).astype(BF16)
            mine = jnp.concatenate(
                [hot_rows(gauge[:, here], first_ref[4 + h], rows // 2) for h in range(2)], axis=0
            )
            near.append(
                lax.dot_general(block, mine, (((1,), (1,)), ((), ())), preferred_element_type=F32)
            )
        near = jnp.concatenate(near, axis=0)
        high = near.astype(BF16)
        rest = near - high.astype(F32)
        hot = jnp.concatenate([hot_rows(gauge, first_ref[m], cols // 4) for m in range(4)], axis=0)
        total_ref[...] += dot(hot, high)

        @pl.when(jnp.max(jnp.abs(rest)) > 0.0)
        def _():
            total_ref[...] += dot(hot, rest.astype(BF16))

        return carry

    lax.fori_loop(0, parts, body, 0)
    if last:
        high, low = pieces(total_ref[...], 2)
        high_ref[...] = high
        low_ref[...] = low


def plane_couple(first, meta, rows, before=None):
    height, wide = meta.shape
    parts = 2 * X_
    shape = (4 * rows, 2 * rows)
    last = before is not None
    args = [first, meta] + ([before] if last else [])
    scratch = [pltpu.VMEM((parts, height, wide // parts), F32)]
    return pl.pallas_call(
        functools.partial(plane_couple_kernel, last),
        in_specs=[pl.BlockSpec(memory_space=pltpu.SMEM)]
        + [pl.BlockSpec(memory_space=pltpu.VMEM)] * (len(args) - 1),
        out_shape=[jax.ShapeDtypeStruct(shape, BF16)] * 2 if last else jax.ShapeDtypeStruct(shape, F32),
        scratch_shapes=([pltpu.VMEM(shape, F32)] if last else []) + scratch,
        compiler_params=params(),
        name="plane_couple",
        cost_estimate=pl.CostEstimate(
            flops=2 * 8 * wide * rows * rows, bytes_accessed=2_000_000, transcendentals=0
        ),
    )(*args)


def plane_mix_kernel(high_ref, low_ref, a_ref, b_ref, c_ref, d_ref, *refs):
    *extra, mine_ref, other_ref = refs
    refs = (a_ref, b_ref, c_ref, d_ref)
    height, rows = a_ref.shape
    body = pl.ds(0, HOURS)
    one, two = pieces(jnp.concatenate([ref[body, :] for ref in refs], axis=1), 2)
    both = dot(jnp.concatenate([two, one], axis=0), high_ref[...])
    result = (both[:HOURS] + dot(one, low_ref[...])) + both[HOURS:]
    mine_ref[body, :] = result[:, :rows]
    other_ref[body, :] = result[:, rows:]
    if height > HOURS:
        tail = pl.ds(HOURS, NOTE)
        note = sum(ref[tail, :] for ref in refs)
        mine_ref[tail, :] = note
        other_ref[tail, :] = note
    for ref in extra:
        other_ref[pl.ds(height, ref.shape[0]), :] = ref[...]


def plane_mix(coupling, values, extra):
    height, rows = values[0].shape
    return pl.pallas_call(
        plane_mix_kernel,
        out_shape=[
            jax.ShapeDtypeStruct((height, rows), F32),
            jax.ShapeDtypeStruct((height + sum(value.shape[0] for value in extra), rows), F32),
        ],
        compiler_params=params(),
        name="plane_mix",
        cost_estimate=SMALL,
    )(*coupling, *values, *extra)


def plane_rows_kernel(first_ref, meta_ref, meta_other_ref, a_ref, b_ref, c_ref, d_ref, *refs):
    if len(refs) > 2:
        *stack, last_ref, beside_ref, mine_ref, other_ref, stack_ref = refs
    else:
        mine_ref, other_ref = refs
    rows = a_ref.shape[1]
    value = jnp.concatenate([ref[pl.ds(0, HOURS), :] for ref in (a_ref, b_ref, c_ref, d_ref)], axis=1)
    one, two = pieces(value, 2)
    stacked = jnp.concatenate([two, one], axis=0)
    picked = []
    for ref in (meta_ref, meta_other_ref):
        gauge = ref[0:1, :]
        hot = jnp.concatenate([hot_rows(gauge, first_ref[m], rows) for m in range(4)], axis=0)
        both = dot(stacked, hot)
        picked.append(both[:HOURS] + both[HOURS:])
    mine_ref[...] = picked[0]
    count = picked[1].shape[1] // rows
    for i in range(count):
        other_ref[pl.ds(i * HOURS, HOURS), :] = picked[1][:, i * rows : (i + 1) * rows]
    if len(refs) > 2:
        top = stack_ref.shape[0] - HOURS
        for ref in stack:
            stack_ref[pl.ds(0, top), :] = ref[...]
        for i in range(count):
            here = pl.ds(i * rows, rows)
            beside = beside_ref[pl.ds(beside_ref.shape[0] - (count - i) * HOURS, HOURS), :]
            stack_ref[pl.ds(top, HOURS), here] = last_ref[:, here] + beside


def plane_rows(first, metas, values, before):
    rows = values[0].shape[1]
    slots = metas[0].shape[1]
    args = [first, *metas, *values, *before]
    shapes = [(HOURS, slots), (slots // rows * HOURS, rows)]
    if before:
        shapes.append(((len(before) - 1) * HOURS, slots))
    return pl.pallas_call(
        plane_rows_kernel,
        in_specs=[pl.BlockSpec(memory_space=pltpu.SMEM)]
        + [pl.BlockSpec(memory_space=pltpu.VMEM)] * (len(args) - 1),
        out_shape=[jax.ShapeDtypeStruct(shape, F32) for shape in shapes],
        compiler_params=params(),
        name="plane_rows",
        cost_estimate=pl.CostEstimate(flops=1_000_000_000, bytes_accessed=2_000_000, transcendentals=0),
    )(*args)


def gain(kernels):
    return jnp.max(jnp.sum(kernels, axis=1, keepdims=True), axis=0, keepdims=True)


def spectra(kind, kernels, wide):
    classes = kernels.shape[0]
    row = lax.broadcasted_iota(jnp.int32, (classes, kind.shape[1]), 0).astype(F32)
    hot = jnp.where(row == kind, 1.0, 0.0).astype(BF16)
    taps = jnp.transpose(kernels / gain(kernels))
    chosen = dot(jnp.concatenate(pieces(taps, 3)[::-1], axis=1), jnp.concatenate([hot] * 3, axis=0))
    return product(wide, chosen, 3)


def plane_spectrum_kernel(class_ref, kernels_ref, wide_ref, out_ref):
    kind = class_ref[1:2, : out_ref.shape[1]]
    out_ref[...] = spectra(kind, kernels_ref[...], wide_ref[...])


def plane_spectrum(meta, kernels, wide, rows):
    return pl.pallas_call(
        plane_spectrum_kernel,
        out_shape=jax.ShapeDtypeStruct((SPAN, rows), F32),
        compiler_params=params(),
        name="plane_spectrum",
        cost_estimate=SMALL,
    )(meta, kernels, wide)


def sides(even, pair, middle):
    return jnp.where(even, middle, pair), jnp.where(even, pair, middle)


def plane_call(kernel, name, shapes, flags, args):
    return pl.pallas_call(
        kernel,
        in_specs=[pl.BlockSpec(memory_space=pltpu.SMEM)] * len(flags)
        + [pl.BlockSpec(memory_space=pltpu.VMEM)] * len(args),
        out_shape=[jax.ShapeDtypeStruct(shape, F32) for shape in shapes],
        compiler_params=params(),
        name=name,
        cost_estimate=SMALL,
    )(*flags, *args)


def plane_first_kernel(
    flag_ref, here_ref, pair_ref, middle_ref, spec_ref, kernels_ref, forward, first, last, out_ref
):
    spec = spec_ref[...]
    before, after = sides(flag_ref[0] > 0.5, pair_ref[...], middle_ref[...])
    here = here_ref[...]
    both = plane_delayed(before[:HOURS], here[:HOURS], after[:HOURS], spec, forward[...], last[...], 3)
    scale = gain(kernels_ref[...])
    now = here[HOURS:] - both[0] * scale
    later = (after[HOURS:] - both[1] * scale) * flag_ref[1]
    out_ref[...] = plane_advanced(now, later, spec, forward[...], first[...], 3)


def plane_delay_kernel(flag_ref, here_ref, pair_ref, middle_ref, spec_ref, forward, last, out_ref):
    body = pl.ds(0, HOURS)
    before, after = sides(flag_ref[0] > 0.5, pair_ref[body, :], middle_ref[body, :])
    out = plane_delayed(before, here_ref[body, :], after, spec_ref[...], forward[...], last[...], 2)
    for i in range(2):
        out_ref[pl.ds(i * HOURS, HOURS), :] = out[i]


def write_note(ref, rows):
    tail = [jnp.zeros((NOTE - len(rows), ref.shape[1]), F32)]
    ref[pl.ds(HOURS, NOTE), :] = jnp.concatenate(rows + tail, axis=0)


def plane_open_kernel(
    flag_ref, here_ref, pair_ref, middle_ref, pulled_ref, spec_ref, forward, first, last, out_ref, delayed_ref
):
    here = here_ref[...]
    spec = spec_ref[...]
    before, after = sides(flag_ref[0] > 0.5, pair_ref[...], middle_ref[...])
    now, later = plane_delayed(before, here, after, spec, forward[...], last[...], 2)
    out_ref[pl.ds(0, HOURS), :] = plane_advanced(now, later * flag_ref[1], spec, forward[...], first[...], 2)
    write_note(out_ref, [lanes(pulled_ref[...], here), lanes(now, now)])
    delayed_ref[pl.ds(0, HOURS), :] = now
    delayed_ref[pl.ds(HOURS, HOURS), :] = later


def plane_step_kernel(
    flag_ref,
    here_ref,
    pair_ref,
    two_ref,
    mirror_ref,
    pulled_ref,
    delayed_ref,
    old_z_ref,
    old_s_ref,
    old_delayed_ref,
    spec_ref,
    forward,
    first,
    total_ref,
    out_ref,
    kept_ref,
):
    tail, body = pl.ds(HOURS, NOTE), pl.ds(0, HOURS)
    total_ref[...] = (here_ref[tail, :] + pair_ref[tail, :]) + (two_ref[...] + mirror_ref[...])
    inverse = total(total_ref, 0) / total(total_ref, 1)
    z = pulled_ref[body, :] * inverse - old_z_ref[...]
    s = here_ref[body, :] * inverse - old_s_ref[...]
    both = delayed_ref[...] * inverse - old_delayed_ref[...]
    now, later = both[:HOURS], both[HOURS:]
    following = plane_advanced(now, later * flag_ref[1], spec_ref[...], forward[...], first[...], 2)
    out_ref[body, :] = following * inverse
    write_note(out_ref, [lanes(z, s), lanes(now, now)])
    for i, value in enumerate((z, s, now)):
        kept_ref[pl.ds(i * HOURS, HOURS), :] = value


def plane_close_kernel(
    here_ref, before_ref, pulled_ref, kept_ref, old_z_ref, old_s_ref, old_delayed_ref, spec_ref, forward, last, out_ref
):
    body = pl.ds(0, HOURS)
    here, raw = here_ref[body, :], pulled_ref[body, :]
    waves = product(forward[...], jnp.concatenate([before_ref[body, :], here], axis=0), 2)
    now = product(last[...], turn(waves, spec_ref[...], 1.0), 2)
    z, s, delayed = (kept_ref[pl.ds(i * HOURS, HOURS), :] for i in range(3))
    note = [pulled_ref[HOURS + i : HOURS + i + 1, :] for i in range(2)]
    for left in (raw, z, old_z_ref[...]):
        note += [lanes(left, right) for right in (here, s, old_s_ref[...])]
    parts = (now, delayed, old_delayed_ref[body, :])
    for i in range(3):
        note += [lanes(parts[i], parts[j]) for j in range(i, 3)]
    note.append(jnp.zeros((24 - len(note), here.shape[1]), F32))
    note = jnp.sum(jnp.concatenate(note, axis=0), axis=1, keepdims=True)
    shape = (24, out_ref.shape[2])
    row, col = (lax.broadcasted_iota(jnp.int32, shape, i) for i in range(2))
    note = jnp.sum(jnp.where(row == col, jnp.broadcast_to(note, shape), 0.0), axis=0, keepdims=True)
    out_ref[...] = jnp.broadcast_to(note[None], out_ref.shape)


def plane_weights(open_ref, close, scale):
    entry = lambda i: close[:, i : i + 1]
    n1, t1 = total(open_ref, 0), total(open_ref, 1)
    n2, t2 = entry(0), entry(1)
    a1 = t1 / n1
    a2, r2 = (t2 / n2) / a1, n2 / n1
    plain = (1.0, -a2, -r2)
    n3 = sum(plain[i] * plain[j] * entry(2 + 3 * i + j) for i in range(3) for j in range(3))
    pairs = [(i, j) for i in range(3) for j in range(i, 3)]
    t3 = sum(
        plain[i] * plain[j] * entry(11 + n) * (1.0 if i == j else 2.0) for n, (i, j) in enumerate(pairs)
    )
    a3, r3 = (t3 / n3) / a1, n3 / n2
    unit = 1.0 / (a1 * scale)
    c3 = unit / (a3 * (a2 - r2) - r3)
    c2 = -a3 * c3
    c1 = unit - r2 * c2
    step = c2 - c3 * a2
    return c1 - step - c3 * r2, step / a1, c3


def plane_combine_kernel(open_ref, close_ref, kernels_ref, stack_ref, mine_ref, beside_ref, out_ref):
    rows = open_ref.shape[1]
    close = jnp.sum(close_ref[...], axis=0)[0:1, :]
    e0, e1, e2 = plane_weights(open_ref, close, gain(kernels_ref[...]))
    for i in range(out_ref.shape[0] // rows):
        here = pl.ds(i * rows, rows)
        last = mine_ref[:, here] + beside_ref[pl.ds(i * HOURS, HOURS), :]
        value = stack_ref[pl.ds(0, HOURS), here] * e0 + stack_ref[pl.ds(HOURS, HOURS), here] * e1 + last * e2
        out_ref[here, :] = jnp.transpose(value)


def plane_finish_kernel(rows_ref, inc_ref, field_ref, out_ref):
    blocks, slots, width = inc_ref.shape
    weights = inc_ref[...].astype(F32).astype(BF16)
    for b in range(blocks):
        here = pl.ds(b * width, width)
        rows = jnp.concatenate(pieces(rows_ref[pl.ds(b * slots, slots), :], 2), axis=0)
        twice = jnp.concatenate([weights[b]] * 2, axis=0)
        added = lax.dot_general(twice, rows, (((0,), (0,)), ((), ())), preferred_element_type=F32)
        out_ref[here, :] = field_ref[here, :] + added


def plane_finish(rows, incidence, field):
    blocks, slots, width = incidence.shape
    hours = field.shape[1]
    step = 8
    return pl.pallas_call(
        plane_finish_kernel,
        grid=(blocks // step,),
        in_specs=[
            pl.BlockSpec((step * slots, hours), lambda i: (i, 0)),
            pl.BlockSpec((step, slots, width), lambda i: (i, 0, 0)),
            pl.BlockSpec((step * width, hours), lambda i: (i, 0)),
        ],
        out_specs=pl.BlockSpec((step * width, hours), lambda i: (i, 0)),
        out_shape=jax.ShapeDtypeStruct(field.shape, F32),
        compiler_params=params(),
        name="plane_finish",
    )(rows, incidence, field)


def plane_shards(incidence, row_gauge, gauge_kernel, kernels, observed, first_guess):
    rows, hours = observed.shape
    basin, tm = lax.axis_index("basin"), lax.axis_index("tm")
    z, x, y, c = basin // X_, basin % X_, tm // C_, tm % C_
    place = 2 * y + x
    first = jnp.stack([4 * c + (place ^ m) for m in range(4)] + [4 * c + place, 4 * (1 - c) + place])
    first = (first * rows).astype(jnp.int32)
    flags = jnp.stack([1 - z % 2, (z < Z_ - 1).astype(z.dtype), (z > 0).astype(z.dtype)]).astype(F32)
    forward, inverse_first, inverse_last, _ = turned_transforms(2)
    forward3, inverse_first3, inverse_last3, short3 = turned_transforms(3)
    block, noted = (hours, rows), (hours + NOTE, rows)

    seen = moved(observed, to_plane)
    parcel = send(incidence, first_guess, row_gauge, gauge_kernel)
    parcel, near = lax.optimization_barrier((parcel, incidence))
    parcel = moved(parcel, to_plane)
    near, seen = lax.optimization_barrier((near, seen))
    meta = describe(near, row_gauge)
    meta = jnp.concatenate([meta, moved(meta, over_x)], axis=1)
    meta = jnp.concatenate([meta, moved(meta, z_pair)], axis=1)
    parcel, seen = lax.optimization_barrier((parcel, seen))
    parcels = [parcel, moved(parcel, over_core)]
    spec = plane_spectrum(parcel[hours:], kernels, short3, rows)
    parcels[1], seen, meta, spec = lax.optimization_barrier((parcels[1], seen, meta, spec))
    half = meta.shape[1] // 2
    far = moved(jnp.where(c == 0, meta[:, :half], meta[:, half:]), z_two)
    dense = spread(first, parcels, rows)
    metas = [value[hours:] for value in parcels]
    sums = dense[0] + sum(moved(value, where) for value, where in zip(dense[1:], SQUARE))
    sums, far = lax.optimization_barrier((sums, far))
    around = [meta, jnp.concatenate([far, moved(far, over_core)], axis=1)]
    sums = jnp.concatenate([sums, jnp.transpose(seen)], axis=0)
    sums = [sums, moved(sums, z_pair), moved(sums, z_middle)]
    coupled = plane_couple(first, around[0], rows)
    coupled, sums = lax.optimization_barrier((coupled, sums))
    coupling = plane_couple(first, around[1], rows, coupled)
    (pulled0,) = plane_call(
        plane_first_kernel,
        "plane_first",
        [block],
        [flags],
        [*sums, spec, kernels, forward3, inverse_first3, inverse_last3],
    )

    def mixing(pulled, extra):
        values = [pulled] + [moved(pulled, where) for where in SQUARE]
        mine, other = plane_mix(coupling, values, extra)
        beside = moved(other, over_core)
        return values, mine + beside[: pulled.shape[0]], beside

    values, mixed0, _ = mixing(pulled0, [])
    picked, theirs = plane_rows(first, metas, values, [])
    sums = [mixed0, moved(mixed0, z_pair), moved(mixed0, z_middle)]
    pulled1, delayed0 = plane_call(
        plane_open_kernel,
        "plane_open",
        [noted, (2 * hours, rows)],
        [flags],
        [*sums, pulled0, spec, forward, inverse_first, inverse_last],
    )

    values, mixed1, beside = mixing(pulled1, [theirs])
    picked, theirs, stack = plane_rows(first, metas, values, [picked, beside])
    sums = [mixed1, moved(mixed1, z_pair), moved(mixed1, z_middle)]
    two, mirror = moved(mixed1[hours:], z_two), moved(mixed1[hours:], z_mirror)
    (delayed1,) = plane_call(
        plane_delay_kernel, "plane_delay", [(2 * hours, rows)], [flags], [*sums, spec, forward, inverse_last]
    )
    open_note, pulled2, kept = plane_call(
        plane_step_kernel,
        "plane_step",
        [(NOTE, rows), noted, (3 * hours, rows)],
        [flags],
        [*sums[:2], two, mirror, pulled1, delayed1, pulled0, mixed0, delayed0, spec, forward, inverse_first],
    )

    values, mixed2, beside = mixing(pulled2, [theirs])
    picked, theirs, stack = plane_rows(first, metas, values, [stack, picked, beside])
    (note,) = plane_call(
        plane_close_kernel,
        "plane_close",
        [(Z_ * X_ * Y_ * C_, 8, rows // 2)],
        [],
        [mixed2, moved(mixed2, z_next), pulled2, kept, pulled0, mixed0, delayed0, spec, forward, inverse_last],
    )
    close_note = lax.all_to_all(note, ("basin", "tm"), 0, 0, tiled=False)
    (answer,) = plane_call(
        plane_combine_kernel,
        "plane_combine",
        [(parcel.shape[1], hours)],
        [],
        [open_note, close_note, kernels, stack, picked, moved(theirs, over_core)],
    )
    return plane_finish(moved(answer, from_plane), incidence, first_guess)


def solution(mesh):
    planes = dict(mesh.shape) == {"basin": Z_ * X_, "tm": Y_ * C_}
    in_specs = (
        P("basin", None, None),
        P("basin"),
        P("basin"),
        P(),
        P("basin", "tm"),
        P("basin", "tm"),
    )
    return jax.shard_map(
        plane_shards if planes else shards, mesh=mesh, in_specs=in_specs, out_specs=P("basin", "tm"), check_vma=False
    )
```

```python
import functools

import jax
import jax.numpy as jnp
import numpy as np
from jax import lax
from jax.experimental import pallas as pl
from jax.experimental.pallas import tpu as pltpu
from jax.sharding import PartitionSpec as P

F32 = jnp.float32
BF16 = jnp.bfloat16
HIGH = lax.Precision.HIGHEST
SPAN = 256
MIB = 1024 * 1024


SMALL = pl.CostEstimate(flops=1, bytes_accessed=1, transcendentals=0)


def params(mib=16):
    return pltpu.CompilerParams(vmem_limit_bytes=mib * MIB)


def transforms():
    half = SPAN // 2
    freq = 2.0 * np.pi * (np.arange(half) + 0.5) / SPAN
    phase = np.arange(SPAN)[:, None] * freq[None, :]
    forward = np.concatenate([np.cos(phase), -np.sin(phase)], axis=1)
    inverse = forward.T * (2.0 / SPAN)
    return (
        jnp.asarray(forward, F32),
        jnp.asarray(inverse[:, :half], F32),
        jnp.asarray(inverse[:, half:], F32),
    )


def dot(a, b):
    return jnp.dot(a, b, preferred_element_type=F32)


def exact(a, b):
    return jnp.dot(a, b, precision=HIGH, preferred_element_type=F32)


def pieces(value, count):
    out = []
    for _ in range(count):
        piece = value.astype(BF16)
        out.append(piece)
        value = value - piece.astype(F32)
    return out


def pick(hot, value):
    return sum(dot(hot, piece) for piece in pieces(value, 3))


def prepare_kernel(inc_ref, field_ref, partial_ref, gram_ref):
    blocks, slots, width = inc_ref.shape
    rows = blocks * slots
    weights = inc_ref[...].astype(F32).astype(BF16)
    for b in range(blocks):
        value = field_ref[pl.ds(b * width, width), :]
        partial_ref[pl.ds(b * slots, slots), :] = pick(weights[b], value)
    flat = weights.reshape(rows, width)
    full = lax.dot_general(flat, flat, (((1,), (1,)), ((), ())), preferred_element_type=F32)
    row = lax.broadcasted_iota(jnp.int32, (rows, rows), 0)
    col = lax.broadcasted_iota(jnp.int32, (rows, rows), 1)
    own = jnp.where(row // slots == col // slots, full, 0.0)
    gram_ref[...] = jnp.sum(own.reshape(blocks, slots, rows), axis=0)


def prepare(incidence, field):
    blocks, slots, width = incidence.shape
    hours = field.shape[1]
    step = 8
    return pl.pallas_call(
        prepare_kernel,
        grid=(blocks // step,),
        in_specs=[
            pl.BlockSpec((step, slots, width), lambda i: (i, 0, 0)),
            pl.BlockSpec((step * width, hours), lambda i: (i, 0)),
        ],
        out_specs=[
            pl.BlockSpec((step * slots, hours), lambda i: (i, 0)),
            pl.BlockSpec((slots, step * slots), lambda i: (0, i)),
        ],
        out_shape=[
            jax.ShapeDtypeStruct((blocks * slots, hours), F32),
            jax.ShapeDtypeStruct((slots, blocks * slots), F32),
        ],
        compiler_params=params(56),
        name="prepare",
    )(incidence, field)


def table_kernel(gauge_ref, partial_ref, out_ref):
    slots = partial_ref.shape[0]
    rows = out_ref.shape[0]
    first = pl.program_id(0) * rows
    gauge = lax.broadcasted_iota(jnp.int32, (rows, slots), 0) + first
    hot = jnp.where(gauge_ref[...] == gauge, 1.0, 0.0).astype(BF16)
    out_ref[...] = pick(hot, partial_ref[...])


def table(row_gauge, partial, gauges):
    slots, hours = partial.shape
    step = 256
    return pl.pallas_call(
        table_kernel,
        grid=(gauges // step,),
        in_specs=[
            pl.BlockSpec((1, slots), lambda i: (0, 0)),
            pl.BlockSpec((slots, hours), lambda i: (0, 0)),
        ],
        out_specs=pl.BlockSpec((step, hours), lambda i: (i, 0)),
        out_shape=jax.ShapeDtypeStruct((gauges, hours), F32),
        compiler_params=params(56),
        name="table",
    )(row_gauge.reshape(1, slots), partial)


def couple_kernel(first_ref, lane_ref, sub_ref, gram_ref, high_ref, low_ref, near_ref):
    slots = gram_ref.shape[0]
    count = lane_ref.shape[1]
    rows, cols = high_ref.shape
    tile = 256
    first = first_ref[0]

    @pl.when(pl.program_id(0) == 0)
    def _():
        row = lax.broadcasted_iota(jnp.int32, (tile, tile), 0)
        col = lax.broadcasted_iota(jnp.int32, (tile, tile), 1)
        same = row // slots == col // slots
        mine = lax.broadcasted_iota(jnp.int32, (rows, tile), 0) + first

        def body(i, carry):
            here = pl.ds(pl.multiple_of(i * tile, tile), tile)
            block = jnp.concatenate([gram_ref[:, here]] * (tile // slots), axis=0)
            block = jnp.where(same, block, 0.0).astype(BF16)
            hot = jnp.where(lane_ref[:, here] == mine, 1.0, 0.0).astype(BF16)
            near_ref[:, here] = dot(hot, block)
            return carry

        lax.fori_loop(0, count // tile, body, 0)

    def chunk(i, total):
        here = pl.ds(pl.multiple_of(i * 1024, 1024), 1024)
        gauge = lax.broadcasted_iota(jnp.int32, (1024, cols), 1) + pl.program_id(0) * cols
        hot = jnp.where(sub_ref[here, :] == gauge, 1.0, 0.0).astype(BF16)
        near = near_ref[:, here]
        high = near.astype(BF16)
        low = (near - high.astype(F32)).astype(BF16)
        return total + dot(high, hot) + dot(low, hot)

    total = lax.fori_loop(0, count // 1024, chunk, jnp.zeros((rows, cols), F32))
    high, low = pieces(total, 2)
    high_ref[...] = high
    low_ref[...] = low


def couple(first, row_gauge, gram, rows, gauges):
    count = row_gauge.shape[0]
    step = 256
    return pl.pallas_call(
        couple_kernel,
        grid=(gauges // step,),
        in_specs=[
            pl.BlockSpec(memory_space=pltpu.SMEM),
            pl.BlockSpec((1, count), lambda i: (0, 0)),
            pl.BlockSpec((count, 1), lambda i: (0, 0)),
            pl.BlockSpec(gram.shape, lambda i: (0, 0)),
        ],
        out_specs=[pl.BlockSpec((rows, step), lambda i: (0, i))] * 2,
        out_shape=[jax.ShapeDtypeStruct((rows, gauges), BF16)] * 2,
        scratch_shapes=[pltpu.VMEM((rows, count), F32)],
        compiler_params=params(56),
        name="couple",
    )(first, row_gauge.reshape(1, count), row_gauge.reshape(count, 1), gram)


def mix_kernel(high_ref, low_ref, value_ref, out_ref):
    high = high_ref[...]
    low = low_ref[...]
    one, two, three = pieces(value_ref[...], 3)
    out_ref[...] = (dot(high, three) + dot(low, two)) + (dot(high, two) + dot(low, one)) + dot(high, one)


def mix(high, low, value):
    return pl.pallas_call(
        mix_kernel,
        out_shape=jax.ShapeDtypeStruct((high.shape[0], value.shape[1]), F32),
        compiler_params=params(56),
        name="mix",
    )(high, low, value)


def spectrum_kernel(class_ref, kernels_ref, forward_ref, out_ref):
    rows = class_ref.shape[0]
    classes, taps = kernels_ref.shape
    kind = lax.broadcasted_iota(jnp.int32, (rows, classes), 1)
    hot = jnp.where(class_ref[...] == kind, 1.0, 0.0)
    out_ref[...] = exact(exact(hot, kernels_ref[...]), forward_ref[pl.ds(0, taps), :])


def spectrum(gauge_kernel, kernels, forward):
    rows = gauge_kernel.shape[0]
    return pl.pallas_call(
        spectrum_kernel,
        out_shape=jax.ShapeDtypeStruct((rows, SPAN), F32),
        compiler_params=params(56),
        name="spectrum",
    )(gauge_kernel.reshape(rows, 1), kernels, forward)


def delayed(before, here, after, spec, forward, inverse_last):
    rows, half = here.shape
    stacked = jnp.concatenate(
        [jnp.concatenate([before, here], axis=1), jnp.concatenate([here, after], axis=1)], axis=0
    )
    waves = exact(stacked, forward)
    real, imag = waves[:, :half], waves[:, half:]
    kr = jnp.concatenate([spec[:, :half]] * 2, axis=0)
    ki = jnp.concatenate([spec[:, half:]] * 2, axis=0)
    turned = jnp.concatenate([real * kr - imag * ki, real * ki + imag * kr], axis=1)
    out = exact(turned, inverse_last)
    return out[:rows], out[rows:]


def advanced(here, after, spec, forward, inverse_first):
    half = here.shape[1]
    waves = exact(jnp.concatenate([here, after], axis=1), forward)
    real, imag = waves[:, :half], waves[:, half:]
    kr, ki = spec[:, :half], spec[:, half:]
    turned = jnp.concatenate([real * kr + imag * ki, imag * kr - real * ki], axis=1)
    return exact(turned, inverse_first)


def lanes(a, b):
    return jnp.sum(a * b, axis=0, keepdims=True)


def total(ref, row):
    return jnp.sum(ref[row : row + 1, :], axis=1, keepdims=True)


def ratios(ref):
    square = total(ref, 0)
    alpha = jnp.sqrt(square)
    beta = jnp.sqrt(jnp.maximum(total(ref, 1) / square - 2.0 * total(ref, 2) + square, 0.0))
    return alpha, beta


def first_kernel(
    more_ref, sums_ref, observed_ref, spec_ref, forward_ref, first_ref, last_ref, out_ref, note_ref
):
    rows, half = observed_ref.shape[0] // 2, observed_ref.shape[1]
    spec, forward = spec_ref[...], forward_ref[...]
    before, here, after = (sums_ref[pl.ds(i * rows, rows), :] for i in range(3))
    now, later = delayed(before, here, after, spec, forward, last_ref[...])
    start = observed_ref[pl.ds(0, rows), :] - now
    start_later = (observed_ref[pl.ds(rows, rows), :] - later) * more_ref[0]
    out_ref[...] = advanced(start, start_later, spec, forward, first_ref[...])
    note_ref[...] = jnp.concatenate([lanes(start, start), jnp.zeros((7, half), F32)], axis=0)


def first_step(more, sums, observed, spec, mats):
    rows, half = spec.shape[0], observed.shape[1]
    return pl.pallas_call(
        first_kernel,
        in_specs=[pl.BlockSpec(memory_space=pltpu.SMEM)] + [pl.BlockSpec(memory_space=pltpu.VMEM)] * 6,
        out_shape=[jax.ShapeDtypeStruct((rows, half), F32), jax.ShapeDtypeStruct((8, half), F32)],
        compiler_params=params(56),
        name="first_step",
    )(more, sums, observed, spec, *mats)


def step_kernel(
    opening,
    final,
    more_ref,
    note_ref,
    sums_ref,
    spec_ref,
    forward_ref,
    first_ref,
    last_ref,
    pulled_ref,
    *refs,
):
    if opening:
        state_ref = None
    else:
        state_ref, *refs = refs
    if final:
        (out_note_ref,) = refs
    else:
        new_ref, out_ref, out_note_ref = refs
    rows, half = pulled_ref.shape
    spec, forward = spec_ref[...], forward_ref[...]
    if opening:
        scale = 1.0 / jnp.sqrt(total(note_ref, 0))
        along = sums_ref[...] * scale
        new_s, new_su = along, along
        new_zu = pulled_ref[...] * scale
        new_z = new_zu
    else:
        alpha, beta = ratios(note_ref)
        a, b, g = 1.0 / (alpha * beta), alpha / beta, beta / alpha
        wide = pl.ds(0, 3 * rows), pl.ds(3 * rows, 3 * rows)
        new_su = sums_ref[...] * a - state_ref[wide[1], :] * b
        new_s = new_su - state_ref[wide[0], :] * g
        new_zu = pulled_ref[...] * a - state_ref[pl.ds(7 * rows, rows), :] * b
        new_z = new_zu - state_ref[pl.ds(6 * rows, rows), :] * g
    before, here, after = (new_s[i * rows : (i + 1) * rows] for i in range(3))
    now, later = delayed(before, here, after, spec, forward, last_ref[...])
    out_note_ref[...] = jnp.concatenate(
        [lanes(new_z, here), lanes(now, now), lanes(new_zu, here), jnp.zeros((5, half), F32)], axis=0
    )
    if not final:
        new_ref[pl.ds(0, 3 * rows), :] = new_s
        new_ref[pl.ds(3 * rows, 3 * rows), :] = new_su
        new_ref[pl.ds(6 * rows, rows), :] = new_z
        new_ref[pl.ds(7 * rows, rows), :] = new_zu
        out_ref[...] = advanced(now, later * more_ref[0], spec, forward, first_ref[...])


def next_step(more, note, sums, spec, mats, pulled, state, final):
    rows, half = pulled.shape
    opening = state is None
    shapes = [
        jax.ShapeDtypeStruct((8 * rows, half), F32),
        jax.ShapeDtypeStruct((rows, half), F32),
        jax.ShapeDtypeStruct((8, half), F32),
    ]
    args = [more, note, sums, spec, *mats, pulled] + ([] if opening else [state])
    return pl.pallas_call(
        functools.partial(step_kernel, opening, final),
        in_specs=[pl.BlockSpec(memory_space=pltpu.SMEM)]
        + [pl.BlockSpec(memory_space=pltpu.VMEM)] * (len(args) - 1),
        out_shape=shapes[2:] if final else shapes,
        compiler_params=params(56),
        name="next_step",
    )(*args)


def weights_of(notes):
    start = jnp.sqrt(total(notes[0], 0))
    zero = jnp.zeros_like(start)
    units = [1.0 / start, zero, zero]
    z, zu = list(units), list(units)
    phibar = start
    alpha, beta = ratios(notes[1])
    rhobar = alpha
    w = [value / alpha for value in z]
    result = [zero] * 3
    steps = len(notes) - 1
    for k in range(steps):
        rho = jnp.sqrt(rhobar * rhobar + beta * beta)
        cosine, sine = rhobar / rho, beta / rho
        phi, phibar = cosine * phibar, sine * phibar
        result = [r + phi / rho * value for r, value in zip(result, w)]
        if k < steps - 1:
            a, b, g = 1.0 / (alpha * beta), alpha / beta, beta / alpha
            zu = [(a if i == k + 1 else 0.0) - b * value for i, value in enumerate(zu)]
            z = [value - g * old for value, old in zip(zu, z)]
            alpha, beta = ratios(notes[k + 2])
            theta = sine * alpha
            rhobar = -cosine * alpha
            w = [value / alpha - theta / rho * old for value, old in zip(z, w)]
    return result


def finish_kernel(n0, n1, n2, n3, gauge_ref, q0, q1, q2, inc_ref, field_ref, out_ref, rows_ref):
    blocks, slots, width = inc_ref.shape
    count = rows_ref.shape[0]
    gauges = q0.shape[0]
    step = pl.program_id(0)

    @pl.when(step == 0)
    def _():
        e0, e1, e2 = weights_of([n0, n1, n2, n3])
        width_ = 512

        def body(i, value):
            here = pl.ds(pl.multiple_of(i * width_, width_), width_)
            mixed = q0[here, :] * e0 + q1[here, :] * e1 + q2[here, :] * e2
            gauge = lax.broadcasted_iota(jnp.int32, (count, width_), 1) + i * width_
            hot = jnp.where(gauge_ref[...] == gauge, 1.0, 0.0).astype(BF16)
            return value + pick(hot, mixed)

        rows_ref[...] = lax.fori_loop(0, gauges // width_, body, jnp.zeros(rows_ref.shape, F32))

    weights = inc_ref[...].astype(F32).astype(BF16)
    for b in range(blocks):
        here = pl.ds(b * width, width)
        rows = rows_ref[pl.ds(pl.multiple_of((step * blocks + b) * slots, slots), slots), :]
        added = sum(
            lax.dot_general(weights[b], piece, (((0,), (0,)), ((), ())), preferred_element_type=F32)
            for piece in pieces(rows, 3)
        )
        out_ref[here, :] = field_ref[here, :] + added


def finish(notes, row_gauge, gathered, incidence, field):
    blocks, slots, width = incidence.shape
    hours = field.shape[1]
    count = row_gauge.shape[0]
    step = 8
    whole = lambda shape: pl.BlockSpec(shape, lambda i: (0, 0))
    return pl.pallas_call(
        finish_kernel,
        grid=(blocks // step,),
        in_specs=[whole(n.shape) for n in notes]
        + [whole((count, 1))]
        + [whole(q.shape) for q in gathered]
        + [
            pl.BlockSpec((step, slots, width), lambda i: (i, 0, 0)),
            pl.BlockSpec((step * width, hours), lambda i: (i, 0)),
        ],
        out_specs=pl.BlockSpec((step * width, hours), lambda i: (i, 0)),
        out_shape=jax.ShapeDtypeStruct(field.shape, F32),
        scratch_shapes=[pltpu.VMEM((count, hours), F32)],
        compiler_params=params(56),
        name="finish",
    )(*notes, row_gauge.reshape(count, 1), *gathered, incidence, field)


def shifted(value, axis, by):
    devices = lax.axis_size(axis)
    pairs = [(i, i + by) for i in range(devices) if 0 <= i + by < devices]
    return lax.ppermute(value, axis, pairs)


def window(value):
    return jnp.concatenate([shifted(value, "tm", 1), value, shifted(value, "tm", -1)], axis=0)


def gathered_rows(value):
    owners = lax.axis_size("basin")
    copies = jnp.broadcast_to(value[None], (owners,) + value.shape)
    return lax.all_to_all(copies, "basin", 0, 0, tiled=False)


def over_hours(note):
    blocks = lax.axis_size("tm")
    result = note
    for by in range(1, blocks):
        result = result + lax.ppermute(note, "tm", [(i, (i + by) % blocks) for i in range(blocks)])
    return result


def shards(incidence, row_gauge, gauge_kernel, kernels, observed, first_guess):
    owners = lax.axis_size("basin")
    rows, hours = observed.shape
    gauges = rows * owners
    mats = transforms()
    spec = spectrum(gauge_kernel, kernels, mats[0])
    more = (lax.axis_index("tm") < lax.axis_size("tm") - 1).astype(F32).reshape(1)
    partial, gram = prepare(incidence, first_guess)
    all_gram = lax.all_gather(gram, "basin", axis=1, tiled=True)
    all_rows = lax.all_gather(row_gauge, "basin", axis=0, tiled=True)
    dense = table(row_gauge, partial, gauges).reshape(owners, rows, hours)
    sums = jnp.sum(lax.all_to_all(dense, "basin", 0, 0, tiled=False), axis=0)
    both = jnp.concatenate([observed, shifted(observed, "tm", -1)], axis=0)
    first = (lax.axis_index("basin") * rows).astype(jnp.int32).reshape(1)
    high, low = couple(first, all_rows, all_gram, rows, gauges)

    pulled, note = first_step(more, window(sums), both, spec, mats)
    notes, kept, state = [], [], None
    for k in range(3):
        everyone = gathered_rows(jnp.concatenate([pulled, note], axis=0))
        value = everyone[:, :rows].reshape(gauges, hours)
        notes.append(over_hours(jnp.sum(everyone[:, rows:], axis=0)))
        kept.append(value)
        around = window(mix(high, low, value))
        final = k == 2
        result = next_step(more, notes[-1], around, spec, mats, pulled, state, final)
        if final:
            (note,) = result
        else:
            state, pulled, note = result
    notes.append(over_hours(jnp.sum(gathered_rows(note), axis=0)))
    return finish(notes, row_gauge, kept, incidence, first_guess)


Z_, X_, Y_, C_ = 4, 2, 2, 2
NOTE = 8
HOURS = SPAN // 2


def device(z, x, y, c):
    return (z * X_ + x) * (Y_ * C_) + y * C_ + c


def moved(value, where):
    pairs = []
    for z, x, y, c in np.ndindex(Z_, X_, Y_, C_):
        target = where(z, x, y, c)
        if target is not None:
            pairs.append((device(z, x, y, c), device(*target)))
    return lax.ppermute(value, ("basin", "tm"), pairs)


def to_plane(z, x, y, c):
    return 2 * y + c, x, z & 1, z >> 1


def hour_before(z, x, y, c):
    t = 2 * y + c - 1
    return (z, x, t >> 1, t & 1) if t >= 0 else None


def from_plane(z, x, y, c):
    return 2 * c + y, x, z >> 1, z & 1


def over_x(z, x, y, c):
    return z, 1 - x, y, c


def over_y(z, x, y, c):
    return z, x, 1 - y, c


def over_xy(z, x, y, c):
    return z, 1 - x, 1 - y, c


def over_core(z, x, y, c):
    return z, x, y, 1 - c


def z_pair(z, x, y, c):
    return z ^ 1, x, y, c


def z_middle(z, x, y, c):
    return (3 - z, x, y, c) if z in (1, 2) else None


def z_two(z, x, y, c):
    return z ^ 2, x, y, c


def z_mirror(z, x, y, c):
    return 3 - z, x, y, c


def z_next(z, x, y, c):
    return (z + 1, x, y, c) if z < 3 else None


SQUARE = (over_x, over_y, over_xy)


def split_constant(value):
    out = []
    for _ in range(3):
        piece = value.astype(jnp.bfloat16)
        out.append(piece)
        value = value - piece.astype(np.float64)
    return out


ORDERS = {2: ((0, 1), (1, 0), (0, 0)), 3: ((0, 2), (1, 1), (2, 0), (0, 1), (1, 0), (0, 0))}


def widened(mat, order):
    parts = split_constant(mat)
    return jnp.asarray(np.concatenate([parts[i] for i, _ in ORDERS[order]], axis=1))


def product(wide, value, order):
    parts = pieces(value, order)
    return dot(wide, jnp.concatenate([parts[j] for _, j in ORDERS[order]], axis=0))


def turned_transforms(order):
    half = SPAN // 2
    freq = 2.0 * np.pi * (np.arange(half) + 0.5) / SPAN
    phase = freq[:, None] * np.arange(SPAN)[None, :]
    forward = np.concatenate([np.cos(phase), -np.sin(phase)], axis=0)
    inverse = forward.T * (2.0 / SPAN)
    return [widened(mat, order) for mat in (forward, inverse[:half], inverse[half:], forward[:, :half])]


def turn(waves, spec, sign):
    half = waves.shape[0] // 2
    real, imag = waves[:half], waves[half:]
    kr, ki = spec[:half], spec[half:] * sign
    return jnp.concatenate([real * kr - imag * ki, real * ki + imag * kr], axis=0)


def plane_delayed(before, here, after, spec, forward, last, order):
    rows = here.shape[1]
    pairs = [jnp.concatenate(pair, axis=0) for pair in ((before, here), (here, after))]
    waves = product(forward, jnp.concatenate(pairs, axis=1), order)
    turned = [turn(waves[:, i * rows : (i + 1) * rows], spec, 1.0) for i in range(2)]
    out = product(last, jnp.concatenate(turned, axis=1), order)
    return out[:, :rows], out[:, rows:]


def plane_advanced(here, after, spec, forward, first, order):
    waves = product(forward, jnp.concatenate([here, after], axis=0), order)
    return product(first, turn(waves, spec, -1.0), order)


def describe_kernel(inc_ref, gauge_ref, out_ref):
    blocks, slots, width = inc_ref.shape
    tile = 8
    side = tile * slots
    weights = inc_ref[...].astype(F32).astype(BF16)
    row = lax.broadcasted_iota(jnp.int32, (side, side), 0)
    col = lax.broadcasted_iota(jnp.int32, (side, side), 1)
    same = row // slots == col // slots
    for i in range(blocks // tile):
        flat = weights[i * tile : (i + 1) * tile].reshape(side, width)
        full = lax.dot_general(flat, flat, (((1,), (1,)), ((), ())), preferred_element_type=F32)
        own = jnp.where(same, full, 0.0)
        out_ref[pl.ds(0, slots), pl.ds(i * side, side)] = jnp.sum(own.reshape(tile, slots, side), axis=0)
    out_ref[pl.ds(slots, 8), :] = jnp.broadcast_to(gauge_ref[...].astype(F32), (8, blocks * slots))


def describe(incidence, row_gauge):
    blocks, slots, _ = incidence.shape
    count = blocks * slots
    return pl.pallas_call(
        describe_kernel,
        out_shape=jax.ShapeDtypeStruct((slots + 8, count), F32),
        compiler_params=params(),
        name="describe",
        cost_estimate=SMALL,
    )(incidence, row_gauge.reshape(1, count))


def send_kernel(
    inc_hbm, field_hbm, gauge_hbm, kind_hbm, out_ref, inc_ref, field_ref, gauge_ref, kind_ref, sems, label_sems
):
    blocks, slots, width = inc_ref.shape
    chunks = sems.shape[0]
    step = blocks // chunks
    copies = []
    for i in range(chunks):
        near = pl.ds(i * step, step)
        far = pl.ds(i * step * width, step * width)
        copies.append(
            (
                pltpu.make_async_copy(inc_hbm.at[near], inc_ref.at[near], sems.at[i, 0]),
                pltpu.make_async_copy(field_hbm.at[far], field_ref.at[far], sems.at[i, 1]),
            )
        )
        for copy in copies[-1]:
            copy.start()
    labels = (
        pltpu.make_async_copy(gauge_hbm, gauge_ref, label_sems.at[0]),
        pltpu.make_async_copy(kind_hbm, kind_ref, label_sems.at[1]),
    )
    for copy in labels:
        copy.start()
    for i in range(chunks):
        for copy in copies[i]:
            copy.wait()
        parts = []
        for b in range(i * step, (i + 1) * step):
            weight = inc_ref[b].astype(F32).astype(BF16)
            value = jnp.concatenate(pieces(field_ref[pl.ds(b * width, width), :], 3)[::-1], axis=0)
            parts.append(dot(jnp.concatenate([weight] * 3, axis=1), value))
        out_ref[pl.ds(0, HOURS), pl.ds(i * step * slots, step * slots)] = jnp.transpose(
            jnp.concatenate(parts, axis=0)
        )
    for copy in labels:
        copy.wait()
    count, kinds = gauge_ref.shape[1], kind_ref.shape[1]
    kind = jnp.concatenate([kind_ref[...].astype(F32), jnp.zeros((1, count - kinds), F32)], axis=1)
    out_ref[pl.ds(HOURS, 8), :] = jnp.concatenate(
        [gauge_ref[...].astype(F32), kind, jnp.zeros((6, count), F32)], axis=0
    )


def send(incidence, field, row_gauge, gauge_kernel):
    count, rows = row_gauge.shape[0], gauge_kernel.shape[0]
    chunks = 8
    return pl.pallas_call(
        send_kernel,
        in_specs=[pl.BlockSpec(memory_space=pltpu.HBM)] * 4,
        out_shape=jax.ShapeDtypeStruct((HOURS + 8, count), F32),
        scratch_shapes=[
            pltpu.VMEM(incidence.shape, incidence.dtype),
            pltpu.VMEM(field.shape, F32),
            pltpu.VMEM((1, count), row_gauge.dtype),
            pltpu.VMEM((1, rows), gauge_kernel.dtype),
            pltpu.SemaphoreType.DMA((chunks, 2)),
            pltpu.SemaphoreType.DMA((2,)),
        ],
        compiler_params=params(60),
        name="send",
        cost_estimate=SMALL,
    )(incidence, field, row_gauge.reshape(1, count), gauge_kernel.reshape(1, rows))


def hot_rows(gauge, first, rows):
    mine = (lax.broadcasted_iota(jnp.int32, (rows, gauge.shape[1]), 0) + first).astype(F32)
    return jnp.where(gauge == mine, 1.0, 0.0).astype(BF16)


def spread_kernel(first_ref, mine_ref, other_ref, *out_refs):
    rows = out_refs[0].shape[1]
    both = jnp.concatenate([mine_ref[...], other_ref[...]], axis=1)
    stacked = jnp.concatenate(pieces(both[:HOURS], 3), axis=0)
    for m, out_ref in enumerate(out_refs):
        hot = hot_rows(both[HOURS : HOURS + 1], first_ref[m], rows)
        result = lax.dot_general(stacked, hot, (((1,), (1,)), ((), ())), preferred_element_type=F32)
        out_ref[...] = (result[2 * HOURS :] + result[HOURS : 2 * HOURS]) + result[:HOURS]


def spread(first, parcels, rows):
    return pl.pallas_call(
        spread_kernel,
        in_specs=[pl.BlockSpec(memory_space=pltpu.SMEM)] + [pl.BlockSpec(memory_space=pltpu.VMEM)] * 2,
        out_shape=[jax.ShapeDtypeStruct((HOURS, rows), F32)] * 4,
        compiler_params=params(),
        name="spread",
        cost_estimate=SMALL,
    )(first, *parcels)


def plane_couple_kernel(last, first_ref, *refs):
    if last:
        all_ref, before_ref, high_ref, low_ref, total_ref, meta_ref = refs
        total_ref[...] = before_ref[...]
    else:
        all_ref, total_ref, meta_ref = refs
        total_ref[...] = jnp.zeros_like(total_ref)
    parts, height, count = meta_ref.shape
    slots = height - 8
    cols, rows = total_ref.shape
    tile = 256
    for i in range(parts):
        meta_ref[i] = all_ref[:, i * count : (i + 1) * count]
    row = lax.broadcasted_iota(jnp.int32, (tile, tile), 0)
    col = lax.broadcasted_iota(jnp.int32, (tile, tile), 1)
    same = row // slots == col // slots

    def body(i, carry):
        gauge = meta_ref[i, slots : slots + 1, :]
        near = []
        for j in range(count // tile):
            here = slice(j * tile, (j + 1) * tile)
            block = jnp.concatenate([meta_ref[i, :slots, here]] * (tile // slots), axis=0)
            block = jnp.where(same, block, 0.0).astype(BF16)
            mine = jnp.concatenate(
                [hot_rows(gauge[:, here], first_ref[4 + h], rows // 2) for h in range(2)], axis=0
            )
            near.append(
                lax.dot_general(block, mine, (((1,), (1,)), ((), ())), preferred_element_type=F32)
            )
        near = jnp.concatenate(near, axis=0)
        high = near.astype(BF16)
        rest = near - high.astype(F32)
        hot = jnp.concatenate([hot_rows(gauge, first_ref[m], cols // 4) for m in range(4)], axis=0)
        total_ref[...] += dot(hot, high)

        @pl.when(jnp.max(jnp.abs(rest)) > 0.0)
        def _():
            total_ref[...] += dot(hot, rest.astype(BF16))

        return carry

    lax.fori_loop(0, parts, body, 0)
    if last:
        high, low = pieces(total_ref[...], 2)
        high_ref[...] = high
        low_ref[...] = low


def plane_couple(first, meta, rows, before=None):
    height, wide = meta.shape
    parts = 2 * X_
    shape = (4 * rows, 2 * rows)
    last = before is not None
    args = [first, meta] + ([before] if last else [])
    scratch = [pltpu.VMEM((parts, height, wide // parts), F32)]
    return pl.pallas_call(
        functools.partial(plane_couple_kernel, last),
        in_specs=[pl.BlockSpec(memory_space=pltpu.SMEM)]
        + [pl.BlockSpec(memory_space=pltpu.VMEM)] * (len(args) - 1),
        out_shape=[jax.ShapeDtypeStruct(shape, BF16)] * 2 if last else jax.ShapeDtypeStruct(shape, F32),
        scratch_shapes=([pltpu.VMEM(shape, F32)] if last else []) + scratch,
        compiler_params=params(),
        name="plane_couple",
        cost_estimate=pl.CostEstimate(
            flops=2 * 8 * wide * rows * rows, bytes_accessed=2_000_000, transcendentals=0
        ),
    )(*args)


def plane_mix_kernel(high_ref, low_ref, a_ref, b_ref, c_ref, d_ref, *refs):
    *extra, mine_ref, other_ref = refs
    refs = (a_ref, b_ref, c_ref, d_ref)
    height, rows = a_ref.shape
    body = pl.ds(0, HOURS)
    one, two = pieces(jnp.concatenate([ref[body, :] for ref in refs], axis=1), 2)
    both = dot(jnp.concatenate([two, one], axis=0), high_ref[...])
    result = (both[:HOURS] + dot(one, low_ref[...])) + both[HOURS:]
    mine_ref[body, :] = result[:, :rows]
    other_ref[body, :] = result[:, rows:]
    if height > HOURS:
        tail = pl.ds(HOURS, NOTE)
        note = sum(ref[tail, :] for ref in refs)
        mine_ref[tail, :] = note
        other_ref[tail, :] = note
    for ref in extra:
        other_ref[pl.ds(height, ref.shape[0]), :] = ref[...]


def plane_mix(coupling, values, extra):
    height, rows = values[0].shape
    return pl.pallas_call(
        plane_mix_kernel,
        out_shape=[
            jax.ShapeDtypeStruct((height, rows), F32),
            jax.ShapeDtypeStruct((height + sum(value.shape[0] for value in extra), rows), F32),
        ],
        compiler_params=params(),
        name="plane_mix",
        cost_estimate=SMALL,
    )(*coupling, *values, *extra)


def plane_rows_kernel(first_ref, meta_ref, meta_other_ref, a_ref, b_ref, c_ref, d_ref, *refs):
    if len(refs) > 2:
        *stack, last_ref, beside_ref, mine_ref, other_ref, stack_ref = refs
    else:
        mine_ref, other_ref = refs
    rows = a_ref.shape[1]
    value = jnp.concatenate([ref[pl.ds(0, HOURS), :] for ref in (a_ref, b_ref, c_ref, d_ref)], axis=1)
    one, two = pieces(value, 2)
    stacked = jnp.concatenate([two, one], axis=0)
    picked = []
    for ref in (meta_ref, meta_other_ref):
        gauge = ref[0:1, :]
        hot = jnp.concatenate([hot_rows(gauge, first_ref[m], rows) for m in range(4)], axis=0)
        both = dot(stacked, hot)
        picked.append(both[:HOURS] + both[HOURS:])
    mine_ref[...] = picked[0]
    count = picked[1].shape[1] // rows
    for i in range(count):
        other_ref[pl.ds(i * HOURS, HOURS), :] = picked[1][:, i * rows : (i + 1) * rows]
    if len(refs) > 2:
        top = stack_ref.shape[0] - HOURS
        for ref in stack:
            stack_ref[pl.ds(0, top), :] = ref[...]
        for i in range(count):
            here = pl.ds(i * rows, rows)
            beside = beside_ref[pl.ds(beside_ref.shape[0] - (count - i) * HOURS, HOURS), :]
            stack_ref[pl.ds(top, HOURS), here] = last_ref[:, here] + beside


def plane_rows(first, metas, values, before):
    rows = values[0].shape[1]
    slots = metas[0].shape[1]
    args = [first, *metas, *values, *before]
    shapes = [(HOURS, slots), (slots // rows * HOURS, rows)]
    if before:
        shapes.append(((len(before) - 1) * HOURS, slots))
    return pl.pallas_call(
        plane_rows_kernel,
        in_specs=[pl.BlockSpec(memory_space=pltpu.SMEM)]
        + [pl.BlockSpec(memory_space=pltpu.VMEM)] * (len(args) - 1),
        out_shape=[jax.ShapeDtypeStruct(shape, F32) for shape in shapes],
        compiler_params=params(),
        name="plane_rows",
        cost_estimate=pl.CostEstimate(flops=1_000_000_000, bytes_accessed=2_000_000, transcendentals=0),
    )(*args)


def gain(kernels):
    return jnp.max(jnp.sum(kernels, axis=1, keepdims=True), axis=0, keepdims=True)


def spectra(kind, kernels, wide):
    classes = kernels.shape[0]
    row = lax.broadcasted_iota(jnp.int32, (classes, kind.shape[1]), 0).astype(F32)
    hot = jnp.where(row == kind, 1.0, 0.0).astype(BF16)
    taps = jnp.transpose(kernels / gain(kernels))
    chosen = dot(jnp.concatenate(pieces(taps, 3)[::-1], axis=1), jnp.concatenate([hot] * 3, axis=0))
    return product(wide, chosen, 3)


def plane_spectrum_kernel(class_ref, kernels_ref, wide_ref, out_ref):
    kind = class_ref[1:2, : out_ref.shape[1]]
    out_ref[...] = spectra(kind, kernels_ref[...], wide_ref[...])


def plane_spectrum(meta, kernels, wide, rows):
    return pl.pallas_call(
        plane_spectrum_kernel,
        out_shape=jax.ShapeDtypeStruct((SPAN, rows), F32),
        compiler_params=params(),
        name="plane_spectrum",
        cost_estimate=SMALL,
    )(meta, kernels, wide)


def sides(even, pair, middle):
    return jnp.where(even, middle, pair), jnp.where(even, pair, middle)


def plane_call(kernel, name, shapes, flags, args):
    return pl.pallas_call(
        kernel,
        in_specs=[pl.BlockSpec(memory_space=pltpu.SMEM)] * len(flags)
        + [pl.BlockSpec(memory_space=pltpu.VMEM)] * len(args),
        out_shape=[jax.ShapeDtypeStruct(shape, F32) for shape in shapes],
        compiler_params=params(),
        name=name,
        cost_estimate=SMALL,
    )(*flags, *args)


def plane_first_kernel(
    flag_ref, here_ref, pair_ref, middle_ref, spec_ref, kernels_ref, forward, first, last, out_ref
):
    spec = spec_ref[...]
    before, after = sides(flag_ref[0] > 0.5, pair_ref[...], middle_ref[...])
    here = here_ref[...]
    both = plane_delayed(before[:HOURS], here[:HOURS], after[:HOURS], spec, forward[...], last[...], 3)
    scale = gain(kernels_ref[...])
    now = here[HOURS:] - both[0] * scale
    later = (after[HOURS:] - both[1] * scale) * flag_ref[1]
    out_ref[...] = plane_advanced(now, later, spec, forward[...], first[...], 3)


def plane_delay_kernel(flag_ref, here_ref, pair_ref, middle_ref, spec_ref, forward, last, out_ref):
    body = pl.ds(0, HOURS)
    before, after = sides(flag_ref[0] > 0.5, pair_ref[body, :], middle_ref[body, :])
    out = plane_delayed(before, here_ref[body, :], after, spec_ref[...], forward[...], last[...], 2)
    for i in range(2):
        out_ref[pl.ds(i * HOURS, HOURS), :] = out[i]


def write_note(ref, rows):
    tail = [jnp.zeros((NOTE - len(rows), ref.shape[1]), F32)]
    ref[pl.ds(HOURS, NOTE), :] = jnp.concatenate(rows + tail, axis=0)


def plane_open_kernel(
    flag_ref, here_ref, pair_ref, middle_ref, pulled_ref, spec_ref, forward, first, last, out_ref, delayed_ref
):
    here = here_ref[...]
    spec = spec_ref[...]
    before, after = sides(flag_ref[0] > 0.5, pair_ref[...], middle_ref[...])
    now, later = plane_delayed(before, here, after, spec, forward[...], last[...], 2)
    out_ref[pl.ds(0, HOURS), :] = plane_advanced(now, later * flag_ref[1], spec, forward[...], first[...], 2)
    write_note(out_ref, [lanes(pulled_ref[...], here), lanes(now, now)])
    delayed_ref[pl.ds(0, HOURS), :] = now
    delayed_ref[pl.ds(HOURS, HOURS), :] = later


def plane_step_kernel(
    flag_ref,
    here_ref,
    pair_ref,
    two_ref,
    mirror_ref,
    pulled_ref,
    delayed_ref,
    old_z_ref,
    old_s_ref,
    old_delayed_ref,
    spec_ref,
    forward,
    first,
    total_ref,
    out_ref,
    kept_ref,
):
    tail, body = pl.ds(HOURS, NOTE), pl.ds(0, HOURS)
    total_ref[...] = (here_ref[tail, :] + pair_ref[tail, :]) + (two_ref[...] + mirror_ref[...])
    inverse = total(total_ref, 0) / total(total_ref, 1)
    z = pulled_ref[body, :] * inverse - old_z_ref[...]
    s = here_ref[body, :] * inverse - old_s_ref[...]
    both = delayed_ref[...] * inverse - old_delayed_ref[...]
    now, later = both[:HOURS], both[HOURS:]
    following = plane_advanced(now, later * flag_ref[1], spec_ref[...], forward[...], first[...], 2)
    out_ref[body, :] = following * inverse
    write_note(out_ref, [lanes(z, s), lanes(now, now)])
    for i, value in enumerate((z, s, now)):
        kept_ref[pl.ds(i * HOURS, HOURS), :] = value


def plane_close_kernel(
    here_ref, before_ref, pulled_ref, kept_ref, old_z_ref, old_s_ref, old_delayed_ref, spec_ref, forward, last, out_ref
):
    body = pl.ds(0, HOURS)
    here, raw = here_ref[body, :], pulled_ref[body, :]
    waves = product(forward[...], jnp.concatenate([before_ref[body, :], here], axis=0), 2)
    now = product(last[...], turn(waves, spec_ref[...], 1.0), 2)
    z, s, delayed = (kept_ref[pl.ds(i * HOURS, HOURS), :] for i in range(3))
    note = [pulled_ref[HOURS + i : HOURS + i + 1, :] for i in range(2)]
    for left in (raw, z, old_z_ref[...]):
        note += [lanes(left, right) for right in (here, s, old_s_ref[...])]
    parts = (now, delayed, old_delayed_ref[body, :])
    for i in range(3):
        note += [lanes(parts[i], parts[j]) for j in range(i, 3)]
    note.append(jnp.zeros((24 - len(note), here.shape[1]), F32))
    note = jnp.sum(jnp.concatenate(note, axis=0), axis=1, keepdims=True)
    shape = (24, out_ref.shape[2])
    row, col = (lax.broadcasted_iota(jnp.int32, shape, i) for i in range(2))
    note = jnp.sum(jnp.where(row == col, jnp.broadcast_to(note, shape), 0.0), axis=0, keepdims=True)
    out_ref[...] = jnp.broadcast_to(note[None], out_ref.shape)


def plane_weights(open_ref, close, scale):
    entry = lambda i: close[:, i : i + 1]
    n1, t1 = total(open_ref, 0), total(open_ref, 1)
    n2, t2 = entry(0), entry(1)
    a1 = t1 / n1
    a2, r2 = (t2 / n2) / a1, n2 / n1
    plain = (1.0, -a2, -r2)
    n3 = sum(plain[i] * plain[j] * entry(2 + 3 * i + j) for i in range(3) for j in range(3))
    pairs = [(i, j) for i in range(3) for j in range(i, 3)]
    t3 = sum(
        plain[i] * plain[j] * entry(11 + n) * (1.0 if i == j else 2.0) for n, (i, j) in enumerate(pairs)
    )
    a3, r3 = (t3 / n3) / a1, n3 / n2
    unit = 1.0 / (a1 * scale)
    c3 = unit / (a3 * (a2 - r2) - r3)
    c2 = -a3 * c3
    c1 = unit - r2 * c2
    step = c2 - c3 * a2
    return c1 - step - c3 * r2, step / a1, c3


def plane_combine_kernel(open_ref, close_ref, kernels_ref, stack_ref, mine_ref, beside_ref, out_ref):
    rows = open_ref.shape[1]
    close = jnp.sum(close_ref[...], axis=0)[0:1, :]
    e0, e1, e2 = plane_weights(open_ref, close, gain(kernels_ref[...]))
    for i in range(out_ref.shape[0] // rows):
        here = pl.ds(i * rows, rows)
        last = mine_ref[:, here] + beside_ref[pl.ds(i * HOURS, HOURS), :]
        value = stack_ref[pl.ds(0, HOURS), here] * e0 + stack_ref[pl.ds(HOURS, HOURS), here] * e1 + last * e2
        out_ref[here, :] = jnp.transpose(value)


def plane_finish_kernel(rows_ref, inc_ref, field_ref, out_ref):
    blocks, slots, width = inc_ref.shape
    weights = inc_ref[...].astype(F32).astype(BF16)
    for b in range(blocks):
        here = pl.ds(b * width, width)
        rows = jnp.concatenate(pieces(rows_ref[pl.ds(b * slots, slots), :], 2), axis=0)
        twice = jnp.concatenate([weights[b]] * 2, axis=0)
        added = lax.dot_general(twice, rows, (((0,), (0,)), ((), ())), preferred_element_type=F32)
        out_ref[here, :] = field_ref[here, :] + added


def plane_finish(rows, incidence, field):
    blocks, slots, width = incidence.shape
    hours = field.shape[1]
    step = 8
    return pl.pallas_call(
        plane_finish_kernel,
        grid=(blocks // step,),
        in_specs=[
            pl.BlockSpec((step * slots, hours), lambda i: (i, 0)),
            pl.BlockSpec((step, slots, width), lambda i: (i, 0, 0)),
            pl.BlockSpec((step * width, hours), lambda i: (i, 0)),
        ],
        out_specs=pl.BlockSpec((step * width, hours), lambda i: (i, 0)),
        out_shape=jax.ShapeDtypeStruct(field.shape, F32),
        compiler_params=params(),
        name="plane_finish",
    )(rows, incidence, field)


def plane_shards(incidence, row_gauge, gauge_kernel, kernels, observed, first_guess):
    rows, hours = observed.shape
    basin, tm = lax.axis_index("basin"), lax.axis_index("tm")
    z, x, y, c = basin // X_, basin % X_, tm // C_, tm % C_
    place = 2 * y + x
    first = jnp.stack([4 * c + (place ^ m) for m in range(4)] + [4 * c + place, 4 * (1 - c) + place])
    first = (first * rows).astype(jnp.int32)
    flags = jnp.stack([1 - z % 2, (z < Z_ - 1).astype(z.dtype), (z > 0).astype(z.dtype)]).astype(F32)
    forward, inverse_first, inverse_last, _ = turned_transforms(2)
    forward3, inverse_first3, inverse_last3, short3 = turned_transforms(3)
    block, noted = (hours, rows), (hours + NOTE, rows)

    parcel = send(incidence, first_guess, row_gauge, gauge_kernel)
    parcel, near, seen = lax.optimization_barrier((parcel, incidence, observed))
    parcel = moved(parcel, to_plane)
    seen = moved(seen, to_plane)
    near, seen = lax.optimization_barrier((near, seen))
    meta = describe(near, row_gauge)
    meta = jnp.concatenate([meta, moved(meta, over_x)], axis=1)
    meta = jnp.concatenate([meta, moved(meta, z_pair)], axis=1)
    parcel, seen = lax.optimization_barrier((parcel, seen))
    parcels = [parcel, moved(parcel, over_core)]
    spec = plane_spectrum(parcel[hours:], kernels, short3, rows)
    parcels[1], seen, meta, spec = lax.optimization_barrier((parcels[1], seen, meta, spec))
    half = meta.shape[1] // 2
    far = moved(jnp.where(c == 0, meta[:, :half], meta[:, half:]), z_two)
    dense = spread(first, parcels, rows)
    metas = [value[hours:] for value in parcels]
    sums = dense[0] + sum(moved(value, where) for value, where in zip(dense[1:], SQUARE))
    sums, far = lax.optimization_barrier((sums, far))
    around = [meta, jnp.concatenate([far, moved(far, over_core)], axis=1)]
    sums = jnp.concatenate([sums, jnp.transpose(seen)], axis=0)
    sums = [sums, moved(sums, z_pair), moved(sums, z_middle)]
    coupled = plane_couple(first, around[0], rows)
    coupled, sums = lax.optimization_barrier((coupled, sums))
    coupling = plane_couple(first, around[1], rows, coupled)
    (pulled0,) = plane_call(
        plane_first_kernel,
        "plane_first",
        [block],
        [flags],
        [*sums, spec, kernels, forward3, inverse_first3, inverse_last3],
    )

    def mixing(pulled, extra):
        values = [pulled] + [moved(pulled, where) for where in SQUARE]
        mine, other = plane_mix(coupling, values, extra)
        beside = moved(other, over_core)
        return values, mine + beside[: pulled.shape[0]], beside

    values, mixed0, _ = mixing(pulled0, [])
    picked, theirs = plane_rows(first, metas, values, [])
    sums = [mixed0, moved(mixed0, z_pair), moved(mixed0, z_middle)]
    pulled1, delayed0 = plane_call(
        plane_open_kernel,
        "plane_open",
        [noted, (2 * hours, rows)],
        [flags],
        [*sums, pulled0, spec, forward, inverse_first, inverse_last],
    )

    values, mixed1, beside = mixing(pulled1, [theirs])
    picked, theirs, stack = plane_rows(first, metas, values, [picked, beside])
    sums = [mixed1, moved(mixed1, z_pair), moved(mixed1, z_middle)]
    two, mirror = moved(mixed1[hours:], z_two), moved(mixed1[hours:], z_mirror)
    (delayed1,) = plane_call(
        plane_delay_kernel, "plane_delay", [(2 * hours, rows)], [flags], [*sums, spec, forward, inverse_last]
    )
    open_note, pulled2, kept = plane_call(
        plane_step_kernel,
        "plane_step",
        [(NOTE, rows), noted, (3 * hours, rows)],
        [flags],
        [*sums[:2], two, mirror, pulled1, delayed1, pulled0, mixed0, delayed0, spec, forward, inverse_first],
    )

    values, mixed2, beside = mixing(pulled2, [theirs])
    picked, theirs, stack = plane_rows(first, metas, values, [stack, picked, beside])
    (note,) = plane_call(
        plane_close_kernel,
        "plane_close",
        [(Z_ * X_ * Y_ * C_, 8, rows // 2)],
        [],
        [mixed2, moved(mixed2, z_next), pulled2, kept, pulled0, mixed0, delayed0, spec, forward, inverse_last],
    )
    close_note = lax.all_to_all(note, ("basin", "tm"), 0, 0, tiled=False)
    (answer,) = plane_call(
        plane_combine_kernel,
        "plane_combine",
        [(parcel.shape[1], hours)],
        [],
        [open_note, close_note, kernels, stack, picked, moved(theirs, over_core)],
    )
    return plane_finish(moved(answer, from_plane), incidence, first_guess)


def solution(mesh):
    planes = dict(mesh.shape) == {"basin": Z_ * X_, "tm": Y_ * C_}
    in_specs = (
        P("basin", None, None),
        P("basin"),
        P("basin"),
        P(),
        P("basin", "tm"),
        P("basin", "tm"),
    )
    return jax.shard_map(
        plane_shards if planes else shards, mesh=mesh, in_specs=in_specs, out_specs=P("basin", "tm"), check_vma=False
    )
```

```python
import functools

import jax
import jax.numpy as jnp
import numpy as np
from jax import lax
from jax.experimental import pallas as pl
from jax.experimental.pallas import tpu as pltpu
from jax.sharding import PartitionSpec as P

F32 = jnp.float32
BF16 = jnp.bfloat16
HIGH = lax.Precision.HIGHEST
SPAN = 256
MIB = 1024 * 1024


SMALL = pl.CostEstimate(flops=1, bytes_accessed=1, transcendentals=0)


def params(mib=16):
    return pltpu.CompilerParams(vmem_limit_bytes=mib * MIB)


def transforms():
    half = SPAN // 2
    freq = 2.0 * np.pi * (np.arange(half) + 0.5) / SPAN
    phase = np.arange(SPAN)[:, None] * freq[None, :]
    forward = np.concatenate([np.cos(phase), -np.sin(phase)], axis=1)
    inverse = forward.T * (2.0 / SPAN)
    return (
        jnp.asarray(forward, F32),
        jnp.asarray(inverse[:, :half], F32),
        jnp.asarray(inverse[:, half:], F32),
    )


def dot(a, b):
    return jnp.dot(a, b, preferred_element_type=F32)


def exact(a, b):
    return jnp.dot(a, b, precision=HIGH, preferred_element_type=F32)


def pieces(value, count):
    out = []
    for _ in range(count):
        piece = value.astype(BF16)
        out.append(piece)
        value = value - piece.astype(F32)
    return out


def pick(hot, value):
    return sum(dot(hot, piece) for piece in pieces(value, 3))


def prepare_kernel(inc_ref, field_ref, partial_ref, gram_ref):
    blocks, slots, width = inc_ref.shape
    rows = blocks * slots
    weights = inc_ref[...].astype(F32).astype(BF16)
    for b in range(blocks):
        value = field_ref[pl.ds(b * width, width), :]
        partial_ref[pl.ds(b * slots, slots), :] = pick(weights[b], value)
    flat = weights.reshape(rows, width)
    full = lax.dot_general(flat, flat, (((1,), (1,)), ((), ())), preferred_element_type=F32)
    row = lax.broadcasted_iota(jnp.int32, (rows, rows), 0)
    col = lax.broadcasted_iota(jnp.int32, (rows, rows), 1)
    own = jnp.where(row // slots == col // slots, full, 0.0)
    gram_ref[...] = jnp.sum(own.reshape(blocks, slots, rows), axis=0)


def prepare(incidence, field):
    blocks, slots, width = incidence.shape
    hours = field.shape[1]
    step = 8
    return pl.pallas_call(
        prepare_kernel,
        grid=(blocks // step,),
        in_specs=[
            pl.BlockSpec((step, slots, width), lambda i: (i, 0, 0)),
            pl.BlockSpec((step * width, hours), lambda i: (i, 0)),
        ],
        out_specs=[
            pl.BlockSpec((step * slots, hours), lambda i: (i, 0)),
            pl.BlockSpec((slots, step * slots), lambda i: (0, i)),
        ],
        out_shape=[
            jax.ShapeDtypeStruct((blocks * slots, hours), F32),
            jax.ShapeDtypeStruct((slots, blocks * slots), F32),
        ],
        compiler_params=params(56),
        name="prepare",
    )(incidence, field)


def table_kernel(gauge_ref, partial_ref, out_ref):
    slots = partial_ref.shape[0]
    rows = out_ref.shape[0]
    first = pl.program_id(0) * rows
    gauge = lax.broadcasted_iota(jnp.int32, (rows, slots), 0) + first
    hot = jnp.where(gauge_ref[...] == gauge, 1.0, 0.0).astype(BF16)
    out_ref[...] = pick(hot, partial_ref[...])


def table(row_gauge, partial, gauges):
    slots, hours = partial.shape
    step = 256
    return pl.pallas_call(
        table_kernel,
        grid=(gauges // step,),
        in_specs=[
            pl.BlockSpec((1, slots), lambda i: (0, 0)),
            pl.BlockSpec((slots, hours), lambda i: (0, 0)),
        ],
        out_specs=pl.BlockSpec((step, hours), lambda i: (i, 0)),
        out_shape=jax.ShapeDtypeStruct((gauges, hours), F32),
        compiler_params=params(56),
        name="table",
    )(row_gauge.reshape(1, slots), partial)


def couple_kernel(first_ref, lane_ref, sub_ref, gram_ref, high_ref, low_ref, near_ref):
    slots = gram_ref.shape[0]
    count = lane_ref.shape[1]
    rows, cols = high_ref.shape
    tile = 256
    first = first_ref[0]

    @pl.when(pl.program_id(0) == 0)
    def _():
        row = lax.broadcasted_iota(jnp.int32, (tile, tile), 0)
        col = lax.broadcasted_iota(jnp.int32, (tile, tile), 1)
        same = row // slots == col // slots
        mine = lax.broadcasted_iota(jnp.int32, (rows, tile), 0) + first

        def body(i, carry):
            here = pl.ds(pl.multiple_of(i * tile, tile), tile)
            block = jnp.concatenate([gram_ref[:, here]] * (tile // slots), axis=0)
            block = jnp.where(same, block, 0.0).astype(BF16)
            hot = jnp.where(lane_ref[:, here] == mine, 1.0, 0.0).astype(BF16)
            near_ref[:, here] = dot(hot, block)
            return carry

        lax.fori_loop(0, count // tile, body, 0)

    def chunk(i, total):
        here = pl.ds(pl.multiple_of(i * 1024, 1024), 1024)
        gauge = lax.broadcasted_iota(jnp.int32, (1024, cols), 1) + pl.program_id(0) * cols
        hot = jnp.where(sub_ref[here, :] == gauge, 1.0, 0.0).astype(BF16)
        near = near_ref[:, here]
        high = near.astype(BF16)
        low = (near - high.astype(F32)).astype(BF16)
        return total + dot(high, hot) + dot(low, hot)

    total = lax.fori_loop(0, count // 1024, chunk, jnp.zeros((rows, cols), F32))
    high, low = pieces(total, 2)
    high_ref[...] = high
    low_ref[...] = low


def couple(first, row_gauge, gram, rows, gauges):
    count = row_gauge.shape[0]
    step = 256
    return pl.pallas_call(
        couple_kernel,
        grid=(gauges // step,),
        in_specs=[
            pl.BlockSpec(memory_space=pltpu.SMEM),
            pl.BlockSpec((1, count), lambda i: (0, 0)),
            pl.BlockSpec((count, 1), lambda i: (0, 0)),
            pl.BlockSpec(gram.shape, lambda i: (0, 0)),
        ],
        out_specs=[pl.BlockSpec((rows, step), lambda i: (0, i))] * 2,
        out_shape=[jax.ShapeDtypeStruct((rows, gauges), BF16)] * 2,
        scratch_shapes=[pltpu.VMEM((rows, count), F32)],
        compiler_params=params(56),
        name="couple",
    )(first, row_gauge.reshape(1, count), row_gauge.reshape(count, 1), gram)


def mix_kernel(high_ref, low_ref, value_ref, out_ref):
    high = high_ref[...]
    low = low_ref[...]
    one, two, three = pieces(value_ref[...], 3)
    out_ref[...] = (dot(high, three) + dot(low, two)) + (dot(high, two) + dot(low, one)) + dot(high, one)


def mix(high, low, value):
    return pl.pallas_call(
        mix_kernel,
        out_shape=jax.ShapeDtypeStruct((high.shape[0], value.shape[1]), F32),
        compiler_params=params(56),
        name="mix",
    )(high, low, value)


def spectrum_kernel(class_ref, kernels_ref, forward_ref, out_ref):
    rows = class_ref.shape[0]
    classes, taps = kernels_ref.shape
    kind = lax.broadcasted_iota(jnp.int32, (rows, classes), 1)
    hot = jnp.where(class_ref[...] == kind, 1.0, 0.0)
    out_ref[...] = exact(exact(hot, kernels_ref[...]), forward_ref[pl.ds(0, taps), :])


def spectrum(gauge_kernel, kernels, forward):
    rows = gauge_kernel.shape[0]
    return pl.pallas_call(
        spectrum_kernel,
        out_shape=jax.ShapeDtypeStruct((rows, SPAN), F32),
        compiler_params=params(56),
        name="spectrum",
    )(gauge_kernel.reshape(rows, 1), kernels, forward)


def delayed(before, here, after, spec, forward, inverse_last):
    rows, half = here.shape
    stacked = jnp.concatenate(
        [jnp.concatenate([before, here], axis=1), jnp.concatenate([here, after], axis=1)], axis=0
    )
    waves = exact(stacked, forward)
    real, imag = waves[:, :half], waves[:, half:]
    kr = jnp.concatenate([spec[:, :half]] * 2, axis=0)
    ki = jnp.concatenate([spec[:, half:]] * 2, axis=0)
    turned = jnp.concatenate([real * kr - imag * ki, real * ki + imag * kr], axis=1)
    out = exact(turned, inverse_last)
    return out[:rows], out[rows:]


def advanced(here, after, spec, forward, inverse_first):
    half = here.shape[1]
    waves = exact(jnp.concatenate([here, after], axis=1), forward)
    real, imag = waves[:, :half], waves[:, half:]
    kr, ki = spec[:, :half], spec[:, half:]
    turned = jnp.concatenate([real * kr + imag * ki, imag * kr - real * ki], axis=1)
    return exact(turned, inverse_first)


def lanes(a, b):
    return jnp.sum(a * b, axis=0, keepdims=True)


def total(ref, row):
    return jnp.sum(ref[row : row + 1, :], axis=1, keepdims=True)


def ratios(ref):
    square = total(ref, 0)
    alpha = jnp.sqrt(square)
    beta = jnp.sqrt(jnp.maximum(total(ref, 1) / square - 2.0 * total(ref, 2) + square, 0.0))
    return alpha, beta


def first_kernel(
    more_ref, sums_ref, observed_ref, spec_ref, forward_ref, first_ref, last_ref, out_ref, note_ref
):
    rows, half = observed_ref.shape[0] // 2, observed_ref.shape[1]
    spec, forward = spec_ref[...], forward_ref[...]
    before, here, after = (sums_ref[pl.ds(i * rows, rows), :] for i in range(3))
    now, later = delayed(before, here, after, spec, forward, last_ref[...])
    start = observed_ref[pl.ds(0, rows), :] - now
    start_later = (observed_ref[pl.ds(rows, rows), :] - later) * more_ref[0]
    out_ref[...] = advanced(start, start_later, spec, forward, first_ref[...])
    note_ref[...] = jnp.concatenate([lanes(start, start), jnp.zeros((7, half), F32)], axis=0)


def first_step(more, sums, observed, spec, mats):
    rows, half = spec.shape[0], observed.shape[1]
    return pl.pallas_call(
        first_kernel,
        in_specs=[pl.BlockSpec(memory_space=pltpu.SMEM)] + [pl.BlockSpec(memory_space=pltpu.VMEM)] * 6,
        out_shape=[jax.ShapeDtypeStruct((rows, half), F32), jax.ShapeDtypeStruct((8, half), F32)],
        compiler_params=params(56),
        name="first_step",
    )(more, sums, observed, spec, *mats)


def step_kernel(
    opening,
    final,
    more_ref,
    note_ref,
    sums_ref,
    spec_ref,
    forward_ref,
    first_ref,
    last_ref,
    pulled_ref,
    *refs,
):
    if opening:
        state_ref = None
    else:
        state_ref, *refs = refs
    if final:
        (out_note_ref,) = refs
    else:
        new_ref, out_ref, out_note_ref = refs
    rows, half = pulled_ref.shape
    spec, forward = spec_ref[...], forward_ref[...]
    if opening:
        scale = 1.0 / jnp.sqrt(total(note_ref, 0))
        along = sums_ref[...] * scale
        new_s, new_su = along, along
        new_zu = pulled_ref[...] * scale
        new_z = new_zu
    else:
        alpha, beta = ratios(note_ref)
        a, b, g = 1.0 / (alpha * beta), alpha / beta, beta / alpha
        wide = pl.ds(0, 3 * rows), pl.ds(3 * rows, 3 * rows)
        new_su = sums_ref[...] * a - state_ref[wide[1], :] * b
        new_s = new_su - state_ref[wide[0], :] * g
        new_zu = pulled_ref[...] * a - state_ref[pl.ds(7 * rows, rows), :] * b
        new_z = new_zu - state_ref[pl.ds(6 * rows, rows), :] * g
    before, here, after = (new_s[i * rows : (i + 1) * rows] for i in range(3))
    now, later = delayed(before, here, after, spec, forward, last_ref[...])
    out_note_ref[...] = jnp.concatenate(
        [lanes(new_z, here), lanes(now, now), lanes(new_zu, here), jnp.zeros((5, half), F32)], axis=0
    )
    if not final:
        new_ref[pl.ds(0, 3 * rows), :] = new_s
        new_ref[pl.ds(3 * rows, 3 * rows), :] = new_su
        new_ref[pl.ds(6 * rows, rows), :] = new_z
        new_ref[pl.ds(7 * rows, rows), :] = new_zu
        out_ref[...] = advanced(now, later * more_ref[0], spec, forward, first_ref[...])


def next_step(more, note, sums, spec, mats, pulled, state, final):
    rows, half = pulled.shape
    opening = state is None
    shapes = [
        jax.ShapeDtypeStruct((8 * rows, half), F32),
        jax.ShapeDtypeStruct((rows, half), F32),
        jax.ShapeDtypeStruct((8, half), F32),
    ]
    args = [more, note, sums, spec, *mats, pulled] + ([] if opening else [state])
    return pl.pallas_call(
        functools.partial(step_kernel, opening, final),
        in_specs=[pl.BlockSpec(memory_space=pltpu.SMEM)]
        + [pl.BlockSpec(memory_space=pltpu.VMEM)] * (len(args) - 1),
        out_shape=shapes[2:] if final else shapes,
        compiler_params=params(56),
        name="next_step",
    )(*args)


def weights_of(notes):
    start = jnp.sqrt(total(notes[0], 0))
    zero = jnp.zeros_like(start)
    units = [1.0 / start, zero, zero]
    z, zu = list(units), list(units)
    phibar = start
    alpha, beta = ratios(notes[1])
    rhobar = alpha
    w = [value / alpha for value in z]
    result = [zero] * 3
    steps = len(notes) - 1
    for k in range(steps):
        rho = jnp.sqrt(rhobar * rhobar + beta * beta)
        cosine, sine = rhobar / rho, beta / rho
        phi, phibar = cosine * phibar, sine * phibar
        result = [r + phi / rho * value for r, value in zip(result, w)]
        if k < steps - 1:
            a, b, g = 1.0 / (alpha * beta), alpha / beta, beta / alpha
            zu = [(a if i == k + 1 else 0.0) - b * value for i, value in enumerate(zu)]
            z = [value - g * old for value, old in zip(zu, z)]
            alpha, beta = ratios(notes[k + 2])
            theta = sine * alpha
            rhobar = -cosine * alpha
            w = [value / alpha - theta / rho * old for value, old in zip(z, w)]
    return result


def finish_kernel(n0, n1, n2, n3, gauge_ref, q0, q1, q2, inc_ref, field_ref, out_ref, rows_ref):
    blocks, slots, width = inc_ref.shape
    count = rows_ref.shape[0]
    gauges = q0.shape[0]
    step = pl.program_id(0)

    @pl.when(step == 0)
    def _():
        e0, e1, e2 = weights_of([n0, n1, n2, n3])
        width_ = 512

        def body(i, value):
            here = pl.ds(pl.multiple_of(i * width_, width_), width_)
            mixed = q0[here, :] * e0 + q1[here, :] * e1 + q2[here, :] * e2
            gauge = lax.broadcasted_iota(jnp.int32, (count, width_), 1) + i * width_
            hot = jnp.where(gauge_ref[...] == gauge, 1.0, 0.0).astype(BF16)
            return value + pick(hot, mixed)

        rows_ref[...] = lax.fori_loop(0, gauges // width_, body, jnp.zeros(rows_ref.shape, F32))

    weights = inc_ref[...].astype(F32).astype(BF16)
    for b in range(blocks):
        here = pl.ds(b * width, width)
        rows = rows_ref[pl.ds(pl.multiple_of((step * blocks + b) * slots, slots), slots), :]
        added = sum(
            lax.dot_general(weights[b], piece, (((0,), (0,)), ((), ())), preferred_element_type=F32)
            for piece in pieces(rows, 3)
        )
        out_ref[here, :] = field_ref[here, :] + added


def finish(notes, row_gauge, gathered, incidence, field):
    blocks, slots, width = incidence.shape
    hours = field.shape[1]
    count = row_gauge.shape[0]
    step = 8
    whole = lambda shape: pl.BlockSpec(shape, lambda i: (0, 0))
    return pl.pallas_call(
        finish_kernel,
        grid=(blocks // step,),
        in_specs=[whole(n.shape) for n in notes]
        + [whole((count, 1))]
        + [whole(q.shape) for q in gathered]
        + [
            pl.BlockSpec((step, slots, width), lambda i: (i, 0, 0)),
            pl.BlockSpec((step * width, hours), lambda i: (i, 0)),
        ],
        out_specs=pl.BlockSpec((step * width, hours), lambda i: (i, 0)),
        out_shape=jax.ShapeDtypeStruct(field.shape, F32),
        scratch_shapes=[pltpu.VMEM((count, hours), F32)],
        compiler_params=params(56),
        name="finish",
    )(*notes, row_gauge.reshape(count, 1), *gathered, incidence, field)


def shifted(value, axis, by):
    devices = lax.axis_size(axis)
    pairs = [(i, i + by) for i in range(devices) if 0 <= i + by < devices]
    return lax.ppermute(value, axis, pairs)


def window(value):
    return jnp.concatenate([shifted(value, "tm", 1), value, shifted(value, "tm", -1)], axis=0)


def gathered_rows(value):
    owners = lax.axis_size("basin")
    copies = jnp.broadcast_to(value[None], (owners,) + value.shape)
    return lax.all_to_all(copies, "basin", 0, 0, tiled=False)


def over_hours(note):
    blocks = lax.axis_size("tm")
    result = note
    for by in range(1, blocks):
        result = result + lax.ppermute(note, "tm", [(i, (i + by) % blocks) for i in range(blocks)])
    return result


def shards(incidence, row_gauge, gauge_kernel, kernels, observed, first_guess):
    owners = lax.axis_size("basin")
    rows, hours = observed.shape
    gauges = rows * owners
    mats = transforms()
    spec = spectrum(gauge_kernel, kernels, mats[0])
    more = (lax.axis_index("tm") < lax.axis_size("tm") - 1).astype(F32).reshape(1)
    partial, gram = prepare(incidence, first_guess)
    all_gram = lax.all_gather(gram, "basin", axis=1, tiled=True)
    all_rows = lax.all_gather(row_gauge, "basin", axis=0, tiled=True)
    dense = table(row_gauge, partial, gauges).reshape(owners, rows, hours)
    sums = jnp.sum(lax.all_to_all(dense, "basin", 0, 0, tiled=False), axis=0)
    both = jnp.concatenate([observed, shifted(observed, "tm", -1)], axis=0)
    first = (lax.axis_index("basin") * rows).astype(jnp.int32).reshape(1)
    high, low = couple(first, all_rows, all_gram, rows, gauges)

    pulled, note = first_step(more, window(sums), both, spec, mats)
    notes, kept, state = [], [], None
    for k in range(3):
        everyone = gathered_rows(jnp.concatenate([pulled, note], axis=0))
        value = everyone[:, :rows].reshape(gauges, hours)
        notes.append(over_hours(jnp.sum(everyone[:, rows:], axis=0)))
        kept.append(value)
        around = window(mix(high, low, value))
        final = k == 2
        result = next_step(more, notes[-1], around, spec, mats, pulled, state, final)
        if final:
            (note,) = result
        else:
            state, pulled, note = result
    notes.append(over_hours(jnp.sum(gathered_rows(note), axis=0)))
    return finish(notes, row_gauge, kept, incidence, first_guess)


Z_, X_, Y_, C_ = 4, 2, 2, 2
NOTE = 8
HOURS = SPAN // 2


def device(z, x, y, c):
    return (z * X_ + x) * (Y_ * C_) + y * C_ + c


def moved(value, where):
    pairs = []
    for z, x, y, c in np.ndindex(Z_, X_, Y_, C_):
        target = where(z, x, y, c)
        if target is not None:
            pairs.append((device(z, x, y, c), device(*target)))
    return lax.ppermute(value, ("basin", "tm"), pairs)


def to_plane(z, x, y, c):
    return 2 * y + c, x, z & 1, z >> 1


def from_plane(z, x, y, c):
    return 2 * c + y, x, z >> 1, z & 1


def over_x(z, x, y, c):
    return z, 1 - x, y, c


def over_y(z, x, y, c):
    return z, x, 1 - y, c


def over_xy(z, x, y, c):
    return z, 1 - x, 1 - y, c


def over_core(z, x, y, c):
    return z, x, y, 1 - c


def z_pair(z, x, y, c):
    return z ^ 1, x, y, c


def z_middle(z, x, y, c):
    return (3 - z, x, y, c) if z in (1, 2) else None


def z_two(z, x, y, c):
    return z ^ 2, x, y, c


def z_mirror(z, x, y, c):
    return 3 - z, x, y, c


def z_next(z, x, y, c):
    return (z + 1, x, y, c) if z < 3 else None


SQUARE = (over_x, over_y, over_xy)


def split_constant(value):
    out = []
    for _ in range(3):
        piece = value.astype(jnp.bfloat16)
        out.append(piece)
        value = value - piece.astype(np.float64)
    return out


ORDERS = {2: ((0, 1), (1, 0), (0, 0)), 3: ((0, 2), (1, 1), (2, 0), (0, 1), (1, 0), (0, 0))}


def widened(mat, order):
    parts = split_constant(mat)
    return jnp.asarray(np.concatenate([parts[i] for i, _ in ORDERS[order]], axis=1))


def product(wide, value, order):
    parts = pieces(value, order)
    return dot(wide, jnp.concatenate([parts[j] for _, j in ORDERS[order]], axis=0))


def turned_transforms(order):
    half = SPAN // 2
    freq = 2.0 * np.pi * (np.arange(half) + 0.5) / SPAN
    phase = freq[:, None] * np.arange(SPAN)[None, :]
    forward = np.concatenate([np.cos(phase), -np.sin(phase)], axis=0)
    inverse = forward.T * (2.0 / SPAN)
    return [widened(mat, order) for mat in (forward, inverse[:half], inverse[half:], forward[:, :half])]


def turn(waves, spec, sign):
    half = waves.shape[0] // 2
    real, imag = waves[:half], waves[half:]
    kr, ki = spec[:half], spec[half:] * sign
    return jnp.concatenate([real * kr - imag * ki, real * ki + imag * kr], axis=0)


def plane_delayed(before, here, after, spec, forward, last, order):
    rows = here.shape[1]
    pairs = [jnp.concatenate(pair, axis=0) for pair in ((before, here), (here, after))]
    waves = product(forward, jnp.concatenate(pairs, axis=1), order)
    turned = [turn(waves[:, i * rows : (i + 1) * rows], spec, 1.0) for i in range(2)]
    out = product(last, jnp.concatenate(turned, axis=1), order)
    return out[:, :rows], out[:, rows:]


def plane_advanced(here, after, spec, forward, first, order):
    waves = product(forward, jnp.concatenate([here, after], axis=0), order)
    return product(first, turn(waves, spec, -1.0), order)


def describe_kernel(inc_ref, gauge_ref, out_ref):
    blocks, slots, width = inc_ref.shape
    tile = 8
    side = tile * slots
    weights = inc_ref[...].astype(F32).astype(BF16)
    row = lax.broadcasted_iota(jnp.int32, (side, side), 0)
    col = lax.broadcasted_iota(jnp.int32, (side, side), 1)
    same = row // slots == col // slots
    for i in range(blocks // tile):
        flat = weights[i * tile : (i + 1) * tile].reshape(side, width)
        full = lax.dot_general(flat, flat, (((1,), (1,)), ((), ())), preferred_element_type=F32)
        own = jnp.where(same, full, 0.0)
        out_ref[pl.ds(0, slots), pl.ds(i * side, side)] = jnp.sum(own.reshape(tile, slots, side), axis=0)
    out_ref[pl.ds(slots, 8), :] = jnp.broadcast_to(gauge_ref[...].astype(F32), (8, blocks * slots))


def describe(incidence, row_gauge):
    blocks, slots, _ = incidence.shape
    count = blocks * slots
    return pl.pallas_call(
        describe_kernel,
        out_shape=jax.ShapeDtypeStruct((slots + 8, count), F32),
        compiler_params=params(),
        name="describe",
        cost_estimate=SMALL,
    )(incidence, row_gauge.reshape(1, count))


def send_kernel(
    inc_hbm, field_hbm, gauge_hbm, kind_hbm, out_ref, inc_ref, field_ref, gauge_ref, kind_ref, sems, label_sems
):
    blocks, slots, width = inc_ref.shape
    chunks = sems.shape[0]
    step = blocks // chunks
    copies = []
    for i in range(chunks):
        near = pl.ds(i * step, step)
        far = pl.ds(i * step * width, step * width)
        copies.append(
            (
                pltpu.make_async_copy(inc_hbm.at[near], inc_ref.at[near], sems.at[i, 0]),
                pltpu.make_async_copy(field_hbm.at[far], field_ref.at[far], sems.at[i, 1]),
            )
        )
        for copy in copies[-1]:
            copy.start()
    labels = (
        pltpu.make_async_copy(gauge_hbm, gauge_ref, label_sems.at[0]),
        pltpu.make_async_copy(kind_hbm, kind_ref, label_sems.at[1]),
    )
    for copy in labels:
        copy.start()
    for i in range(chunks):
        for copy in copies[i]:
            copy.wait()
        parts = []
        for b in range(i * step, (i + 1) * step):
            weight = inc_ref[b].astype(F32).astype(BF16)
            value = jnp.concatenate(pieces(field_ref[pl.ds(b * width, width), :], 3)[::-1], axis=0)
            parts.append(dot(jnp.concatenate([weight] * 3, axis=1), value))
        out_ref[pl.ds(0, HOURS), pl.ds(i * step * slots, step * slots)] = jnp.transpose(
            jnp.concatenate(parts, axis=0)
        )
    for copy in labels:
        copy.wait()
    count, kinds = gauge_ref.shape[1], kind_ref.shape[1]
    kind = jnp.concatenate([kind_ref[...].astype(F32), jnp.zeros((1, count - kinds), F32)], axis=1)
    out_ref[pl.ds(HOURS, 8), :] = jnp.concatenate(
        [gauge_ref[...].astype(F32), kind, jnp.zeros((6, count), F32)], axis=0
    )


def send(incidence, field, row_gauge, gauge_kernel):
    count, rows = row_gauge.shape[0], gauge_kernel.shape[0]
    chunks = 4
    return pl.pallas_call(
        send_kernel,
        in_specs=[pl.BlockSpec(memory_space=pltpu.HBM)] * 4,
        out_shape=jax.ShapeDtypeStruct((HOURS + 8, count), F32),
        scratch_shapes=[
            pltpu.VMEM(incidence.shape, incidence.dtype),
            pltpu.VMEM(field.shape, F32),
            pltpu.VMEM((1, count), row_gauge.dtype),
            pltpu.VMEM((1, rows), gauge_kernel.dtype),
            pltpu.SemaphoreType.DMA((chunks, 2)),
            pltpu.SemaphoreType.DMA((2,)),
        ],
        compiler_params=params(60),
        name="send",
        cost_estimate=SMALL,
    )(incidence, field, row_gauge.reshape(1, count), gauge_kernel.reshape(1, rows))


def hot_rows(gauge, first, rows):
    mine = (lax.broadcasted_iota(jnp.int32, (rows, gauge.shape[1]), 0) + first).astype(F32)
    return jnp.where(gauge == mine, 1.0, 0.0).astype(BF16)


def spread_kernel(first_ref, mine_ref, other_ref, *out_refs):
    rows = out_refs[0].shape[1]
    both = jnp.concatenate([mine_ref[...], other_ref[...]], axis=1)
    stacked = jnp.concatenate(pieces(both[:HOURS], 3), axis=0)
    for m, out_ref in enumerate(out_refs):
        hot = hot_rows(both[HOURS : HOURS + 1], first_ref[m], rows)
        result = lax.dot_general(stacked, hot, (((1,), (1,)), ((), ())), preferred_element_type=F32)
        out_ref[...] = (result[2 * HOURS :] + result[HOURS : 2 * HOURS]) + result[:HOURS]


def spread(first, parcels, rows):
    return pl.pallas_call(
        spread_kernel,
        in_specs=[pl.BlockSpec(memory_space=pltpu.SMEM)] + [pl.BlockSpec(memory_space=pltpu.VMEM)] * 2,
        out_shape=[jax.ShapeDtypeStruct((HOURS, rows), F32)] * 4,
        compiler_params=params(),
        name="spread",
        cost_estimate=SMALL,
    )(first, *parcels)


def plane_couple_kernel(last, first_ref, *refs):
    if last:
        all_ref, before_ref, high_ref, low_ref, total_ref, meta_ref = refs
        total_ref[...] = before_ref[...]
    else:
        all_ref, total_ref, meta_ref = refs
        total_ref[...] = jnp.zeros_like(total_ref)
    parts, height, count = meta_ref.shape
    slots = height - 8
    cols, rows = total_ref.shape
    tile = 256
    for i in range(parts):
        meta_ref[i] = all_ref[:, i * count : (i + 1) * count]
    row = lax.broadcasted_iota(jnp.int32, (tile, tile), 0)
    col = lax.broadcasted_iota(jnp.int32, (tile, tile), 1)
    same = row // slots == col // slots

    def body(i, carry):
        gauge = meta_ref[i, slots : slots + 1, :]
        near = []
        for j in range(count // tile):
            here = slice(j * tile, (j + 1) * tile)
            block = jnp.concatenate([meta_ref[i, :slots, here]] * (tile // slots), axis=0)
            block = jnp.where(same, block, 0.0).astype(BF16)
            mine = jnp.concatenate(
                [hot_rows(gauge[:, here], first_ref[4 + h], rows // 2) for h in range(2)], axis=0
            )
            near.append(
                lax.dot_general(block, mine, (((1,), (1,)), ((), ())), preferred_element_type=F32)
            )
        near = jnp.concatenate(near, axis=0)
        high = near.astype(BF16)
        rest = near - high.astype(F32)
        hot = jnp.concatenate([hot_rows(gauge, first_ref[m], cols // 4) for m in range(4)], axis=0)
        total_ref[...] += dot(hot, high)

        @pl.when(jnp.max(jnp.abs(rest)) > 0.0)
        def _():
            total_ref[...] += dot(hot, rest.astype(BF16))

        return carry

    lax.fori_loop(0, parts, body, 0)
    if last:
        high, low = pieces(total_ref[...], 2)
        high_ref[...] = high
        low_ref[...] = low


def plane_couple(first, meta, rows, before=None):
    height, wide = meta.shape
    parts = 2 * X_
    shape = (4 * rows, 2 * rows)
    last = before is not None
    args = [first, meta] + ([before] if last else [])
    scratch = [pltpu.VMEM((parts, height, wide // parts), F32)]
    return pl.pallas_call(
        functools.partial(plane_couple_kernel, last),
        in_specs=[pl.BlockSpec(memory_space=pltpu.SMEM)]
        + [pl.BlockSpec(memory_space=pltpu.VMEM)] * (len(args) - 1),
        out_shape=[jax.ShapeDtypeStruct(shape, BF16)] * 2 if last else jax.ShapeDtypeStruct(shape, F32),
        scratch_shapes=([pltpu.VMEM(shape, F32)] if last else []) + scratch,
        compiler_params=params(),
        name="plane_couple",
        cost_estimate=pl.CostEstimate(
            flops=2 * 8 * wide * rows * rows, bytes_accessed=2_000_000, transcendentals=0
        ),
    )(*args)


def plane_mix_kernel(high_ref, low_ref, a_ref, b_ref, c_ref, d_ref, *refs):
    *extra, mine_ref, other_ref = refs
    refs = (a_ref, b_ref, c_ref, d_ref)
    height, rows = a_ref.shape
    body = pl.ds(0, HOURS)
    one, two = pieces(jnp.concatenate([ref[body, :] for ref in refs], axis=1), 2)
    both = dot(jnp.concatenate([two, one], axis=0), high_ref[...])
    result = (both[:HOURS] + dot(one, low_ref[...])) + both[HOURS:]
    mine_ref[body, :] = result[:, :rows]
    other_ref[body, :] = result[:, rows:]
    if height > HOURS:
        tail = pl.ds(HOURS, NOTE)
        note = sum(ref[tail, :] for ref in refs)
        mine_ref[tail, :] = note
        other_ref[tail, :] = note
    for ref in extra:
        other_ref[pl.ds(height, ref.shape[0]), :] = ref[...]


def plane_mix(coupling, values, extra):
    height, rows = values[0].shape
    return pl.pallas_call(
        plane_mix_kernel,
        out_shape=[
            jax.ShapeDtypeStruct((height, rows), F32),
            jax.ShapeDtypeStruct((height + sum(value.shape[0] for value in extra), rows), F32),
        ],
        compiler_params=params(),
        name="plane_mix",
        cost_estimate=SMALL,
    )(*coupling, *values, *extra)


def plane_rows_kernel(first_ref, meta_ref, meta_other_ref, a_ref, b_ref, c_ref, d_ref, *refs):
    if len(refs) > 2:
        *stack, last_ref, beside_ref, mine_ref, other_ref, stack_ref = refs
    else:
        mine_ref, other_ref = refs
    rows = a_ref.shape[1]
    value = jnp.concatenate([ref[pl.ds(0, HOURS), :] for ref in (a_ref, b_ref, c_ref, d_ref)], axis=1)
    one, two = pieces(value, 2)
    stacked = jnp.concatenate([two, one], axis=0)
    picked = []
    for ref in (meta_ref, meta_other_ref):
        gauge = ref[0:1, :]
        hot = jnp.concatenate([hot_rows(gauge, first_ref[m], rows) for m in range(4)], axis=0)
        both = dot(stacked, hot)
        picked.append(both[:HOURS] + both[HOURS:])
    mine_ref[...] = picked[0]
    count = picked[1].shape[1] // rows
    for i in range(count):
        other_ref[pl.ds(i * HOURS, HOURS), :] = picked[1][:, i * rows : (i + 1) * rows]
    if len(refs) > 2:
        top = stack_ref.shape[0] - HOURS
        for ref in stack:
            stack_ref[pl.ds(0, top), :] = ref[...]
        for i in range(count):
            here = pl.ds(i * rows, rows)
            beside = beside_ref[pl.ds(beside_ref.shape[0] - (count - i) * HOURS, HOURS), :]
            stack_ref[pl.ds(top, HOURS), here] = last_ref[:, here] + beside


def plane_rows(first, metas, values, before):
    rows = values[0].shape[1]
    slots = metas[0].shape[1]
    args = [first, *metas, *values, *before]
    shapes = [(HOURS, slots), (slots // rows * HOURS, rows)]
    if before:
        shapes.append(((len(before) - 1) * HOURS, slots))
    return pl.pallas_call(
        plane_rows_kernel,
        in_specs=[pl.BlockSpec(memory_space=pltpu.SMEM)]
        + [pl.BlockSpec(memory_space=pltpu.VMEM)] * (len(args) - 1),
        out_shape=[jax.ShapeDtypeStruct(shape, F32) for shape in shapes],
        compiler_params=params(),
        name="plane_rows",
        cost_estimate=pl.CostEstimate(flops=1_000_000_000, bytes_accessed=2_000_000, transcendentals=0),
    )(*args)


def gain(kernels):
    return jnp.max(jnp.sum(kernels, axis=1, keepdims=True), axis=0, keepdims=True)


def spectra(kind, kernels, wide):
    classes = kernels.shape[0]
    row = lax.broadcasted_iota(jnp.int32, (classes, kind.shape[1]), 0).astype(F32)
    hot = jnp.where(row == kind, 1.0, 0.0).astype(BF16)
    taps = jnp.transpose(kernels / gain(kernels))
    chosen = dot(jnp.concatenate(pieces(taps, 3)[::-1], axis=1), jnp.concatenate([hot] * 3, axis=0))
    return product(wide, chosen, 3)


def plane_spectrum_kernel(class_ref, kernels_ref, wide_ref, out_ref):
    kind = class_ref[1:2, : out_ref.shape[1]]
    out_ref[...] = spectra(kind, kernels_ref[...], wide_ref[...])


def plane_spectrum(meta, kernels, wide, rows):
    return pl.pallas_call(
        plane_spectrum_kernel,
        out_shape=jax.ShapeDtypeStruct((SPAN, rows), F32),
        compiler_params=params(),
        name="plane_spectrum",
        cost_estimate=SMALL,
    )(meta, kernels, wide)


def sides(even, pair, middle):
    return jnp.where(even, middle, pair), jnp.where(even, pair, middle)


def plane_call(kernel, name, shapes, flags, args):
    return pl.pallas_call(
        kernel,
        in_specs=[pl.BlockSpec(memory_space=pltpu.SMEM)] * len(flags)
        + [pl.BlockSpec(memory_space=pltpu.VMEM)] * len(args),
        out_shape=[jax.ShapeDtypeStruct(shape, F32) for shape in shapes],
        compiler_params=params(),
        name=name,
        cost_estimate=SMALL,
    )(*flags, *args)


def plane_first_kernel(
    flag_ref, here_ref, pair_ref, middle_ref, spec_ref, kernels_ref, forward3, last3, forward, first, out_ref
):
    spec = spec_ref[...]
    before, after = sides(flag_ref[0] > 0.5, pair_ref[...], middle_ref[...])
    here = here_ref[...]
    both = plane_delayed(before[:HOURS], here[:HOURS], after[:HOURS], spec, forward3[...], last3[...], 3)
    scale = gain(kernels_ref[...])
    now = here[HOURS:] - both[0] * scale
    later = (after[HOURS:] - both[1] * scale) * flag_ref[1]
    out_ref[...] = plane_advanced(now, later, spec, forward[...], first[...], 2)


def plane_delay_kernel(flag_ref, here_ref, pair_ref, middle_ref, spec_ref, forward, last, out_ref):
    body = pl.ds(0, HOURS)
    before, after = sides(flag_ref[0] > 0.5, pair_ref[body, :], middle_ref[body, :])
    out = plane_delayed(before, here_ref[body, :], after, spec_ref[...], forward[...], last[...], 2)
    for i in range(2):
        out_ref[pl.ds(i * HOURS, HOURS), :] = out[i]


def write_note(ref, rows):
    tail = [jnp.zeros((NOTE - len(rows), ref.shape[1]), F32)]
    ref[pl.ds(HOURS, NOTE), :] = jnp.concatenate(rows + tail, axis=0)


def plane_open_kernel(
    flag_ref, here_ref, pair_ref, middle_ref, pulled_ref, spec_ref, forward, first, last, out_ref, delayed_ref
):
    here = here_ref[...]
    spec = spec_ref[...]
    before, after = sides(flag_ref[0] > 0.5, pair_ref[...], middle_ref[...])
    now, later = plane_delayed(before, here, after, spec, forward[...], last[...], 2)
    out_ref[pl.ds(0, HOURS), :] = plane_advanced(now, later * flag_ref[1], spec, forward[...], first[...], 2)
    write_note(out_ref, [lanes(pulled_ref[...], here), lanes(now, now)])
    delayed_ref[pl.ds(0, HOURS), :] = now
    delayed_ref[pl.ds(HOURS, HOURS), :] = later


def plane_step_kernel(
    flag_ref,
    here_ref,
    pair_ref,
    two_ref,
    mirror_ref,
    pulled_ref,
    delayed_ref,
    old_z_ref,
    old_s_ref,
    old_delayed_ref,
    spec_ref,
    forward,
    first,
    total_ref,
    out_ref,
    kept_ref,
):
    tail, body = pl.ds(HOURS, NOTE), pl.ds(0, HOURS)
    total_ref[...] = (here_ref[tail, :] + pair_ref[tail, :]) + (two_ref[...] + mirror_ref[...])
    inverse = total(total_ref, 0) / total(total_ref, 1)
    z = pulled_ref[body, :] * inverse - old_z_ref[...]
    s = here_ref[body, :] * inverse - old_s_ref[...]
    both = delayed_ref[...] * inverse - old_delayed_ref[...]
    now, later = both[:HOURS], both[HOURS:]
    following = plane_advanced(now, later * flag_ref[1], spec_ref[...], forward[...], first[...], 2)
    out_ref[body, :] = following * inverse
    write_note(out_ref, [lanes(z, s), lanes(now, now)])
    for i, value in enumerate((z, s, now)):
        kept_ref[pl.ds(i * HOURS, HOURS), :] = value


def plane_close_kernel(
    here_ref,
    before_ref,
    pulled_ref,
    kept_ref,
    old_z_ref,
    old_s_ref,
    old_delayed_ref,
    open_ref,
    spec_ref,
    kernels_ref,
    forward,
    last,
    out_ref,
):
    body = pl.ds(0, HOURS)
    here, raw = here_ref[body, :], pulled_ref[body, :]
    waves = product(forward[...], jnp.concatenate([before_ref[body, :], here], axis=0), 2)
    now = product(last[...], turn(waves, spec_ref[...], 1.0), 2)
    z, s, delayed = (kept_ref[pl.ds(i * HOURS, HOURS), :] for i in range(3))
    note = [pulled_ref[HOURS + i : HOURS + i + 1, :] for i in range(2)]
    for left in (raw, z, old_z_ref[...]):
        note += [lanes(left, right) for right in (here, s, old_s_ref[...])]
    parts = (now, delayed, old_delayed_ref[body, :])
    for i in range(3):
        note += [lanes(parts[i], parts[j]) for j in range(i, 3)]
    known = [total(open_ref, 0), total(open_ref, 1), gain(kernels_ref[...])]
    note = [jnp.sum(jnp.concatenate(note, axis=0), axis=1, keepdims=True)]
    note += [value / out_ref.shape[0] for value in known]
    count = sum(value.shape[0] for value in note)
    note = jnp.concatenate(note + [jnp.zeros((24 - count, 1), F32)], axis=0)
    shape = (24, out_ref.shape[2])
    row, col = (lax.broadcasted_iota(jnp.int32, shape, i) for i in range(2))
    note = jnp.sum(jnp.where(row == col, jnp.broadcast_to(note, shape), 0.0), axis=0, keepdims=True)
    out_ref[...] = jnp.broadcast_to(note[None], out_ref.shape)


def plane_weights(close):
    entry = lambda i: close[:, i : i + 1]
    n1, t1, scale = (entry(17 + i) for i in range(3))
    n2, t2 = entry(0), entry(1)
    a1 = t1 / n1
    a2, r2 = (t2 / n2) / a1, n2 / n1
    plain = (1.0, -a2, -r2)
    n3 = sum(plain[i] * plain[j] * entry(2 + 3 * i + j) for i in range(3) for j in range(3))
    pairs = [(i, j) for i in range(3) for j in range(i, 3)]
    t3 = sum(
        plain[i] * plain[j] * entry(11 + n) * (1.0 if i == j else 2.0) for n, (i, j) in enumerate(pairs)
    )
    a3, r3 = (t3 / n3) / a1, n3 / n2
    unit = 1.0 / (a1 * scale)
    c3 = unit / (a3 * (a2 - r2) - r3)
    c2 = -a3 * c3
    c1 = unit - r2 * c2
    step = c2 - c3 * a2
    return c1 - step - c3 * r2, step / a1, c3


def plane_combine_kernel(close_ref, stack_ref, mine_ref, beside_ref, out_ref):
    rows = beside_ref.shape[1]
    close = jnp.sum(close_ref[...], axis=0)[0:1, :]
    e0, e1, e2 = plane_weights(close)
    for i in range(out_ref.shape[0] // rows):
        here = pl.ds(i * rows, rows)
        last = mine_ref[:, here] + beside_ref[pl.ds(i * HOURS, HOURS), :]
        value = stack_ref[pl.ds(0, HOURS), here] * e0 + stack_ref[pl.ds(HOURS, HOURS), here] * e1 + last * e2
        out_ref[here, :] = jnp.transpose(value)


def plane_finish_kernel(rows_ref, inc_ref, field_ref, out_ref):
    blocks, slots, width = inc_ref.shape
    weights = inc_ref[...].astype(F32).astype(BF16)
    for b in range(blocks):
        here = pl.ds(b * width, width)
        rows = jnp.concatenate(pieces(rows_ref[pl.ds(b * slots, slots), :], 2), axis=0)
        twice = jnp.concatenate([weights[b]] * 2, axis=0)
        added = lax.dot_general(twice, rows, (((0,), (0,)), ((), ())), preferred_element_type=F32)
        out_ref[here, :] = field_ref[here, :] + added


def plane_finish(rows, incidence, field):
    blocks, slots, width = incidence.shape
    hours = field.shape[1]
    step = 16
    return pl.pallas_call(
        plane_finish_kernel,
        grid=(blocks // step,),
        in_specs=[
            pl.BlockSpec((step * slots, hours), lambda i: (i, 0)),
            pl.BlockSpec((step, slots, width), lambda i: (i, 0, 0)),
            pl.BlockSpec((step * width, hours), lambda i: (i, 0)),
        ],
        out_specs=pl.BlockSpec((step * width, hours), lambda i: (i, 0)),
        out_shape=jax.ShapeDtypeStruct(field.shape, F32),
        compiler_params=params(),
        name="plane_finish",
    )(rows, incidence, field)


def plane_shards(incidence, row_gauge, gauge_kernel, kernels, observed, first_guess):
    rows, hours = observed.shape
    basin, tm = lax.axis_index("basin"), lax.axis_index("tm")
    z, x, y, c = basin // X_, basin % X_, tm // C_, tm % C_
    place = 2 * y + x
    first = jnp.stack([4 * c + (place ^ m) for m in range(4)] + [4 * c + place, 4 * (1 - c) + place])
    first = (first * rows).astype(jnp.int32)
    flags = jnp.stack([1 - z % 2, (z < Z_ - 1).astype(z.dtype), (z > 0).astype(z.dtype)]).astype(F32)
    forward, inverse_first, inverse_last, _ = turned_transforms(2)
    forward3, _, inverse_last3, short3 = turned_transforms(3)
    block, noted = (hours, rows), (hours + NOTE, rows)

    seen = moved(observed, to_plane)
    parcel = send(incidence, first_guess, row_gauge, gauge_kernel)
    parcel, near = lax.optimization_barrier((parcel, incidence))
    parcel = moved(parcel, to_plane)
    near, seen = lax.optimization_barrier((near, seen))
    meta = describe(near, row_gauge)
    meta = jnp.concatenate([meta, moved(meta, over_x)], axis=1)
    meta = jnp.concatenate([meta, moved(meta, z_pair)], axis=1)
    parcel, seen = lax.optimization_barrier((parcel, seen))
    parcels = [parcel, moved(parcel, over_core)]
    spec = plane_spectrum(parcel[hours:], kernels, short3, rows)
    parcels[1], seen, meta, spec = lax.optimization_barrier((parcels[1], seen, meta, spec))
    half = meta.shape[1] // 2
    far = moved(jnp.where(c == 0, meta[:, :half], meta[:, half:]), z_two)
    dense = spread(first, parcels, rows)
    metas = [value[hours:] for value in parcels]
    sums = dense[0] + sum(moved(value, where) for value, where in zip(dense[1:], SQUARE))
    sums, far = lax.optimization_barrier((sums, far))
    around = [meta, jnp.concatenate([far, moved(far, over_core)], axis=1)]
    sums = jnp.concatenate([sums, jnp.transpose(seen)], axis=0)
    sums = [sums, moved(sums, z_pair), moved(sums, z_middle)]
    coupled = plane_couple(first, around[0], rows)
    coupled, sums = lax.optimization_barrier((coupled, sums))
    coupling = plane_couple(first, around[1], rows, coupled)
    (pulled0,) = plane_call(
        plane_first_kernel,
        "plane_first",
        [block],
        [flags],
        [*sums, spec, kernels, forward3, inverse_last3, forward, inverse_first],
    )

    def mixing(pulled, extra):
        values = [pulled] + [moved(pulled, where) for where in SQUARE]
        mine, other = plane_mix(coupling, values, extra)
        beside = moved(other, over_core)
        return values, mine + beside[: pulled.shape[0]], beside

    values, mixed0, _ = mixing(pulled0, [])
    picked, theirs = plane_rows(first, metas, values, [])
    sums = [mixed0, moved(mixed0, z_pair), moved(mixed0, z_middle)]
    pulled1, delayed0 = plane_call(
        plane_open_kernel,
        "plane_open",
        [noted, (2 * hours, rows)],
        [flags],
        [*sums, pulled0, spec, forward, inverse_first, inverse_last],
    )

    values, mixed1, beside = mixing(pulled1, [theirs])
    picked, theirs, stack = plane_rows(first, metas, values, [picked, beside])
    sums = [mixed1, moved(mixed1, z_pair), moved(mixed1, z_middle)]
    two, mirror = moved(mixed1[hours:], z_two), moved(mixed1[hours:], z_mirror)
    (delayed1,) = plane_call(
        plane_delay_kernel, "plane_delay", [(2 * hours, rows)], [flags], [*sums, spec, forward, inverse_last]
    )
    open_note, pulled2, kept = plane_call(
        plane_step_kernel,
        "plane_step",
        [(NOTE, rows), noted, (3 * hours, rows)],
        [flags],
        [*sums[:2], two, mirror, pulled1, delayed1, pulled0, mixed0, delayed0, spec, forward, inverse_first],
    )

    values, mixed2, beside = mixing(pulled2, [theirs])
    picked, theirs, stack = plane_rows(first, metas, values, [stack, picked, beside])
    (note,) = plane_call(
        plane_close_kernel,
        "plane_close",
        [(Z_ * X_ * Y_ * C_, 8, rows // 2)],
        [],
        [
            *(mixed2, moved(mixed2, z_next), pulled2, kept, pulled0, mixed0, delayed0),
            *(open_note, spec, kernels, forward, inverse_last),
        ],
    )
    close_note = lax.all_to_all(note, ("basin", "tm"), 0, 0, tiled=False)
    (answer,) = plane_call(
        plane_combine_kernel,
        "plane_combine",
        [(parcel.shape[1], hours)],
        [],
        [close_note, stack, picked, moved(theirs, over_core)],
    )
    return plane_finish(moved(answer, from_plane), incidence, first_guess)


def solution(mesh):
    planes = dict(mesh.shape) == {"basin": Z_ * X_, "tm": Y_ * C_}
    in_specs = (
        P("basin", None, None),
        P("basin"),
        P("basin"),
        P(),
        P("basin", "tm"),
        P("basin", "tm"),
    )
    return jax.shard_map(
        plane_shards if planes else shards, mesh=mesh, in_specs=in_specs, out_specs=P("basin", "tm"), check_vma=False
    )
```

```python
import functools

import jax
import jax.numpy as jnp
import numpy as np
from jax import lax
from jax.experimental import pallas as pl
from jax.experimental.pallas import tpu as pltpu
from jax.sharding import PartitionSpec as P

F32 = jnp.float32
BF16 = jnp.bfloat16
HIGH = lax.Precision.HIGHEST
SPAN = 256
MIB = 1024 * 1024


SMALL = pl.CostEstimate(flops=1, bytes_accessed=1, transcendentals=0)


def params(mib=16):
    return pltpu.CompilerParams(vmem_limit_bytes=mib * MIB)


def transforms():
    half = SPAN // 2
    freq = 2.0 * np.pi * (np.arange(half) + 0.5) / SPAN
    phase = np.arange(SPAN)[:, None] * freq[None, :]
    forward = np.concatenate([np.cos(phase), -np.sin(phase)], axis=1)
    inverse = forward.T * (2.0 / SPAN)
    return (
        jnp.asarray(forward, F32),
        jnp.asarray(inverse[:, :half], F32),
        jnp.asarray(inverse[:, half:], F32),
    )


def dot(a, b):
    return jnp.dot(a, b, preferred_element_type=F32)


def exact(a, b):
    return jnp.dot(a, b, precision=HIGH, preferred_element_type=F32)


def pieces(value, count):
    out = []
    for _ in range(count):
        piece = value.astype(BF16)
        out.append(piece)
        value = value - piece.astype(F32)
    return out


def pick(hot, value):
    return sum(dot(hot, piece) for piece in pieces(value, 3))


def prepare_kernel(inc_ref, field_ref, partial_ref, gram_ref):
    blocks, slots, width = inc_ref.shape
    rows = blocks * slots
    weights = inc_ref[...].astype(F32).astype(BF16)
    for b in range(blocks):
        value = field_ref[pl.ds(b * width, width), :]
        partial_ref[pl.ds(b * slots, slots), :] = pick(weights[b], value)
    flat = weights.reshape(rows, width)
    full = lax.dot_general(flat, flat, (((1,), (1,)), ((), ())), preferred_element_type=F32)
    row = lax.broadcasted_iota(jnp.int32, (rows, rows), 0)
    col = lax.broadcasted_iota(jnp.int32, (rows, rows), 1)
    own = jnp.where(row // slots == col // slots, full, 0.0)
    gram_ref[...] = jnp.sum(own.reshape(blocks, slots, rows), axis=0)


def prepare(incidence, field):
    blocks, slots, width = incidence.shape
    hours = field.shape[1]
    step = 8
    return pl.pallas_call(
        prepare_kernel,
        grid=(blocks // step,),
        in_specs=[
            pl.BlockSpec((step, slots, width), lambda i: (i, 0, 0)),
            pl.BlockSpec((step * width, hours), lambda i: (i, 0)),
        ],
        out_specs=[
            pl.BlockSpec((step * slots, hours), lambda i: (i, 0)),
            pl.BlockSpec((slots, step * slots), lambda i: (0, i)),
        ],
        out_shape=[
            jax.ShapeDtypeStruct((blocks * slots, hours), F32),
            jax.ShapeDtypeStruct((slots, blocks * slots), F32),
        ],
        compiler_params=params(56),
        name="prepare",
    )(incidence, field)


def table_kernel(gauge_ref, partial_ref, out_ref):
    slots = partial_ref.shape[0]
    rows = out_ref.shape[0]
    first = pl.program_id(0) * rows
    gauge = lax.broadcasted_iota(jnp.int32, (rows, slots), 0) + first
    hot = jnp.where(gauge_ref[...] == gauge, 1.0, 0.0).astype(BF16)
    out_ref[...] = pick(hot, partial_ref[...])


def table(row_gauge, partial, gauges):
    slots, hours = partial.shape
    step = 256
    return pl.pallas_call(
        table_kernel,
        grid=(gauges // step,),
        in_specs=[
            pl.BlockSpec((1, slots), lambda i: (0, 0)),
            pl.BlockSpec((slots, hours), lambda i: (0, 0)),
        ],
        out_specs=pl.BlockSpec((step, hours), lambda i: (i, 0)),
        out_shape=jax.ShapeDtypeStruct((gauges, hours), F32),
        compiler_params=params(56),
        name="table",
    )(row_gauge.reshape(1, slots), partial)


def couple_kernel(first_ref, lane_ref, sub_ref, gram_ref, high_ref, low_ref, near_ref):
    slots = gram_ref.shape[0]
    count = lane_ref.shape[1]
    rows, cols = high_ref.shape
    tile = 256
    first = first_ref[0]

    @pl.when(pl.program_id(0) == 0)
    def _():
        row = lax.broadcasted_iota(jnp.int32, (tile, tile), 0)
        col = lax.broadcasted_iota(jnp.int32, (tile, tile), 1)
        same = row // slots == col // slots
        mine = lax.broadcasted_iota(jnp.int32, (rows, tile), 0) + first

        def body(i, carry):
            here = pl.ds(pl.multiple_of(i * tile, tile), tile)
            block = jnp.concatenate([gram_ref[:, here]] * (tile // slots), axis=0)
            block = jnp.where(same, block, 0.0).astype(BF16)
            hot = jnp.where(lane_ref[:, here] == mine, 1.0, 0.0).astype(BF16)
            near_ref[:, here] = dot(hot, block)
            return carry

        lax.fori_loop(0, count // tile, body, 0)

    def chunk(i, total):
        here = pl.ds(pl.multiple_of(i * 1024, 1024), 1024)
        gauge = lax.broadcasted_iota(jnp.int32, (1024, cols), 1) + pl.program_id(0) * cols
        hot = jnp.where(sub_ref[here, :] == gauge, 1.0, 0.0).astype(BF16)
        near = near_ref[:, here]
        high = near.astype(BF16)
        low = (near - high.astype(F32)).astype(BF16)
        return total + dot(high, hot) + dot(low, hot)

    total = lax.fori_loop(0, count // 1024, chunk, jnp.zeros((rows, cols), F32))
    high, low = pieces(total, 2)
    high_ref[...] = high
    low_ref[...] = low


def couple(first, row_gauge, gram, rows, gauges):
    count = row_gauge.shape[0]
    step = 256
    return pl.pallas_call(
        couple_kernel,
        grid=(gauges // step,),
        in_specs=[
            pl.BlockSpec(memory_space=pltpu.SMEM),
            pl.BlockSpec((1, count), lambda i: (0, 0)),
            pl.BlockSpec((count, 1), lambda i: (0, 0)),
            pl.BlockSpec(gram.shape, lambda i: (0, 0)),
        ],
        out_specs=[pl.BlockSpec((rows, step), lambda i: (0, i))] * 2,
        out_shape=[jax.ShapeDtypeStruct((rows, gauges), BF16)] * 2,
        scratch_shapes=[pltpu.VMEM((rows, count), F32)],
        compiler_params=params(56),
        name="couple",
    )(first, row_gauge.reshape(1, count), row_gauge.reshape(count, 1), gram)


def mix_kernel(high_ref, low_ref, value_ref, out_ref):
    high = high_ref[...]
    low = low_ref[...]
    one, two, three = pieces(value_ref[...], 3)
    out_ref[...] = (dot(high, three) + dot(low, two)) + (dot(high, two) + dot(low, one)) + dot(high, one)


def mix(high, low, value):
    return pl.pallas_call(
        mix_kernel,
        out_shape=jax.ShapeDtypeStruct((high.shape[0], value.shape[1]), F32),
        compiler_params=params(56),
        name="mix",
    )(high, low, value)


def spectrum_kernel(class_ref, kernels_ref, forward_ref, out_ref):
    rows = class_ref.shape[0]
    classes, taps = kernels_ref.shape
    kind = lax.broadcasted_iota(jnp.int32, (rows, classes), 1)
    hot = jnp.where(class_ref[...] == kind, 1.0, 0.0)
    out_ref[...] = exact(exact(hot, kernels_ref[...]), forward_ref[pl.ds(0, taps), :])


def spectrum(gauge_kernel, kernels, forward):
    rows = gauge_kernel.shape[0]
    return pl.pallas_call(
        spectrum_kernel,
        out_shape=jax.ShapeDtypeStruct((rows, SPAN), F32),
        compiler_params=params(56),
        name="spectrum",
    )(gauge_kernel.reshape(rows, 1), kernels, forward)


def delayed(before, here, after, spec, forward, inverse_last):
    rows, half = here.shape
    stacked = jnp.concatenate(
        [jnp.concatenate([before, here], axis=1), jnp.concatenate([here, after], axis=1)], axis=0
    )
    waves = exact(stacked, forward)
    real, imag = waves[:, :half], waves[:, half:]
    kr = jnp.concatenate([spec[:, :half]] * 2, axis=0)
    ki = jnp.concatenate([spec[:, half:]] * 2, axis=0)
    turned = jnp.concatenate([real * kr - imag * ki, real * ki + imag * kr], axis=1)
    out = exact(turned, inverse_last)
    return out[:rows], out[rows:]


def advanced(here, after, spec, forward, inverse_first):
    half = here.shape[1]
    waves = exact(jnp.concatenate([here, after], axis=1), forward)
    real, imag = waves[:, :half], waves[:, half:]
    kr, ki = spec[:, :half], spec[:, half:]
    turned = jnp.concatenate([real * kr + imag * ki, imag * kr - real * ki], axis=1)
    return exact(turned, inverse_first)


def lanes(a, b):
    return jnp.sum(a * b, axis=0, keepdims=True)


def total(ref, row):
    return jnp.sum(ref[row : row + 1, :], axis=1, keepdims=True)


def ratios(ref):
    square = total(ref, 0)
    alpha = jnp.sqrt(square)
    beta = jnp.sqrt(jnp.maximum(total(ref, 1) / square - 2.0 * total(ref, 2) + square, 0.0))
    return alpha, beta


def first_kernel(
    more_ref, sums_ref, observed_ref, spec_ref, forward_ref, first_ref, last_ref, out_ref, note_ref
):
    rows, half = observed_ref.shape[0] // 2, observed_ref.shape[1]
    spec, forward = spec_ref[...], forward_ref[...]
    before, here, after = (sums_ref[pl.ds(i * rows, rows), :] for i in range(3))
    now, later = delayed(before, here, after, spec, forward, last_ref[...])
    start = observed_ref[pl.ds(0, rows), :] - now
    start_later = (observed_ref[pl.ds(rows, rows), :] - later) * more_ref[0]
    out_ref[...] = advanced(start, start_later, spec, forward, first_ref[...])
    note_ref[...] = jnp.concatenate([lanes(start, start), jnp.zeros((7, half), F32)], axis=0)


def first_step(more, sums, observed, spec, mats):
    rows, half = spec.shape[0], observed.shape[1]
    return pl.pallas_call(
        first_kernel,
        in_specs=[pl.BlockSpec(memory_space=pltpu.SMEM)] + [pl.BlockSpec(memory_space=pltpu.VMEM)] * 6,
        out_shape=[jax.ShapeDtypeStruct((rows, half), F32), jax.ShapeDtypeStruct((8, half), F32)],
        compiler_params=params(56),
        name="first_step",
    )(more, sums, observed, spec, *mats)


def step_kernel(
    opening,
    final,
    more_ref,
    note_ref,
    sums_ref,
    spec_ref,
    forward_ref,
    first_ref,
    last_ref,
    pulled_ref,
    *refs,
):
    if opening:
        state_ref = None
    else:
        state_ref, *refs = refs
    if final:
        (out_note_ref,) = refs
    else:
        new_ref, out_ref, out_note_ref = refs
    rows, half = pulled_ref.shape
    spec, forward = spec_ref[...], forward_ref[...]
    if opening:
        scale = 1.0 / jnp.sqrt(total(note_ref, 0))
        along = sums_ref[...] * scale
        new_s, new_su = along, along
        new_zu = pulled_ref[...] * scale
        new_z = new_zu
    else:
        alpha, beta = ratios(note_ref)
        a, b, g = 1.0 / (alpha * beta), alpha / beta, beta / alpha
        wide = pl.ds(0, 3 * rows), pl.ds(3 * rows, 3 * rows)
        new_su = sums_ref[...] * a - state_ref[wide[1], :] * b
        new_s = new_su - state_ref[wide[0], :] * g
        new_zu = pulled_ref[...] * a - state_ref[pl.ds(7 * rows, rows), :] * b
        new_z = new_zu - state_ref[pl.ds(6 * rows, rows), :] * g
    before, here, after = (new_s[i * rows : (i + 1) * rows] for i in range(3))
    now, later = delayed(before, here, after, spec, forward, last_ref[...])
    out_note_ref[...] = jnp.concatenate(
        [lanes(new_z, here), lanes(now, now), lanes(new_zu, here), jnp.zeros((5, half), F32)], axis=0
    )
    if not final:
        new_ref[pl.ds(0, 3 * rows), :] = new_s
        new_ref[pl.ds(3 * rows, 3 * rows), :] = new_su
        new_ref[pl.ds(6 * rows, rows), :] = new_z
        new_ref[pl.ds(7 * rows, rows), :] = new_zu
        out_ref[...] = advanced(now, later * more_ref[0], spec, forward, first_ref[...])


def next_step(more, note, sums, spec, mats, pulled, state, final):
    rows, half = pulled.shape
    opening = state is None
    shapes = [
        jax.ShapeDtypeStruct((8 * rows, half), F32),
        jax.ShapeDtypeStruct((rows, half), F32),
        jax.ShapeDtypeStruct((8, half), F32),
    ]
    args = [more, note, sums, spec, *mats, pulled] + ([] if opening else [state])
    return pl.pallas_call(
        functools.partial(step_kernel, opening, final),
        in_specs=[pl.BlockSpec(memory_space=pltpu.SMEM)]
        + [pl.BlockSpec(memory_space=pltpu.VMEM)] * (len(args) - 1),
        out_shape=shapes[2:] if final else shapes,
        compiler_params=params(56),
        name="next_step",
    )(*args)


def weights_of(notes):
    start = jnp.sqrt(total(notes[0], 0))
    zero = jnp.zeros_like(start)
    units = [1.0 / start, zero, zero]
    z, zu = list(units), list(units)
    phibar = start
    alpha, beta = ratios(notes[1])
    rhobar = alpha
    w = [value / alpha for value in z]
    result = [zero] * 3
    steps = len(notes) - 1
    for k in range(steps):
        rho = jnp.sqrt(rhobar * rhobar + beta * beta)
        cosine, sine = rhobar / rho, beta / rho
        phi, phibar = cosine * phibar, sine * phibar
        result = [r + phi / rho * value for r, value in zip(result, w)]
        if k < steps - 1:
            a, b, g = 1.0 / (alpha * beta), alpha / beta, beta / alpha
            zu = [(a if i == k + 1 else 0.0) - b * value for i, value in enumerate(zu)]
            z = [value - g * old for value, old in zip(zu, z)]
            alpha, beta = ratios(notes[k + 2])
            theta = sine * alpha
            rhobar = -cosine * alpha
            w = [value / alpha - theta / rho * old for value, old in zip(z, w)]
    return result


def finish_kernel(n0, n1, n2, n3, gauge_ref, q0, q1, q2, inc_ref, field_ref, out_ref, rows_ref):
    blocks, slots, width = inc_ref.shape
    count = rows_ref.shape[0]
    gauges = q0.shape[0]
    step = pl.program_id(0)

    @pl.when(step == 0)
    def _():
        e0, e1, e2 = weights_of([n0, n1, n2, n3])
        width_ = 512

        def body(i, value):
            here = pl.ds(pl.multiple_of(i * width_, width_), width_)
            mixed = q0[here, :] * e0 + q1[here, :] * e1 + q2[here, :] * e2
            gauge = lax.broadcasted_iota(jnp.int32, (count, width_), 1) + i * width_
            hot = jnp.where(gauge_ref[...] == gauge, 1.0, 0.0).astype(BF16)
            return value + pick(hot, mixed)

        rows_ref[...] = lax.fori_loop(0, gauges // width_, body, jnp.zeros(rows_ref.shape, F32))

    weights = inc_ref[...].astype(F32).astype(BF16)
    for b in range(blocks):
        here = pl.ds(b * width, width)
        rows = rows_ref[pl.ds(pl.multiple_of((step * blocks + b) * slots, slots), slots), :]
        added = sum(
            lax.dot_general(weights[b], piece, (((0,), (0,)), ((), ())), preferred_element_type=F32)
            for piece in pieces(rows, 3)
        )
        out_ref[here, :] = field_ref[here, :] + added


def finish(notes, row_gauge, gathered, incidence, field):
    blocks, slots, width = incidence.shape
    hours = field.shape[1]
    count = row_gauge.shape[0]
    step = 8
    whole = lambda shape: pl.BlockSpec(shape, lambda i: (0, 0))
    return pl.pallas_call(
        finish_kernel,
        grid=(blocks // step,),
        in_specs=[whole(n.shape) for n in notes]
        + [whole((count, 1))]
        + [whole(q.shape) for q in gathered]
        + [
            pl.BlockSpec((step, slots, width), lambda i: (i, 0, 0)),
            pl.BlockSpec((step * width, hours), lambda i: (i, 0)),
        ],
        out_specs=pl.BlockSpec((step * width, hours), lambda i: (i, 0)),
        out_shape=jax.ShapeDtypeStruct(field.shape, F32),
        scratch_shapes=[pltpu.VMEM((count, hours), F32)],
        compiler_params=params(56),
        name="finish",
    )(*notes, row_gauge.reshape(count, 1), *gathered, incidence, field)


def shifted(value, axis, by):
    devices = lax.axis_size(axis)
    pairs = [(i, i + by) for i in range(devices) if 0 <= i + by < devices]
    return lax.ppermute(value, axis, pairs)


def window(value):
    return jnp.concatenate([shifted(value, "tm", 1), value, shifted(value, "tm", -1)], axis=0)


def gathered_rows(value):
    owners = lax.axis_size("basin")
    copies = jnp.broadcast_to(value[None], (owners,) + value.shape)
    return lax.all_to_all(copies, "basin", 0, 0, tiled=False)


def over_hours(note):
    blocks = lax.axis_size("tm")
    result = note
    for by in range(1, blocks):
        result = result + lax.ppermute(note, "tm", [(i, (i + by) % blocks) for i in range(blocks)])
    return result


def shards(incidence, row_gauge, gauge_kernel, kernels, observed, first_guess):
    owners = lax.axis_size("basin")
    rows, hours = observed.shape
    gauges = rows * owners
    mats = transforms()
    spec = spectrum(gauge_kernel, kernels, mats[0])
    more = (lax.axis_index("tm") < lax.axis_size("tm") - 1).astype(F32).reshape(1)
    partial, gram = prepare(incidence, first_guess)
    all_gram = lax.all_gather(gram, "basin", axis=1, tiled=True)
    all_rows = lax.all_gather(row_gauge, "basin", axis=0, tiled=True)
    dense = table(row_gauge, partial, gauges).reshape(owners, rows, hours)
    sums = jnp.sum(lax.all_to_all(dense, "basin", 0, 0, tiled=False), axis=0)
    both = jnp.concatenate([observed, shifted(observed, "tm", -1)], axis=0)
    first = (lax.axis_index("basin") * rows).astype(jnp.int32).reshape(1)
    high, low = couple(first, all_rows, all_gram, rows, gauges)

    pulled, note = first_step(more, window(sums), both, spec, mats)
    notes, kept, state = [], [], None
    for k in range(3):
        everyone = gathered_rows(jnp.concatenate([pulled, note], axis=0))
        value = everyone[:, :rows].reshape(gauges, hours)
        notes.append(over_hours(jnp.sum(everyone[:, rows:], axis=0)))
        kept.append(value)
        around = window(mix(high, low, value))
        final = k == 2
        result = next_step(more, notes[-1], around, spec, mats, pulled, state, final)
        if final:
            (note,) = result
        else:
            state, pulled, note = result
    notes.append(over_hours(jnp.sum(gathered_rows(note), axis=0)))
    return finish(notes, row_gauge, kept, incidence, first_guess)


Z_, X_, Y_, C_ = 4, 2, 2, 2
NOTE = 8
HOURS = SPAN // 2


def device(z, x, y, c):
    return (z * X_ + x) * (Y_ * C_) + y * C_ + c


def moved(value, where):
    pairs = []
    for z, x, y, c in np.ndindex(Z_, X_, Y_, C_):
        target = where(z, x, y, c)
        if target is not None:
            pairs.append((device(z, x, y, c), device(*target)))
    return lax.ppermute(value, ("basin", "tm"), pairs)


def to_plane(z, x, y, c):
    return 2 * y + c, x, z & 1, z >> 1


def from_plane(z, x, y, c):
    return 2 * c + y, x, z >> 1, z & 1


def over_x(z, x, y, c):
    return z, 1 - x, y, c


def over_y(z, x, y, c):
    return z, x, 1 - y, c


def over_xy(z, x, y, c):
    return z, 1 - x, 1 - y, c


def over_core(z, x, y, c):
    return z, x, y, 1 - c


def z_pair(z, x, y, c):
    return z ^ 1, x, y, c


def z_middle(z, x, y, c):
    return (3 - z, x, y, c) if z in (1, 2) else None


def z_two(z, x, y, c):
    return z ^ 2, x, y, c


def z_mirror(z, x, y, c):
    return 3 - z, x, y, c


def z_next(z, x, y, c):
    return (z + 1, x, y, c) if z < 3 else None


SQUARE = (over_x, over_y, over_xy)


def split_constant(value):
    out = []
    for _ in range(3):
        piece = value.astype(jnp.bfloat16)
        out.append(piece)
        value = value - piece.astype(np.float64)
    return out


ORDERS = {2: ((0, 1), (1, 0), (0, 0)), 3: ((0, 2), (1, 1), (2, 0), (0, 1), (1, 0), (0, 0))}


def widened(mat, order):
    parts = split_constant(mat)
    return jnp.asarray(np.concatenate([parts[i] for i, _ in ORDERS[order]], axis=1))


def product(wide, value, order):
    parts = pieces(value, order)
    return dot(wide, jnp.concatenate([parts[j] for _, j in ORDERS[order]], axis=0))


def turned_transforms(order):
    half = SPAN // 2
    freq = 2.0 * np.pi * (np.arange(half) + 0.5) / SPAN
    phase = freq[:, None] * np.arange(SPAN)[None, :]
    forward = np.concatenate([np.cos(phase), -np.sin(phase)], axis=0)
    inverse = forward.T * (2.0 / SPAN)
    return [widened(mat, order) for mat in (forward, inverse[:half], inverse[half:], forward[:, :half])]


def turn(waves, spec, sign):
    half = waves.shape[0] // 2
    real, imag = waves[:half], waves[half:]
    kr, ki = spec[:half], spec[half:] * sign
    return jnp.concatenate([real * kr - imag * ki, real * ki + imag * kr], axis=0)


def plane_delayed(before, here, after, spec, forward, last, order):
    rows = here.shape[1]
    pairs = [jnp.concatenate(pair, axis=0) for pair in ((before, here), (here, after))]
    waves = product(forward, jnp.concatenate(pairs, axis=1), order)
    turned = [turn(waves[:, i * rows : (i + 1) * rows], spec, 1.0) for i in range(2)]
    out = product(last, jnp.concatenate(turned, axis=1), order)
    return out[:, :rows], out[:, rows:]


def plane_advanced(here, after, spec, forward, first, order):
    waves = product(forward, jnp.concatenate([here, after], axis=0), order)
    return product(first, turn(waves, spec, -1.0), order)


def describe_kernel(inc_ref, gauge_ref, out_ref):
    blocks, slots, width = inc_ref.shape
    tile = 8
    side = tile * slots
    weights = inc_ref[...].astype(F32).astype(BF16)
    row = lax.broadcasted_iota(jnp.int32, (side, side), 0)
    col = lax.broadcasted_iota(jnp.int32, (side, side), 1)
    same = row // slots == col // slots
    for i in range(blocks // tile):
        flat = weights[i * tile : (i + 1) * tile].reshape(side, width)
        full = lax.dot_general(flat, flat, (((1,), (1,)), ((), ())), preferred_element_type=F32)
        own = jnp.where(same, full, 0.0)
        out_ref[pl.ds(0, slots), pl.ds(i * side, side)] = jnp.sum(own.reshape(tile, slots, side), axis=0)
    out_ref[pl.ds(slots, 8), :] = jnp.broadcast_to(gauge_ref[...].astype(F32), (8, blocks * slots))


def describe(incidence, row_gauge):
    blocks, slots, _ = incidence.shape
    count = blocks * slots
    return pl.pallas_call(
        describe_kernel,
        out_shape=jax.ShapeDtypeStruct((slots + 8, count), F32),
        compiler_params=params(),
        name="describe",
        cost_estimate=SMALL,
    )(incidence, row_gauge.reshape(1, count))


def send_kernel(
    inc_hbm, field_hbm, gauge_hbm, kind_hbm, out_ref, inc_ref, field_ref, gauge_ref, kind_ref, sems, label_sems
):
    blocks, slots, width = inc_ref.shape
    chunks = sems.shape[0]
    step = blocks // chunks
    copies = []
    for i in range(chunks):
        near = pl.ds(i * step, step)
        far = pl.ds(i * step * width, step * width)
        copies.append(
            (
                pltpu.make_async_copy(inc_hbm.at[near], inc_ref.at[near], sems.at[i, 0]),
                pltpu.make_async_copy(field_hbm.at[far], field_ref.at[far], sems.at[i, 1]),
            )
        )
        for copy in copies[-1]:
            copy.start()
    labels = (
        pltpu.make_async_copy(gauge_hbm, gauge_ref, label_sems.at[0]),
        pltpu.make_async_copy(kind_hbm, kind_ref, label_sems.at[1]),
    )
    for copy in labels:
        copy.start()
    for i in range(chunks):
        for copy in copies[i]:
            copy.wait()
        parts = []
        for b in range(i * step, (i + 1) * step):
            weight = inc_ref[b].astype(F32).astype(BF16)
            value = jnp.concatenate(pieces(field_ref[pl.ds(b * width, width), :], 3)[::-1], axis=0)
            parts.append(dot(jnp.concatenate([weight] * 3, axis=1), value))
        out_ref[pl.ds(0, HOURS), pl.ds(i * step * slots, step * slots)] = jnp.transpose(
            jnp.concatenate(parts, axis=0)
        )
    for copy in labels:
        copy.wait()
    count, kinds = gauge_ref.shape[1], kind_ref.shape[1]
    kind = jnp.concatenate([kind_ref[...].astype(F32), jnp.zeros((1, count - kinds), F32)], axis=1)
    out_ref[pl.ds(HOURS, 8), :] = jnp.concatenate(
        [gauge_ref[...].astype(F32), kind, jnp.zeros((6, count), F32)], axis=0
    )


def send(incidence, field, row_gauge, gauge_kernel):
    count, rows = row_gauge.shape[0], gauge_kernel.shape[0]
    chunks = 4
    return pl.pallas_call(
        send_kernel,
        in_specs=[pl.BlockSpec(memory_space=pltpu.HBM)] * 4,
        out_shape=jax.ShapeDtypeStruct((HOURS + 8, count), F32),
        scratch_shapes=[
            pltpu.VMEM(incidence.shape, incidence.dtype),
            pltpu.VMEM(field.shape, F32),
            pltpu.VMEM((1, count), row_gauge.dtype),
            pltpu.VMEM((1, rows), gauge_kernel.dtype),
            pltpu.SemaphoreType.DMA((chunks, 2)),
            pltpu.SemaphoreType.DMA((2,)),
        ],
        compiler_params=params(60),
        name="send",
        cost_estimate=SMALL,
    )(incidence, field, row_gauge.reshape(1, count), gauge_kernel.reshape(1, rows))


def hot_rows(gauge, first, rows):
    mine = (lax.broadcasted_iota(jnp.int32, (rows, gauge.shape[1]), 0) + first).astype(F32)
    return jnp.where(gauge == mine, 1.0, 0.0).astype(BF16)


def spread_kernel(first_ref, mine_ref, other_ref, *out_refs):
    rows = out_refs[0].shape[1]
    both = jnp.concatenate([mine_ref[...], other_ref[...]], axis=1)
    stacked = jnp.concatenate(pieces(both[:HOURS], 3), axis=0)
    for m, out_ref in enumerate(out_refs):
        hot = hot_rows(both[HOURS : HOURS + 1], first_ref[m], rows)
        result = lax.dot_general(stacked, hot, (((1,), (1,)), ((), ())), preferred_element_type=F32)
        out_ref[...] = (result[2 * HOURS :] + result[HOURS : 2 * HOURS]) + result[:HOURS]


def spread(first, parcels, rows):
    return pl.pallas_call(
        spread_kernel,
        in_specs=[pl.BlockSpec(memory_space=pltpu.SMEM)] + [pl.BlockSpec(memory_space=pltpu.VMEM)] * 2,
        out_shape=[jax.ShapeDtypeStruct((HOURS, rows), F32)] * 4,
        compiler_params=params(),
        name="spread",
        cost_estimate=SMALL,
    )(first, *parcels)


def plane_couple_kernel(last, first_ref, *refs):
    if last:
        all_ref, before_ref, high_ref, low_ref, total_ref, meta_ref = refs
        total_ref[...] = before_ref[...]
    else:
        all_ref, total_ref, meta_ref = refs
        total_ref[...] = jnp.zeros_like(total_ref)
    parts, height, count = meta_ref.shape
    slots = height - 8
    cols, rows = total_ref.shape
    tile = 256
    for i in range(parts):
        meta_ref[i] = all_ref[:, i * count : (i + 1) * count]
    row = lax.broadcasted_iota(jnp.int32, (tile, tile), 0)
    col = lax.broadcasted_iota(jnp.int32, (tile, tile), 1)
    same = row // slots == col // slots

    def body(i, carry):
        gauge = meta_ref[i, slots : slots + 1, :]
        near = []
        for j in range(count // tile):
            here = slice(j * tile, (j + 1) * tile)
            block = jnp.concatenate([meta_ref[i, :slots, here]] * (tile // slots), axis=0)
            block = jnp.where(same, block, 0.0).astype(BF16)
            mine = jnp.concatenate(
                [hot_rows(gauge[:, here], first_ref[4 + h], rows // 2) for h in range(2)], axis=0
            )
            near.append(
                lax.dot_general(block, mine, (((1,), (1,)), ((), ())), preferred_element_type=F32)
            )
        near = jnp.concatenate(near, axis=0)
        high = near.astype(BF16)
        rest = near - high.astype(F32)
        hot = jnp.concatenate([hot_rows(gauge, first_ref[m], cols // 4) for m in range(4)], axis=0)
        total_ref[...] += dot(hot, high)

        @pl.when(jnp.max(jnp.abs(rest)) > 0.0)
        def _():
            total_ref[...] += dot(hot, rest.astype(BF16))

        return carry

    lax.fori_loop(0, parts, body, 0)
    if last:
        high, low = pieces(total_ref[...], 2)
        high_ref[...] = high
        low_ref[...] = low


def plane_couple(first, meta, rows, before=None):
    height, wide = meta.shape
    parts = 2 * X_
    shape = (4 * rows, 2 * rows)
    last = before is not None
    args = [first, meta] + ([before] if last else [])
    scratch = [pltpu.VMEM((parts, height, wide // parts), F32)]
    return pl.pallas_call(
        functools.partial(plane_couple_kernel, last),
        in_specs=[pl.BlockSpec(memory_space=pltpu.SMEM)]
        + [pl.BlockSpec(memory_space=pltpu.VMEM)] * (len(args) - 1),
        out_shape=[jax.ShapeDtypeStruct(shape, BF16)] * 2 if last else jax.ShapeDtypeStruct(shape, F32),
        scratch_shapes=([pltpu.VMEM(shape, F32)] if last else []) + scratch,
        compiler_params=params(),
        name="plane_couple",
        cost_estimate=pl.CostEstimate(
            flops=2 * 8 * wide * rows * rows, bytes_accessed=2_000_000, transcendentals=0
        ),
    )(*args)


def plane_mix_kernel(high_ref, low_ref, a_ref, b_ref, c_ref, d_ref, *refs):
    *extra, mine_ref, other_ref = refs
    refs = (a_ref, b_ref, c_ref, d_ref)
    height, rows = a_ref.shape
    body = pl.ds(0, HOURS)
    one, two = pieces(jnp.concatenate([ref[body, :] for ref in refs], axis=1), 2)
    both = dot(jnp.concatenate([two, one], axis=0), high_ref[...])
    result = (both[:HOURS] + dot(one, low_ref[...])) + both[HOURS:]
    mine_ref[body, :] = result[:, :rows]
    other_ref[body, :] = result[:, rows:]
    if height > HOURS:
        tail = pl.ds(HOURS, NOTE)
        note = sum(ref[tail, :] for ref in refs)
        mine_ref[tail, :] = note
        other_ref[tail, :] = note
    for ref in extra:
        other_ref[pl.ds(height, ref.shape[0]), :] = ref[...]


def plane_mix(coupling, values, extra):
    height, rows = values[0].shape
    return pl.pallas_call(
        plane_mix_kernel,
        out_shape=[
            jax.ShapeDtypeStruct((height, rows), F32),
            jax.ShapeDtypeStruct((height + sum(value.shape[0] for value in extra), rows), F32),
        ],
        compiler_params=params(),
        name="plane_mix",
        cost_estimate=SMALL,
    )(*coupling, *values, *extra)


def plane_rows_kernel(first_ref, meta_ref, meta_other_ref, a_ref, b_ref, c_ref, d_ref, *refs):
    if len(refs) > 2:
        *stack, last_ref, beside_ref, mine_ref, other_ref, stack_ref = refs
    else:
        mine_ref, other_ref = refs
    rows = a_ref.shape[1]
    value = jnp.concatenate([ref[pl.ds(0, HOURS), :] for ref in (a_ref, b_ref, c_ref, d_ref)], axis=1)
    one, two = pieces(value, 2)
    stacked = jnp.concatenate([two, one], axis=0)
    picked = []
    for ref in (meta_ref, meta_other_ref):
        gauge = ref[0:1, :]
        hot = jnp.concatenate([hot_rows(gauge, first_ref[m], rows) for m in range(4)], axis=0)
        both = dot(stacked, hot)
        picked.append(both[:HOURS] + both[HOURS:])
    mine_ref[...] = picked[0]
    count = picked[1].shape[1] // rows
    for i in range(count):
        other_ref[pl.ds(i * HOURS, HOURS), :] = picked[1][:, i * rows : (i + 1) * rows]
    if len(refs) > 2:
        top = stack_ref.shape[0] - HOURS
        for ref in stack:
            stack_ref[pl.ds(0, top), :] = ref[...]
        for i in range(count):
            here = pl.ds(i * rows, rows)
            beside = beside_ref[pl.ds(beside_ref.shape[0] - (count - i) * HOURS, HOURS), :]
            stack_ref[pl.ds(top, HOURS), here] = last_ref[:, here] + beside


def plane_rows(first, metas, values, before):
    rows = values[0].shape[1]
    slots = metas[0].shape[1]
    args = [first, *metas, *values, *before]
    shapes = [(HOURS, slots), (slots // rows * HOURS, rows)]
    if before:
        shapes.append(((len(before) - 1) * HOURS, slots))
    return pl.pallas_call(
        plane_rows_kernel,
        in_specs=[pl.BlockSpec(memory_space=pltpu.SMEM)]
        + [pl.BlockSpec(memory_space=pltpu.VMEM)] * (len(args) - 1),
        out_shape=[jax.ShapeDtypeStruct(shape, F32) for shape in shapes],
        compiler_params=params(),
        name="plane_rows",
        cost_estimate=pl.CostEstimate(flops=1_000_000_000, bytes_accessed=2_000_000, transcendentals=0),
    )(*args)


def gain(kernels):
    return jnp.max(jnp.sum(kernels, axis=1, keepdims=True), axis=0, keepdims=True)


def spectra(kind, kernels, wide):
    classes = kernels.shape[0]
    row = lax.broadcasted_iota(jnp.int32, (classes, kind.shape[1]), 0).astype(F32)
    hot = jnp.where(row == kind, 1.0, 0.0).astype(BF16)
    taps = jnp.transpose(kernels / gain(kernels))
    chosen = dot(jnp.concatenate(pieces(taps, 3)[::-1], axis=1), jnp.concatenate([hot] * 3, axis=0))
    return product(wide, chosen, 3)


def plane_spectrum_kernel(class_ref, kernels_ref, wide_ref, out_ref):
    kind = class_ref[1:2, : out_ref.shape[1]]
    out_ref[...] = spectra(kind, kernels_ref[...], wide_ref[...])


def plane_spectrum(meta, kernels, wide, rows):
    return pl.pallas_call(
        plane_spectrum_kernel,
        out_shape=jax.ShapeDtypeStruct((SPAN, rows), F32),
        compiler_params=params(),
        name="plane_spectrum",
        cost_estimate=SMALL,
    )(meta, kernels, wide)


def sides(even, pair, middle):
    return jnp.where(even, middle, pair), jnp.where(even, pair, middle)


def plane_call(kernel, name, shapes, flags, args):
    return pl.pallas_call(
        kernel,
        in_specs=[pl.BlockSpec(memory_space=pltpu.SMEM)] * len(flags)
        + [pl.BlockSpec(memory_space=pltpu.VMEM)] * len(args),
        out_shape=[jax.ShapeDtypeStruct(shape, F32) for shape in shapes],
        compiler_params=params(),
        name=name,
        cost_estimate=SMALL,
    )(*flags, *args)


def plane_first_kernel(
    flag_ref, here_ref, pair_ref, middle_ref, spec_ref, kernels_ref, forward3, last3, forward, first, out_ref
):
    spec = spec_ref[...]
    before, after = sides(flag_ref[0] > 0.5, pair_ref[...], middle_ref[...])
    here = here_ref[...]
    both = plane_delayed(before[:HOURS], here[:HOURS], after[:HOURS], spec, forward3[...], last3[...], 3)
    scale = gain(kernels_ref[...])
    now = here[HOURS:] - both[0] * scale
    later = (after[HOURS:] - both[1] * scale) * flag_ref[1]
    out_ref[...] = plane_advanced(now, later, spec, forward[...], first[...], 2)


def plane_delay_kernel(flag_ref, here_ref, pair_ref, middle_ref, spec_ref, forward, last, out_ref):
    body = pl.ds(0, HOURS)
    before, after = sides(flag_ref[0] > 0.5, pair_ref[body, :], middle_ref[body, :])
    out = plane_delayed(before, here_ref[body, :], after, spec_ref[...], forward[...], last[...], 2)
    for i in range(2):
        out_ref[pl.ds(i * HOURS, HOURS), :] = out[i]


def write_note(ref, rows):
    tail = [jnp.zeros((NOTE - len(rows), ref.shape[1]), F32)]
    ref[pl.ds(HOURS, NOTE), :] = jnp.concatenate(rows + tail, axis=0)


def plane_open_kernel(
    flag_ref, here_ref, pair_ref, middle_ref, pulled_ref, spec_ref, forward, first, last, out_ref, delayed_ref
):
    here = here_ref[...]
    spec = spec_ref[...]
    before, after = sides(flag_ref[0] > 0.5, pair_ref[...], middle_ref[...])
    now, later = plane_delayed(before, here, after, spec, forward[...], last[...], 2)
    out_ref[pl.ds(0, HOURS), :] = plane_advanced(now, later * flag_ref[1], spec, forward[...], first[...], 2)
    write_note(out_ref, [lanes(pulled_ref[...], here), lanes(now, now)])
    delayed_ref[pl.ds(0, HOURS), :] = now
    delayed_ref[pl.ds(HOURS, HOURS), :] = later


def plane_step_kernel(
    flag_ref,
    here_ref,
    pair_ref,
    two_ref,
    mirror_ref,
    pulled_ref,
    delayed_ref,
    old_z_ref,
    old_s_ref,
    old_delayed_ref,
    spec_ref,
    forward,
    first,
    total_ref,
    out_ref,
    kept_ref,
):
    tail, body = pl.ds(HOURS, NOTE), pl.ds(0, HOURS)
    total_ref[...] = (here_ref[tail, :] + pair_ref[tail, :]) + (two_ref[...] + mirror_ref[...])
    inverse = total(total_ref, 0) / total(total_ref, 1)
    z = pulled_ref[body, :] * inverse - old_z_ref[...]
    s = here_ref[body, :] * inverse - old_s_ref[...]
    both = delayed_ref[...] * inverse - old_delayed_ref[...]
    now, later = both[:HOURS], both[HOURS:]
    following = plane_advanced(now, later * flag_ref[1], spec_ref[...], forward[...], first[...], 2)
    out_ref[body, :] = following * inverse
    write_note(out_ref, [lanes(z, s), lanes(now, now)])
    for i, value in enumerate((z, s, now)):
        kept_ref[pl.ds(i * HOURS, HOURS), :] = value


def plane_close_kernel(
    here_ref,
    before_ref,
    pulled_ref,
    kept_ref,
    old_z_ref,
    old_s_ref,
    old_delayed_ref,
    open_ref,
    spec_ref,
    kernels_ref,
    forward,
    last,
    out_ref,
):
    body = pl.ds(0, HOURS)
    here, raw = here_ref[body, :], pulled_ref[body, :]
    waves = product(forward[...], jnp.concatenate([before_ref[body, :], here], axis=0), 2)
    now = product(last[...], turn(waves, spec_ref[...], 1.0), 2)
    z, s, delayed = (kept_ref[pl.ds(i * HOURS, HOURS), :] for i in range(3))
    note = [pulled_ref[HOURS + i : HOURS + i + 1, :] for i in range(2)]
    for left in (raw, z, old_z_ref[...]):
        note += [lanes(left, right) for right in (here, s, old_s_ref[...])]
    parts = (now, delayed, old_delayed_ref[body, :])
    for i in range(3):
        note += [lanes(parts[i], parts[j]) for j in range(i, 3)]
    known = [total(open_ref, 0), total(open_ref, 1), gain(kernels_ref[...])]
    note = [jnp.sum(jnp.concatenate(note, axis=0), axis=1, keepdims=True)]
    note += [value / out_ref.shape[0] for value in known]
    count = sum(value.shape[0] for value in note)
    note = jnp.concatenate(note + [jnp.zeros((24 - count, 1), F32)], axis=0)
    shape = (24, out_ref.shape[2])
    row, col = (lax.broadcasted_iota(jnp.int32, shape, i) for i in range(2))
    note = jnp.sum(jnp.where(row == col, jnp.broadcast_to(note, shape), 0.0), axis=0, keepdims=True)
    out_ref[...] = jnp.broadcast_to(note[None], out_ref.shape)


def plane_weights(close):
    entry = lambda i: close[:, i : i + 1]
    n1, t1, scale = (entry(17 + i) for i in range(3))
    n2, t2 = entry(0), entry(1)
    a1 = t1 / n1
    a2, r2 = (t2 / n2) / a1, n2 / n1
    plain = (1.0, -a2, -r2)
    n3 = sum(plain[i] * plain[j] * entry(2 + 3 * i + j) for i in range(3) for j in range(3))
    pairs = [(i, j) for i in range(3) for j in range(i, 3)]
    t3 = sum(
        plain[i] * plain[j] * entry(11 + n) * (1.0 if i == j else 2.0) for n, (i, j) in enumerate(pairs)
    )
    a3, r3 = (t3 / n3) / a1, n3 / n2
    unit = 1.0 / (a1 * scale)
    c3 = unit / (a3 * (a2 - r2) - r3)
    c2 = -a3 * c3
    c1 = unit - r2 * c2
    step = c2 - c3 * a2
    return c1 - step - c3 * r2, step / a1, c3


def plane_combine_kernel(close_ref, stack_ref, mine_ref, beside_ref, out_ref):
    rows = beside_ref.shape[1]
    close = jnp.sum(close_ref[...], axis=0)[0:1, :]
    e0, e1, e2 = plane_weights(close)
    for i in range(out_ref.shape[0] // rows):
        here = pl.ds(i * rows, rows)
        last = mine_ref[:, here] + beside_ref[pl.ds(i * HOURS, HOURS), :]
        value = stack_ref[pl.ds(0, HOURS), here] * e0 + stack_ref[pl.ds(HOURS, HOURS), here] * e1 + last * e2
        out_ref[here, :] = jnp.transpose(value)


def plane_finish_kernel(rows_ref, inc_ref, field_ref, out_ref):
    blocks, slots, width = inc_ref.shape
    weights = inc_ref[...].astype(F32).astype(BF16)
    for b in range(blocks):
        here = pl.ds(b * width, width)
        rows = jnp.concatenate(pieces(rows_ref[pl.ds(b * slots, slots), :], 2), axis=0)
        twice = jnp.concatenate([weights[b]] * 2, axis=0)
        added = lax.dot_general(twice, rows, (((0,), (0,)), ((), ())), preferred_element_type=F32)
        out_ref[here, :] = field_ref[here, :] + added


def plane_finish(rows, incidence, field):
    blocks, slots, width = incidence.shape
    hours = field.shape[1]
    step = 16
    return pl.pallas_call(
        plane_finish_kernel,
        grid=(blocks // step,),
        in_specs=[
            pl.BlockSpec((step * slots, hours), lambda i: (i, 0)),
            pl.BlockSpec((step, slots, width), lambda i: (i, 0, 0)),
            pl.BlockSpec((step * width, hours), lambda i: (i, 0)),
        ],
        out_specs=pl.BlockSpec((step * width, hours), lambda i: (i, 0)),
        out_shape=jax.ShapeDtypeStruct(field.shape, F32),
        compiler_params=params(),
        name="plane_finish",
    )(rows, incidence, field)


def plane_shards(incidence, row_gauge, gauge_kernel, kernels, observed, first_guess):
    rows, hours = observed.shape
    basin, tm = lax.axis_index("basin"), lax.axis_index("tm")
    z, x, y, c = basin // X_, basin % X_, tm // C_, tm % C_
    place = 2 * y + x
    first = jnp.stack([4 * c + (place ^ m) for m in range(4)] + [4 * c + place, 4 * (1 - c) + place])
    first = (first * rows).astype(jnp.int32)
    flags = jnp.stack([1 - z % 2, (z < Z_ - 1).astype(z.dtype), (z > 0).astype(z.dtype)]).astype(F32)
    forward, inverse_first, inverse_last, _ = turned_transforms(2)
    forward3, _, inverse_last3, short3 = turned_transforms(3)
    block, noted = (hours, rows), (hours + NOTE, rows)

    parcel = send(incidence, first_guess, row_gauge, gauge_kernel)
    parcel, near = lax.optimization_barrier((parcel, incidence))
    parcel = moved(parcel, to_plane)
    meta = describe(near, row_gauge)
    meta = jnp.concatenate([meta, moved(meta, over_x)], axis=1)
    meta, seen = lax.optimization_barrier((meta, observed))
    seen = moved(seen, to_plane)
    meta = jnp.concatenate([meta, moved(meta, z_pair)], axis=1)
    parcel, seen = lax.optimization_barrier((parcel, seen))
    parcels = [parcel, moved(parcel, over_core)]
    spec = plane_spectrum(parcel[hours:], kernels, short3, rows)
    parcels[1], seen, meta, spec = lax.optimization_barrier((parcels[1], seen, meta, spec))
    half = meta.shape[1] // 2
    far = moved(jnp.where(c == 0, meta[:, :half], meta[:, half:]), z_two)
    dense = spread(first, parcels, rows)
    metas = [value[hours:] for value in parcels]
    sums = dense[0] + sum(moved(value, where) for value, where in zip(dense[1:], SQUARE))
    sums, far = lax.optimization_barrier((sums, far))
    around = [meta, jnp.concatenate([far, moved(far, over_core)], axis=1)]
    sums = jnp.concatenate([sums, jnp.transpose(seen)], axis=0)
    sums = [sums, moved(sums, z_pair), moved(sums, z_middle)]
    coupled = plane_couple(first, around[0], rows)
    coupled, sums = lax.optimization_barrier((coupled, sums))
    coupling = plane_couple(first, around[1], rows, coupled)
    (pulled0,) = plane_call(
        plane_first_kernel,
        "plane_first",
        [block],
        [flags],
        [*sums, spec, kernels, forward3, inverse_last3, forward, inverse_first],
    )

    def mixing(pulled, extra):
        values = [pulled] + [moved(pulled, where) for where in SQUARE]
        mine, other = plane_mix(coupling, values, extra)
        beside = moved(other, over_core)
        return values, mine + beside[: pulled.shape[0]], beside

    values, mixed0, _ = mixing(pulled0, [])
    picked, theirs = plane_rows(first, metas, values, [])
    sums = [mixed0, moved(mixed0, z_pair), moved(mixed0, z_middle)]
    pulled1, delayed0 = plane_call(
        plane_open_kernel,
        "plane_open",
        [noted, (2 * hours, rows)],
        [flags],
        [*sums, pulled0, spec, forward, inverse_first, inverse_last],
    )

    values, mixed1, beside = mixing(pulled1, [theirs])
    picked, theirs, stack = plane_rows(first, metas, values, [picked, beside])
    sums = [mixed1, moved(mixed1, z_pair), moved(mixed1, z_middle)]
    two, mirror = moved(mixed1[hours:], z_two), moved(mixed1[hours:], z_mirror)
    (delayed1,) = plane_call(
        plane_delay_kernel, "plane_delay", [(2 * hours, rows)], [flags], [*sums, spec, forward, inverse_last]
    )
    open_note, pulled2, kept = plane_call(
        plane_step_kernel,
        "plane_step",
        [(NOTE, rows), noted, (3 * hours, rows)],
        [flags],
        [*sums[:2], two, mirror, pulled1, delayed1, pulled0, mixed0, delayed0, spec, forward, inverse_first],
    )

    values, mixed2, beside = mixing(pulled2, [theirs])
    picked, theirs, stack = plane_rows(first, metas, values, [stack, picked, beside])
    (note,) = plane_call(
        plane_close_kernel,
        "plane_close",
        [(Z_ * X_ * Y_ * C_, 8, rows // 2)],
        [],
        [
            *(mixed2, moved(mixed2, z_next), pulled2, kept, pulled0, mixed0, delayed0),
            *(open_note, spec, kernels, forward, inverse_last),
        ],
    )
    close_note = lax.all_to_all(note, ("basin", "tm"), 0, 0, tiled=False)
    (answer,) = plane_call(
        plane_combine_kernel,
        "plane_combine",
        [(parcel.shape[1], hours)],
        [],
        [close_note, stack, picked, moved(theirs, over_core)],
    )
    return plane_finish(moved(answer, from_plane), incidence, first_guess)


def solution(mesh):
    planes = dict(mesh.shape) == {"basin": Z_ * X_, "tm": Y_ * C_}
    in_specs = (
        P("basin", None, None),
        P("basin"),
        P("basin"),
        P(),
        P("basin", "tm"),
        P("basin", "tm"),
    )
    return jax.shard_map(
        plane_shards if planes else shards, mesh=mesh, in_specs=in_specs, out_specs=P("basin", "tm"), check_vma=False
    )
```

```python
import functools

import jax
import jax.numpy as jnp
import numpy as np
from jax import lax
from jax.experimental import pallas as pl
from jax.experimental.pallas import tpu as pltpu
from jax.sharding import PartitionSpec as P

F32 = jnp.float32
BF16 = jnp.bfloat16
HIGH = lax.Precision.HIGHEST
SPAN = 256
MIB = 1024 * 1024


SMALL = pl.CostEstimate(flops=1, bytes_accessed=1, transcendentals=0)


def params(mib=16):
    return pltpu.CompilerParams(vmem_limit_bytes=mib * MIB)


def transforms():
    half = SPAN // 2
    freq = 2.0 * np.pi * (np.arange(half) + 0.5) / SPAN
    phase = np.arange(SPAN)[:, None] * freq[None, :]
    forward = np.concatenate([np.cos(phase), -np.sin(phase)], axis=1)
    inverse = forward.T * (2.0 / SPAN)
    return (
        jnp.asarray(forward, F32),
        jnp.asarray(inverse[:, :half], F32),
        jnp.asarray(inverse[:, half:], F32),
    )


def dot(a, b):
    return jnp.dot(a, b, preferred_element_type=F32)


def exact(a, b):
    return jnp.dot(a, b, precision=HIGH, preferred_element_type=F32)


def pieces(value, count):
    out = []
    for _ in range(count):
        piece = value.astype(BF16)
        out.append(piece)
        value = value - piece.astype(F32)
    return out


def pick(hot, value):
    return sum(dot(hot, piece) for piece in pieces(value, 3))


def prepare_kernel(inc_ref, field_ref, partial_ref, gram_ref):
    blocks, slots, width = inc_ref.shape
    rows = blocks * slots
    weights = inc_ref[...].astype(F32).astype(BF16)
    for b in range(blocks):
        value = field_ref[pl.ds(b * width, width), :]
        partial_ref[pl.ds(b * slots, slots), :] = pick(weights[b], value)
    flat = weights.reshape(rows, width)
    full = lax.dot_general(flat, flat, (((1,), (1,)), ((), ())), preferred_element_type=F32)
    row = lax.broadcasted_iota(jnp.int32, (rows, rows), 0)
    col = lax.broadcasted_iota(jnp.int32, (rows, rows), 1)
    own = jnp.where(row // slots == col // slots, full, 0.0)
    gram_ref[...] = jnp.sum(own.reshape(blocks, slots, rows), axis=0)


def prepare(incidence, field):
    blocks, slots, width = incidence.shape
    hours = field.shape[1]
    step = 8
    return pl.pallas_call(
        prepare_kernel,
        grid=(blocks // step,),
        in_specs=[
            pl.BlockSpec((step, slots, width), lambda i: (i, 0, 0)),
            pl.BlockSpec((step * width, hours), lambda i: (i, 0)),
        ],
        out_specs=[
            pl.BlockSpec((step * slots, hours), lambda i: (i, 0)),
            pl.BlockSpec((slots, step * slots), lambda i: (0, i)),
        ],
        out_shape=[
            jax.ShapeDtypeStruct((blocks * slots, hours), F32),
            jax.ShapeDtypeStruct((slots, blocks * slots), F32),
        ],
        compiler_params=params(56),
        name="prepare",
    )(incidence, field)


def table_kernel(gauge_ref, partial_ref, out_ref):
    slots = partial_ref.shape[0]
    rows = out_ref.shape[0]
    first = pl.program_id(0) * rows
    gauge = lax.broadcasted_iota(jnp.int32, (rows, slots), 0) + first
    hot = jnp.where(gauge_ref[...] == gauge, 1.0, 0.0).astype(BF16)
    out_ref[...] = pick(hot, partial_ref[...])


def table(row_gauge, partial, gauges):
    slots, hours = partial.shape
    step = 256
    return pl.pallas_call(
        table_kernel,
        grid=(gauges // step,),
        in_specs=[
            pl.BlockSpec((1, slots), lambda i: (0, 0)),
            pl.BlockSpec((slots, hours), lambda i: (0, 0)),
        ],
        out_specs=pl.BlockSpec((step, hours), lambda i: (i, 0)),
        out_shape=jax.ShapeDtypeStruct((gauges, hours), F32),
        compiler_params=params(56),
        name="table",
    )(row_gauge.reshape(1, slots), partial)


def couple_kernel(first_ref, lane_ref, sub_ref, gram_ref, high_ref, low_ref, near_ref):
    slots = gram_ref.shape[0]
    count = lane_ref.shape[1]
    rows, cols = high_ref.shape
    tile = 256
    first = first_ref[0]

    @pl.when(pl.program_id(0) == 0)
    def _():
        row = lax.broadcasted_iota(jnp.int32, (tile, tile), 0)
        col = lax.broadcasted_iota(jnp.int32, (tile, tile), 1)
        same = row // slots == col // slots
        mine = lax.broadcasted_iota(jnp.int32, (rows, tile), 0) + first

        def body(i, carry):
            here = pl.ds(pl.multiple_of(i * tile, tile), tile)
            block = jnp.concatenate([gram_ref[:, here]] * (tile // slots), axis=0)
            block = jnp.where(same, block, 0.0).astype(BF16)
            hot = jnp.where(lane_ref[:, here] == mine, 1.0, 0.0).astype(BF16)
            near_ref[:, here] = dot(hot, block)
            return carry

        lax.fori_loop(0, count // tile, body, 0)

    def chunk(i, total):
        here = pl.ds(pl.multiple_of(i * 1024, 1024), 1024)
        gauge = lax.broadcasted_iota(jnp.int32, (1024, cols), 1) + pl.program_id(0) * cols
        hot = jnp.where(sub_ref[here, :] == gauge, 1.0, 0.0).astype(BF16)
        near = near_ref[:, here]
        high = near.astype(BF16)
        low = (near - high.astype(F32)).astype(BF16)
        return total + dot(high, hot) + dot(low, hot)

    total = lax.fori_loop(0, count // 1024, chunk, jnp.zeros((rows, cols), F32))
    high, low = pieces(total, 2)
    high_ref[...] = high
    low_ref[...] = low


def couple(first, row_gauge, gram, rows, gauges):
    count = row_gauge.shape[0]
    step = 256
    return pl.pallas_call(
        couple_kernel,
        grid=(gauges // step,),
        in_specs=[
            pl.BlockSpec(memory_space=pltpu.SMEM),
            pl.BlockSpec((1, count), lambda i: (0, 0)),
            pl.BlockSpec((count, 1), lambda i: (0, 0)),
            pl.BlockSpec(gram.shape, lambda i: (0, 0)),
        ],
        out_specs=[pl.BlockSpec((rows, step), lambda i: (0, i))] * 2,
        out_shape=[jax.ShapeDtypeStruct((rows, gauges), BF16)] * 2,
        scratch_shapes=[pltpu.VMEM((rows, count), F32)],
        compiler_params=params(56),
        name="couple",
    )(first, row_gauge.reshape(1, count), row_gauge.reshape(count, 1), gram)


def mix_kernel(high_ref, low_ref, value_ref, out_ref):
    high = high_ref[...]
    low = low_ref[...]
    one, two, three = pieces(value_ref[...], 3)
    out_ref[...] = (dot(high, three) + dot(low, two)) + (dot(high, two) + dot(low, one)) + dot(high, one)


def mix(high, low, value):
    return pl.pallas_call(
        mix_kernel,
        out_shape=jax.ShapeDtypeStruct((high.shape[0], value.shape[1]), F32),
        compiler_params=params(56),
        name="mix",
    )(high, low, value)


def spectrum_kernel(class_ref, kernels_ref, forward_ref, out_ref):
    rows = class_ref.shape[0]
    classes, taps = kernels_ref.shape
    kind = lax.broadcasted_iota(jnp.int32, (rows, classes), 1)
    hot = jnp.where(class_ref[...] == kind, 1.0, 0.0)
    out_ref[...] = exact(exact(hot, kernels_ref[...]), forward_ref[pl.ds(0, taps), :])


def spectrum(gauge_kernel, kernels, forward):
    rows = gauge_kernel.shape[0]
    return pl.pallas_call(
        spectrum_kernel,
        out_shape=jax.ShapeDtypeStruct((rows, SPAN), F32),
        compiler_params=params(56),
        name="spectrum",
    )(gauge_kernel.reshape(rows, 1), kernels, forward)


def delayed(before, here, after, spec, forward, inverse_last):
    rows, half = here.shape
    stacked = jnp.concatenate(
        [jnp.concatenate([before, here], axis=1), jnp.concatenate([here, after], axis=1)], axis=0
    )
    waves = exact(stacked, forward)
    real, imag = waves[:, :half], waves[:, half:]
    kr = jnp.concatenate([spec[:, :half]] * 2, axis=0)
    ki = jnp.concatenate([spec[:, half:]] * 2, axis=0)
    turned = jnp.concatenate([real * kr - imag * ki, real * ki + imag * kr], axis=1)
    out = exact(turned, inverse_last)
    return out[:rows], out[rows:]


def advanced(here, after, spec, forward, inverse_first):
    half = here.shape[1]
    waves = exact(jnp.concatenate([here, after], axis=1), forward)
    real, imag = waves[:, :half], waves[:, half:]
    kr, ki = spec[:, :half], spec[:, half:]
    turned = jnp.concatenate([real * kr + imag * ki, imag * kr - real * ki], axis=1)
    return exact(turned, inverse_first)


def lanes(a, b):
    return jnp.sum(a * b, axis=0, keepdims=True)


def total(ref, row):
    return jnp.sum(ref[row : row + 1, :], axis=1, keepdims=True)


def ratios(ref):
    square = total(ref, 0)
    alpha = jnp.sqrt(square)
    beta = jnp.sqrt(jnp.maximum(total(ref, 1) / square - 2.0 * total(ref, 2) + square, 0.0))
    return alpha, beta


def first_kernel(
    more_ref, sums_ref, observed_ref, spec_ref, forward_ref, first_ref, last_ref, out_ref, note_ref
):
    rows, half = observed_ref.shape[0] // 2, observed_ref.shape[1]
    spec, forward = spec_ref[...], forward_ref[...]
    before, here, after = (sums_ref[pl.ds(i * rows, rows), :] for i in range(3))
    now, later = delayed(before, here, after, spec, forward, last_ref[...])
    start = observed_ref[pl.ds(0, rows), :] - now
    start_later = (observed_ref[pl.ds(rows, rows), :] - later) * more_ref[0]
    out_ref[...] = advanced(start, start_later, spec, forward, first_ref[...])
    note_ref[...] = jnp.concatenate([lanes(start, start), jnp.zeros((7, half), F32)], axis=0)


def first_step(more, sums, observed, spec, mats):
    rows, half = spec.shape[0], observed.shape[1]
    return pl.pallas_call(
        first_kernel,
        in_specs=[pl.BlockSpec(memory_space=pltpu.SMEM)] + [pl.BlockSpec(memory_space=pltpu.VMEM)] * 6,
        out_shape=[jax.ShapeDtypeStruct((rows, half), F32), jax.ShapeDtypeStruct((8, half), F32)],
        compiler_params=params(56),
        name="first_step",
    )(more, sums, observed, spec, *mats)


def step_kernel(
    opening,
    final,
    more_ref,
    note_ref,
    sums_ref,
    spec_ref,
    forward_ref,
    first_ref,
    last_ref,
    pulled_ref,
    *refs,
):
    if opening:
        state_ref = None
    else:
        state_ref, *refs = refs
    if final:
        (out_note_ref,) = refs
    else:
        new_ref, out_ref, out_note_ref = refs
    rows, half = pulled_ref.shape
    spec, forward = spec_ref[...], forward_ref[...]
    if opening:
        scale = 1.0 / jnp.sqrt(total(note_ref, 0))
        along = sums_ref[...] * scale
        new_s, new_su = along, along
        new_zu = pulled_ref[...] * scale
        new_z = new_zu
    else:
        alpha, beta = ratios(note_ref)
        a, b, g = 1.0 / (alpha * beta), alpha / beta, beta / alpha
        wide = pl.ds(0, 3 * rows), pl.ds(3 * rows, 3 * rows)
        new_su = sums_ref[...] * a - state_ref[wide[1], :] * b
        new_s = new_su - state_ref[wide[0], :] * g
        new_zu = pulled_ref[...] * a - state_ref[pl.ds(7 * rows, rows), :] * b
        new_z = new_zu - state_ref[pl.ds(6 * rows, rows), :] * g
    before, here, after = (new_s[i * rows : (i + 1) * rows] for i in range(3))
    now, later = delayed(before, here, after, spec, forward, last_ref[...])
    out_note_ref[...] = jnp.concatenate(
        [lanes(new_z, here), lanes(now, now), lanes(new_zu, here), jnp.zeros((5, half), F32)], axis=0
    )
    if not final:
        new_ref[pl.ds(0, 3 * rows), :] = new_s
        new_ref[pl.ds(3 * rows, 3 * rows), :] = new_su
        new_ref[pl.ds(6 * rows, rows), :] = new_z
        new_ref[pl.ds(7 * rows, rows), :] = new_zu
        out_ref[...] = advanced(now, later * more_ref[0], spec, forward, first_ref[...])


def next_step(more, note, sums, spec, mats, pulled, state, final):
    rows, half = pulled.shape
    opening = state is None
    shapes = [
        jax.ShapeDtypeStruct((8 * rows, half), F32),
        jax.ShapeDtypeStruct((rows, half), F32),
        jax.ShapeDtypeStruct((8, half), F32),
    ]
    args = [more, note, sums, spec, *mats, pulled] + ([] if opening else [state])
    return pl.pallas_call(
        functools.partial(step_kernel, opening, final),
        in_specs=[pl.BlockSpec(memory_space=pltpu.SMEM)]
        + [pl.BlockSpec(memory_space=pltpu.VMEM)] * (len(args) - 1),
        out_shape=shapes[2:] if final else shapes,
        compiler_params=params(56),
        name="next_step",
    )(*args)


def weights_of(notes):
    start = jnp.sqrt(total(notes[0], 0))
    zero = jnp.zeros_like(start)
    units = [1.0 / start, zero, zero]
    z, zu = list(units), list(units)
    phibar = start
    alpha, beta = ratios(notes[1])
    rhobar = alpha
    w = [value / alpha for value in z]
    result = [zero] * 3
    steps = len(notes) - 1
    for k in range(steps):
        rho = jnp.sqrt(rhobar * rhobar + beta * beta)
        cosine, sine = rhobar / rho, beta / rho
        phi, phibar = cosine * phibar, sine * phibar
        result = [r + phi / rho * value for r, value in zip(result, w)]
        if k < steps - 1:
            a, b, g = 1.0 / (alpha * beta), alpha / beta, beta / alpha
            zu = [(a if i == k + 1 else 0.0) - b * value for i, value in enumerate(zu)]
            z = [value - g * old for value, old in zip(zu, z)]
            alpha, beta = ratios(notes[k + 2])
            theta = sine * alpha
            rhobar = -cosine * alpha
            w = [value / alpha - theta / rho * old for value, old in zip(z, w)]
    return result


def finish_kernel(n0, n1, n2, n3, gauge_ref, q0, q1, q2, inc_ref, field_ref, out_ref, rows_ref):
    blocks, slots, width = inc_ref.shape
    count = rows_ref.shape[0]
    gauges = q0.shape[0]
    step = pl.program_id(0)

    @pl.when(step == 0)
    def _():
        e0, e1, e2 = weights_of([n0, n1, n2, n3])
        width_ = 512

        def body(i, value):
            here = pl.ds(pl.multiple_of(i * width_, width_), width_)
            mixed = q0[here, :] * e0 + q1[here, :] * e1 + q2[here, :] * e2
            gauge = lax.broadcasted_iota(jnp.int32, (count, width_), 1) + i * width_
            hot = jnp.where(gauge_ref[...] == gauge, 1.0, 0.0).astype(BF16)
            return value + pick(hot, mixed)

        rows_ref[...] = lax.fori_loop(0, gauges // width_, body, jnp.zeros(rows_ref.shape, F32))

    weights = inc_ref[...].astype(F32).astype(BF16)
    for b in range(blocks):
        here = pl.ds(b * width, width)
        rows = rows_ref[pl.ds(pl.multiple_of((step * blocks + b) * slots, slots), slots), :]
        added = sum(
            lax.dot_general(weights[b], piece, (((0,), (0,)), ((), ())), preferred_element_type=F32)
            for piece in pieces(rows, 3)
        )
        out_ref[here, :] = field_ref[here, :] + added


def finish(notes, row_gauge, gathered, incidence, field):
    blocks, slots, width = incidence.shape
    hours = field.shape[1]
    count = row_gauge.shape[0]
    step = 8
    whole = lambda shape: pl.BlockSpec(shape, lambda i: (0, 0))
    return pl.pallas_call(
        finish_kernel,
        grid=(blocks // step,),
        in_specs=[whole(n.shape) for n in notes]
        + [whole((count, 1))]
        + [whole(q.shape) for q in gathered]
        + [
            pl.BlockSpec((step, slots, width), lambda i: (i, 0, 0)),
            pl.BlockSpec((step * width, hours), lambda i: (i, 0)),
        ],
        out_specs=pl.BlockSpec((step * width, hours), lambda i: (i, 0)),
        out_shape=jax.ShapeDtypeStruct(field.shape, F32),
        scratch_shapes=[pltpu.VMEM((count, hours), F32)],
        compiler_params=params(56),
        name="finish",
    )(*notes, row_gauge.reshape(count, 1), *gathered, incidence, field)


def shifted(value, axis, by):
    devices = lax.axis_size(axis)
    pairs = [(i, i + by) for i in range(devices) if 0 <= i + by < devices]
    return lax.ppermute(value, axis, pairs)


def window(value):
    return jnp.concatenate([shifted(value, "tm", 1), value, shifted(value, "tm", -1)], axis=0)


def gathered_rows(value):
    owners = lax.axis_size("basin")
    copies = jnp.broadcast_to(value[None], (owners,) + value.shape)
    return lax.all_to_all(copies, "basin", 0, 0, tiled=False)


def over_hours(note):
    blocks = lax.axis_size("tm")
    result = note
    for by in range(1, blocks):
        result = result + lax.ppermute(note, "tm", [(i, (i + by) % blocks) for i in range(blocks)])
    return result


def shards(incidence, row_gauge, gauge_kernel, kernels, observed, first_guess):
    owners = lax.axis_size("basin")
    rows, hours = observed.shape
    gauges = rows * owners
    mats = transforms()
    spec = spectrum(gauge_kernel, kernels, mats[0])
    more = (lax.axis_index("tm") < lax.axis_size("tm") - 1).astype(F32).reshape(1)
    partial, gram = prepare(incidence, first_guess)
    all_gram = lax.all_gather(gram, "basin", axis=1, tiled=True)
    all_rows = lax.all_gather(row_gauge, "basin", axis=0, tiled=True)
    dense = table(row_gauge, partial, gauges).reshape(owners, rows, hours)
    sums = jnp.sum(lax.all_to_all(dense, "basin", 0, 0, tiled=False), axis=0)
    both = jnp.concatenate([observed, shifted(observed, "tm", -1)], axis=0)
    first = (lax.axis_index("basin") * rows).astype(jnp.int32).reshape(1)
    high, low = couple(first, all_rows, all_gram, rows, gauges)

    pulled, note = first_step(more, window(sums), both, spec, mats)
    notes, kept, state = [], [], None
    for k in range(3):
        everyone = gathered_rows(jnp.concatenate([pulled, note], axis=0))
        value = everyone[:, :rows].reshape(gauges, hours)
        notes.append(over_hours(jnp.sum(everyone[:, rows:], axis=0)))
        kept.append(value)
        around = window(mix(high, low, value))
        final = k == 2
        result = next_step(more, notes[-1], around, spec, mats, pulled, state, final)
        if final:
            (note,) = result
        else:
            state, pulled, note = result
    notes.append(over_hours(jnp.sum(gathered_rows(note), axis=0)))
    return finish(notes, row_gauge, kept, incidence, first_guess)


Z_, X_, Y_, C_ = 4, 2, 2, 2
NOTE = 8
HOURS = SPAN // 2


def device(z, x, y, c):
    return (z * X_ + x) * (Y_ * C_) + y * C_ + c


def moved(value, where):
    pairs = []
    for z, x, y, c in np.ndindex(Z_, X_, Y_, C_):
        target = where(z, x, y, c)
        if target is not None:
            pairs.append((device(z, x, y, c), device(*target)))
    return lax.ppermute(value, ("basin", "tm"), pairs)


def to_plane(z, x, y, c):
    return 2 * y + c, x, z & 1, z >> 1


def from_plane(z, x, y, c):
    return 2 * c + y, x, z >> 1, z & 1


def over_x(z, x, y, c):
    return z, 1 - x, y, c


def over_y(z, x, y, c):
    return z, x, 1 - y, c


def over_xy(z, x, y, c):
    return z, 1 - x, 1 - y, c


def over_core(z, x, y, c):
    return z, x, y, 1 - c


def z_pair(z, x, y, c):
    return z ^ 1, x, y, c


def z_middle(z, x, y, c):
    return (3 - z, x, y, c) if z in (1, 2) else None


def z_two(z, x, y, c):
    return z ^ 2, x, y, c


def z_mirror(z, x, y, c):
    return 3 - z, x, y, c


def z_next(z, x, y, c):
    return (z + 1, x, y, c) if z < 3 else None


SQUARE = (over_x, over_y, over_xy)


def split_constant(value):
    out = []
    for _ in range(3):
        piece = value.astype(jnp.bfloat16)
        out.append(piece)
        value = value - piece.astype(np.float64)
    return out


ORDERS = {2: ((0, 1), (1, 0), (0, 0)), 3: ((0, 2), (1, 1), (2, 0), (0, 1), (1, 0), (0, 0))}


def widened(mat, order):
    parts = split_constant(mat)
    return jnp.asarray(np.concatenate([parts[i] for i, _ in ORDERS[order]], axis=1))


def product(wide, value, order):
    parts = pieces(value, order)
    return dot(wide, jnp.concatenate([parts[j] for _, j in ORDERS[order]], axis=0))


def turned_transforms(order):
    half = SPAN // 2
    freq = 2.0 * np.pi * (np.arange(half) + 0.5) / SPAN
    phase = freq[:, None] * np.arange(SPAN)[None, :]
    forward = np.concatenate([np.cos(phase), -np.sin(phase)], axis=0)
    inverse = forward.T * (2.0 / SPAN)
    return [widened(mat, order) for mat in (forward, inverse[:half], inverse[half:], forward[:, :half])]


def turn(waves, spec, sign):
    half = waves.shape[0] // 2
    real, imag = waves[:half], waves[half:]
    kr, ki = spec[:half], spec[half:] * sign
    return jnp.concatenate([real * kr - imag * ki, real * ki + imag * kr], axis=0)


def plane_delayed(before, here, after, spec, forward, last, order):
    rows = here.shape[1]
    pairs = [jnp.concatenate(pair, axis=0) for pair in ((before, here), (here, after))]
    waves = product(forward, jnp.concatenate(pairs, axis=1), order)
    turned = [turn(waves[:, i * rows : (i + 1) * rows], spec, 1.0) for i in range(2)]
    out = product(last, jnp.concatenate(turned, axis=1), order)
    return out[:, :rows], out[:, rows:]


def plane_advanced(here, after, spec, forward, first, order):
    waves = product(forward, jnp.concatenate([here, after], axis=0), order)
    return product(first, turn(waves, spec, -1.0), order)


def describe_kernel(inc_ref, gauge_ref, out_ref):
    blocks, slots, width = inc_ref.shape
    tile = 8
    side = tile * slots
    weights = inc_ref[...].astype(F32).astype(BF16)
    row = lax.broadcasted_iota(jnp.int32, (side, side), 0)
    col = lax.broadcasted_iota(jnp.int32, (side, side), 1)
    same = row // slots == col // slots
    for i in range(blocks // tile):
        flat = weights[i * tile : (i + 1) * tile].reshape(side, width)
        full = lax.dot_general(flat, flat, (((1,), (1,)), ((), ())), preferred_element_type=F32)
        own = jnp.where(same, full, 0.0)
        out_ref[pl.ds(0, slots), pl.ds(i * side, side)] = jnp.sum(own.reshape(tile, slots, side), axis=0)
    out_ref[pl.ds(slots, 8), :] = jnp.broadcast_to(gauge_ref[...].astype(F32), (8, blocks * slots))


def describe(incidence, row_gauge):
    blocks, slots, _ = incidence.shape
    count = blocks * slots
    return pl.pallas_call(
        describe_kernel,
        out_shape=jax.ShapeDtypeStruct((slots + 8, count), F32),
        compiler_params=params(),
        name="describe",
        cost_estimate=SMALL,
    )(incidence, row_gauge.reshape(1, count))


def send_kernel(
    inc_hbm, field_hbm, gauge_hbm, kind_hbm, out_ref, inc_ref, field_ref, gauge_ref, kind_ref, sems, label_sems
):
    blocks, slots, width = inc_ref.shape
    chunks = sems.shape[0]
    step = blocks // chunks
    copies = []
    for i in range(chunks):
        near = pl.ds(i * step, step)
        far = pl.ds(i * step * width, step * width)
        copies.append(
            (
                pltpu.make_async_copy(inc_hbm.at[near], inc_ref.at[near], sems.at[i, 0]),
                pltpu.make_async_copy(field_hbm.at[far], field_ref.at[far], sems.at[i, 1]),
            )
        )
        for copy in copies[-1]:
            copy.start()
    labels = (
        pltpu.make_async_copy(gauge_hbm, gauge_ref, label_sems.at[0]),
        pltpu.make_async_copy(kind_hbm, kind_ref, label_sems.at[1]),
    )
    for copy in labels:
        copy.start()
    for i in range(chunks):
        for copy in copies[i]:
            copy.wait()
        parts = []
        for b in range(i * step, (i + 1) * step):
            weight = inc_ref[b].astype(F32).astype(BF16)
            value = jnp.concatenate(pieces(field_ref[pl.ds(b * width, width), :], 3)[::-1], axis=0)
            parts.append(dot(jnp.concatenate([weight] * 3, axis=1), value))
        out_ref[pl.ds(0, HOURS), pl.ds(i * step * slots, step * slots)] = jnp.transpose(
            jnp.concatenate(parts, axis=0)
        )
    for copy in labels:
        copy.wait()
    count, kinds = gauge_ref.shape[1], kind_ref.shape[1]
    kind = jnp.concatenate([kind_ref[...].astype(F32), jnp.zeros((1, count - kinds), F32)], axis=1)
    out_ref[pl.ds(HOURS, 8), :] = jnp.concatenate(
        [gauge_ref[...].astype(F32), kind, jnp.zeros((6, count), F32)], axis=0
    )


def send(incidence, field, row_gauge, gauge_kernel):
    count, rows = row_gauge.shape[0], gauge_kernel.shape[0]
    chunks = 4
    return pl.pallas_call(
        send_kernel,
        in_specs=[pl.BlockSpec(memory_space=pltpu.HBM)] * 4,
        out_shape=jax.ShapeDtypeStruct((HOURS + 8, count), F32),
        scratch_shapes=[
            pltpu.VMEM(incidence.shape, incidence.dtype),
            pltpu.VMEM(field.shape, F32),
            pltpu.VMEM((1, count), row_gauge.dtype),
            pltpu.VMEM((1, rows), gauge_kernel.dtype),
            pltpu.SemaphoreType.DMA((chunks, 2)),
            pltpu.SemaphoreType.DMA((2,)),
        ],
        compiler_params=params(60),
        name="send",
        cost_estimate=SMALL,
    )(incidence, field, row_gauge.reshape(1, count), gauge_kernel.reshape(1, rows))


def hot_rows(gauge, first, rows):
    mine = (lax.broadcasted_iota(jnp.int32, (rows, gauge.shape[1]), 0) + first).astype(F32)
    return jnp.where(gauge == mine, 1.0, 0.0).astype(BF16)


def spread_kernel(first_ref, mine_ref, other_ref, *out_refs):
    rows = out_refs[0].shape[1]
    both = jnp.concatenate([mine_ref[...], other_ref[...]], axis=1)
    stacked = jnp.concatenate(pieces(both[:HOURS], 3), axis=0)
    for m, out_ref in enumerate(out_refs):
        hot = hot_rows(both[HOURS : HOURS + 1], first_ref[m], rows)
        result = lax.dot_general(stacked, hot, (((1,), (1,)), ((), ())), preferred_element_type=F32)
        out_ref[...] = (result[2 * HOURS :] + result[HOURS : 2 * HOURS]) + result[:HOURS]


def spread(first, parcels, rows):
    return pl.pallas_call(
        spread_kernel,
        in_specs=[pl.BlockSpec(memory_space=pltpu.SMEM)] + [pl.BlockSpec(memory_space=pltpu.VMEM)] * 2,
        out_shape=[jax.ShapeDtypeStruct((HOURS, rows), F32)] * 4,
        compiler_params=params(),
        name="spread",
        cost_estimate=SMALL,
    )(first, *parcels)


def plane_couple_kernel(last, first_ref, *refs):
    if last:
        all_ref, before_ref, high_ref, low_ref, total_ref, meta_ref = refs
        total_ref[...] = before_ref[...]
    else:
        all_ref, total_ref, meta_ref = refs
        total_ref[...] = jnp.zeros_like(total_ref)
    parts, height, count = meta_ref.shape
    slots = height - 8
    cols, rows = total_ref.shape
    tile = 256
    for i in range(parts):
        meta_ref[i] = all_ref[:, i * count : (i + 1) * count]
    row = lax.broadcasted_iota(jnp.int32, (tile, tile), 0)
    col = lax.broadcasted_iota(jnp.int32, (tile, tile), 1)
    same = row // slots == col // slots

    def body(i, carry):
        gauge = meta_ref[i, slots : slots + 1, :]
        near = []
        for j in range(count // tile):
            here = slice(j * tile, (j + 1) * tile)
            block = jnp.concatenate([meta_ref[i, :slots, here]] * (tile // slots), axis=0)
            block = jnp.where(same, block, 0.0).astype(BF16)
            mine = jnp.concatenate(
                [hot_rows(gauge[:, here], first_ref[4 + h], rows // 2) for h in range(2)], axis=0
            )
            near.append(
                lax.dot_general(block, mine, (((1,), (1,)), ((), ())), preferred_element_type=F32)
            )
        near = jnp.concatenate(near, axis=0)
        high = near.astype(BF16)
        rest = near - high.astype(F32)
        hot = jnp.concatenate([hot_rows(gauge, first_ref[m], cols // 4) for m in range(4)], axis=0)
        total_ref[...] += dot(hot, high)

        @pl.when(jnp.max(jnp.abs(rest)) > 0.0)
        def _():
            total_ref[...] += dot(hot, rest.astype(BF16))

        return carry

    lax.fori_loop(0, parts, body, 0)
    if last:
        high, low = pieces(total_ref[...], 2)
        high_ref[...] = high
        low_ref[...] = low


def plane_couple(first, meta, rows, before=None):
    height, wide = meta.shape
    parts = 2 * X_
    shape = (4 * rows, 2 * rows)
    last = before is not None
    args = [first, meta] + ([before] if last else [])
    scratch = [pltpu.VMEM((parts, height, wide // parts), F32)]
    return pl.pallas_call(
        functools.partial(plane_couple_kernel, last),
        in_specs=[pl.BlockSpec(memory_space=pltpu.SMEM)]
        + [pl.BlockSpec(memory_space=pltpu.VMEM)] * (len(args) - 1),
        out_shape=[jax.ShapeDtypeStruct(shape, BF16)] * 2 if last else jax.ShapeDtypeStruct(shape, F32),
        scratch_shapes=([pltpu.VMEM(shape, F32)] if last else []) + scratch,
        compiler_params=params(),
        name="plane_couple",
        cost_estimate=pl.CostEstimate(
            flops=2 * 8 * wide * rows * rows, bytes_accessed=2_000_000, transcendentals=0
        ),
    )(*args)


def plane_mix_kernel(high_ref, low_ref, a_ref, b_ref, c_ref, d_ref, *refs):
    *extra, mine_ref, other_ref = refs
    refs = (a_ref, b_ref, c_ref, d_ref)
    height, rows = a_ref.shape
    body = pl.ds(0, HOURS)
    one, two = pieces(jnp.concatenate([ref[body, :] for ref in refs], axis=1), 2)
    both = dot(jnp.concatenate([two, one], axis=0), high_ref[...])
    result = (both[:HOURS] + dot(one, low_ref[...])) + both[HOURS:]
    mine_ref[body, :] = result[:, :rows]
    other_ref[body, :] = result[:, rows:]
    if height > HOURS:
        tail = pl.ds(HOURS, NOTE)
        note = sum(ref[tail, :] for ref in refs)
        mine_ref[tail, :] = note
        other_ref[tail, :] = note
    for ref in extra:
        other_ref[pl.ds(height, ref.shape[0]), :] = ref[...]


def plane_mix(coupling, values, extra):
    height, rows = values[0].shape
    return pl.pallas_call(
        plane_mix_kernel,
        out_shape=[
            jax.ShapeDtypeStruct((height, rows), F32),
            jax.ShapeDtypeStruct((height + sum(value.shape[0] for value in extra), rows), F32),
        ],
        compiler_params=params(),
        name="plane_mix",
        cost_estimate=SMALL,
    )(*coupling, *values, *extra)


def plane_rows_kernel(first_ref, meta_ref, meta_other_ref, a_ref, b_ref, c_ref, d_ref, *refs):
    if len(refs) > 2:
        *stack, last_ref, beside_ref, mine_ref, other_ref, stack_ref = refs
    else:
        mine_ref, other_ref = refs
    rows = a_ref.shape[1]
    value = jnp.concatenate([ref[pl.ds(0, HOURS), :] for ref in (a_ref, b_ref, c_ref, d_ref)], axis=1)
    one, two = pieces(value, 2)
    stacked = jnp.concatenate([two, one], axis=0)
    picked = []
    for ref in (meta_ref, meta_other_ref):
        gauge = ref[0:1, :]
        hot = jnp.concatenate([hot_rows(gauge, first_ref[m], rows) for m in range(4)], axis=0)
        both = dot(stacked, hot)
        picked.append(both[:HOURS] + both[HOURS:])
    mine_ref[...] = picked[0]
    count = picked[1].shape[1] // rows
    for i in range(count):
        other_ref[pl.ds(i * HOURS, HOURS), :] = picked[1][:, i * rows : (i + 1) * rows]
    if len(refs) > 2:
        top = stack_ref.shape[0] - HOURS
        for ref in stack:
            stack_ref[pl.ds(0, top), :] = ref[...]
        for i in range(count):
            here = pl.ds(i * rows, rows)
            beside = beside_ref[pl.ds(beside_ref.shape[0] - (count - i) * HOURS, HOURS), :]
            stack_ref[pl.ds(top, HOURS), here] = last_ref[:, here] + beside


def plane_rows(first, metas, values, before):
    rows = values[0].shape[1]
    slots = metas[0].shape[1]
    args = [first, *metas, *values, *before]
    shapes = [(HOURS, slots), (slots // rows * HOURS, rows)]
    if before:
        shapes.append(((len(before) - 1) * HOURS, slots))
    return pl.pallas_call(
        plane_rows_kernel,
        in_specs=[pl.BlockSpec(memory_space=pltpu.SMEM)]
        + [pl.BlockSpec(memory_space=pltpu.VMEM)] * (len(args) - 1),
        out_shape=[jax.ShapeDtypeStruct(shape, F32) for shape in shapes],
        compiler_params=params(),
        name="plane_rows",
        cost_estimate=pl.CostEstimate(flops=1_000_000_000, bytes_accessed=2_000_000, transcendentals=0),
    )(*args)


def gain(kernels):
    return jnp.max(jnp.sum(kernels, axis=1, keepdims=True), axis=0, keepdims=True)


def spectra(kind, kernels, wide):
    classes = kernels.shape[0]
    row = lax.broadcasted_iota(jnp.int32, (classes, kind.shape[1]), 0).astype(F32)
    hot = jnp.where(row == kind, 1.0, 0.0).astype(BF16)
    taps = jnp.transpose(kernels / gain(kernels))
    chosen = dot(jnp.concatenate(pieces(taps, 3)[::-1], axis=1), jnp.concatenate([hot] * 3, axis=0))
    return product(wide, chosen, 3)


def plane_spectrum_kernel(class_ref, kernels_ref, wide_ref, out_ref):
    kind = class_ref[1:2, : out_ref.shape[1]]
    out_ref[...] = spectra(kind, kernels_ref[...], wide_ref[...])


def plane_spectrum(meta, kernels, wide, rows):
    return pl.pallas_call(
        plane_spectrum_kernel,
        out_shape=jax.ShapeDtypeStruct((SPAN, rows), F32),
        compiler_params=params(),
        name="plane_spectrum",
        cost_estimate=SMALL,
    )(meta, kernels, wide)


def sides(even, pair, middle):
    return jnp.where(even, middle, pair), jnp.where(even, pair, middle)


def plane_call(kernel, name, shapes, flags, args):
    return pl.pallas_call(
        kernel,
        in_specs=[pl.BlockSpec(memory_space=pltpu.SMEM)] * len(flags)
        + [pl.BlockSpec(memory_space=pltpu.VMEM)] * len(args),
        out_shape=[jax.ShapeDtypeStruct(shape, F32) for shape in shapes],
        compiler_params=params(),
        name=name,
        cost_estimate=SMALL,
    )(*flags, *args)


def plane_first_kernel(
    flag_ref, here_ref, pair_ref, middle_ref, spec_ref, kernels_ref, forward3, last3, forward, first, out_ref
):
    spec = spec_ref[...]
    before, after = sides(flag_ref[0] > 0.5, pair_ref[...], middle_ref[...])
    here = here_ref[...]
    both = plane_delayed(before[:HOURS], here[:HOURS], after[:HOURS], spec, forward3[...], last3[...], 3)
    scale = gain(kernels_ref[...])
    now = here[HOURS:] - both[0] * scale
    later = (after[HOURS:] - both[1] * scale) * flag_ref[1]
    out_ref[...] = plane_advanced(now, later, spec, forward[...], first[...], 2)


def plane_delay_kernel(flag_ref, here_ref, pair_ref, middle_ref, spec_ref, forward, last, out_ref):
    body = pl.ds(0, HOURS)
    before, after = sides(flag_ref[0] > 0.5, pair_ref[body, :], middle_ref[body, :])
    out = plane_delayed(before, here_ref[body, :], after, spec_ref[...], forward[...], last[...], 2)
    for i in range(2):
        out_ref[pl.ds(i * HOURS, HOURS), :] = out[i]


def write_note(ref, rows):
    tail = [jnp.zeros((NOTE - len(rows), ref.shape[1]), F32)]
    ref[pl.ds(HOURS, NOTE), :] = jnp.concatenate(rows + tail, axis=0)


def plane_open_kernel(
    flag_ref, here_ref, pair_ref, middle_ref, pulled_ref, spec_ref, forward, first, last, out_ref, delayed_ref
):
    here = here_ref[...]
    spec = spec_ref[...]
    before, after = sides(flag_ref[0] > 0.5, pair_ref[...], middle_ref[...])
    now, later = plane_delayed(before, here, after, spec, forward[...], last[...], 2)
    out_ref[pl.ds(0, HOURS), :] = plane_advanced(now, later * flag_ref[1], spec, forward[...], first[...], 2)
    write_note(out_ref, [lanes(pulled_ref[...], here), lanes(now, now)])
    delayed_ref[pl.ds(0, HOURS), :] = now
    delayed_ref[pl.ds(HOURS, HOURS), :] = later


def plane_step_kernel(
    flag_ref,
    here_ref,
    pair_ref,
    two_ref,
    mirror_ref,
    pulled_ref,
    delayed_ref,
    old_z_ref,
    old_s_ref,
    old_delayed_ref,
    spec_ref,
    forward,
    first,
    total_ref,
    out_ref,
    kept_ref,
):
    tail, body = pl.ds(HOURS, NOTE), pl.ds(0, HOURS)
    total_ref[...] = (here_ref[tail, :] + pair_ref[tail, :]) + (two_ref[...] + mirror_ref[...])
    inverse = total(total_ref, 0) / total(total_ref, 1)
    z = pulled_ref[body, :] * inverse - old_z_ref[...]
    s = here_ref[body, :] * inverse - old_s_ref[...]
    both = delayed_ref[...] * inverse - old_delayed_ref[...]
    now, later = both[:HOURS], both[HOURS:]
    following = plane_advanced(now, later * flag_ref[1], spec_ref[...], forward[...], first[...], 2)
    out_ref[body, :] = following * inverse
    write_note(out_ref, [lanes(z, s), lanes(now, now)])
    for i, value in enumerate((z, s, now)):
        kept_ref[pl.ds(i * HOURS, HOURS), :] = value


def plane_close_kernel(
    here_ref,
    before_ref,
    pulled_ref,
    kept_ref,
    old_z_ref,
    old_s_ref,
    old_delayed_ref,
    open_ref,
    spec_ref,
    kernels_ref,
    forward,
    last,
    out_ref,
):
    body = pl.ds(0, HOURS)
    here, raw = here_ref[body, :], pulled_ref[body, :]
    waves = product(forward[...], jnp.concatenate([before_ref[body, :], here], axis=0), 2)
    now = product(last[...], turn(waves, spec_ref[...], 1.0), 2)
    z, s, delayed = (kept_ref[pl.ds(i * HOURS, HOURS), :] for i in range(3))
    note = [pulled_ref[HOURS + i : HOURS + i + 1, :] for i in range(2)]
    for left in (raw, z, old_z_ref[...]):
        note += [lanes(left, right) for right in (here, s, old_s_ref[...])]
    parts = (now, delayed, old_delayed_ref[body, :])
    for i in range(3):
        note += [lanes(parts[i], parts[j]) for j in range(i, 3)]
    known = [total(open_ref, 0), total(open_ref, 1), gain(kernels_ref[...])]
    note = [jnp.sum(jnp.concatenate(note, axis=0), axis=1, keepdims=True)]
    note += [value / out_ref.shape[0] for value in known]
    count = sum(value.shape[0] for value in note)
    note = jnp.concatenate(note + [jnp.zeros((24 - count, 1), F32)], axis=0)
    shape = (24, out_ref.shape[1])
    row, col = (lax.broadcasted_iota(jnp.int32, shape, i) for i in range(2))
    note = jnp.sum(jnp.where(row == col, jnp.broadcast_to(note, shape), 0.0), axis=0, keepdims=True)
    out_ref[...] = jnp.broadcast_to(note, out_ref.shape)


def plane_weights(close):
    entry = lambda i: close[:, i : i + 1]
    n1, t1, scale = (entry(17 + i) for i in range(3))
    n2, t2 = entry(0), entry(1)
    a1 = t1 / n1
    a2, r2 = (t2 / n2) / a1, n2 / n1
    plain = (1.0, -a2, -r2)
    n3 = sum(plain[i] * plain[j] * entry(2 + 3 * i + j) for i in range(3) for j in range(3))
    pairs = [(i, j) for i in range(3) for j in range(i, 3)]
    t3 = sum(
        plain[i] * plain[j] * entry(11 + n) * (1.0 if i == j else 2.0) for n, (i, j) in enumerate(pairs)
    )
    a3, r3 = (t3 / n3) / a1, n3 / n2
    unit = 1.0 / (a1 * scale)
    c3 = unit / (a3 * (a2 - r2) - r3)
    c2 = -a3 * c3
    c1 = unit - r2 * c2
    step = c2 - c3 * a2
    return c1 - step - c3 * r2, step / a1, c3


def plane_combine_kernel(close_ref, stack_ref, mine_ref, beside_ref, out_ref):
    rows = beside_ref.shape[1]
    close = jnp.sum(close_ref[...], axis=0, keepdims=True)
    e0, e1, e2 = plane_weights(close)
    for i in range(out_ref.shape[0] // rows):
        here = pl.ds(i * rows, rows)
        last = mine_ref[:, here] + beside_ref[pl.ds(i * HOURS, HOURS), :]
        value = stack_ref[pl.ds(0, HOURS), here] * e0 + stack_ref[pl.ds(HOURS, HOURS), here] * e1 + last * e2
        out_ref[here, :] = jnp.transpose(value)


def plane_finish_kernel(rows_ref, inc_ref, field_ref, out_ref):
    blocks, slots, width = inc_ref.shape
    weights = inc_ref[...].astype(F32).astype(BF16)
    for b in range(blocks):
        here = pl.ds(b * width, width)
        rows = jnp.concatenate(pieces(rows_ref[pl.ds(b * slots, slots), :], 2), axis=0)
        twice = jnp.concatenate([weights[b]] * 2, axis=0)
        added = lax.dot_general(twice, rows, (((0,), (0,)), ((), ())), preferred_element_type=F32)
        out_ref[here, :] = field_ref[here, :] + added


def plane_finish(rows, incidence, field):
    blocks, slots, width = incidence.shape
    hours = field.shape[1]
    step = 16
    return pl.pallas_call(
        plane_finish_kernel,
        grid=(blocks // step,),
        in_specs=[
            pl.BlockSpec((step * slots, hours), lambda i: (i, 0)),
            pl.BlockSpec((step, slots, width), lambda i: (i, 0, 0)),
            pl.BlockSpec((step * width, hours), lambda i: (i, 0)),
        ],
        out_specs=pl.BlockSpec((step * width, hours), lambda i: (i, 0)),
        out_shape=jax.ShapeDtypeStruct(field.shape, F32),
        compiler_params=params(),
        name="plane_finish",
    )(rows, incidence, field)


def plane_shards(incidence, row_gauge, gauge_kernel, kernels, observed, first_guess):
    rows, hours = observed.shape
    basin, tm = lax.axis_index("basin"), lax.axis_index("tm")
    z, x, y, c = basin // X_, basin % X_, tm // C_, tm % C_
    place = 2 * y + x
    first = jnp.stack([4 * c + (place ^ m) for m in range(4)] + [4 * c + place, 4 * (1 - c) + place])
    first = (first * rows).astype(jnp.int32)
    flags = jnp.stack([1 - z % 2, (z < Z_ - 1).astype(z.dtype), (z > 0).astype(z.dtype)]).astype(F32)
    forward, inverse_first, inverse_last, _ = turned_transforms(2)
    forward3, _, inverse_last3, short3 = turned_transforms(3)
    block, noted = (hours, rows), (hours + NOTE, rows)

    seen = moved(observed, to_plane)
    parcel = send(incidence, first_guess, row_gauge, gauge_kernel)
    parcel, near = lax.optimization_barrier((parcel, incidence))
    parcel = moved(parcel, to_plane)
    near, seen = lax.optimization_barrier((near, seen))
    meta = describe(near, row_gauge)
    meta = jnp.concatenate([meta, moved(meta, over_x)], axis=1)
    meta = jnp.concatenate([meta, moved(meta, z_pair)], axis=1)
    parcel, seen = lax.optimization_barrier((parcel, seen))
    parcels = [parcel, moved(parcel, over_core)]
    spec = plane_spectrum(parcel[hours:], kernels, short3, rows)
    parcels[1], seen, meta, spec = lax.optimization_barrier((parcels[1], seen, meta, spec))
    half = meta.shape[1] // 2
    far = moved(jnp.where(c == 0, meta[:, :half], meta[:, half:]), z_two)
    dense = spread(first, parcels, rows)
    metas = [value[hours:] for value in parcels]
    sums = dense[0] + sum(moved(value, where) for value, where in zip(dense[1:], SQUARE))
    sums, far = lax.optimization_barrier((sums, far))
    around = [meta, jnp.concatenate([far, moved(far, over_core)], axis=1)]
    sums = jnp.concatenate([sums, jnp.transpose(seen)], axis=0)
    sums = [sums, moved(sums, z_pair), moved(sums, z_middle)]
    coupled = plane_couple(first, around[0], rows)
    coupled, sums = lax.optimization_barrier((coupled, sums))
    coupling = plane_couple(first, around[1], rows, coupled)
    (pulled0,) = plane_call(
        plane_first_kernel,
        "plane_first",
        [block],
        [flags],
        [*sums, spec, kernels, forward3, inverse_last3, forward, inverse_first],
    )

    def mixing(pulled, extra):
        values = [pulled] + [moved(pulled, where) for where in SQUARE]
        mine, other = plane_mix(coupling, values, extra)
        beside = moved(other, over_core)
        return values, mine + beside[: pulled.shape[0]], beside

    values, mixed0, _ = mixing(pulled0, [])
    picked, theirs = plane_rows(first, metas, values, [])
    sums = [mixed0, moved(mixed0, z_pair), moved(mixed0, z_middle)]
    pulled1, delayed0 = plane_call(
        plane_open_kernel,
        "plane_open",
        [noted, (2 * hours, rows)],
        [flags],
        [*sums, pulled0, spec, forward, inverse_first, inverse_last],
    )

    values, mixed1, beside = mixing(pulled1, [theirs])
    picked, theirs, stack = plane_rows(first, metas, values, [picked, beside])
    sums = [mixed1, moved(mixed1, z_pair), moved(mixed1, z_middle)]
    two, mirror = moved(mixed1[hours:], z_two), moved(mixed1[hours:], z_mirror)
    (delayed1,) = plane_call(
        plane_delay_kernel, "plane_delay", [(2 * hours, rows)], [flags], [*sums, spec, forward, inverse_last]
    )
    open_note, pulled2, kept = plane_call(
        plane_step_kernel,
        "plane_step",
        [(NOTE, rows), noted, (3 * hours, rows)],
        [flags],
        [*sums[:2], two, mirror, pulled1, delayed1, pulled0, mixed0, delayed0, spec, forward, inverse_first],
    )

    values, mixed2, beside = mixing(pulled2, [theirs])
    picked, theirs, stack = plane_rows(first, metas, values, [stack, picked, beside])
    (note,) = plane_call(
        plane_close_kernel,
        "plane_close",
        [(Z_ * X_ * Y_ * C_, rows // 2)],
        [],
        [
            *(mixed2, moved(mixed2, z_next), pulled2, kept, pulled0, mixed0, delayed0),
            *(open_note, spec, kernels, forward, inverse_last),
        ],
    )
    close_note = lax.all_to_all(note, ("basin", "tm"), 0, 0, tiled=True)
    (answer,) = plane_call(
        plane_combine_kernel,
        "plane_combine",
        [(parcel.shape[1], hours)],
        [],
        [close_note, stack, picked, moved(theirs, over_core)],
    )
    return plane_finish(moved(answer, from_plane), incidence, first_guess)


def solution(mesh):
    planes = dict(mesh.shape) == {"basin": Z_ * X_, "tm": Y_ * C_}
    in_specs = (
        P("basin", None, None),
        P("basin"),
        P("basin"),
        P(),
        P("basin", "tm"),
        P("basin", "tm"),
    )
    return jax.shard_map(
        plane_shards if planes else shards, mesh=mesh, in_specs=in_specs, out_specs=P("basin", "tm"), check_vma=False
    )
```

```python
import functools

import jax
import jax.numpy as jnp
import numpy as np
from jax import lax
from jax.experimental import pallas as pl
from jax.experimental.pallas import tpu as pltpu
from jax.sharding import PartitionSpec as P

F32 = jnp.float32
BF16 = jnp.bfloat16
HIGH = lax.Precision.HIGHEST
SPAN = 256
MIB = 1024 * 1024


SMALL = pl.CostEstimate(flops=1, bytes_accessed=1, transcendentals=0)


def params(mib=16):
    return pltpu.CompilerParams(vmem_limit_bytes=mib * MIB)


def transforms():
    half = SPAN // 2
    freq = 2.0 * np.pi * (np.arange(half) + 0.5) / SPAN
    phase = np.arange(SPAN)[:, None] * freq[None, :]
    forward = np.concatenate([np.cos(phase), -np.sin(phase)], axis=1)
    inverse = forward.T * (2.0 / SPAN)
    return (
        jnp.asarray(forward, F32),
        jnp.asarray(inverse[:, :half], F32),
        jnp.asarray(inverse[:, half:], F32),
    )


def dot(a, b):
    return jnp.dot(a, b, preferred_element_type=F32)


def exact(a, b):
    return jnp.dot(a, b, precision=HIGH, preferred_element_type=F32)


def pieces(value, count):
    out = []
    for _ in range(count):
        piece = value.astype(BF16)
        out.append(piece)
        value = value - piece.astype(F32)
    return out


def pick(hot, value):
    return sum(dot(hot, piece) for piece in pieces(value, 3))


def prepare_kernel(inc_ref, field_ref, partial_ref, gram_ref):
    blocks, slots, width = inc_ref.shape
    rows = blocks * slots
    weights = inc_ref[...].astype(F32).astype(BF16)
    for b in range(blocks):
        value = field_ref[pl.ds(b * width, width), :]
        partial_ref[pl.ds(b * slots, slots), :] = pick(weights[b], value)
    flat = weights.reshape(rows, width)
    full = lax.dot_general(flat, flat, (((1,), (1,)), ((), ())), preferred_element_type=F32)
    row = lax.broadcasted_iota(jnp.int32, (rows, rows), 0)
    col = lax.broadcasted_iota(jnp.int32, (rows, rows), 1)
    own = jnp.where(row // slots == col // slots, full, 0.0)
    gram_ref[...] = jnp.sum(own.reshape(blocks, slots, rows), axis=0)


def prepare(incidence, field):
    blocks, slots, width = incidence.shape
    hours = field.shape[1]
    step = 8
    return pl.pallas_call(
        prepare_kernel,
        grid=(blocks // step,),
        in_specs=[
            pl.BlockSpec((step, slots, width), lambda i: (i, 0, 0)),
            pl.BlockSpec((step * width, hours), lambda i: (i, 0)),
        ],
        out_specs=[
            pl.BlockSpec((step * slots, hours), lambda i: (i, 0)),
            pl.BlockSpec((slots, step * slots), lambda i: (0, i)),
        ],
        out_shape=[
            jax.ShapeDtypeStruct((blocks * slots, hours), F32),
            jax.ShapeDtypeStruct((slots, blocks * slots), F32),
        ],
        compiler_params=params(56),
        name="prepare",
    )(incidence, field)


def table_kernel(gauge_ref, partial_ref, out_ref):
    slots = partial_ref.shape[0]
    rows = out_ref.shape[0]
    first = pl.program_id(0) * rows
    gauge = lax.broadcasted_iota(jnp.int32, (rows, slots), 0) + first
    hot = jnp.where(gauge_ref[...] == gauge, 1.0, 0.0).astype(BF16)
    out_ref[...] = pick(hot, partial_ref[...])


def table(row_gauge, partial, gauges):
    slots, hours = partial.shape
    step = 256
    return pl.pallas_call(
        table_kernel,
        grid=(gauges // step,),
        in_specs=[
            pl.BlockSpec((1, slots), lambda i: (0, 0)),
            pl.BlockSpec((slots, hours), lambda i: (0, 0)),
        ],
        out_specs=pl.BlockSpec((step, hours), lambda i: (i, 0)),
        out_shape=jax.ShapeDtypeStruct((gauges, hours), F32),
        compiler_params=params(56),
        name="table",
    )(row_gauge.reshape(1, slots), partial)


def couple_kernel(first_ref, lane_ref, sub_ref, gram_ref, high_ref, low_ref, near_ref):
    slots = gram_ref.shape[0]
    count = lane_ref.shape[1]
    rows, cols = high_ref.shape
    tile = 256
    first = first_ref[0]

    @pl.when(pl.program_id(0) == 0)
    def _():
        row = lax.broadcasted_iota(jnp.int32, (tile, tile), 0)
        col = lax.broadcasted_iota(jnp.int32, (tile, tile), 1)
        same = row // slots == col // slots
        mine = lax.broadcasted_iota(jnp.int32, (rows, tile), 0) + first

        def body(i, carry):
            here = pl.ds(pl.multiple_of(i * tile, tile), tile)
            block = jnp.concatenate([gram_ref[:, here]] * (tile // slots), axis=0)
            block = jnp.where(same, block, 0.0).astype(BF16)
            hot = jnp.where(lane_ref[:, here] == mine, 1.0, 0.0).astype(BF16)
            near_ref[:, here] = dot(hot, block)
            return carry

        lax.fori_loop(0, count // tile, body, 0)

    def chunk(i, total):
        here = pl.ds(pl.multiple_of(i * 1024, 1024), 1024)
        gauge = lax.broadcasted_iota(jnp.int32, (1024, cols), 1) + pl.program_id(0) * cols
        hot = jnp.where(sub_ref[here, :] == gauge, 1.0, 0.0).astype(BF16)
        near = near_ref[:, here]
        high = near.astype(BF16)
        low = (near - high.astype(F32)).astype(BF16)
        return total + dot(high, hot) + dot(low, hot)

    total = lax.fori_loop(0, count // 1024, chunk, jnp.zeros((rows, cols), F32))
    high, low = pieces(total, 2)
    high_ref[...] = high
    low_ref[...] = low


def couple(first, row_gauge, gram, rows, gauges):
    count = row_gauge.shape[0]
    step = 256
    return pl.pallas_call(
        couple_kernel,
        grid=(gauges // step,),
        in_specs=[
            pl.BlockSpec(memory_space=pltpu.SMEM),
            pl.BlockSpec((1, count), lambda i: (0, 0)),
            pl.BlockSpec((count, 1), lambda i: (0, 0)),
            pl.BlockSpec(gram.shape, lambda i: (0, 0)),
        ],
        out_specs=[pl.BlockSpec((rows, step), lambda i: (0, i))] * 2,
        out_shape=[jax.ShapeDtypeStruct((rows, gauges), BF16)] * 2,
        scratch_shapes=[pltpu.VMEM((rows, count), F32)],
        compiler_params=params(56),
        name="couple",
    )(first, row_gauge.reshape(1, count), row_gauge.reshape(count, 1), gram)


def mix_kernel(high_ref, low_ref, value_ref, out_ref):
    high = high_ref[...]
    low = low_ref[...]
    one, two, three = pieces(value_ref[...], 3)
    out_ref[...] = (dot(high, three) + dot(low, two)) + (dot(high, two) + dot(low, one)) + dot(high, one)


def mix(high, low, value):
    return pl.pallas_call(
        mix_kernel,
        out_shape=jax.ShapeDtypeStruct((high.shape[0], value.shape[1]), F32),
        compiler_params=params(56),
        name="mix",
    )(high, low, value)


def spectrum_kernel(class_ref, kernels_ref, forward_ref, out_ref):
    rows = class_ref.shape[0]
    classes, taps = kernels_ref.shape
    kind = lax.broadcasted_iota(jnp.int32, (rows, classes), 1)
    hot = jnp.where(class_ref[...] == kind, 1.0, 0.0)
    out_ref[...] = exact(exact(hot, kernels_ref[...]), forward_ref[pl.ds(0, taps), :])


def spectrum(gauge_kernel, kernels, forward):
    rows = gauge_kernel.shape[0]
    return pl.pallas_call(
        spectrum_kernel,
        out_shape=jax.ShapeDtypeStruct((rows, SPAN), F32),
        compiler_params=params(56),
        name="spectrum",
    )(gauge_kernel.reshape(rows, 1), kernels, forward)


def delayed(before, here, after, spec, forward, inverse_last):
    rows, half = here.shape
    stacked = jnp.concatenate(
        [jnp.concatenate([before, here], axis=1), jnp.concatenate([here, after], axis=1)], axis=0
    )
    waves = exact(stacked, forward)
    real, imag = waves[:, :half], waves[:, half:]
    kr = jnp.concatenate([spec[:, :half]] * 2, axis=0)
    ki = jnp.concatenate([spec[:, half:]] * 2, axis=0)
    turned = jnp.concatenate([real * kr - imag * ki, real * ki + imag * kr], axis=1)
    out = exact(turned, inverse_last)
    return out[:rows], out[rows:]


def advanced(here, after, spec, forward, inverse_first):
    half = here.shape[1]
    waves = exact(jnp.concatenate([here, after], axis=1), forward)
    real, imag = waves[:, :half], waves[:, half:]
    kr, ki = spec[:, :half], spec[:, half:]
    turned = jnp.concatenate([real * kr + imag * ki, imag * kr - real * ki], axis=1)
    return exact(turned, inverse_first)


def lanes(a, b):
    return jnp.sum(a * b, axis=0, keepdims=True)


def total(ref, row):
    return jnp.sum(ref[row : row + 1, :], axis=1, keepdims=True)


def ratios(ref):
    square = total(ref, 0)
    alpha = jnp.sqrt(square)
    beta = jnp.sqrt(jnp.maximum(total(ref, 1) / square - 2.0 * total(ref, 2) + square, 0.0))
    return alpha, beta


def first_kernel(
    more_ref, sums_ref, observed_ref, spec_ref, forward_ref, first_ref, last_ref, out_ref, note_ref
):
    rows, half = observed_ref.shape[0] // 2, observed_ref.shape[1]
    spec, forward = spec_ref[...], forward_ref[...]
    before, here, after = (sums_ref[pl.ds(i * rows, rows), :] for i in range(3))
    now, later = delayed(before, here, after, spec, forward, last_ref[...])
    start = observed_ref[pl.ds(0, rows), :] - now
    start_later = (observed_ref[pl.ds(rows, rows), :] - later) * more_ref[0]
    out_ref[...] = advanced(start, start_later, spec, forward, first_ref[...])
    note_ref[...] = jnp.concatenate([lanes(start, start), jnp.zeros((7, half), F32)], axis=0)


def first_step(more, sums, observed, spec, mats):
    rows, half = spec.shape[0], observed.shape[1]
    return pl.pallas_call(
        first_kernel,
        in_specs=[pl.BlockSpec(memory_space=pltpu.SMEM)] + [pl.BlockSpec(memory_space=pltpu.VMEM)] * 6,
        out_shape=[jax.ShapeDtypeStruct((rows, half), F32), jax.ShapeDtypeStruct((8, half), F32)],
        compiler_params=params(56),
        name="first_step",
    )(more, sums, observed, spec, *mats)


def step_kernel(
    opening,
    final,
    more_ref,
    note_ref,
    sums_ref,
    spec_ref,
    forward_ref,
    first_ref,
    last_ref,
    pulled_ref,
    *refs,
):
    if opening:
        state_ref = None
    else:
        state_ref, *refs = refs
    if final:
        (out_note_ref,) = refs
    else:
        new_ref, out_ref, out_note_ref = refs
    rows, half = pulled_ref.shape
    spec, forward = spec_ref[...], forward_ref[...]
    if opening:
        scale = 1.0 / jnp.sqrt(total(note_ref, 0))
        along = sums_ref[...] * scale
        new_s, new_su = along, along
        new_zu = pulled_ref[...] * scale
        new_z = new_zu
    else:
        alpha, beta = ratios(note_ref)
        a, b, g = 1.0 / (alpha * beta), alpha / beta, beta / alpha
        wide = pl.ds(0, 3 * rows), pl.ds(3 * rows, 3 * rows)
        new_su = sums_ref[...] * a - state_ref[wide[1], :] * b
        new_s = new_su - state_ref[wide[0], :] * g
        new_zu = pulled_ref[...] * a - state_ref[pl.ds(7 * rows, rows), :] * b
        new_z = new_zu - state_ref[pl.ds(6 * rows, rows), :] * g
    before, here, after = (new_s[i * rows : (i + 1) * rows] for i in range(3))
    now, later = delayed(before, here, after, spec, forward, last_ref[...])
    out_note_ref[...] = jnp.concatenate(
        [lanes(new_z, here), lanes(now, now), lanes(new_zu, here), jnp.zeros((5, half), F32)], axis=0
    )
    if not final:
        new_ref[pl.ds(0, 3 * rows), :] = new_s
        new_ref[pl.ds(3 * rows, 3 * rows), :] = new_su
        new_ref[pl.ds(6 * rows, rows), :] = new_z
        new_ref[pl.ds(7 * rows, rows), :] = new_zu
        out_ref[...] = advanced(now, later * more_ref[0], spec, forward, first_ref[...])


def next_step(more, note, sums, spec, mats, pulled, state, final):
    rows, half = pulled.shape
    opening = state is None
    shapes = [
        jax.ShapeDtypeStruct((8 * rows, half), F32),
        jax.ShapeDtypeStruct((rows, half), F32),
        jax.ShapeDtypeStruct((8, half), F32),
    ]
    args = [more, note, sums, spec, *mats, pulled] + ([] if opening else [state])
    return pl.pallas_call(
        functools.partial(step_kernel, opening, final),
        in_specs=[pl.BlockSpec(memory_space=pltpu.SMEM)]
        + [pl.BlockSpec(memory_space=pltpu.VMEM)] * (len(args) - 1),
        out_shape=shapes[2:] if final else shapes,
        compiler_params=params(56),
        name="next_step",
    )(*args)


def weights_of(notes):
    start = jnp.sqrt(total(notes[0], 0))
    zero = jnp.zeros_like(start)
    units = [1.0 / start, zero, zero]
    z, zu = list(units), list(units)
    phibar = start
    alpha, beta = ratios(notes[1])
    rhobar = alpha
    w = [value / alpha for value in z]
    result = [zero] * 3
    steps = len(notes) - 1
    for k in range(steps):
        rho = jnp.sqrt(rhobar * rhobar + beta * beta)
        cosine, sine = rhobar / rho, beta / rho
        phi, phibar = cosine * phibar, sine * phibar
        result = [r + phi / rho * value for r, value in zip(result, w)]
        if k < steps - 1:
            a, b, g = 1.0 / (alpha * beta), alpha / beta, beta / alpha
            zu = [(a if i == k + 1 else 0.0) - b * value for i, value in enumerate(zu)]
            z = [value - g * old for value, old in zip(zu, z)]
            alpha, beta = ratios(notes[k + 2])
            theta = sine * alpha
            rhobar = -cosine * alpha
            w = [value / alpha - theta / rho * old for value, old in zip(z, w)]
    return result


def finish_kernel(n0, n1, n2, n3, gauge_ref, q0, q1, q2, inc_ref, field_ref, out_ref, rows_ref):
    blocks, slots, width = inc_ref.shape
    count = rows_ref.shape[0]
    gauges = q0.shape[0]
    step = pl.program_id(0)

    @pl.when(step == 0)
    def _():
        e0, e1, e2 = weights_of([n0, n1, n2, n3])
        width_ = 512

        def body(i, value):
            here = pl.ds(pl.multiple_of(i * width_, width_), width_)
            mixed = q0[here, :] * e0 + q1[here, :] * e1 + q2[here, :] * e2
            gauge = lax.broadcasted_iota(jnp.int32, (count, width_), 1) + i * width_
            hot = jnp.where(gauge_ref[...] == gauge, 1.0, 0.0).astype(BF16)
            return value + pick(hot, mixed)

        rows_ref[...] = lax.fori_loop(0, gauges // width_, body, jnp.zeros(rows_ref.shape, F32))

    weights = inc_ref[...].astype(F32).astype(BF16)
    for b in range(blocks):
        here = pl.ds(b * width, width)
        rows = rows_ref[pl.ds(pl.multiple_of((step * blocks + b) * slots, slots), slots), :]
        added = sum(
            lax.dot_general(weights[b], piece, (((0,), (0,)), ((), ())), preferred_element_type=F32)
            for piece in pieces(rows, 3)
        )
        out_ref[here, :] = field_ref[here, :] + added


def finish(notes, row_gauge, gathered, incidence, field):
    blocks, slots, width = incidence.shape
    hours = field.shape[1]
    count = row_gauge.shape[0]
    step = 8
    whole = lambda shape: pl.BlockSpec(shape, lambda i: (0, 0))
    return pl.pallas_call(
        finish_kernel,
        grid=(blocks // step,),
        in_specs=[whole(n.shape) for n in notes]
        + [whole((count, 1))]
        + [whole(q.shape) for q in gathered]
        + [
            pl.BlockSpec((step, slots, width), lambda i: (i, 0, 0)),
            pl.BlockSpec((step * width, hours), lambda i: (i, 0)),
        ],
        out_specs=pl.BlockSpec((step * width, hours), lambda i: (i, 0)),
        out_shape=jax.ShapeDtypeStruct(field.shape, F32),
        scratch_shapes=[pltpu.VMEM((count, hours), F32)],
        compiler_params=params(56),
        name="finish",
    )(*notes, row_gauge.reshape(count, 1), *gathered, incidence, field)


def shifted(value, axis, by):
    devices = lax.axis_size(axis)
    pairs = [(i, i + by) for i in range(devices) if 0 <= i + by < devices]
    return lax.ppermute(value, axis, pairs)


def window(value):
    return jnp.concatenate([shifted(value, "tm", 1), value, shifted(value, "tm", -1)], axis=0)


def gathered_rows(value):
    owners = lax.axis_size("basin")
    copies = jnp.broadcast_to(value[None], (owners,) + value.shape)
    return lax.all_to_all(copies, "basin", 0, 0, tiled=False)


def over_hours(note):
    blocks = lax.axis_size("tm")
    result = note
    for by in range(1, blocks):
        result = result + lax.ppermute(note, "tm", [(i, (i + by) % blocks) for i in range(blocks)])
    return result


def shards(incidence, row_gauge, gauge_kernel, kernels, observed, first_guess):
    owners = lax.axis_size("basin")
    rows, hours = observed.shape
    gauges = rows * owners
    mats = transforms()
    spec = spectrum(gauge_kernel, kernels, mats[0])
    more = (lax.axis_index("tm") < lax.axis_size("tm") - 1).astype(F32).reshape(1)
    partial, gram = prepare(incidence, first_guess)
    all_gram = lax.all_gather(gram, "basin", axis=1, tiled=True)
    all_rows = lax.all_gather(row_gauge, "basin", axis=0, tiled=True)
    dense = table(row_gauge, partial, gauges).reshape(owners, rows, hours)
    sums = jnp.sum(lax.all_to_all(dense, "basin", 0, 0, tiled=False), axis=0)
    both = jnp.concatenate([observed, shifted(observed, "tm", -1)], axis=0)
    first = (lax.axis_index("basin") * rows).astype(jnp.int32).reshape(1)
    high, low = couple(first, all_rows, all_gram, rows, gauges)

    pulled, note = first_step(more, window(sums), both, spec, mats)
    notes, kept, state = [], [], None
    for k in range(3):
        everyone = gathered_rows(jnp.concatenate([pulled, note], axis=0))
        value = everyone[:, :rows].reshape(gauges, hours)
        notes.append(over_hours(jnp.sum(everyone[:, rows:], axis=0)))
        kept.append(value)
        around = window(mix(high, low, value))
        final = k == 2
        result = next_step(more, notes[-1], around, spec, mats, pulled, state, final)
        if final:
            (note,) = result
        else:
            state, pulled, note = result
    notes.append(over_hours(jnp.sum(gathered_rows(note), axis=0)))
    return finish(notes, row_gauge, kept, incidence, first_guess)


Z_, X_, Y_, C_ = 4, 2, 2, 2
NOTE = 8
HOURS = SPAN // 2


def device(z, x, y, c):
    return (z * X_ + x) * (Y_ * C_) + y * C_ + c


def moved(value, where):
    pairs = []
    for z, x, y, c in np.ndindex(Z_, X_, Y_, C_):
        target = where(z, x, y, c)
        if target is not None:
            pairs.append((device(z, x, y, c), device(*target)))
    return lax.ppermute(value, ("basin", "tm"), pairs)


def to_plane(z, x, y, c):
    return 2 * y + c, x, z & 1, z >> 1


def from_plane(z, x, y, c):
    return 2 * c + y, x, z >> 1, z & 1


def over_x(z, x, y, c):
    return z, 1 - x, y, c


def over_y(z, x, y, c):
    return z, x, 1 - y, c


def over_xy(z, x, y, c):
    return z, 1 - x, 1 - y, c


def over_core(z, x, y, c):
    return z, x, y, 1 - c


def z_pair(z, x, y, c):
    return z ^ 1, x, y, c


def z_middle(z, x, y, c):
    return (3 - z, x, y, c) if z in (1, 2) else None


def z_two(z, x, y, c):
    return z ^ 2, x, y, c


def z_mirror(z, x, y, c):
    return 3 - z, x, y, c


def z_next(z, x, y, c):
    return (z + 1, x, y, c) if z < 3 else None


SQUARE = (over_x, over_y, over_xy)


def split_constant(value):
    out = []
    for _ in range(3):
        piece = value.astype(jnp.bfloat16)
        out.append(piece)
        value = value - piece.astype(np.float64)
    return out


ORDERS = {2: ((0, 1), (1, 0), (0, 0)), 3: ((0, 2), (1, 1), (2, 0), (0, 1), (1, 0), (0, 0))}


def widened(mat, order):
    parts = split_constant(mat)
    return jnp.asarray(np.concatenate([parts[i] for i, _ in ORDERS[order]], axis=1))


def product(wide, value, order):
    parts = pieces(value, order)
    return dot(wide, jnp.concatenate([parts[j] for _, j in ORDERS[order]], axis=0))


def turned_transforms(order):
    half = SPAN // 2
    freq = 2.0 * np.pi * (np.arange(half) + 0.5) / SPAN
    phase = freq[:, None] * np.arange(SPAN)[None, :]
    forward = np.concatenate([np.cos(phase), -np.sin(phase)], axis=0)
    inverse = forward.T * (2.0 / SPAN)
    return [widened(mat, order) for mat in (forward, inverse[:half], inverse[half:], forward[:, :half])]


def turn(waves, spec, sign):
    half = waves.shape[0] // 2
    real, imag = waves[:half], waves[half:]
    kr, ki = spec[:half], spec[half:] * sign
    return jnp.concatenate([real * kr - imag * ki, real * ki + imag * kr], axis=0)


def plane_delayed(before, here, after, spec, forward, last, order):
    rows = here.shape[1]
    pairs = [jnp.concatenate(pair, axis=0) for pair in ((before, here), (here, after))]
    waves = product(forward, jnp.concatenate(pairs, axis=1), order)
    turned = [turn(waves[:, i * rows : (i + 1) * rows], spec, 1.0) for i in range(2)]
    out = product(last, jnp.concatenate(turned, axis=1), order)
    return out[:, :rows], out[:, rows:]


def plane_advanced(here, after, spec, forward, first, order):
    waves = product(forward, jnp.concatenate([here, after], axis=0), order)
    return product(first, turn(waves, spec, -1.0), order)


def describe_kernel(inc_ref, gauge_ref, out_ref):
    blocks, slots, width = inc_ref.shape
    tile = 8
    side = tile * slots
    weights = inc_ref[...].astype(F32).astype(BF16)
    row = lax.broadcasted_iota(jnp.int32, (side, side), 0)
    col = lax.broadcasted_iota(jnp.int32, (side, side), 1)
    same = row // slots == col // slots
    for i in range(blocks // tile):
        flat = weights[i * tile : (i + 1) * tile].reshape(side, width)
        full = lax.dot_general(flat, flat, (((1,), (1,)), ((), ())), preferred_element_type=F32)
        own = jnp.where(same, full, 0.0)
        out_ref[pl.ds(0, slots), pl.ds(i * side, side)] = jnp.sum(own.reshape(tile, slots, side), axis=0)
    out_ref[pl.ds(slots, 8), :] = jnp.broadcast_to(gauge_ref[...].astype(F32), (8, blocks * slots))


def describe(incidence, row_gauge):
    blocks, slots, _ = incidence.shape
    count = blocks * slots
    return pl.pallas_call(
        describe_kernel,
        out_shape=jax.ShapeDtypeStruct((slots + 8, count), F32),
        compiler_params=params(),
        name="describe",
        cost_estimate=SMALL,
    )(incidence, row_gauge.reshape(1, count))


def send_kernel(
    inc_hbm, field_hbm, gauge_hbm, kind_hbm, out_ref, inc_ref, field_ref, gauge_ref, kind_ref, sems, label_sems
):
    blocks, slots, width = inc_ref.shape
    chunks = sems.shape[0]
    step = blocks // chunks
    copies = []
    for i in range(chunks):
        near = pl.ds(i * step, step)
        far = pl.ds(i * step * width, step * width)
        copies.append(
            (
                pltpu.make_async_copy(inc_hbm.at[near], inc_ref.at[near], sems.at[i, 0]),
                pltpu.make_async_copy(field_hbm.at[far], field_ref.at[far], sems.at[i, 1]),
            )
        )
        for copy in copies[-1]:
            copy.start()
    labels = (
        pltpu.make_async_copy(gauge_hbm, gauge_ref, label_sems.at[0]),
        pltpu.make_async_copy(kind_hbm, kind_ref, label_sems.at[1]),
    )
    for copy in labels:
        copy.start()
    for i in range(chunks):
        for copy in copies[i]:
            copy.wait()
        parts = []
        for b in range(i * step, (i + 1) * step):
            weight = inc_ref[b].astype(F32).astype(BF16)
            value = jnp.concatenate(pieces(field_ref[pl.ds(b * width, width), :], 3)[::-1], axis=0)
            parts.append(dot(jnp.concatenate([weight] * 3, axis=1), value))
        out_ref[pl.ds(0, HOURS), pl.ds(i * step * slots, step * slots)] = jnp.transpose(
            jnp.concatenate(parts, axis=0)
        )
    for copy in labels:
        copy.wait()
    count, kinds = gauge_ref.shape[1], kind_ref.shape[1]
    kind = jnp.concatenate([kind_ref[...].astype(F32), jnp.zeros((1, count - kinds), F32)], axis=1)
    out_ref[pl.ds(HOURS, 8), :] = jnp.concatenate(
        [gauge_ref[...].astype(F32), kind, jnp.zeros((6, count), F32)], axis=0
    )


def send(incidence, field, row_gauge, gauge_kernel):
    count, rows = row_gauge.shape[0], gauge_kernel.shape[0]
    chunks = 4
    return pl.pallas_call(
        send_kernel,
        in_specs=[pl.BlockSpec(memory_space=pltpu.HBM)] * 4,
        out_shape=jax.ShapeDtypeStruct((HOURS + 8, count), F32),
        scratch_shapes=[
            pltpu.VMEM(incidence.shape, incidence.dtype),
            pltpu.VMEM(field.shape, F32),
            pltpu.VMEM((1, count), row_gauge.dtype),
            pltpu.VMEM((1, rows), gauge_kernel.dtype),
            pltpu.SemaphoreType.DMA((chunks, 2)),
            pltpu.SemaphoreType.DMA((2,)),
        ],
        compiler_params=params(60),
        name="send",
        cost_estimate=SMALL,
    )(incidence, field, row_gauge.reshape(1, count), gauge_kernel.reshape(1, rows))


def hot_rows(gauge, first, rows):
    mine = (lax.broadcasted_iota(jnp.int32, (rows, gauge.shape[1]), 0) + first).astype(F32)
    return jnp.where(gauge == mine, 1.0, 0.0).astype(BF16)


def spread_kernel(first_ref, mine_ref, other_ref, *out_refs):
    rows = out_refs[0].shape[1]
    both = jnp.concatenate([mine_ref[...], other_ref[...]], axis=1)
    stacked = jnp.concatenate(pieces(both[:HOURS], 3), axis=0)
    for m, out_ref in enumerate(out_refs):
        hot = hot_rows(both[HOURS : HOURS + 1], first_ref[m], rows)
        result = lax.dot_general(stacked, hot, (((1,), (1,)), ((), ())), preferred_element_type=F32)
        out_ref[...] = (result[2 * HOURS :] + result[HOURS : 2 * HOURS]) + result[:HOURS]


def spread(first, parcels, rows):
    return pl.pallas_call(
        spread_kernel,
        in_specs=[pl.BlockSpec(memory_space=pltpu.SMEM)] + [pl.BlockSpec(memory_space=pltpu.VMEM)] * 2,
        out_shape=[jax.ShapeDtypeStruct((HOURS, rows), F32)] * 4,
        compiler_params=params(),
        name="spread",
        cost_estimate=SMALL,
    )(first, *parcels)


def plane_couple_kernel(last, first_ref, *refs):
    if last:
        all_ref, before_ref, high_ref, low_ref, total_ref, meta_ref = refs
        total_ref[...] = before_ref[...]
    else:
        all_ref, total_ref, meta_ref = refs
        total_ref[...] = jnp.zeros_like(total_ref)
    parts, height, count = meta_ref.shape
    slots = height - 8
    cols, rows = total_ref.shape
    tile = 256
    for i in range(parts):
        meta_ref[i] = all_ref[:, i * count : (i + 1) * count]
    row = lax.broadcasted_iota(jnp.int32, (tile, tile), 0)
    col = lax.broadcasted_iota(jnp.int32, (tile, tile), 1)
    same = row // slots == col // slots

    def body(i, carry):
        gauge = meta_ref[i, slots : slots + 1, :]
        near = []
        for j in range(count // tile):
            here = slice(j * tile, (j + 1) * tile)
            block = jnp.concatenate([meta_ref[i, :slots, here]] * (tile // slots), axis=0)
            block = jnp.where(same, block, 0.0).astype(BF16)
            mine = jnp.concatenate(
                [hot_rows(gauge[:, here], first_ref[4 + h], rows // 2) for h in range(2)], axis=0
            )
            near.append(
                lax.dot_general(block, mine, (((1,), (1,)), ((), ())), preferred_element_type=F32)
            )
        near = jnp.concatenate(near, axis=0)
        high = near.astype(BF16)
        rest = near - high.astype(F32)
        hot = jnp.concatenate([hot_rows(gauge, first_ref[m], cols // 4) for m in range(4)], axis=0)
        total_ref[...] += dot(hot, high)

        @pl.when(jnp.max(jnp.abs(rest)) > 0.0)
        def _():
            total_ref[...] += dot(hot, rest.astype(BF16))

        return carry

    lax.fori_loop(0, parts, body, 0)
    if last:
        high, low = pieces(total_ref[...], 2)
        high_ref[...] = high
        low_ref[...] = low


def plane_couple(first, meta, rows, before=None):
    height, wide = meta.shape
    parts = 2 * X_
    shape = (4 * rows, 2 * rows)
    last = before is not None
    args = [first, meta] + ([before] if last else [])
    scratch = [pltpu.VMEM((parts, height, wide // parts), F32)]
    return pl.pallas_call(
        functools.partial(plane_couple_kernel, last),
        in_specs=[pl.BlockSpec(memory_space=pltpu.SMEM)]
        + [pl.BlockSpec(memory_space=pltpu.VMEM)] * (len(args) - 1),
        out_shape=[jax.ShapeDtypeStruct(shape, BF16)] * 2 if last else jax.ShapeDtypeStruct(shape, F32),
        scratch_shapes=([pltpu.VMEM(shape, F32)] if last else []) + scratch,
        compiler_params=params(),
        name="plane_couple",
        cost_estimate=pl.CostEstimate(
            flops=2 * 8 * wide * rows * rows, bytes_accessed=2_000_000, transcendentals=0
        ),
    )(*args)


def plane_mix_kernel(high_ref, low_ref, a_ref, b_ref, c_ref, d_ref, *refs):
    *extra, mine_ref, other_ref = refs
    refs = (a_ref, b_ref, c_ref, d_ref)
    height, rows = a_ref.shape
    body = pl.ds(0, HOURS)
    one, two = pieces(jnp.concatenate([ref[body, :] for ref in refs], axis=1), 2)
    both = dot(jnp.concatenate([two, one], axis=0), high_ref[...])
    result = (both[:HOURS] + dot(one, low_ref[...])) + both[HOURS:]
    mine_ref[body, :] = result[:, :rows]
    other_ref[body, :] = result[:, rows:]
    if height > HOURS:
        tail = pl.ds(HOURS, NOTE)
        note = sum(ref[tail, :] for ref in refs)
        mine_ref[tail, :] = note
        other_ref[tail, :] = note
    for ref in extra:
        other_ref[pl.ds(height, ref.shape[0]), :] = ref[...]


def plane_mix(coupling, values, extra):
    height, rows = values[0].shape
    return pl.pallas_call(
        plane_mix_kernel,
        out_shape=[
            jax.ShapeDtypeStruct((height, rows), F32),
            jax.ShapeDtypeStruct((height + sum(value.shape[0] for value in extra), rows), F32),
        ],
        compiler_params=params(),
        name="plane_mix",
        cost_estimate=SMALL,
    )(*coupling, *values, *extra)


def plane_rows_kernel(first_ref, meta_ref, meta_other_ref, a_ref, b_ref, c_ref, d_ref, *refs):
    if len(refs) > 2:
        *stack, last_ref, beside_ref, mine_ref, other_ref, stack_ref = refs
    else:
        mine_ref, other_ref = refs
    rows = a_ref.shape[1]
    value = jnp.concatenate([ref[pl.ds(0, HOURS), :] for ref in (a_ref, b_ref, c_ref, d_ref)], axis=1)
    one, two = pieces(value, 2)
    stacked = jnp.concatenate([two, one], axis=0)
    picked = []
    for ref in (meta_ref, meta_other_ref):
        gauge = ref[0:1, :]
        hot = jnp.concatenate([hot_rows(gauge, first_ref[m], rows) for m in range(4)], axis=0)
        both = dot(stacked, hot)
        picked.append(both[:HOURS] + both[HOURS:])
    mine_ref[...] = picked[0]
    count = picked[1].shape[1] // rows
    for i in range(count):
        other_ref[pl.ds(i * HOURS, HOURS), :] = picked[1][:, i * rows : (i + 1) * rows]
    if len(refs) > 2:
        top = stack_ref.shape[0] - HOURS
        for ref in stack:
            stack_ref[pl.ds(0, top), :] = ref[...]
        for i in range(count):
            here = pl.ds(i * rows, rows)
            beside = beside_ref[pl.ds(beside_ref.shape[0] - (count - i) * HOURS, HOURS), :]
            stack_ref[pl.ds(top, HOURS), here] = last_ref[:, here] + beside


def plane_rows(first, metas, values, before):
    rows = values[0].shape[1]
    slots = metas[0].shape[1]
    args = [first, *metas, *values, *before]
    shapes = [(HOURS, slots), (slots // rows * HOURS, rows)]
    if before:
        shapes.append(((len(before) - 1) * HOURS, slots))
    return pl.pallas_call(
        plane_rows_kernel,
        in_specs=[pl.BlockSpec(memory_space=pltpu.SMEM)]
        + [pl.BlockSpec(memory_space=pltpu.VMEM)] * (len(args) - 1),
        out_shape=[jax.ShapeDtypeStruct(shape, F32) for shape in shapes],
        compiler_params=params(),
        name="plane_rows",
        cost_estimate=pl.CostEstimate(flops=1_000_000_000, bytes_accessed=2_000_000, transcendentals=0),
    )(*args)


def gain(kernels):
    return jnp.max(jnp.sum(kernels, axis=1, keepdims=True), axis=0, keepdims=True)


def spectra(kind, kernels, wide):
    classes = kernels.shape[0]
    row = lax.broadcasted_iota(jnp.int32, (classes, kind.shape[1]), 0).astype(F32)
    hot = jnp.where(row == kind, 1.0, 0.0).astype(BF16)
    taps = jnp.transpose(kernels / gain(kernels))
    chosen = dot(jnp.concatenate(pieces(taps, 3)[::-1], axis=1), jnp.concatenate([hot] * 3, axis=0))
    return product(wide, chosen, 3)


def plane_spectrum_kernel(class_ref, kernels_ref, wide_ref, out_ref):
    kind = class_ref[1:2, : out_ref.shape[1]]
    out_ref[...] = spectra(kind, kernels_ref[...], wide_ref[...])


def plane_spectrum(meta, kernels, wide, rows):
    return pl.pallas_call(
        plane_spectrum_kernel,
        out_shape=jax.ShapeDtypeStruct((SPAN, rows), F32),
        compiler_params=params(),
        name="plane_spectrum",
        cost_estimate=SMALL,
    )(meta, kernels, wide)


def sides(even, pair, middle):
    return jnp.where(even, middle, pair), jnp.where(even, pair, middle)


def plane_call(kernel, name, shapes, flags, args):
    return pl.pallas_call(
        kernel,
        in_specs=[pl.BlockSpec(memory_space=pltpu.SMEM)] * len(flags)
        + [pl.BlockSpec(memory_space=pltpu.VMEM)] * len(args),
        out_shape=[jax.ShapeDtypeStruct(shape, F32) for shape in shapes],
        compiler_params=params(),
        name=name,
        cost_estimate=SMALL,
    )(*flags, *args)


def plane_first_kernel(
    flag_ref, here_ref, pair_ref, middle_ref, spec_ref, kernels_ref, forward3, last3, forward, first, out_ref
):
    spec = spec_ref[...]
    before, after = sides(flag_ref[0] > 0.5, pair_ref[...], middle_ref[...])
    here = here_ref[...]
    both = plane_delayed(before[:HOURS], here[:HOURS], after[:HOURS], spec, forward3[...], last3[...], 3)
    scale = gain(kernels_ref[...])
    now = here[HOURS:] - both[0] * scale
    later = (after[HOURS:] - both[1] * scale) * flag_ref[1]
    out_ref[...] = plane_advanced(now, later, spec, forward[...], first[...], 2)


def plane_delay_kernel(flag_ref, here_ref, pair_ref, middle_ref, spec_ref, forward, last, out_ref):
    body = pl.ds(0, HOURS)
    before, after = sides(flag_ref[0] > 0.5, pair_ref[body, :], middle_ref[body, :])
    out = plane_delayed(before, here_ref[body, :], after, spec_ref[...], forward[...], last[...], 2)
    for i in range(2):
        out_ref[pl.ds(i * HOURS, HOURS), :] = out[i]


def write_note(ref, rows):
    tail = [jnp.zeros((NOTE - len(rows), ref.shape[1]), F32)]
    ref[pl.ds(HOURS, NOTE), :] = jnp.concatenate(rows + tail, axis=0)


def plane_open_kernel(
    flag_ref, here_ref, pair_ref, middle_ref, pulled_ref, spec_ref, forward, first, last, out_ref, delayed_ref
):
    here = here_ref[...]
    spec = spec_ref[...]
    before, after = sides(flag_ref[0] > 0.5, pair_ref[...], middle_ref[...])
    now, later = plane_delayed(before, here, after, spec, forward[...], last[...], 2)
    out_ref[pl.ds(0, HOURS), :] = plane_advanced(now, later * flag_ref[1], spec, forward[...], first[...], 2)
    write_note(out_ref, [lanes(pulled_ref[...], here), lanes(now, now)])
    delayed_ref[pl.ds(0, HOURS), :] = now
    delayed_ref[pl.ds(HOURS, HOURS), :] = later


def plane_step_kernel(
    flag_ref,
    here_ref,
    pair_ref,
    two_ref,
    mirror_ref,
    pulled_ref,
    delayed_ref,
    old_z_ref,
    old_s_ref,
    old_delayed_ref,
    spec_ref,
    forward,
    first,
    total_ref,
    out_ref,
    kept_ref,
):
    tail, body = pl.ds(HOURS, NOTE), pl.ds(0, HOURS)
    total_ref[...] = (here_ref[tail, :] + pair_ref[tail, :]) + (two_ref[...] + mirror_ref[...])
    inverse = total(total_ref, 0) / total(total_ref, 1)
    z = pulled_ref[body, :] * inverse - old_z_ref[...]
    s = here_ref[body, :] * inverse - old_s_ref[...]
    both = delayed_ref[...] * inverse - old_delayed_ref[...]
    now, later = both[:HOURS], both[HOURS:]
    following = plane_advanced(now, later * flag_ref[1], spec_ref[...], forward[...], first[...], 2)
    out_ref[body, :] = following * inverse
    write_note(out_ref, [lanes(z, s), lanes(now, now)])
    for i, value in enumerate((z, s, now)):
        kept_ref[pl.ds(i * HOURS, HOURS), :] = value


def plane_close_kernel(
    here_ref,
    before_ref,
    pulled_ref,
    kept_ref,
    old_z_ref,
    old_s_ref,
    old_delayed_ref,
    open_ref,
    spec_ref,
    kernels_ref,
    forward,
    last,
    out_ref,
):
    body = pl.ds(0, HOURS)
    here, raw = here_ref[body, :], pulled_ref[body, :]
    waves = product(forward[...], jnp.concatenate([before_ref[body, :], here], axis=0), 2)
    now = product(last[...], turn(waves, spec_ref[...], 1.0), 2)
    z, s, delayed = (kept_ref[pl.ds(i * HOURS, HOURS), :] for i in range(3))
    note = [pulled_ref[HOURS + i : HOURS + i + 1, :] for i in range(2)]
    for left in (raw, z, old_z_ref[...]):
        note += [lanes(left, right) for right in (here, s, old_s_ref[...])]
    parts = (now, delayed, old_delayed_ref[body, :])
    for i in range(3):
        note += [lanes(parts[i], parts[j]) for j in range(i, 3)]
    known = [total(open_ref, 0), total(open_ref, 1), gain(kernels_ref[...])]
    note = [jnp.sum(jnp.concatenate(note, axis=0), axis=1, keepdims=True)]
    note += [value / out_ref.shape[0] for value in known]
    count = sum(value.shape[0] for value in note)
    note = jnp.concatenate(note + [jnp.zeros((24 - count, 1), F32)], axis=0)
    shape = (24, out_ref.shape[1])
    row, col = (lax.broadcasted_iota(jnp.int32, shape, i) for i in range(2))
    note = jnp.sum(jnp.where(row == col, jnp.broadcast_to(note, shape), 0.0), axis=0, keepdims=True)
    out_ref[...] = jnp.broadcast_to(note, out_ref.shape)


def plane_weights(close):
    entry = lambda i: close[:, i : i + 1]
    n1, t1, scale = (entry(17 + i) for i in range(3))
    n2, t2 = entry(0), entry(1)
    a1 = t1 / n1
    a2, r2 = (t2 / n2) / a1, n2 / n1
    plain = (1.0, -a2, -r2)
    n3 = sum(plain[i] * plain[j] * entry(2 + 3 * i + j) for i in range(3) for j in range(3))
    pairs = [(i, j) for i in range(3) for j in range(i, 3)]
    t3 = sum(
        plain[i] * plain[j] * entry(11 + n) * (1.0 if i == j else 2.0) for n, (i, j) in enumerate(pairs)
    )
    a3, r3 = (t3 / n3) / a1, n3 / n2
    unit = 1.0 / (a1 * scale)
    c3 = unit / (a3 * (a2 - r2) - r3)
    c2 = -a3 * c3
    c1 = unit - r2 * c2
    step = c2 - c3 * a2
    return c1 - step - c3 * r2, step / a1, c3


def plane_combine_kernel(close_ref, stack_ref, mine_ref, beside_ref, out_ref):
    rows = beside_ref.shape[1]
    close = jnp.sum(close_ref[...], axis=0, keepdims=True)
    e0, e1, e2 = plane_weights(close)
    for i in range(out_ref.shape[0] // rows):
        here = pl.ds(i * rows, rows)
        last = mine_ref[:, here] + beside_ref[pl.ds(i * HOURS, HOURS), :]
        value = stack_ref[pl.ds(0, HOURS), here] * e0 + stack_ref[pl.ds(HOURS, HOURS), here] * e1 + last * e2
        out_ref[here, :] = jnp.transpose(value)


def plane_finish_kernel(rows_ref, inc_ref, field_ref, out_ref):
    blocks, slots, width = inc_ref.shape
    weights = inc_ref[...].astype(F32).astype(BF16)
    for b in range(blocks):
        here = pl.ds(b * width, width)
        rows = jnp.concatenate(pieces(rows_ref[pl.ds(b * slots, slots), :], 2), axis=0)
        twice = jnp.concatenate([weights[b]] * 2, axis=0)
        added = lax.dot_general(twice, rows, (((0,), (0,)), ((), ())), preferred_element_type=F32)
        out_ref[here, :] = field_ref[here, :] + added


def plane_finish(rows, incidence, field):
    blocks, slots, width = incidence.shape
    hours = field.shape[1]
    step = 16
    return pl.pallas_call(
        plane_finish_kernel,
        grid=(blocks // step,),
        in_specs=[
            pl.BlockSpec((step * slots, hours), lambda i: (i, 0)),
            pl.BlockSpec((step, slots, width), lambda i: (i, 0, 0)),
            pl.BlockSpec((step * width, hours), lambda i: (i, 0)),
        ],
        out_specs=pl.BlockSpec((step * width, hours), lambda i: (i, 0)),
        out_shape=jax.ShapeDtypeStruct(field.shape, F32),
        compiler_params=params(),
        name="plane_finish",
    )(rows, incidence, field)


def plane_shards(incidence, row_gauge, gauge_kernel, kernels, observed, first_guess):
    rows, hours = observed.shape
    basin, tm = lax.axis_index("basin"), lax.axis_index("tm")
    z, x, y, c = basin // X_, basin % X_, tm // C_, tm % C_
    place = 2 * y + x
    first = jnp.stack([4 * c + (place ^ m) for m in range(4)] + [4 * c + place, 4 * (1 - c) + place])
    first = (first * rows).astype(jnp.int32)
    flags = jnp.stack([1 - z % 2, (z < Z_ - 1).astype(z.dtype), (z > 0).astype(z.dtype)]).astype(F32)
    forward, inverse_first, inverse_last, _ = turned_transforms(2)
    forward3, _, inverse_last3, short3 = turned_transforms(3)
    block, noted = (hours, rows), (hours + NOTE, rows)

    seen = moved(observed, to_plane)
    parcel = send(incidence, first_guess, row_gauge, gauge_kernel)
    parcel, near = lax.optimization_barrier((parcel, incidence))
    parcel = moved(parcel, to_plane)
    near, seen = lax.optimization_barrier((near, seen))
    meta = describe(near, row_gauge)
    meta = jnp.concatenate([meta, moved(meta, over_x)], axis=1)
    half = meta.shape[1] // 2
    share = jnp.where(c == 0, meta[:, :half], meta[:, half:])
    close = moved(share, z_pair)
    parcel, seen = lax.optimization_barrier((parcel, seen))
    parcels = [parcel, moved(parcel, over_core)]
    spec = plane_spectrum(parcel[hours:], kernels, short3, rows)
    parcels[1], seen, close, spec = lax.optimization_barrier((parcels[1], seen, close, spec))
    far = moved(jnp.concatenate([share, close], axis=1), z_two)
    dense = spread(first, parcels, rows)
    metas = [value[hours:] for value in parcels]
    sums = dense[0] + sum(moved(value, where) for value, where in zip(dense[1:], SQUARE))
    sums, far = lax.optimization_barrier((sums, far))
    held = jnp.concatenate([close, far], axis=1)
    around = [
        jnp.concatenate([meta, held[:, : 2 * half]], axis=1),
        jnp.concatenate([held[:, 2 * half :], moved(held, over_core)], axis=1),
    ]
    sums = jnp.concatenate([sums, jnp.transpose(seen)], axis=0)
    sums = [sums, moved(sums, z_pair), moved(sums, z_middle)]
    coupled = plane_couple(first, around[0], rows)
    coupled, sums = lax.optimization_barrier((coupled, sums))
    coupling = plane_couple(first, around[1], rows, coupled)
    (pulled0,) = plane_call(
        plane_first_kernel,
        "plane_first",
        [block],
        [flags],
        [*sums, spec, kernels, forward3, inverse_last3, forward, inverse_first],
    )

    def mixing(pulled, extra):
        values = [pulled] + [moved(pulled, where) for where in SQUARE]
        mine, other = plane_mix(coupling, values, extra)
        beside = moved(other, over_core)
        return values, mine + beside[: pulled.shape[0]], beside

    values, mixed0, _ = mixing(pulled0, [])
    picked, theirs = plane_rows(first, metas, values, [])
    sums = [mixed0, moved(mixed0, z_pair), moved(mixed0, z_middle)]
    pulled1, delayed0 = plane_call(
        plane_open_kernel,
        "plane_open",
        [noted, (2 * hours, rows)],
        [flags],
        [*sums, pulled0, spec, forward, inverse_first, inverse_last],
    )

    values, mixed1, beside = mixing(pulled1, [theirs])
    picked, theirs, stack = plane_rows(first, metas, values, [picked, beside])
    sums = [mixed1, moved(mixed1, z_pair), moved(mixed1, z_middle)]
    two, mirror = moved(mixed1[hours:], z_two), moved(mixed1[hours:], z_mirror)
    (delayed1,) = plane_call(
        plane_delay_kernel, "plane_delay", [(2 * hours, rows)], [flags], [*sums, spec, forward, inverse_last]
    )
    open_note, pulled2, kept = plane_call(
        plane_step_kernel,
        "plane_step",
        [(NOTE, rows), noted, (3 * hours, rows)],
        [flags],
        [*sums[:2], two, mirror, pulled1, delayed1, pulled0, mixed0, delayed0, spec, forward, inverse_first],
    )

    values, mixed2, beside = mixing(pulled2, [theirs])
    picked, theirs, stack = plane_rows(first, metas, values, [stack, picked, beside])
    (note,) = plane_call(
        plane_close_kernel,
        "plane_close",
        [(Z_ * X_ * Y_ * C_, rows // 2)],
        [],
        [
            *(mixed2, moved(mixed2, z_next), pulled2, kept, pulled0, mixed0, delayed0),
            *(open_note, spec, kernels, forward, inverse_last),
        ],
    )
    close_note = lax.all_to_all(note, ("basin", "tm"), 0, 0, tiled=True)
    (answer,) = plane_call(
        plane_combine_kernel,
        "plane_combine",
        [(parcel.shape[1], hours)],
        [],
        [close_note, stack, picked, moved(theirs, over_core)],
    )
    return plane_finish(moved(answer, from_plane), incidence, first_guess)


def solution(mesh):
    planes = dict(mesh.shape) == {"basin": Z_ * X_, "tm": Y_ * C_}
    in_specs = (
        P("basin", None, None),
        P("basin"),
        P("basin"),
        P(),
        P("basin", "tm"),
        P("basin", "tm"),
    )
    return jax.shard_map(
        plane_shards if planes else shards, mesh=mesh, in_specs=in_specs, out_specs=P("basin", "tm"), check_vma=False
    )
```

```python
import functools

import jax
import jax.numpy as jnp
import numpy as np
from jax import lax
from jax.experimental import pallas as pl
from jax.experimental.pallas import tpu as pltpu
from jax.sharding import PartitionSpec as P

F32 = jnp.float32
BF16 = jnp.bfloat16
HIGH = lax.Precision.HIGHEST
SPAN = 256
MIB = 1024 * 1024


SMALL = pl.CostEstimate(flops=1, bytes_accessed=1, transcendentals=0)


def params(mib=16):
    return pltpu.CompilerParams(vmem_limit_bytes=mib * MIB)


def transforms():
    half = SPAN // 2
    freq = 2.0 * np.pi * (np.arange(half) + 0.5) / SPAN
    phase = np.arange(SPAN)[:, None] * freq[None, :]
    forward = np.concatenate([np.cos(phase), -np.sin(phase)], axis=1)
    inverse = forward.T * (2.0 / SPAN)
    return (
        jnp.asarray(forward, F32),
        jnp.asarray(inverse[:, :half], F32),
        jnp.asarray(inverse[:, half:], F32),
    )


def dot(a, b):
    return jnp.dot(a, b, preferred_element_type=F32)


def exact(a, b):
    return jnp.dot(a, b, precision=HIGH, preferred_element_type=F32)


def pieces(value, count):
    out = []
    for _ in range(count):
        piece = value.astype(BF16)
        out.append(piece)
        value = value - piece.astype(F32)
    return out


def pick(hot, value):
    return sum(dot(hot, piece) for piece in pieces(value, 3))


def prepare_kernel(inc_ref, field_ref, partial_ref, gram_ref):
    blocks, slots, width = inc_ref.shape
    rows = blocks * slots
    weights = inc_ref[...].astype(F32).astype(BF16)
    for b in range(blocks):
        value = field_ref[pl.ds(b * width, width), :]
        partial_ref[pl.ds(b * slots, slots), :] = pick(weights[b], value)
    flat = weights.reshape(rows, width)
    full = lax.dot_general(flat, flat, (((1,), (1,)), ((), ())), preferred_element_type=F32)
    row = lax.broadcasted_iota(jnp.int32, (rows, rows), 0)
    col = lax.broadcasted_iota(jnp.int32, (rows, rows), 1)
    own = jnp.where(row // slots == col // slots, full, 0.0)
    gram_ref[...] = jnp.sum(own.reshape(blocks, slots, rows), axis=0)


def prepare(incidence, field):
    blocks, slots, width = incidence.shape
    hours = field.shape[1]
    step = 8
    return pl.pallas_call(
        prepare_kernel,
        grid=(blocks // step,),
        in_specs=[
            pl.BlockSpec((step, slots, width), lambda i: (i, 0, 0)),
            pl.BlockSpec((step * width, hours), lambda i: (i, 0)),
        ],
        out_specs=[
            pl.BlockSpec((step * slots, hours), lambda i: (i, 0)),
            pl.BlockSpec((slots, step * slots), lambda i: (0, i)),
        ],
        out_shape=[
            jax.ShapeDtypeStruct((blocks * slots, hours), F32),
            jax.ShapeDtypeStruct((slots, blocks * slots), F32),
        ],
        compiler_params=params(56),
        name="prepare",
    )(incidence, field)


def table_kernel(gauge_ref, partial_ref, out_ref):
    slots = partial_ref.shape[0]
    rows = out_ref.shape[0]
    first = pl.program_id(0) * rows
    gauge = lax.broadcasted_iota(jnp.int32, (rows, slots), 0) + first
    hot = jnp.where(gauge_ref[...] == gauge, 1.0, 0.0).astype(BF16)
    out_ref[...] = pick(hot, partial_ref[...])


def table(row_gauge, partial, gauges):
    slots, hours = partial.shape
    step = 256
    return pl.pallas_call(
        table_kernel,
        grid=(gauges // step,),
        in_specs=[
            pl.BlockSpec((1, slots), lambda i: (0, 0)),
            pl.BlockSpec((slots, hours), lambda i: (0, 0)),
        ],
        out_specs=pl.BlockSpec((step, hours), lambda i: (i, 0)),
        out_shape=jax.ShapeDtypeStruct((gauges, hours), F32),
        compiler_params=params(56),
        name="table",
    )(row_gauge.reshape(1, slots), partial)


def couple_kernel(first_ref, lane_ref, sub_ref, gram_ref, high_ref, low_ref, near_ref):
    slots = gram_ref.shape[0]
    count = lane_ref.shape[1]
    rows, cols = high_ref.shape
    tile = 256
    first = first_ref[0]

    @pl.when(pl.program_id(0) == 0)
    def _():
        row = lax.broadcasted_iota(jnp.int32, (tile, tile), 0)
        col = lax.broadcasted_iota(jnp.int32, (tile, tile), 1)
        same = row // slots == col // slots
        mine = lax.broadcasted_iota(jnp.int32, (rows, tile), 0) + first

        def body(i, carry):
            here = pl.ds(pl.multiple_of(i * tile, tile), tile)
            block = jnp.concatenate([gram_ref[:, here]] * (tile // slots), axis=0)
            block = jnp.where(same, block, 0.0).astype(BF16)
            hot = jnp.where(lane_ref[:, here] == mine, 1.0, 0.0).astype(BF16)
            near_ref[:, here] = dot(hot, block)
            return carry

        lax.fori_loop(0, count // tile, body, 0)

    def chunk(i, total):
        here = pl.ds(pl.multiple_of(i * 1024, 1024), 1024)
        gauge = lax.broadcasted_iota(jnp.int32, (1024, cols), 1) + pl.program_id(0) * cols
        hot = jnp.where(sub_ref[here, :] == gauge, 1.0, 0.0).astype(BF16)
        near = near_ref[:, here]
        high = near.astype(BF16)
        low = (near - high.astype(F32)).astype(BF16)
        return total + dot(high, hot) + dot(low, hot)

    total = lax.fori_loop(0, count // 1024, chunk, jnp.zeros((rows, cols), F32))
    high, low = pieces(total, 2)
    high_ref[...] = high
    low_ref[...] = low


def couple(first, row_gauge, gram, rows, gauges):
    count = row_gauge.shape[0]
    step = 256
    return pl.pallas_call(
        couple_kernel,
        grid=(gauges // step,),
        in_specs=[
            pl.BlockSpec(memory_space=pltpu.SMEM),
            pl.BlockSpec((1, count), lambda i: (0, 0)),
            pl.BlockSpec((count, 1), lambda i: (0, 0)),
            pl.BlockSpec(gram.shape, lambda i: (0, 0)),
        ],
        out_specs=[pl.BlockSpec((rows, step), lambda i: (0, i))] * 2,
        out_shape=[jax.ShapeDtypeStruct((rows, gauges), BF16)] * 2,
        scratch_shapes=[pltpu.VMEM((rows, count), F32)],
        compiler_params=params(56),
        name="couple",
    )(first, row_gauge.reshape(1, count), row_gauge.reshape(count, 1), gram)


def mix_kernel(high_ref, low_ref, value_ref, out_ref):
    high = high_ref[...]
    low = low_ref[...]
    one, two, three = pieces(value_ref[...], 3)
    out_ref[...] = (dot(high, three) + dot(low, two)) + (dot(high, two) + dot(low, one)) + dot(high, one)


def mix(high, low, value):
    return pl.pallas_call(
        mix_kernel,
        out_shape=jax.ShapeDtypeStruct((high.shape[0], value.shape[1]), F32),
        compiler_params=params(56),
        name="mix",
    )(high, low, value)


def spectrum_kernel(class_ref, kernels_ref, forward_ref, out_ref):
    rows = class_ref.shape[0]
    classes, taps = kernels_ref.shape
    kind = lax.broadcasted_iota(jnp.int32, (rows, classes), 1)
    hot = jnp.where(class_ref[...] == kind, 1.0, 0.0)
    out_ref[...] = exact(exact(hot, kernels_ref[...]), forward_ref[pl.ds(0, taps), :])


def spectrum(gauge_kernel, kernels, forward):
    rows = gauge_kernel.shape[0]
    return pl.pallas_call(
        spectrum_kernel,
        out_shape=jax.ShapeDtypeStruct((rows, SPAN), F32),
        compiler_params=params(56),
        name="spectrum",
    )(gauge_kernel.reshape(rows, 1), kernels, forward)


def delayed(before, here, after, spec, forward, inverse_last):
    rows, half = here.shape
    stacked = jnp.concatenate(
        [jnp.concatenate([before, here], axis=1), jnp.concatenate([here, after], axis=1)], axis=0
    )
    waves = exact(stacked, forward)
    real, imag = waves[:, :half], waves[:, half:]
    kr = jnp.concatenate([spec[:, :half]] * 2, axis=0)
    ki = jnp.concatenate([spec[:, half:]] * 2, axis=0)
    turned = jnp.concatenate([real * kr - imag * ki, real * ki + imag * kr], axis=1)
    out = exact(turned, inverse_last)
    return out[:rows], out[rows:]


def advanced(here, after, spec, forward, inverse_first):
    half = here.shape[1]
    waves = exact(jnp.concatenate([here, after], axis=1), forward)
    real, imag = waves[:, :half], waves[:, half:]
    kr, ki = spec[:, :half], spec[:, half:]
    turned = jnp.concatenate([real * kr + imag * ki, imag * kr - real * ki], axis=1)
    return exact(turned, inverse_first)


def lanes(a, b):
    return jnp.sum(a * b, axis=0, keepdims=True)


def total(ref, row):
    return jnp.sum(ref[row : row + 1, :], axis=1, keepdims=True)


def ratios(ref):
    square = total(ref, 0)
    alpha = jnp.sqrt(square)
    beta = jnp.sqrt(jnp.maximum(total(ref, 1) / square - 2.0 * total(ref, 2) + square, 0.0))
    return alpha, beta


def first_kernel(
    more_ref, sums_ref, observed_ref, spec_ref, forward_ref, first_ref, last_ref, out_ref, note_ref
):
    rows, half = observed_ref.shape[0] // 2, observed_ref.shape[1]
    spec, forward = spec_ref[...], forward_ref[...]
    before, here, after = (sums_ref[pl.ds(i * rows, rows), :] for i in range(3))
    now, later = delayed(before, here, after, spec, forward, last_ref[...])
    start = observed_ref[pl.ds(0, rows), :] - now
    start_later = (observed_ref[pl.ds(rows, rows), :] - later) * more_ref[0]
    out_ref[...] = advanced(start, start_later, spec, forward, first_ref[...])
    note_ref[...] = jnp.concatenate([lanes(start, start), jnp.zeros((7, half), F32)], axis=0)


def first_step(more, sums, observed, spec, mats):
    rows, half = spec.shape[0], observed.shape[1]
    return pl.pallas_call(
        first_kernel,
        in_specs=[pl.BlockSpec(memory_space=pltpu.SMEM)] + [pl.BlockSpec(memory_space=pltpu.VMEM)] * 6,
        out_shape=[jax.ShapeDtypeStruct((rows, half), F32), jax.ShapeDtypeStruct((8, half), F32)],
        compiler_params=params(56),
        name="first_step",
    )(more, sums, observed, spec, *mats)


def step_kernel(
    opening,
    final,
    more_ref,
    note_ref,
    sums_ref,
    spec_ref,
    forward_ref,
    first_ref,
    last_ref,
    pulled_ref,
    *refs,
):
    if opening:
        state_ref = None
    else:
        state_ref, *refs = refs
    if final:
        (out_note_ref,) = refs
    else:
        new_ref, out_ref, out_note_ref = refs
    rows, half = pulled_ref.shape
    spec, forward = spec_ref[...], forward_ref[...]
    if opening:
        scale = 1.0 / jnp.sqrt(total(note_ref, 0))
        along = sums_ref[...] * scale
        new_s, new_su = along, along
        new_zu = pulled_ref[...] * scale
        new_z = new_zu
    else:
        alpha, beta = ratios(note_ref)
        a, b, g = 1.0 / (alpha * beta), alpha / beta, beta / alpha
        wide = pl.ds(0, 3 * rows), pl.ds(3 * rows, 3 * rows)
        new_su = sums_ref[...] * a - state_ref[wide[1], :] * b
        new_s = new_su - state_ref[wide[0], :] * g
        new_zu = pulled_ref[...] * a - state_ref[pl.ds(7 * rows, rows), :] * b
        new_z = new_zu - state_ref[pl.ds(6 * rows, rows), :] * g
    before, here, after = (new_s[i * rows : (i + 1) * rows] for i in range(3))
    now, later = delayed(before, here, after, spec, forward, last_ref[...])
    out_note_ref[...] = jnp.concatenate(
        [lanes(new_z, here), lanes(now, now), lanes(new_zu, here), jnp.zeros((5, half), F32)], axis=0
    )
    if not final:
        new_ref[pl.ds(0, 3 * rows), :] = new_s
        new_ref[pl.ds(3 * rows, 3 * rows), :] = new_su
        new_ref[pl.ds(6 * rows, rows), :] = new_z
        new_ref[pl.ds(7 * rows, rows), :] = new_zu
        out_ref[...] = advanced(now, later * more_ref[0], spec, forward, first_ref[...])


def next_step(more, note, sums, spec, mats, pulled, state, final):
    rows, half = pulled.shape
    opening = state is None
    shapes = [
        jax.ShapeDtypeStruct((8 * rows, half), F32),
        jax.ShapeDtypeStruct((rows, half), F32),
        jax.ShapeDtypeStruct((8, half), F32),
    ]
    args = [more, note, sums, spec, *mats, pulled] + ([] if opening else [state])
    return pl.pallas_call(
        functools.partial(step_kernel, opening, final),
        in_specs=[pl.BlockSpec(memory_space=pltpu.SMEM)]
        + [pl.BlockSpec(memory_space=pltpu.VMEM)] * (len(args) - 1),
        out_shape=shapes[2:] if final else shapes,
        compiler_params=params(56),
        name="next_step",
    )(*args)


def weights_of(notes):
    start = jnp.sqrt(total(notes[0], 0))
    zero = jnp.zeros_like(start)
    units = [1.0 / start, zero, zero]
    z, zu = list(units), list(units)
    phibar = start
    alpha, beta = ratios(notes[1])
    rhobar = alpha
    w = [value / alpha for value in z]
    result = [zero] * 3
    steps = len(notes) - 1
    for k in range(steps):
        rho = jnp.sqrt(rhobar * rhobar + beta * beta)
        cosine, sine = rhobar / rho, beta / rho
        phi, phibar = cosine * phibar, sine * phibar
        result = [r + phi / rho * value for r, value in zip(result, w)]
        if k < steps - 1:
            a, b, g = 1.0 / (alpha * beta), alpha / beta, beta / alpha
            zu = [(a if i == k + 1 else 0.0) - b * value for i, value in enumerate(zu)]
            z = [value - g * old for value, old in zip(zu, z)]
            alpha, beta = ratios(notes[k + 2])
            theta = sine * alpha
            rhobar = -cosine * alpha
            w = [value / alpha - theta / rho * old for value, old in zip(z, w)]
    return result


def finish_kernel(n0, n1, n2, n3, gauge_ref, q0, q1, q2, inc_ref, field_ref, out_ref, rows_ref):
    blocks, slots, width = inc_ref.shape
    count = rows_ref.shape[0]
    gauges = q0.shape[0]
    step = pl.program_id(0)

    @pl.when(step == 0)
    def _():
        e0, e1, e2 = weights_of([n0, n1, n2, n3])
        width_ = 512

        def body(i, value):
            here = pl.ds(pl.multiple_of(i * width_, width_), width_)
            mixed = q0[here, :] * e0 + q1[here, :] * e1 + q2[here, :] * e2
            gauge = lax.broadcasted_iota(jnp.int32, (count, width_), 1) + i * width_
            hot = jnp.where(gauge_ref[...] == gauge, 1.0, 0.0).astype(BF16)
            return value + pick(hot, mixed)

        rows_ref[...] = lax.fori_loop(0, gauges // width_, body, jnp.zeros(rows_ref.shape, F32))

    weights = inc_ref[...].astype(F32).astype(BF16)
    for b in range(blocks):
        here = pl.ds(b * width, width)
        rows = rows_ref[pl.ds(pl.multiple_of((step * blocks + b) * slots, slots), slots), :]
        added = sum(
            lax.dot_general(weights[b], piece, (((0,), (0,)), ((), ())), preferred_element_type=F32)
            for piece in pieces(rows, 3)
        )
        out_ref[here, :] = field_ref[here, :] + added


def finish(notes, row_gauge, gathered, incidence, field):
    blocks, slots, width = incidence.shape
    hours = field.shape[1]
    count = row_gauge.shape[0]
    step = 8
    whole = lambda shape: pl.BlockSpec(shape, lambda i: (0, 0))
    return pl.pallas_call(
        finish_kernel,
        grid=(blocks // step,),
        in_specs=[whole(n.shape) for n in notes]
        + [whole((count, 1))]
        + [whole(q.shape) for q in gathered]
        + [
            pl.BlockSpec((step, slots, width), lambda i: (i, 0, 0)),
            pl.BlockSpec((step * width, hours), lambda i: (i, 0)),
        ],
        out_specs=pl.BlockSpec((step * width, hours), lambda i: (i, 0)),
        out_shape=jax.ShapeDtypeStruct(field.shape, F32),
        scratch_shapes=[pltpu.VMEM((count, hours), F32)],
        compiler_params=params(56),
        name="finish",
    )(*notes, row_gauge.reshape(count, 1), *gathered, incidence, field)


def shifted(value, axis, by):
    devices = lax.axis_size(axis)
    pairs = [(i, i + by) for i in range(devices) if 0 <= i + by < devices]
    return lax.ppermute(value, axis, pairs)


def window(value):
    return jnp.concatenate([shifted(value, "tm", 1), value, shifted(value, "tm", -1)], axis=0)


def gathered_rows(value):
    owners = lax.axis_size("basin")
    copies = jnp.broadcast_to(value[None], (owners,) + value.shape)
    return lax.all_to_all(copies, "basin", 0, 0, tiled=False)


def over_hours(note):
    blocks = lax.axis_size("tm")
    result = note
    for by in range(1, blocks):
        result = result + lax.ppermute(note, "tm", [(i, (i + by) % blocks) for i in range(blocks)])
    return result


def shards(incidence, row_gauge, gauge_kernel, kernels, observed, first_guess):
    owners = lax.axis_size("basin")
    rows, hours = observed.shape
    gauges = rows * owners
    mats = transforms()
    spec = spectrum(gauge_kernel, kernels, mats[0])
    more = (lax.axis_index("tm") < lax.axis_size("tm") - 1).astype(F32).reshape(1)
    partial, gram = prepare(incidence, first_guess)
    all_gram = lax.all_gather(gram, "basin", axis=1, tiled=True)
    all_rows = lax.all_gather(row_gauge, "basin", axis=0, tiled=True)
    dense = table(row_gauge, partial, gauges).reshape(owners, rows, hours)
    sums = jnp.sum(lax.all_to_all(dense, "basin", 0, 0, tiled=False), axis=0)
    both = jnp.concatenate([observed, shifted(observed, "tm", -1)], axis=0)
    first = (lax.axis_index("basin") * rows).astype(jnp.int32).reshape(1)
    high, low = couple(first, all_rows, all_gram, rows, gauges)

    pulled, note = first_step(more, window(sums), both, spec, mats)
    notes, kept, state = [], [], None
    for k in range(3):
        everyone = gathered_rows(jnp.concatenate([pulled, note], axis=0))
        value = everyone[:, :rows].reshape(gauges, hours)
        notes.append(over_hours(jnp.sum(everyone[:, rows:], axis=0)))
        kept.append(value)
        around = window(mix(high, low, value))
        final = k == 2
        result = next_step(more, notes[-1], around, spec, mats, pulled, state, final)
        if final:
            (note,) = result
        else:
            state, pulled, note = result
    notes.append(over_hours(jnp.sum(gathered_rows(note), axis=0)))
    return finish(notes, row_gauge, kept, incidence, first_guess)


Z_, X_, Y_, C_ = 4, 2, 2, 2
NOTE = 8
HOURS = SPAN // 2


def device(z, x, y, c):
    return (z * X_ + x) * (Y_ * C_) + y * C_ + c


def moved(value, where):
    pairs = []
    for z, x, y, c in np.ndindex(Z_, X_, Y_, C_):
        target = where(z, x, y, c)
        if target is not None:
            pairs.append((device(z, x, y, c), device(*target)))
    return lax.ppermute(value, ("basin", "tm"), pairs)


def to_plane(z, x, y, c):
    return 2 * y + c, x, z & 1, z >> 1


def from_plane(z, x, y, c):
    return 2 * c + y, x, z >> 1, z & 1


def over_x(z, x, y, c):
    return z, 1 - x, y, c


def over_y(z, x, y, c):
    return z, x, 1 - y, c


def over_xy(z, x, y, c):
    return z, 1 - x, 1 - y, c


def over_core(z, x, y, c):
    return z, x, y, 1 - c


def z_pair(z, x, y, c):
    return z ^ 1, x, y, c


def z_middle(z, x, y, c):
    return (3 - z, x, y, c) if z in (1, 2) else None


def z_two(z, x, y, c):
    return z ^ 2, x, y, c


def z_mirror(z, x, y, c):
    return 3 - z, x, y, c


def z_next(z, x, y, c):
    return (z + 1, x, y, c) if z < 3 else None


SQUARE = (over_x, over_y, over_xy)


def split_constant(value):
    out = []
    for _ in range(3):
        piece = value.astype(jnp.bfloat16)
        out.append(piece)
        value = value - piece.astype(np.float64)
    return out


ORDERS = {2: ((0, 1), (1, 0), (0, 0)), 3: ((0, 2), (1, 1), (2, 0), (0, 1), (1, 0), (0, 0))}


def widened(mat, order):
    parts = split_constant(mat)
    return jnp.asarray(np.concatenate([parts[i] for i, _ in ORDERS[order]], axis=1))


def product(wide, value, order):
    parts = pieces(value, order)
    return dot(wide, jnp.concatenate([parts[j] for _, j in ORDERS[order]], axis=0))


def turned_transforms(order):
    half = SPAN // 2
    freq = 2.0 * np.pi * (np.arange(half) + 0.5) / SPAN
    phase = freq[:, None] * np.arange(SPAN)[None, :]
    forward = np.concatenate([np.cos(phase), -np.sin(phase)], axis=0)
    inverse = forward.T * (2.0 / SPAN)
    return [widened(mat, order) for mat in (forward, inverse[:half], inverse[half:], forward[:, :half])]


def turn(waves, spec, sign):
    half = waves.shape[0] // 2
    real, imag = waves[:half], waves[half:]
    kr, ki = spec[:half], spec[half:] * sign
    return jnp.concatenate([real * kr - imag * ki, real * ki + imag * kr], axis=0)


def plane_delayed(before, here, after, spec, forward, last, order):
    rows = here.shape[1]
    pairs = [jnp.concatenate(pair, axis=0) for pair in ((before, here), (here, after))]
    waves = product(forward, jnp.concatenate(pairs, axis=1), order)
    turned = [turn(waves[:, i * rows : (i + 1) * rows], spec, 1.0) for i in range(2)]
    out = product(last, jnp.concatenate(turned, axis=1), order)
    return out[:, :rows], out[:, rows:]


def plane_advanced(here, after, spec, forward, first, order):
    waves = product(forward, jnp.concatenate([here, after], axis=0), order)
    return product(first, turn(waves, spec, -1.0), order)


def describe_kernel(inc_ref, gauge_ref, out_ref):
    blocks, slots, width = inc_ref.shape
    tile = 8
    side = tile * slots
    weights = inc_ref[...].astype(F32).astype(BF16)
    row = lax.broadcasted_iota(jnp.int32, (side, side), 0)
    col = lax.broadcasted_iota(jnp.int32, (side, side), 1)
    same = row // slots == col // slots
    for i in range(blocks // tile):
        flat = weights[i * tile : (i + 1) * tile].reshape(side, width)
        full = lax.dot_general(flat, flat, (((1,), (1,)), ((), ())), preferred_element_type=F32)
        own = jnp.where(same, full, 0.0)
        out_ref[pl.ds(0, slots), pl.ds(i * side, side)] = jnp.sum(own.reshape(tile, slots, side), axis=0)
    out_ref[pl.ds(slots, 8), :] = jnp.broadcast_to(gauge_ref[...].astype(F32), (8, blocks * slots))


def describe(incidence, row_gauge):
    blocks, slots, _ = incidence.shape
    count = blocks * slots
    return pl.pallas_call(
        describe_kernel,
        out_shape=jax.ShapeDtypeStruct((slots + 8, count), F32),
        compiler_params=params(),
        name="describe",
        cost_estimate=SMALL,
    )(incidence, row_gauge.reshape(1, count))


def send_kernel(
    inc_hbm, field_hbm, gauge_hbm, kind_hbm, out_ref, inc_ref, field_ref, gauge_ref, kind_ref, sems, label_sems
):
    blocks, slots, width = inc_ref.shape
    chunks = sems.shape[0]
    step = blocks // chunks
    copies = []
    for i in range(chunks):
        near = pl.ds(i * step, step)
        far = pl.ds(i * step * width, step * width)
        copies.append(
            (
                pltpu.make_async_copy(inc_hbm.at[near], inc_ref.at[near], sems.at[i, 0]),
                pltpu.make_async_copy(field_hbm.at[far], field_ref.at[far], sems.at[i, 1]),
            )
        )
        for copy in copies[-1]:
            copy.start()
    labels = (
        pltpu.make_async_copy(gauge_hbm, gauge_ref, label_sems.at[0]),
        pltpu.make_async_copy(kind_hbm, kind_ref, label_sems.at[1]),
    )
    for copy in labels:
        copy.start()
    for i in range(chunks):
        for copy in copies[i]:
            copy.wait()
        parts = []
        for b in range(i * step, (i + 1) * step):
            weight = inc_ref[b].astype(F32).astype(BF16)
            value = jnp.concatenate(pieces(field_ref[pl.ds(b * width, width), :], 3)[::-1], axis=0)
            parts.append(dot(jnp.concatenate([weight] * 3, axis=1), value))
        out_ref[pl.ds(0, HOURS), pl.ds(i * step * slots, step * slots)] = jnp.transpose(
            jnp.concatenate(parts, axis=0)
        )
    for copy in labels:
        copy.wait()
    count, kinds = gauge_ref.shape[1], kind_ref.shape[1]
    kind = jnp.concatenate([kind_ref[...].astype(F32), jnp.zeros((1, count - kinds), F32)], axis=1)
    out_ref[pl.ds(HOURS, 8), :] = jnp.concatenate(
        [gauge_ref[...].astype(F32), kind, jnp.zeros((6, count), F32)], axis=0
    )


def send(incidence, field, row_gauge, gauge_kernel):
    count, rows = row_gauge.shape[0], gauge_kernel.shape[0]
    chunks = 4
    return pl.pallas_call(
        send_kernel,
        in_specs=[pl.BlockSpec(memory_space=pltpu.HBM)] * 4,
        out_shape=jax.ShapeDtypeStruct((HOURS + 8, count), F32),
        scratch_shapes=[
            pltpu.VMEM(incidence.shape, incidence.dtype),
            pltpu.VMEM(field.shape, F32),
            pltpu.VMEM((1, count), row_gauge.dtype),
            pltpu.VMEM((1, rows), gauge_kernel.dtype),
            pltpu.SemaphoreType.DMA((chunks, 2)),
            pltpu.SemaphoreType.DMA((2,)),
        ],
        compiler_params=params(60),
        name="send",
        cost_estimate=SMALL,
    )(incidence, field, row_gauge.reshape(1, count), gauge_kernel.reshape(1, rows))


def hot_rows(gauge, first, rows):
    mine = (lax.broadcasted_iota(jnp.int32, (rows, gauge.shape[1]), 0) + first).astype(F32)
    return jnp.where(gauge == mine, 1.0, 0.0).astype(BF16)


def spread_kernel(first_ref, mine_ref, other_ref, *out_refs):
    rows = out_refs[0].shape[1]
    both = jnp.concatenate([mine_ref[...], other_ref[...]], axis=1)
    stacked = jnp.concatenate(pieces(both[:HOURS], 3), axis=0)
    for m, out_ref in enumerate(out_refs):
        hot = hot_rows(both[HOURS : HOURS + 1], first_ref[m], rows)
        result = lax.dot_general(stacked, hot, (((1,), (1,)), ((), ())), preferred_element_type=F32)
        out_ref[...] = (result[2 * HOURS :] + result[HOURS : 2 * HOURS]) + result[:HOURS]


def spread(first, parcels, rows):
    return pl.pallas_call(
        spread_kernel,
        in_specs=[pl.BlockSpec(memory_space=pltpu.SMEM)] + [pl.BlockSpec(memory_space=pltpu.VMEM)] * 2,
        out_shape=[jax.ShapeDtypeStruct((HOURS, rows), F32)] * 4,
        compiler_params=params(),
        name="spread",
        cost_estimate=SMALL,
    )(first, *parcels)


def plane_couple_kernel(last, first_ref, *refs):
    if last:
        all_ref, before_ref, high_ref, low_ref, total_ref, meta_ref = refs
        total_ref[...] = before_ref[...]
    else:
        all_ref, total_ref, meta_ref = refs
        total_ref[...] = jnp.zeros_like(total_ref)
    parts, height, count = meta_ref.shape
    slots = height - 8
    cols, rows = total_ref.shape
    tile = 256
    for i in range(parts):
        meta_ref[i] = all_ref[:, i * count : (i + 1) * count]
    row = lax.broadcasted_iota(jnp.int32, (tile, tile), 0)
    col = lax.broadcasted_iota(jnp.int32, (tile, tile), 1)
    same = row // slots == col // slots

    def body(i, carry):
        gauge = meta_ref[i, slots : slots + 1, :]
        near = []
        for j in range(count // tile):
            here = slice(j * tile, (j + 1) * tile)
            block = jnp.concatenate([meta_ref[i, :slots, here]] * (tile // slots), axis=0)
            block = jnp.where(same, block, 0.0).astype(BF16)
            mine = jnp.concatenate(
                [hot_rows(gauge[:, here], first_ref[4 + h], rows // 2) for h in range(2)], axis=0
            )
            near.append(
                lax.dot_general(block, mine, (((1,), (1,)), ((), ())), preferred_element_type=F32)
            )
        near = jnp.concatenate(near, axis=0)
        high = near.astype(BF16)
        rest = near - high.astype(F32)
        hot = jnp.concatenate([hot_rows(gauge, first_ref[m], cols // 4) for m in range(4)], axis=0)
        total_ref[...] += dot(hot, high)

        @pl.when(jnp.max(jnp.abs(rest)) > 0.0)
        def _():
            total_ref[...] += dot(hot, rest.astype(BF16))

        return carry

    lax.fori_loop(0, parts, body, 0)
    if last:
        high, low = pieces(total_ref[...], 2)
        high_ref[...] = high
        low_ref[...] = low


def plane_couple(first, meta, rows, before=None):
    height, wide = meta.shape
    parts = 2 * X_
    shape = (4 * rows, 2 * rows)
    last = before is not None
    args = [first, meta] + ([before] if last else [])
    scratch = [pltpu.VMEM((parts, height, wide // parts), F32)]
    return pl.pallas_call(
        functools.partial(plane_couple_kernel, last),
        in_specs=[pl.BlockSpec(memory_space=pltpu.SMEM)]
        + [pl.BlockSpec(memory_space=pltpu.VMEM)] * (len(args) - 1),
        out_shape=[jax.ShapeDtypeStruct(shape, BF16)] * 2 if last else jax.ShapeDtypeStruct(shape, F32),
        scratch_shapes=([pltpu.VMEM(shape, F32)] if last else []) + scratch,
        compiler_params=params(),
        name="plane_couple",
        cost_estimate=pl.CostEstimate(
            flops=2 * 8 * wide * rows * rows, bytes_accessed=2_000_000, transcendentals=0
        ),
    )(*args)


def plane_mix_kernel(high_ref, low_ref, a_ref, b_ref, c_ref, d_ref, *refs):
    *extra, mine_ref, other_ref = refs
    refs = (a_ref, b_ref, c_ref, d_ref)
    height, rows = a_ref.shape
    body = pl.ds(0, HOURS)
    one, two = pieces(jnp.concatenate([ref[body, :] for ref in refs], axis=1), 2)
    both = dot(jnp.concatenate([two, one], axis=0), high_ref[...])
    result = (both[:HOURS] + dot(one, low_ref[...])) + both[HOURS:]
    mine_ref[body, :] = result[:, :rows]
    other_ref[body, :] = result[:, rows:]
    if height > HOURS:
        tail = pl.ds(HOURS, NOTE)
        note = sum(ref[tail, :] for ref in refs)
        mine_ref[tail, :] = note
        other_ref[tail, :] = note
    for ref in extra:
        other_ref[pl.ds(height, ref.shape[0]), :] = ref[...]


def plane_mix(coupling, values, extra):
    height, rows = values[0].shape
    return pl.pallas_call(
        plane_mix_kernel,
        out_shape=[
            jax.ShapeDtypeStruct((height, rows), F32),
            jax.ShapeDtypeStruct((height + sum(value.shape[0] for value in extra), rows), F32),
        ],
        compiler_params=params(),
        name="plane_mix",
        cost_estimate=SMALL,
    )(*coupling, *values, *extra)


def plane_rows_kernel(first_ref, meta_ref, meta_other_ref, a_ref, b_ref, c_ref, d_ref, *refs):
    if len(refs) > 2:
        *stack, last_ref, beside_ref, mine_ref, other_ref, stack_ref = refs
    else:
        mine_ref, other_ref = refs
    rows = a_ref.shape[1]
    value = jnp.concatenate([ref[pl.ds(0, HOURS), :] for ref in (a_ref, b_ref, c_ref, d_ref)], axis=1)
    one, two = pieces(value, 2)
    stacked = jnp.concatenate([two, one], axis=0)
    picked = []
    for ref in (meta_ref, meta_other_ref):
        gauge = ref[0:1, :]
        hot = jnp.concatenate([hot_rows(gauge, first_ref[m], rows) for m in range(4)], axis=0)
        both = dot(stacked, hot)
        picked.append(both[:HOURS] + both[HOURS:])
    mine_ref[...] = picked[0]
    count = picked[1].shape[1] // rows
    for i in range(count):
        other_ref[pl.ds(i * HOURS, HOURS), :] = picked[1][:, i * rows : (i + 1) * rows]
    if len(refs) > 2:
        top = stack_ref.shape[0] - HOURS
        for ref in stack:
            stack_ref[pl.ds(0, top), :] = ref[...]
        for i in range(count):
            here = pl.ds(i * rows, rows)
            beside = beside_ref[pl.ds(beside_ref.shape[0] - (count - i) * HOURS, HOURS), :]
            stack_ref[pl.ds(top, HOURS), here] = last_ref[:, here] + beside


def plane_rows(first, metas, values, before):
    rows = values[0].shape[1]
    slots = metas[0].shape[1]
    args = [first, *metas, *values, *before]
    shapes = [(HOURS, slots), (slots // rows * HOURS, rows)]
    if before:
        shapes.append(((len(before) - 1) * HOURS, slots))
    return pl.pallas_call(
        plane_rows_kernel,
        in_specs=[pl.BlockSpec(memory_space=pltpu.SMEM)]
        + [pl.BlockSpec(memory_space=pltpu.VMEM)] * (len(args) - 1),
        out_shape=[jax.ShapeDtypeStruct(shape, F32) for shape in shapes],
        compiler_params=params(),
        name="plane_rows",
        cost_estimate=pl.CostEstimate(flops=1_000_000_000, bytes_accessed=2_000_000, transcendentals=0),
    )(*args)


def gain(kernels):
    return jnp.max(jnp.sum(kernels, axis=1, keepdims=True), axis=0, keepdims=True)


def spectra(kind, kernels, wide):
    classes = kernels.shape[0]
    row = lax.broadcasted_iota(jnp.int32, (classes, kind.shape[1]), 0).astype(F32)
    hot = jnp.where(row == kind, 1.0, 0.0).astype(BF16)
    taps = jnp.transpose(kernels / gain(kernels))
    chosen = dot(jnp.concatenate(pieces(taps, 3)[::-1], axis=1), jnp.concatenate([hot] * 3, axis=0))
    return product(wide, chosen, 3)


def plane_spectrum_kernel(class_ref, kernels_ref, wide_ref, out_ref):
    kind = class_ref[1:2, : out_ref.shape[1]]
    out_ref[...] = spectra(kind, kernels_ref[...], wide_ref[...])


def plane_spectrum(meta, kernels, wide, rows):
    return pl.pallas_call(
        plane_spectrum_kernel,
        out_shape=jax.ShapeDtypeStruct((SPAN, rows), F32),
        compiler_params=params(),
        name="plane_spectrum",
        cost_estimate=SMALL,
    )(meta, kernels, wide)


def sides(even, pair, middle):
    return jnp.where(even, middle, pair), jnp.where(even, pair, middle)


def plane_call(kernel, name, shapes, flags, args):
    return pl.pallas_call(
        kernel,
        in_specs=[pl.BlockSpec(memory_space=pltpu.SMEM)] * len(flags)
        + [pl.BlockSpec(memory_space=pltpu.VMEM)] * len(args),
        out_shape=[jax.ShapeDtypeStruct(shape, F32) for shape in shapes],
        compiler_params=params(),
        name=name,
        cost_estimate=SMALL,
    )(*flags, *args)


def plane_first_kernel(
    flag_ref, here_ref, pair_ref, middle_ref, spec_ref, kernels_ref, forward3, last3, forward, first, out_ref
):
    spec = spec_ref[...]
    before, after = sides(flag_ref[0] > 0.5, pair_ref[...], middle_ref[...])
    here = here_ref[...]
    both = plane_delayed(before[:HOURS], here[:HOURS], after[:HOURS], spec, forward3[...], last3[...], 3)
    scale = gain(kernels_ref[...])
    now = here[HOURS:] - both[0] * scale
    later = (after[HOURS:] - both[1] * scale) * flag_ref[1]
    out_ref[...] = plane_advanced(now, later, spec, forward[...], first[...], 2)


def plane_delay_kernel(flag_ref, here_ref, pair_ref, middle_ref, spec_ref, forward, last, out_ref):
    body = pl.ds(0, HOURS)
    before, after = sides(flag_ref[0] > 0.5, pair_ref[body, :], middle_ref[body, :])
    out = plane_delayed(before, here_ref[body, :], after, spec_ref[...], forward[...], last[...], 2)
    for i in range(2):
        out_ref[pl.ds(i * HOURS, HOURS), :] = out[i]


def write_note(ref, rows):
    tail = [jnp.zeros((NOTE - len(rows), ref.shape[1]), F32)]
    ref[pl.ds(HOURS, NOTE), :] = jnp.concatenate(rows + tail, axis=0)


def plane_open_kernel(
    flag_ref, here_ref, pair_ref, middle_ref, pulled_ref, spec_ref, forward, first, last, out_ref, delayed_ref
):
    here = here_ref[...]
    spec = spec_ref[...]
    before, after = sides(flag_ref[0] > 0.5, pair_ref[...], middle_ref[...])
    now, later = plane_delayed(before, here, after, spec, forward[...], last[...], 2)
    out_ref[pl.ds(0, HOURS), :] = plane_advanced(now, later * flag_ref[1], spec, forward[...], first[...], 2)
    write_note(out_ref, [lanes(pulled_ref[...], here), lanes(now, now)])
    delayed_ref[pl.ds(0, HOURS), :] = now
    delayed_ref[pl.ds(HOURS, HOURS), :] = later


def plane_step_kernel(
    flag_ref,
    here_ref,
    pair_ref,
    two_ref,
    mirror_ref,
    pulled_ref,
    delayed_ref,
    old_z_ref,
    old_s_ref,
    old_delayed_ref,
    spec_ref,
    forward,
    first,
    total_ref,
    out_ref,
    kept_ref,
):
    tail, body = pl.ds(HOURS, NOTE), pl.ds(0, HOURS)
    total_ref[...] = (here_ref[tail, :] + pair_ref[tail, :]) + (two_ref[...] + mirror_ref[...])
    inverse = total(total_ref, 0) / total(total_ref, 1)
    z = pulled_ref[body, :] * inverse - old_z_ref[...]
    s = here_ref[body, :] * inverse - old_s_ref[...]
    both = delayed_ref[...] * inverse - old_delayed_ref[...]
    now, later = both[:HOURS], both[HOURS:]
    following = plane_advanced(now, later * flag_ref[1], spec_ref[...], forward[...], first[...], 2)
    out_ref[body, :] = following * inverse
    write_note(out_ref, [lanes(z, s), lanes(now, now)])
    for i, value in enumerate((z, s, now)):
        kept_ref[pl.ds(i * HOURS, HOURS), :] = value


def plane_close_kernel(
    here_ref,
    before_ref,
    pulled_ref,
    kept_ref,
    old_z_ref,
    old_s_ref,
    old_delayed_ref,
    open_ref,
    spec_ref,
    kernels_ref,
    forward,
    last,
    out_ref,
):
    body = pl.ds(0, HOURS)
    here, raw = here_ref[body, :], pulled_ref[body, :]
    waves = product(forward[...], jnp.concatenate([before_ref[body, :], here], axis=0), 2)
    now = product(last[...], turn(waves, spec_ref[...], 1.0), 2)
    z, s, delayed = (kept_ref[pl.ds(i * HOURS, HOURS), :] for i in range(3))
    note = [pulled_ref[HOURS + i : HOURS + i + 1, :] for i in range(2)]
    for left in (raw, z, old_z_ref[...]):
        note += [lanes(left, right) for right in (here, s, old_s_ref[...])]
    parts = (now, delayed, old_delayed_ref[body, :])
    for i in range(3):
        note += [lanes(parts[i], parts[j]) for j in range(i, 3)]
    known = [total(open_ref, 0), total(open_ref, 1), gain(kernels_ref[...])]
    note = [jnp.sum(jnp.concatenate(note, axis=0), axis=1, keepdims=True)]
    note += [value / out_ref.shape[0] for value in known]
    count = sum(value.shape[0] for value in note)
    note = jnp.concatenate(note + [jnp.zeros((24 - count, 1), F32)], axis=0)
    shape = (24, out_ref.shape[1])
    row, col = (lax.broadcasted_iota(jnp.int32, shape, i) for i in range(2))
    note = jnp.sum(jnp.where(row == col, jnp.broadcast_to(note, shape), 0.0), axis=0, keepdims=True)
    out_ref[...] = jnp.broadcast_to(note, out_ref.shape)


def plane_weights(close):
    entry = lambda i: close[:, i : i + 1]
    n1, t1, scale = (entry(17 + i) for i in range(3))
    n2, t2 = entry(0), entry(1)
    a1 = t1 / n1
    a2, r2 = (t2 / n2) / a1, n2 / n1
    plain = (1.0, -a2, -r2)
    n3 = sum(plain[i] * plain[j] * entry(2 + 3 * i + j) for i in range(3) for j in range(3))
    pairs = [(i, j) for i in range(3) for j in range(i, 3)]
    t3 = sum(
        plain[i] * plain[j] * entry(11 + n) * (1.0 if i == j else 2.0) for n, (i, j) in enumerate(pairs)
    )
    a3, r3 = (t3 / n3) / a1, n3 / n2
    unit = 1.0 / (a1 * scale)
    c3 = unit / (a3 * (a2 - r2) - r3)
    c2 = -a3 * c3
    c1 = unit - r2 * c2
    step = c2 - c3 * a2
    return c1 - step - c3 * r2, step / a1, c3


def plane_combine_kernel(close_ref, stack_ref, mine_ref, beside_ref, out_ref):
    rows = beside_ref.shape[1]
    close = jnp.sum(close_ref[...], axis=0, keepdims=True)
    e0, e1, e2 = plane_weights(close)
    for i in range(out_ref.shape[0] // rows):
        here = pl.ds(i * rows, rows)
        last = mine_ref[:, here] + beside_ref[pl.ds(i * HOURS, HOURS), :]
        value = stack_ref[pl.ds(0, HOURS), here] * e0 + stack_ref[pl.ds(HOURS, HOURS), here] * e1 + last * e2
        out_ref[here, :] = jnp.transpose(value)


def plane_finish_kernel(rows_ref, inc_ref, field_ref, out_ref):
    blocks, slots, width = inc_ref.shape
    weights = inc_ref[...].astype(F32).astype(BF16)
    for b in range(blocks):
        here = pl.ds(b * width, width)
        rows = jnp.concatenate(pieces(rows_ref[pl.ds(b * slots, slots), :], 2), axis=0)
        twice = jnp.concatenate([weights[b]] * 2, axis=0)
        added = lax.dot_general(twice, rows, (((0,), (0,)), ((), ())), preferred_element_type=F32)
        out_ref[here, :] = field_ref[here, :] + added


def plane_finish(rows, incidence, field):
    blocks, slots, width = incidence.shape
    hours = field.shape[1]
    step = 16
    return pl.pallas_call(
        plane_finish_kernel,
        grid=(blocks // step,),
        in_specs=[
            pl.BlockSpec((step * slots, hours), lambda i: (i, 0)),
            pl.BlockSpec((step, slots, width), lambda i: (i, 0, 0)),
            pl.BlockSpec((step * width, hours), lambda i: (i, 0)),
        ],
        out_specs=pl.BlockSpec((step * width, hours), lambda i: (i, 0)),
        out_shape=jax.ShapeDtypeStruct(field.shape, F32),
        compiler_params=params(),
        name="plane_finish",
    )(rows, incidence, field)


def plane_shards(incidence, row_gauge, gauge_kernel, kernels, observed, first_guess):
    rows, hours = observed.shape
    basin, tm = lax.axis_index("basin"), lax.axis_index("tm")
    z, x, y, c = basin // X_, basin % X_, tm // C_, tm % C_
    place = 2 * y + x
    first = jnp.stack([4 * c + (place ^ m) for m in range(4)] + [4 * c + place, 4 * (1 - c) + place])
    first = (first * rows).astype(jnp.int32)
    flags = jnp.stack([1 - z % 2, (z < Z_ - 1).astype(z.dtype), (z > 0).astype(z.dtype)]).astype(F32)
    forward, inverse_first, inverse_last, _ = turned_transforms(2)
    forward3, _, inverse_last3, short3 = turned_transforms(3)
    block, noted = (hours, rows), (hours + NOTE, rows)

    seen = moved(observed, to_plane)
    parcel = send(incidence, first_guess, row_gauge, gauge_kernel)
    parcel, near = lax.optimization_barrier((parcel, incidence))
    parcel = moved(parcel, to_plane)
    near, seen = lax.optimization_barrier((near, seen))
    meta = describe(near, row_gauge)
    meta = jnp.concatenate([meta, moved(meta, over_x)], axis=1)
    half = meta.shape[1] // 2
    share = jnp.where(c == 0, meta[:, :half], meta[:, half:])
    close = moved(share, z_pair)
    parcel, seen, close = lax.optimization_barrier((parcel, seen, close))
    parcels = [parcel, moved(parcel, over_core)]
    spec = plane_spectrum(parcel[hours:], kernels, short3, rows)
    parcels[1], seen, spec = lax.optimization_barrier((parcels[1], seen, spec))
    far = moved(jnp.concatenate([share, close], axis=1), z_two)
    dense = spread(first, parcels, rows)
    metas = [value[hours:] for value in parcels]
    sums = dense[0] + sum(moved(value, where) for value, where in zip(dense[1:], SQUARE))
    sums, far = lax.optimization_barrier((sums, far))
    held = jnp.concatenate([close, far], axis=1)
    around = [
        jnp.concatenate([meta, held[:, : 2 * half]], axis=1),
        jnp.concatenate([held[:, 2 * half :], moved(held, over_core)], axis=1),
    ]
    sums = jnp.concatenate([sums, jnp.transpose(seen)], axis=0)
    sums = [sums, moved(sums, z_pair), moved(sums, z_middle)]
    coupled = plane_couple(first, around[0], rows)
    coupled, sums = lax.optimization_barrier((coupled, sums))
    coupling = plane_couple(first, around[1], rows, coupled)
    (pulled0,) = plane_call(
        plane_first_kernel,
        "plane_first",
        [block],
        [flags],
        [*sums, spec, kernels, forward3, inverse_last3, forward, inverse_first],
    )

    def mixing(pulled, extra):
        values = [pulled] + [moved(pulled, where) for where in SQUARE]
        mine, other = plane_mix(coupling, values, extra)
        beside = moved(other, over_core)
        return values, mine + beside[: pulled.shape[0]], beside

    values, mixed0, _ = mixing(pulled0, [])
    picked, theirs = plane_rows(first, metas, values, [])
    sums = [mixed0, moved(mixed0, z_pair), moved(mixed0, z_middle)]
    pulled1, delayed0 = plane_call(
        plane_open_kernel,
        "plane_open",
        [noted, (2 * hours, rows)],
        [flags],
        [*sums, pulled0, spec, forward, inverse_first, inverse_last],
    )

    values, mixed1, beside = mixing(pulled1, [theirs])
    picked, theirs, stack = plane_rows(first, metas, values, [picked, beside])
    sums = [mixed1, moved(mixed1, z_pair), moved(mixed1, z_middle)]
    two, mirror = moved(mixed1[hours:], z_two), moved(mixed1[hours:], z_mirror)
    (delayed1,) = plane_call(
        plane_delay_kernel, "plane_delay", [(2 * hours, rows)], [flags], [*sums, spec, forward, inverse_last]
    )
    open_note, pulled2, kept = plane_call(
        plane_step_kernel,
        "plane_step",
        [(NOTE, rows), noted, (3 * hours, rows)],
        [flags],
        [*sums[:2], two, mirror, pulled1, delayed1, pulled0, mixed0, delayed0, spec, forward, inverse_first],
    )

    values, mixed2, beside = mixing(pulled2, [theirs])
    picked, theirs, stack = plane_rows(first, metas, values, [stack, picked, beside])
    (note,) = plane_call(
        plane_close_kernel,
        "plane_close",
        [(Z_ * X_ * Y_ * C_, rows // 2)],
        [],
        [
            *(mixed2, moved(mixed2, z_next), pulled2, kept, pulled0, mixed0, delayed0),
            *(open_note, spec, kernels, forward, inverse_last),
        ],
    )
    close_note = lax.all_to_all(note, ("basin", "tm"), 0, 0, tiled=True)
    (answer,) = plane_call(
        plane_combine_kernel,
        "plane_combine",
        [(parcel.shape[1], hours)],
        [],
        [close_note, stack, picked, moved(theirs, over_core)],
    )
    return plane_finish(moved(answer, from_plane), incidence, first_guess)


def solution(mesh):
    planes = dict(mesh.shape) == {"basin": Z_ * X_, "tm": Y_ * C_}
    in_specs = (
        P("basin", None, None),
        P("basin"),
        P("basin"),
        P(),
        P("basin", "tm"),
        P("basin", "tm"),
    )
    return jax.shard_map(
        plane_shards if planes else shards, mesh=mesh, in_specs=in_specs, out_specs=P("basin", "tm"), check_vma=False
    )
```
